32 devices in a mesh: rows: 8 (over y, x, core), mem: 4 (over z).
Axes of the slice: x: 2, y: 2, z: 4, core: 2. Of those that a mesh axis runs over, the one named last changes fastest.
Arguments:
- tokens: bfloat16 [32, 256, 1024], P(('rows', 'mem')), may hold values from -6 to 6
- memory: bfloat16 [32, 256, 1024], P('rows', 'mem'), may hold values from -6 to 6
- token_ids: int32 [32, 256], P('rows'), may hold values from 0 to 7, never falling along the last dimension, each value on 1 to 64 neighbouring positions
- memory_ids: int32 [32, 256], P('rows'), may hold values from 0 to 7, as said below
- out_grad: bfloat16 [32, 256, 1024], P(('rows', 'mem')), may hold values from -6 to 6
- self_query: bfloat16 [1024, 1024], P(('rows', 'mem')), may hold values from -0.375 to 0.375
- self_key: bfloat16 [1024, 1024], P(('rows', 'mem')), may hold values from -0.1875 to 0.1875
- self_value: bfloat16 [1024, 1024], P(('rows', 'mem')), may hold values from -0.1875 to 0.1875
- self_output: bfloat16 [1024, 1024], P(('rows', 'mem')), may hold values from -1.5 to 1.5
- cross_query: bfloat16 [1024, 1024], P(('rows', 'mem')), may hold values from -0.375 to 0.375
- cross_key: bfloat16 [1024, 1024], P(('rows', 'mem')), may hold values from -0.1875 to 0.1875
- cross_value: bfloat16 [1024, 1024], P(('rows', 'mem')), may hold values from -0.1875 to 0.1875
- cross_output: bfloat16 [1024, 1024], P(('rows', 'mem')), may hold values from -1.5 to 1.5
- expand_weight: bfloat16 [1024, 4096], P(('rows', 'mem')), may hold values from -0.1875 to 0.1875
- contract_weight: bfloat16 [4096, 1024], P(('rows', 'mem')), may hold values from -0.375 to 0.375
- norm_gains: bfloat16 [3, 1024], P(None, ('rows', 'mem')), may hold values from 0.099609375 to 1.8984375
- norm_shifts: bfloat16 [3, 1024], P(None, ('rows', 'mem')), may hold values from -1 to 1
Outputs:
- result: float32 [32, 256, 1024], P(('rows', 'mem'))
- input_grad: float32 [32, 256, 1024], P(('rows', 'mem'))
- memory_grad: float32 [32, 256, 1024], P('rows', 'mem')
- self_query_grad: float32 [1024, 1024], P(('rows', 'mem'))
- self_key_grad: float32 [1024, 1024], P(('rows', 'mem'))
- self_value_grad: float32 [1024, 1024], P(('rows', 'mem'))
- decoder_mixing_cotangent: float32 [1024, 1024], P(('rows', 'mem'))
- cross_query_grad: float32 [1024, 1024], P(('rows', 'mem'))
- cross_key_grad: float32 [1024, 1024], P(('rows', 'mem'))
- cross_value_grad: float32 [1024, 1024], P(('rows', 'mem'))
- cross_output_grad: float32 [1024, 1024], P(('rows', 'mem'))
- expand_grad: float32 [1024, 4096], P(('rows', 'mem'))
- down_projection_gradient: float32 [4096, 1024], P(('rows', 'mem'))
- gains_grad: float32 [3, 1024], P(None, ('rows', 'mem'))
- shifts_grad: float32 [3, 1024], P(None, ('rows', 'mem'))
The draws below stay inside these ranges and needn't reach their ends.
Inputs may be any that keep to these rules, and one draw needn't show every extreme that they name: `token_ids`: along each row the ids never fall, and every id from 0 to 7 covers 1 to 64 tokens. `memory_ids`: along each row the ids never fall, and every id from 0 to 7 covers at least one token.
All inputs are finite; a program needn't handle non-finite values.
Results may differ from the reference program's by a relative error of at most 0.019.
The reference program's roundings to bfloat16 on the way count: a program that leaves them out, or rounds other values in their place, can miss the bound.
Values may be sent and summed in bfloat16 or wider, within the bound.
A program may use at most 256 MiB of HBM per device.

```python
import math
import jax
import jax.numpy as jnp
import numpy as np
from jax import lax

D = 1024
FF = 4096
HEADS = 16
HEAD_DIM = 64
DOCS = 8
LEN = 256
MLEN = 256
SEQS = 32
GROUP_SEQS = 4


def draw_memory_ids(key, part):
    key = jax.random.fold_in(key, 7)
    jitter_key, choose_key = jax.random.split(key)
    block = MLEN // DOCS
    jitter = block // 4
    marks = jnp.arange(1, DOCS, dtype=jnp.int32) * block
    moves = jax.random.randint(jitter_key, (SEQS, DOCS - 1), -jitter, jitter + 1, dtype=jnp.int32)
    cuts = marks[None, :] + moves
    tail = MLEN - DOCS + jnp.arange(1, DOCS, dtype=jnp.int32)
    chosen = jax.random.randint(choose_key, (SEQS // GROUP_SEQS,), 0, GROUP_SEQS, dtype=jnp.int32)
    row_index = jnp.arange(SEQS, dtype=jnp.int32)
    special = row_index % GROUP_SEQS == jnp.repeat(chosen, GROUP_SEQS)
    cuts = jnp.where(special[:, None], tail[None, :], cuts)
    places = jnp.arange(MLEN, dtype=jnp.int32)
    return jnp.sum((places[None, :, None] >= cuts[:, None, :]).astype(jnp.int32), axis=2)


def shard_levels(own_key, extent, cuts, smallest, high):
    def one(dim, parts):
        steps = jax.random.uniform(jax.random.fold_in(jax.random.fold_in(own_key, 6), dim), (parts,), jnp.float32, smallest / len(cuts), high / len(cuts))
        return jnp.repeat(jnp.exp(steps), extent[dim] // parts).reshape((-1,) + (1,) * (len(extent) - dim - 1))

    level = one(*cuts[0])
    for cut in cuts[1:]:
        level = level * one(*cut)
    return level


def length_profile(number_of, total, reach, skew):
    weights = [(1 << 20) // math.isqrt(standing ** skew) + 1 for standing in range(2, number_of + 1)]
    rest, holding = total - reach - (number_of - 1), [1] * (number_of - 1)
    while rest > 0:
        candidates = [i for i in range(number_of - 1) if holding[i] < reach]
        mass, remaining = sum([weights[i] for i in candidates]), rest
        for i in candidates:
            more = min(reach - holding[i], max(1, remaining * weights[i] // mass), rest)
            holding[i] = holding[i] + more
            rest = rest - more
    return np.array([reach] + holding)


def ragged(key, count, total, limit, slope):
    if count == 2:
        one = jax.random.randint(key, (), max(1, total - limit), min(limit, total - 1) + 1)
        return jnp.stack([one, total - one])
    sizes = jnp.asarray(length_profile(count, total, limit, slope), jnp.int32)
    twos = (count - 1) // 2
    source_of, receiver = sizes[1:1 + 2 * twos:2], sizes[2:2 + 2 * twos:2]
    room = jnp.minimum(source_of - 1, limit - receiver)
    shifted = jax.random.randint(jax.random.fold_in(key, 1), (twos,), 0, 1 << 20) % (room + 1)
    sizes = sizes.at[1:1 + 2 * twos:2].set(source_of - shifted).at[2:2 + 2 * twos:2].set(receiver + shifted)
    return sizes[jax.random.permutation(jax.random.fold_in(key, 2), count)]


def normal_values(stream_key, dims, scale, limit, cuts=(), held_as=jnp.bfloat16):
    drawn = jax.random.normal(stream_key, dims, jnp.float32) * scale
    if len(cuts) > 0:
        drawn = shard_levels(stream_key, dims, cuts, -0.22, 0.18) * drawn
    return jnp.clip(drawn, min=-limit, max=limit).astype(held_as)


def setup_inputs(seed: int = 0) -> dict:
    arg_keys = jax.random.split(jax.random.key(seed), 18)
    tokens = normal_values(arg_keys[0], (SEQS, LEN, D), 1.0, 6.0, ((0, 32),))
    memory = normal_values(arg_keys[1], (SEQS, MLEN, D), 1.0, 6.0, ((0, 8), (1, 4)))
    token_ids = jax.vmap(lambda own: jnp.searchsorted(jnp.cumsum(ragged(own, DOCS, LEN, LEN // 4, 1)), jnp.arange(LEN), side="right"))(jax.random.split(arg_keys[2], SEQS)).reshape((SEQS, LEN)).astype(jnp.int32)
    memory_ids = draw_memory_ids(jax.random.fold_in(arg_keys[17], 71), 0)
    out_grad = normal_values(arg_keys[4], (SEQS, LEN, D), 1.0, 6.0, ((0, 32),))
    self_query = normal_values(arg_keys[5], (D, D), (D // 4) ** -0.5, 0.375, ((0, 32),))
    self_key = normal_values(arg_keys[6], (D, D), D ** -0.5, 0.1875, ((0, 32),))
    self_value = normal_values(arg_keys[7], (D, D), D ** -0.5, 0.1875, ((0, 32),))
    self_output = normal_values(arg_keys[8], (D, D), (D // 64) ** -0.5, 1.5, ((0, 32),))
    cross_query = normal_values(arg_keys[9], (D, D), (D // 4) ** -0.5, 0.375, ((0, 32),))
    cross_key = normal_values(arg_keys[10], (D, D), D ** -0.5, 0.1875, ((0, 32),))
    cross_value = normal_values(arg_keys[11], (D, D), D ** -0.5, 0.1875, ((0, 32),))
    cross_output = normal_values(arg_keys[12], (D, D), (D // 64) ** -0.5, 1.5, ((0, 32),))
    expand_weight = normal_values(arg_keys[13], (D, FF), D ** -0.5, 0.1875, ((0, 32),))
    contract_weight = normal_values(arg_keys[14], (FF, D), (FF // 16) ** -0.5, 0.375, ((0, 32),))
    norm_gains = jnp.clip(1.0 + 0.18 * jax.random.normal(arg_keys[15], (3, D), jnp.float32), 0.099609375, 1.8984375).astype(jnp.bfloat16)
    norm_shifts = normal_values(arg_keys[16], (3, D), 0.2, 1.0, ((1, 32),))
    return dict(tokens=tokens, memory=memory, token_ids=token_ids, memory_ids=memory_ids, out_grad=out_grad, self_query=self_query, self_key=self_key, self_value=self_value, self_output=self_output, cross_query=cross_query, cross_key=cross_key, cross_value=cross_value, cross_output=cross_output, expand_weight=expand_weight, contract_weight=contract_weight, norm_gains=norm_gains, norm_shifts=norm_shifts)


ALPHA = 4.16
EPS = 1e-05
SCALE = 0.125
NEG = -1e+30
HIGH = lax.Precision.HIGHEST

@jax.custom_vjp
def low(v):
    return lax.optimization_barrier(v.astype(jnp.bfloat16)).astype(jnp.float32)

@jax.custom_vjp
def low_back(v):
    return v

def low_keep(v):
    return (low(v), None)

def low_pass(kept, grad):
    return (grad,)

def back_keep(v):
    return (v, None)

def back_low(kept, grad):
    return (low(grad),)
low.defvjp(low_keep, low_pass)
low_back.defvjp(back_keep, back_low)

def both(value):
    return low_back(low(value))

def layer_norm(hidden_activation, gain, shift):
    centre = hidden_activation - lax.optimization_barrier(jnp.mean(hidden_activation, axis=-1, keepdims=True))
    spread = lax.optimization_barrier(jnp.mean(centre * centre, axis=-1, keepdims=True))
    return centre * lax.rsqrt(spread + EPS) * gain + shift

def mix(left, right):
    return jnp.dot(left, right, precision=HIGH)

def attend(query, keys, values, allowed):
    heads_query = query.reshape(query.shape[0], HEADS, HEAD_DIM)
    heads_keys = keys.reshape(keys.shape[0], HEADS, HEAD_DIM)
    heads_values = values.reshape(values.shape[0], HEADS, HEAD_DIM)
    raw = jnp.einsum('khe,qhe->hkq', heads_keys, heads_query, precision=HIGH)
    scores = jnp.where(allowed[None], low_back(raw * SCALE), NEG)
    top = lax.optimization_barrier(jnp.max(scores, axis=1, keepdims=True))
    weight = jnp.exp(scores - top)
    probs = low(weight / lax.optimization_barrier(jnp.sum(weight, axis=1, keepdims=True)))
    mixed = jnp.einsum('hkq,khe->qhe', probs, heads_values, precision=HIGH)
    return both(mixed.reshape(query.shape[0], HEADS * HEAD_DIM))

def layer(weights, row, memory_row, row_ids, memory_row_ids):
    self_attention_query, decoder_match_label, self_attention_value, self_attention_output, encoder_lookup_probe, key_cross, value_cross, cross_attention_output, up_projection, narrowing_matrix, gain_rows, shift_rows = weights
    positions = jnp.arange(row.shape[0], dtype=jnp.int32)
    self_allowed = (row_ids[:, None] == row_ids[None, :]) & (positions[:, None] <= positions[None, :])
    cross_allowed = memory_row_ids[:, None] == row_ids[None, :]
    attention_result = attend(both(mix(row, self_attention_query)), both(mix(row, decoder_match_label)), both(mix(row, self_attention_value)), self_allowed)
    first = layer_norm(ALPHA * row + low_back(mix(attention_result, self_attention_output)), gain_rows[0], shift_rows[0])
    cross_attention_result = attend(both(mix(low(first), encoder_lookup_probe)), both(mix(memory_row, key_cross)), both(mix(memory_row, value_cross)), cross_allowed)
    second = layer_norm(ALPHA * first + low_back(mix(cross_attention_result, cross_attention_output)), gain_rows[1], shift_rows[1])
    hidden_activation = low(jax.nn.gelu(low_back(mix(low(second), up_projection)), approximate=False))
    return layer_norm(ALPHA * second + low_back(mix(hidden_activation, narrowing_matrix)), gain_rows[2], shift_rows[2])

def reference(tokens, memory, token_ids, memory_ids, out_grad, self_query, self_key, self_value, self_output, cross_query, cross_key, cross_value, cross_output, expand_weight, contract_weight, norm_gains, norm_shifts):
    weights = tuple((item.astype(jnp.float32) for item in (self_query, self_key, self_value, self_output, cross_query, cross_key, cross_value, cross_output, expand_weight, contract_weight, norm_gains, norm_shifts)))

    def one_row(total, items):
        row, memory_row, row_ids, memory_row_ids, cotangent = items

        def evaluate_layer(params, row_value, memory_value):
            return layer(params, row_value, memory_value, row_ids, memory_row_ids)
        output, pull = jax.vjp(evaluate_layer, weights, row.astype(jnp.float32), memory_row.astype(jnp.float32))
        weight_grads, row_grad, memory_row_grad = pull(cotangent.astype(jnp.float32))
        return (jax.tree.map(jnp.add, total, weight_grads), (output, row_grad, memory_row_grad))
    start = jax.tree.map(jnp.zeros_like, weights)
    sums, (result, input_grad, memory_grad) = lax.scan(one_row, start, (tokens, memory, token_ids, memory_ids, out_grad))
    return (result, input_grad, memory_grad, sums[0], sums[1], sums[2], sums[3], sums[4], sums[5], sums[6], sums[7], sums[8], sums[9], sums[10], sums[11])
```

```python
import functools

import jax
import jax.numpy as jnp
from jax import lax
from jax.experimental import pallas as pl
from jax.experimental.pallas import tpu as pltpu
from jax.sharding import PartitionSpec as P

MESH = pl.DeviceIdType.MESH

HEADS = 16
HEAD_DIM = 64


ALPHA = 4.16
EPS = 1e-05
SCALE = 0.125
NEG = -1e30


def layer_norm(hidden_activation, gain, shift):
    centre = hidden_activation - jnp.mean(hidden_activation, axis=-1, keepdims=True)
    spread = jnp.mean(centre * centre, axis=-1, keepdims=True)
    return centre * lax.rsqrt(spread + EPS) * gain + shift


def gelu_exact(value):
    return jax.nn.gelu(value, approximate=False)


def product(left, right):
    return jnp.dot(left, right, preferred_element_type=jnp.float32)


def split_heads(matrix):
    return matrix.reshape(matrix.shape[0], matrix.shape[1] // HEAD_DIM, HEAD_DIM)


def grouped(matrix):
    return jnp.moveaxis(matrix.reshape(matrix.shape[0], HEADS // 4, 4 * HEAD_DIM), 1, 0)


def ungrouped(stack):
    return jnp.moveaxis(stack, 0, 1).reshape(stack.shape[1], stack.shape[0] * stack.shape[2])


def row_map(function, items):
    return lax.map(lambda entry: function(*entry), items)


def score_block(query, keys, allowed):
    raw = jnp.einsum(
        "khe,qhe->hkq", split_heads(keys), split_heads(query), preferred_element_type=jnp.float32
    )
    return jnp.where(allowed[None], raw * SCALE, NEG)


def attend_probs(query, keys, allowed, lse):
    scores = score_block(query, keys, allowed)
    return jnp.where(allowed[None], jnp.exp(scores - lse[:, None, :]), 0.0)


def attend_forward(query, keys, values, allowed):
    scores = score_block(query, keys, allowed)
    top = jnp.max(scores, axis=1)
    weight = jnp.where(allowed[None], jnp.exp(scores - top[:, None, :]), 0.0)
    total = jnp.sum(weight, axis=1)
    probs = (weight / total[:, None, :]).astype(jnp.bfloat16)
    mixed = jnp.einsum(
        "hkq,khe->qhe", probs, split_heads(values), preferred_element_type=jnp.float32
    )
    return (mixed.reshape(query.shape), top + jnp.log(total))


def value_pull(grad, values):
    return jnp.einsum(
        "qhe,khe->hkq", split_heads(grad), split_heads(values), preferred_element_type=jnp.float32
    )


def score_grads(probs, pulled, inner):
    return (probs * (pulled - inner[:, None, :]) * SCALE).astype(jnp.bfloat16)


def query_from(score_grad, keys, shape):
    moved = jnp.einsum(
        "hkq,khe->qhe", score_grad, split_heads(keys), preferred_element_type=jnp.float32
    )
    return moved.reshape(shape)


def key_from(score_grad, query, shape):
    moved = jnp.einsum(
        "hkq,qhe->khe", score_grad, split_heads(query), preferred_element_type=jnp.float32
    )
    return moved.reshape(shape)


def value_from(probs, grad, values):
    moved = jnp.einsum(
        "hkq,qhe->khe",
        probs.astype(jnp.bfloat16),
        split_heads(grad),
        preferred_element_type=jnp.float32,
    )
    return moved.reshape(values.shape)


def local_forward(query, keys, values, allowed):

    def one_group(items):
        return attend_forward(items[0], items[1], items[2], allowed)

    mixed, lse = lax.map(one_group, (grouped(query), grouped(keys), grouped(values)))
    return (ungrouped(mixed), lse)


def local_backward(query, keys, values, allowed, lse, grad):

    def one_group(items):
        part_query, part_keys, part_values, part_lse, part_grad = items
        probs = attend_probs(part_query, part_keys, allowed, part_lse)
        pulled = value_pull(part_grad, part_values)
        inner = jnp.sum(probs * pulled, axis=1)
        score_grad = score_grads(probs, pulled, inner)
        return (
            query_from(score_grad, part_keys, part_query.shape),
            key_from(score_grad, part_query, part_keys.shape),
            value_from(probs, part_grad, part_values),
        )

    parts = lax.map(one_group, (grouped(query), grouped(keys), grouped(values), lse, grouped(grad)))
    return (ungrouped(parts[0]), ungrouped(parts[1]), ungrouped(parts[2]))


def flip(index, unit):
    return index + unit * (1 - 2 * ((index // unit) % 2))


class Place:
    def __init__(self, n_rows, n_mem):
        self.n_rows, self.n_mem = n_rows, n_mem
        self.digits = (n_rows // 2).bit_length() - 1
        self.row = lax.axis_index("rows")
        self.mem = lax.axis_index("mem")
        self.lane = self.row % 2

    def turn(self, index, stage):
        rising, falling = 2 << stage, 2 << (self.digits - 1 - stage)
        return flip(index, rising) * (1 - self.lane) + flip(index, falling) * self.lane

    def sibling(self):
        return (flip(self.row, 1), self.mem)

    def partner(self, stage):
        return (self.turn(self.row, stage), self.mem)

    def far(self, step):
        return (self.row, (self.mem + step) % self.n_mem)

    def greet(self):
        barrier = pltpu.get_barrier_semaphore()
        others = [self.far(step) for step in range(1, self.n_mem)]
        others += [self.partner(stage) for stage in range(self.digits)]
        others += [self.sibling()]
        for other in others:
            pl.semaphore_signal(barrier, inc=1, device_id=other, device_id_type=MESH)
        pl.semaphore_wait(barrier, len(others))


def remote(source, target, send_sem, recv_sem, device):
    return pltpu.make_async_remote_copy(
        src_ref=source,
        dst_ref=target,
        send_sem=send_sem,
        recv_sem=recv_sem,
        device_id=device,
        device_id_type=MESH,
    )


def gather_kernel(n_rows, n_mem, parts, count, *refs):
    ins, outs = refs[:count], refs[count : 2 * count]
    own_sem, far_send, far_recv, plane_send, plane_recv, core_send, core_recv = refs[2 * count :]
    place = Place(n_rows, n_mem)
    row, mem = place.row, place.mem

    def shard(part):
        array, picked = parts[part]
        return ins[array].at[picked]

    def blocks(part, *lead):
        array, picked = parts[part]
        return outs[array].at[lead + picked]

    def own(part):
        return pltpu.make_async_copy(shard(part), blocks(part, row, mem), own_sem.at[part])

    def spread_far(part):
        own(part).start()
        for step in range(1, n_mem):
            remote(
                shard(part),
                blocks(part, row, mem),
                far_send.at[part],
                far_recv.at[part],
                place.far(step),
            ).start()

    def held(stage):
        groups = [row]
        for before in range(stage):
            groups = groups + [place.turn(group, before) for group in groups]
        return groups

    def far_total(part):
        some = blocks(part, row, pl.ds(0, n_mem - 1))
        return remote(some, some, far_send.at[part], far_recv.at[part], place.far(1))

    def plane_total(part, stage):
        some = blocks(part, pl.ds(0, 1 << stage), ALL)
        return remote(
            some, some, plane_send.at[stage, part], plane_recv.at[stage, part], place.partner(stage)
        )

    def core_total(part):
        some = blocks(part, pl.ds(0, n_rows // 2), ALL)
        return remote(some, some, core_send.at[part], core_recv.at[part], place.sibling())

    def spread_plane(part, stage):
        if stage == 0:
            own(part).wait()
            far_total(part).wait_recv()
        else:
            plane_total(part, stage - 1).wait_recv()
        for group in held(stage):
            remote(
                blocks(part, group, ALL),
                blocks(part, group, ALL),
                plane_send.at[stage, part],
                plane_recv.at[stage, part],
                place.partner(stage),
            ).start()

    def spread_core(part):
        plane_total(part, place.digits - 1).wait_recv()
        for group in held(place.digits):
            remote(
                blocks(part, group, ALL),
                blocks(part, group, ALL),
                core_send.at[part],
                core_recv.at[part],
                place.sibling(),
            ).start()

    place.greet()
    n_parts = len(parts)
    for step in range(n_parts + place.digits + 1):
        if step < n_parts:
            spread_far(step)
        for stage in range(place.digits):
            if 0 <= step - 1 - stage < n_parts:
                spread_plane(step - 1 - stage, stage)
        if 0 <= step - 1 - place.digits < n_parts:
            spread_core(step - 1 - place.digits)
    for part in range(n_parts):
        core_total(part).wait_recv()
        far_total(part).wait_send()
        for stage in range(place.digits):
            plane_total(part, stage).wait_send()
        core_total(part).wait_send()


ALL = slice(None)


def gather(n_rows, n_mem, shards, cuts):
    parts = [(array, cut) for array, pieces in enumerate(cuts) for cut in pieces]
    n_parts, digits = len(parts), (n_rows // 2).bit_length() - 1
    dma = pltpu.SemaphoreType.DMA
    return pl.pallas_call(
        functools.partial(gather_kernel, n_rows, n_mem, parts, len(shards)),
        out_shape=[
            jax.ShapeDtypeStruct((n_rows, n_mem) + item.shape, item.dtype) for item in shards
        ],
        in_specs=[pl.BlockSpec(memory_space=pl.ANY)] * len(shards),
        out_specs=[pl.BlockSpec(memory_space=pl.ANY)] * len(shards),
        scratch_shapes=[
            dma((n_parts,)),
            dma((n_parts,)),
            dma((n_parts,)),
            dma((digits, n_parts)),
            dma((digits, n_parts)),
            dma((n_parts,)),
            dma((n_parts,)),
        ],
        compiler_params=pltpu.CompilerParams(
            collective_id=0, has_side_effects=True, vmem_limit_bytes=VMEM_LIMIT
        ),
        name="gather",
    )(*shards)


def reduce_kernel(n_rows, n_mem, shard, jobs, n_in, n_out, *refs):
    ins, outs, scratch = refs[:n_in], refs[n_in : n_in + n_out], list(refs[n_in + n_out :])
    place = Place(n_rows, n_mem)
    digits, lane, mem, half = place.digits, place.lane, place.mem, n_rows // 2
    core_send, core_recv = scratch[0], scratch[1]
    plane_send, plane_recv = scratch[2], scratch[3]
    far_send, far_recv = scratch[4], scratch[5]
    kinds = {}
    at = 6
    for kind in sorted({job[0] for job in jobs}):
        kinds[kind] = scratch[at : at + 4 + 2 * digits]
        at += 4 + 2 * digits
    slots, numbers = {}, {}
    for number, job in enumerate(jobs):
        index = numbers.get(job[0], 0)
        numbers[job[0]] = index + 1
        slots[number] = index
    before = {}
    for number, job in enumerate(jobs):
        older = [n for n in range(number) if jobs[n][0] == job[0] and slots[n] == slots[number] - 2]
        before[number] = older[0] if older else None

    wanted = [place.row]
    for stage in reversed(range(digits)):
        wanted = wanted + [place.turn(group, stage) for group in wanted]
    wanted = [group // 2 for group in wanted]

    def buffers(number):
        kind = kinds[jobs[number][0]]
        slot, index = slots[number] % 2, slots[number]
        return {
            "out": kind[0].at[slot],
            "lanes": kind[1].at[slot],
            "plane": [kind[2 + s].at[slot] for s in range(digits)],
            "core_in": kind[2 + digits].at[index],
            "plane_in": [kind[3 + digits + s].at[index] for s in range(digits)],
            "far_in": kind[3 + 2 * digits].at[index],
        }

    def core_copy(number):
        held = buffers(number)
        kind, left = jobs[number][0], jobs[number][1]
        source = held["out"]
        if kind == "small":
            source = ins[left].at[1 - lane]
        return remote(
            source, held["core_in"], core_send.at[number], core_recv.at[number], place.sibling()
        )

    def product_of(number, side, store):
        kind, left, right, first, _, _ = jobs[number]
        rows = ins[left].shape[1]
        group = rows // half
        if kind == "wide":
            width = 256

            def column_step(step, carry):
                columns = pl.ds(pl.multiple_of(step * width, width), width)
                source = pl.ds(pl.multiple_of(first + step * width, width), width)
                value = jnp.dot(
                    ins[left][side], ins[right][:, source], preferred_element_type=jnp.float32
                )
                for index in range(half):
                    store(index, columns, value[index * group : (index + 1) * group])
                return carry

            lax.fori_loop(0, D_BLOCK // width, column_step, 0)
        else:
            columns = pl.ds(first, right_width(kind))

            def group_step(step, carry):
                rows_here = pl.ds(pl.multiple_of(step * group, group), group)
                value = jnp.dot(
                    ins[left][side, rows_here],
                    ins[right][:, columns],
                    preferred_element_type=jnp.float32,
                )
                store(step, ALL, value)
                return carry

            lax.fori_loop(0, half, group_step, 0)

    def core_stage(number):
        if jobs[number][0] != "small":
            if before[number] is not None:
                core_copy(before[number]).wait_send()
            out = buffers(number)["out"]

            def store(index, columns, value):
                out[index, :, columns] = value.astype(out.dtype)

            product_of(number, 1 - lane, store)
        core_copy(number).start()

    def plane_copy(number, stage, which):
        held = buffers(number)
        count = 1 << (digits - 1 - stage)
        if stage == 0:
            source = held["lanes"].at[wanted[count + which]]
        else:
            source = held["plane"][stage - 1].at[count + which]
        return remote(
            source,
            held["plane_in"][stage].at[which],
            plane_send.at[stage, number],
            plane_recv.at[stage, number],
            place.partner(stage),
        )

    def plane_total(number, stage):
        some = buffers(number)["plane_in"][stage]
        return remote(
            some,
            some,
            plane_send.at[stage, number],
            plane_recv.at[stage, number],
            place.partner(stage),
        )

    def lane_stage(number):
        held = buffers(number)
        if before[number] is not None:
            plane_total(before[number], 0).wait_send()
        lanes, arrived = held["lanes"], held["core_in"]
        core_copy(number).wait_recv()
        if jobs[number][0] == "small":
            lanes[...] = ins[jobs[number][1]][lane] + arrived[...]
        else:

            def store(index, columns, value):
                total = value + arrived[index, :, columns].astype(jnp.float32)
                lanes[index, :, columns] = total.astype(lanes.dtype)

            product_of(number, lane, store)
        for which in range(1 << (digits - 1)):
            plane_copy(number, 0, which).start()

    def plane_stage(number, stage):
        held = buffers(number)
        count = 1 << (digits - 1 - stage)
        if stage < digits - 1 and before[number] is not None:
            plane_total(before[number], stage + 1).wait_send()
        if stage == digits - 1 and before[number] is not None:
            far_total(before[number]).wait_send()
        plane_total(number, stage).wait_recv()
        for which in range(count):
            if stage == 0:
                mine = held["lanes"][wanted[which]]
            else:
                mine = held["plane"][stage - 1][which]
            total = mine.astype(jnp.float32) + held["plane_in"][stage][which].astype(jnp.float32)
            held["plane"][stage][which] = total.astype(mine.dtype)
        if stage < digits - 1:
            for which in range(1 << (digits - 2 - stage)):
                plane_copy(number, stage + 1, which).start()
        else:
            for step in range(1, n_mem):
                far_copy(number, step).start()

    def rows_of(number, index):
        size = buffers(number)["far_in"].shape[1]
        return pl.ds(pl.multiple_of(index * size, size), size)

    def far_copy(number, step):
        held = buffers(number)
        return remote(
            held["plane"][digits - 1].at[0, rows_of(number, (mem + step) % n_mem)],
            held["far_in"].at[step - 1],
            far_send.at[number],
            far_recv.at[number],
            place.far(step),
        )

    def far_total(number):
        some = buffers(number)["far_in"]
        return remote(some, some, far_send.at[number], far_recv.at[number], place.far(1))

    def last_stage(number):
        held = buffers(number)
        far_total(number).wait_recv()
        total = held["plane"][digits - 1][0, rows_of(number, mem)].astype(jnp.float32)
        for step in range(n_mem - 1):
            total = total + held["far_in"][step].astype(jnp.float32)
        _, _, _, _, target, columns = jobs[number]
        outs[target][:, columns] = total

    place.greet()
    n_jobs = len(jobs)
    for step in range(n_jobs + 2 + digits):
        if step < n_jobs:
            core_stage(step)
        if 0 <= step - 1 < n_jobs:
            lane_stage(step - 1)
        for stage in range(digits):
            if 0 <= step - 2 - stage < n_jobs:
                plane_stage(step - 2 - stage, stage)
        if 0 <= step - 2 - digits < n_jobs:
            last_stage(step - 2 - digits)
    for number in range(n_jobs):
        last = not any(before[later] == number for later in range(n_jobs))
        if last or jobs[number][0] == "small":
            core_copy(number).wait_send()
        if last:
            for stage in range(digits):
                plane_total(number, stage).wait_send()
            far_total(number).wait_send()


def right_width(kind):
    return {"tall": 256}[kind]


D_BLOCK = 1024
VMEM_LIMIT = 60 * 1024 * 1024


def reduce_sums(n_rows, n_mem, shard, ins, jobs, outs):
    half, digits = n_rows // 2, (n_rows // 2).bit_length() - 1
    shapes = {
        "wide": (shard, D_BLOCK, jnp.bfloat16),
        "tall": (shard * D_BLOCK // 256, 256, jnp.bfloat16),
        "small": (8, 128, jnp.float32),
    }
    dma = pltpu.SemaphoreType.DMA
    n_jobs = len(jobs)
    scratch = [
        dma((n_jobs,)),
        dma((n_jobs,)),
        dma((digits, n_jobs)),
        dma((digits, n_jobs)),
        dma((n_jobs,)),
        dma((n_jobs,)),
    ]
    for kind in sorted({job[0] for job in jobs}):
        rows, columns, dtype = shapes[kind]
        number = sum(job[0] == kind for job in jobs)
        group = (n_mem * rows, columns)
        counts = [1 << (digits - 1 - stage) for stage in range(digits)]
        scratch += [pltpu.VMEM((2, half) + group, dtype), pltpu.VMEM((2, half) + group, dtype)]
        scratch += [pltpu.VMEM((2, count) + group, dtype) for count in counts]
        scratch += [pltpu.VMEM((number, half) + group, dtype)]
        scratch += [pltpu.VMEM((number, count) + group, dtype) for count in counts]
        scratch += [pltpu.VMEM((number, n_mem - 1, rows, columns), dtype)]
    return pl.pallas_call(
        functools.partial(reduce_kernel, n_rows, n_mem, shard, jobs, len(ins), len(outs)),
        out_shape=outs,
        in_specs=[pl.BlockSpec(memory_space=pltpu.VMEM)] * len(ins),
        out_specs=[pl.BlockSpec(memory_space=pltpu.VMEM)] * len(outs),
        scratch_shapes=scratch,
        compiler_params=pltpu.CompilerParams(
            collective_id=1, has_side_effects=True, vmem_limit_bytes=VMEM_LIMIT
        ),
        name="reduce_sums",
    )(*ins)


def by_lane(left, n_rows):
    tokens, features = left.shape
    group = features // n_rows
    turned = jnp.transpose(left).reshape(n_rows // 2, 2, group, tokens)
    return jnp.transpose(turned, (1, 0, 2, 3)).reshape(2, features // 2, tokens)


def local(
    n_rows,
    n_mem,
    tokens,
    memory,
    token_ids,
    memory_ids,
    out_grad,
    self_query,
    self_key,
    self_value,
    self_output,
    cross_query,
    cross_key,
    cross_value,
    cross_output,
    expand_weight,
    contract_weight,
    norm_gains,
    norm_shifts,
):
    fast = self_query.shape[0] % 16 == 0 and norm_gains.shape[1] <= 128
    square = (
        self_query,
        self_key,
        self_value,
        self_output,
        cross_query,
        cross_key,
        cross_value,
        cross_output,
    )
    shard, width = self_query.shape
    if fast:
        ff = expand_weight.shape[1]
        small = jnp.concatenate([norm_gains, norm_shifts], axis=0)
        small = jnp.pad(small, ((0, 16 - small.shape[0]), (0, 128 - small.shape[1])))
        whole = [(ALL, ALL)]
        columns = [(ALL, pl.ds(first, width)) for first in range(0, ff, width)]
        rows = [(pl.ds(first, shard), ALL) for first in range(0, contract_weight.shape[0], shard)]
        full = gather(
            n_rows,
            n_mem,
            [small, *square, expand_weight, contract_weight],
            [whole] * 9 + [columns, rows],
        )
        small = full[0][:, :, :, : norm_gains.shape[1]]
        small = jnp.transpose(small, (2, 0, 1, 3)).reshape(16, width)
        gain_rows = small[:3].astype(jnp.float32)
        shift_rows = small[3:6].astype(jnp.float32)
        full = [item.reshape(-1, item.shape[-1]) for item in full[1:]]
    else:
        full = [
            lax.all_gather(item, ("rows", "mem"), axis=0, tiled=True)
            for item in square + (expand_weight, contract_weight)
        ]
        gain_rows = lax.all_gather(norm_gains, ("rows", "mem"), axis=1, tiled=True)
        shift_rows = lax.all_gather(norm_shifts, ("rows", "mem"), axis=1, tiled=True)
        gain_rows = gain_rows.astype(jnp.float32)
        shift_rows = shift_rows.astype(jnp.float32)
    (
        self_attention_query,
        decoder_match_label,
        self_attention_value,
        self_attention_output,
        encoder_lookup_probe,
        key_cross,
        value_cross,
        cross_attention_output,
        up_projection,
        narrowing_matrix,
    ) = full
    rows_here = tokens.shape[0]
    member = lax.axis_index("mem")
    own_ids = lax.dynamic_slice_in_dim(token_ids, member * rows_here, rows_here, 0)
    positions = jnp.arange(tokens.shape[1], dtype=jnp.int32)
    self_allowed = (own_ids[:, :, None] == own_ids[:, None, :]) & (
        positions[:, None] <= positions[None, :]
    )[None]
    query = product(tokens, self_attention_query).astype(jnp.bfloat16)
    keys = product(tokens, decoder_match_label).astype(jnp.bfloat16)
    values = product(tokens, self_attention_value).astype(jnp.bfloat16)
    self_mixed, self_lse = row_map(local_forward, (query, keys, values, self_allowed))
    attention_result = self_mixed.astype(jnp.bfloat16)
    first, first_back = jax.vjp(
        layer_norm,
        ALPHA * tokens.astype(jnp.float32) + product(attention_result, self_attention_output),
        gain_rows[0],
        shift_rows[0],
    )
    first_reduced = first.astype(jnp.bfloat16)
    cross_queries = product(first_reduced, encoder_lookup_probe).astype(jnp.bfloat16)
    memory_rows = lax.all_to_all(memory, "mem", split_axis=0, concat_axis=1, tiled=True)
    row_ids = lax.dynamic_slice_in_dim(memory_ids, member * rows_here, rows_here, 0)
    cross_allowed = row_ids[:, :, None] == own_ids[:, None, :]
    cross_keys = product(memory_rows, key_cross).astype(jnp.bfloat16)
    cross_values = product(memory_rows, value_cross).astype(jnp.bfloat16)
    cross_mixed, cross_lse = row_map(
        local_forward, (cross_queries, cross_keys, cross_values, cross_allowed)
    )
    cross_attention_result = cross_mixed.astype(jnp.bfloat16)
    second, second_back = jax.vjp(
        layer_norm,
        ALPHA * first + product(cross_attention_result, cross_attention_output),
        gain_rows[1],
        shift_rows[1],
    )
    second_reduced = second.astype(jnp.bfloat16)
    hidden_value, gelu_back = jax.vjp(gelu_exact, product(second_reduced, up_projection))
    hidden_activation = hidden_value.astype(jnp.bfloat16)
    result, third_back = jax.vjp(
        layer_norm,
        ALPHA * second + product(hidden_activation, narrowing_matrix),
        gain_rows[2],
        shift_rows[2],
    )
    third_grad, gain_three, shift_three = third_back(out_grad.astype(jnp.float32))
    feedforward_gradient = third_grad.astype(jnp.bfloat16)
    (inner_grad,) = gelu_back(
        jnp.einsum(
            "hpu,ku->hpk",
            feedforward_gradient,
            narrowing_matrix,
            preferred_element_type=jnp.float32,
        )
    )
    inner_reduced = inner_grad.astype(jnp.bfloat16)
    second_total = ALPHA * third_grad + jnp.einsum(
        "iwm,fm->iwf", inner_reduced, up_projection, preferred_element_type=jnp.float32
    )
    second_grad, gain_two, shift_two = second_back(second_total)
    cross_branch_gradient = second_grad.astype(jnp.bfloat16)
    crossed_grad = jnp.einsum(
        "qwp,up->qwu",
        cross_branch_gradient,
        cross_attention_output,
        preferred_element_type=jnp.float32,
    ).astype(jnp.bfloat16)
    query_grads, key_grads, value_grads = row_map(
        local_backward,
        (cross_queries, cross_keys, cross_values, cross_allowed, cross_lse, crossed_grad),
    )
    key_low = key_grads.astype(jnp.bfloat16)
    value_low = value_grads.astype(jnp.bfloat16)
    row_grad = jnp.einsum(
        "sme,de->smd", key_low, key_cross, preferred_element_type=jnp.float32
    ) + jnp.einsum("sme,de->smd", value_low, value_cross, preferred_element_type=jnp.float32)
    memory_grad = lax.all_to_all(
        row_grad.astype(jnp.bfloat16), "mem", split_axis=1, concat_axis=0, tiled=True
    ).astype(row_grad.dtype)
    probe_lowered_precision = query_grads.astype(jnp.bfloat16)
    first_total = ALPHA * second_grad + jnp.einsum(
        "qwp,up->qwu",
        probe_lowered_precision,
        encoder_lookup_probe,
        preferred_element_type=jnp.float32,
    )
    first_grad, gain_one, shift_one = first_back(first_total)
    self_branch_gradient = first_grad.astype(jnp.bfloat16)
    attended_grad = jnp.einsum(
        "qwp,up->qwu",
        self_branch_gradient,
        self_attention_output,
        preferred_element_type=jnp.float32,
    ).astype(jnp.bfloat16)
    self_query_reduced, decoder_label_lowered, self_value_reduced = row_map(
        local_backward, (query, keys, values, self_allowed, self_lse, attended_grad)
    )
    self_query_reduced = self_query_reduced.astype(jnp.bfloat16)
    decoder_label_lowered = decoder_label_lowered.astype(jnp.bfloat16)
    self_value_reduced = self_value_reduced.astype(jnp.bfloat16)
    input_grad = (
        ALPHA * first_grad
        + jnp.einsum(
            "qwp,up->qwu",
            self_query_reduced,
            self_attention_query,
            preferred_element_type=jnp.float32,
        )
        + jnp.einsum(
            "qwp,up->qwu",
            decoder_label_lowered,
            decoder_match_label,
            preferred_element_type=jnp.float32,
        )
        + jnp.einsum(
            "qwp,up->qwu",
            self_value_reduced,
            self_attention_value,
            preferred_element_type=jnp.float32,
        )
    )
    pairs = [
        (tokens, self_query_reduced),
        (tokens, decoder_label_lowered),
        (tokens, self_value_reduced),
        (attention_result, self_branch_gradient),
        (first_reduced, probe_lowered_precision),
        (memory_rows, key_low),
        (memory_rows, value_low),
        (cross_attention_result, cross_branch_gradient),
        (second_reduced, inner_reduced),
        (hidden_activation, feedforward_gradient),
    ]
    small_sums = jnp.stack([gain_one, gain_two, gain_three, shift_one, shift_two, shift_three])
    if fast:
        lefts, rights, left_of, right_of = [], [], [], []
        seen = {}
        for left, right in pairs:
            if id(left) not in seen:
                seen[id(left)] = len(lefts)
                lefts.append(by_lane(left.reshape(-1, left.shape[-1]), n_rows))
            left_of.append(seen[id(left)])
            right_of.append(len(rights))
            rights.append(right.reshape(-1, right.shape[-1]))
        own = small_sums.shape[1] // (n_rows * n_mem)
        packed = small_sums.reshape(6, n_rows // 2, 2, n_mem, own)
        packed = jnp.transpose(packed, (2, 1, 3, 0, 4))
        packed = jnp.pad(packed, ((0, 0),) * 3 + ((0, 2), (0, 128 - own)))
        packed = packed.reshape(2, n_rows // 2, n_mem * 8, 128)
        ins = lefts + rights + [packed]
        base = len(lefts)
        jobs = [
            ("tall", left_of[9], base + right_of[9], first, 9, pl.ds(first, 256))
            for first in range(0, width, 256)
        ]
        jobs += [
            ("wide", left_of[8], base + right_of[8], first, 8, pl.ds(first, width))
            for first in range(0, ff, width)
        ]
        jobs += [
            ("wide", left_of[item], base + right_of[item], 0, item, ALL)
            for item in (7, 5, 6, 4, 3, 0, 1, 2)
        ]
        jobs += [("small", len(ins) - 1, None, None, 10, ALL)]
        outs = [jax.ShapeDtypeStruct((shard, width), jnp.float32)] * 8
        outs += [
            jax.ShapeDtypeStruct((shard, ff), jnp.float32),
            jax.ShapeDtypeStruct(contract_weight.shape, jnp.float32),
            jax.ShapeDtypeStruct((8, 128), jnp.float32),
        ]
        sums = list(reduce_sums(n_rows, n_mem, shard, ins, jobs, outs))
        small_own = sums[10][:6, :own]
    else:
        sums = [
            lax.psum_scatter(
                jnp.einsum("nhb,nhc->bc", left, right, preferred_element_type=jnp.float32),
                ("rows", "mem"),
                scatter_dimension=0,
                tiled=True,
            )
            for left, right in pairs
        ]
        small_own = lax.psum_scatter(
            small_sums, ("rows", "mem"), scatter_dimension=1, tiled=True
        )
    return (
        result,
        input_grad,
        memory_grad,
        sums[0],
        sums[1],
        sums[2],
        sums[3],
        sums[4],
        sums[5],
        sums[6],
        sums[7],
        sums[8],
        sums[9],
        small_own[:3],
        small_own[3:],
    )


def solution(mesh):
    in_specs = (
        P(("rows", "mem"), None, None),
        P("rows", "mem", None),
        P("rows", None),
        P("rows", None),
        P(("rows", "mem"), None, None),
        P(("rows", "mem"), None),
        P(("rows", "mem"), None),
        P(("rows", "mem"), None),
        P(("rows", "mem"), None),
        P(("rows", "mem"), None),
        P(("rows", "mem"), None),
        P(("rows", "mem"), None),
        P(("rows", "mem"), None),
        P(("rows", "mem"), None),
        P(("rows", "mem"), None),
        P(None, ("rows", "mem")),
        P(None, ("rows", "mem")),
    )
    out_specs = (
        P(("rows", "mem"), None, None),
        P(("rows", "mem"), None, None),
        P("rows", "mem", None),
        P(("rows", "mem"), None),
        P(("rows", "mem"), None),
        P(("rows", "mem"), None),
        P(("rows", "mem"), None),
        P(("rows", "mem"), None),
        P(("rows", "mem"), None),
        P(("rows", "mem"), None),
        P(("rows", "mem"), None),
        P(("rows", "mem"), None),
        P(("rows", "mem"), None),
        P(None, ("rows", "mem")),
        P(None, ("rows", "mem")),
    )
    layer = functools.partial(local, mesh.shape["rows"], mesh.shape["mem"])
    return jax.shard_map(layer, mesh=mesh, in_specs=in_specs, out_specs=out_specs, check_vma=False)
```

```python
import functools
import math

import jax
import jax.numpy as jnp
from jax import lax
from jax.experimental import pallas as pl
from jax.experimental.pallas import tpu as pltpu
from jax.sharding import PartitionSpec as P

MESH = pl.DeviceIdType.MESH

HEADS = 16
HEAD_DIM = 64


ALPHA = 4.16
EPS = 1e-05
SCALE = 0.125
NEG = -1e30


def layer_norm(hidden_activation, gain, shift):
    centre = hidden_activation - jnp.mean(hidden_activation, axis=-1, keepdims=True)
    spread = jnp.mean(centre * centre, axis=-1, keepdims=True)
    return centre * lax.rsqrt(spread + EPS) * gain + shift


def gelu_exact(value):
    return jax.nn.gelu(value, approximate=False)


def product(left, right):
    return jnp.dot(left, right, preferred_element_type=jnp.float32)


def split_heads(matrix):
    return matrix.reshape(matrix.shape[0], matrix.shape[1] // HEAD_DIM, HEAD_DIM)


def grouped(matrix):
    return jnp.moveaxis(matrix.reshape(matrix.shape[0], HEADS // 4, 4 * HEAD_DIM), 1, 0)


def ungrouped(stack):
    return jnp.moveaxis(stack, 0, 1).reshape(stack.shape[1], stack.shape[0] * stack.shape[2])


def row_map(function, items):
    return lax.map(lambda entry: function(*entry), items)


def score_block(query, keys, allowed):
    raw = jnp.einsum(
        "khe,qhe->hkq", split_heads(keys), split_heads(query), preferred_element_type=jnp.float32
    )
    return jnp.where(allowed[None], raw * SCALE, NEG)


def attend_probs(query, keys, allowed, lse):
    scores = score_block(query, keys, allowed)
    return jnp.where(allowed[None], jnp.exp(scores - lse[:, None, :]), 0.0)


def attend_forward(query, keys, values, allowed):
    scores = score_block(query, keys, allowed)
    top = jnp.max(scores, axis=1)
    weight = jnp.where(allowed[None], jnp.exp(scores - top[:, None, :]), 0.0)
    total = jnp.sum(weight, axis=1)
    probs = (weight / total[:, None, :]).astype(jnp.bfloat16)
    mixed = jnp.einsum(
        "hkq,khe->qhe", probs, split_heads(values), preferred_element_type=jnp.float32
    )
    return (mixed.reshape(query.shape), top + jnp.log(total))


def value_pull(grad, values):
    return jnp.einsum(
        "qhe,khe->hkq", split_heads(grad), split_heads(values), preferred_element_type=jnp.float32
    )


def score_grads(probs, pulled, inner):
    return (probs * (pulled - inner[:, None, :]) * SCALE).astype(jnp.bfloat16)


def query_from(score_grad, keys, shape):
    moved = jnp.einsum(
        "hkq,khe->qhe", score_grad, split_heads(keys), preferred_element_type=jnp.float32
    )
    return moved.reshape(shape)


def key_from(score_grad, query, shape):
    moved = jnp.einsum(
        "hkq,qhe->khe", score_grad, split_heads(query), preferred_element_type=jnp.float32
    )
    return moved.reshape(shape)


def value_from(probs, grad, values):
    moved = jnp.einsum(
        "hkq,qhe->khe",
        probs.astype(jnp.bfloat16),
        split_heads(grad),
        preferred_element_type=jnp.float32,
    )
    return moved.reshape(values.shape)


def local_forward(query, keys, values, allowed):

    def one_group(items):
        return attend_forward(items[0], items[1], items[2], allowed)

    mixed, lse = lax.map(one_group, (grouped(query), grouped(keys), grouped(values)))
    return (ungrouped(mixed), lse)


def local_backward(query, keys, values, allowed, lse, grad):

    def one_group(items):
        part_query, part_keys, part_values, part_lse, part_grad = items
        probs = attend_probs(part_query, part_keys, allowed, part_lse)
        pulled = value_pull(part_grad, part_values)
        inner = jnp.sum(probs * pulled, axis=1)
        score_grad = score_grads(probs, pulled, inner)
        return (
            query_from(score_grad, part_keys, part_query.shape),
            key_from(score_grad, part_query, part_keys.shape),
            value_from(probs, part_grad, part_values),
        )

    parts = lax.map(one_group, (grouped(query), grouped(keys), grouped(values), lse, grouped(grad)))
    return (ungrouped(parts[0]), ungrouped(parts[1]), ungrouped(parts[2]))


def plain(
    tokens,
    memory,
    token_ids,
    memory_ids,
    out_grad,
    self_query,
    self_key,
    self_value,
    self_output,
    cross_query,
    cross_key,
    cross_value,
    cross_output,
    expand_weight,
    contract_weight,
    norm_gains,
    norm_shifts,
):
    full = (
        lax.all_gather(self_query, ("rows", "mem"), axis=0, tiled=True),
        lax.all_gather(self_key, ("rows", "mem"), axis=0, tiled=True),
        lax.all_gather(self_value, ("rows", "mem"), axis=0, tiled=True),
        lax.all_gather(self_output, ("rows", "mem"), axis=0, tiled=True),
        lax.all_gather(cross_query, ("rows", "mem"), axis=0, tiled=True),
        lax.all_gather(cross_key, ("rows", "mem"), axis=0, tiled=True),
        lax.all_gather(cross_value, ("rows", "mem"), axis=0, tiled=True),
        lax.all_gather(cross_output, ("rows", "mem"), axis=0, tiled=True),
        lax.all_gather(expand_weight, ("rows", "mem"), axis=0, tiled=True),
        lax.all_gather(contract_weight, ("rows", "mem"), axis=0, tiled=True),
        lax.all_gather(jnp.transpose(norm_gains), ("rows", "mem"), axis=0, tiled=True),
        lax.all_gather(jnp.transpose(norm_shifts), ("rows", "mem"), axis=0, tiled=True),
    )
    (
        self_attention_query,
        decoder_match_label,
        self_attention_value,
        self_attention_output,
        encoder_lookup_probe,
        key_cross,
        value_cross,
        cross_attention_output,
        up_projection,
        narrowing_matrix,
        gain_cols,
        shift_cols,
    ) = full
    gain_rows = jnp.transpose(gain_cols).astype(jnp.float32)
    shift_rows = jnp.transpose(shift_cols).astype(jnp.float32)
    rows_here = tokens.shape[0]
    member = lax.axis_index("mem")
    own_ids = lax.dynamic_slice_in_dim(token_ids, member * rows_here, rows_here, 0)
    positions = jnp.arange(tokens.shape[1], dtype=jnp.int32)
    self_allowed = (own_ids[:, :, None] == own_ids[:, None, :]) & (
        positions[:, None] <= positions[None, :]
    )[None]
    query = product(tokens, self_attention_query).astype(jnp.bfloat16)
    keys = product(tokens, decoder_match_label).astype(jnp.bfloat16)
    values = product(tokens, self_attention_value).astype(jnp.bfloat16)
    self_mixed, self_lse = row_map(local_forward, (query, keys, values, self_allowed))
    attention_result = self_mixed.astype(jnp.bfloat16)
    first, first_back = jax.vjp(
        layer_norm,
        ALPHA * tokens.astype(jnp.float32) + product(attention_result, self_attention_output),
        gain_rows[0],
        shift_rows[0],
    )
    first_reduced = first.astype(jnp.bfloat16)
    cross_queries = product(first_reduced, encoder_lookup_probe).astype(jnp.bfloat16)
    memory_rows = lax.all_to_all(memory, "mem", split_axis=0, concat_axis=1, tiled=True)
    row_ids = lax.dynamic_slice_in_dim(memory_ids, member * rows_here, rows_here, 0)
    cross_allowed = row_ids[:, :, None] == own_ids[:, None, :]
    cross_keys = product(memory_rows, key_cross).astype(jnp.bfloat16)
    cross_values = product(memory_rows, value_cross).astype(jnp.bfloat16)
    cross_mixed, cross_lse = row_map(
        local_forward, (cross_queries, cross_keys, cross_values, cross_allowed)
    )
    cross_attention_result = cross_mixed.astype(jnp.bfloat16)
    second, second_back = jax.vjp(
        layer_norm,
        ALPHA * first + product(cross_attention_result, cross_attention_output),
        gain_rows[1],
        shift_rows[1],
    )
    second_reduced = second.astype(jnp.bfloat16)
    hidden_value, gelu_back = jax.vjp(gelu_exact, product(second_reduced, up_projection))
    hidden_activation = hidden_value.astype(jnp.bfloat16)
    result, third_back = jax.vjp(
        layer_norm,
        ALPHA * second + product(hidden_activation, narrowing_matrix),
        gain_rows[2],
        shift_rows[2],
    )
    third_grad, gain_three, shift_three = third_back(out_grad.astype(jnp.float32))
    feedforward_gradient = third_grad.astype(jnp.bfloat16)
    down_projection_gradient = jnp.einsum(
        "ehj,ehc->jc", hidden_activation, feedforward_gradient, preferred_element_type=jnp.float32
    )
    (inner_grad,) = gelu_back(
        jnp.einsum(
            "hpu,ku->hpk",
            feedforward_gradient,
            narrowing_matrix,
            preferred_element_type=jnp.float32,
        )
    )
    inner_reduced = inner_grad.astype(jnp.bfloat16)
    expand_grad = jnp.einsum(
        "iqg,iqe->ge", second_reduced, inner_reduced, preferred_element_type=jnp.float32
    )
    second_total = ALPHA * third_grad + jnp.einsum(
        "iwm,fm->iwf", inner_reduced, up_projection, preferred_element_type=jnp.float32
    )
    second_grad, gain_two, shift_two = second_back(second_total)
    cross_branch_gradient = second_grad.astype(jnp.bfloat16)
    output_cross_grad = jnp.einsum(
        "nhb,nhc->bc",
        cross_attention_result,
        cross_branch_gradient,
        preferred_element_type=jnp.float32,
    )
    crossed_grad = jnp.einsum(
        "qwp,up->qwu",
        cross_branch_gradient,
        cross_attention_output,
        preferred_element_type=jnp.float32,
    ).astype(jnp.bfloat16)
    query_grads, key_grads, value_grads = row_map(
        local_backward,
        (cross_queries, cross_keys, cross_values, cross_allowed, cross_lse, crossed_grad),
    )
    key_low = key_grads.astype(jnp.bfloat16)
    value_low = value_grads.astype(jnp.bfloat16)
    row_grad = jnp.einsum(
        "sme,de->smd", key_low, key_cross, preferred_element_type=jnp.float32
    ) + jnp.einsum("sme,de->smd", value_low, value_cross, preferred_element_type=jnp.float32)
    key_cross_grad = jnp.einsum(
        "smd,sme->de", memory_rows, key_low, preferred_element_type=jnp.float32
    )
    value_cross_grad = jnp.einsum(
        "smd,sme->de", memory_rows, value_low, preferred_element_type=jnp.float32
    )
    memory_grad = lax.all_to_all(
        row_grad.astype(jnp.bfloat16), "mem", split_axis=1, concat_axis=0, tiled=True
    ).astype(row_grad.dtype)
    probe_lowered_precision = query_grads.astype(jnp.bfloat16)
    query_cross_grad = jnp.einsum(
        "nhb,nhc->bc", first_reduced, probe_lowered_precision, preferred_element_type=jnp.float32
    )
    first_total = ALPHA * second_grad + jnp.einsum(
        "qwp,up->qwu",
        probe_lowered_precision,
        encoder_lookup_probe,
        preferred_element_type=jnp.float32,
    )
    first_grad, gain_one, shift_one = first_back(first_total)
    self_branch_gradient = first_grad.astype(jnp.bfloat16)
    output_self_grad = jnp.einsum(
        "nhb,nhc->bc", attention_result, self_branch_gradient, preferred_element_type=jnp.float32
    )
    attended_grad = jnp.einsum(
        "qwp,up->qwu",
        self_branch_gradient,
        self_attention_output,
        preferred_element_type=jnp.float32,
    ).astype(jnp.bfloat16)
    self_query_reduced, decoder_label_lowered, self_value_reduced = row_map(
        local_backward, (query, keys, values, self_allowed, self_lse, attended_grad)
    )
    self_query_reduced = self_query_reduced.astype(jnp.bfloat16)
    decoder_label_lowered = decoder_label_lowered.astype(jnp.bfloat16)
    self_value_reduced = self_value_reduced.astype(jnp.bfloat16)
    query_self_grad = jnp.einsum(
        "nhb,nhc->bc", tokens, self_query_reduced, preferred_element_type=jnp.float32
    )
    key_self_grad = jnp.einsum(
        "nhb,nhc->bc", tokens, decoder_label_lowered, preferred_element_type=jnp.float32
    )
    value_self_grad = jnp.einsum(
        "nhb,nhc->bc", tokens, self_value_reduced, preferred_element_type=jnp.float32
    )
    input_grad = (
        ALPHA * first_grad
        + jnp.einsum(
            "qwp,up->qwu",
            self_query_reduced,
            self_attention_query,
            preferred_element_type=jnp.float32,
        )
        + jnp.einsum(
            "qwp,up->qwu",
            decoder_label_lowered,
            decoder_match_label,
            preferred_element_type=jnp.float32,
        )
        + jnp.einsum(
            "qwp,up->qwu",
            self_value_reduced,
            self_attention_value,
            preferred_element_type=jnp.float32,
        )
    )
    gain_grad = jnp.stack([gain_one, gain_two, gain_three], axis=1)
    shift_grad = jnp.stack([shift_one, shift_two, shift_three], axis=1)
    sums = (
        lax.psum_scatter(query_self_grad, ("rows", "mem"), scatter_dimension=0, tiled=True),
        lax.psum_scatter(key_self_grad, ("rows", "mem"), scatter_dimension=0, tiled=True),
        lax.psum_scatter(value_self_grad, ("rows", "mem"), scatter_dimension=0, tiled=True),
        lax.psum_scatter(output_self_grad, ("rows", "mem"), scatter_dimension=0, tiled=True),
        lax.psum_scatter(query_cross_grad, ("rows", "mem"), scatter_dimension=0, tiled=True),
        lax.psum_scatter(key_cross_grad, ("rows", "mem"), scatter_dimension=0, tiled=True),
        lax.psum_scatter(value_cross_grad, ("rows", "mem"), scatter_dimension=0, tiled=True),
        lax.psum_scatter(output_cross_grad, ("rows", "mem"), scatter_dimension=0, tiled=True),
        lax.psum_scatter(expand_grad, ("rows", "mem"), scatter_dimension=0, tiled=True),
        lax.psum_scatter(
            down_projection_gradient, ("rows", "mem"), scatter_dimension=0, tiled=True
        ),
        lax.psum_scatter(gain_grad, ("rows", "mem"), scatter_dimension=0, tiled=True),
        lax.psum_scatter(shift_grad, ("rows", "mem"), scatter_dimension=0, tiled=True),
    )
    return (
        result,
        input_grad,
        memory_grad,
        sums[0],
        sums[1],
        sums[2],
        sums[3],
        sums[4],
        sums[5],
        sums[6],
        sums[7],
        sums[8],
        sums[9],
        jnp.transpose(sums[10]),
        jnp.transpose(sums[11]),
    )


ALL = slice(None)
TILE = 256
RING = 4
SLOTS = 3
VMEM_LIMIT = 61 * 1024 * 1024


def flip(index, unit):
    return index + unit * (1 - 2 * ((index // unit) % 2))


def span(index, size):
    return pl.ds(pl.multiple_of(index * size, size), size)


class Place:
    def __init__(self, n_rows, n_mem):
        self.n_rows, self.n_mem = n_rows, n_mem
        self.digits = (n_rows // 2).bit_length() - 1
        self.row = lax.axis_index("rows")
        self.mem = lax.axis_index("mem")
        self.lane = self.row % 2

    def turn(self, index, stage):
        rising, falling = 2 << stage, 2 << (self.digits - 1 - stage)
        return flip(index, rising) * (1 - self.lane) + flip(index, falling) * self.lane

    def sibling(self):
        return (flip(self.row, 1), self.mem)

    def partner(self, stage):
        return (self.turn(self.row, stage), self.mem)

    def far(self, step):
        return (self.row, (self.mem + step) % self.n_mem)

    def greet(self):
        barrier = pltpu.get_barrier_semaphore()
        others = [self.far(step) for step in range(1, self.n_mem)]
        others += [self.partner(stage) for stage in range(self.digits)]
        others += [self.sibling()]
        for other in others:
            pl.semaphore_signal(barrier, inc=1, device_id=other, device_id_type=MESH)
        pl.semaphore_wait(barrier, len(others))


def remote(source, target, send_sem, recv_sem, device):
    return pltpu.make_async_remote_copy(
        src_ref=source,
        dst_ref=target,
        send_sem=send_sem,
        recv_sem=recv_sem,
        device_id=device,
        device_id_type=MESH,
    )


class Gather:
    def __init__(self, place, parts, sems):
        self.place, self.parts = place, parts
        (
            self.own_sem,
            self.far_send,
            self.far_recv,
            self.plane_send,
            self.plane_recv,
            self.core_send,
            self.core_recv,
        ) = sems

    def rows(self, part, first, count):
        source, target, columns = self.parts[part]
        size = source.shape[0]
        return target.at[pl.ds(pl.multiple_of(first * size, size), count * size), columns]

    def group(self, part, group):
        return self.rows(part, group * self.place.n_mem, self.place.n_mem)

    def shard(self, part):
        source, _, columns = self.parts[part]
        return source.at[:, columns]

    def mine(self, part):
        return self.rows(part, self.place.row * self.place.n_mem + self.place.mem, 1)

    def own(self, part):
        return pltpu.make_async_copy(self.shard(part), self.mine(part), self.own_sem.at[part])

    def spread_far(self, part):
        self.own(part).start()
        for step in range(1, self.place.n_mem):
            remote(
                self.shard(part),
                self.mine(part),
                self.far_send.at[part],
                self.far_recv.at[part],
                self.place.far(step),
            ).start()

    def held(self, stage):
        groups = [self.place.row]
        for before in range(stage):
            groups = groups + [self.place.turn(group, before) for group in groups]
        return groups

    def far_total(self, part):
        some = self.rows(part, 0, self.place.n_mem - 1)
        return remote(some, some, self.far_send.at[part], self.far_recv.at[part], self.place.far(1))

    def plane_total(self, part, stage):
        some = self.rows(part, 0, self.place.n_mem << stage)
        return remote(
            some,
            some,
            self.plane_send.at[stage, part],
            self.plane_recv.at[stage, part],
            self.place.partner(stage),
        )

    def core_total(self, part):
        some = self.rows(part, 0, self.place.n_mem * self.place.n_rows // 2)
        return remote(
            some, some, self.core_send.at[part], self.core_recv.at[part], self.place.sibling()
        )

    def spread_plane(self, part, stage):
        if stage == 0:
            self.own(part).wait()
            self.far_total(part).wait_recv()
        else:
            self.plane_total(part, stage - 1).wait_recv()
        for group in self.held(stage):
            block = self.group(part, group)
            remote(
                block,
                block,
                self.plane_send.at[stage, part],
                self.plane_recv.at[stage, part],
                self.place.partner(stage),
            ).start()

    def spread_core(self, part):
        self.plane_total(part, self.place.digits - 1).wait_recv()
        for group in self.held(self.place.digits):
            block = self.group(part, group)
            remote(
                block,
                block,
                self.core_send.at[part],
                self.core_recv.at[part],
                self.place.sibling(),
            ).start()

    def step(self, number):
        digits, n_parts = self.place.digits, len(self.parts)
        if number < n_parts:
            self.spread_far(number)
        for stage in range(digits):
            if 0 <= number - 1 - stage < n_parts:
                self.spread_plane(number - 1 - stage, stage)
        if 0 <= number - 1 - digits < n_parts:
            self.spread_core(number - 1 - digits)

    def finish(self):
        for part in range(len(self.parts)):
            self.far_total(part).wait_send()
            for stage in range(self.place.digits):
                self.plane_total(part, stage).wait_send()
            self.core_total(part).wait_send()


class Reduce:
    def __init__(self, place, jobs, sems, wide, small):
        self.place, self.jobs, self.wide, self.small = place, jobs, wide, small
        (
            self.core_send,
            self.core_recv,
            self.plane_send,
            self.plane_recv,
            self.far_send,
            self.far_recv,
        ) = sems
        wanted = [place.row]
        for stage in reversed(range(place.digits)):
            wanted = wanted + [place.turn(group, stage) for group in wanted]
        self.wanted = [group // 2 for group in wanted]

    def is_small(self, number):
        return self.jobs[number][1] is None

    def before(self, number):
        return None if number < 2 or self.is_small(number) else number - 2

    def buffers(self, number):
        digits = self.place.digits
        refs = self.small if self.is_small(number) else self.wide
        send, ring = (0, 0) if self.is_small(number) else (number % 2, number % RING)
        return {
            "out": refs[0].at[send],
            "lanes": refs[1].at[send],
            "plane": [refs[2 + s].at[send] for s in range(digits)],
            "core_in": refs[2 + digits].at[ring],
            "plane_in": [refs[3 + digits + s].at[ring] for s in range(digits)],
            "far_in": refs[3 + 2 * digits].at[ring],
        }

    def core_copy(self, number):
        held = self.buffers(number)
        source = held["out"]
        if self.is_small(number):
            source = self.jobs[number][0].at[1 - self.place.lane]
        return remote(
            source,
            held["core_in"],
            self.core_send.at[number],
            self.core_recv.at[number],
            self.place.sibling(),
        )

    def product(self, number, side, store):
        left, right, first, _ = self.jobs[number]
        half = self.place.n_rows // 2
        rows = left.shape[1]
        group = rows // half
        width = min(TILE, self.wide[0].shape[-1])

        def column_step(step, carry):
            source = pl.ds(pl.multiple_of(first + step * width, width), width)
            value = jnp.dot(left[side], right[:, source], preferred_element_type=jnp.float32)
            for index in range(half):
                store(index, span(step, width), value[index * group : (index + 1) * group])
            return carry

        lax.fori_loop(0, self.wide[0].shape[-1] // width, column_step, 0)

    def core_stage(self, number):
        if not self.is_small(number):
            if self.before(number) is not None:
                self.core_copy(self.before(number)).wait_send()
            out = self.buffers(number)["out"]

            def store(index, columns, value):
                out[index, :, columns] = value.astype(out.dtype)

            self.product(number, 1 - self.place.lane, store)
        self.core_copy(number).start()

    def plane_copy(self, number, stage, which):
        held = self.buffers(number)
        count = 1 << (self.place.digits - 1 - stage)
        if stage == 0:
            source = held["lanes"].at[self.wanted[count + which]]
        else:
            source = held["plane"][stage - 1].at[count + which]
        return remote(
            source,
            held["plane_in"][stage].at[which],
            self.plane_send.at[stage, number],
            self.plane_recv.at[stage, number],
            self.place.partner(stage),
        )

    def plane_total(self, number, stage):
        some = self.buffers(number)["plane_in"][stage]
        return remote(
            some,
            some,
            self.plane_send.at[stage, number],
            self.plane_recv.at[stage, number],
            self.place.partner(stage),
        )

    def lane_stage(self, number):
        held = self.buffers(number)
        if self.before(number) is not None:
            self.plane_total(self.before(number), 0).wait_send()
        lanes, arrived = held["lanes"], held["core_in"]
        self.core_copy(number).wait_recv()
        if self.is_small(number):
            lanes[...] = self.jobs[number][0][self.place.lane] + arrived[...]
        else:

            def store(index, columns, value):
                total = value + arrived[index, :, columns].astype(jnp.float32)
                lanes[index, :, columns] = total.astype(lanes.dtype)

            self.product(number, self.place.lane, store)
        for which in range(1 << (self.place.digits - 1)):
            self.plane_copy(number, 0, which).start()

    def plane_stage(self, number, stage):
        held, digits = self.buffers(number), self.place.digits
        count = 1 << (digits - 1 - stage)
        if self.before(number) is not None:
            if stage < digits - 1:
                self.plane_total(self.before(number), stage + 1).wait_send()
            else:
                self.far_total(self.before(number)).wait_send()
        self.plane_total(number, stage).wait_recv()
        for which in range(count):
            if stage == 0:
                mine = held["lanes"].at[self.wanted[which]]
            else:
                mine = held["plane"][stage - 1].at[which]
            arrived, total = held["plane_in"][stage].at[which], held["plane"][stage].at[which]
            size = mine.shape[0]
            block = min(32, size)

            def add(step, carry, mine=mine, arrived=arrived, total=total, block=block):
                rows = span(step, block)
                value = mine[rows].astype(jnp.float32) + arrived[rows].astype(jnp.float32)
                total[rows] = value.astype(total.dtype)
                return carry

            lax.fori_loop(0, size // block, add, 0)
        if stage < digits - 1:
            for which in range(1 << (digits - 2 - stage)):
                self.plane_copy(number, stage + 1, which).start()
        else:
            for step in range(1, self.place.n_mem):
                self.far_copy(number, step).start()

    def piece(self, number, member):
        whole = self.buffers(number)["plane"][self.place.digits - 1].at[0]
        size = self.buffers(number)["far_in"].shape[1]
        return whole if self.is_small(number) else whole.at[span(member, size)]

    def far_copy(self, number, step):
        place = self.place
        return remote(
            self.piece(number, (place.mem + step) % place.n_mem),
            self.buffers(number)["far_in"].at[step - 1],
            self.far_send.at[number],
            self.far_recv.at[number],
            place.far(step),
        )

    def far_total(self, number):
        some = self.buffers(number)["far_in"]
        return remote(
            some, some, self.far_send.at[number], self.far_recv.at[number], self.place.far(1)
        )

    def last_stage(self, number):
        self.far_total(number).wait_recv()
        arrived = self.buffers(number)["far_in"]
        total = self.piece(number, self.place.mem)[...].astype(jnp.float32)
        for step in range(self.place.n_mem - 1):
            total = total + arrived[step].astype(jnp.float32)
        self.jobs[number][3][...] = total

    def step(self, number):
        digits, n_jobs = self.place.digits, len(self.jobs)
        if number < n_jobs:
            self.core_stage(number)
        if 0 <= number - 1 < n_jobs:
            self.lane_stage(number - 1)
        for stage in range(digits):
            if 0 <= number - 2 - stage < n_jobs:
                self.plane_stage(number - 2 - stage, stage)
        if 0 <= number - 2 - digits < n_jobs:
            self.last_stage(number - 2 - digits)

    def finish(self):
        n_jobs = len(self.jobs)
        waited = [self.before(number) for number in range(n_jobs)]
        for number in range(n_jobs):
            if number not in waited:
                self.core_copy(number).wait_send()
                for stage in range(self.place.digits):
                    self.plane_total(number, stage).wait_send()
                self.far_total(number).wait_send()


NORMAL = (((1,), (0,)), ((), ()))
TURNED = (((1,), (1,)), ((), ()))
LEFT_TURNED = (((0,), (0,)), ((), ()))


def dot(left, right, dims=NORMAL):
    return lax.dot_general(left, right, dims, preferred_element_type=jnp.float32)


def times(left, weight, store):
    width = min(TILE, weight.shape[1])

    def column_step(step, carry):
        columns = span(step, width)
        store(columns, dot(left[...], weight[:, columns]))
        return carry

    lax.fori_loop(0, weight.shape[1] // width, column_step, 0)


def times_turned(left, weight, store):
    width = min(TILE, weight.shape[0])

    def column_step(step, carry):
        columns = span(step, width)
        store(columns, dot(left[...], weight[columns, :], TURNED))
        return carry

    lax.fori_loop(0, weight.shape[0] // width, column_step, 0)


def into(target):
    def store(columns, value):
        target[:, columns] = value.astype(target.dtype)

    return store


ROWS = 32


def by_rows(count, step):
    def body(index, carry):
        step(span(index, ROWS))
        return carry

    lax.fori_loop(0, count // ROWS, body, 0)


def norm_forward(total, gains, index, unit, scale, use):
    gain, shift = gains[index : index + 1, :], gains[index + 3 : index + 4, :]

    def step(rows):
        value = total[rows, :]
        centre = value - jnp.mean(value, axis=-1, keepdims=True)
        spread = jnp.mean(centre * centre, axis=-1, keepdims=True)
        root = lax.rsqrt(spread + EPS)
        scaled = centre * root
        unit[rows, :] = scaled
        scale[rows, :] = root
        use(rows, scaled * gain + shift)

    by_rows(total.shape[0], step)


def norm_backward(grad, gains, index, unit, scale, target, target_low, small):
    gain = gains[index : index + 1, :]
    width = unit.shape[1]

    def body(block, sums):
        rows = span(block, ROWS)
        incoming, scaled = grad(rows), unit[rows, :]
        scaled_grad = incoming * gain
        first = jnp.mean(scaled_grad, axis=-1, keepdims=True)
        second = jnp.mean(scaled_grad * scaled, axis=-1, keepdims=True)
        value = scale[rows, :] * (scaled_grad - first - scaled * second)
        target[rows, :] = value
        target_low[rows, :] = value.astype(target_low.dtype)
        of_gain = jnp.sum((incoming * scaled).reshape(ROWS // 8, 8, width), axis=0)
        of_shift = jnp.sum(incoming.reshape(ROWS // 8, 8, width), axis=0)
        return (sums[0] + of_gain, sums[1] + of_shift)

    zero = jnp.zeros((8, width), jnp.float32)
    sums = lax.fori_loop(0, unit.shape[0] // ROWS, body, (zero, zero))
    for offset, partial in ((index, sums[0]), (index + 3, sums[1])):
        line = jnp.sum(partial, axis=0, keepdims=True)
        for group in range(2 * small.shape[1]):
            small[group % 2, group // 2, offset : offset + 1, :] = line[
                :, group * 128 : (group + 1) * 128
            ]


def lane_masks(dtype):
    low = lax.broadcasted_iota(jnp.int32, (1, 2 * HEAD_DIM), 1) < HEAD_DIM
    first = jnp.where(low, 1.0, 0.0)
    return first.astype(dtype), (1.0 - first).astype(dtype)


def attention_forward(query, keys, values, bias, mixed, lse):
    masks = lane_masks(query.dtype)
    keep = lane_masks(jnp.float32)

    def pair_step(pair, carry):
        lanes = span(pair, 2 * HEAD_DIM)
        two_query, two_keys, two_values = query[:, lanes], keys[:, lanes], values[:, lanes]
        total = None
        for head in range(2):
            scores = dot(two_keys, two_query * masks[head], TURNED) * SCALE + bias[...]
            top = jnp.max(scores, axis=0, keepdims=True)
            weight = jnp.exp(scores - top)
            norm = jnp.sum(weight, axis=0, keepdims=True)
            probs = (weight * (1.0 / norm)).astype(query.dtype)
            part = dot(probs, two_values, LEFT_TURNED) * keep[head]
            total = part if total is None else total + part
            lse[pair, head : head + 1, :] = top + jnp.log(norm)
        mixed[:, lanes] = total.astype(mixed.dtype)
        return carry

    lax.fori_loop(0, lse.shape[0], pair_step, 0)


def attention_backward(query, keys, values, bias, lse, grad, query_grad, key_grad, value_grad):
    masks = lane_masks(query.dtype)
    keep = lane_masks(jnp.float32)

    def pair_step(pair, carry):
        lanes = span(pair, 2 * HEAD_DIM)
        two_query, two_keys, two_values = query[:, lanes], keys[:, lanes], values[:, lanes]
        two_grad = grad[:, lanes]
        sums = [None, None, None]
        for head in range(2):
            scores = dot(two_keys, two_query * masks[head], TURNED) * SCALE + bias[...]
            probs = jnp.exp(scores - lse[pair, head : head + 1, :])
            pulled = dot(two_values, two_grad * masks[head], TURNED)
            inner = jnp.sum(probs * pulled, axis=0, keepdims=True)
            slope = (probs * (pulled - inner) * SCALE).astype(query.dtype)
            parts = (
                dot(slope, two_keys, LEFT_TURNED),
                dot(slope, two_query),
                dot(probs.astype(query.dtype), two_grad),
            )
            for index, part in enumerate(parts):
                part = part * keep[head]
                sums[index] = part if sums[index] is None else sums[index] + part
        query_grad[:, lanes] = sums[0].astype(query_grad.dtype)
        key_grad[:, lanes] = sums[1].astype(key_grad.dtype)
        value_grad[:, lanes] = sums[2].astype(value_grad.dtype)
        return carry

    lax.fori_loop(0, lse.shape[0], pair_step, 0)


def turn_blocks(left, eye, store):
    width = eye.shape[0]
    for block in range(left.shape[1] // width):
        columns = pl.ds(block * width, width)
        store(block, dot(eye[...], left[:, columns], TURNED).astype(left.dtype))


def turn_by_lane(left, eye, target):
    group = eye.shape[0] // 2

    def store(block, value):
        target[0, pl.ds(block * group, group), :] = value[:group]
        target[1, pl.ds(block * group, group), :] = value[group:]

    turn_blocks(left, eye, store)


SQUARES = 8


def layer_kernel(names, sizes, *refs):
    n_rows, n_mem, width, ff, tokens_here, mem_tokens, shard = sizes
    ref = dict(zip(names, refs))
    place = Place(n_rows, n_mem)
    many = ff // width
    own_ff = ff // (n_rows * n_mem)
    (
        at_query,
        at_key,
        at_value,
        at_output,
        at_cross_query,
        at_cross_key,
        at_cross_value,
        at_cross_output,
    ) = range(SQUARES)
    square = [ref[f"square{index}"] for index in range(SQUARES)]
    full = [ref[f"full{index}"] for index in range(SQUARES)]
    expand, contract = ref["expand_full"], ref["contract_full"]
    tokens, gains = ref["tokens"], ref["gains"]

    parts = [(ref["small"], ref["small_full"], ALL)]
    order = [
        at_query,
        at_key,
        at_value,
        at_output,
        at_cross_key,
        at_cross_value,
        at_cross_query,
        at_cross_output,
    ]
    parts += [(square[index], full[index], ALL) for index in order]
    parts += [(ref["expand"], expand, pl.ds(j * width, width)) for j in range(many)]
    narrow = width // many
    parts += [(ref["contract"], contract, pl.ds(j * narrow, narrow)) for j in range(many)]
    gather = Gather(place, parts, [ref[f"gather_sem{i}"] for i in range(7)])

    slots, slot_sem = ref["slots"], ref["slot_sem"]
    count = [0]

    def load(pieces):
        number = count[0]
        count[0] += 1
        slot = slots.at[number % SLOTS]
        for source, columns in pieces:
            pltpu.make_async_copy(source, slot.at[:, columns], slot_sem.at[number % SLOTS]).start()
        return number

    def ready(number):
        slot = slots.at[number % SLOTS]
        pltpu.make_async_copy(slot, slot, slot_sem.at[number % SLOTS]).wait()
        return slot

    def expand_block(j):
        return [(expand.at[:, pl.ds(j * width, width)], ALL)]

    def contract_columns(j):
        return [
            (
                contract.at[pl.ds(i * width, width), pl.ds(j * narrow, narrow)],
                pl.ds(i * narrow, narrow),
            )
            for i in range(many)
        ]

    def contract_rows(j):
        return [(contract.at[pl.ds(j * width, width), :], ALL)]

    mem_block = mem_tokens // n_mem
    memory, mem_rows = ref["memory"], ref["mem_rows"]

    def memory_own():
        return pltpu.make_async_copy(
            memory.at[place.mem], mem_rows.at[span(place.mem, mem_block)], ref["mem_sem"].at[0]
        )

    def memory_total():
        some = mem_rows.at[pl.ds(0, (n_mem - 1) * mem_block)]
        return remote(some, some, ref["mem_sem"].at[1], ref["mem_sem"].at[2], place.far(1))

    place.greet()
    gather.step(0)
    gather.step(1)
    memory_own().start()
    for step in range(1, n_mem):
        remote(
            memory.at[(place.mem + step) % n_mem],
            mem_rows.at[span(place.mem, mem_block)],
            ref["mem_sem"].at[1],
            ref["mem_sem"].at[2],
            place.far(step),
        ).start()

    own_row, own_column, mem_column = ref["ids_row"], ref["ids_column"], ref["mem_ids"]
    self_bias, cross_bias, eye = ref["self_bias"], ref["cross_bias"], ref["eye"]
    key_place = lax.broadcasted_iota(jnp.int32, self_bias.shape, 0)
    query_place = lax.broadcasted_iota(jnp.int32, self_bias.shape, 1)
    same = (own_column[...] == own_row[...]) & (key_place <= query_place)
    self_bias[...] = jnp.where(same, 0.0, NEG)
    cross_bias[...] = jnp.where(mem_column[...] == own_row[...], 0.0, NEG)
    eye_row = lax.broadcasted_iota(jnp.int32, eye.shape, 0)
    eye_column = lax.broadcasted_iota(jnp.int32, eye.shape, 1)
    eye[...] = jnp.where(eye_row == eye_column, 1.0, 0.0).astype(eye.dtype)
    turned = {name: ref["turned"].at[i] for i, name in enumerate(TURNED_NAMES)}
    turn_by_lane(tokens, eye, turned["tokens"])

    accumulated, other = ref["accumulated"], ref["other"]
    hidden, slope, hidden_turned = ref["hidden"], ref["slope"], ref["hidden_turned"]

    def small_piece():
        blocks = ref["small_full"]
        for group in range(n_rows):
            total = None
            for member in range(n_mem):
                first = (group * n_mem + member) * 16
                value = blocks[first : first + 16, :].astype(jnp.float32)
                total = value if total is None else total + value
            gains[:, group * 128 : (group + 1) * 128] = total[:8]

    def query_piece(slot):
        times(tokens, slot, into(ref["query"]))

    def key_piece(slot):
        times(tokens, slot, into(ref["keys"]))

    def value_piece(slot):
        times(tokens, slot, into(ref["values"]))
        attention_forward(
            ref["query"], ref["keys"], ref["values"], self_bias, ref["attended"], ref["self_lse"]
        )

    def output_piece(slot):
        def store(columns, value):
            accumulated[:, columns] = ALPHA * tokens[:, columns].astype(jnp.float32) + value

        times(ref["attended"], slot, store)

        def use(rows, value):
            ref["first_low"][rows, :] = value.astype(jnp.bfloat16)
            other[rows, :] = value

        norm_forward(accumulated, gains, 0, ref["unit1"], ref["scale1"], use)
        turn_by_lane(ref["attended"], eye, turned["attended"])

    def cross_key_piece(slot):
        memory_own().wait()
        memory_total().wait_recv()
        times(mem_rows, slot, into(ref["cross_keys"]))
        turn_by_lane(mem_rows, eye, turned["memory"])

    def cross_value_piece(slot):
        times(mem_rows, slot, into(ref["cross_values"]))
        turn_by_lane(ref["first_low"], eye, turned["first"])

    def cross_query_piece(slot):
        times(ref["first_low"], slot, into(ref["cross_query"]))
        attention_forward(
            ref["cross_query"],
            ref["cross_keys"],
            ref["cross_values"],
            cross_bias,
            ref["crossed"],
            ref["cross_lse"],
        )

    def cross_output_piece(slot):
        def store(columns, value):
            accumulated[:, columns] = ALPHA * other[:, columns] + value

        times(ref["crossed"], slot, store)

        def use(rows, value):
            ref["second_low"][rows, :] = value.astype(jnp.bfloat16)
            other[rows, :] = value

        norm_forward(accumulated, gains, 1, ref["unit2"], ref["scale2"], use)
        turn_by_lane(ref["crossed"], eye, turned["crossed"])

    def expand_piece(j, slot):
        def store(columns, value):
            there = pl.ds(pl.multiple_of(j * width + columns.start, TILE), columns.size)
            bell = 0.5 * (1.0 + lax.erf(value * math.sqrt(0.5)))
            density = jnp.exp(value * value * -0.5) * (1.0 / math.sqrt(2.0 * math.pi))
            hidden[:, there] = (value * bell).astype(hidden.dtype)
            slope[:, there] = (bell + value * density).astype(slope.dtype)

        times(ref["second_low"], slot, store)

        def keep(block, value):
            for index in range(value.shape[0] // shard):
                first = j * width + block * value.shape[0] + index * shard
                device, job = first // own_ff, first % own_ff // shard
                group, member = device // n_mem, device % n_mem
                at = group // 2 * n_mem * shard + member * shard
                hidden_turned[job, group % 2, at : at + shard, :] = value[
                    index * shard : (index + 1) * shard
                ]

        turn_blocks(hidden.at[:, pl.ds(j * width, width)], eye, keep)

    def contract_piece(j, slot):
        total = None
        for i in range(many):
            value = dot(
                hidden[:, i * width : (i + 1) * width], slot[:, i * narrow : (i + 1) * narrow]
            )
            total = value if total is None else total + value
        columns = pl.ds(j * narrow, narrow)
        accumulated[:, columns] = ALPHA * other[:, columns] + total

    pieces = [
        query_piece,
        key_piece,
        value_piece,
        output_piece,
        cross_key_piece,
        cross_value_piece,
        cross_query_piece,
        cross_output_piece,
    ]
    sources = [[(full[index], ALL)] for index in order]
    for j in range(many):
        pieces.append(functools.partial(expand_piece, j))
        sources.append(expand_block(j))
    for j in range(many):
        pieces.append(functools.partial(contract_piece, j))
        sources.append(contract_columns(j))

    n_parts = len(parts)
    lag = place.digits + 2
    waiting = None
    for step in range(2, n_parts + lag + 1):
        if step < n_parts + place.digits + 1:
            gather.step(step)
        part = step - lag
        coming = None
        if 0 <= part < n_parts:
            gather.core_total(part).wait_recv()
            if part > 0:
                coming = (part - 1, load(sources[part - 1]))
        if part == 0:
            small_piece()
        if waiting is not None:
            pieces[waiting[0]](ready(waiting[1]))
        waiting = coming

    backward_sources = [contract_rows(j) for j in range(many)]
    backward_sources += [expand_block(j) for j in range(many)]
    backward_sources += [
        [(full[index], ALL)]
        for index in (
            at_cross_output,
            at_cross_query,
            at_output,
            at_cross_key,
            at_cross_value,
            at_query,
            at_key,
            at_value,
        )
    ]
    loads = [load(backward_sources[0]), load(backward_sources[1])]
    used = [0]

    def next_slot():
        slot = ready(loads[used[0]])
        used[0] += 1
        if len(loads) < len(backward_sources):
            loads.append(load(backward_sources[len(loads)]))
        return slot

    low = {name: ref["low"].at[i] for i, name in enumerate(LOW_NAMES)}
    small_sums = ref["small_sums"]
    small_sums[...] = jnp.zeros_like(small_sums)

    def use_result(rows, value):
        ref["result"][rows, :] = value

    norm_forward(accumulated, gains, 2, ref["unit3"], ref["scale3"], use_result)

    def grad_of(array):
        def grad(rows):
            return array[rows, :].astype(jnp.float32)

        return grad

    norm_backward(
        grad_of(ref["out_grad"]),
        gains,
        2,
        ref["unit3"],
        ref["scale3"],
        accumulated,
        low["third"],
        small_sums,
    )

    def inner_piece(j):
        slot = next_slot()

        def store(columns, value):
            there = pl.ds(pl.multiple_of(j * width + columns.start, TILE), columns.size)
            slope[:, there] = (value * slope[:, there].astype(jnp.float32)).astype(slope.dtype)

        times_turned(low["third"], slot, store)

    def second_piece(j):
        slot = next_slot()

        def store(columns, value):
            if j == 0:
                other[:, columns] = ALPHA * accumulated[:, columns] + value
            else:
                other[:, columns] = other[:, columns] + value

        times_turned(slope.at[:, pl.ds(j * width, width)], slot, store)

    def second_norm_piece():
        norm_backward(
            grad_of(other),
            gains,
            1,
            ref["unit2"],
            ref["scale2"],
            accumulated,
            low["second"],
            small_sums,
        )

    def cross_piece():
        times_turned(low["second"], next_slot(), into(low["branch"]))
        attention_backward(
            ref["cross_query"],
            ref["cross_keys"],
            ref["cross_values"],
            cross_bias,
            ref["cross_lse"],
            low["branch"],
            low["cross_query"],
            low["cross_key"],
            low["cross_value"],
        )

    def first_piece():
        def store(columns, value):
            other[:, columns] = ALPHA * accumulated[:, columns] + value

        times_turned(low["cross_query"], next_slot(), store)
        norm_backward(
            grad_of(other),
            gains,
            0,
            ref["unit1"],
            ref["scale1"],
            accumulated,
            low["first"],
            small_sums,
        )

    def self_piece():
        times_turned(low["first"], next_slot(), into(low["branch"]))
        attention_backward(
            ref["query"],
            ref["keys"],
            ref["values"],
            self_bias,
            ref["self_lse"],
            low["branch"],
            low["query"],
            low["key"],
            low["value"],
        )

    mem_out, mem_in = ref["mem_out"], ref["mem_in"]

    def grad_own():
        return pltpu.make_async_copy(
            mem_out.at[span(place.mem, mem_block)], mem_in.at[place.mem], ref["mem_sem"].at[3]
        )

    def grad_total():
        some = mem_in.at[pl.ds(0, n_mem - 1)]
        return remote(some, some, ref["mem_sem"].at[4], ref["mem_sem"].at[5], place.far(1))

    def memory_key_piece():
        times_turned(low["cross_key"], next_slot(), into(other))

    def memory_value_piece():
        def store(columns, value):
            mem_out[:, columns] = (other[:, columns] + value).astype(mem_out.dtype)

        times_turned(low["cross_value"], next_slot(), store)
        grad_own().start()
        for step in range(1, n_mem):
            remote(
                mem_out.at[span((place.mem + step) % n_mem, mem_block)],
                mem_in.at[place.mem],
                ref["mem_sem"].at[4],
                ref["mem_sem"].at[5],
                place.far(step),
            ).start()

    def input_piece(name):
        target = ref["input_grad"]

        def store(columns, value):
            if name == "query":
                target[:, columns] = ALPHA * accumulated[:, columns] + value
            else:
                target[:, columns] = target[:, columns] + value

        times_turned(low[name], next_slot(), store)

    def memory_end_piece():
        grad_own().wait()
        grad_total().wait_recv()
        for member in range(n_mem):
            ref["memory_grad"][member] = mem_in[member].astype(jnp.float32)

    jobs = [
        (
            hidden_turned.at[j],
            low["third"],
            0,
            ref["contract_grad"].at[pl.ds(j * shard, shard), :],
        )
        for j in range(many)
    ]
    jobs += [
        (turned["second"], slope, j * width, ref["expand_grad"].at[:, pl.ds(j * width, width)])
        for j in range(many)
    ]
    grads = [ref[f"grad{index}"] for index in range(SQUARES)]
    jobs += [
        (turned["crossed"], low["second"], 0, grads[at_cross_output]),
        (turned["memory"], low["cross_key"], 0, grads[at_cross_key]),
        (turned["memory"], low["cross_value"], 0, grads[at_cross_value]),
        (turned["first"], low["cross_query"], 0, grads[at_cross_query]),
        (turned["attended"], low["first"], 0, grads[at_output]),
        (turned["tokens"], low["query"], 0, grads[at_query]),
        (turned["tokens"], low["key"], 0, grads[at_key]),
        (turned["tokens"], low["value"], 0, grads[at_value]),
        (small_sums, None, 0, ref["small_grad"]),
    ]
    wide = [ref[f"wide{i}"] for i in range(4 + 2 * place.digits)]
    little = [ref[f"little{i}"] for i in range(4 + 2 * place.digits)]
    reduce = Reduce(place, jobs, [ref[f"reduce_sem{i}"] for i in range(6)], wide, little)

    work = [[functools.partial(inner_piece, j)] for j in range(many)]
    work[0].append(functools.partial(turn_by_lane, ref["second_low"], eye, turned["second"]))
    work += [[functools.partial(second_piece, j)] for j in range(many)]
    work[-1].append(second_norm_piece)
    work += [
        [cross_piece],
        [first_piece],
        [self_piece],
        [memory_key_piece],
        [memory_value_piece],
        [functools.partial(input_piece, "query")],
        [functools.partial(input_piece, "key")],
        [functools.partial(input_piece, "value")],
        [memory_end_piece],
    ]
    n_jobs = len(jobs)
    for step in range(n_jobs + 2 + place.digits):
        reduce.step(step)
        if step < len(work):
            for piece in work[step]:
                piece()
    gather.finish()
    reduce.finish()
    memory_total().wait_send()
    grad_total().wait_send()


TURNED_NAMES = ("tokens", "attended", "first", "memory", "crossed", "second")
LOW_NAMES = (
    "third",
    "second",
    "first",
    "branch",
    "cross_query",
    "cross_key",
    "cross_value",
    "query",
    "key",
    "value",
)


def fused(n_rows, n_mem, tokens, memory, ids, mem_ids, out_grad, small, squares, expand, contract):
    tokens_here, width = tokens.shape
    ff = expand.shape[1]
    shard = squares[0].shape[0]
    mem_tokens = memory.shape[0] * memory.shape[1]
    digits, half, many = (n_rows // 2).bit_length() - 1, n_rows // 2, ff // width
    pairs = width // (2 * HEAD_DIM)
    low, high = jnp.bfloat16, jnp.float32
    n_parts, n_jobs = 1 + SQUARES + 2 * many, 1 + SQUARES + 2 * many
    dma, vmem = pltpu.SemaphoreType.DMA, pltpu.VMEM
    anywhere, near = pl.BlockSpec(memory_space=pl.ANY), pl.BlockSpec(memory_space=pltpu.VMEM)

    ins = {"tokens": (tokens, near), "out_grad": (out_grad, near)}
    ins["ids_row"] = (ids.reshape(1, -1), near)
    ins["ids_column"] = (ids.reshape(-1, 1), near)
    ins["mem_ids"] = (mem_ids.reshape(-1, 1), near)
    ins["memory"] = (memory, anywhere)
    ins["small"] = (small, anywhere)
    for index, item in enumerate(squares):
        ins[f"square{index}"] = (item, anywhere)
    ins["expand"] = (expand, anywhere)
    ins["contract"] = (contract, anywhere)

    def out(shape, dtype, spec):
        return (jax.ShapeDtypeStruct(shape, dtype), spec)

    outs = {"result": out((tokens_here, width), high, near)}
    outs["input_grad"] = out((tokens_here, width), high, near)
    outs["memory_grad"] = out(memory.shape, high, near)
    for index, item in enumerate(squares):
        outs[f"grad{index}"] = out(item.shape, high, near)
    outs["expand_grad"] = out(expand.shape, high, near)
    outs["contract_grad"] = out(contract.shape, high, near)
    outs["small_grad"] = out((8, 128), high, near)
    n_kept = len(outs)
    for index in range(SQUARES):
        outs[f"full{index}"] = out((width, width), low, anywhere)
    outs["expand_full"] = out((width, ff), low, anywhere)
    outs["contract_full"] = out((ff, width), low, anywhere)

    scratch = {}
    scratch["small_full"] = vmem((n_rows * n_mem * 16, 128), low)
    scratch["slots"] = vmem((SLOTS, width, width), low)
    scratch["slot_sem"] = dma((SLOTS,))
    scratch["mem_sem"] = dma((6,))
    for index, shape in enumerate(((), (), (), (digits,), (digits,), (), ())):
        scratch[f"gather_sem{index}"] = dma(shape + (n_parts,))
    for index, shape in enumerate(((), (), (digits,), (digits,), (), ())):
        scratch[f"reduce_sem{index}"] = dma(shape + (n_jobs,))
    scratch["gains"] = vmem((8, width), high)
    for name in ("query", "keys", "values", "attended", "first_low", "second_low"):
        scratch[name] = vmem((tokens_here, width), low)
    for name in ("cross_query", "crossed"):
        scratch[name] = vmem((tokens_here, width), low)
    for name in ("cross_keys", "cross_values", "mem_rows", "mem_out"):
        scratch[name] = vmem((mem_tokens, width), low)
    scratch["mem_in"] = vmem(memory.shape, low)
    for name in ("unit1", "unit2", "unit3", "accumulated", "other"):
        scratch[name] = vmem((tokens_here, width), high)
    for name in ("scale1", "scale2", "scale3"):
        scratch[name] = vmem((tokens_here, 1), high)
    scratch["self_bias"] = vmem((tokens_here, tokens_here), high)
    scratch["cross_bias"] = vmem((mem_tokens, tokens_here), high)
    scratch["self_lse"] = vmem((pairs, 2, tokens_here), high)
    scratch["cross_lse"] = vmem((pairs, 2, tokens_here), high)
    scratch["eye"] = vmem((TILE, TILE), low)
    scratch["hidden"] = vmem((tokens_here, ff), low)
    scratch["slope"] = vmem((tokens_here, ff), low)
    scratch["hidden_turned"] = vmem((many, 2, width // 2, tokens_here), low)
    scratch["turned"] = vmem((len(TURNED_NAMES), 2, width // 2, tokens_here), low)
    scratch["low"] = vmem((len(LOW_NAMES), tokens_here, width), low)
    scratch["small_sums"] = vmem((2, half, 8, 128), high)
    counts = [1 << (digits - 1 - stage) for stage in range(digits)]
    for kind, sends, ring, group, dtype, piece in (
        ("wide", 2, RING, (n_mem * shard, width), low, (shard, width)),
        ("little", 1, 1, (8, 128), high, (8, 128)),
    ):
        shapes = [(sends, half) + group, (sends, half) + group]
        if kind == "little":
            shapes[0] = (1, 1, 8, 128)
        shapes += [(sends, count) + group for count in counts]
        shapes += [(ring, half) + group]
        shapes += [(ring, count) + group for count in counts]
        shapes += [(ring, n_mem - 1) + piece]
        for index, shape in enumerate(shapes):
            scratch[f"{kind}{index}"] = vmem(shape, dtype)

    sizes = (n_rows, n_mem, width, ff, tokens_here, mem_tokens, shard)
    names = list(ins) + list(outs) + list(scratch)
    values = pl.pallas_call(
        functools.partial(layer_kernel, names, sizes),
        out_shape=[shape for shape, _ in outs.values()],
        in_specs=[spec for _, spec in ins.values()],
        out_specs=[spec for _, spec in outs.values()],
        scratch_shapes=list(scratch.values()),
        compiler_params=pltpu.CompilerParams(
            collective_id=0, has_side_effects=True, vmem_limit_bytes=VMEM_LIMIT
        ),
        name="layer",
    )(*[value for value, _ in ins.values()])
    return values[:n_kept]


def local(n_rows, n_mem, *args):
    (
        tokens,
        memory,
        token_ids,
        memory_ids,
        out_grad,
        self_query,
        self_key,
        self_value,
        self_output,
        cross_query,
        cross_key,
        cross_value,
        cross_output,
        expand_weight,
        contract_weight,
        norm_gains,
        norm_shifts,
    ) = args
    shard, width = self_query.shape
    suits = width == 128 * n_rows and shard % 16 == 0 and tokens.shape[0] == 1
    if not suits or n_rows < 4 or n_rows & (n_rows - 1) or n_mem < 2:
        return plain(*args)
    member = lax.axis_index("mem")
    ids = lax.dynamic_slice_in_dim(token_ids, member, 1, 0)
    mem_ids = lax.dynamic_slice_in_dim(memory_ids, member, 1, 0)
    small = jnp.concatenate([norm_gains, norm_shifts], axis=0)
    lanes = jnp.arange(128, dtype=jnp.int32) // shard == member
    small = jnp.where(lanes[None], jnp.tile(small, (1, 128 // shard)), 0)
    small = jnp.pad(small.astype(jnp.bfloat16), ((0, 10), (0, 0)))
    squares = (
        self_query,
        self_key,
        self_value,
        self_output,
        cross_query,
        cross_key,
        cross_value,
        cross_output,
    )
    values = fused(
        n_rows,
        n_mem,
        tokens[0],
        memory,
        ids,
        mem_ids,
        out_grad[0],
        small,
        squares,
        expand_weight,
        contract_weight,
    )
    own = lax.dynamic_slice_in_dim(values[-1], member * shard, shard, 1)
    return (values[0][None], values[1][None], *values[2:-1], own[:3], own[3:6])


def solution(mesh):
    in_specs = (
        P(("rows", "mem"), None, None),
        P("rows", "mem", None),
        P("rows", None),
        P("rows", None),
        P(("rows", "mem"), None, None),
        P(("rows", "mem"), None),
        P(("rows", "mem"), None),
        P(("rows", "mem"), None),
        P(("rows", "mem"), None),
        P(("rows", "mem"), None),
        P(("rows", "mem"), None),
        P(("rows", "mem"), None),
        P(("rows", "mem"), None),
        P(("rows", "mem"), None),
        P(("rows", "mem"), None),
        P(None, ("rows", "mem")),
        P(None, ("rows", "mem")),
    )
    out_specs = (
        P(("rows", "mem"), None, None),
        P(("rows", "mem"), None, None),
        P("rows", "mem", None),
        P(("rows", "mem"), None),
        P(("rows", "mem"), None),
        P(("rows", "mem"), None),
        P(("rows", "mem"), None),
        P(("rows", "mem"), None),
        P(("rows", "mem"), None),
        P(("rows", "mem"), None),
        P(("rows", "mem"), None),
        P(("rows", "mem"), None),
        P(("rows", "mem"), None),
        P(None, ("rows", "mem")),
        P(None, ("rows", "mem")),
    )
    layer = functools.partial(local, mesh.shape["rows"], mesh.shape["mem"])
    return jax.shard_map(layer, mesh=mesh, in_specs=in_specs, out_specs=out_specs, check_vma=False)
```

```python
import functools
import math
from types import SimpleNamespace

import jax
import jax.numpy as jnp
from jax import lax
from jax.experimental import pallas as pl
from jax.experimental.pallas import tpu as pltpu
from jax.sharding import PartitionSpec as P

MESH = pl.DeviceIdType.MESH

HEADS = 16
HEAD_DIM = 64


ALPHA = 4.16
EPS = 1e-05
SCALE = 0.125
NEG = -1e30


def layer_norm(hidden_activation, gain, shift):
    centre = hidden_activation - jnp.mean(hidden_activation, axis=-1, keepdims=True)
    spread = jnp.mean(centre * centre, axis=-1, keepdims=True)
    return centre * lax.rsqrt(spread + EPS) * gain + shift


def gelu_exact(value):
    return jax.nn.gelu(value, approximate=False)


def product(left, right):
    return jnp.dot(left, right, preferred_element_type=jnp.float32)


def split_heads(matrix):
    return matrix.reshape(matrix.shape[0], matrix.shape[1] // HEAD_DIM, HEAD_DIM)


def grouped(matrix):
    return jnp.moveaxis(matrix.reshape(matrix.shape[0], HEADS // 4, 4 * HEAD_DIM), 1, 0)


def ungrouped(stack):
    return jnp.moveaxis(stack, 0, 1).reshape(stack.shape[1], stack.shape[0] * stack.shape[2])


def row_map(function, items):
    return lax.map(lambda entry: function(*entry), items)


def score_block(query, keys, allowed):
    raw = jnp.einsum(
        "khe,qhe->hkq", split_heads(keys), split_heads(query), preferred_element_type=jnp.float32
    )
    return jnp.where(allowed[None], raw * SCALE, NEG)


def attend_probs(query, keys, allowed, lse):
    scores = score_block(query, keys, allowed)
    return jnp.where(allowed[None], jnp.exp(scores - lse[:, None, :]), 0.0)


def attend_forward(query, keys, values, allowed):
    scores = score_block(query, keys, allowed)
    top = jnp.max(scores, axis=1)
    weight = jnp.where(allowed[None], jnp.exp(scores - top[:, None, :]), 0.0)
    total = jnp.sum(weight, axis=1)
    probs = (weight / total[:, None, :]).astype(jnp.bfloat16)
    mixed = jnp.einsum(
        "hkq,khe->qhe", probs, split_heads(values), preferred_element_type=jnp.float32
    )
    return (mixed.reshape(query.shape), top + jnp.log(total))


def value_pull(grad, values):
    return jnp.einsum(
        "qhe,khe->hkq", split_heads(grad), split_heads(values), preferred_element_type=jnp.float32
    )


def score_grads(probs, pulled, inner):
    return (probs * (pulled - inner[:, None, :]) * SCALE).astype(jnp.bfloat16)


def query_from(score_grad, keys, shape):
    moved = jnp.einsum(
        "hkq,khe->qhe", score_grad, split_heads(keys), preferred_element_type=jnp.float32
    )
    return moved.reshape(shape)


def key_from(score_grad, query, shape):
    moved = jnp.einsum(
        "hkq,qhe->khe", score_grad, split_heads(query), preferred_element_type=jnp.float32
    )
    return moved.reshape(shape)


def value_from(probs, grad, values):
    moved = jnp.einsum(
        "hkq,qhe->khe",
        probs.astype(jnp.bfloat16),
        split_heads(grad),
        preferred_element_type=jnp.float32,
    )
    return moved.reshape(values.shape)


def local_forward(query, keys, values, allowed):

    def one_group(items):
        return attend_forward(items[0], items[1], items[2], allowed)

    mixed, lse = lax.map(one_group, (grouped(query), grouped(keys), grouped(values)))
    return (ungrouped(mixed), lse)


def local_backward(query, keys, values, allowed, lse, grad):

    def one_group(items):
        part_query, part_keys, part_values, part_lse, part_grad = items
        probs = attend_probs(part_query, part_keys, allowed, part_lse)
        pulled = value_pull(part_grad, part_values)
        inner = jnp.sum(probs * pulled, axis=1)
        score_grad = score_grads(probs, pulled, inner)
        return (
            query_from(score_grad, part_keys, part_query.shape),
            key_from(score_grad, part_query, part_keys.shape),
            value_from(probs, part_grad, part_values),
        )

    parts = lax.map(one_group, (grouped(query), grouped(keys), grouped(values), lse, grouped(grad)))
    return (ungrouped(parts[0]), ungrouped(parts[1]), ungrouped(parts[2]))


def plain(
    tokens,
    memory,
    token_ids,
    memory_ids,
    out_grad,
    self_query,
    self_key,
    self_value,
    self_output,
    cross_query,
    cross_key,
    cross_value,
    cross_output,
    expand_weight,
    contract_weight,
    norm_gains,
    norm_shifts,
):
    full = (
        lax.all_gather(self_query, ("rows", "mem"), axis=0, tiled=True),
        lax.all_gather(self_key, ("rows", "mem"), axis=0, tiled=True),
        lax.all_gather(self_value, ("rows", "mem"), axis=0, tiled=True),
        lax.all_gather(self_output, ("rows", "mem"), axis=0, tiled=True),
        lax.all_gather(cross_query, ("rows", "mem"), axis=0, tiled=True),
        lax.all_gather(cross_key, ("rows", "mem"), axis=0, tiled=True),
        lax.all_gather(cross_value, ("rows", "mem"), axis=0, tiled=True),
        lax.all_gather(cross_output, ("rows", "mem"), axis=0, tiled=True),
        lax.all_gather(expand_weight, ("rows", "mem"), axis=0, tiled=True),
        lax.all_gather(contract_weight, ("rows", "mem"), axis=0, tiled=True),
        lax.all_gather(jnp.transpose(norm_gains), ("rows", "mem"), axis=0, tiled=True),
        lax.all_gather(jnp.transpose(norm_shifts), ("rows", "mem"), axis=0, tiled=True),
    )
    (
        self_attention_query,
        decoder_match_label,
        self_attention_value,
        self_attention_output,
        encoder_lookup_probe,
        key_cross,
        value_cross,
        cross_attention_output,
        up_projection,
        narrowing_matrix,
        gain_cols,
        shift_cols,
    ) = full
    gain_rows = jnp.transpose(gain_cols).astype(jnp.float32)
    shift_rows = jnp.transpose(shift_cols).astype(jnp.float32)
    rows_here = tokens.shape[0]
    member = lax.axis_index("mem")
    own_ids = lax.dynamic_slice_in_dim(token_ids, member * rows_here, rows_here, 0)
    positions = jnp.arange(tokens.shape[1], dtype=jnp.int32)
    self_allowed = (own_ids[:, :, None] == own_ids[:, None, :]) & (
        positions[:, None] <= positions[None, :]
    )[None]
    query = product(tokens, self_attention_query).astype(jnp.bfloat16)
    keys = product(tokens, decoder_match_label).astype(jnp.bfloat16)
    values = product(tokens, self_attention_value).astype(jnp.bfloat16)
    self_mixed, self_lse = row_map(local_forward, (query, keys, values, self_allowed))
    attention_result = self_mixed.astype(jnp.bfloat16)
    first, first_back = jax.vjp(
        layer_norm,
        ALPHA * tokens.astype(jnp.float32) + product(attention_result, self_attention_output),
        gain_rows[0],
        shift_rows[0],
    )
    first_reduced = first.astype(jnp.bfloat16)
    cross_queries = product(first_reduced, encoder_lookup_probe).astype(jnp.bfloat16)
    memory_rows = lax.all_to_all(memory, "mem", split_axis=0, concat_axis=1, tiled=True)
    row_ids = lax.dynamic_slice_in_dim(memory_ids, member * rows_here, rows_here, 0)
    cross_allowed = row_ids[:, :, None] == own_ids[:, None, :]
    cross_keys = product(memory_rows, key_cross).astype(jnp.bfloat16)
    cross_values = product(memory_rows, value_cross).astype(jnp.bfloat16)
    cross_mixed, cross_lse = row_map(
        local_forward, (cross_queries, cross_keys, cross_values, cross_allowed)
    )
    cross_attention_result = cross_mixed.astype(jnp.bfloat16)
    second, second_back = jax.vjp(
        layer_norm,
        ALPHA * first + product(cross_attention_result, cross_attention_output),
        gain_rows[1],
        shift_rows[1],
    )
    second_reduced = second.astype(jnp.bfloat16)
    hidden_value, gelu_back = jax.vjp(gelu_exact, product(second_reduced, up_projection))
    hidden_activation = hidden_value.astype(jnp.bfloat16)
    result, third_back = jax.vjp(
        layer_norm,
        ALPHA * second + product(hidden_activation, narrowing_matrix),
        gain_rows[2],
        shift_rows[2],
    )
    third_grad, gain_three, shift_three = third_back(out_grad.astype(jnp.float32))
    feedforward_gradient = third_grad.astype(jnp.bfloat16)
    down_projection_gradient = jnp.einsum(
        "ehj,ehc->jc", hidden_activation, feedforward_gradient, preferred_element_type=jnp.float32
    )
    (inner_grad,) = gelu_back(
        jnp.einsum(
            "hpu,ku->hpk",
            feedforward_gradient,
            narrowing_matrix,
            preferred_element_type=jnp.float32,
        )
    )
    inner_reduced = inner_grad.astype(jnp.bfloat16)
    expand_grad = jnp.einsum(
        "iqg,iqe->ge", second_reduced, inner_reduced, preferred_element_type=jnp.float32
    )
    second_total = ALPHA * third_grad + jnp.einsum(
        "iwm,fm->iwf", inner_reduced, up_projection, preferred_element_type=jnp.float32
    )
    second_grad, gain_two, shift_two = second_back(second_total)
    cross_branch_gradient = second_grad.astype(jnp.bfloat16)
    output_cross_grad = jnp.einsum(
        "nhb,nhc->bc",
        cross_attention_result,
        cross_branch_gradient,
        preferred_element_type=jnp.float32,
    )
    crossed_grad = jnp.einsum(
        "qwp,up->qwu",
        cross_branch_gradient,
        cross_attention_output,
        preferred_element_type=jnp.float32,
    ).astype(jnp.bfloat16)
    query_grads, key_grads, value_grads = row_map(
        local_backward,
        (cross_queries, cross_keys, cross_values, cross_allowed, cross_lse, crossed_grad),
    )
    key_low = key_grads.astype(jnp.bfloat16)
    value_low = value_grads.astype(jnp.bfloat16)
    row_grad = jnp.einsum(
        "sme,de->smd", key_low, key_cross, preferred_element_type=jnp.float32
    ) + jnp.einsum("sme,de->smd", value_low, value_cross, preferred_element_type=jnp.float32)
    key_cross_grad = jnp.einsum(
        "smd,sme->de", memory_rows, key_low, preferred_element_type=jnp.float32
    )
    value_cross_grad = jnp.einsum(
        "smd,sme->de", memory_rows, value_low, preferred_element_type=jnp.float32
    )
    memory_grad = lax.all_to_all(
        row_grad.astype(jnp.bfloat16), "mem", split_axis=1, concat_axis=0, tiled=True
    ).astype(row_grad.dtype)
    probe_lowered_precision = query_grads.astype(jnp.bfloat16)
    query_cross_grad = jnp.einsum(
        "nhb,nhc->bc", first_reduced, probe_lowered_precision, preferred_element_type=jnp.float32
    )
    first_total = ALPHA * second_grad + jnp.einsum(
        "qwp,up->qwu",
        probe_lowered_precision,
        encoder_lookup_probe,
        preferred_element_type=jnp.float32,
    )
    first_grad, gain_one, shift_one = first_back(first_total)
    self_branch_gradient = first_grad.astype(jnp.bfloat16)
    output_self_grad = jnp.einsum(
        "nhb,nhc->bc", attention_result, self_branch_gradient, preferred_element_type=jnp.float32
    )
    attended_grad = jnp.einsum(
        "qwp,up->qwu",
        self_branch_gradient,
        self_attention_output,
        preferred_element_type=jnp.float32,
    ).astype(jnp.bfloat16)
    self_query_reduced, decoder_label_lowered, self_value_reduced = row_map(
        local_backward, (query, keys, values, self_allowed, self_lse, attended_grad)
    )
    self_query_reduced = self_query_reduced.astype(jnp.bfloat16)
    decoder_label_lowered = decoder_label_lowered.astype(jnp.bfloat16)
    self_value_reduced = self_value_reduced.astype(jnp.bfloat16)
    query_self_grad = jnp.einsum(
        "nhb,nhc->bc", tokens, self_query_reduced, preferred_element_type=jnp.float32
    )
    key_self_grad = jnp.einsum(
        "nhb,nhc->bc", tokens, decoder_label_lowered, preferred_element_type=jnp.float32
    )
    value_self_grad = jnp.einsum(
        "nhb,nhc->bc", tokens, self_value_reduced, preferred_element_type=jnp.float32
    )
    input_grad = (
        ALPHA * first_grad
        + jnp.einsum(
            "qwp,up->qwu",
            self_query_reduced,
            self_attention_query,
            preferred_element_type=jnp.float32,
        )
        + jnp.einsum(
            "qwp,up->qwu",
            decoder_label_lowered,
            decoder_match_label,
            preferred_element_type=jnp.float32,
        )
        + jnp.einsum(
            "qwp,up->qwu",
            self_value_reduced,
            self_attention_value,
            preferred_element_type=jnp.float32,
        )
    )
    gain_grad = jnp.stack([gain_one, gain_two, gain_three], axis=1)
    shift_grad = jnp.stack([shift_one, shift_two, shift_three], axis=1)
    sums = (
        lax.psum_scatter(query_self_grad, ("rows", "mem"), scatter_dimension=0, tiled=True),
        lax.psum_scatter(key_self_grad, ("rows", "mem"), scatter_dimension=0, tiled=True),
        lax.psum_scatter(value_self_grad, ("rows", "mem"), scatter_dimension=0, tiled=True),
        lax.psum_scatter(output_self_grad, ("rows", "mem"), scatter_dimension=0, tiled=True),
        lax.psum_scatter(query_cross_grad, ("rows", "mem"), scatter_dimension=0, tiled=True),
        lax.psum_scatter(key_cross_grad, ("rows", "mem"), scatter_dimension=0, tiled=True),
        lax.psum_scatter(value_cross_grad, ("rows", "mem"), scatter_dimension=0, tiled=True),
        lax.psum_scatter(output_cross_grad, ("rows", "mem"), scatter_dimension=0, tiled=True),
        lax.psum_scatter(expand_grad, ("rows", "mem"), scatter_dimension=0, tiled=True),
        lax.psum_scatter(
            down_projection_gradient, ("rows", "mem"), scatter_dimension=0, tiled=True
        ),
        lax.psum_scatter(gain_grad, ("rows", "mem"), scatter_dimension=0, tiled=True),
        lax.psum_scatter(shift_grad, ("rows", "mem"), scatter_dimension=0, tiled=True),
    )
    return (
        result,
        input_grad,
        memory_grad,
        sums[0],
        sums[1],
        sums[2],
        sums[3],
        sums[4],
        sums[5],
        sums[6],
        sums[7],
        sums[8],
        sums[9],
        jnp.transpose(sums[10]),
        jnp.transpose(sums[11]),
    )


ALL = slice(None)
TILE = 256
SLOTS = 3
VMEM_LIMIT = 61 * 1024 * 1024


def flip(index, unit):
    return index + unit * (1 - 2 * ((index // unit) % 2))


def span(index, size):
    return pl.ds(pl.multiple_of(index * size, size), size)


class Place:
    def __init__(self, n_rows, n_mem):
        self.n_rows, self.n_mem = n_rows, n_mem
        self.digits = (n_rows // 2).bit_length() - 1
        self.row = lax.axis_index("rows")
        self.mem = lax.axis_index("mem")
        self.lane = self.row % 2

    def turn(self, index, stage):
        rising, falling = 2 << stage, 2 << (self.digits - 1 - stage)
        return flip(index, rising) * (1 - self.lane) + flip(index, falling) * self.lane

    def sibling(self):
        return (flip(self.row, 1), self.mem)

    def partner(self, stage):
        return (self.turn(self.row, stage), self.mem)

    def far(self, step):
        return (self.row, (self.mem + step) % self.n_mem)

    def greet(self):
        barrier = pltpu.get_barrier_semaphore()
        others = [self.far(step) for step in range(1, self.n_mem)]
        others += [self.partner(stage) for stage in range(self.digits)]
        others += [self.sibling()]
        for other in others:
            pl.semaphore_signal(barrier, inc=1, device_id=other, device_id_type=MESH)
        pl.semaphore_wait(barrier, len(others))


def remote(source, target, send_sem, recv_sem, device):
    return pltpu.make_async_remote_copy(
        src_ref=source,
        dst_ref=target,
        send_sem=send_sem,
        recv_sem=recv_sem,
        device_id=device,
        device_id_type=MESH,
    )


class Gather:
    def __init__(self, place, parts, sems):
        self.place, self.parts = place, parts
        (
            self.own_sem,
            self.far_send,
            self.far_recv,
            self.plane_send,
            self.plane_recv,
            self.core_send,
            self.core_recv,
            self.line_send,
            self.line_recv,
        ) = sems

    def near_first(self, part):
        return self.parts[part][3]

    def rows(self, part, first, count):
        source, target, columns, _ = self.parts[part]
        size = source.shape[0]
        return target.at[pl.ds(pl.multiple_of(first * size, size), count * size), columns]

    def group(self, part, group):
        return self.rows(part, group * self.place.n_mem, self.place.n_mem)

    def one(self, part, group, member):
        return self.rows(part, group * self.place.n_mem + member, 1)

    def shard(self, part):
        source, _, columns, _ = self.parts[part]
        return source.at[:, columns]

    def mine(self, part):
        return self.one(part, self.place.row, self.place.mem)

    def own(self, part):
        return pltpu.make_async_copy(self.shard(part), self.mine(part), self.own_sem.at[part])

    def held(self, stage):
        groups = [self.place.row]
        for before in range(stage):
            groups = groups + [self.place.turn(group, before) for group in groups]
        return groups

    def far_total(self, part):
        some = self.rows(part, 0, self.place.n_mem - 1)
        return remote(some, some, self.far_send.at[part], self.far_recv.at[part], self.place.far(1))

    def plane_total(self, part, stage):
        shards = 1 if self.near_first(part) else self.place.n_mem
        some = self.rows(part, 0, shards << stage)
        return remote(
            some,
            some,
            self.plane_send.at[stage, part],
            self.plane_recv.at[stage, part],
            self.place.partner(stage),
        )

    def core_total(self, part):
        some = self.rows(part, 0, self.place.n_mem * self.place.n_rows // 2)
        return remote(
            some, some, self.core_send.at[part], self.core_recv.at[part], self.place.sibling()
        )

    def line_total(self, part, step, side):
        some = self.rows(part, 0, self.place.n_rows // 2)
        at = 2 * step + side
        return remote(
            some, some, self.line_send.at[at, part], self.line_recv.at[at, part], self.place.far(1)
        )

    def set_out(self, part):
        self.own(part).start()
        if self.near_first(part):
            remote(
                self.shard(part),
                self.mine(part),
                self.plane_send.at[0, part],
                self.plane_recv.at[0, part],
                self.place.partner(0),
            ).start()
            return
        for step in range(1, self.place.n_mem):
            remote(
                self.shard(part),
                self.mine(part),
                self.far_send.at[part],
                self.far_recv.at[part],
                self.place.far(step),
            ).start()

    def spread_plane(self, part, stage):
        place = self.place
        if stage == 0:
            self.own(part).wait()
            self.far_total(part).wait_recv()
        else:
            if stage == 1 and self.near_first(part):
                self.own(part).wait()
            self.plane_total(part, stage - 1).wait_recv()
        for group in self.held(stage):
            if self.near_first(part):
                block = self.one(part, group, place.mem)
            else:
                block = self.group(part, group)
            remote(
                block,
                block,
                self.plane_send.at[stage, part],
                self.plane_recv.at[stage, part],
                place.partner(stage),
            ).start()

    def sides(self, step):
        mem, n_mem = self.place.mem, self.place.n_mem
        return (
            ((mem - step >= 0) & (mem + 1 < n_mem), mem - step, 1, mem - 1 - step >= 0),
            ((mem + step < n_mem) & (mem >= 1), mem + step, n_mem - 1, mem + 1 + step < n_mem),
        )

    def line_arrived(self, part, step):
        for side, (_, _, _, receives) in enumerate(self.sides(step)):

            @pl.when(receives)
            def _(side=side):
                self.line_total(part, step, side).wait_recv()

    def spread_line(self, part, step):
        place = self.place
        if step == 0:
            if place.digits == 1:
                self.own(part).wait()
            self.plane_total(part, place.digits - 1).wait_recv()
        else:
            self.line_arrived(part, step - 1)
        for side, (sends, member, towards, _) in enumerate(self.sides(step)):
            member = (member + place.n_mem) % place.n_mem

            @pl.when(sends)
            def _(side=side, member=member, towards=towards):
                for group in self.held(place.digits):
                    block = self.one(part, group, member)
                    remote(
                        block,
                        block,
                        self.line_send.at[2 * step + side, part],
                        self.line_recv.at[2 * step + side, part],
                        place.far(towards),
                    ).start()

    def spread_core(self, part):
        if self.near_first(part):
            self.line_arrived(part, self.place.n_mem - 2)
        else:
            self.plane_total(part, self.place.digits - 1).wait_recv()
        for group in self.held(self.place.digits):
            block = self.group(part, group)
            remote(
                block,
                block,
                self.core_send.at[part],
                self.core_recv.at[part],
                self.place.sibling(),
            ).start()

    def events(self, part):
        digits, n_mem = self.place.digits, self.place.n_mem
        time = float(part)
        found = [(time, functools.partial(self.set_out, part))]
        for stage in range(1 if self.near_first(part) else 0, digits):
            time += 1.6
            found.append((time, functools.partial(self.spread_plane, part, stage)))
        if self.near_first(part):
            time += 1.2
            for step in range(n_mem - 1):
                found.append((time, functools.partial(self.spread_line, part, step)))
                time += 0.8
            time -= 1.4
        time += 1.5
        found.append((time, functools.partial(self.spread_core, part)))
        return found, time + 0.9

    def finish(self):
        for part in range(len(self.parts)):
            for stage in range(self.place.digits):
                self.plane_total(part, stage).wait_send()
            self.core_total(part).wait_send()
            if self.near_first(part):
                for step in range(self.place.n_mem - 1):
                    for side, (sends, _, _, _) in enumerate(self.sides(step)):

                        @pl.when(sends)
                        def _(step=step, side=side, part=part):
                            self.line_total(part, step, side).wait_send()
            else:
                self.far_total(part).wait_send()


class Job:
    def __init__(self, left, right, first, target, far_first=False):
        self.left, self.right, self.first, self.target = left, right, first, target
        self.small = right is None
        self.far_first = far_first
        self.width = target.shape[-1]
        self.at = 0


OUT_SLOTS, LANE_SLOTS, PLANE_SLOTS, CORE_RING, FIRST_RING, RING = 2, 3, 2, 2, 6, 4


class Reduce:
    def __init__(self, place, jobs, sems, wide, small, early):
        self.place, self.jobs, self.wide, self.small, self.early = place, jobs, wide, small, early
        (
            self.core_send,
            self.core_recv,
            self.plane_send,
            self.plane_recv,
            self.far_send,
            self.far_recv,
        ) = sems
        wanted = [place.row]
        for stage in reversed(range(place.digits)):
            wanted = wanted + [place.turn(group, stage) for group in wanted]
        self.wanted = [group // 2 for group in wanted]
        large, plain, other = 0, 0, 0
        for job in jobs:
            if not job.small:
                job.large = large
                large += 1
                if job.far_first:
                    job.at = other
                    other += 1
                else:
                    job.at = plain
                    plain += 1

    def cut(self, ref, job):
        return ref if job.width == ref.shape[-1] else ref.at[:, :, pl.ds(0, job.width)]

    def out(self, job):
        return self.cut(self.wide[0].at[job.large % OUT_SLOTS], job)

    def lanes(self, job):
        if job.small:
            return self.small[1].at[0]
        return self.cut(self.wide[1].at[job.large % LANE_SLOTS], job)

    def core_in(self, job):
        if job.small:
            return self.small[2 + self.place.digits].at[0]
        return self.cut(self.wide[2 + self.place.digits].at[job.large % CORE_RING], job)

    def plane(self, job, stage):
        if job.small:
            return self.small[2 + stage].at[0]
        if job.far_first:
            return self.cut(self.early[1 + stage].at[job.at], job)
        return self.cut(self.wide[2 + stage].at[job.at % PLANE_SLOTS], job)

    def plane_in(self, job, stage):
        digits = self.place.digits
        if job.small:
            return self.small[3 + digits + stage].at[0]
        if job.far_first:
            return self.cut(self.early[1 + digits + stage].at[job.at], job)
        ring = FIRST_RING if stage == 0 else RING
        return self.cut(self.wide[3 + digits + stage].at[job.at % ring], job)

    def far_in(self, job):
        digits = self.place.digits
        if job.small:
            return self.small[3 + 2 * digits].at[0]
        if job.far_first:
            whole = self.early[1 + 2 * digits].at[job.at]
            return whole if job.width == whole.shape[-1] else whole.at[:, :, :, pl.ds(0, job.width)]
        return self.cut(self.wide[3 + 2 * digits].at[job.at % RING], job)

    def far_sum(self, job):
        return self.cut(self.early[0].at[job.at], job)

    def previous(self, number, same, distance):
        found = [n for n in range(number) if same(self.jobs[n])]
        return found[-distance] if len(found) >= distance else None

    def is_large(self, job):
        return not job.small

    def is_plain(self, job):
        return not job.small and not job.far_first

    def core_copy(self, number):
        job = self.jobs[number]
        source = job.left.at[1 - self.place.lane] if job.small else self.out(job)
        return remote(
            source,
            self.core_in(job),
            self.core_send.at[number],
            self.core_recv.at[number],
            self.place.sibling(),
        )

    def product(self, job, side, store):
        half = self.place.n_rows // 2
        group = job.left.shape[1] // half
        width = min(TILE, job.width)

        def column_step(step, carry):
            source = pl.ds(pl.multiple_of(job.first + step * width, width), width)
            value = dot(job.left[side], job.right[:, source])
            for index in range(half):
                store(index, span(step, width), value[index * group : (index + 1) * group])
            return carry

        lax.fori_loop(0, job.width // width, column_step, 0)

    def core_stage(self, number):
        job = self.jobs[number]
        if not job.small:
            before = self.previous(number, self.is_large, OUT_SLOTS)
            if before is not None:
                self.core_copy(before).wait_send()
            out = self.out(job)

            def store(index, columns, value):
                out[index, :, columns] = value.astype(out.dtype)

            self.product(job, 1 - self.place.lane, store)
        self.core_copy(number).start()

    def plane_copy(self, number, stage, which):
        job = self.jobs[number]
        count = 1 << (self.place.digits - 1 - stage)
        if stage == 0:
            source = self.far_sum(job) if job.far_first else self.lanes(job)
            source = source.at[self.wanted[count + which]]
        else:
            source = self.plane(job, stage - 1).at[count + which]
        return remote(
            source,
            self.plane_in(job, stage).at[which],
            self.plane_send.at[stage, number],
            self.plane_recv.at[stage, number],
            self.place.partner(stage),
        )

    def plane_total(self, number, stage):
        some = self.plane_in(self.jobs[number], stage)
        return remote(
            some,
            some,
            self.plane_send.at[stage, number],
            self.plane_recv.at[stage, number],
            self.place.partner(stage),
        )

    def plane_send_out(self, number, stage):
        for which in range(1 << (self.place.digits - 1 - stage)):
            self.plane_copy(number, stage, which).start()

    def lanes_sent(self, number):
        if self.jobs[number].far_first:
            self.far_total(number).wait_send()
        else:
            self.plane_total(number, 0).wait_send()

    def lane_stage(self, number):
        job = self.jobs[number]
        if not job.small:
            before = self.previous(number, self.is_large, LANE_SLOTS)
            if before is not None:
                self.lanes_sent(before)
        lanes, arrived = self.lanes(job), self.core_in(job)
        self.core_copy(number).wait_recv()
        if job.small:
            lanes[...] = job.left[self.place.lane] + arrived[...]
        else:

            def store(index, columns, value):
                total = value + arrived[index, :, columns].astype(jnp.float32)
                lanes[index, :, columns] = total.astype(lanes.dtype)

            self.product(job, self.place.lane, store)
        if job.far_first:
            self.far_send_out(number)
        else:
            self.plane_send_out(number, 0)

    def plane_stage(self, number, stage):
        job, digits = self.jobs[number], self.place.digits
        last = stage == digits - 1
        if self.is_plain(job):
            before = self.previous(number, self.is_plain, PLANE_SLOTS)
            if before is not None and last:
                self.far_total(before).wait_send()
            elif before is not None:
                self.plane_total(before, stage + 1).wait_send()
        self.plane_total(number, stage).wait_recv()
        for which in range(1 << (digits - 1 - stage)):
            if stage == 0:
                mine = self.far_sum(job) if job.far_first else self.lanes(job)
                mine = mine.at[self.wanted[which]]
            else:
                mine = self.plane(job, stage - 1).at[which]
            arrived = self.plane_in(job, stage).at[which]
            total = job.target if job.far_first and last else self.plane(job, stage).at[which]
            block = min(32, mine.shape[0])

            def add(step, carry, mine=mine, arrived=arrived, total=total, block=block):
                rows = span(step, block)
                value = mine[rows].astype(jnp.float32) + arrived[rows].astype(jnp.float32)
                total[rows] = value.astype(total.dtype)
                return carry

            lax.fori_loop(0, mine.shape[0] // block, add, 0)
        if not last:
            self.plane_send_out(number, stage + 1)
        elif not job.far_first:
            self.far_send_out(number)

    def member_rows(self, member):
        size = self.wide[3 + 2 * self.place.digits].shape[2]
        return span(member, size)

    def piece(self, job, member):
        if job.far_first:
            return self.lanes(job).at[:, self.member_rows(member), :]
        whole = self.plane(job, self.place.digits - 1).at[0]
        return whole if job.small else whole.at[self.member_rows(member)]

    def far_copy(self, number, step):
        place, job = self.place, self.jobs[number]
        return remote(
            self.piece(job, (place.mem + step) % place.n_mem),
            self.far_in(job).at[step - 1],
            self.far_send.at[number],
            self.far_recv.at[number],
            place.far(step),
        )

    def far_send_out(self, number):
        for step in range(1, self.place.n_mem):
            self.far_copy(number, step).start()

    def far_total(self, number):
        some = self.far_in(self.jobs[number])
        return remote(
            some, some, self.far_send.at[number], self.far_recv.at[number], self.place.far(1)
        )

    def far_stage(self, number):
        job = self.jobs[number]
        self.far_total(number).wait_recv()
        arrived = self.far_in(job)
        if job.far_first:
            mine, total = self.piece(job, self.place.mem), self.far_sum(job)
            for group in range(total.shape[0]):
                value = mine[group].astype(jnp.float32)
                for step in range(self.place.n_mem - 1):
                    value = value + arrived[step, group].astype(jnp.float32)
                total[group] = value.astype(total.dtype)
            self.plane_send_out(number, 0)
        else:
            value = self.piece(job, self.place.mem)[...].astype(jnp.float32)
            for step in range(self.place.n_mem - 1):
                value = value + arrived[step].astype(jnp.float32)
            job.target[...] = value

    def events(self, number):
        job, digits = self.jobs[number], self.place.digits
        found = [(0.0, functools.partial(self.core_stage, number))]
        found.append((0.9, functools.partial(self.lane_stage, number)))
        stages = [functools.partial(self.plane_stage, number, stage) for stage in range(digits)]
        far = functools.partial(self.far_stage, number)
        time = 3.2
        for action in [far] + stages if job.far_first else stages + [far]:
            found.append((time, action))
            time += 1.4 if time + 1.4 < 3.1 + 1.4 * digits else 1.1
        return [(number + time, action) for time, action in found]

    def finish(self):
        for number, job in enumerate(self.jobs):
            later = range(number + 1, len(self.jobs))
            out = [n for n in later if self.previous(n, self.is_large, OUT_SLOTS) == number]
            lanes = [n for n in later if self.previous(n, self.is_large, LANE_SLOTS) == number]
            plane = [n for n in later if self.previous(n, self.is_plain, PLANE_SLOTS) == number]
            out = [n for n in out if not self.jobs[n].small]
            lanes = [n for n in lanes if not self.jobs[n].small]
            plane = [n for n in plane if self.is_plain(self.jobs[n])]
            if not out or job.small:
                self.core_copy(number).wait_send()
            if not lanes or job.small:
                self.lanes_sent(number)
            if not plane or not self.is_plain(job):
                for stage in range(0 if job.far_first else 1, self.place.digits):
                    self.plane_total(number, stage).wait_send()
                if not job.far_first:
                    self.far_total(number).wait_send()


NORMAL = (((1,), (0,)), ((), ()))
TURNED = (((1,), (1,)), ((), ()))
LEFT_TURNED = (((0,), (0,)), ((), ()))


def dot(left, right, dims=NORMAL):
    return lax.dot_general(left, right, dims, preferred_element_type=jnp.float32)


def times(left, weight, store):
    width = min(TILE, weight.shape[1])

    def column_step(step, carry):
        columns = span(step, width)
        store(columns, dot(left[...], weight[:, columns]))
        return carry

    lax.fori_loop(0, weight.shape[1] // width, column_step, 0)


def times_turned(left, weight, store):
    width = min(TILE, weight.shape[0])

    def column_step(step, carry):
        columns = span(step, width)
        store(columns, dot(left[...], weight[columns, :], TURNED))
        return carry

    lax.fori_loop(0, weight.shape[0] // width, column_step, 0)


def into(target):
    def store(columns, value):
        target[:, columns] = value.astype(target.dtype)

    return store


ROWS = 32


def by_rows(count, step):
    def body(index, carry):
        step(span(index, ROWS))
        return carry

    lax.fori_loop(0, count // ROWS, body, 0)


def norm_forward(total, gains, index, unit, scale, use):
    gain, shift = gains[index : index + 1, :], gains[index + 3 : index + 4, :]

    def step(rows):
        value = total[rows, :]
        centre = value - jnp.mean(value, axis=-1, keepdims=True)
        spread = jnp.mean(centre * centre, axis=-1, keepdims=True)
        root = lax.rsqrt(spread + EPS)
        scaled = centre * root
        unit[rows, :] = scaled
        scale[rows, :] = root
        use(rows, scaled * gain + shift)

    by_rows(total.shape[0], step)


def norm_slope(incoming, scaled, root, gain):
    width = scaled.shape[1]
    scaled_grad = incoming * gain
    first = jnp.mean(scaled_grad, axis=-1, keepdims=True)
    second = jnp.mean(scaled_grad * scaled, axis=-1, keepdims=True)
    value = root * (scaled_grad - first - scaled * second)
    of_gain = jnp.sum((incoming * scaled).reshape(ROWS // 8, 8, width), axis=0)
    of_shift = jnp.sum(incoming.reshape(ROWS // 8, 8, width), axis=0)
    return value, of_gain, of_shift


def keep_small(index, sums, small):
    for offset, partial in ((index, sums[0]), (index + 3, sums[1])):
        line = jnp.sum(partial, axis=0, keepdims=True)
        for group in range(2 * small.shape[1]):
            small[group % 2, group // 2, offset : offset + 1, :] = line[
                :, group * 128 : (group + 1) * 128
            ]


def norm_backward(grad, gains, index, unit, scale, target, target_low, small):
    gain = gains[index : index + 1, :]

    def body(block, sums):
        rows = span(block, ROWS)
        value, of_gain, of_shift = norm_slope(grad[rows, :], unit[rows, :], scale[rows, :], gain)
        target[rows, :] = value
        target_low[rows, :] = value.astype(target_low.dtype)
        return (sums[0] + of_gain, sums[1] + of_shift)

    zero = jnp.zeros((8, unit.shape[1]), jnp.float32)
    keep_small(index, lax.fori_loop(0, unit.shape[0] // ROWS, body, (zero, zero)), small)


def norm_both(total, grad, gains, index, result, target, target_low, small):
    gain, shift = gains[index : index + 1, :], gains[index + 3 : index + 4, :]

    def body(block, sums):
        rows = span(block, ROWS)
        value = total[rows, :]
        centre = value - jnp.mean(value, axis=-1, keepdims=True)
        spread = jnp.mean(centre * centre, axis=-1, keepdims=True)
        root = lax.rsqrt(spread + EPS)
        scaled = centre * root
        result[rows, :] = scaled * gain + shift
        incoming = grad[rows, :].astype(jnp.float32)
        value, of_gain, of_shift = norm_slope(incoming, scaled, root, gain)
        target[rows, :] = value
        target_low[rows, :] = value.astype(target_low.dtype)
        return (sums[0] + of_gain, sums[1] + of_shift)

    zero = jnp.zeros((8, total.shape[1]), jnp.float32)
    keep_small(index, lax.fori_loop(0, total.shape[0] // ROWS, body, (zero, zero)), small)


def lane_masks(dtype):
    low = lax.broadcasted_iota(jnp.int32, (1, 2 * HEAD_DIM), 1) < HEAD_DIM
    first = jnp.where(low, 1.0, 0.0)
    return first.astype(dtype), (1.0 - first).astype(dtype)


def attention_forward(query, keys, values, bias, mixed, lse):
    masks = lane_masks(query.dtype)
    keep = lane_masks(jnp.float32)

    def pair_step(pair, carry):
        lanes = span(pair, 2 * HEAD_DIM)
        two_query, two_keys, two_values = query[:, lanes], keys[:, lanes], values[:, lanes]
        total = None
        for head in range(2):
            scores = dot(two_keys, two_query * masks[head], TURNED) * SCALE + bias[...]
            top = jnp.max(scores, axis=0, keepdims=True)
            weight = jnp.exp(scores - top)
            norm = jnp.sum(weight, axis=0, keepdims=True)
            probs = (weight * (1.0 / norm)).astype(query.dtype)
            part = dot(probs, two_values, LEFT_TURNED) * keep[head]
            total = part if total is None else total + part
            lse[pair, head : head + 1, :] = top + jnp.log(norm)
        mixed[:, lanes] = total.astype(mixed.dtype)
        return carry

    lax.fori_loop(0, lse.shape[0], pair_step, 0)


def attention_backward(
    query, keys, values, bias, lse, grad, query_grad, key_grad, value_grad, first, last
):
    masks = lane_masks(query.dtype)
    keep = lane_masks(jnp.float32)

    def pair_step(pair, carry):
        lanes = span(pair, 2 * HEAD_DIM)
        two_query, two_keys, two_values = query[:, lanes], keys[:, lanes], values[:, lanes]
        two_grad = grad[:, lanes]
        sums = [None, None, None]
        for head in range(2):
            scores = dot(two_keys, two_query * masks[head], TURNED) * SCALE + bias[...]
            probs = jnp.exp(scores - lse[pair, head : head + 1, :])
            pulled = dot(two_values, two_grad * masks[head], TURNED)
            inner = jnp.sum(probs * pulled, axis=0, keepdims=True)
            slope = (probs * (pulled - inner) * SCALE).astype(query.dtype)
            parts = (
                dot(slope, two_keys, LEFT_TURNED),
                dot(slope, two_query),
                dot(probs.astype(query.dtype), two_grad),
            )
            for index, part in enumerate(parts):
                part = part * keep[head]
                sums[index] = part if sums[index] is None else sums[index] + part
        query_grad[:, lanes] = sums[0].astype(query_grad.dtype)
        key_grad[:, lanes] = sums[1].astype(key_grad.dtype)
        value_grad[:, lanes] = sums[2].astype(value_grad.dtype)
        return carry

    lax.fori_loop(first, last, pair_step, 0)


def turn_blocks(left, eye, store):
    width = eye.shape[0]
    for block in range(left.shape[1] // width):
        columns = pl.ds(block * width, width)
        store(block, dot(eye[...], left[:, columns], TURNED).astype(left.dtype))


def turn_by_lane(left, eye, target):
    group = eye.shape[0] // 2

    def store(block, value):
        target[0, pl.ds(block * group, group), :] = value[:group]
        target[1, pl.ds(block * group, group), :] = value[group:]

    turn_blocks(left, eye, store)


SQUARES = 8


def layer_kernel(places, sizes, *refs):
    n_rows, n_mem, width, ff, shard = sizes
    ref = SimpleNamespace(**jax.tree.map(lambda place: refs[place], places))
    place = Place(n_rows, n_mem)
    many = ff // width
    own_ff = ff // (n_rows * n_mem)
    (
        at_query,
        at_key,
        at_value,
        at_output,
        at_cross_query,
        at_cross_key,
        at_cross_value,
        at_cross_output,
    ) = range(SQUARES)
    full = ref.full
    expand, contract = ref.expand_full, ref.contract_full
    tokens, gains = ref.tokens, ref.gains
    low, turned = SimpleNamespace(**ref.low), SimpleNamespace(**ref.turned)

    order = [
        at_query,
        at_key,
        at_value,
        at_output,
        at_cross_key,
        at_cross_value,
        at_cross_query,
        at_cross_output,
    ]
    narrow = width // many
    weights = [(ref.squares[index], full[index], ALL) for index in order]
    weights += [(ref.expand, expand, pl.ds(j * width, width)) for j in range(many)]
    weights += [(ref.contract, contract, pl.ds(j * narrow, narrow)) for j in range(many)]
    near = (1, 5, 9)
    parts = [weight + (number in near,) for number, weight in enumerate(weights)]
    parts.insert(SMALL_AT, (ref.small, ref.small_full, ALL, False))
    gather = Gather(place, parts, ref.gather_sems)

    slots, slot_sem = ref.slots, ref.slot_sem
    count = [0]

    def load(pieces):
        number = count[0]
        count[0] += 1
        slot = slots.at[number % SLOTS]
        for source, columns in pieces:
            pltpu.make_async_copy(source, slot.at[:, columns], slot_sem.at[number % SLOTS]).start()
        return number

    def ready(number):
        slot = slots.at[number % SLOTS]
        pltpu.make_async_copy(slot, slot, slot_sem.at[number % SLOTS]).wait()
        return slot

    def expand_block(j):
        return [(expand.at[:, pl.ds(j * width, width)], ALL)]

    def contract_columns(j):
        return [
            (
                contract.at[pl.ds(i * width, width), pl.ds(j * narrow, narrow)],
                pl.ds(i * narrow, narrow),
            )
            for i in range(many)
        ]

    def contract_rows(j):
        return [(contract.at[pl.ds(j * width, width), :], ALL)]

    mem_block = ref.memory.shape[1]
    memory, mem_rows = ref.memory, ref.mem_rows

    def memory_own():
        return pltpu.make_async_copy(
            memory.at[place.mem], mem_rows.at[span(place.mem, mem_block)], ref.mem_sem.at[0]
        )

    def memory_total():
        some = mem_rows.at[pl.ds(0, (n_mem - 1) * mem_block)]
        return remote(some, some, ref.mem_sem.at[1], ref.mem_sem.at[2], place.far(1))

    ref.small[...] = jnp.zeros_like(ref.small)
    for member in range(n_mem):

        @pl.when(place.mem == member)
        def _(member=member):
            lanes = slice(member * shard, (member + 1) * shard)
            ref.small[0:3, lanes] = ref.norm_gains[...].astype(jnp.float32)
            ref.small[3:6, lanes] = ref.norm_shifts[...].astype(jnp.float32)

    place.greet()
    actions = []
    whole = []
    for part in range(len(parts)):
        found, time = gather.events(part)
        actions += found
        whole.append(time)
    actions.sort(key=lambda item: item[0])
    start = [action for action in actions if action[0] < 2]
    actions = actions[len(start) :]
    for _, action in start:
        action()
    memory_own().start()
    for step in range(1, n_mem):
        remote(
            memory.at[(place.mem + step) % n_mem],
            mem_rows.at[span(place.mem, mem_block)],
            ref.mem_sem.at[1],
            ref.mem_sem.at[2],
            place.far(step),
        ).start()

    self_bias, cross_bias, eye = ref.self_bias, ref.cross_bias, ref.eye
    own_row = ref.token_ids[pl.ds(place.mem, 1), :].astype(jnp.float32)
    mem_row = ref.memory_ids[pl.ds(place.mem, 1), :].astype(jnp.float32)
    key_place = lax.broadcasted_iota(jnp.int32, self_bias.shape, 0)
    query_place = lax.broadcasted_iota(jnp.int32, self_bias.shape, 1)
    own_wide = jnp.broadcast_to(own_row, self_bias.shape)
    mem_wide = jnp.broadcast_to(mem_row, (cross_bias.shape[1], cross_bias.shape[0]))
    same = (jnp.transpose(own_wide) == own_wide) & (key_place <= query_place)
    self_bias[...] = jnp.where(same, 0.0, NEG)
    cross_bias[...] = jnp.where(jnp.transpose(mem_wide) == own_row, 0.0, NEG)
    eye_row = lax.broadcasted_iota(jnp.int32, eye.shape, 0)
    eye_column = lax.broadcasted_iota(jnp.int32, eye.shape, 1)
    eye[...] = jnp.where(eye_row == eye_column, 1.0, 0.0).astype(eye.dtype)
    turn_by_lane(tokens, eye, turned.tokens)

    accumulated, other = ref.accumulated, ref.other
    hidden, slope, hidden_turned = ref.hidden, ref.slope, ref.hidden_turned

    def small_piece():
        blocks = ref.small_full
        for group in range(n_rows):
            total = None
            for member in range(n_mem):
                first = (group * n_mem + member) * 8
                value = blocks[first : first + 8, :]
                total = value if total is None else total + value
            gains[:, group * 128 : (group + 1) * 128] = total

    def query_piece(slot):
        times(tokens, slot, into(ref.query))

    def key_piece(slot):
        times(tokens, slot, into(ref.keys))

    def value_piece(slot):
        times(tokens, slot, into(ref.values))
        attention_forward(
            ref.query, ref.keys, ref.values, self_bias, ref.attended, ref.self_lse
        )

    def output_piece(slot):
        def store(columns, value):
            accumulated[:, columns] = ALPHA * tokens[:, columns].astype(jnp.float32) + value

        times(ref.attended, slot, store)

        def use(rows, value):
            ref.first_low[rows, :] = value.astype(jnp.bfloat16)
            other[rows, :] = value

        norm_forward(accumulated, gains, 0, ref.unit1, ref.scale1, use)
        turn_by_lane(ref.attended, eye, turned.attended)

    def cross_key_piece(slot):
        memory_own().wait()
        memory_total().wait_recv()
        times(mem_rows, slot, into(ref.cross_keys))
        turn_by_lane(mem_rows, eye, turned.memory)

    def cross_value_piece(slot):
        times(mem_rows, slot, into(ref.cross_values))
        turn_by_lane(ref.first_low, eye, turned.first)

    def cross_query_piece(slot):
        times(ref.first_low, slot, into(ref.cross_query))
        attention_forward(
            ref.cross_query,
            ref.cross_keys,
            ref.cross_values,
            cross_bias,
            ref.crossed,
            ref.cross_lse,
        )

    def cross_output_piece(slot):
        def store(columns, value):
            accumulated[:, columns] = ALPHA * other[:, columns] + value

        times(ref.crossed, slot, store)

        def use(rows, value):
            ref.second_low[rows, :] = value.astype(jnp.bfloat16)
            other[rows, :] = value

        norm_forward(accumulated, gains, 1, ref.unit2, ref.scale2, use)
        turn_by_lane(ref.crossed, eye, turned.crossed)

    def expand_piece(j, slot):
        def store(columns, value):
            there = pl.ds(pl.multiple_of(j * width + columns.start, TILE), columns.size)
            bell = 0.5 * (1.0 + lax.erf(value * math.sqrt(0.5)))
            density = jnp.exp(value * value * -0.5) * (1.0 / math.sqrt(2.0 * math.pi))
            hidden[:, there] = (value * bell).astype(hidden.dtype)
            slope[:, there] = (bell + value * density).astype(slope.dtype)

        times(ref.second_low, slot, store)

        def keep(block, value):
            for index in range(value.shape[0] // shard):
                first = j * width + block * value.shape[0] + index * shard
                device, job = first // own_ff, first % own_ff // shard
                group, member = device // n_mem, device % n_mem
                at = group // 2 * n_mem * shard + member * shard
                hidden_turned[job, group % 2, at : at + shard, :] = value[
                    index * shard : (index + 1) * shard
                ]

        turn_blocks(hidden.at[:, pl.ds(j * width, width)], eye, keep)

    def contract_piece(j, slot):
        total = None
        for i in range(many):
            value = dot(
                hidden[:, i * width : (i + 1) * width], slot[:, i * narrow : (i + 1) * narrow]
            )
            total = value if total is None else total + value
        columns = pl.ds(j * narrow, narrow)
        accumulated[:, columns] = ALPHA * other[:, columns] + total

    pieces = [
        query_piece,
        key_piece,
        value_piece,
        output_piece,
        cross_key_piece,
        cross_value_piece,
        cross_query_piece,
        cross_output_piece,
    ]
    sources = [[(full[index], ALL)] for index in order]
    for j in range(many):
        pieces.append(functools.partial(expand_piece, j))
        sources.append(expand_block(j))
    for j in range(many):
        pieces.append(functools.partial(contract_piece, j))
        sources.append(contract_columns(j))

    waiting = []

    def arrive(part):
        gather.core_total(part).wait_recv()
        if part != SMALL_AT:
            number = part - (part > SMALL_AT)
            waiting.append((number, load(sources[number])))

    def use():
        number, slot = waiting.pop(0)
        pieces[number](ready(slot))

    last = 0.0
    for part, time in enumerate(whole):
        time = max(time, last + 0.2)
        actions.append((time, functools.partial(arrive, part)))
        actions.append((time + 0.5, small_piece if part == SMALL_AT else use))
        last = time
    actions.sort(key=lambda item: item[0])
    for _, action in actions:
        action()

    backward_sources = [contract_rows(j) for j in range(many)]
    backward_sources += [expand_block(j) for j in range(many)]
    backward_sources += [
        [(full[index], ALL)]
        for index in (
            at_cross_output,
            at_cross_query,
            at_output,
            at_cross_key,
            at_cross_value,
            at_query,
            at_key,
            at_value,
        )
    ]
    loads = [load(backward_sources[0]), load(backward_sources[1])]
    used = [0]

    def next_slot():
        slot = ready(loads[used[0]])
        used[0] += 1
        if len(loads) < len(backward_sources):
            loads.append(load(backward_sources[len(loads)]))
        return slot

    small_sums = ref.small_sums
    small_sums[...] = jnp.zeros_like(small_sums)
    norm_both(
        accumulated, ref.out_grad, gains, 2, ref.result, accumulated, low.third, small_sums
    )

    def inner_piece(j):
        slot = next_slot()

        def store(columns, value):
            there = pl.ds(pl.multiple_of(j * width + columns.start, TILE), columns.size)
            slope[:, there] = (value * slope[:, there].astype(jnp.float32)).astype(slope.dtype)

        times_turned(low.third, slot, store)

    def second_piece(j):
        slot = next_slot()

        def store(columns, value):
            if j == 0:
                other[:, columns] = ALPHA * accumulated[:, columns] + value
            else:
                other[:, columns] = other[:, columns] + value

        times_turned(slope.at[:, pl.ds(j * width, width)], slot, store)

    def second_norm_piece():
        norm_backward(
            other, gains, 1, ref.unit2, ref.scale2, accumulated, low.second, small_sums
        )

    pairs = width // (2 * HEAD_DIM)

    def cross_start_piece():
        times_turned(low.second, next_slot(), into(low.branch))

    def cross_piece(first, last):
        attention_backward(
            ref.cross_query,
            ref.cross_keys,
            ref.cross_values,
            cross_bias,
            ref.cross_lse,
            low.branch,
            low.cross_query,
            low.cross_key,
            low.cross_value,
            first,
            last,
        )

    def first_piece():
        def store(columns, value):
            other[:, columns] = ALPHA * accumulated[:, columns] + value

        times_turned(low.cross_query, next_slot(), store)
        norm_backward(other, gains, 0, ref.unit1, ref.scale1, accumulated, low.first, small_sums)

    def self_start_piece():
        times_turned(low.first, next_slot(), into(low.branch))

    def self_piece(first, last):
        attention_backward(
            ref.query,
            ref.keys,
            ref.values,
            self_bias,
            ref.self_lse,
            low.branch,
            low.query,
            low.key,
            low.value,
            first,
            last,
        )

    mem_out, mem_in = ref.mem_out, ref.mem_in

    def grad_own():
        return pltpu.make_async_copy(
            mem_out.at[span(place.mem, mem_block)], mem_in.at[place.mem], ref.mem_sem.at[3]
        )

    def grad_total():
        some = mem_in.at[pl.ds(0, n_mem - 1)]
        return remote(some, some, ref.mem_sem.at[4], ref.mem_sem.at[5], place.far(1))

    def memory_key_piece():
        times_turned(low.cross_key, next_slot(), into(other))

    def memory_value_piece():
        def store(columns, value):
            mem_out[:, columns] = (other[:, columns] + value).astype(mem_out.dtype)

        times_turned(low.cross_value, next_slot(), store)
        grad_own().start()
        for step in range(1, n_mem):
            remote(
                mem_out.at[span((place.mem + step) % n_mem, mem_block)],
                mem_in.at[place.mem],
                ref.mem_sem.at[4],
                ref.mem_sem.at[5],
                place.far(step),
            ).start()

    def input_piece(left, start):
        target = ref.input_grad

        def store(columns, value):
            if start:
                target[:, columns] = ALPHA * accumulated[:, columns] + value
            else:
                target[:, columns] = target[:, columns] + value

        times_turned(left, next_slot(), store)

    def memory_end_piece():
        grad_own().wait()
        grad_total().wait_recv()
        for member in range(n_mem):
            ref.memory_grad[member] = mem_in[member].astype(jnp.float32)

    def contract_job(j, first, columns, far_first=False):
        target = ref.contract_grad.at[pl.ds(j * shard, shard), pl.ds(first, columns)]
        return Job(hidden_turned.at[j], low.third, first, target, far_first)

    halves = ((0, width // 2), (width // 2, width // 2))
    jobs = [contract_job(0, *half) for half in halves]
    jobs += [contract_job(j, 0, width, j == many // 2) for j in range(1, many)]
    for j in range(many):
        columns = pl.ds(j * width, width)
        jobs.append(Job(turned.second, slope, j * width, ref.expand_grad.at[:, columns]))
    grads = ref.grads
    jobs += [
        Job(turned.crossed, low.second, 0, grads[at_cross_output]),
        Job(turned.memory, low.cross_key, 0, grads[at_cross_key], True),
        Job(turned.memory, low.cross_value, 0, grads[at_cross_value]),
        Job(turned.first, low.cross_query, 0, grads[at_cross_query]),
        Job(turned.attended, low.first, 0, grads[at_output]),
        Job(small_sums, None, 0, ref.small_total),
        Job(turned.tokens, low.query, 0, grads[at_query]),
        Job(turned.tokens, low.key, 0, grads[at_key]),
    ]
    for first, columns in halves:
        target = grads[at_value].at[:, pl.ds(first, columns)]
        jobs.append(Job(turned.tokens, low.value, first, target))
    reduce = Reduce(place, jobs, ref.reduce_sems, ref.wide, ref.little, ref.early)

    work = [[functools.partial(inner_piece, j)] for j in range(many)]
    work[1].append(functools.partial(turn_by_lane, ref.second_low, eye, turned.second))
    work += [[functools.partial(second_piece, j)] for j in range(many)]
    work[-1].append(second_norm_piece)
    work += [
        [
            cross_start_piece,
            functools.partial(cross_piece, 0, pairs // 2),
            functools.partial(cross_piece, pairs // 2, pairs),
        ],
        [first_piece],
        [
            self_start_piece,
            functools.partial(self_piece, 0, pairs // 2),
            functools.partial(self_piece, pairs // 2, pairs),
        ],
        [memory_key_piece],
        [memory_value_piece],
        [functools.partial(input_piece, low.query, True)],
        [functools.partial(input_piece, low.key, False)],
        [functools.partial(input_piece, low.value, False)],
        [memory_end_piece],
    ]
    actions = []
    for number in range(len(jobs)):
        actions += reduce.events(number)
    for number, found in enumerate(work):
        for index, action in enumerate(found):
            actions.append((number + 0.1 + 0.25 * index, action))
    actions.sort(key=lambda item: item[0])
    for _, action in actions:
        action()

    total = ref.small_total[...]
    own = jnp.zeros((8, shard), jnp.float32)
    for member in range(n_mem):
        here = jnp.where(place.mem == member, 1.0, 0.0)
        own = own + here * total[:, member * shard : (member + 1) * shard]
    ref.gains_grad[...] = own[0:3]
    ref.shifts_grad[...] = own[3:6]
    gather.finish()
    reduce.finish()
    memory_total().wait_send()
    grad_total().wait_send()


SMALL_AT = 2


def copy_kernel(count, *refs):
    copies = [
        pltpu.make_async_copy(refs[i], refs[count + i], refs[-1].at[i]) for i in range(count)
    ]
    for copy in copies:
        copy.start()
    for copy in copies:
        copy.wait()


def copied(values):
    anywhere = pl.BlockSpec(memory_space=pl.ANY)
    return pl.pallas_call(
        functools.partial(copy_kernel, len(values)),
        out_shape=[jax.ShapeDtypeStruct(value.shape, value.dtype) for value in values],
        in_specs=[anywhere] * len(values),
        out_specs=[anywhere] * len(values),
        scratch_shapes=[pltpu.SemaphoreType.DMA((len(values),))],
        name="results",
    )(*values)


def fused(n_rows, n_mem, ins):
    tokens, memory, squares = ins["tokens"], ins["memory"], ins["squares"]
    expand, contract = ins["expand"], ins["contract"]
    tokens_here, width = tokens.shape
    ff = expand.shape[1]
    shard = squares[0].shape[0]
    mem_tokens = memory.shape[0] * memory.shape[1]
    digits, half, many = (n_rows // 2).bit_length() - 1, n_rows // 2, ff // width
    pairs = width // (2 * HEAD_DIM)
    low, high = jnp.bfloat16, jnp.float32
    n_parts = 1 + SQUARES + 2 * many
    n_jobs = n_parts + 2
    dma, vmem = pltpu.SemaphoreType.DMA, pltpu.VMEM
    anywhere, near = pl.BlockSpec(memory_space=pl.ANY), pl.BlockSpec(memory_space=pltpu.VMEM)

    far_ins = dict(memory=memory, squares=squares, expand=expand, contract=contract)
    in_specs = {
        name: jax.tree.map(lambda _: anywhere if name in far_ins else near, value)
        for name, value in ins.items()
    }

    def out(shape, dtype=high):
        return jax.ShapeDtypeStruct(shape, dtype)

    outs = dict(
        result=out(tokens.shape),
        input_grad=out(tokens.shape),
        memory_grad=out(memory.shape),
        grads=[out(item.shape) for item in squares],
        expand_grad=out(expand.shape),
        contract_grad=out(contract.shape),
        gains_grad=out((3, shard)),
        shifts_grad=out((3, shard)),
    )
    far_outs = dict(
        full=[out((width, width), low)] * SQUARES,
        expand_full=out((width, ff), low),
        contract_full=out((ff, width), low),
    )
    out_specs = jax.tree.map(lambda _: near, outs)
    out_specs.update(jax.tree.map(lambda _: anywhere, far_outs))
    outs.update(far_outs)

    def token_rows(dtype):
        return vmem((tokens_here, width), dtype)

    def memory_rows(dtype):
        return vmem((mem_tokens, width), dtype)

    counts = [1 << (digits - 1 - stage) for stage in range(digits)]
    group, tiny = (n_mem * shard, width), (8, 128)
    wide = [(OUT_SLOTS, half) + group, (LANE_SLOTS, half) + group]
    wide += [(PLANE_SLOTS, count) + group for count in counts]
    wide += [(CORE_RING, half) + group]
    wide += [(RING if i else FIRST_RING, count) + group for i, count in enumerate(counts)]
    wide += [(RING, n_mem - 1, shard, width)]
    little = [(1, 1) + tiny, (1, half) + tiny]
    little += [(1, count) + tiny for count in counts]
    little += [(1, half) + tiny]
    little += [(1, count) + tiny for count in counts]
    little += [(1, n_mem - 1) + tiny]
    early = [(2, half, shard, width)]
    early += [(2, count, shard, width) for count in counts]
    early += [(2, count, shard, width) for count in counts]
    early += [(2, n_mem - 1, half, shard, width)]
    left = vmem((2, width // 2, tokens_here), low)
    scratch = dict(
        small=vmem(tiny, high),
        small_full=vmem((n_rows * n_mem * 8, 128), high),
        small_total=vmem(tiny, high),
        slots=vmem((SLOTS, width, width), low),
        slot_sem=dma((SLOTS,)),
        mem_sem=dma((6,)),
        gather_sems=[
            dma(shape + (n_parts,))
            for shape in ((), (), (), (digits,), (digits,), (), ())
            + ((2 * (n_mem - 1),), (2 * (n_mem - 1),))
        ],
        reduce_sems=[
            dma(shape + (n_jobs,)) for shape in ((), (), (digits,), (digits,), (), ())
        ],
        gains=vmem((8, width), high),
        query=token_rows(low),
        keys=token_rows(low),
        values=token_rows(low),
        attended=token_rows(low),
        first_low=token_rows(low),
        second_low=token_rows(low),
        cross_query=token_rows(low),
        crossed=token_rows(low),
        cross_keys=memory_rows(low),
        cross_values=memory_rows(low),
        mem_rows=memory_rows(low),
        mem_out=memory_rows(low),
        mem_in=vmem(memory.shape, low),
        unit1=token_rows(high),
        unit2=token_rows(high),
        accumulated=token_rows(high),
        other=token_rows(high),
        scale1=vmem((tokens_here, 1), high),
        scale2=vmem((tokens_here, 1), high),
        self_bias=vmem((tokens_here, tokens_here), high),
        cross_bias=vmem((mem_tokens, tokens_here), high),
        self_lse=vmem((pairs, 2, tokens_here), high),
        cross_lse=vmem((pairs, 2, tokens_here), high),
        eye=vmem((TILE, TILE), low),
        hidden=vmem((tokens_here, ff), low),
        slope=vmem((tokens_here, ff), low),
        hidden_turned=vmem((many, 2, width // 2, tokens_here), low),
        turned=dict(
            tokens=left, attended=left, first=left, memory=left, crossed=left, second=left
        ),
        low=dict(
            third=token_rows(low),
            second=token_rows(low),
            first=token_rows(low),
            branch=token_rows(low),
            cross_query=token_rows(low),
            cross_key=memory_rows(low),
            cross_value=memory_rows(low),
            query=token_rows(low),
            key=token_rows(low),
            value=token_rows(low),
        ),
        small_sums=vmem((2, half) + tiny, high),
        wide=[vmem(shape, low) for shape in wide],
        little=[vmem(shape, high) for shape in little],
        early=[vmem(shape, low) for shape in early],
    )
    in_values, in_tree = jax.tree.flatten(ins)
    out_shapes, out_tree = jax.tree.flatten(outs)
    scratch_shapes, scratch_tree = jax.tree.flatten(scratch)
    places = jax.tree.unflatten(in_tree, range(len(in_values)))
    at = len(in_values)
    places.update(jax.tree.unflatten(out_tree, range(at, at + len(out_shapes))))
    at += len(out_shapes)
    places.update(jax.tree.unflatten(scratch_tree, range(at, at + len(scratch_shapes))))
    values = pl.pallas_call(
        functools.partial(layer_kernel, places, (n_rows, n_mem, width, ff, shard)),
        out_shape=out_shapes,
        in_specs=jax.tree.leaves(in_specs),
        out_specs=jax.tree.leaves(out_specs),
        scratch_shapes=scratch_shapes,
        compiler_params=pltpu.CompilerParams(
            collective_id=0, has_side_effects=True, vmem_limit_bytes=VMEM_LIMIT
        ),
        name="layer",
    )(*in_values)
    found = jax.tree.unflatten(out_tree, values)
    for name in far_outs:
        del found[name]
    return found


def local(n_rows, n_mem, *args):
    (
        tokens,
        memory,
        token_ids,
        memory_ids,
        out_grad,
        self_query,
        self_key,
        self_value,
        self_output,
        cross_query,
        cross_key,
        cross_value,
        cross_output,
        expand_weight,
        contract_weight,
        norm_gains,
        norm_shifts,
    ) = args
    shard, width = self_query.shape
    suits = width == 128 * n_rows and shard % 16 == 0 and tokens.shape[0] == 1
    if not suits or n_rows < 4 or n_rows & (n_rows - 1) or n_mem < 2:
        return plain(*args)
    found = fused(
        n_rows,
        n_mem,
        dict(
            tokens=tokens[0],
            memory=memory,
            token_ids=token_ids,
            memory_ids=memory_ids,
            out_grad=out_grad[0],
            squares=[
                self_query,
                self_key,
                self_value,
                self_output,
                cross_query,
                cross_key,
                cross_value,
                cross_output,
            ],
            expand=expand_weight,
            contract=contract_weight,
            norm_gains=norm_gains,
            norm_shifts=norm_shifts,
        ),
    )
    values, tree = jax.tree.flatten(found)
    found = SimpleNamespace(**jax.tree.unflatten(tree, copied(values)))
    return (
        found.result[None],
        found.input_grad[None],
        found.memory_grad,
        *found.grads,
        found.expand_grad,
        found.contract_grad,
        found.gains_grad,
        found.shifts_grad,
    )


def solution(mesh):
    in_specs = (
        P(("rows", "mem"), None, None),
        P("rows", "mem", None),
        P("rows", None),
        P("rows", None),
        P(("rows", "mem"), None, None),
        P(("rows", "mem"), None),
        P(("rows", "mem"), None),
        P(("rows", "mem"), None),
        P(("rows", "mem"), None),
        P(("rows", "mem"), None),
        P(("rows", "mem"), None),
        P(("rows", "mem"), None),
        P(("rows", "mem"), None),
        P(("rows", "mem"), None),
        P(("rows", "mem"), None),
        P(None, ("rows", "mem")),
        P(None, ("rows", "mem")),
    )
    out_specs = (
        P(("rows", "mem"), None, None),
        P(("rows", "mem"), None, None),
        P("rows", "mem", None),
        P(("rows", "mem"), None),
        P(("rows", "mem"), None),
        P(("rows", "mem"), None),
        P(("rows", "mem"), None),
        P(("rows", "mem"), None),
        P(("rows", "mem"), None),
        P(("rows", "mem"), None),
        P(("rows", "mem"), None),
        P(("rows", "mem"), None),
        P(("rows", "mem"), None),
        P(None, ("rows", "mem")),
        P(None, ("rows", "mem")),
    )
    layer = functools.partial(local, mesh.shape["rows"], mesh.shape["mem"])
    return jax.shard_map(layer, mesh=mesh, in_specs=in_specs, out_specs=out_specs, check_vma=False)
```

```python
import functools
import math
from types import SimpleNamespace

import jax
import jax.numpy as jnp
from jax import lax
from jax.experimental import pallas as pl
from jax.experimental.pallas import tpu as pltpu
from jax.sharding import PartitionSpec as P

MESH = pl.DeviceIdType.MESH

HEADS = 16
HEAD_DIM = 64


ALPHA = 4.16
EPS = 1e-05
SCALE = 0.125
NEG = -1e30


def layer_norm(hidden_activation, gain, shift):
    centre = hidden_activation - jnp.mean(hidden_activation, axis=-1, keepdims=True)
    spread = jnp.mean(centre * centre, axis=-1, keepdims=True)
    return centre * lax.rsqrt(spread + EPS) * gain + shift


def gelu_exact(value):
    return jax.nn.gelu(value, approximate=False)


def product(left, right):
    return jnp.dot(left, right, preferred_element_type=jnp.float32)


def split_heads(matrix):
    return matrix.reshape(matrix.shape[0], matrix.shape[1] // HEAD_DIM, HEAD_DIM)


def grouped(matrix):
    return jnp.moveaxis(matrix.reshape(matrix.shape[0], HEADS // 4, 4 * HEAD_DIM), 1, 0)


def ungrouped(stack):
    return jnp.moveaxis(stack, 0, 1).reshape(stack.shape[1], stack.shape[0] * stack.shape[2])


def row_map(function, items):
    return lax.map(lambda entry: function(*entry), items)


def score_block(query, keys, allowed):
    raw = jnp.einsum(
        "khe,qhe->hkq", split_heads(keys), split_heads(query), preferred_element_type=jnp.float32
    )
    return jnp.where(allowed[None], raw * SCALE, NEG)


def attend_probs(query, keys, allowed, lse):
    scores = score_block(query, keys, allowed)
    return jnp.where(allowed[None], jnp.exp(scores - lse[:, None, :]), 0.0)


def attend_forward(query, keys, values, allowed):
    scores = score_block(query, keys, allowed)
    top = jnp.max(scores, axis=1)
    weight = jnp.where(allowed[None], jnp.exp(scores - top[:, None, :]), 0.0)
    total = jnp.sum(weight, axis=1)
    probs = (weight / total[:, None, :]).astype(jnp.bfloat16)
    mixed = jnp.einsum(
        "hkq,khe->qhe", probs, split_heads(values), preferred_element_type=jnp.float32
    )
    return (mixed.reshape(query.shape), top + jnp.log(total))


def value_pull(grad, values):
    return jnp.einsum(
        "qhe,khe->hkq", split_heads(grad), split_heads(values), preferred_element_type=jnp.float32
    )


def score_grads(probs, pulled, inner):
    return (probs * (pulled - inner[:, None, :]) * SCALE).astype(jnp.bfloat16)


def query_from(score_grad, keys, shape):
    moved = jnp.einsum(
        "hkq,khe->qhe", score_grad, split_heads(keys), preferred_element_type=jnp.float32
    )
    return moved.reshape(shape)


def key_from(score_grad, query, shape):
    moved = jnp.einsum(
        "hkq,qhe->khe", score_grad, split_heads(query), preferred_element_type=jnp.float32
    )
    return moved.reshape(shape)


def value_from(probs, grad, values):
    moved = jnp.einsum(
        "hkq,qhe->khe",
        probs.astype(jnp.bfloat16),
        split_heads(grad),
        preferred_element_type=jnp.float32,
    )
    return moved.reshape(values.shape)


def local_forward(query, keys, values, allowed):

    def one_group(items):
        return attend_forward(items[0], items[1], items[2], allowed)

    mixed, lse = lax.map(one_group, (grouped(query), grouped(keys), grouped(values)))
    return (ungrouped(mixed), lse)


def local_backward(query, keys, values, allowed, lse, grad):

    def one_group(items):
        part_query, part_keys, part_values, part_lse, part_grad = items
        probs = attend_probs(part_query, part_keys, allowed, part_lse)
        pulled = value_pull(part_grad, part_values)
        inner = jnp.sum(probs * pulled, axis=1)
        score_grad = score_grads(probs, pulled, inner)
        return (
            query_from(score_grad, part_keys, part_query.shape),
            key_from(score_grad, part_query, part_keys.shape),
            value_from(probs, part_grad, part_values),
        )

    parts = lax.map(one_group, (grouped(query), grouped(keys), grouped(values), lse, grouped(grad)))
    return (ungrouped(parts[0]), ungrouped(parts[1]), ungrouped(parts[2]))


def plain(
    tokens,
    memory,
    token_ids,
    memory_ids,
    out_grad,
    self_query,
    self_key,
    self_value,
    self_output,
    cross_query,
    cross_key,
    cross_value,
    cross_output,
    expand_weight,
    contract_weight,
    norm_gains,
    norm_shifts,
):
    full = (
        lax.all_gather(self_query, ("rows", "mem"), axis=0, tiled=True),
        lax.all_gather(self_key, ("rows", "mem"), axis=0, tiled=True),
        lax.all_gather(self_value, ("rows", "mem"), axis=0, tiled=True),
        lax.all_gather(self_output, ("rows", "mem"), axis=0, tiled=True),
        lax.all_gather(cross_query, ("rows", "mem"), axis=0, tiled=True),
        lax.all_gather(cross_key, ("rows", "mem"), axis=0, tiled=True),
        lax.all_gather(cross_value, ("rows", "mem"), axis=0, tiled=True),
        lax.all_gather(cross_output, ("rows", "mem"), axis=0, tiled=True),
        lax.all_gather(expand_weight, ("rows", "mem"), axis=0, tiled=True),
        lax.all_gather(contract_weight, ("rows", "mem"), axis=0, tiled=True),
        lax.all_gather(jnp.transpose(norm_gains), ("rows", "mem"), axis=0, tiled=True),
        lax.all_gather(jnp.transpose(norm_shifts), ("rows", "mem"), axis=0, tiled=True),
    )
    (
        self_attention_query,
        decoder_match_label,
        self_attention_value,
        self_attention_output,
        encoder_lookup_probe,
        key_cross,
        value_cross,
        cross_attention_output,
        up_projection,
        narrowing_matrix,
        gain_cols,
        shift_cols,
    ) = full
    gain_rows = jnp.transpose(gain_cols).astype(jnp.float32)
    shift_rows = jnp.transpose(shift_cols).astype(jnp.float32)
    rows_here = tokens.shape[0]
    member = lax.axis_index("mem")
    own_ids = lax.dynamic_slice_in_dim(token_ids, member * rows_here, rows_here, 0)
    positions = jnp.arange(tokens.shape[1], dtype=jnp.int32)
    self_allowed = (own_ids[:, :, None] == own_ids[:, None, :]) & (
        positions[:, None] <= positions[None, :]
    )[None]
    query = product(tokens, self_attention_query).astype(jnp.bfloat16)
    keys = product(tokens, decoder_match_label).astype(jnp.bfloat16)
    values = product(tokens, self_attention_value).astype(jnp.bfloat16)
    self_mixed, self_lse = row_map(local_forward, (query, keys, values, self_allowed))
    attention_result = self_mixed.astype(jnp.bfloat16)
    first, first_back = jax.vjp(
        layer_norm,
        ALPHA * tokens.astype(jnp.float32) + product(attention_result, self_attention_output),
        gain_rows[0],
        shift_rows[0],
    )
    first_reduced = first.astype(jnp.bfloat16)
    cross_queries = product(first_reduced, encoder_lookup_probe).astype(jnp.bfloat16)
    memory_rows = lax.all_to_all(memory, "mem", split_axis=0, concat_axis=1, tiled=True)
    row_ids = lax.dynamic_slice_in_dim(memory_ids, member * rows_here, rows_here, 0)
    cross_allowed = row_ids[:, :, None] == own_ids[:, None, :]
    cross_keys = product(memory_rows, key_cross).astype(jnp.bfloat16)
    cross_values = product(memory_rows, value_cross).astype(jnp.bfloat16)
    cross_mixed, cross_lse = row_map(
        local_forward, (cross_queries, cross_keys, cross_values, cross_allowed)
    )
    cross_attention_result = cross_mixed.astype(jnp.bfloat16)
    second, second_back = jax.vjp(
        layer_norm,
        ALPHA * first + product(cross_attention_result, cross_attention_output),
        gain_rows[1],
        shift_rows[1],
    )
    second_reduced = second.astype(jnp.bfloat16)
    hidden_value, gelu_back = jax.vjp(gelu_exact, product(second_reduced, up_projection))
    hidden_activation = hidden_value.astype(jnp.bfloat16)
    result, third_back = jax.vjp(
        layer_norm,
        ALPHA * second + product(hidden_activation, narrowing_matrix),
        gain_rows[2],
        shift_rows[2],
    )
    third_grad, gain_three, shift_three = third_back(out_grad.astype(jnp.float32))
    feedforward_gradient = third_grad.astype(jnp.bfloat16)
    down_projection_gradient = jnp.einsum(
        "ehj,ehc->jc", hidden_activation, feedforward_gradient, preferred_element_type=jnp.float32
    )
    (inner_grad,) = gelu_back(
        jnp.einsum(
            "hpu,ku->hpk",
            feedforward_gradient,
            narrowing_matrix,
            preferred_element_type=jnp.float32,
        )
    )
    inner_reduced = inner_grad.astype(jnp.bfloat16)
    expand_grad = jnp.einsum(
        "iqg,iqe->ge", second_reduced, inner_reduced, preferred_element_type=jnp.float32
    )
    second_total = ALPHA * third_grad + jnp.einsum(
        "iwm,fm->iwf", inner_reduced, up_projection, preferred_element_type=jnp.float32
    )
    second_grad, gain_two, shift_two = second_back(second_total)
    cross_branch_gradient = second_grad.astype(jnp.bfloat16)
    output_cross_grad = jnp.einsum(
        "nhb,nhc->bc",
        cross_attention_result,
        cross_branch_gradient,
        preferred_element_type=jnp.float32,
    )
    crossed_grad = jnp.einsum(
        "qwp,up->qwu",
        cross_branch_gradient,
        cross_attention_output,
        preferred_element_type=jnp.float32,
    ).astype(jnp.bfloat16)
    query_grads, key_grads, value_grads = row_map(
        local_backward,
        (cross_queries, cross_keys, cross_values, cross_allowed, cross_lse, crossed_grad),
    )
    key_low = key_grads.astype(jnp.bfloat16)
    value_low = value_grads.astype(jnp.bfloat16)
    row_grad = jnp.einsum(
        "sme,de->smd", key_low, key_cross, preferred_element_type=jnp.float32
    ) + jnp.einsum("sme,de->smd", value_low, value_cross, preferred_element_type=jnp.float32)
    key_cross_grad = jnp.einsum(
        "smd,sme->de", memory_rows, key_low, preferred_element_type=jnp.float32
    )
    value_cross_grad = jnp.einsum(
        "smd,sme->de", memory_rows, value_low, preferred_element_type=jnp.float32
    )
    memory_grad = lax.all_to_all(
        row_grad.astype(jnp.bfloat16), "mem", split_axis=1, concat_axis=0, tiled=True
    ).astype(row_grad.dtype)
    probe_lowered_precision = query_grads.astype(jnp.bfloat16)
    query_cross_grad = jnp.einsum(
        "nhb,nhc->bc", first_reduced, probe_lowered_precision, preferred_element_type=jnp.float32
    )
    first_total = ALPHA * second_grad + jnp.einsum(
        "qwp,up->qwu",
        probe_lowered_precision,
        encoder_lookup_probe,
        preferred_element_type=jnp.float32,
    )
    first_grad, gain_one, shift_one = first_back(first_total)
    self_branch_gradient = first_grad.astype(jnp.bfloat16)
    output_self_grad = jnp.einsum(
        "nhb,nhc->bc", attention_result, self_branch_gradient, preferred_element_type=jnp.float32
    )
    attended_grad = jnp.einsum(
        "qwp,up->qwu",
        self_branch_gradient,
        self_attention_output,
        preferred_element_type=jnp.float32,
    ).astype(jnp.bfloat16)
    self_query_reduced, decoder_label_lowered, self_value_reduced = row_map(
        local_backward, (query, keys, values, self_allowed, self_lse, attended_grad)
    )
    self_query_reduced = self_query_reduced.astype(jnp.bfloat16)
    decoder_label_lowered = decoder_label_lowered.astype(jnp.bfloat16)
    self_value_reduced = self_value_reduced.astype(jnp.bfloat16)
    query_self_grad = jnp.einsum(
        "nhb,nhc->bc", tokens, self_query_reduced, preferred_element_type=jnp.float32
    )
    key_self_grad = jnp.einsum(
        "nhb,nhc->bc", tokens, decoder_label_lowered, preferred_element_type=jnp.float32
    )
    value_self_grad = jnp.einsum(
        "nhb,nhc->bc", tokens, self_value_reduced, preferred_element_type=jnp.float32
    )
    input_grad = (
        ALPHA * first_grad
        + jnp.einsum(
            "qwp,up->qwu",
            self_query_reduced,
            self_attention_query,
            preferred_element_type=jnp.float32,
        )
        + jnp.einsum(
            "qwp,up->qwu",
            decoder_label_lowered,
            decoder_match_label,
            preferred_element_type=jnp.float32,
        )
        + jnp.einsum(
            "qwp,up->qwu",
            self_value_reduced,
            self_attention_value,
            preferred_element_type=jnp.float32,
        )
    )
    gain_grad = jnp.stack([gain_one, gain_two, gain_three], axis=1)
    shift_grad = jnp.stack([shift_one, shift_two, shift_three], axis=1)
    sums = (
        lax.psum_scatter(query_self_grad, ("rows", "mem"), scatter_dimension=0, tiled=True),
        lax.psum_scatter(key_self_grad, ("rows", "mem"), scatter_dimension=0, tiled=True),
        lax.psum_scatter(value_self_grad, ("rows", "mem"), scatter_dimension=0, tiled=True),
        lax.psum_scatter(output_self_grad, ("rows", "mem"), scatter_dimension=0, tiled=True),
        lax.psum_scatter(query_cross_grad, ("rows", "mem"), scatter_dimension=0, tiled=True),
        lax.psum_scatter(key_cross_grad, ("rows", "mem"), scatter_dimension=0, tiled=True),
        lax.psum_scatter(value_cross_grad, ("rows", "mem"), scatter_dimension=0, tiled=True),
        lax.psum_scatter(output_cross_grad, ("rows", "mem"), scatter_dimension=0, tiled=True),
        lax.psum_scatter(expand_grad, ("rows", "mem"), scatter_dimension=0, tiled=True),
        lax.psum_scatter(
            down_projection_gradient, ("rows", "mem"), scatter_dimension=0, tiled=True
        ),
        lax.psum_scatter(gain_grad, ("rows", "mem"), scatter_dimension=0, tiled=True),
        lax.psum_scatter(shift_grad, ("rows", "mem"), scatter_dimension=0, tiled=True),
    )
    return (
        result,
        input_grad,
        memory_grad,
        sums[0],
        sums[1],
        sums[2],
        sums[3],
        sums[4],
        sums[5],
        sums[6],
        sums[7],
        sums[8],
        sums[9],
        jnp.transpose(sums[10]),
        jnp.transpose(sums[11]),
    )


ALL = slice(None)
TILE = 256
SLOTS = 3
VMEM_LIMIT = 61 * 1024 * 1024


def flip(index, unit):
    return index + unit * (1 - 2 * ((index // unit) % 2))


def span(index, size):
    return pl.ds(pl.multiple_of(index * size, size), size)


class Place:
    def __init__(self, n_rows, n_mem):
        self.n_rows, self.n_mem = n_rows, n_mem
        self.digits = (n_rows // 2).bit_length() - 1
        self.row = lax.axis_index("rows")
        self.mem = lax.axis_index("mem")
        self.lane = self.row % 2

    def turn(self, index, stage):
        rising, falling = 2 << stage, 2 << (self.digits - 1 - stage)
        return flip(index, rising) * (1 - self.lane) + flip(index, falling) * self.lane

    def sibling(self):
        return (flip(self.row, 1), self.mem)

    def partner(self, stage):
        return (self.turn(self.row, stage), self.mem)

    def far(self, step):
        return (self.row, (self.mem + step) % self.n_mem)

    def greet(self):
        barrier = pltpu.get_barrier_semaphore()
        others = [self.far(step) for step in range(1, self.n_mem)]
        others += [self.partner(stage) for stage in range(self.digits)]
        others += [self.sibling()]
        for other in others:
            pl.semaphore_signal(barrier, inc=1, device_id=other, device_id_type=MESH)
        pl.semaphore_wait(barrier, len(others))


def remote(source, target, send_sem, recv_sem, device):
    return pltpu.make_async_remote_copy(
        src_ref=source,
        dst_ref=target,
        send_sem=send_sem,
        recv_sem=recv_sem,
        device_id=device,
        device_id_type=MESH,
    )


class Gather:
    def __init__(self, place, parts, sems):
        self.place, self.parts = place, parts
        (
            self.own_sem,
            self.far_send,
            self.far_recv,
            self.plane_send,
            self.plane_recv,
            self.core_send,
            self.core_recv,
            self.line_send,
            self.line_recv,
        ) = sems

    def near_first(self, part):
        return self.parts[part][3]

    def rows(self, part, first, count):
        source, target, columns, _ = self.parts[part]
        size = source.shape[0]
        return target.at[pl.ds(pl.multiple_of(first * size, size), count * size), columns]

    def group(self, part, group):
        return self.rows(part, group * self.place.n_mem, self.place.n_mem)

    def one(self, part, group, member):
        return self.rows(part, group * self.place.n_mem + member, 1)

    def shard(self, part):
        source, _, columns, _ = self.parts[part]
        return source.at[:, columns]

    def mine(self, part):
        return self.one(part, self.place.row, self.place.mem)

    def own(self, part):
        return pltpu.make_async_copy(self.shard(part), self.mine(part), self.own_sem.at[part])

    def held(self, stage):
        groups = [self.place.row]
        for before in range(stage):
            groups = groups + [self.place.turn(group, before) for group in groups]
        return groups

    def far_total(self, part):
        some = self.rows(part, 0, self.place.n_mem - 1)
        return remote(some, some, self.far_send.at[part], self.far_recv.at[part], self.place.far(1))

    def plane_total(self, part, stage):
        shards = 1 if self.near_first(part) else self.place.n_mem
        some = self.rows(part, 0, shards << stage)
        return remote(
            some,
            some,
            self.plane_send.at[stage, part],
            self.plane_recv.at[stage, part],
            self.place.partner(stage),
        )

    def core_total(self, part):
        some = self.rows(part, 0, self.place.n_mem * self.place.n_rows // 2)
        return remote(
            some, some, self.core_send.at[part], self.core_recv.at[part], self.place.sibling()
        )

    def line_total(self, part, step, side):
        some = self.rows(part, 0, self.place.n_rows // 2)
        at = 2 * step + side
        return remote(
            some, some, self.line_send.at[at, part], self.line_recv.at[at, part], self.place.far(1)
        )

    def set_out(self, part):
        self.own(part).start()
        if self.near_first(part):
            remote(
                self.shard(part),
                self.mine(part),
                self.plane_send.at[0, part],
                self.plane_recv.at[0, part],
                self.place.partner(0),
            ).start()
            return
        for step in range(1, self.place.n_mem):
            remote(
                self.shard(part),
                self.mine(part),
                self.far_send.at[part],
                self.far_recv.at[part],
                self.place.far(step),
            ).start()

    def spread_plane(self, part, stage):
        place = self.place
        if stage == 0:
            self.own(part).wait()
            self.far_total(part).wait_recv()
        else:
            if stage == 1 and self.near_first(part):
                self.own(part).wait()
            self.plane_total(part, stage - 1).wait_recv()
        for group in self.held(stage):
            if self.near_first(part):
                block = self.one(part, group, place.mem)
            else:
                block = self.group(part, group)
            remote(
                block,
                block,
                self.plane_send.at[stage, part],
                self.plane_recv.at[stage, part],
                place.partner(stage),
            ).start()

    def sides(self, step):
        mem, n_mem = self.place.mem, self.place.n_mem
        return (
            ((mem - step >= 0) & (mem + 1 < n_mem), mem - step, 1, mem - 1 - step >= 0),
            ((mem + step < n_mem) & (mem >= 1), mem + step, n_mem - 1, mem + 1 + step < n_mem),
        )

    def line_arrived(self, part, step):
        for side, (_, _, _, receives) in enumerate(self.sides(step)):

            @pl.when(receives)
            def _(side=side):
                self.line_total(part, step, side).wait_recv()

    def spread_line(self, part, step):
        place = self.place
        if step == 0:
            if place.digits == 1:
                self.own(part).wait()
            self.plane_total(part, place.digits - 1).wait_recv()
        else:
            self.line_arrived(part, step - 1)
        for side, (sends, member, towards, _) in enumerate(self.sides(step)):
            member = (member + place.n_mem) % place.n_mem

            @pl.when(sends)
            def _(side=side, member=member, towards=towards):
                for group in self.held(place.digits):
                    block = self.one(part, group, member)
                    remote(
                        block,
                        block,
                        self.line_send.at[2 * step + side, part],
                        self.line_recv.at[2 * step + side, part],
                        place.far(towards),
                    ).start()

    def spread_core(self, part):
        if self.near_first(part):
            self.line_arrived(part, self.place.n_mem - 2)
        else:
            self.plane_total(part, self.place.digits - 1).wait_recv()
        for group in self.held(self.place.digits):
            block = self.group(part, group)
            remote(
                block,
                block,
                self.core_send.at[part],
                self.core_recv.at[part],
                self.place.sibling(),
            ).start()

    def events(self, part):
        digits, n_mem = self.place.digits, self.place.n_mem
        time = float(part)
        found = [(time, functools.partial(self.set_out, part))]
        for stage in range(1 if self.near_first(part) else 0, digits):
            time += 1.6
            found.append((time, functools.partial(self.spread_plane, part, stage)))
        if self.near_first(part):
            time += 1.2
            for step in range(n_mem - 1):
                found.append((time, functools.partial(self.spread_line, part, step)))
                time += 0.8
            time -= 1.4
        time += 1.5
        found.append((time, functools.partial(self.spread_core, part)))
        return found, time + 0.9

    def finish(self):
        for part in range(len(self.parts)):
            for stage in range(self.place.digits):
                self.plane_total(part, stage).wait_send()
            self.core_total(part).wait_send()
            if self.near_first(part):
                for step in range(self.place.n_mem - 1):
                    for side, (sends, _, _, _) in enumerate(self.sides(step)):

                        @pl.when(sends)
                        def _(step=step, side=side, part=part):
                            self.line_total(part, step, side).wait_send()
            else:
                self.far_total(part).wait_send()


class Job:
    def __init__(self, left, right, first, target, far_first=False):
        self.left, self.right, self.first, self.target = left, right, first, target
        self.small = right is None
        self.far_first = far_first
        self.width = target.shape[-1]
        self.at = 0


OUT_SLOTS, LANE_SLOTS, PLANE_SLOTS, CORE_RING, FIRST_RING, RING = 2, 3, 2, 2, 6, 4


class Reduce:
    def __init__(self, place, jobs, sems, wide, small, early):
        self.place, self.jobs, self.wide, self.small, self.early = place, jobs, wide, small, early
        (
            self.core_send,
            self.core_recv,
            self.plane_send,
            self.plane_recv,
            self.far_send,
            self.far_recv,
        ) = sems
        wanted = [place.row]
        for stage in reversed(range(place.digits)):
            wanted = wanted + [place.turn(group, stage) for group in wanted]
        self.wanted = [group // 2 for group in wanted]
        large, plain, other = 0, 0, 0
        for job in jobs:
            if not job.small:
                job.large = large
                large += 1
                if job.far_first:
                    job.at = other
                    other += 1
                else:
                    job.at = plain
                    plain += 1

    def cut(self, ref, job):
        return ref if job.width == ref.shape[-1] else ref.at[:, :, pl.ds(0, job.width)]

    def out(self, job):
        return self.cut(self.wide[0].at[job.large % OUT_SLOTS], job)

    def lanes(self, job):
        if job.small:
            return self.small[1].at[0]
        return self.cut(self.wide[1].at[job.large % LANE_SLOTS], job)

    def core_in(self, job):
        if job.small:
            return self.small[2 + self.place.digits].at[0]
        return self.cut(self.wide[2 + self.place.digits].at[job.large % CORE_RING], job)

    def plane(self, job, stage):
        if job.small:
            return self.small[2 + stage].at[0]
        if job.far_first:
            return self.cut(self.early[1 + stage].at[job.at], job)
        return self.cut(self.wide[2 + stage].at[job.at % PLANE_SLOTS], job)

    def plane_in(self, job, stage):
        digits = self.place.digits
        if job.small:
            return self.small[3 + digits + stage].at[0]
        if job.far_first:
            return self.cut(self.early[1 + digits + stage].at[job.at], job)
        ring = FIRST_RING if stage == 0 else RING
        return self.cut(self.wide[3 + digits + stage].at[job.at % ring], job)

    def far_in(self, job):
        digits = self.place.digits
        if job.small:
            return self.small[3 + 2 * digits].at[0]
        if job.far_first:
            whole = self.early[1 + 2 * digits].at[job.at]
            return whole if job.width == whole.shape[-1] else whole.at[:, :, :, pl.ds(0, job.width)]
        return self.cut(self.wide[3 + 2 * digits].at[job.at % RING], job)

    def far_sum(self, job):
        return self.cut(self.early[0].at[job.at], job)

    def previous(self, number, same, distance):
        found = [n for n in range(number) if same(self.jobs[n])]
        return found[-distance] if len(found) >= distance else None

    def is_large(self, job):
        return not job.small

    def is_plain(self, job):
        return not job.small and not job.far_first

    def core_copy(self, number):
        job = self.jobs[number]
        source = job.left.at[1 - self.place.lane] if job.small else self.out(job)
        return remote(
            source,
            self.core_in(job),
            self.core_send.at[number],
            self.core_recv.at[number],
            self.place.sibling(),
        )

    def product(self, job, side, store):
        half = self.place.n_rows // 2
        group = job.left.shape[1] // half
        width = min(TILE, job.width)

        def column_step(step, carry):
            source = pl.ds(pl.multiple_of(job.first + step * width, width), width)
            value = dot(job.left[side], job.right[:, source])
            for index in range(half):
                store(index, span(step, width), value[index * group : (index + 1) * group])
            return carry

        lax.fori_loop(0, job.width // width, column_step, 0)

    def core_stage(self, number):
        job = self.jobs[number]
        if not job.small:
            before = self.previous(number, self.is_large, OUT_SLOTS)
            if before is not None:
                self.core_copy(before).wait_send()
            out = self.out(job)

            def store(index, columns, value):
                out[index, :, columns] = value.astype(out.dtype)

            self.product(job, 1 - self.place.lane, store)
        self.core_copy(number).start()

    def plane_copy(self, number, stage, which):
        job = self.jobs[number]
        count = 1 << (self.place.digits - 1 - stage)
        if stage == 0:
            source = self.far_sum(job) if job.far_first else self.lanes(job)
            source = source.at[self.wanted[count + which]]
        else:
            source = self.plane(job, stage - 1).at[count + which]
        return remote(
            source,
            self.plane_in(job, stage).at[which],
            self.plane_send.at[stage, number],
            self.plane_recv.at[stage, number],
            self.place.partner(stage),
        )

    def plane_total(self, number, stage):
        some = self.plane_in(self.jobs[number], stage)
        return remote(
            some,
            some,
            self.plane_send.at[stage, number],
            self.plane_recv.at[stage, number],
            self.place.partner(stage),
        )

    def plane_send_out(self, number, stage):
        for which in range(1 << (self.place.digits - 1 - stage)):
            self.plane_copy(number, stage, which).start()

    def lanes_sent(self, number):
        if self.jobs[number].far_first:
            self.far_total(number).wait_send()
        else:
            self.plane_total(number, 0).wait_send()

    def lane_stage(self, number):
        job = self.jobs[number]
        if not job.small:
            before = self.previous(number, self.is_large, LANE_SLOTS)
            if before is not None:
                self.lanes_sent(before)
        lanes, arrived = self.lanes(job), self.core_in(job)
        self.core_copy(number).wait_recv()
        if job.small:
            lanes[...] = job.left[self.place.lane] + arrived[...]
        else:

            def store(index, columns, value):
                total = value + arrived[index, :, columns].astype(jnp.float32)
                lanes[index, :, columns] = total.astype(lanes.dtype)

            self.product(job, self.place.lane, store)
        if job.far_first:
            self.far_send_out(number)
        else:
            self.plane_send_out(number, 0)

    def plane_stage(self, number, stage):
        job, digits = self.jobs[number], self.place.digits
        last = stage == digits - 1
        if self.is_plain(job):
            before = self.previous(number, self.is_plain, PLANE_SLOTS)
            if before is not None and last:
                self.far_total(before).wait_send()
            elif before is not None:
                self.plane_total(before, stage + 1).wait_send()
        self.plane_total(number, stage).wait_recv()
        for which in range(1 << (digits - 1 - stage)):
            if stage == 0:
                mine = self.far_sum(job) if job.far_first else self.lanes(job)
                mine = mine.at[self.wanted[which]]
            else:
                mine = self.plane(job, stage - 1).at[which]
            arrived = self.plane_in(job, stage).at[which]
            total = job.target if job.far_first and last else self.plane(job, stage).at[which]
            block = min(32, mine.shape[0])

            def add(step, carry, mine=mine, arrived=arrived, total=total, block=block):
                rows = span(step, block)
                value = mine[rows].astype(jnp.float32) + arrived[rows].astype(jnp.float32)
                total[rows] = value.astype(total.dtype)
                return carry

            lax.fori_loop(0, mine.shape[0] // block, add, 0)
        if not last:
            self.plane_send_out(number, stage + 1)
        elif not job.far_first:
            self.far_send_out(number)

    def member_rows(self, member):
        size = self.wide[3 + 2 * self.place.digits].shape[2]
        return span(member, size)

    def piece(self, job, member):
        if job.far_first:
            return self.lanes(job).at[:, self.member_rows(member), :]
        whole = self.plane(job, self.place.digits - 1).at[0]
        return whole if job.small else whole.at[self.member_rows(member)]

    def far_copy(self, number, step):
        place, job = self.place, self.jobs[number]
        return remote(
            self.piece(job, (place.mem + step) % place.n_mem),
            self.far_in(job).at[step - 1],
            self.far_send.at[number],
            self.far_recv.at[number],
            place.far(step),
        )

    def far_send_out(self, number):
        for step in range(1, self.place.n_mem):
            self.far_copy(number, step).start()

    def far_total(self, number):
        some = self.far_in(self.jobs[number])
        return remote(
            some, some, self.far_send.at[number], self.far_recv.at[number], self.place.far(1)
        )

    def far_stage(self, number):
        job = self.jobs[number]
        self.far_total(number).wait_recv()
        arrived = self.far_in(job)
        if job.far_first:
            mine, total = self.piece(job, self.place.mem), self.far_sum(job)
            for group in range(total.shape[0]):
                value = mine[group].astype(jnp.float32)
                for step in range(self.place.n_mem - 1):
                    value = value + arrived[step, group].astype(jnp.float32)
                total[group] = value.astype(total.dtype)
            self.plane_send_out(number, 0)
        else:
            value = self.piece(job, self.place.mem)[...].astype(jnp.float32)
            for step in range(self.place.n_mem - 1):
                value = value + arrived[step].astype(jnp.float32)
            job.target[...] = value

    def events(self, number):
        job, digits = self.jobs[number], self.place.digits
        found = [(0.0, functools.partial(self.core_stage, number))]
        found.append((0.9, functools.partial(self.lane_stage, number)))
        stages = [functools.partial(self.plane_stage, number, stage) for stage in range(digits)]
        far = functools.partial(self.far_stage, number)
        time = 2.2 if number < 2 else 3.2
        for action in [far] + stages if job.far_first else stages + [far]:
            found.append((time, action))
            time += 1.4
        found[-1] = (found[-1][0] - 0.3, found[-1][1])
        return [(number + time, action) for time, action in found]

    def finish(self):
        for number, job in enumerate(self.jobs):
            later = range(number + 1, len(self.jobs))
            out = [n for n in later if self.previous(n, self.is_large, OUT_SLOTS) == number]
            lanes = [n for n in later if self.previous(n, self.is_large, LANE_SLOTS) == number]
            plane = [n for n in later if self.previous(n, self.is_plain, PLANE_SLOTS) == number]
            out = [n for n in out if not self.jobs[n].small]
            lanes = [n for n in lanes if not self.jobs[n].small]
            plane = [n for n in plane if self.is_plain(self.jobs[n])]
            if not out or job.small:
                self.core_copy(number).wait_send()
            if not lanes or job.small:
                self.lanes_sent(number)
            if not plane or not self.is_plain(job):
                for stage in range(0 if job.far_first else 1, self.place.digits):
                    self.plane_total(number, stage).wait_send()
                if not job.far_first:
                    self.far_total(number).wait_send()


NORMAL = (((1,), (0,)), ((), ()))
TURNED = (((1,), (1,)), ((), ()))
LEFT_TURNED = (((0,), (0,)), ((), ()))


def dot(left, right, dims=NORMAL):
    return lax.dot_general(left, right, dims, preferred_element_type=jnp.float32)


def times(left, weight, store):
    width = min(TILE, weight.shape[1])

    def column_step(step, carry):
        columns = span(step, width)
        store(columns, dot(left[...], weight[:, columns]))
        return carry

    lax.fori_loop(0, weight.shape[1] // width, column_step, 0)


def times_turned(left, weight, store):
    width = min(TILE, weight.shape[0])

    def column_step(step, carry):
        columns = span(step, width)
        store(columns, dot(left[...], weight[columns, :], TURNED))
        return carry

    lax.fori_loop(0, weight.shape[0] // width, column_step, 0)


def into(target):
    def store(columns, value):
        target[:, columns] = value.astype(target.dtype)

    return store


ROWS = 32


def by_rows(count, step):
    def body(index, carry):
        step(span(index, ROWS))
        return carry

    lax.fori_loop(0, count // ROWS, body, 0)


def norm_forward(total, gains, index, unit, scale, use):
    gain, shift = gains[index : index + 1, :], gains[index + 3 : index + 4, :]

    def step(rows):
        value = total[rows, :]
        centre = value - jnp.mean(value, axis=-1, keepdims=True)
        spread = jnp.mean(centre * centre, axis=-1, keepdims=True)
        root = lax.rsqrt(spread + EPS)
        scaled = centre * root
        unit[rows, :] = scaled
        scale[rows, :] = root
        use(rows, scaled * gain + shift)

    by_rows(total.shape[0], step)


def norm_slope(incoming, scaled, root, gain):
    width = scaled.shape[1]
    scaled_grad = incoming * gain
    first = jnp.mean(scaled_grad, axis=-1, keepdims=True)
    second = jnp.mean(scaled_grad * scaled, axis=-1, keepdims=True)
    value = root * (scaled_grad - first - scaled * second)
    of_gain = jnp.sum((incoming * scaled).reshape(ROWS // 8, 8, width), axis=0)
    of_shift = jnp.sum(incoming.reshape(ROWS // 8, 8, width), axis=0)
    return value, of_gain, of_shift


def keep_small(index, sums, small):
    for offset, partial in ((index, sums[0]), (index + 3, sums[1])):
        line = jnp.sum(partial, axis=0, keepdims=True)
        for group in range(2 * small.shape[1]):
            small[group % 2, group // 2, offset : offset + 1, :] = line[
                :, group * 128 : (group + 1) * 128
            ]


def norm_backward(grad, gains, index, unit, scale, target, target_low, small):
    gain = gains[index : index + 1, :]

    def body(block, sums):
        rows = span(block, ROWS)
        value, of_gain, of_shift = norm_slope(grad[rows, :], unit[rows, :], scale[rows, :], gain)
        target[rows, :] = value
        target_low[rows, :] = value.astype(target_low.dtype)
        return (sums[0] + of_gain, sums[1] + of_shift)

    zero = jnp.zeros((8, unit.shape[1]), jnp.float32)
    keep_small(index, lax.fori_loop(0, unit.shape[0] // ROWS, body, (zero, zero)), small)


def norm_both(total, grad, gains, index, result, target, target_low, small):
    gain, shift = gains[index : index + 1, :], gains[index + 3 : index + 4, :]

    def body(block, sums):
        rows = span(block, ROWS)
        value = total[rows, :]
        centre = value - jnp.mean(value, axis=-1, keepdims=True)
        spread = jnp.mean(centre * centre, axis=-1, keepdims=True)
        root = lax.rsqrt(spread + EPS)
        scaled = centre * root
        result[rows, :] = scaled * gain + shift
        incoming = grad[rows, :].astype(jnp.float32)
        value, of_gain, of_shift = norm_slope(incoming, scaled, root, gain)
        target[rows, :] = value
        target_low[rows, :] = value.astype(target_low.dtype)
        return (sums[0] + of_gain, sums[1] + of_shift)

    zero = jnp.zeros((8, total.shape[1]), jnp.float32)
    keep_small(index, lax.fori_loop(0, total.shape[0] // ROWS, body, (zero, zero)), small)


def lane_masks(dtype):
    low = lax.broadcasted_iota(jnp.int32, (1, 2 * HEAD_DIM), 1) < HEAD_DIM
    first = jnp.where(low, 1.0, 0.0)
    return first.astype(dtype), (1.0 - first).astype(dtype)


def attention_forward(query, keys, values, bias, mixed, lse):
    masks = lane_masks(query.dtype)
    keep = lane_masks(jnp.float32)

    def pair_step(pair, carry):
        lanes = span(pair, 2 * HEAD_DIM)
        two_query, two_keys, two_values = query[:, lanes], keys[:, lanes], values[:, lanes]
        total = None
        for head in range(2):
            scores = dot(two_keys, two_query * masks[head], TURNED) * SCALE + bias[...]
            top = jnp.max(scores, axis=0, keepdims=True)
            weight = jnp.exp(scores - top)
            norm = jnp.sum(weight, axis=0, keepdims=True)
            probs = (weight * (1.0 / norm)).astype(query.dtype)
            part = dot(probs, two_values, LEFT_TURNED) * keep[head]
            total = part if total is None else total + part
            lse[pair, head : head + 1, :] = top + jnp.log(norm)
        mixed[:, lanes] = total.astype(mixed.dtype)
        return carry

    lax.fori_loop(0, lse.shape[0], pair_step, 0)


def attention_backward(
    query, keys, values, bias, lse, grad, query_grad, key_grad, value_grad, first, last
):
    masks = lane_masks(query.dtype)
    keep = lane_masks(jnp.float32)

    def pair_step(pair, carry):
        lanes = span(pair, 2 * HEAD_DIM)
        two_query, two_keys, two_values = query[:, lanes], keys[:, lanes], values[:, lanes]
        two_grad = grad[:, lanes]
        sums = [None, None, None]
        for head in range(2):
            scores = dot(two_keys, two_query * masks[head], TURNED) * SCALE + bias[...]
            probs = jnp.exp(scores - lse[pair, head : head + 1, :])
            pulled = dot(two_values, two_grad * masks[head], TURNED)
            inner = jnp.sum(probs * pulled, axis=0, keepdims=True)
            slope = (probs * (pulled - inner) * SCALE).astype(query.dtype)
            parts = (
                dot(slope, two_keys, LEFT_TURNED),
                dot(slope, two_query),
                dot(probs.astype(query.dtype), two_grad),
            )
            for index, part in enumerate(parts):
                part = part * keep[head]
                sums[index] = part if sums[index] is None else sums[index] + part
        query_grad[:, lanes] = sums[0].astype(query_grad.dtype)
        key_grad[:, lanes] = sums[1].astype(key_grad.dtype)
        value_grad[:, lanes] = sums[2].astype(value_grad.dtype)
        return carry

    lax.fori_loop(first, last, pair_step, 0)


def turn_blocks(left, eye, store):
    width = eye.shape[0]
    for block in range(left.shape[1] // width):
        columns = pl.ds(block * width, width)
        store(block, dot(eye[...], left[:, columns], TURNED).astype(left.dtype))


def turn_by_lane(left, eye, target):
    group = eye.shape[0] // 2

    def store(block, value):
        target[0, pl.ds(block * group, group), :] = value[:group]
        target[1, pl.ds(block * group, group), :] = value[group:]

    turn_blocks(left, eye, store)


SQUARES = 8


def layer_kernel(places, sizes, *refs):
    n_rows, n_mem, width, ff, shard = sizes
    ref = SimpleNamespace(**jax.tree.map(lambda place: refs[place], places))
    place = Place(n_rows, n_mem)
    many = ff // width
    own_ff = ff // (n_rows * n_mem)
    (
        at_query,
        at_key,
        at_value,
        at_output,
        at_cross_query,
        at_cross_key,
        at_cross_value,
        at_cross_output,
    ) = range(SQUARES)
    full = ref.full
    expand, contract = ref.expand_full, ref.contract_full
    tokens, gains = ref.tokens, ref.gains
    low, turned = SimpleNamespace(**ref.low), SimpleNamespace(**ref.turned)

    order = [
        at_query,
        at_key,
        at_value,
        at_output,
        at_cross_key,
        at_cross_value,
        at_cross_query,
        at_cross_output,
    ]
    narrow = width // many
    weights = [(ref.squares[index], full[index], ALL) for index in order]
    weights += [(ref.expand, expand, pl.ds(j * width, width)) for j in range(many)]
    weights += [(ref.contract, contract, pl.ds(j * narrow, narrow)) for j in range(many)]
    near = ()
    parts = [weight + (number in near,) for number, weight in enumerate(weights)]
    parts.insert(SMALL_AT, (ref.small, ref.small_full, ALL, False))
    gather = Gather(place, parts, ref.gather_sems)

    slots, slot_sem = ref.slots, ref.slot_sem
    count = [0]

    def load(pieces):
        number = count[0]
        count[0] += 1
        slot = slots.at[number % SLOTS]
        for source, columns in pieces:
            pltpu.make_async_copy(source, slot.at[:, columns], slot_sem.at[number % SLOTS]).start()
        return number

    def ready(number):
        slot = slots.at[number % SLOTS]
        pltpu.make_async_copy(slot, slot, slot_sem.at[number % SLOTS]).wait()
        return slot

    def expand_block(j):
        return [(expand.at[:, pl.ds(j * width, width)], ALL)]

    def contract_columns(j):
        return [
            (
                contract.at[pl.ds(i * width, width), pl.ds(j * narrow, narrow)],
                pl.ds(i * narrow, narrow),
            )
            for i in range(many)
        ]

    def contract_rows(j):
        return [(contract.at[pl.ds(j * width, width), :], ALL)]

    mem_block = ref.memory.shape[1]
    memory, mem_rows = ref.memory, ref.mem_rows

    def memory_own():
        return pltpu.make_async_copy(
            memory.at[place.mem], mem_rows.at[span(place.mem, mem_block)], ref.mem_sem.at[0]
        )

    def memory_total():
        some = mem_rows.at[pl.ds(0, (n_mem - 1) * mem_block)]
        return remote(some, some, ref.mem_sem.at[1], ref.mem_sem.at[2], place.far(1))

    ref.small[...] = jnp.zeros_like(ref.small)
    for member in range(n_mem):

        @pl.when(place.mem == member)
        def _(member=member):
            lanes = slice(member * shard, (member + 1) * shard)
            ref.small[0:3, lanes] = ref.norm_gains[...].astype(jnp.float32)
            ref.small[3:6, lanes] = ref.norm_shifts[...].astype(jnp.float32)

    place.greet()
    actions = []
    whole = []
    for part in range(len(parts)):
        found, time = gather.events(part)
        actions += found
        whole.append(time)
    actions.sort(key=lambda item: item[0])
    start = [action for action in actions if action[0] < 2]
    actions = actions[len(start) :]
    for _, action in start:
        action()
    memory_own().start()
    for step in range(1, n_mem):
        remote(
            memory.at[(place.mem + step) % n_mem],
            mem_rows.at[span(place.mem, mem_block)],
            ref.mem_sem.at[1],
            ref.mem_sem.at[2],
            place.far(step),
        ).start()

    self_bias, cross_bias, eye = ref.self_bias, ref.cross_bias, ref.eye
    own_row = ref.token_ids[pl.ds(place.mem, 1), :].astype(jnp.float32)
    mem_row = ref.memory_ids[pl.ds(place.mem, 1), :].astype(jnp.float32)
    key_place = lax.broadcasted_iota(jnp.int32, self_bias.shape, 0)
    query_place = lax.broadcasted_iota(jnp.int32, self_bias.shape, 1)
    own_wide = jnp.broadcast_to(own_row, self_bias.shape)
    mem_wide = jnp.broadcast_to(mem_row, (cross_bias.shape[1], cross_bias.shape[0]))
    same = (jnp.transpose(own_wide) == own_wide) & (key_place <= query_place)
    self_bias[...] = jnp.where(same, 0.0, NEG)
    cross_bias[...] = jnp.where(jnp.transpose(mem_wide) == own_row, 0.0, NEG)
    eye_row = lax.broadcasted_iota(jnp.int32, eye.shape, 0)
    eye_column = lax.broadcasted_iota(jnp.int32, eye.shape, 1)
    eye[...] = jnp.where(eye_row == eye_column, 1.0, 0.0).astype(eye.dtype)
    turn_by_lane(tokens, eye, turned.tokens)

    accumulated, other = ref.accumulated, ref.other
    hidden, slope, hidden_turned = ref.hidden, ref.slope, ref.hidden_turned

    def small_piece():
        blocks = ref.small_full
        for group in range(n_rows):
            total = None
            for member in range(n_mem):
                first = (group * n_mem + member) * 8
                value = blocks[first : first + 8, :]
                total = value if total is None else total + value
            gains[:, group * 128 : (group + 1) * 128] = total

    def query_piece(slot):
        times(tokens, slot, into(ref.query))

    def key_piece(slot):
        times(tokens, slot, into(ref.keys))

    def value_piece(slot):
        times(tokens, slot, into(ref.values))
        attention_forward(
            ref.query, ref.keys, ref.values, self_bias, ref.attended, ref.self_lse
        )

    def output_piece(slot):
        def store(columns, value):
            accumulated[:, columns] = ALPHA * tokens[:, columns].astype(jnp.float32) + value

        times(ref.attended, slot, store)

        def use(rows, value):
            ref.first_low[rows, :] = value.astype(jnp.bfloat16)
            other[rows, :] = value

        norm_forward(accumulated, gains, 0, ref.unit1, ref.scale1, use)
        turn_by_lane(ref.attended, eye, turned.attended)

    def cross_key_piece(slot):
        memory_own().wait()
        memory_total().wait_recv()
        times(mem_rows, slot, into(ref.cross_keys))
        turn_by_lane(mem_rows, eye, turned.memory)

    def cross_value_piece(slot):
        times(mem_rows, slot, into(ref.cross_values))
        turn_by_lane(ref.first_low, eye, turned.first)

    def cross_query_piece(slot):
        times(ref.first_low, slot, into(ref.cross_query))
        attention_forward(
            ref.cross_query,
            ref.cross_keys,
            ref.cross_values,
            cross_bias,
            ref.crossed,
            ref.cross_lse,
        )

    def cross_output_piece(slot):
        def store(columns, value):
            accumulated[:, columns] = ALPHA * other[:, columns] + value

        times(ref.crossed, slot, store)

        def use(rows, value):
            ref.second_low[rows, :] = value.astype(jnp.bfloat16)
            other[rows, :] = value

        norm_forward(accumulated, gains, 1, ref.unit2, ref.scale2, use)
        turn_by_lane(ref.crossed, eye, turned.crossed)

    def expand_piece(j, slot):
        def store(columns, value):
            there = pl.ds(pl.multiple_of(j * width + columns.start, TILE), columns.size)
            bell = 0.5 * (1.0 + lax.erf(value * math.sqrt(0.5)))
            density = jnp.exp(value * value * -0.5) * (1.0 / math.sqrt(2.0 * math.pi))
            hidden[:, there] = (value * bell).astype(hidden.dtype)
            slope[:, there] = (bell + value * density).astype(slope.dtype)

        times(ref.second_low, slot, store)

        def keep(block, value):
            for index in range(value.shape[0] // shard):
                first = j * width + block * value.shape[0] + index * shard
                device, job = first // own_ff, first % own_ff // shard
                group, member = device // n_mem, device % n_mem
                at = group // 2 * n_mem * shard + member * shard
                hidden_turned[job, group % 2, at : at + shard, :] = value[
                    index * shard : (index + 1) * shard
                ]

        turn_blocks(hidden.at[:, pl.ds(j * width, width)], eye, keep)

    def contract_piece(j, slot):
        total = None
        for i in range(many):
            value = dot(
                hidden[:, i * width : (i + 1) * width], slot[:, i * narrow : (i + 1) * narrow]
            )
            total = value if total is None else total + value
        columns = pl.ds(j * narrow, narrow)
        accumulated[:, columns] = ALPHA * other[:, columns] + total

    pieces = [
        query_piece,
        key_piece,
        value_piece,
        output_piece,
        cross_key_piece,
        cross_value_piece,
        cross_query_piece,
        cross_output_piece,
    ]
    sources = [[(full[index], ALL)] for index in order]
    for j in range(many):
        pieces.append(functools.partial(expand_piece, j))
        sources.append(expand_block(j))
    for j in range(many):
        pieces.append(functools.partial(contract_piece, j))
        sources.append(contract_columns(j))

    waiting = []

    def arrive(part):
        gather.core_total(part).wait_recv()
        if part != SMALL_AT:
            number = part - (part > SMALL_AT)
            waiting.append((number, load(sources[number])))

    def use():
        number, slot = waiting.pop(0)
        pieces[number](ready(slot))

    last = 0.0
    for part, time in enumerate(whole):
        time = max(time, last + 0.2)
        actions.append((time, functools.partial(arrive, part)))
        actions.append((time + 0.5, small_piece if part == SMALL_AT else use))
        last = time
    actions.sort(key=lambda item: item[0])
    for _, action in actions:
        action()

    backward_sources, loads = [], []
    used = [0]

    def next_slot():
        slot = ready(loads[used[0]])
        used[0] += 1
        if len(loads) < len(backward_sources):
            loads.append(load(backward_sources[len(loads)]))
        return slot

    small_sums = ref.small_sums
    small_sums[...] = jnp.zeros_like(small_sums)
    def inner_piece(j):
        slot = next_slot()

        def store(columns, value):
            there = pl.ds(pl.multiple_of(j * width + columns.start, TILE), columns.size)
            slope[:, there] = (value * slope[:, there].astype(jnp.float32)).astype(slope.dtype)

        times_turned(low.third, slot, store)

    def second_piece(j):
        slot = next_slot()

        def store(columns, value):
            if j == 0:
                other[:, columns] = ALPHA * accumulated[:, columns] + value
            else:
                other[:, columns] = other[:, columns] + value

        times_turned(slope.at[:, pl.ds(j * width, width)], slot, store)

    def second_norm_piece():
        norm_backward(
            other, gains, 1, ref.unit2, ref.scale2, accumulated, low.second, small_sums
        )

    pairs = width // (2 * HEAD_DIM)

    def cross_start_piece():
        times_turned(low.second, next_slot(), into(low.branch))

    def cross_piece(first, last):
        attention_backward(
            ref.cross_query,
            ref.cross_keys,
            ref.cross_values,
            cross_bias,
            ref.cross_lse,
            low.branch,
            low.cross_query,
            low.cross_key,
            low.cross_value,
            first,
            last,
        )

    def first_piece():
        def store(columns, value):
            other[:, columns] = ALPHA * accumulated[:, columns] + value

        times_turned(low.cross_query, next_slot(), store)
        norm_backward(other, gains, 0, ref.unit1, ref.scale1, accumulated, low.first, small_sums)

    def self_start_piece():
        times_turned(low.first, next_slot(), into(low.branch))

    def self_piece(first, last):
        attention_backward(
            ref.query,
            ref.keys,
            ref.values,
            self_bias,
            ref.self_lse,
            low.branch,
            low.query,
            low.key,
            low.value,
            first,
            last,
        )

    mem_out, mem_in = ref.mem_out, ref.mem_in

    def grad_own():
        return pltpu.make_async_copy(
            mem_out.at[span(place.mem, mem_block)], mem_in.at[place.mem], ref.mem_sem.at[3]
        )

    def grad_total():
        some = mem_in.at[pl.ds(0, n_mem - 1)]
        return remote(some, some, ref.mem_sem.at[4], ref.mem_sem.at[5], place.far(1))

    def memory_key_piece():
        times_turned(low.cross_key, next_slot(), into(other))

    def memory_value_piece():
        def store(columns, value):
            mem_out[:, columns] = (other[:, columns] + value).astype(mem_out.dtype)

        times_turned(low.cross_value, next_slot(), store)
        grad_own().start()
        for step in range(1, n_mem):
            remote(
                mem_out.at[span((place.mem + step) % n_mem, mem_block)],
                mem_in.at[place.mem],
                ref.mem_sem.at[4],
                ref.mem_sem.at[5],
                place.far(step),
            ).start()

    def input_piece(left, start):
        target = ref.input_grad

        def store(columns, value):
            if start:
                target[:, columns] = ALPHA * accumulated[:, columns] + value
            else:
                target[:, columns] = target[:, columns] + value

        times_turned(left, next_slot(), store)

    def memory_end_piece():
        grad_own().wait()
        grad_total().wait_recv()
        for member in range(n_mem):
            ref.memory_grad[member] = mem_in[member].astype(jnp.float32)

    def contract_job(j, first, columns, far_first=False):
        target = ref.contract_grad.at[pl.ds(j * shard, shard), pl.ds(first, columns)]
        return Job(hidden_turned.at[j], low.third, first, target, far_first)

    halves = ((0, width // 2), (width // 2, width // 2))
    jobs = [contract_job(0, *half) for half in halves]
    jobs += [contract_job(j, 0, width) for j in range(1, many)]
    for j in range(many):
        columns = pl.ds(j * width, width)
        jobs.append(Job(turned.second, slope, j * width, ref.expand_grad.at[:, columns]))
    grads = ref.grads
    jobs += [
        Job(turned.crossed, low.second, 0, grads[at_cross_output]),
        Job(turned.memory, low.cross_key, 0, grads[at_cross_key]),
        Job(turned.memory, low.cross_value, 0, grads[at_cross_value]),
        Job(turned.first, low.cross_query, 0, grads[at_cross_query]),
        Job(turned.attended, low.first, 0, grads[at_output]),
        Job(small_sums, None, 0, ref.small_total),
        Job(turned.tokens, low.query, 0, grads[at_query]),
        Job(turned.tokens, low.key, 0, grads[at_key]),
    ]
    for first, columns in halves:
        target = grads[at_value].at[:, pl.ds(first, columns)]
        jobs.append(Job(turned.tokens, low.value, first, target))
    reduce = Reduce(place, jobs, ref.reduce_sems, ref.wide, ref.little, ref.early)

    inner = [functools.partial(inner_piece, j) for j in range(many)]
    second = [functools.partial(second_piece, j) for j in range(many)]
    middle = pairs // 2
    base = many + 1
    def weight(index):
        return [(full[index], ALL)]

    turn = functools.partial(turn_by_lane, ref.second_low, eye, turned.second)
    work = [(base - 1.7, inner[0], contract_rows(0)), (base - 1.3, turn, None)]
    work += [(base - 1.7 + j, inner[j], contract_rows(j)) for j in range(1, many)]
    work += [(base - 0.3 + j, second[j], expand_block(j)) for j in range(many)]
    base = 2 * many + 1
    work += [
        (base - 0.2, second_norm_piece, None),
        (base - 0.15, cross_start_piece, weight(at_cross_output)),
        (base + 0.3, functools.partial(cross_piece, 0, middle), None),
        (base + 0.7, functools.partial(cross_piece, middle, pairs), None),
        (base + 1.3, first_piece, weight(at_cross_query)),
        (base + 1.7, self_start_piece, weight(at_output)),
        (base + 2.3, functools.partial(self_piece, 0, middle), None),
        (base + 3.3, functools.partial(self_piece, middle, pairs), None),
        (base + 3.7, memory_key_piece, weight(at_cross_key)),
        (base + 4.3, memory_value_piece, weight(at_cross_value)),
        (base + 4.7, functools.partial(input_piece, low.query, True), weight(at_query)),
        (base + 5.5, functools.partial(input_piece, low.key, False), weight(at_key)),
        (base + 6.5, functools.partial(input_piece, low.value, False), weight(at_value)),
        (base + 8.5, memory_end_piece, None),
    ]
    work.sort(key=lambda item: item[0])
    backward_sources += [source for _, _, source in work if source is not None]
    loads += [load(backward_sources[0]), load(backward_sources[1])]
    norm_both(
        accumulated, ref.out_grad, gains, 2, ref.result, accumulated, low.third, small_sums
    )

    actions = [(time, piece) for time, piece, _ in work]
    for number in range(len(jobs)):
        actions += reduce.events(number)
    actions.sort(key=lambda item: item[0])
    for _, action in actions:
        action()

    total = ref.small_total[...]
    own = jnp.zeros((8, shard), jnp.float32)
    for member in range(n_mem):
        here = jnp.where(place.mem == member, 1.0, 0.0)
        own = own + here * total[:, member * shard : (member + 1) * shard]
    ref.gains_grad[...] = own[0:3]
    ref.shifts_grad[...] = own[3:6]
    gather.finish()
    reduce.finish()
    memory_total().wait_send()
    grad_total().wait_send()


SMALL_AT = 2


def copy_kernel(count, *refs):
    for source, target in zip(refs[:count], refs[count:]):
        target[...] = source[...]


def copied(values):
    near = pl.BlockSpec(memory_space=pltpu.VMEM)
    return pl.pallas_call(
        functools.partial(copy_kernel, len(values)),
        out_shape=[jax.ShapeDtypeStruct(value.shape, value.dtype) for value in values],
        in_specs=[near] * len(values),
        out_specs=[near] * len(values),
        compiler_params=pltpu.CompilerParams(vmem_limit_bytes=VMEM_LIMIT),
        name="results",
    )(*values)


def fused(n_rows, n_mem, ins):
    tokens, memory, squares = ins["tokens"], ins["memory"], ins["squares"]
    expand, contract = ins["expand"], ins["contract"]
    tokens_here, width = tokens.shape
    ff = expand.shape[1]
    shard = squares[0].shape[0]
    mem_tokens = memory.shape[0] * memory.shape[1]
    digits, half, many = (n_rows // 2).bit_length() - 1, n_rows // 2, ff // width
    pairs = width // (2 * HEAD_DIM)
    low, high = jnp.bfloat16, jnp.float32
    n_parts = 1 + SQUARES + 2 * many
    n_jobs = n_parts + 2
    dma, vmem = pltpu.SemaphoreType.DMA, pltpu.VMEM
    anywhere, near = pl.BlockSpec(memory_space=pl.ANY), pl.BlockSpec(memory_space=pltpu.VMEM)

    far_ins = dict(memory=memory, squares=squares, expand=expand, contract=contract)
    in_specs = {
        name: jax.tree.map(lambda _: anywhere if name in far_ins else near, value)
        for name, value in ins.items()
    }

    def out(shape, dtype=high):
        return jax.ShapeDtypeStruct(shape, dtype)

    outs = dict(
        result=out(tokens.shape),
        input_grad=out(tokens.shape),
        memory_grad=out(memory.shape),
        grads=[out(item.shape) for item in squares],
        expand_grad=out(expand.shape),
        contract_grad=out(contract.shape),
        gains_grad=out((3, shard)),
        shifts_grad=out((3, shard)),
    )
    far_outs = dict(
        full=[out((width, width), low)] * SQUARES,
        expand_full=out((width, ff), low),
        contract_full=out((ff, width), low),
    )
    out_specs = jax.tree.map(lambda _: near, outs)
    out_specs.update(jax.tree.map(lambda _: anywhere, far_outs))
    outs.update(far_outs)

    def token_rows(dtype):
        return vmem((tokens_here, width), dtype)

    def memory_rows(dtype):
        return vmem((mem_tokens, width), dtype)

    counts = [1 << (digits - 1 - stage) for stage in range(digits)]
    group, tiny = (n_mem * shard, width), (8, 128)
    wide = [(OUT_SLOTS, half) + group, (LANE_SLOTS, half) + group]
    wide += [(PLANE_SLOTS, count) + group for count in counts]
    wide += [(CORE_RING, half) + group]
    wide += [(RING if i else FIRST_RING, count) + group for i, count in enumerate(counts)]
    wide += [(RING, n_mem - 1, shard, width)]
    little = [(1, 1) + tiny, (1, half) + tiny]
    little += [(1, count) + tiny for count in counts]
    little += [(1, half) + tiny]
    little += [(1, count) + tiny for count in counts]
    little += [(1, n_mem - 1) + tiny]
    early = [(2, half, shard, width)]
    early += [(2, count, shard, width) for count in counts]
    early += [(2, count, shard, width) for count in counts]
    early += [(2, n_mem - 1, half, shard, width)]
    left = vmem((2, width // 2, tokens_here), low)
    scratch = dict(
        small=vmem(tiny, high),
        small_full=vmem((n_rows * n_mem * 8, 128), high),
        small_total=vmem(tiny, high),
        slots=vmem((SLOTS, width, width), low),
        slot_sem=dma((SLOTS,)),
        mem_sem=dma((6,)),
        gather_sems=[
            dma(shape + (n_parts,))
            for shape in ((), (), (), (digits,), (digits,), (), ())
            + ((2 * (n_mem - 1),), (2 * (n_mem - 1),))
        ],
        reduce_sems=[
            dma(shape + (n_jobs,)) for shape in ((), (), (digits,), (digits,), (), ())
        ],
        gains=vmem((8, width), high),
        query=token_rows(low),
        keys=token_rows(low),
        values=token_rows(low),
        attended=token_rows(low),
        first_low=token_rows(low),
        second_low=token_rows(low),
        cross_query=token_rows(low),
        crossed=token_rows(low),
        cross_keys=memory_rows(low),
        cross_values=memory_rows(low),
        mem_rows=memory_rows(low),
        mem_out=memory_rows(low),
        mem_in=vmem(memory.shape, low),
        unit1=token_rows(high),
        unit2=token_rows(high),
        accumulated=token_rows(high),
        other=token_rows(high),
        scale1=vmem((tokens_here, 1), high),
        scale2=vmem((tokens_here, 1), high),
        self_bias=vmem((tokens_here, tokens_here), high),
        cross_bias=vmem((mem_tokens, tokens_here), high),
        self_lse=vmem((pairs, 2, tokens_here), high),
        cross_lse=vmem((pairs, 2, tokens_here), high),
        eye=vmem((TILE, TILE), low),
        hidden=vmem((tokens_here, ff), low),
        slope=vmem((tokens_here, ff), low),
        hidden_turned=vmem((many, 2, width // 2, tokens_here), low),
        turned=dict(
            tokens=left, attended=left, first=left, memory=left, crossed=left, second=left
        ),
        low=dict(
            third=token_rows(low),
            second=token_rows(low),
            first=token_rows(low),
            branch=token_rows(low),
            cross_query=token_rows(low),
            cross_key=memory_rows(low),
            cross_value=memory_rows(low),
            query=token_rows(low),
            key=token_rows(low),
            value=token_rows(low),
        ),
        small_sums=vmem((2, half) + tiny, high),
        wide=[vmem(shape, low) for shape in wide],
        little=[vmem(shape, high) for shape in little],
        early=[vmem(shape, low) for shape in early],
    )
    in_values, in_tree = jax.tree.flatten(ins)
    out_shapes, out_tree = jax.tree.flatten(outs)
    scratch_shapes, scratch_tree = jax.tree.flatten(scratch)
    places = jax.tree.unflatten(in_tree, range(len(in_values)))
    at = len(in_values)
    places.update(jax.tree.unflatten(out_tree, range(at, at + len(out_shapes))))
    at += len(out_shapes)
    places.update(jax.tree.unflatten(scratch_tree, range(at, at + len(scratch_shapes))))
    values = pl.pallas_call(
        functools.partial(layer_kernel, places, (n_rows, n_mem, width, ff, shard)),
        out_shape=out_shapes,
        in_specs=jax.tree.leaves(in_specs),
        out_specs=jax.tree.leaves(out_specs),
        scratch_shapes=scratch_shapes,
        compiler_params=pltpu.CompilerParams(
            collective_id=0, has_side_effects=True, vmem_limit_bytes=VMEM_LIMIT
        ),
        name="layer",
    )(*in_values)
    found = jax.tree.unflatten(out_tree, values)
    for name in far_outs:
        del found[name]
    return found


def local(n_rows, n_mem, *args):
    (
        tokens,
        memory,
        token_ids,
        memory_ids,
        out_grad,
        self_query,
        self_key,
        self_value,
        self_output,
        cross_query,
        cross_key,
        cross_value,
        cross_output,
        expand_weight,
        contract_weight,
        norm_gains,
        norm_shifts,
    ) = args
    shard, width = self_query.shape
    suits = width == 128 * n_rows and shard % 16 == 0 and tokens.shape[0] == 1
    if not suits or n_rows < 4 or n_rows & (n_rows - 1) or n_mem < 2:
        return plain(*args)
    found = fused(
        n_rows,
        n_mem,
        dict(
            tokens=tokens[0],
            memory=memory,
            token_ids=token_ids,
            memory_ids=memory_ids,
            out_grad=out_grad[0],
            squares=[
                self_query,
                self_key,
                self_value,
                self_output,
                cross_query,
                cross_key,
                cross_value,
                cross_output,
            ],
            expand=expand_weight,
            contract=contract_weight,
            norm_gains=norm_gains,
            norm_shifts=norm_shifts,
        ),
    )
    values, tree = jax.tree.flatten(found)
    found = SimpleNamespace(**jax.tree.unflatten(tree, copied(values)))
    return (
        found.result[None],
        found.input_grad[None],
        found.memory_grad,
        *found.grads,
        found.expand_grad,
        found.contract_grad,
        found.gains_grad,
        found.shifts_grad,
    )


def solution(mesh):
    in_specs = (
        P(("rows", "mem"), None, None),
        P("rows", "mem", None),
        P("rows", None),
        P("rows", None),
        P(("rows", "mem"), None, None),
        P(("rows", "mem"), None),
        P(("rows", "mem"), None),
        P(("rows", "mem"), None),
        P(("rows", "mem"), None),
        P(("rows", "mem"), None),
        P(("rows", "mem"), None),
        P(("rows", "mem"), None),
        P(("rows", "mem"), None),
        P(("rows", "mem"), None),
        P(("rows", "mem"), None),
        P(None, ("rows", "mem")),
        P(None, ("rows", "mem")),
    )
    out_specs = (
        P(("rows", "mem"), None, None),
        P(("rows", "mem"), None, None),
        P("rows", "mem", None),
        P(("rows", "mem"), None),
        P(("rows", "mem"), None),
        P(("rows", "mem"), None),
        P(("rows", "mem"), None),
        P(("rows", "mem"), None),
        P(("rows", "mem"), None),
        P(("rows", "mem"), None),
        P(("rows", "mem"), None),
        P(("rows", "mem"), None),
        P(("rows", "mem"), None),
        P(None, ("rows", "mem")),
        P(None, ("rows", "mem")),
    )
    layer = functools.partial(local, mesh.shape["rows"], mesh.shape["mem"])
    return jax.shard_map(layer, mesh=mesh, in_specs=in_specs, out_specs=out_specs, check_vma=False)
```

```python
import functools
import math
from types import SimpleNamespace

import jax
import jax.numpy as jnp
from jax import lax
from jax.experimental import pallas as pl
from jax.experimental.pallas import tpu as pltpu
from jax.sharding import PartitionSpec as P

MESH = pl.DeviceIdType.MESH

HEADS = 16
HEAD_DIM = 64


ALPHA = 4.16
EPS = 1e-05
SCALE = 0.125
NEG = -1e30


def layer_norm(hidden_activation, gain, shift):
    centre = hidden_activation - jnp.mean(hidden_activation, axis=-1, keepdims=True)
    spread = jnp.mean(centre * centre, axis=-1, keepdims=True)
    return centre * lax.rsqrt(spread + EPS) * gain + shift


def gelu_exact(value):
    return jax.nn.gelu(value, approximate=False)


def product(left, right):
    return jnp.dot(left, right, preferred_element_type=jnp.float32)


def split_heads(matrix):
    return matrix.reshape(matrix.shape[0], matrix.shape[1] // HEAD_DIM, HEAD_DIM)


def grouped(matrix):
    return jnp.moveaxis(matrix.reshape(matrix.shape[0], HEADS // 4, 4 * HEAD_DIM), 1, 0)


def ungrouped(stack):
    return jnp.moveaxis(stack, 0, 1).reshape(stack.shape[1], stack.shape[0] * stack.shape[2])


def row_map(function, items):
    return lax.map(lambda entry: function(*entry), items)


def score_block(query, keys, allowed):
    raw = jnp.einsum(
        "khe,qhe->hkq", split_heads(keys), split_heads(query), preferred_element_type=jnp.float32
    )
    return jnp.where(allowed[None], raw * SCALE, NEG)


def attend_probs(query, keys, allowed, lse):
    scores = score_block(query, keys, allowed)
    return jnp.where(allowed[None], jnp.exp(scores - lse[:, None, :]), 0.0)


def attend_forward(query, keys, values, allowed):
    scores = score_block(query, keys, allowed)
    top = jnp.max(scores, axis=1)
    weight = jnp.where(allowed[None], jnp.exp(scores - top[:, None, :]), 0.0)
    total = jnp.sum(weight, axis=1)
    probs = (weight / total[:, None, :]).astype(jnp.bfloat16)
    mixed = jnp.einsum(
        "hkq,khe->qhe", probs, split_heads(values), preferred_element_type=jnp.float32
    )
    return (mixed.reshape(query.shape), top + jnp.log(total))


def value_pull(grad, values):
    return jnp.einsum(
        "qhe,khe->hkq", split_heads(grad), split_heads(values), preferred_element_type=jnp.float32
    )


def score_grads(probs, pulled, inner):
    return (probs * (pulled - inner[:, None, :]) * SCALE).astype(jnp.bfloat16)


def query_from(score_grad, keys, shape):
    moved = jnp.einsum(
        "hkq,khe->qhe", score_grad, split_heads(keys), preferred_element_type=jnp.float32
    )
    return moved.reshape(shape)


def key_from(score_grad, query, shape):
    moved = jnp.einsum(
        "hkq,qhe->khe", score_grad, split_heads(query), preferred_element_type=jnp.float32
    )
    return moved.reshape(shape)


def value_from(probs, grad, values):
    moved = jnp.einsum(
        "hkq,qhe->khe",
        probs.astype(jnp.bfloat16),
        split_heads(grad),
        preferred_element_type=jnp.float32,
    )
    return moved.reshape(values.shape)


def local_forward(query, keys, values, allowed):

    def one_group(items):
        return attend_forward(items[0], items[1], items[2], allowed)

    mixed, lse = lax.map(one_group, (grouped(query), grouped(keys), grouped(values)))
    return (ungrouped(mixed), lse)


def local_backward(query, keys, values, allowed, lse, grad):

    def one_group(items):
        part_query, part_keys, part_values, part_lse, part_grad = items
        probs = attend_probs(part_query, part_keys, allowed, part_lse)
        pulled = value_pull(part_grad, part_values)
        inner = jnp.sum(probs * pulled, axis=1)
        score_grad = score_grads(probs, pulled, inner)
        return (
            query_from(score_grad, part_keys, part_query.shape),
            key_from(score_grad, part_query, part_keys.shape),
            value_from(probs, part_grad, part_values),
        )

    parts = lax.map(one_group, (grouped(query), grouped(keys), grouped(values), lse, grouped(grad)))
    return (ungrouped(parts[0]), ungrouped(parts[1]), ungrouped(parts[2]))


def plain(
    tokens,
    memory,
    token_ids,
    memory_ids,
    out_grad,
    self_query,
    self_key,
    self_value,
    self_output,
    cross_query,
    cross_key,
    cross_value,
    cross_output,
    expand_weight,
    contract_weight,
    norm_gains,
    norm_shifts,
):
    full = (
        lax.all_gather(self_query, ("rows", "mem"), axis=0, tiled=True),
        lax.all_gather(self_key, ("rows", "mem"), axis=0, tiled=True),
        lax.all_gather(self_value, ("rows", "mem"), axis=0, tiled=True),
        lax.all_gather(self_output, ("rows", "mem"), axis=0, tiled=True),
        lax.all_gather(cross_query, ("rows", "mem"), axis=0, tiled=True),
        lax.all_gather(cross_key, ("rows", "mem"), axis=0, tiled=True),
        lax.all_gather(cross_value, ("rows", "mem"), axis=0, tiled=True),
        lax.all_gather(cross_output, ("rows", "mem"), axis=0, tiled=True),
        lax.all_gather(expand_weight, ("rows", "mem"), axis=0, tiled=True),
        lax.all_gather(contract_weight, ("rows", "mem"), axis=0, tiled=True),
        lax.all_gather(jnp.transpose(norm_gains), ("rows", "mem"), axis=0, tiled=True),
        lax.all_gather(jnp.transpose(norm_shifts), ("rows", "mem"), axis=0, tiled=True),
    )
    (
        self_attention_query,
        decoder_match_label,
        self_attention_value,
        self_attention_output,
        encoder_lookup_probe,
        key_cross,
        value_cross,
        cross_attention_output,
        up_projection,
        narrowing_matrix,
        gain_cols,
        shift_cols,
    ) = full
    gain_rows = jnp.transpose(gain_cols).astype(jnp.float32)
    shift_rows = jnp.transpose(shift_cols).astype(jnp.float32)
    rows_here = tokens.shape[0]
    member = lax.axis_index("mem")
    own_ids = lax.dynamic_slice_in_dim(token_ids, member * rows_here, rows_here, 0)
    positions = jnp.arange(tokens.shape[1], dtype=jnp.int32)
    self_allowed = (own_ids[:, :, None] == own_ids[:, None, :]) & (
        positions[:, None] <= positions[None, :]
    )[None]
    query = product(tokens, self_attention_query).astype(jnp.bfloat16)
    keys = product(tokens, decoder_match_label).astype(jnp.bfloat16)
    values = product(tokens, self_attention_value).astype(jnp.bfloat16)
    self_mixed, self_lse = row_map(local_forward, (query, keys, values, self_allowed))
    attention_result = self_mixed.astype(jnp.bfloat16)
    first, first_back = jax.vjp(
        layer_norm,
        ALPHA * tokens.astype(jnp.float32) + product(attention_result, self_attention_output),
        gain_rows[0],
        shift_rows[0],
    )
    first_reduced = first.astype(jnp.bfloat16)
    cross_queries = product(first_reduced, encoder_lookup_probe).astype(jnp.bfloat16)
    memory_rows = lax.all_to_all(memory, "mem", split_axis=0, concat_axis=1, tiled=True)
    row_ids = lax.dynamic_slice_in_dim(memory_ids, member * rows_here, rows_here, 0)
    cross_allowed = row_ids[:, :, None] == own_ids[:, None, :]
    cross_keys = product(memory_rows, key_cross).astype(jnp.bfloat16)
    cross_values = product(memory_rows, value_cross).astype(jnp.bfloat16)
    cross_mixed, cross_lse = row_map(
        local_forward, (cross_queries, cross_keys, cross_values, cross_allowed)
    )
    cross_attention_result = cross_mixed.astype(jnp.bfloat16)
    second, second_back = jax.vjp(
        layer_norm,
        ALPHA * first + product(cross_attention_result, cross_attention_output),
        gain_rows[1],
        shift_rows[1],
    )
    second_reduced = second.astype(jnp.bfloat16)
    hidden_value, gelu_back = jax.vjp(gelu_exact, product(second_reduced, up_projection))
    hidden_activation = hidden_value.astype(jnp.bfloat16)
    result, third_back = jax.vjp(
        layer_norm,
        ALPHA * second + product(hidden_activation, narrowing_matrix),
        gain_rows[2],
        shift_rows[2],
    )
    third_grad, gain_three, shift_three = third_back(out_grad.astype(jnp.float32))
    feedforward_gradient = third_grad.astype(jnp.bfloat16)
    down_projection_gradient = jnp.einsum(
        "ehj,ehc->jc", hidden_activation, feedforward_gradient, preferred_element_type=jnp.float32
    )
    (inner_grad,) = gelu_back(
        jnp.einsum(
            "hpu,ku->hpk",
            feedforward_gradient,
            narrowing_matrix,
            preferred_element_type=jnp.float32,
        )
    )
    inner_reduced = inner_grad.astype(jnp.bfloat16)
    expand_grad = jnp.einsum(
        "iqg,iqe->ge", second_reduced, inner_reduced, preferred_element_type=jnp.float32
    )
    second_total = ALPHA * third_grad + jnp.einsum(
        "iwm,fm->iwf", inner_reduced, up_projection, preferred_element_type=jnp.float32
    )
    second_grad, gain_two, shift_two = second_back(second_total)
    cross_branch_gradient = second_grad.astype(jnp.bfloat16)
    output_cross_grad = jnp.einsum(
        "nhb,nhc->bc",
        cross_attention_result,
        cross_branch_gradient,
        preferred_element_type=jnp.float32,
    )
    crossed_grad = jnp.einsum(
        "qwp,up->qwu",
        cross_branch_gradient,
        cross_attention_output,
        preferred_element_type=jnp.float32,
    ).astype(jnp.bfloat16)
    query_grads, key_grads, value_grads = row_map(
        local_backward,
        (cross_queries, cross_keys, cross_values, cross_allowed, cross_lse, crossed_grad),
    )
    key_low = key_grads.astype(jnp.bfloat16)
    value_low = value_grads.astype(jnp.bfloat16)
    row_grad = jnp.einsum(
        "sme,de->smd", key_low, key_cross, preferred_element_type=jnp.float32
    ) + jnp.einsum("sme,de->smd", value_low, value_cross, preferred_element_type=jnp.float32)
    key_cross_grad = jnp.einsum(
        "smd,sme->de", memory_rows, key_low, preferred_element_type=jnp.float32
    )
    value_cross_grad = jnp.einsum(
        "smd,sme->de", memory_rows, value_low, preferred_element_type=jnp.float32
    )
    memory_grad = lax.all_to_all(
        row_grad.astype(jnp.bfloat16), "mem", split_axis=1, concat_axis=0, tiled=True
    ).astype(row_grad.dtype)
    probe_lowered_precision = query_grads.astype(jnp.bfloat16)
    query_cross_grad = jnp.einsum(
        "nhb,nhc->bc", first_reduced, probe_lowered_precision, preferred_element_type=jnp.float32
    )
    first_total = ALPHA * second_grad + jnp.einsum(
        "qwp,up->qwu",
        probe_lowered_precision,
        encoder_lookup_probe,
        preferred_element_type=jnp.float32,
    )
    first_grad, gain_one, shift_one = first_back(first_total)
    self_branch_gradient = first_grad.astype(jnp.bfloat16)
    output_self_grad = jnp.einsum(
        "nhb,nhc->bc", attention_result, self_branch_gradient, preferred_element_type=jnp.float32
    )
    attended_grad = jnp.einsum(
        "qwp,up->qwu",
        self_branch_gradient,
        self_attention_output,
        preferred_element_type=jnp.float32,
    ).astype(jnp.bfloat16)
    self_query_reduced, decoder_label_lowered, self_value_reduced = row_map(
        local_backward, (query, keys, values, self_allowed, self_lse, attended_grad)
    )
    self_query_reduced = self_query_reduced.astype(jnp.bfloat16)
    decoder_label_lowered = decoder_label_lowered.astype(jnp.bfloat16)
    self_value_reduced = self_value_reduced.astype(jnp.bfloat16)
    query_self_grad = jnp.einsum(
        "nhb,nhc->bc", tokens, self_query_reduced, preferred_element_type=jnp.float32
    )
    key_self_grad = jnp.einsum(
        "nhb,nhc->bc", tokens, decoder_label_lowered, preferred_element_type=jnp.float32
    )
    value_self_grad = jnp.einsum(
        "nhb,nhc->bc", tokens, self_value_reduced, preferred_element_type=jnp.float32
    )
    input_grad = (
        ALPHA * first_grad
        + jnp.einsum(
            "qwp,up->qwu",
            self_query_reduced,
            self_attention_query,
            preferred_element_type=jnp.float32,
        )
        + jnp.einsum(
            "qwp,up->qwu",
            decoder_label_lowered,
            decoder_match_label,
            preferred_element_type=jnp.float32,
        )
        + jnp.einsum(
            "qwp,up->qwu",
            self_value_reduced,
            self_attention_value,
            preferred_element_type=jnp.float32,
        )
    )
    gain_grad = jnp.stack([gain_one, gain_two, gain_three], axis=1)
    shift_grad = jnp.stack([shift_one, shift_two, shift_three], axis=1)
    sums = (
        lax.psum_scatter(query_self_grad, ("rows", "mem"), scatter_dimension=0, tiled=True),
        lax.psum_scatter(key_self_grad, ("rows", "mem"), scatter_dimension=0, tiled=True),
        lax.psum_scatter(value_self_grad, ("rows", "mem"), scatter_dimension=0, tiled=True),
        lax.psum_scatter(output_self_grad, ("rows", "mem"), scatter_dimension=0, tiled=True),
        lax.psum_scatter(query_cross_grad, ("rows", "mem"), scatter_dimension=0, tiled=True),
        lax.psum_scatter(key_cross_grad, ("rows", "mem"), scatter_dimension=0, tiled=True),
        lax.psum_scatter(value_cross_grad, ("rows", "mem"), scatter_dimension=0, tiled=True),
        lax.psum_scatter(output_cross_grad, ("rows", "mem"), scatter_dimension=0, tiled=True),
        lax.psum_scatter(expand_grad, ("rows", "mem"), scatter_dimension=0, tiled=True),
        lax.psum_scatter(
            down_projection_gradient, ("rows", "mem"), scatter_dimension=0, tiled=True
        ),
        lax.psum_scatter(gain_grad, ("rows", "mem"), scatter_dimension=0, tiled=True),
        lax.psum_scatter(shift_grad, ("rows", "mem"), scatter_dimension=0, tiled=True),
    )
    return (
        result,
        input_grad,
        memory_grad,
        sums[0],
        sums[1],
        sums[2],
        sums[3],
        sums[4],
        sums[5],
        sums[6],
        sums[7],
        sums[8],
        sums[9],
        jnp.transpose(sums[10]),
        jnp.transpose(sums[11]),
    )


ALL = slice(None)
TILE = 256
SLOTS = 3
VMEM_LIMIT = 61 * 1024 * 1024


def flip(index, unit):
    return index + unit * (1 - 2 * ((index // unit) % 2))


def span(index, size):
    return pl.ds(pl.multiple_of(index * size, size), size)


class Place:
    def __init__(self, n_rows, n_mem):
        self.n_rows, self.n_mem = n_rows, n_mem
        self.digits = (n_rows // 2).bit_length() - 1
        self.row = lax.axis_index("rows")
        self.mem = lax.axis_index("mem")
        self.lane = self.row % 2

    def turn(self, index, stage):
        rising, falling = 2 << stage, 2 << (self.digits - 1 - stage)
        return flip(index, rising) * (1 - self.lane) + flip(index, falling) * self.lane

    def sibling(self):
        return (flip(self.row, 1), self.mem)

    def partner(self, stage):
        return (self.turn(self.row, stage), self.mem)

    def far(self, step):
        return (self.row, (self.mem + step) % self.n_mem)

    def greet(self):
        barrier = pltpu.get_barrier_semaphore()
        others = [self.far(step) for step in range(1, self.n_mem)]
        others += [self.partner(stage) for stage in range(self.digits)]
        others += [self.sibling()]
        for other in others:
            pl.semaphore_signal(barrier, inc=1, device_id=other, device_id_type=MESH)
        pl.semaphore_wait(barrier, len(others))


def remote(source, target, send_sem, recv_sem, device):
    return pltpu.make_async_remote_copy(
        src_ref=source,
        dst_ref=target,
        send_sem=send_sem,
        recv_sem=recv_sem,
        device_id=device,
        device_id_type=MESH,
    )


class Part:
    def __init__(self, source, target, columns, far_at=0):
        self.source, self.target, self.columns, self.far_at = source, target, columns, far_at


class Gather:
    def __init__(self, place, parts, sems):
        self.place, self.parts = place, parts
        (
            self.own_sem,
            self.far_send,
            self.far_recv,
            self.plane_send,
            self.plane_recv,
            self.core_send,
            self.core_recv,
        ) = sems

    def rows(self, number, first, count):
        part = self.parts[number]
        size = part.source.shape[0]
        rows = pl.ds(pl.multiple_of(first * size, size), count * size)
        return part.target.at[rows, part.columns]

    def group(self, number, group):
        return self.rows(number, group * self.place.n_mem, self.place.n_mem)

    def one(self, number, group, member):
        return self.rows(number, group * self.place.n_mem + member, 1)

    def shard(self, number):
        part = self.parts[number]
        return part.source.at[:, part.columns]

    def mine(self, number):
        return self.one(number, self.place.row, self.place.mem)

    def own(self, number):
        return pltpu.make_async_copy(self.shard(number), self.mine(number), self.own_sem.at[number])

    def held(self, stage):
        groups = [self.place.row]
        for before in range(stage):
            groups = groups + [self.place.turn(group, before) for group in groups]
        return groups

    def far_total(self, number):
        some = self.rows(number, 0, (self.place.n_mem - 1) << self.parts[number].far_at)
        return remote(
            some, some, self.far_send.at[number], self.far_recv.at[number], self.place.far(1)
        )

    def plane_total(self, number, stage):
        shards = 1 if stage < self.parts[number].far_at else self.place.n_mem
        some = self.rows(number, 0, shards << stage)
        return remote(
            some,
            some,
            self.plane_send.at[stage, number],
            self.plane_recv.at[stage, number],
            self.place.partner(stage),
        )

    def core_total(self, number):
        some = self.rows(number, 0, self.place.n_mem * self.place.n_rows // 2)
        return remote(
            some, some, self.core_send.at[number], self.core_recv.at[number], self.place.sibling()
        )

    def total(self, number, hop):
        far_at = self.parts[number].far_at
        if hop == far_at:
            return self.far_total(number)
        return self.plane_total(number, hop - (hop > far_at))

    def hop(self, number, hop):
        place, far_at = self.place, self.parts[number].far_at
        if hop == 0:
            self.own(number).start()
        else:
            if hop == 1:
                self.own(number).wait()
            self.total(number, hop - 1).wait_recv()
        if hop == far_at:
            for group in self.held(hop):
                source = self.one(number, group, place.mem) if hop else self.shard(number)
                for step in range(1, place.n_mem):
                    remote(
                        source,
                        self.one(number, group, place.mem),
                        self.far_send.at[number],
                        self.far_recv.at[number],
                        place.far(step),
                    ).start()
            return
        stage = hop - (hop > far_at)
        for group in self.held(stage):
            if stage < far_at:
                target = self.one(number, group, place.mem)
                source = target if hop else self.shard(number)
            else:
                source = target = self.group(number, group)
            remote(
                source,
                target,
                self.plane_send.at[stage, number],
                self.plane_recv.at[stage, number],
                place.partner(stage),
            ).start()

    def spread_core(self, number):
        self.total(number, self.place.digits).wait_recv()
        for group in self.held(self.place.digits):
            block = self.group(number, group)
            remote(
                block,
                block,
                self.core_send.at[number],
                self.core_recv.at[number],
                self.place.sibling(),
            ).start()

    def events(self, number):
        time, digits = float(number), self.place.digits
        found = []
        for hop in range(digits + 1):
            found.append((time + 1.6 * hop, functools.partial(self.hop, number, hop)))
        time += 1.6 * digits + 1.5
        found.append((time, functools.partial(self.spread_core, number)))
        return found, time + 0.9

    def finish(self):
        for number in range(len(self.parts)):
            for hop in range(self.place.digits + 1):
                self.total(number, hop).wait_send()
            self.core_total(number).wait_send()


class Job:
    def __init__(self, left, right, first, target, far_at):
        self.left, self.right, self.first, self.target = left, right, first, target
        self.small = right is None
        self.far_at = far_at
        self.width = target.shape[-1]
        self.large = self.at = 0


OUT_SLOTS, LANE_SLOTS, SUM_SLOTS, CORE_RING, FIRST_RING, RING = 2, 3, 2, 2, 6, 4


class Reduce:
    def __init__(self, place, jobs, sems, buffers):
        self.place, self.jobs, self.buffers = place, jobs, buffers
        self.core_send, self.core_recv, self.stage_send, self.stage_recv = sems
        wanted = [place.row]
        for stage in reversed(range(place.digits)):
            wanted = wanted + [place.turn(group, stage) for group in wanted]
        self.wanted = [group // 2 for group in wanted]
        large = [job for job in jobs if not job.small]
        for number, job in enumerate(large):
            job.large = number
            job.at = [item for item in large if item.far_at == job.far_at].index(job)

    def cut(self, ref, job):
        columns = pl.ds(0, job.width)
        return ref if job.width == ref.shape[-1] else ref.at[(ALL,) * (len(ref.shape) - 1) + (columns,)]

    def out(self, job):
        return self.cut(self.buffers.out.at[job.large % OUT_SLOTS], job)

    def lanes(self, job):
        if job.small:
            return self.buffers.small_lanes
        return self.cut(self.buffers.lanes.at[job.large % LANE_SLOTS], job)

    def core_in(self, job):
        if job.small:
            return self.buffers.small_core_in
        return self.cut(self.buffers.core_in.at[job.large % CORE_RING], job)

    def count(self, job, stage):
        return 1 << (self.place.digits - stage - (stage < job.far_at))

    def sums(self, job, stage):
        if stage == self.place.digits:
            return job.target
        if job.small:
            return self.buffers.small_sums[stage]
        if stage == 0 and job.far_at > 0:
            return self.cut(self.buffers.first_sums.at[job.large % SUM_SLOTS], job)
        return self.cut(self.buffers.sums[job.far_at][stage].at[job.at % SUM_SLOTS], job)

    def arrived(self, job, stage):
        if job.small:
            return self.buffers.small_arrived[stage]
        if stage == 0 and job.far_at > 0:
            return self.cut(self.buffers.first_arrived.at[job.large % FIRST_RING], job)
        ring = self.buffers.arrived[job.far_at][stage]
        return self.cut(ring.at[job.at % ring.shape[0]], job)

    def previous(self, number, same, distance):
        found = [n for n in range(number) if same(self.jobs[n])]
        return found[-distance] if len(found) >= distance else None

    def is_large(self, job):
        return not job.small

    def reuse(self, number, stage):
        job = self.jobs[number]
        if job.small:
            return None
        if stage == 0 and job.far_at > 0:
            return self.previous(number, lambda item: not item.small and item.far_at > 0, SUM_SLOTS)
        return self.previous(
            number, lambda item: not item.small and item.far_at == job.far_at, SUM_SLOTS
        )

    def core_copy(self, number):
        job = self.jobs[number]
        source = job.left.at[1 - self.place.lane] if job.small else self.out(job)
        return remote(
            source,
            self.core_in(job),
            self.core_send.at[number],
            self.core_recv.at[number],
            self.place.sibling(),
        )

    def product(self, job, side, store):
        half = self.place.n_rows // 2
        group = job.left.shape[1] // half
        width = min(TILE, job.width)

        def column_step(step, carry):
            source = pl.ds(pl.multiple_of(job.first + step * width, width), width)
            value = dot(job.left[side], job.right[:, source])
            for index in range(half):
                store(index, span(step, width), value[index * group : (index + 1) * group])
            return carry

        lax.fori_loop(0, job.width // width, column_step, 0)

    def core_stage(self, number):
        job = self.jobs[number]
        if not job.small:
            before = self.previous(number, self.is_large, OUT_SLOTS)
            if before is not None:
                self.core_copy(before).wait_send()
            out = self.out(job)

            def store(index, columns, value):
                out[index, :, columns] = value.astype(out.dtype)

            self.product(job, 1 - self.place.lane, store)
        self.core_copy(number).start()

    def lane_stage(self, number):
        job = self.jobs[number]
        if not job.small:
            before = self.previous(number, self.is_large, LANE_SLOTS)
            if before is not None:
                self.total(before, 0).wait_send()
        lanes, arrived = self.lanes(job), self.core_in(job)
        self.core_copy(number).wait_recv()
        if job.small:
            lanes[...] = job.left[self.place.lane] + arrived[...]
        else:

            def store(index, columns, value):
                total = value + arrived[index, :, columns].astype(jnp.float32)
                lanes[index, :, columns] = total.astype(lanes.dtype)

            self.product(job, self.place.lane, store)
        self.send(number, 0)

    def unit(self, job, stage, index):
        if stage == 0:
            return self.lanes(job).at[self.wanted[index]]
        return self.sums(job, stage - 1).at[index]

    def member_rows(self, job, unit, member):
        if job.small:
            return unit
        size = unit.shape[0] // self.place.n_mem
        return unit.at[span(member, size)]

    def send(self, number, stage):
        job, place = self.jobs[number], self.place
        left = self.count(job, stage)
        arrived = self.arrived(job, stage)
        sems = (self.stage_send.at[stage, number], self.stage_recv.at[stage, number])
        for index in range(left):
            if stage == job.far_at:
                unit = self.unit(job, stage, index)
                for step in range(1, place.n_mem):
                    source = self.member_rows(job, unit, (place.mem + step) % place.n_mem)
                    remote(source, arrived.at[step - 1, index], *sems, place.far(step)).start()
            else:
                source = self.unit(job, stage, left + index)
                partner = place.partner(stage - (stage > job.far_at))
                remote(source, arrived.at[index], *sems, partner).start()

    def total(self, number, stage):
        some = self.arrived(self.jobs[number], stage)
        sems = (self.stage_send.at[stage, number], self.stage_recv.at[stage, number])
        return remote(some, some, *sems, self.place.far(1))

    def stage(self, number, stage):
        job, place = self.jobs[number], self.place
        last = stage == place.digits
        before = self.reuse(number, stage)
        if before is not None and not last:
            self.total(before, stage + 1).wait_send()
        self.total(number, stage).wait_recv()
        arrived, sums = self.arrived(job, stage), self.sums(job, stage)
        for index in range(self.count(job, stage)):
            unit = self.unit(job, stage, index)
            if stage == job.far_at:
                unit = self.member_rows(job, unit, place.mem)
                coming = [arrived.at[step, index] for step in range(place.n_mem - 1)]
            else:
                coming = [arrived.at[index]]
            target = sums if last else sums.at[index]
            block = min(32, unit.shape[0])

            def add(step, carry, unit=unit, coming=coming, target=target, block=block):
                rows = span(step, block)
                value = unit[rows].astype(jnp.float32)
                for item in coming:
                    value = value + item[rows].astype(jnp.float32)
                target[rows] = value.astype(target.dtype)
                return carry

            lax.fori_loop(0, unit.shape[0] // block, add, 0)
        if not last:
            self.send(number, stage + 1)

    def events(self, number):
        found = [(0.0, functools.partial(self.core_stage, number))]
        found.append((0.9, functools.partial(self.lane_stage, number)))
        time = 2.2 if number < 2 else 3.2
        for stage in range(self.place.digits + 1):
            found.append((time, functools.partial(self.stage, number, stage)))
            time += 1.4
        found[-1] = (found[-1][0] - 0.3, found[-1][1])
        return [(number + time, action) for time, action in found]

    def finish(self):
        n_jobs, last = len(self.jobs), self.place.digits
        out, lanes, sums = set(), set(), set()
        for number in range(n_jobs):
            if not self.jobs[number].small:
                out.add(self.previous(number, self.is_large, OUT_SLOTS))
                lanes.add(self.previous(number, self.is_large, LANE_SLOTS))
                for stage in range(last):
                    sums.add((self.reuse(number, stage), stage + 1))
        for number in range(n_jobs):
            if number not in out:
                self.core_copy(number).wait_send()
            if number not in lanes:
                self.total(number, 0).wait_send()
            for stage in range(1, last + 1):
                if (number, stage) not in sums:
                    self.total(number, stage).wait_send()


NORMAL = (((1,), (0,)), ((), ()))
TURNED = (((1,), (1,)), ((), ()))
LEFT_TURNED = (((0,), (0,)), ((), ()))


def dot(left, right, dims=NORMAL):
    return lax.dot_general(left, right, dims, preferred_element_type=jnp.float32)


def times(left, weight, store):
    width = min(TILE, weight.shape[1])

    def column_step(step, carry):
        columns = span(step, width)
        store(columns, dot(left[...], weight[:, columns]))
        return carry

    lax.fori_loop(0, weight.shape[1] // width, column_step, 0)


def times_turned(left, weight, store):
    width = min(TILE, weight.shape[0])

    def column_step(step, carry):
        columns = span(step, width)
        store(columns, dot(left[...], weight[columns, :], TURNED))
        return carry

    lax.fori_loop(0, weight.shape[0] // width, column_step, 0)


def into(target):
    def store(columns, value):
        target[:, columns] = value.astype(target.dtype)

    return store


ROWS = 32


def by_rows(count, step):
    def body(index, carry):
        step(span(index, ROWS))
        return carry

    lax.fori_loop(0, count // ROWS, body, 0)


def norm_forward(total, gains, index, unit, scale, use):
    gain, shift = gains[index : index + 1, :], gains[index + 3 : index + 4, :]

    def step(rows):
        value = total[rows, :]
        centre = value - jnp.mean(value, axis=-1, keepdims=True)
        spread = jnp.mean(centre * centre, axis=-1, keepdims=True)
        root = lax.rsqrt(spread + EPS)
        scaled = centre * root
        unit[rows, :] = scaled
        scale[rows, :] = root
        use(rows, scaled * gain + shift)

    by_rows(total.shape[0], step)


def norm_slope(incoming, scaled, root, gain):
    width = scaled.shape[1]
    scaled_grad = incoming * gain
    first = jnp.mean(scaled_grad, axis=-1, keepdims=True)
    second = jnp.mean(scaled_grad * scaled, axis=-1, keepdims=True)
    value = root * (scaled_grad - first - scaled * second)
    of_gain = jnp.sum((incoming * scaled).reshape(ROWS // 8, 8, width), axis=0)
    of_shift = jnp.sum(incoming.reshape(ROWS // 8, 8, width), axis=0)
    return value, of_gain, of_shift


def keep_small(index, sums, small):
    for offset, partial in ((index, sums[0]), (index + 3, sums[1])):
        line = jnp.sum(partial, axis=0, keepdims=True)
        for group in range(2 * small.shape[1]):
            small[group % 2, group // 2, offset : offset + 1, :] = line[
                :, group * 128 : (group + 1) * 128
            ]


def norm_backward(grad, gains, index, unit, scale, target, target_low, small):
    gain = gains[index : index + 1, :]

    def body(block, sums):
        rows = span(block, ROWS)
        value, of_gain, of_shift = norm_slope(grad[rows, :], unit[rows, :], scale[rows, :], gain)
        target[rows, :] = value
        target_low[rows, :] = value.astype(target_low.dtype)
        return (sums[0] + of_gain, sums[1] + of_shift)

    zero = jnp.zeros((8, unit.shape[1]), jnp.float32)
    keep_small(index, lax.fori_loop(0, unit.shape[0] // ROWS, body, (zero, zero)), small)


def norm_both(total, grad, gains, index, result, target, target_low, small):
    gain, shift = gains[index : index + 1, :], gains[index + 3 : index + 4, :]

    def body(block, sums):
        rows = span(block, ROWS)
        value = total[rows, :]
        centre = value - jnp.mean(value, axis=-1, keepdims=True)
        spread = jnp.mean(centre * centre, axis=-1, keepdims=True)
        root = lax.rsqrt(spread + EPS)
        scaled = centre * root
        result[rows, :] = scaled * gain + shift
        incoming = grad[rows, :].astype(jnp.float32)
        value, of_gain, of_shift = norm_slope(incoming, scaled, root, gain)
        target[rows, :] = value
        target_low[rows, :] = value.astype(target_low.dtype)
        return (sums[0] + of_gain, sums[1] + of_shift)

    zero = jnp.zeros((8, total.shape[1]), jnp.float32)
    keep_small(index, lax.fori_loop(0, total.shape[0] // ROWS, body, (zero, zero)), small)


def lane_masks(dtype):
    low = lax.broadcasted_iota(jnp.int32, (1, 2 * HEAD_DIM), 1) < HEAD_DIM
    first = jnp.where(low, 1.0, 0.0)
    return first.astype(dtype), (1.0 - first).astype(dtype)


def attention_forward(query, keys, values, bias, mixed, lse):
    masks = lane_masks(query.dtype)
    keep = lane_masks(jnp.float32)

    def pair_step(pair, carry):
        lanes = span(pair, 2 * HEAD_DIM)
        two_query, two_keys, two_values = query[:, lanes], keys[:, lanes], values[:, lanes]
        total = None
        for head in range(2):
            scores = dot(two_keys, two_query * masks[head], TURNED) * SCALE + bias[...]
            top = jnp.max(scores, axis=0, keepdims=True)
            weight = jnp.exp(scores - top)
            norm = jnp.sum(weight, axis=0, keepdims=True)
            probs = (weight * (1.0 / norm)).astype(query.dtype)
            part = dot(probs, two_values, LEFT_TURNED) * keep[head]
            total = part if total is None else total + part
            lse[pair, head : head + 1, :] = top + jnp.log(norm)
        mixed[:, lanes] = total.astype(mixed.dtype)
        return carry

    lax.fori_loop(0, lse.shape[0], pair_step, 0)


def attention_backward(
    query, keys, values, bias, lse, grad, query_grad, key_grad, value_grad, first, last
):
    masks = lane_masks(query.dtype)
    keep = lane_masks(jnp.float32)

    def pair_step(pair, carry):
        lanes = span(pair, 2 * HEAD_DIM)
        two_query, two_keys, two_values = query[:, lanes], keys[:, lanes], values[:, lanes]
        two_grad = grad[:, lanes]
        sums = [None, None, None]
        for head in range(2):
            scores = dot(two_keys, two_query * masks[head], TURNED) * SCALE + bias[...]
            probs = jnp.exp(scores - lse[pair, head : head + 1, :])
            pulled = dot(two_values, two_grad * masks[head], TURNED)
            inner = jnp.sum(probs * pulled, axis=0, keepdims=True)
            slope = (probs * (pulled - inner) * SCALE).astype(query.dtype)
            parts = (
                dot(slope, two_keys, LEFT_TURNED),
                dot(slope, two_query),
                dot(probs.astype(query.dtype), two_grad),
            )
            for index, part in enumerate(parts):
                part = part * keep[head]
                sums[index] = part if sums[index] is None else sums[index] + part
        query_grad[:, lanes] = sums[0].astype(query_grad.dtype)
        key_grad[:, lanes] = sums[1].astype(key_grad.dtype)
        value_grad[:, lanes] = sums[2].astype(value_grad.dtype)
        return carry

    lax.fori_loop(first, last, pair_step, 0)


def turn_blocks(left, eye, store):
    width = eye.shape[0]
    for block in range(left.shape[1] // width):
        columns = pl.ds(block * width, width)
        store(block, dot(eye[...], left[:, columns], TURNED).astype(left.dtype))


def turn_by_lane(left, eye, target):
    group = eye.shape[0] // 2

    def store(block, value):
        target[0, pl.ds(block * group, group), :] = value[:group]
        target[1, pl.ds(block * group, group), :] = value[group:]

    turn_blocks(left, eye, store)


SQUARES = 8


def layer_kernel(places, sizes, *refs):
    n_rows, n_mem, width, ff, shard = sizes
    ref = SimpleNamespace(**jax.tree.map(lambda place: refs[place], places))
    place = Place(n_rows, n_mem)
    many = ff // width
    own_ff = ff // (n_rows * n_mem)
    (
        at_query,
        at_key,
        at_value,
        at_output,
        at_cross_query,
        at_cross_key,
        at_cross_value,
        at_cross_output,
    ) = range(SQUARES)
    full = ref.full
    expand, contract = ref.expand_full, ref.contract_full
    tokens, gains = ref.tokens, ref.gains
    low, turned = SimpleNamespace(**ref.low), SimpleNamespace(**ref.turned)

    order = [
        at_query,
        at_key,
        at_value,
        at_output,
        at_cross_key,
        at_cross_value,
        at_cross_query,
        at_cross_output,
    ]
    narrow = width // many
    weights = [(ref.squares[index], full[index], ALL) for index in order]
    weights += [(ref.expand, expand, pl.ds(j * width, width)) for j in range(many)]
    weights += [(ref.contract, contract, pl.ds(j * narrow, narrow)) for j in range(many)]
    parts = [Part(*weight, number % 3 == 1) for number, weight in enumerate(weights)]
    parts.insert(SMALL_AT, Part(ref.small, ref.small_full, ALL))
    gather = Gather(place, parts, ref.gather_sems)

    slots, slot_sem = ref.slots, ref.slot_sem
    count = [0]

    def load(pieces):
        number = count[0]
        count[0] += 1
        slot = slots.at[number % SLOTS]
        for source, columns in pieces:
            pltpu.make_async_copy(source, slot.at[:, columns], slot_sem.at[number % SLOTS]).start()
        return number

    def ready(number):
        slot = slots.at[number % SLOTS]
        pltpu.make_async_copy(slot, slot, slot_sem.at[number % SLOTS]).wait()
        return slot

    def expand_block(j):
        return [(expand.at[:, pl.ds(j * width, width)], ALL)]

    def contract_columns(j):
        return [
            (
                contract.at[pl.ds(i * width, width), pl.ds(j * narrow, narrow)],
                pl.ds(i * narrow, narrow),
            )
            for i in range(many)
        ]

    def contract_rows(j):
        return [(contract.at[pl.ds(j * width, width), :], ALL)]

    mem_block = ref.memory.shape[1]
    memory, mem_rows = ref.memory, ref.mem_rows

    def memory_own():
        return pltpu.make_async_copy(
            memory.at[place.mem], mem_rows.at[span(place.mem, mem_block)], ref.mem_sem.at[0]
        )

    def memory_total():
        some = mem_rows.at[pl.ds(0, (n_mem - 1) * mem_block)]
        return remote(some, some, ref.mem_sem.at[1], ref.mem_sem.at[2], place.far(1))

    ref.small[...] = jnp.zeros_like(ref.small)
    for member in range(n_mem):

        @pl.when(place.mem == member)
        def _(member=member):
            lanes = slice(member * shard, (member + 1) * shard)
            ref.small[0:3, lanes] = ref.norm_gains[...].astype(jnp.float32)
            ref.small[3:6, lanes] = ref.norm_shifts[...].astype(jnp.float32)

    place.greet()
    actions = []
    whole = []
    for part in range(len(parts)):
        found, time = gather.events(part)
        actions += found
        whole.append(time)
    actions.sort(key=lambda item: item[0])
    start = [action for action in actions if action[0] < 2]
    actions = actions[len(start) :]
    for _, action in start:
        action()
    memory_own().start()
    for step in range(1, n_mem):
        remote(
            memory.at[(place.mem + step) % n_mem],
            mem_rows.at[span(place.mem, mem_block)],
            ref.mem_sem.at[1],
            ref.mem_sem.at[2],
            place.far(step),
        ).start()

    self_bias, cross_bias, eye = ref.self_bias, ref.cross_bias, ref.eye
    own_row = ref.token_ids[pl.ds(place.mem, 1), :].astype(jnp.float32)
    mem_row = ref.memory_ids[pl.ds(place.mem, 1), :].astype(jnp.float32)
    key_place = lax.broadcasted_iota(jnp.int32, self_bias.shape, 0)
    query_place = lax.broadcasted_iota(jnp.int32, self_bias.shape, 1)
    own_wide = jnp.broadcast_to(own_row, self_bias.shape)
    mem_wide = jnp.broadcast_to(mem_row, (cross_bias.shape[1], cross_bias.shape[0]))
    same = (jnp.transpose(own_wide) == own_wide) & (key_place <= query_place)
    self_bias[...] = jnp.where(same, 0.0, NEG)
    cross_bias[...] = jnp.where(jnp.transpose(mem_wide) == own_row, 0.0, NEG)
    eye_row = lax.broadcasted_iota(jnp.int32, eye.shape, 0)
    eye_column = lax.broadcasted_iota(jnp.int32, eye.shape, 1)
    eye[...] = jnp.where(eye_row == eye_column, 1.0, 0.0).astype(eye.dtype)
    turn_by_lane(tokens, eye, turned.tokens)

    accumulated, other = ref.accumulated, ref.other
    hidden, slope, hidden_turned = ref.hidden, ref.slope, ref.hidden_turned

    def small_piece():
        blocks = ref.small_full
        for group in range(n_rows):
            total = None
            for member in range(n_mem):
                first = (group * n_mem + member) * 8
                value = blocks[first : first + 8, :]
                total = value if total is None else total + value
            gains[:, group * 128 : (group + 1) * 128] = total

    def query_piece(slot):
        times(tokens, slot, into(ref.query))

    def key_piece(slot):
        times(tokens, slot, into(ref.keys))

    def value_piece(slot):
        times(tokens, slot, into(ref.values))
        attention_forward(
            ref.query, ref.keys, ref.values, self_bias, ref.attended, ref.self_lse
        )

    def output_piece(slot):
        def store(columns, value):
            accumulated[:, columns] = ALPHA * tokens[:, columns].astype(jnp.float32) + value

        times(ref.attended, slot, store)

        def use(rows, value):
            ref.first_low[rows, :] = value.astype(jnp.bfloat16)
            other[rows, :] = value

        norm_forward(accumulated, gains, 0, ref.unit1, ref.scale1, use)
        turn_by_lane(ref.attended, eye, turned.attended)

    def cross_key_piece(slot):
        memory_own().wait()
        memory_total().wait_recv()
        times(mem_rows, slot, into(ref.cross_keys))
        turn_by_lane(mem_rows, eye, turned.memory)

    def cross_value_piece(slot):
        times(mem_rows, slot, into(ref.cross_values))
        turn_by_lane(ref.first_low, eye, turned.first)

    def cross_query_piece(slot):
        times(ref.first_low, slot, into(ref.cross_query))
        attention_forward(
            ref.cross_query,
            ref.cross_keys,
            ref.cross_values,
            cross_bias,
            ref.crossed,
            ref.cross_lse,
        )

    def cross_output_piece(slot):
        def store(columns, value):
            accumulated[:, columns] = ALPHA * other[:, columns] + value

        times(ref.crossed, slot, store)

        def use(rows, value):
            ref.second_low[rows, :] = value.astype(jnp.bfloat16)
            other[rows, :] = value

        norm_forward(accumulated, gains, 1, ref.unit2, ref.scale2, use)
        turn_by_lane(ref.crossed, eye, turned.crossed)

    def expand_piece(j, slot):
        def store(columns, value):
            there = pl.ds(pl.multiple_of(j * width + columns.start, TILE), columns.size)
            bell = 0.5 * (1.0 + lax.erf(value * math.sqrt(0.5)))
            density = jnp.exp(value * value * -0.5) * (1.0 / math.sqrt(2.0 * math.pi))
            hidden[:, there] = (value * bell).astype(hidden.dtype)
            slope[:, there] = (bell + value * density).astype(slope.dtype)

        times(ref.second_low, slot, store)

        def keep(block, value):
            for index in range(value.shape[0] // shard):
                first = j * width + block * value.shape[0] + index * shard
                device, job = first // own_ff, first % own_ff // shard
                group, member = device // n_mem, device % n_mem
                at = group // 2 * n_mem * shard + member * shard
                hidden_turned[job, group % 2, at : at + shard, :] = value[
                    index * shard : (index + 1) * shard
                ]

        turn_blocks(hidden.at[:, pl.ds(j * width, width)], eye, keep)

    def contract_piece(j, slot):
        total = None
        for i in range(many):
            value = dot(
                hidden[:, i * width : (i + 1) * width], slot[:, i * narrow : (i + 1) * narrow]
            )
            total = value if total is None else total + value
        columns = pl.ds(j * narrow, narrow)
        accumulated[:, columns] = ALPHA * other[:, columns] + total

    pieces = [
        query_piece,
        key_piece,
        value_piece,
        output_piece,
        cross_key_piece,
        cross_value_piece,
        cross_query_piece,
        cross_output_piece,
    ]
    sources = [[(full[index], ALL)] for index in order]
    for j in range(many):
        pieces.append(functools.partial(expand_piece, j))
        sources.append(expand_block(j))
    for j in range(many):
        pieces.append(functools.partial(contract_piece, j))
        sources.append(contract_columns(j))

    waiting = []

    def arrive(part):
        gather.core_total(part).wait_recv()
        if part != SMALL_AT:
            number = part - (part > SMALL_AT)
            waiting.append((number, load(sources[number])))

    def use():
        number, slot = waiting.pop(0)
        pieces[number](ready(slot))

    last = 0.0
    for part, time in enumerate(whole):
        time = max(time, last + 0.2)
        actions.append((time, functools.partial(arrive, part)))
        actions.append((time + 0.5, small_piece if part == SMALL_AT else use))
        last = time
    actions.sort(key=lambda item: item[0])
    for _, action in actions:
        action()

    backward_sources, loads = [], []
    used = [0]

    def next_slot():
        slot = ready(loads[used[0]])
        used[0] += 1
        if len(loads) < len(backward_sources):
            loads.append(load(backward_sources[len(loads)]))
        return slot

    small_sums = ref.small_sums
    small_sums[...] = jnp.zeros_like(small_sums)
    def inner_piece(j):
        slot = next_slot()

        def store(columns, value):
            there = pl.ds(pl.multiple_of(j * width + columns.start, TILE), columns.size)
            slope[:, there] = (value * slope[:, there].astype(jnp.float32)).astype(slope.dtype)

        times_turned(low.third, slot, store)

    def second_piece(j):
        slot = next_slot()

        def store(columns, value):
            if j == 0:
                other[:, columns] = ALPHA * accumulated[:, columns] + value
            else:
                other[:, columns] = other[:, columns] + value

        times_turned(slope.at[:, pl.ds(j * width, width)], slot, store)

    def second_norm_piece():
        norm_backward(
            other, gains, 1, ref.unit2, ref.scale2, accumulated, low.second, small_sums
        )

    pairs = width // (2 * HEAD_DIM)

    def cross_start_piece():
        times_turned(low.second, next_slot(), into(low.branch))

    def cross_piece(first, last):
        attention_backward(
            ref.cross_query,
            ref.cross_keys,
            ref.cross_values,
            cross_bias,
            ref.cross_lse,
            low.branch,
            low.cross_query,
            low.cross_key,
            low.cross_value,
            first,
            last,
        )

    def first_piece():
        def store(columns, value):
            other[:, columns] = ALPHA * accumulated[:, columns] + value

        times_turned(low.cross_query, next_slot(), store)
        norm_backward(other, gains, 0, ref.unit1, ref.scale1, accumulated, low.first, small_sums)

    def self_start_piece():
        times_turned(low.first, next_slot(), into(low.branch))

    def self_piece(first, last):
        attention_backward(
            ref.query,
            ref.keys,
            ref.values,
            self_bias,
            ref.self_lse,
            low.branch,
            low.query,
            low.key,
            low.value,
            first,
            last,
        )

    mem_out, mem_in = ref.mem_out, ref.mem_in

    def grad_own():
        return pltpu.make_async_copy(
            mem_out.at[span(place.mem, mem_block)], mem_in.at[place.mem], ref.mem_sem.at[3]
        )

    def grad_total():
        some = mem_in.at[pl.ds(0, n_mem - 1)]
        return remote(some, some, ref.mem_sem.at[4], ref.mem_sem.at[5], place.far(1))

    def memory_key_piece():
        times_turned(low.cross_key, next_slot(), into(other))

    def memory_value_piece():
        def store(columns, value):
            mem_out[:, columns] = (other[:, columns] + value).astype(mem_out.dtype)

        times_turned(low.cross_value, next_slot(), store)
        grad_own().start()
        for step in range(1, n_mem):
            remote(
                mem_out.at[span((place.mem + step) % n_mem, mem_block)],
                mem_in.at[place.mem],
                ref.mem_sem.at[4],
                ref.mem_sem.at[5],
                place.far(step),
            ).start()

    def input_piece(left, start):
        target = ref.input_grad

        def store(columns, value):
            if start:
                target[:, columns] = ALPHA * accumulated[:, columns] + value
            else:
                target[:, columns] = target[:, columns] + value

        times_turned(left, next_slot(), store)

    def memory_end_piece():
        grad_own().wait()
        grad_total().wait_recv()
        for member in range(n_mem):
            ref.memory_grad[member] = mem_in[member].astype(jnp.float32)

    halves = ((0, width // 2), (width // 2, width // 2))
    grads = ref.grads
    plans = []
    for j in range(many):
        for first, columns in halves if j == 0 else ((0, width),):
            target = ref.contract_grad.at[pl.ds(j * shard, shard), pl.ds(first, columns)]
            plans.append((hidden_turned.at[j], low.third, first, target))
    for j in range(many):
        target = ref.expand_grad.at[:, pl.ds(j * width, width)]
        plans.append((turned.second, slope, j * width, target))
    plans += [
        (turned.crossed, low.second, 0, grads[at_cross_output]),
        (turned.memory, low.cross_key, 0, grads[at_cross_key]),
        (turned.memory, low.cross_value, 0, grads[at_cross_value]),
        (turned.first, low.cross_query, 0, grads[at_cross_query]),
        (turned.attended, low.first, 0, grads[at_output]),
        (small_sums, None, 0, ref.small_total),
        (turned.tokens, low.query, 0, grads[at_query]),
        (turned.tokens, low.key, 0, grads[at_key]),
    ]
    for first, columns in halves:
        target = grads[at_value].at[:, pl.ds(first, columns)]
        plans.append((turned.tokens, low.value, first, target))
    jobs = []
    for number, plan in enumerate(plans):
        early = number % 3 == 1 and plan[1] is not None
        jobs.append(Job(*plan, place.digits - early))
    reduce = Reduce(place, jobs, ref.reduce_sems, SimpleNamespace(**ref.buffers))

    inner = [functools.partial(inner_piece, j) for j in range(many)]
    second = [functools.partial(second_piece, j) for j in range(many)]
    middle = pairs // 2
    base = many + 1
    def weight(index):
        return [(full[index], ALL)]

    turn = functools.partial(turn_by_lane, ref.second_low, eye, turned.second)
    work = [(base - 1.7, inner[0], contract_rows(0)), (base - 1.3, turn, None)]
    work += [(base - 1.7 + j, inner[j], contract_rows(j)) for j in range(1, many)]
    work += [(base - 0.3 + j, second[j], expand_block(j)) for j in range(many)]
    base = 2 * many + 1
    work += [
        (base - 0.2, second_norm_piece, None),
        (base - 0.15, cross_start_piece, weight(at_cross_output)),
        (base + 0.3, functools.partial(cross_piece, 0, middle), None),
        (base + 0.7, functools.partial(cross_piece, middle, pairs), None),
        (base + 1.3, first_piece, weight(at_cross_query)),
        (base + 1.7, self_start_piece, weight(at_output)),
        (base + 2.3, functools.partial(self_piece, 0, middle), None),
        (base + 3.3, functools.partial(self_piece, middle, pairs), None),
        (base + 3.7, memory_key_piece, weight(at_cross_key)),
        (base + 4.3, memory_value_piece, weight(at_cross_value)),
        (base + 4.7, functools.partial(input_piece, low.query, True), weight(at_query)),
        (base + 5.5, functools.partial(input_piece, low.key, False), weight(at_key)),
        (base + 6.5, functools.partial(input_piece, low.value, False), weight(at_value)),
        (base + 8.5, memory_end_piece, None),
    ]
    work.sort(key=lambda item: item[0])
    backward_sources += [source for _, _, source in work if source is not None]
    loads += [load(backward_sources[0]), load(backward_sources[1])]
    norm_both(
        accumulated, ref.out_grad, gains, 2, ref.result, accumulated, low.third, small_sums
    )

    actions = [(time, piece) for time, piece, _ in work]
    for number in range(len(jobs)):
        actions += reduce.events(number)
    actions.sort(key=lambda item: item[0])
    for _, action in actions:
        action()

    total = ref.small_total[...]
    own = jnp.zeros((8, shard), jnp.float32)
    for member in range(n_mem):
        here = jnp.where(place.mem == member, 1.0, 0.0)
        own = own + here * total[:, member * shard : (member + 1) * shard]
    ref.gains_grad[...] = own[0:3]
    ref.shifts_grad[...] = own[3:6]
    gather.finish()
    reduce.finish()
    memory_total().wait_send()
    grad_total().wait_send()


SMALL_AT = 2


def copy_kernel(count, *refs):
    for source, target in zip(refs[:count], refs[count:]):
        target[...] = source[...]


def copied(values):
    near = pl.BlockSpec(memory_space=pltpu.VMEM)
    return pl.pallas_call(
        functools.partial(copy_kernel, len(values)),
        out_shape=[jax.ShapeDtypeStruct(value.shape, value.dtype) for value in values],
        in_specs=[near] * len(values),
        out_specs=[near] * len(values),
        compiler_params=pltpu.CompilerParams(vmem_limit_bytes=VMEM_LIMIT),
        name="results",
    )(*values)


def fused(n_rows, n_mem, ins):
    tokens, memory, squares = ins["tokens"], ins["memory"], ins["squares"]
    expand, contract = ins["expand"], ins["contract"]
    tokens_here, width = tokens.shape
    ff = expand.shape[1]
    shard = squares[0].shape[0]
    mem_tokens = memory.shape[0] * memory.shape[1]
    digits, half, many = (n_rows // 2).bit_length() - 1, n_rows // 2, ff // width
    pairs = width // (2 * HEAD_DIM)
    low, high = jnp.bfloat16, jnp.float32
    n_parts = 1 + SQUARES + 2 * many
    n_jobs = n_parts + 2
    dma, vmem = pltpu.SemaphoreType.DMA, pltpu.VMEM
    anywhere, near = pl.BlockSpec(memory_space=pl.ANY), pl.BlockSpec(memory_space=pltpu.VMEM)

    far_ins = dict(memory=memory, squares=squares, expand=expand, contract=contract)
    in_specs = {
        name: jax.tree.map(lambda _: anywhere if name in far_ins else near, value)
        for name, value in ins.items()
    }

    def out(shape, dtype=high):
        return jax.ShapeDtypeStruct(shape, dtype)

    outs = dict(
        result=out(tokens.shape),
        input_grad=out(tokens.shape),
        memory_grad=out(memory.shape),
        grads=[out(item.shape) for item in squares],
        expand_grad=out(expand.shape),
        contract_grad=out(contract.shape),
        gains_grad=out((3, shard)),
        shifts_grad=out((3, shard)),
    )
    far_outs = dict(
        full=[out((width, width), low)] * SQUARES,
        expand_full=out((width, ff), low),
        contract_full=out((ff, width), low),
    )
    out_specs = jax.tree.map(lambda _: near, outs)
    out_specs.update(jax.tree.map(lambda _: anywhere, far_outs))
    outs.update(far_outs)

    def token_rows(dtype):
        return vmem((tokens_here, width), dtype)

    def memory_rows(dtype):
        return vmem((mem_tokens, width), dtype)

    tiny = (8, 128)

    def unit(stage, far_at):
        count = 1 << (digits - stage - (stage < far_at))
        return (count, n_mem * shard if stage < far_at else shard, width)

    sums, arrived = {}, {}
    for far_at, ring in ((digits, RING), (digits - 1, 2)):
        sums[far_at], arrived[far_at] = {}, {}
        for stage in range(digits + 1):
            if stage == 0 and far_at > 0:
                continue
            others = (n_mem - 1,) if stage == far_at else ()
            arrived[far_at][stage] = vmem((ring,) + others + unit(stage, far_at), low)
            if stage < digits:
                sums[far_at][stage] = vmem((SUM_SLOTS,) + unit(stage, far_at), low)
    whole = (half, n_mem * shard, width)
    counts = [1 << (digits - 1 - stage) for stage in range(digits)]
    buffers = dict(
        out=vmem((OUT_SLOTS,) + whole, low),
        lanes=vmem((LANE_SLOTS,) + whole, low),
        core_in=vmem((CORE_RING,) + whole, low),
        first_sums=vmem((SUM_SLOTS,) + unit(0, digits), low),
        first_arrived=vmem((FIRST_RING,) + unit(0, digits), low),
        sums=sums,
        arrived=arrived,
        small_lanes=vmem((half,) + tiny, high),
        small_core_in=vmem((half,) + tiny, high),
        small_sums=[vmem((count,) + tiny, high) for count in counts],
        small_arrived=[vmem((count,) + tiny, high) for count in counts]
        + [vmem((n_mem - 1, 1) + tiny, high)],
    )
    left = vmem((2, width // 2, tokens_here), low)
    scratch = dict(
        small=vmem(tiny, high),
        small_full=vmem((n_rows * n_mem * 8, 128), high),
        small_total=vmem(tiny, high),
        slots=vmem((SLOTS, width, width), low),
        slot_sem=dma((SLOTS,)),
        mem_sem=dma((6,)),
        gather_sems=[
            dma(shape + (n_parts,)) for shape in ((), (), (), (digits,), (digits,), (), ())
        ],
        reduce_sems=[dma(shape + (n_jobs,)) for shape in ((), (), (digits + 1,), (digits + 1,))],
        gains=vmem((8, width), high),
        query=token_rows(low),
        keys=token_rows(low),
        values=token_rows(low),
        attended=token_rows(low),
        first_low=token_rows(low),
        second_low=token_rows(low),
        cross_query=token_rows(low),
        crossed=token_rows(low),
        cross_keys=memory_rows(low),
        cross_values=memory_rows(low),
        mem_rows=memory_rows(low),
        mem_out=memory_rows(low),
        mem_in=vmem(memory.shape, low),
        unit1=token_rows(high),
        unit2=token_rows(high),
        accumulated=token_rows(high),
        other=token_rows(high),
        scale1=vmem((tokens_here, 1), high),
        scale2=vmem((tokens_here, 1), high),
        self_bias=vmem((tokens_here, tokens_here), high),
        cross_bias=vmem((mem_tokens, tokens_here), high),
        self_lse=vmem((pairs, 2, tokens_here), high),
        cross_lse=vmem((pairs, 2, tokens_here), high),
        eye=vmem((TILE, TILE), low),
        hidden=vmem((tokens_here, ff), low),
        slope=vmem((tokens_here, ff), low),
        hidden_turned=vmem((many, 2, width // 2, tokens_here), low),
        turned=dict(
            tokens=left, attended=left, first=left, memory=left, crossed=left, second=left
        ),
        low=dict(
            third=token_rows(low),
            second=token_rows(low),
            first=token_rows(low),
            branch=token_rows(low),
            cross_query=token_rows(low),
            cross_key=memory_rows(low),
            cross_value=memory_rows(low),
            query=token_rows(low),
            key=token_rows(low),
            value=token_rows(low),
        ),
        small_sums=vmem((2, half) + tiny, high),
        buffers=buffers,
    )
    in_values, in_tree = jax.tree.flatten(ins)
    out_shapes, out_tree = jax.tree.flatten(outs)
    scratch_shapes, scratch_tree = jax.tree.flatten(scratch)
    places = jax.tree.unflatten(in_tree, range(len(in_values)))
    at = len(in_values)
    places.update(jax.tree.unflatten(out_tree, range(at, at + len(out_shapes))))
    at += len(out_shapes)
    places.update(jax.tree.unflatten(scratch_tree, range(at, at + len(scratch_shapes))))
    values = pl.pallas_call(
        functools.partial(layer_kernel, places, (n_rows, n_mem, width, ff, shard)),
        out_shape=out_shapes,
        in_specs=jax.tree.leaves(in_specs),
        out_specs=jax.tree.leaves(out_specs),
        scratch_shapes=scratch_shapes,
        compiler_params=pltpu.CompilerParams(
            collective_id=0, has_side_effects=True, vmem_limit_bytes=VMEM_LIMIT
        ),
        name="layer",
    )(*in_values)
    found = jax.tree.unflatten(out_tree, values)
    for name in far_outs:
        del found[name]
    return found


def local(n_rows, n_mem, *args):
    (
        tokens,
        memory,
        token_ids,
        memory_ids,
        out_grad,
        self_query,
        self_key,
        self_value,
        self_output,
        cross_query,
        cross_key,
        cross_value,
        cross_output,
        expand_weight,
        contract_weight,
        norm_gains,
        norm_shifts,
    ) = args
    shard, width = self_query.shape
    suits = width == 128 * n_rows and shard % 16 == 0 and tokens.shape[0] == 1
    if not suits or n_rows < 4 or n_rows & (n_rows - 1) or n_mem < 2:
        return plain(*args)
    found = fused(
        n_rows,
        n_mem,
        dict(
            tokens=tokens[0],
            memory=memory,
            token_ids=token_ids,
            memory_ids=memory_ids,
            out_grad=out_grad[0],
            squares=[
                self_query,
                self_key,
                self_value,
                self_output,
                cross_query,
                cross_key,
                cross_value,
                cross_output,
            ],
            expand=expand_weight,
            contract=contract_weight,
            norm_gains=norm_gains,
            norm_shifts=norm_shifts,
        ),
    )
    values, tree = jax.tree.flatten(found)
    found = SimpleNamespace(**jax.tree.unflatten(tree, copied(values)))
    return (
        found.result[None],
        found.input_grad[None],
        found.memory_grad,
        *found.grads,
        found.expand_grad,
        found.contract_grad,
        found.gains_grad,
        found.shifts_grad,
    )


def solution(mesh):
    in_specs = (
        P(("rows", "mem"), None, None),
        P("rows", "mem", None),
        P("rows", None),
        P("rows", None),
        P(("rows", "mem"), None, None),
        P(("rows", "mem"), None),
        P(("rows", "mem"), None),
        P(("rows", "mem"), None),
        P(("rows", "mem"), None),
        P(("rows", "mem"), None),
        P(("rows", "mem"), None),
        P(("rows", "mem"), None),
        P(("rows", "mem"), None),
        P(("rows", "mem"), None),
        P(("rows", "mem"), None),
        P(None, ("rows", "mem")),
        P(None, ("rows", "mem")),
    )
    out_specs = (
        P(("rows", "mem"), None, None),
        P(("rows", "mem"), None, None),
        P("rows", "mem", None),
        P(("rows", "mem"), None),
        P(("rows", "mem"), None),
        P(("rows", "mem"), None),
        P(("rows", "mem"), None),
        P(("rows", "mem"), None),
        P(("rows", "mem"), None),
        P(("rows", "mem"), None),
        P(("rows", "mem"), None),
        P(("rows", "mem"), None),
        P(("rows", "mem"), None),
        P(None, ("rows", "mem")),
        P(None, ("rows", "mem")),
    )
    layer = functools.partial(local, mesh.shape["rows"], mesh.shape["mem"])
    return jax.shard_map(layer, mesh=mesh, in_specs=in_specs, out_specs=out_specs, check_vma=False)
```

```python
import functools
import math
from types import SimpleNamespace

import jax
import jax.numpy as jnp
from jax import lax
from jax.experimental import pallas as pl
from jax.experimental.pallas import tpu as pltpu
from jax.sharding import PartitionSpec as P

MESH = pl.DeviceIdType.MESH

HEADS = 16
HEAD_DIM = 64


ALPHA = 4.16
EPS = 1e-05
SCALE = 0.125
NEG = -1e30


def layer_norm(hidden_activation, gain, shift):
    centre = hidden_activation - jnp.mean(hidden_activation, axis=-1, keepdims=True)
    spread = jnp.mean(centre * centre, axis=-1, keepdims=True)
    return centre * lax.rsqrt(spread + EPS) * gain + shift


def gelu_exact(value):
    return jax.nn.gelu(value, approximate=False)


def product(left, right):
    return jnp.dot(left, right, preferred_element_type=jnp.float32)


def split_heads(matrix):
    return matrix.reshape(matrix.shape[0], matrix.shape[1] // HEAD_DIM, HEAD_DIM)


def grouped(matrix):
    return jnp.moveaxis(matrix.reshape(matrix.shape[0], HEADS // 4, 4 * HEAD_DIM), 1, 0)


def ungrouped(stack):
    return jnp.moveaxis(stack, 0, 1).reshape(stack.shape[1], stack.shape[0] * stack.shape[2])


def row_map(function, items):
    return lax.map(lambda entry: function(*entry), items)


def score_block(query, keys, allowed):
    raw = jnp.einsum(
        "khe,qhe->hkq", split_heads(keys), split_heads(query), preferred_element_type=jnp.float32
    )
    return jnp.where(allowed[None], raw * SCALE, NEG)


def attend_probs(query, keys, allowed, lse):
    scores = score_block(query, keys, allowed)
    return jnp.where(allowed[None], jnp.exp(scores - lse[:, None, :]), 0.0)


def attend_forward(query, keys, values, allowed):
    scores = score_block(query, keys, allowed)
    top = jnp.max(scores, axis=1)
    weight = jnp.where(allowed[None], jnp.exp(scores - top[:, None, :]), 0.0)
    total = jnp.sum(weight, axis=1)
    probs = (weight / total[:, None, :]).astype(jnp.bfloat16)
    mixed = jnp.einsum(
        "hkq,khe->qhe", probs, split_heads(values), preferred_element_type=jnp.float32
    )
    return (mixed.reshape(query.shape), top + jnp.log(total))


def value_pull(grad, values):
    return jnp.einsum(
        "qhe,khe->hkq", split_heads(grad), split_heads(values), preferred_element_type=jnp.float32
    )


def score_grads(probs, pulled, inner):
    return (probs * (pulled - inner[:, None, :]) * SCALE).astype(jnp.bfloat16)


def query_from(score_grad, keys, shape):
    moved = jnp.einsum(
        "hkq,khe->qhe", score_grad, split_heads(keys), preferred_element_type=jnp.float32
    )
    return moved.reshape(shape)


def key_from(score_grad, query, shape):
    moved = jnp.einsum(
        "hkq,qhe->khe", score_grad, split_heads(query), preferred_element_type=jnp.float32
    )
    return moved.reshape(shape)


def value_from(probs, grad, values):
    moved = jnp.einsum(
        "hkq,qhe->khe",
        probs.astype(jnp.bfloat16),
        split_heads(grad),
        preferred_element_type=jnp.float32,
    )
    return moved.reshape(values.shape)


def local_forward(query, keys, values, allowed):

    def one_group(items):
        return attend_forward(items[0], items[1], items[2], allowed)

    mixed, lse = lax.map(one_group, (grouped(query), grouped(keys), grouped(values)))
    return (ungrouped(mixed), lse)


def local_backward(query, keys, values, allowed, lse, grad):

    def one_group(items):
        part_query, part_keys, part_values, part_lse, part_grad = items
        probs = attend_probs(part_query, part_keys, allowed, part_lse)
        pulled = value_pull(part_grad, part_values)
        inner = jnp.sum(probs * pulled, axis=1)
        score_grad = score_grads(probs, pulled, inner)
        return (
            query_from(score_grad, part_keys, part_query.shape),
            key_from(score_grad, part_query, part_keys.shape),
            value_from(probs, part_grad, part_values),
        )

    parts = lax.map(one_group, (grouped(query), grouped(keys), grouped(values), lse, grouped(grad)))
    return (ungrouped(parts[0]), ungrouped(parts[1]), ungrouped(parts[2]))


def plain(
    tokens,
    memory,
    token_ids,
    memory_ids,
    out_grad,
    self_query,
    self_key,
    self_value,
    self_output,
    cross_query,
    cross_key,
    cross_value,
    cross_output,
    expand_weight,
    contract_weight,
    norm_gains,
    norm_shifts,
):
    full = (
        lax.all_gather(self_query, ("rows", "mem"), axis=0, tiled=True),
        lax.all_gather(self_key, ("rows", "mem"), axis=0, tiled=True),
        lax.all_gather(self_value, ("rows", "mem"), axis=0, tiled=True),
        lax.all_gather(self_output, ("rows", "mem"), axis=0, tiled=True),
        lax.all_gather(cross_query, ("rows", "mem"), axis=0, tiled=True),
        lax.all_gather(cross_key, ("rows", "mem"), axis=0, tiled=True),
        lax.all_gather(cross_value, ("rows", "mem"), axis=0, tiled=True),
        lax.all_gather(cross_output, ("rows", "mem"), axis=0, tiled=True),
        lax.all_gather(expand_weight, ("rows", "mem"), axis=0, tiled=True),
        lax.all_gather(contract_weight, ("rows", "mem"), axis=0, tiled=True),
        lax.all_gather(jnp.transpose(norm_gains), ("rows", "mem"), axis=0, tiled=True),
        lax.all_gather(jnp.transpose(norm_shifts), ("rows", "mem"), axis=0, tiled=True),
    )
    (
        self_attention_query,
        decoder_match_label,
        self_attention_value,
        self_attention_output,
        encoder_lookup_probe,
        key_cross,
        value_cross,
        cross_attention_output,
        up_projection,
        narrowing_matrix,
        gain_cols,
        shift_cols,
    ) = full
    gain_rows = jnp.transpose(gain_cols).astype(jnp.float32)
    shift_rows = jnp.transpose(shift_cols).astype(jnp.float32)
    rows_here = tokens.shape[0]
    member = lax.axis_index("mem")
    own_ids = lax.dynamic_slice_in_dim(token_ids, member * rows_here, rows_here, 0)
    positions = jnp.arange(tokens.shape[1], dtype=jnp.int32)
    self_allowed = (own_ids[:, :, None] == own_ids[:, None, :]) & (
        positions[:, None] <= positions[None, :]
    )[None]
    query = product(tokens, self_attention_query).astype(jnp.bfloat16)
    keys = product(tokens, decoder_match_label).astype(jnp.bfloat16)
    values = product(tokens, self_attention_value).astype(jnp.bfloat16)
    self_mixed, self_lse = row_map(local_forward, (query, keys, values, self_allowed))
    attention_result = self_mixed.astype(jnp.bfloat16)
    first, first_back = jax.vjp(
        layer_norm,
        ALPHA * tokens.astype(jnp.float32) + product(attention_result, self_attention_output),
        gain_rows[0],
        shift_rows[0],
    )
    first_reduced = first.astype(jnp.bfloat16)
    cross_queries = product(first_reduced, encoder_lookup_probe).astype(jnp.bfloat16)
    memory_rows = lax.all_to_all(memory, "mem", split_axis=0, concat_axis=1, tiled=True)
    row_ids = lax.dynamic_slice_in_dim(memory_ids, member * rows_here, rows_here, 0)
    cross_allowed = row_ids[:, :, None] == own_ids[:, None, :]
    cross_keys = product(memory_rows, key_cross).astype(jnp.bfloat16)
    cross_values = product(memory_rows, value_cross).astype(jnp.bfloat16)
    cross_mixed, cross_lse = row_map(
        local_forward, (cross_queries, cross_keys, cross_values, cross_allowed)
    )
    cross_attention_result = cross_mixed.astype(jnp.bfloat16)
    second, second_back = jax.vjp(
        layer_norm,
        ALPHA * first + product(cross_attention_result, cross_attention_output),
        gain_rows[1],
        shift_rows[1],
    )
    second_reduced = second.astype(jnp.bfloat16)
    hidden_value, gelu_back = jax.vjp(gelu_exact, product(second_reduced, up_projection))
    hidden_activation = hidden_value.astype(jnp.bfloat16)
    result, third_back = jax.vjp(
        layer_norm,
        ALPHA * second + product(hidden_activation, narrowing_matrix),
        gain_rows[2],
        shift_rows[2],
    )
    third_grad, gain_three, shift_three = third_back(out_grad.astype(jnp.float32))
    feedforward_gradient = third_grad.astype(jnp.bfloat16)
    down_projection_gradient = jnp.einsum(
        "ehj,ehc->jc", hidden_activation, feedforward_gradient, preferred_element_type=jnp.float32
    )
    (inner_grad,) = gelu_back(
        jnp.einsum(
            "hpu,ku->hpk",
            feedforward_gradient,
            narrowing_matrix,
            preferred_element_type=jnp.float32,
        )
    )
    inner_reduced = inner_grad.astype(jnp.bfloat16)
    expand_grad = jnp.einsum(
        "iqg,iqe->ge", second_reduced, inner_reduced, preferred_element_type=jnp.float32
    )
    second_total = ALPHA * third_grad + jnp.einsum(
        "iwm,fm->iwf", inner_reduced, up_projection, preferred_element_type=jnp.float32
    )
    second_grad, gain_two, shift_two = second_back(second_total)
    cross_branch_gradient = second_grad.astype(jnp.bfloat16)
    output_cross_grad = jnp.einsum(
        "nhb,nhc->bc",
        cross_attention_result,
        cross_branch_gradient,
        preferred_element_type=jnp.float32,
    )
    crossed_grad = jnp.einsum(
        "qwp,up->qwu",
        cross_branch_gradient,
        cross_attention_output,
        preferred_element_type=jnp.float32,
    ).astype(jnp.bfloat16)
    query_grads, key_grads, value_grads = row_map(
        local_backward,
        (cross_queries, cross_keys, cross_values, cross_allowed, cross_lse, crossed_grad),
    )
    key_low = key_grads.astype(jnp.bfloat16)
    value_low = value_grads.astype(jnp.bfloat16)
    row_grad = jnp.einsum(
        "sme,de->smd", key_low, key_cross, preferred_element_type=jnp.float32
    ) + jnp.einsum("sme,de->smd", value_low, value_cross, preferred_element_type=jnp.float32)
    key_cross_grad = jnp.einsum(
        "smd,sme->de", memory_rows, key_low, preferred_element_type=jnp.float32
    )
    value_cross_grad = jnp.einsum(
        "smd,sme->de", memory_rows, value_low, preferred_element_type=jnp.float32
    )
    memory_grad = lax.all_to_all(
        row_grad.astype(jnp.bfloat16), "mem", split_axis=1, concat_axis=0, tiled=True
    ).astype(row_grad.dtype)
    probe_lowered_precision = query_grads.astype(jnp.bfloat16)
    query_cross_grad = jnp.einsum(
        "nhb,nhc->bc", first_reduced, probe_lowered_precision, preferred_element_type=jnp.float32
    )
    first_total = ALPHA * second_grad + jnp.einsum(
        "qwp,up->qwu",
        probe_lowered_precision,
        encoder_lookup_probe,
        preferred_element_type=jnp.float32,
    )
    first_grad, gain_one, shift_one = first_back(first_total)
    self_branch_gradient = first_grad.astype(jnp.bfloat16)
    output_self_grad = jnp.einsum(
        "nhb,nhc->bc", attention_result, self_branch_gradient, preferred_element_type=jnp.float32
    )
    attended_grad = jnp.einsum(
        "qwp,up->qwu",
        self_branch_gradient,
        self_attention_output,
        preferred_element_type=jnp.float32,
    ).astype(jnp.bfloat16)
    self_query_reduced, decoder_label_lowered, self_value_reduced = row_map(
        local_backward, (query, keys, values, self_allowed, self_lse, attended_grad)
    )
    self_query_reduced = self_query_reduced.astype(jnp.bfloat16)
    decoder_label_lowered = decoder_label_lowered.astype(jnp.bfloat16)
    self_value_reduced = self_value_reduced.astype(jnp.bfloat16)
    query_self_grad = jnp.einsum(
        "nhb,nhc->bc", tokens, self_query_reduced, preferred_element_type=jnp.float32
    )
    key_self_grad = jnp.einsum(
        "nhb,nhc->bc", tokens, decoder_label_lowered, preferred_element_type=jnp.float32
    )
    value_self_grad = jnp.einsum(
        "nhb,nhc->bc", tokens, self_value_reduced, preferred_element_type=jnp.float32
    )
    input_grad = (
        ALPHA * first_grad
        + jnp.einsum(
            "qwp,up->qwu",
            self_query_reduced,
            self_attention_query,
            preferred_element_type=jnp.float32,
        )
        + jnp.einsum(
            "qwp,up->qwu",
            decoder_label_lowered,
            decoder_match_label,
            preferred_element_type=jnp.float32,
        )
        + jnp.einsum(
            "qwp,up->qwu",
            self_value_reduced,
            self_attention_value,
            preferred_element_type=jnp.float32,
        )
    )
    gain_grad = jnp.stack([gain_one, gain_two, gain_three], axis=1)
    shift_grad = jnp.stack([shift_one, shift_two, shift_three], axis=1)
    sums = (
        lax.psum_scatter(query_self_grad, ("rows", "mem"), scatter_dimension=0, tiled=True),
        lax.psum_scatter(key_self_grad, ("rows", "mem"), scatter_dimension=0, tiled=True),
        lax.psum_scatter(value_self_grad, ("rows", "mem"), scatter_dimension=0, tiled=True),
        lax.psum_scatter(output_self_grad, ("rows", "mem"), scatter_dimension=0, tiled=True),
        lax.psum_scatter(query_cross_grad, ("rows", "mem"), scatter_dimension=0, tiled=True),
        lax.psum_scatter(key_cross_grad, ("rows", "mem"), scatter_dimension=0, tiled=True),
        lax.psum_scatter(value_cross_grad, ("rows", "mem"), scatter_dimension=0, tiled=True),
        lax.psum_scatter(output_cross_grad, ("rows", "mem"), scatter_dimension=0, tiled=True),
        lax.psum_scatter(expand_grad, ("rows", "mem"), scatter_dimension=0, tiled=True),
        lax.psum_scatter(
            down_projection_gradient, ("rows", "mem"), scatter_dimension=0, tiled=True
        ),
        lax.psum_scatter(gain_grad, ("rows", "mem"), scatter_dimension=0, tiled=True),
        lax.psum_scatter(shift_grad, ("rows", "mem"), scatter_dimension=0, tiled=True),
    )
    return (
        result,
        input_grad,
        memory_grad,
        sums[0],
        sums[1],
        sums[2],
        sums[3],
        sums[4],
        sums[5],
        sums[6],
        sums[7],
        sums[8],
        sums[9],
        jnp.transpose(sums[10]),
        jnp.transpose(sums[11]),
    )


ALL = slice(None)
TILE = 256
SLOTS = 3
VMEM_LIMIT = 61 * 1024 * 1024


def flip(index, unit):
    return index + unit * (1 - 2 * ((index // unit) % 2))


def span(index, size):
    return pl.ds(pl.multiple_of(index * size, size), size)


class Place:
    def __init__(self, n_rows, n_mem):
        self.n_rows, self.n_mem = n_rows, n_mem
        self.digits = (n_rows // 2).bit_length() - 1
        self.row = lax.axis_index("rows")
        self.mem = lax.axis_index("mem")
        self.lane = self.row % 2

    def turn(self, index, stage):
        rising, falling = 2 << stage, 2 << (self.digits - 1 - stage)
        return flip(index, rising) * (1 - self.lane) + flip(index, falling) * self.lane

    def sibling(self):
        return (flip(self.row, 1), self.mem)

    def partner(self, stage):
        return (self.turn(self.row, stage), self.mem)

    def far(self, step):
        return (self.row, (self.mem + step) % self.n_mem)

    def greet(self):
        barrier = pltpu.get_barrier_semaphore()
        others = [self.far(step) for step in range(1, self.n_mem)]
        others += [self.partner(stage) for stage in range(self.digits)]
        others += [self.sibling()]
        for other in others:
            pl.semaphore_signal(barrier, inc=1, device_id=other, device_id_type=MESH)
        pl.semaphore_wait(barrier, len(others))


def remote(source, target, send_sem, recv_sem, device):
    return pltpu.make_async_remote_copy(
        src_ref=source,
        dst_ref=target,
        send_sem=send_sem,
        recv_sem=recv_sem,
        device_id=device,
        device_id_type=MESH,
    )


def waits(total):
    return (lambda: total().wait_recv(), lambda: total().wait_send())


class Part:
    def __init__(self, source, target, columns, near=0, straight=False):
        self.source, self.target, self.columns = source, target, columns
        self.near, self.straight = near, straight


class Gather:
    def __init__(self, place, parts, sems):
        self.place, self.parts = place, parts
        (
            self.own_sem,
            self.far_send,
            self.far_recv,
            self.plane_send,
            self.plane_recv,
            self.core_send,
            self.core_recv,
            self.line_send,
            self.line_recv,
        ) = sems

    def rows(self, number, first, count):
        part = self.parts[number]
        size = part.source.shape[0]
        rows = pl.ds(pl.multiple_of(first * size, size), count * size)
        return part.target.at[rows, part.columns]

    def group(self, number, group):
        return self.rows(number, group * self.place.n_mem, self.place.n_mem)

    def one(self, number, group, member):
        return self.rows(number, group * self.place.n_mem + member, 1)

    def shard(self, number):
        part = self.parts[number]
        return part.source.at[:, part.columns]

    def mine(self, number):
        return self.one(number, self.place.row, self.place.mem)

    def own(self, number):
        return pltpu.make_async_copy(self.shard(number), self.mine(number), self.own_sem.at[number])

    def held(self, stage):
        groups = [self.place.row]
        for before in range(stage):
            groups = groups + [self.place.turn(group, before) for group in groups]
        return groups

    def far_total(self, number):
        some = self.rows(number, 0, (self.place.n_mem - 1) << self.parts[number].near)
        return remote(
            some, some, self.far_send.at[number], self.far_recv.at[number], self.place.far(1)
        )

    def far_hop(self, number, first):
        place = self.place
        for group in self.held(self.parts[number].near):
            target = self.one(number, group, place.mem)
            source = self.shard(number) if first else target
            for step in range(1, place.n_mem):
                remote(
                    source,
                    target,
                    self.far_send.at[number],
                    self.far_recv.at[number],
                    place.far(step),
                ).start()

    def sides(self, step):
        mem, n_mem = self.place.mem, self.place.n_mem
        return (
            ((mem - step >= 0) & (mem + 1 < n_mem), mem - step, 1, mem - 1 - step >= 0),
            ((mem + step < n_mem) & (mem >= 1), mem + step, n_mem - 1, mem + 1 + step < n_mem),
        )

    def line_total(self, number, step, side):
        some = self.rows(number, 0, 1 << self.parts[number].near)
        sems = (self.line_send.at[2 * step + side, number], self.line_recv.at[2 * step + side, number])
        return remote(some, some, *sems, self.place.far(1))

    def line_arrived(self, number, step):
        for side, (_, _, _, receives) in enumerate(self.sides(step)):

            @pl.when(receives)
            def _(side=side):
                self.line_total(number, step, side).wait_recv()

    def line_sent(self, number, step):
        for side, (sends, _, _, _) in enumerate(self.sides(step)):

            @pl.when(sends)
            def _(side=side):
                self.line_total(number, step, side).wait_send()

    def line_hop(self, number, step, first):
        place = self.place
        for side, (sends, member, towards, _) in enumerate(self.sides(step)):
            member = (member + place.n_mem) % place.n_mem

            @pl.when(sends)
            def _(side=side, member=member, towards=towards):
                for group in self.held(self.parts[number].near):
                    target = self.one(number, group, member)
                    remote(
                        self.shard(number) if first else target,
                        target,
                        self.line_send.at[2 * step + side, number],
                        self.line_recv.at[2 * step + side, number],
                        place.far(towards),
                    ).start()

    def plane_total(self, number, stage):
        shards = 1 if stage < self.parts[number].near else self.place.n_mem
        some = self.rows(number, 0, shards << stage)
        return remote(
            some,
            some,
            self.plane_send.at[stage, number],
            self.plane_recv.at[stage, number],
            self.place.partner(stage),
        )

    def plane_hop(self, number, stage, first):
        for group in self.held(stage):
            if stage < self.parts[number].near:
                target = self.one(number, group, self.place.mem)
            else:
                target = self.group(number, group)
            remote(
                self.shard(number) if first else target,
                target,
                self.plane_send.at[stage, number],
                self.plane_recv.at[stage, number],
                self.place.partner(stage),
            ).start()

    def core_total(self, number):
        some = self.rows(number, 0, self.place.n_mem * self.place.n_rows // 2)
        return remote(
            some, some, self.core_send.at[number], self.core_recv.at[number], self.place.sibling()
        )

    def core_hop(self, number, first):
        for group in self.held(self.place.digits):
            block = self.group(number, group)
            remote(
                block,
                block,
                self.core_send.at[number],
                self.core_recv.at[number],
                self.place.sibling(),
            ).start()

    def hops(self, number):
        part, take = self.parts[number], functools.partial
        along = []
        if part.straight:
            along.append((1.6, take(self.far_hop, number)) + waits(take(self.far_total, number)))
        else:
            for step in range(self.place.n_mem - 1):
                along.append(
                    (
                        0.55 if step else 1.4,
                        take(self.line_hop, number, step),
                        take(self.line_arrived, number, step),
                        take(self.line_sent, number, step),
                    )
                )
        plane = []
        for stage in range(self.place.digits):
            total = take(self.plane_total, number, stage)
            plane.append((1.5, take(self.plane_hop, number, stage)) + waits(total))
        core = (1.5, take(self.core_hop, number)) + waits(take(self.core_total, number))
        return plane[: part.near] + along + plane[part.near :] + [core]

    def events(self, number):
        hops = self.hops(number)
        time, found = float(number), []

        def act(at):
            if at == 0:
                self.own(number).start()
            else:
                if at == 1:
                    self.own(number).wait()
                hops[at - 1][2]()
            hops[at][1](at == 0)

        for at in range(len(hops)):
            time += hops[at][0] if at else 0.0
            found.append((time, functools.partial(act, at)))
        return found, time + 0.9

    def finish(self):
        for number in range(len(self.parts)):
            for hop in self.hops(number):
                hop[3]()


class Job:
    def __init__(self, left, right, first, target, far_at):
        self.left, self.right, self.first, self.target = left, right, first, target
        self.small = right is None
        self.far_at = far_at
        self.width = target.shape[-1]
        self.large = self.at = 0


OUT_SLOTS, LANE_SLOTS, SUM_SLOTS, CORE_RING, FIRST_RING, RING = 2, 3, 2, 2, 6, 4


class Reduce:
    def __init__(self, place, jobs, sems, buffers):
        self.place, self.jobs, self.buffers = place, jobs, buffers
        self.core_send, self.core_recv, self.stage_send, self.stage_recv = sems
        wanted = [place.row]
        for stage in reversed(range(place.digits)):
            wanted = wanted + [place.turn(group, stage) for group in wanted]
        self.wanted = [group // 2 for group in wanted]
        large = [job for job in jobs if not job.small]
        for number, job in enumerate(large):
            job.large = number
            job.at = [item for item in large if item.far_at == job.far_at].index(job)

    def cut(self, ref, job):
        columns = pl.ds(0, job.width)
        return ref if job.width == ref.shape[-1] else ref.at[(ALL,) * (len(ref.shape) - 1) + (columns,)]

    def out(self, job):
        return self.cut(self.buffers.out.at[job.large % OUT_SLOTS], job)

    def lanes(self, job):
        if job.small:
            return self.buffers.small_lanes
        return self.cut(self.buffers.lanes.at[job.large % LANE_SLOTS], job)

    def core_in(self, job):
        if job.small:
            return self.buffers.small_core_in
        return self.cut(self.buffers.core_in.at[job.large % CORE_RING], job)

    def count(self, job, stage):
        return 1 << (self.place.digits - stage - (stage < job.far_at))

    def sums(self, job, stage):
        if stage == self.place.digits:
            return job.target
        if job.small:
            return self.buffers.small_sums[stage]
        if stage == 0 and job.far_at > 0:
            return self.cut(self.buffers.first_sums.at[job.large % SUM_SLOTS], job)
        return self.cut(self.buffers.sums[job.far_at][stage].at[job.at % SUM_SLOTS], job)

    def arrived(self, job, stage):
        if job.small:
            return self.buffers.small_arrived[stage]
        if stage == 0 and job.far_at > 0:
            return self.cut(self.buffers.first_arrived.at[job.large % FIRST_RING], job)
        ring = self.buffers.arrived[job.far_at][stage]
        return self.cut(ring.at[job.at % ring.shape[0]], job)

    def previous(self, number, same, distance):
        found = [n for n in range(number) if same(self.jobs[n])]
        return found[-distance] if len(found) >= distance else None

    def is_large(self, job):
        return not job.small

    def reuse(self, number, stage):
        job = self.jobs[number]
        if job.small:
            return None
        if stage == 0 and job.far_at > 0:
            return self.previous(number, lambda item: not item.small and item.far_at > 0, SUM_SLOTS)
        return self.previous(
            number, lambda item: not item.small and item.far_at == job.far_at, SUM_SLOTS
        )

    def core_copy(self, number):
        job = self.jobs[number]
        source = job.left.at[1 - self.place.lane] if job.small else self.out(job)
        return remote(
            source,
            self.core_in(job),
            self.core_send.at[number],
            self.core_recv.at[number],
            self.place.sibling(),
        )

    def product(self, job, side, store):
        half = self.place.n_rows // 2
        group = job.left.shape[1] // half
        width = min(TILE, job.width)

        def column_step(step, carry):
            source = pl.ds(pl.multiple_of(job.first + step * width, width), width)
            value = dot(job.left[side], job.right[:, source])
            for index in range(half):
                store(index, span(step, width), value[index * group : (index + 1) * group])
            return carry

        lax.fori_loop(0, job.width // width, column_step, 0)

    def core_stage(self, number):
        job = self.jobs[number]
        if not job.small:
            before = self.previous(number, self.is_large, OUT_SLOTS)
            if before is not None:
                self.core_copy(before).wait_send()
            out = self.out(job)

            def store(index, columns, value):
                out[index, :, columns] = value.astype(out.dtype)

            self.product(job, 1 - self.place.lane, store)
        self.core_copy(number).start()

    def lane_stage(self, number):
        job = self.jobs[number]
        if not job.small:
            before = self.previous(number, self.is_large, LANE_SLOTS)
            if before is not None:
                self.total(before, 0).wait_send()
        lanes, arrived = self.lanes(job), self.core_in(job)
        self.core_copy(number).wait_recv()
        if job.small:
            lanes[...] = job.left[self.place.lane] + arrived[...]
        else:

            def store(index, columns, value):
                total = value + arrived[index, :, columns].astype(jnp.float32)
                lanes[index, :, columns] = total.astype(lanes.dtype)

            self.product(job, self.place.lane, store)
        self.send(number, 0)

    def unit(self, job, stage, index):
        if stage == 0:
            return self.lanes(job).at[self.wanted[index]]
        return self.sums(job, stage - 1).at[index]

    def member_rows(self, job, unit, member):
        if job.small:
            return unit
        size = unit.shape[0] // self.place.n_mem
        return unit.at[span(member, size)]

    def send(self, number, stage):
        job, place = self.jobs[number], self.place
        left = self.count(job, stage)
        arrived = self.arrived(job, stage)
        sems = (self.stage_send.at[stage, number], self.stage_recv.at[stage, number])
        for index in range(left):
            if stage == job.far_at:
                unit = self.unit(job, stage, index)
                for step in range(1, place.n_mem):
                    source = self.member_rows(job, unit, (place.mem + step) % place.n_mem)
                    remote(source, arrived.at[step - 1, index], *sems, place.far(step)).start()
            else:
                source = self.unit(job, stage, left + index)
                partner = place.partner(stage - (stage > job.far_at))
                remote(source, arrived.at[index], *sems, partner).start()

    def total(self, number, stage):
        some = self.arrived(self.jobs[number], stage)
        sems = (self.stage_send.at[stage, number], self.stage_recv.at[stage, number])
        return remote(some, some, *sems, self.place.far(1))

    def stage(self, number, stage):
        job, place = self.jobs[number], self.place
        last = stage == place.digits
        before = self.reuse(number, stage)
        if before is not None and not last:
            self.total(before, stage + 1).wait_send()
        self.total(number, stage).wait_recv()
        arrived, sums = self.arrived(job, stage), self.sums(job, stage)
        for index in range(self.count(job, stage)):
            unit = self.unit(job, stage, index)
            if stage == job.far_at:
                unit = self.member_rows(job, unit, place.mem)
                coming = [arrived.at[step, index] for step in range(place.n_mem - 1)]
            else:
                coming = [arrived.at[index]]
            target = sums if last else sums.at[index]
            block = min(32, unit.shape[0])

            def add(step, carry, unit=unit, coming=coming, target=target, block=block):
                rows = span(step, block)
                value = unit[rows].astype(jnp.float32)
                for item in coming:
                    value = value + item[rows].astype(jnp.float32)
                target[rows] = value.astype(target.dtype)
                return carry

            lax.fori_loop(0, unit.shape[0] // block, add, 0)
        if not last:
            self.send(number, stage + 1)

    def events(self, number):
        found = [(0.0, functools.partial(self.core_stage, number))]
        found.append((0.9, functools.partial(self.lane_stage, number)))
        time = 2.2 if number < 2 else 3.2
        for stage in range(self.place.digits + 1):
            found.append((time, functools.partial(self.stage, number, stage)))
            time += 1.4
        found[-1] = (found[-1][0] - 0.3, found[-1][1])
        return [(number + time, action) for time, action in found]

    def finish(self):
        n_jobs, last = len(self.jobs), self.place.digits
        out, lanes, sums = set(), set(), set()
        for number in range(n_jobs):
            if not self.jobs[number].small:
                out.add(self.previous(number, self.is_large, OUT_SLOTS))
                lanes.add(self.previous(number, self.is_large, LANE_SLOTS))
                for stage in range(last):
                    sums.add((self.reuse(number, stage), stage + 1))
        for number in range(n_jobs):
            if number not in out:
                self.core_copy(number).wait_send()
            if number not in lanes:
                self.total(number, 0).wait_send()
            for stage in range(1, last + 1):
                if (number, stage) not in sums:
                    self.total(number, stage).wait_send()


NORMAL = (((1,), (0,)), ((), ()))
TURNED = (((1,), (1,)), ((), ()))
LEFT_TURNED = (((0,), (0,)), ((), ()))


def dot(left, right, dims=NORMAL):
    return lax.dot_general(left, right, dims, preferred_element_type=jnp.float32)


def times(left, weight, store):
    width = min(TILE, weight.shape[1])

    def column_step(step, carry):
        columns = span(step, width)
        store(columns, dot(left[...], weight[:, columns]))
        return carry

    lax.fori_loop(0, weight.shape[1] // width, column_step, 0)


def times_turned(left, weight, store):
    width = min(TILE, weight.shape[0])

    def column_step(step, carry):
        columns = span(step, width)
        store(columns, dot(left[...], weight[columns, :], TURNED))
        return carry

    lax.fori_loop(0, weight.shape[0] // width, column_step, 0)


def into(target):
    def store(columns, value):
        target[:, columns] = value.astype(target.dtype)

    return store


ROWS = 32


def by_rows(count, step):
    def body(index, carry):
        step(span(index, ROWS))
        return carry

    lax.fori_loop(0, count // ROWS, body, 0)


def norm_forward(total, gains, index, unit, scale, use):
    gain, shift = gains[index : index + 1, :], gains[index + 3 : index + 4, :]

    def step(rows):
        value = total[rows, :]
        centre = value - jnp.mean(value, axis=-1, keepdims=True)
        spread = jnp.mean(centre * centre, axis=-1, keepdims=True)
        root = lax.rsqrt(spread + EPS)
        scaled = centre * root
        unit[rows, :] = scaled
        scale[rows, :] = root
        use(rows, scaled * gain + shift)

    by_rows(total.shape[0], step)


def norm_slope(incoming, scaled, root, gain):
    width = scaled.shape[1]
    scaled_grad = incoming * gain
    first = jnp.mean(scaled_grad, axis=-1, keepdims=True)
    second = jnp.mean(scaled_grad * scaled, axis=-1, keepdims=True)
    value = root * (scaled_grad - first - scaled * second)
    of_gain = jnp.sum((incoming * scaled).reshape(ROWS // 8, 8, width), axis=0)
    of_shift = jnp.sum(incoming.reshape(ROWS // 8, 8, width), axis=0)
    return value, of_gain, of_shift


def keep_small(index, sums, small):
    for offset, partial in ((index, sums[0]), (index + 3, sums[1])):
        line = jnp.sum(partial, axis=0, keepdims=True)
        for group in range(2 * small.shape[1]):
            small[group % 2, group // 2, offset : offset + 1, :] = line[
                :, group * 128 : (group + 1) * 128
            ]


def norm_backward(grad, gains, index, unit, scale, target, target_low, small):
    gain = gains[index : index + 1, :]

    def body(block, sums):
        rows = span(block, ROWS)
        value, of_gain, of_shift = norm_slope(grad[rows, :], unit[rows, :], scale[rows, :], gain)
        target[rows, :] = value
        target_low[rows, :] = value.astype(target_low.dtype)
        return (sums[0] + of_gain, sums[1] + of_shift)

    zero = jnp.zeros((8, unit.shape[1]), jnp.float32)
    keep_small(index, lax.fori_loop(0, unit.shape[0] // ROWS, body, (zero, zero)), small)


def norm_both(total, grad, gains, index, result, target, target_low, small):
    gain, shift = gains[index : index + 1, :], gains[index + 3 : index + 4, :]

    def body(block, sums):
        rows = span(block, ROWS)
        value = total[rows, :]
        centre = value - jnp.mean(value, axis=-1, keepdims=True)
        spread = jnp.mean(centre * centre, axis=-1, keepdims=True)
        root = lax.rsqrt(spread + EPS)
        scaled = centre * root
        result[rows, :] = scaled * gain + shift
        incoming = grad[rows, :].astype(jnp.float32)
        value, of_gain, of_shift = norm_slope(incoming, scaled, root, gain)
        target[rows, :] = value
        target_low[rows, :] = value.astype(target_low.dtype)
        return (sums[0] + of_gain, sums[1] + of_shift)

    zero = jnp.zeros((8, total.shape[1]), jnp.float32)
    keep_small(index, lax.fori_loop(0, total.shape[0] // ROWS, body, (zero, zero)), small)


def lane_masks(dtype):
    low = lax.broadcasted_iota(jnp.int32, (1, 2 * HEAD_DIM), 1) < HEAD_DIM
    first = jnp.where(low, 1.0, 0.0)
    return first.astype(dtype), (1.0 - first).astype(dtype)


def attention_forward(query, keys, values, bias, mixed, lse):
    masks = lane_masks(query.dtype)
    keep = lane_masks(jnp.float32)

    def pair_step(pair, carry):
        lanes = span(pair, 2 * HEAD_DIM)
        two_query, two_keys, two_values = query[:, lanes], keys[:, lanes], values[:, lanes]
        total = None
        for head in range(2):
            scores = dot(two_keys, two_query * masks[head], TURNED) * SCALE + bias[...]
            top = jnp.max(scores, axis=0, keepdims=True)
            weight = jnp.exp(scores - top)
            norm = jnp.sum(weight, axis=0, keepdims=True)
            probs = (weight * (1.0 / norm)).astype(query.dtype)
            part = dot(probs, two_values, LEFT_TURNED) * keep[head]
            total = part if total is None else total + part
            lse[pair, head : head + 1, :] = top + jnp.log(norm)
        mixed[:, lanes] = total.astype(mixed.dtype)
        return carry

    lax.fori_loop(0, lse.shape[0], pair_step, 0)


def attention_backward(
    query, keys, values, bias, lse, grad, query_grad, key_grad, value_grad, first, last
):
    masks = lane_masks(query.dtype)
    keep = lane_masks(jnp.float32)

    def pair_step(pair, carry):
        lanes = span(pair, 2 * HEAD_DIM)
        two_query, two_keys, two_values = query[:, lanes], keys[:, lanes], values[:, lanes]
        two_grad = grad[:, lanes]
        sums = [None, None, None]
        for head in range(2):
            scores = dot(two_keys, two_query * masks[head], TURNED) * SCALE + bias[...]
            probs = jnp.exp(scores - lse[pair, head : head + 1, :])
            pulled = dot(two_values, two_grad * masks[head], TURNED)
            inner = jnp.sum(probs * pulled, axis=0, keepdims=True)
            slope = (probs * (pulled - inner) * SCALE).astype(query.dtype)
            parts = (
                dot(slope, two_keys, LEFT_TURNED),
                dot(slope, two_query),
                dot(probs.astype(query.dtype), two_grad),
            )
            for index, part in enumerate(parts):
                part = part * keep[head]
                sums[index] = part if sums[index] is None else sums[index] + part
        query_grad[:, lanes] = sums[0].astype(query_grad.dtype)
        key_grad[:, lanes] = sums[1].astype(key_grad.dtype)
        value_grad[:, lanes] = sums[2].astype(value_grad.dtype)
        return carry

    lax.fori_loop(first, last, pair_step, 0)


def turn_blocks(left, eye, store):
    width = eye.shape[0]
    for block in range(left.shape[1] // width):
        columns = pl.ds(block * width, width)
        store(block, dot(eye[...], left[:, columns], TURNED).astype(left.dtype))


def turn_by_lane(left, eye, target):
    group = eye.shape[0] // 2

    def store(block, value):
        target[0, pl.ds(block * group, group), :] = value[:group]
        target[1, pl.ds(block * group, group), :] = value[group:]

    turn_blocks(left, eye, store)


SQUARES = 8


def layer_kernel(places, sizes, *refs):
    n_rows, n_mem, width, ff, shard = sizes
    ref = SimpleNamespace(**jax.tree.map(lambda place: refs[place], places))
    place = Place(n_rows, n_mem)
    many = ff // width
    own_ff = ff // (n_rows * n_mem)
    (
        at_query,
        at_key,
        at_value,
        at_output,
        at_cross_query,
        at_cross_key,
        at_cross_value,
        at_cross_output,
    ) = range(SQUARES)
    full = ref.full
    expand, contract = ref.expand_full, ref.contract_full
    tokens, gains = ref.tokens, ref.gains
    low, turned = SimpleNamespace(**ref.low), SimpleNamespace(**ref.turned)

    order = [
        at_query,
        at_key,
        at_value,
        at_output,
        at_cross_key,
        at_cross_value,
        at_cross_query,
        at_cross_output,
    ]
    narrow = width // many
    weights = [(ref.squares[index], full[index], ALL) for index in order]
    weights += [(ref.expand, expand, pl.ds(j * width, width)) for j in range(many)]
    weights += [(ref.contract, contract, pl.ds(j * narrow, narrow)) for j in range(many)]
    parts = [Part(*weight, number % 3 != 0) for number, weight in enumerate(weights)]
    parts.insert(SMALL_AT, Part(ref.small, ref.small_full, ALL, 0, True))
    gather = Gather(place, parts, ref.gather_sems)

    slots, slot_sem = ref.slots, ref.slot_sem
    count = [0]

    def load(pieces):
        number = count[0]
        count[0] += 1
        slot = slots.at[number % SLOTS]
        for source, columns in pieces:
            pltpu.make_async_copy(source, slot.at[:, columns], slot_sem.at[number % SLOTS]).start()
        return number

    def ready(number):
        slot = slots.at[number % SLOTS]
        pltpu.make_async_copy(slot, slot, slot_sem.at[number % SLOTS]).wait()
        return slot

    def expand_block(j):
        return [(expand.at[:, pl.ds(j * width, width)], ALL)]

    def contract_columns(j):
        return [
            (
                contract.at[pl.ds(i * width, width), pl.ds(j * narrow, narrow)],
                pl.ds(i * narrow, narrow),
            )
            for i in range(many)
        ]

    def contract_rows(j):
        return [(contract.at[pl.ds(j * width, width), :], ALL)]

    mem_block = ref.memory.shape[1]
    memory, mem_rows = ref.memory, ref.mem_rows

    def memory_own():
        return pltpu.make_async_copy(
            memory.at[place.mem], mem_rows.at[span(place.mem, mem_block)], ref.mem_sem.at[0]
        )

    def memory_total():
        some = mem_rows.at[pl.ds(0, (n_mem - 1) * mem_block)]
        return remote(some, some, ref.mem_sem.at[1], ref.mem_sem.at[2], place.far(1))

    ref.small[...] = jnp.zeros_like(ref.small)
    for member in range(n_mem):

        @pl.when(place.mem == member)
        def _(member=member):
            lanes = slice(member * shard, (member + 1) * shard)
            ref.small[0:3, lanes] = ref.norm_gains[...].astype(jnp.float32)
            ref.small[3:6, lanes] = ref.norm_shifts[...].astype(jnp.float32)

    place.greet()
    actions = []
    whole = []
    for part in range(len(parts)):
        found, time = gather.events(part)
        actions += found
        whole.append(time)
    actions.sort(key=lambda item: item[0])
    start = [action for action in actions if action[0] < 2]
    actions = actions[len(start) :]
    for _, action in start:
        action()
    memory_own().start()
    for step in range(1, n_mem):
        remote(
            memory.at[(place.mem + step) % n_mem],
            mem_rows.at[span(place.mem, mem_block)],
            ref.mem_sem.at[1],
            ref.mem_sem.at[2],
            place.far(step),
        ).start()

    self_bias, cross_bias, eye = ref.self_bias, ref.cross_bias, ref.eye
    own_row = ref.token_ids[pl.ds(place.mem, 1), :].astype(jnp.float32)
    mem_row = ref.memory_ids[pl.ds(place.mem, 1), :].astype(jnp.float32)
    key_place = lax.broadcasted_iota(jnp.int32, self_bias.shape, 0)
    query_place = lax.broadcasted_iota(jnp.int32, self_bias.shape, 1)
    own_wide = jnp.broadcast_to(own_row, self_bias.shape)
    mem_wide = jnp.broadcast_to(mem_row, (cross_bias.shape[1], cross_bias.shape[0]))
    same = (jnp.transpose(own_wide) == own_wide) & (key_place <= query_place)
    self_bias[...] = jnp.where(same, 0.0, NEG)
    cross_bias[...] = jnp.where(jnp.transpose(mem_wide) == own_row, 0.0, NEG)
    eye_row = lax.broadcasted_iota(jnp.int32, eye.shape, 0)
    eye_column = lax.broadcasted_iota(jnp.int32, eye.shape, 1)
    eye[...] = jnp.where(eye_row == eye_column, 1.0, 0.0).astype(eye.dtype)
    turn_by_lane(tokens, eye, turned.tokens)

    accumulated, other = ref.accumulated, ref.other
    hidden, slope, hidden_turned = ref.hidden, ref.slope, ref.hidden_turned

    def small_piece():
        blocks = ref.small_full
        for group in range(n_rows):
            total = None
            for member in range(n_mem):
                first = (group * n_mem + member) * 8
                value = blocks[first : first + 8, :]
                total = value if total is None else total + value
            gains[:, group * 128 : (group + 1) * 128] = total

    def query_piece(slot):
        times(tokens, slot, into(ref.query))

    def key_piece(slot):
        times(tokens, slot, into(ref.keys))

    def value_piece(slot):
        times(tokens, slot, into(ref.values))
        attention_forward(
            ref.query, ref.keys, ref.values, self_bias, ref.attended, ref.self_lse
        )

    def output_piece(slot):
        def store(columns, value):
            accumulated[:, columns] = ALPHA * tokens[:, columns].astype(jnp.float32) + value

        times(ref.attended, slot, store)

        def use(rows, value):
            ref.first_low[rows, :] = value.astype(jnp.bfloat16)
            other[rows, :] = value

        norm_forward(accumulated, gains, 0, ref.unit1, ref.scale1, use)
        turn_by_lane(ref.attended, eye, turned.attended)

    def cross_key_piece(slot):
        memory_own().wait()
        memory_total().wait_recv()
        times(mem_rows, slot, into(ref.cross_keys))
        turn_by_lane(mem_rows, eye, turned.memory)

    def cross_value_piece(slot):
        times(mem_rows, slot, into(ref.cross_values))
        turn_by_lane(ref.first_low, eye, turned.first)

    def cross_query_piece(slot):
        times(ref.first_low, slot, into(ref.cross_query))
        attention_forward(
            ref.cross_query,
            ref.cross_keys,
            ref.cross_values,
            cross_bias,
            ref.crossed,
            ref.cross_lse,
        )

    def cross_output_piece(slot):
        def store(columns, value):
            accumulated[:, columns] = ALPHA * other[:, columns] + value

        times(ref.crossed, slot, store)

        def use(rows, value):
            ref.second_low[rows, :] = value.astype(jnp.bfloat16)
            other[rows, :] = value

        norm_forward(accumulated, gains, 1, ref.unit2, ref.scale2, use)
        turn_by_lane(ref.crossed, eye, turned.crossed)

    def expand_piece(j, slot):
        def store(columns, value):
            there = pl.ds(pl.multiple_of(j * width + columns.start, TILE), columns.size)
            bell = 0.5 * (1.0 + lax.erf(value * math.sqrt(0.5)))
            density = jnp.exp(value * value * -0.5) * (1.0 / math.sqrt(2.0 * math.pi))
            hidden[:, there] = (value * bell).astype(hidden.dtype)
            slope[:, there] = (bell + value * density).astype(slope.dtype)

        times(ref.second_low, slot, store)

        def keep(block, value):
            for index in range(value.shape[0] // shard):
                first = j * width + block * value.shape[0] + index * shard
                device, job = first // own_ff, first % own_ff // shard
                group, member = device // n_mem, device % n_mem
                at = group // 2 * n_mem * shard + member * shard
                hidden_turned[job, group % 2, at : at + shard, :] = value[
                    index * shard : (index + 1) * shard
                ]

        turn_blocks(hidden.at[:, pl.ds(j * width, width)], eye, keep)

    def contract_piece(j, slot):
        total = None
        for i in range(many):
            value = dot(
                hidden[:, i * width : (i + 1) * width], slot[:, i * narrow : (i + 1) * narrow]
            )
            total = value if total is None else total + value
        columns = pl.ds(j * narrow, narrow)
        accumulated[:, columns] = ALPHA * other[:, columns] + total

    pieces = [
        query_piece,
        key_piece,
        value_piece,
        output_piece,
        cross_key_piece,
        cross_value_piece,
        cross_query_piece,
        cross_output_piece,
    ]
    sources = [[(full[index], ALL)] for index in order]
    for j in range(many):
        pieces.append(functools.partial(expand_piece, j))
        sources.append(expand_block(j))
    for j in range(many):
        pieces.append(functools.partial(contract_piece, j))
        sources.append(contract_columns(j))

    waiting = []

    def arrive(part):
        gather.core_total(part).wait_recv()
        if part != SMALL_AT:
            number = part - (part > SMALL_AT)
            waiting.append((number, load(sources[number])))

    def use():
        number, slot = waiting.pop(0)
        pieces[number](ready(slot))

    last = 0.0
    for part, time in enumerate(whole):
        time = max(time, last + 0.2)
        actions.append((time, functools.partial(arrive, part)))
        actions.append((time + 0.5, small_piece if part == SMALL_AT else use))
        last = time
    actions.sort(key=lambda item: item[0])
    for _, action in actions:
        action()

    backward_sources, loads = [], []
    used = [0]

    def next_slot():
        slot = ready(loads[used[0]])
        used[0] += 1
        if len(loads) < len(backward_sources):
            loads.append(load(backward_sources[len(loads)]))
        return slot

    small_sums = ref.small_sums
    small_sums[...] = jnp.zeros_like(small_sums)
    def inner_piece(j):
        slot = next_slot()

        def store(columns, value):
            there = pl.ds(pl.multiple_of(j * width + columns.start, TILE), columns.size)
            slope[:, there] = (value * slope[:, there].astype(jnp.float32)).astype(slope.dtype)

        times_turned(low.third, slot, store)

    def second_piece(j):
        slot = next_slot()

        def store(columns, value):
            if j == 0:
                other[:, columns] = ALPHA * accumulated[:, columns] + value
            else:
                other[:, columns] = other[:, columns] + value

        times_turned(slope.at[:, pl.ds(j * width, width)], slot, store)

    def second_norm_piece():
        norm_backward(
            other, gains, 1, ref.unit2, ref.scale2, accumulated, low.second, small_sums
        )

    pairs = width // (2 * HEAD_DIM)

    def cross_start_piece():
        times_turned(low.second, next_slot(), into(low.branch))

    def cross_piece(first, last):
        attention_backward(
            ref.cross_query,
            ref.cross_keys,
            ref.cross_values,
            cross_bias,
            ref.cross_lse,
            low.branch,
            low.cross_query,
            low.cross_key,
            low.cross_value,
            first,
            last,
        )

    def first_piece():
        def store(columns, value):
            other[:, columns] = ALPHA * accumulated[:, columns] + value

        times_turned(low.cross_query, next_slot(), store)
        norm_backward(other, gains, 0, ref.unit1, ref.scale1, accumulated, low.first, small_sums)

    def self_start_piece():
        times_turned(low.first, next_slot(), into(low.branch))

    def self_piece(first, last):
        attention_backward(
            ref.query,
            ref.keys,
            ref.values,
            self_bias,
            ref.self_lse,
            low.branch,
            low.query,
            low.key,
            low.value,
            first,
            last,
        )

    mem_out, mem_in = ref.mem_out, ref.mem_in

    def grad_own():
        return pltpu.make_async_copy(
            mem_out.at[span(place.mem, mem_block)], mem_in.at[place.mem], ref.mem_sem.at[3]
        )

    def grad_total():
        some = mem_in.at[pl.ds(0, n_mem - 1)]
        return remote(some, some, ref.mem_sem.at[4], ref.mem_sem.at[5], place.far(1))

    def memory_key_piece():
        times_turned(low.cross_key, next_slot(), into(other))

    def memory_value_piece():
        def store(columns, value):
            mem_out[:, columns] = (other[:, columns] + value).astype(mem_out.dtype)

        times_turned(low.cross_value, next_slot(), store)
        grad_own().start()
        for step in range(1, n_mem):
            remote(
                mem_out.at[span((place.mem + step) % n_mem, mem_block)],
                mem_in.at[place.mem],
                ref.mem_sem.at[4],
                ref.mem_sem.at[5],
                place.far(step),
            ).start()

    def input_piece(left, start):
        target = ref.input_grad

        def store(columns, value):
            if start:
                target[:, columns] = ALPHA * accumulated[:, columns] + value
            else:
                target[:, columns] = target[:, columns] + value

        times_turned(left, next_slot(), store)

    def memory_end_piece():
        grad_own().wait()
        grad_total().wait_recv()
        for member in range(n_mem):
            ref.memory_grad[member] = mem_in[member].astype(jnp.float32)

    halves = ((0, width // 2), (width // 2, width // 2))
    grads = ref.grads
    plans = []
    for j in range(many):
        for first, columns in halves if j == 0 else ((0, width),):
            target = ref.contract_grad.at[pl.ds(j * shard, shard), pl.ds(first, columns)]
            plans.append((hidden_turned.at[j], low.third, first, target))
    for j in range(many):
        target = ref.expand_grad.at[:, pl.ds(j * width, width)]
        plans.append((turned.second, slope, j * width, target))
    plans += [
        (turned.crossed, low.second, 0, grads[at_cross_output]),
        (turned.memory, low.cross_key, 0, grads[at_cross_key]),
        (turned.memory, low.cross_value, 0, grads[at_cross_value]),
        (turned.first, low.cross_query, 0, grads[at_cross_query]),
        (turned.attended, low.first, 0, grads[at_output]),
        (small_sums, None, 0, ref.small_total),
        (turned.tokens, low.query, 0, grads[at_query]),
        (turned.tokens, low.key, 0, grads[at_key]),
    ]
    for first, columns in halves:
        target = grads[at_value].at[:, pl.ds(first, columns)]
        plans.append((turned.tokens, low.value, first, target))
    jobs = []
    for number, plan in enumerate(plans):
        jobs.append(Job(*plan, place.digits))
    reduce = Reduce(place, jobs, ref.reduce_sems, SimpleNamespace(**ref.buffers))

    inner = [functools.partial(inner_piece, j) for j in range(many)]
    second = [functools.partial(second_piece, j) for j in range(many)]
    middle = pairs // 2
    base = many + 1
    def weight(index):
        return [(full[index], ALL)]

    turn = functools.partial(turn_by_lane, ref.second_low, eye, turned.second)
    work = [(base - 1.7, inner[0], contract_rows(0)), (base - 1.3, turn, None)]
    work += [(base - 1.7 + j, inner[j], contract_rows(j)) for j in range(1, many)]
    work += [(base - 0.3 + j, second[j], expand_block(j)) for j in range(many)]
    base = 2 * many + 1
    work += [
        (base - 0.2, second_norm_piece, None),
        (base - 0.15, cross_start_piece, weight(at_cross_output)),
        (base + 0.3, functools.partial(cross_piece, 0, middle), None),
        (base + 0.7, functools.partial(cross_piece, middle, pairs), None),
        (base + 1.3, first_piece, weight(at_cross_query)),
        (base + 1.7, self_start_piece, weight(at_output)),
        (base + 2.3, functools.partial(self_piece, 0, middle), None),
        (base + 3.3, functools.partial(self_piece, middle, pairs), None),
        (base + 3.7, memory_key_piece, weight(at_cross_key)),
        (base + 4.3, memory_value_piece, weight(at_cross_value)),
        (base + 4.7, functools.partial(input_piece, low.query, True), weight(at_query)),
        (base + 5.5, functools.partial(input_piece, low.key, False), weight(at_key)),
        (base + 6.5, functools.partial(input_piece, low.value, False), weight(at_value)),
        (base + 8.5, memory_end_piece, None),
    ]
    work.sort(key=lambda item: item[0])
    backward_sources += [source for _, _, source in work if source is not None]
    loads += [load(backward_sources[0]), load(backward_sources[1])]
    norm_both(
        accumulated, ref.out_grad, gains, 2, ref.result, accumulated, low.third, small_sums
    )

    actions = [(time, piece) for time, piece, _ in work]
    for number in range(len(jobs)):
        actions += reduce.events(number)
    actions.sort(key=lambda item: item[0])
    for _, action in actions:
        action()

    total = ref.small_total[...]
    own = jnp.zeros((8, shard), jnp.float32)
    for member in range(n_mem):
        here = jnp.where(place.mem == member, 1.0, 0.0)
        own = own + here * total[:, member * shard : (member + 1) * shard]
    ref.gains_grad[...] = own[0:3]
    ref.shifts_grad[...] = own[3:6]
    gather.finish()
    reduce.finish()
    memory_total().wait_send()
    grad_total().wait_send()


SMALL_AT = 2


def copy_kernel(count, *refs):
    for source, target in zip(refs[:count], refs[count:]):
        target[...] = source[...]


def copied(values):
    near = pl.BlockSpec(memory_space=pltpu.VMEM)
    return pl.pallas_call(
        functools.partial(copy_kernel, len(values)),
        out_shape=[jax.ShapeDtypeStruct(value.shape, value.dtype) for value in values],
        in_specs=[near] * len(values),
        out_specs=[near] * len(values),
        compiler_params=pltpu.CompilerParams(vmem_limit_bytes=VMEM_LIMIT),
        name="results",
    )(*values)


def fused(n_rows, n_mem, ins):
    tokens, memory, squares = ins["tokens"], ins["memory"], ins["squares"]
    expand, contract = ins["expand"], ins["contract"]
    tokens_here, width = tokens.shape
    ff = expand.shape[1]
    shard = squares[0].shape[0]
    mem_tokens = memory.shape[0] * memory.shape[1]
    digits, half, many = (n_rows // 2).bit_length() - 1, n_rows // 2, ff // width
    pairs = width // (2 * HEAD_DIM)
    low, high = jnp.bfloat16, jnp.float32
    n_parts = 1 + SQUARES + 2 * many
    n_jobs = n_parts + 2
    dma, vmem = pltpu.SemaphoreType.DMA, pltpu.VMEM
    anywhere, near = pl.BlockSpec(memory_space=pl.ANY), pl.BlockSpec(memory_space=pltpu.VMEM)

    far_ins = dict(memory=memory, squares=squares, expand=expand, contract=contract)
    in_specs = {
        name: jax.tree.map(lambda _: anywhere if name in far_ins else near, value)
        for name, value in ins.items()
    }

    def out(shape, dtype=high):
        return jax.ShapeDtypeStruct(shape, dtype)

    outs = dict(
        result=out(tokens.shape),
        input_grad=out(tokens.shape),
        memory_grad=out(memory.shape),
        grads=[out(item.shape) for item in squares],
        expand_grad=out(expand.shape),
        contract_grad=out(contract.shape),
        gains_grad=out((3, shard)),
        shifts_grad=out((3, shard)),
    )
    far_outs = dict(
        full=[out((width, width), low)] * SQUARES,
        expand_full=out((width, ff), low),
        contract_full=out((ff, width), low),
    )
    out_specs = jax.tree.map(lambda _: near, outs)
    out_specs.update(jax.tree.map(lambda _: anywhere, far_outs))
    outs.update(far_outs)

    def token_rows(dtype):
        return vmem((tokens_here, width), dtype)

    def memory_rows(dtype):
        return vmem((mem_tokens, width), dtype)

    tiny = (8, 128)

    def unit(stage, far_at):
        count = 1 << (digits - stage - (stage < far_at))
        return (count, n_mem * shard if stage < far_at else shard, width)

    sums, arrived = {}, {}
    for far_at, ring in ((digits, RING), (digits - 1, 2)):
        sums[far_at], arrived[far_at] = {}, {}
        for stage in range(digits + 1):
            if stage == 0 and far_at > 0:
                continue
            others = (n_mem - 1,) if stage == far_at else ()
            arrived[far_at][stage] = vmem((ring,) + others + unit(stage, far_at), low)
            if stage < digits:
                sums[far_at][stage] = vmem((SUM_SLOTS,) + unit(stage, far_at), low)
    whole = (half, n_mem * shard, width)
    counts = [1 << (digits - 1 - stage) for stage in range(digits)]
    buffers = dict(
        out=vmem((OUT_SLOTS,) + whole, low),
        lanes=vmem((LANE_SLOTS,) + whole, low),
        core_in=vmem((CORE_RING,) + whole, low),
        first_sums=vmem((SUM_SLOTS,) + unit(0, digits), low),
        first_arrived=vmem((FIRST_RING,) + unit(0, digits), low),
        sums=sums,
        arrived=arrived,
        small_lanes=vmem((half,) + tiny, high),
        small_core_in=vmem((half,) + tiny, high),
        small_sums=[vmem((count,) + tiny, high) for count in counts],
        small_arrived=[vmem((count,) + tiny, high) for count in counts]
        + [vmem((n_mem - 1, 1) + tiny, high)],
    )
    left = vmem((2, width // 2, tokens_here), low)
    scratch = dict(
        small=vmem(tiny, high),
        small_full=vmem((n_rows * n_mem * 8, 128), high),
        small_total=vmem(tiny, high),
        slots=vmem((SLOTS, width, width), low),
        slot_sem=dma((SLOTS,)),
        mem_sem=dma((6,)),
        gather_sems=[
            dma(shape + (n_parts,))
            for shape in ((), (), (), (digits,), (digits,), (), ())
            + ((2 * (n_mem - 1),), (2 * (n_mem - 1),))
        ],
        reduce_sems=[dma(shape + (n_jobs,)) for shape in ((), (), (digits + 1,), (digits + 1,))],
        gains=vmem((8, width), high),
        query=token_rows(low),
        keys=token_rows(low),
        values=token_rows(low),
        attended=token_rows(low),
        first_low=token_rows(low),
        second_low=token_rows(low),
        cross_query=token_rows(low),
        crossed=token_rows(low),
        cross_keys=memory_rows(low),
        cross_values=memory_rows(low),
        mem_rows=memory_rows(low),
        mem_out=memory_rows(low),
        mem_in=vmem(memory.shape, low),
        unit1=token_rows(high),
        unit2=token_rows(high),
        accumulated=token_rows(high),
        other=token_rows(high),
        scale1=vmem((tokens_here, 1), high),
        scale2=vmem((tokens_here, 1), high),
        self_bias=vmem((tokens_here, tokens_here), high),
        cross_bias=vmem((mem_tokens, tokens_here), high),
        self_lse=vmem((pairs, 2, tokens_here), high),
        cross_lse=vmem((pairs, 2, tokens_here), high),
        eye=vmem((TILE, TILE), low),
        hidden=vmem((tokens_here, ff), low),
        slope=vmem((tokens_here, ff), low),
        hidden_turned=vmem((many, 2, width // 2, tokens_here), low),
        turned=dict(
            tokens=left, attended=left, first=left, memory=left, crossed=left, second=left
        ),
        low=dict(
            third=token_rows(low),
            second=token_rows(low),
            first=token_rows(low),
            branch=token_rows(low),
            cross_query=token_rows(low),
            cross_key=memory_rows(low),
            cross_value=memory_rows(low),
            query=token_rows(low),
            key=token_rows(low),
            value=token_rows(low),
        ),
        small_sums=vmem((2, half) + tiny, high),
        buffers=buffers,
    )
    in_values, in_tree = jax.tree.flatten(ins)
    out_shapes, out_tree = jax.tree.flatten(outs)
    scratch_shapes, scratch_tree = jax.tree.flatten(scratch)
    places = jax.tree.unflatten(in_tree, range(len(in_values)))
    at = len(in_values)
    places.update(jax.tree.unflatten(out_tree, range(at, at + len(out_shapes))))
    at += len(out_shapes)
    places.update(jax.tree.unflatten(scratch_tree, range(at, at + len(scratch_shapes))))
    values = pl.pallas_call(
        functools.partial(layer_kernel, places, (n_rows, n_mem, width, ff, shard)),
        out_shape=out_shapes,
        in_specs=jax.tree.leaves(in_specs),
        out_specs=jax.tree.leaves(out_specs),
        scratch_shapes=scratch_shapes,
        compiler_params=pltpu.CompilerParams(
            collective_id=0, has_side_effects=True, vmem_limit_bytes=VMEM_LIMIT
        ),
        name="layer",
    )(*in_values)
    found = jax.tree.unflatten(out_tree, values)
    for name in far_outs:
        del found[name]
    return found


def local(n_rows, n_mem, *args):
    (
        tokens,
        memory,
        token_ids,
        memory_ids,
        out_grad,
        self_query,
        self_key,
        self_value,
        self_output,
        cross_query,
        cross_key,
        cross_value,
        cross_output,
        expand_weight,
        contract_weight,
        norm_gains,
        norm_shifts,
    ) = args
    shard, width = self_query.shape
    suits = width == 128 * n_rows and shard % 16 == 0 and tokens.shape[0] == 1
    if not suits or n_rows < 4 or n_rows & (n_rows - 1) or n_mem < 2:
        return plain(*args)
    found = fused(
        n_rows,
        n_mem,
        dict(
            tokens=tokens[0],
            memory=memory,
            token_ids=token_ids,
            memory_ids=memory_ids,
            out_grad=out_grad[0],
            squares=[
                self_query,
                self_key,
                self_value,
                self_output,
                cross_query,
                cross_key,
                cross_value,
                cross_output,
            ],
            expand=expand_weight,
            contract=contract_weight,
            norm_gains=norm_gains,
            norm_shifts=norm_shifts,
        ),
    )
    values, tree = jax.tree.flatten(found)
    found = SimpleNamespace(**jax.tree.unflatten(tree, copied(values)))
    return (
        found.result[None],
        found.input_grad[None],
        found.memory_grad,
        *found.grads,
        found.expand_grad,
        found.contract_grad,
        found.gains_grad,
        found.shifts_grad,
    )


def solution(mesh):
    in_specs = (
        P(("rows", "mem"), None, None),
        P("rows", "mem", None),
        P("rows", None),
        P("rows", None),
        P(("rows", "mem"), None, None),
        P(("rows", "mem"), None),
        P(("rows", "mem"), None),
        P(("rows", "mem"), None),
        P(("rows", "mem"), None),
        P(("rows", "mem"), None),
        P(("rows", "mem"), None),
        P(("rows", "mem"), None),
        P(("rows", "mem"), None),
        P(("rows", "mem"), None),
        P(("rows", "mem"), None),
        P(None, ("rows", "mem")),
        P(None, ("rows", "mem")),
    )
    out_specs = (
        P(("rows", "mem"), None, None),
        P(("rows", "mem"), None, None),
        P("rows", "mem", None),
        P(("rows", "mem"), None),
        P(("rows", "mem"), None),
        P(("rows", "mem"), None),
        P(("rows", "mem"), None),
        P(("rows", "mem"), None),
        P(("rows", "mem"), None),
        P(("rows", "mem"), None),
        P(("rows", "mem"), None),
        P(("rows", "mem"), None),
        P(("rows", "mem"), None),
        P(None, ("rows", "mem")),
        P(None, ("rows", "mem")),
    )
    layer = functools.partial(local, mesh.shape["rows"], mesh.shape["mem"])
    return jax.shard_map(layer, mesh=mesh, in_specs=in_specs, out_specs=out_specs, check_vma=False)
```

```python
import functools
import math
from types import SimpleNamespace

import jax
import jax.numpy as jnp
from jax import lax
from jax.experimental import pallas as pl
from jax.experimental.pallas import tpu as pltpu
from jax.sharding import PartitionSpec as P

MESH = pl.DeviceIdType.MESH

HEADS = 16
HEAD_DIM = 64


ALPHA = 4.16
EPS = 1e-05
SCALE = 0.125
NEG = -1e30


def layer_norm(hidden_activation, gain, shift):
    centre = hidden_activation - jnp.mean(hidden_activation, axis=-1, keepdims=True)
    spread = jnp.mean(centre * centre, axis=-1, keepdims=True)
    return centre * lax.rsqrt(spread + EPS) * gain + shift


def gelu_exact(value):
    return jax.nn.gelu(value, approximate=False)


def product(left, right):
    return jnp.dot(left, right, preferred_element_type=jnp.float32)


def split_heads(matrix):
    return matrix.reshape(matrix.shape[0], matrix.shape[1] // HEAD_DIM, HEAD_DIM)


def grouped(matrix):
    return jnp.moveaxis(matrix.reshape(matrix.shape[0], HEADS // 4, 4 * HEAD_DIM), 1, 0)


def ungrouped(stack):
    return jnp.moveaxis(stack, 0, 1).reshape(stack.shape[1], stack.shape[0] * stack.shape[2])


def row_map(function, items):
    return lax.map(lambda entry: function(*entry), items)


def score_block(query, keys, allowed):
    raw = jnp.einsum(
        "khe,qhe->hkq", split_heads(keys), split_heads(query), preferred_element_type=jnp.float32
    )
    return jnp.where(allowed[None], raw * SCALE, NEG)


def attend_probs(query, keys, allowed, lse):
    scores = score_block(query, keys, allowed)
    return jnp.where(allowed[None], jnp.exp(scores - lse[:, None, :]), 0.0)


def attend_forward(query, keys, values, allowed):
    scores = score_block(query, keys, allowed)
    top = jnp.max(scores, axis=1)
    weight = jnp.where(allowed[None], jnp.exp(scores - top[:, None, :]), 0.0)
    total = jnp.sum(weight, axis=1)
    probs = (weight / total[:, None, :]).astype(jnp.bfloat16)
    mixed = jnp.einsum(
        "hkq,khe->qhe", probs, split_heads(values), preferred_element_type=jnp.float32
    )
    return (mixed.reshape(query.shape), top + jnp.log(total))


def value_pull(grad, values):
    return jnp.einsum(
        "qhe,khe->hkq", split_heads(grad), split_heads(values), preferred_element_type=jnp.float32
    )


def score_grads(probs, pulled, inner):
    return (probs * (pulled - inner[:, None, :]) * SCALE).astype(jnp.bfloat16)


def query_from(score_grad, keys, shape):
    moved = jnp.einsum(
        "hkq,khe->qhe", score_grad, split_heads(keys), preferred_element_type=jnp.float32
    )
    return moved.reshape(shape)


def key_from(score_grad, query, shape):
    moved = jnp.einsum(
        "hkq,qhe->khe", score_grad, split_heads(query), preferred_element_type=jnp.float32
    )
    return moved.reshape(shape)


def value_from(probs, grad, values):
    moved = jnp.einsum(
        "hkq,qhe->khe",
        probs.astype(jnp.bfloat16),
        split_heads(grad),
        preferred_element_type=jnp.float32,
    )
    return moved.reshape(values.shape)


def local_forward(query, keys, values, allowed):

    def one_group(items):
        return attend_forward(items[0], items[1], items[2], allowed)

    mixed, lse = lax.map(one_group, (grouped(query), grouped(keys), grouped(values)))
    return (ungrouped(mixed), lse)


def local_backward(query, keys, values, allowed, lse, grad):

    def one_group(items):
        part_query, part_keys, part_values, part_lse, part_grad = items
        probs = attend_probs(part_query, part_keys, allowed, part_lse)
        pulled = value_pull(part_grad, part_values)
        inner = jnp.sum(probs * pulled, axis=1)
        score_grad = score_grads(probs, pulled, inner)
        return (
            query_from(score_grad, part_keys, part_query.shape),
            key_from(score_grad, part_query, part_keys.shape),
            value_from(probs, part_grad, part_values),
        )

    parts = lax.map(one_group, (grouped(query), grouped(keys), grouped(values), lse, grouped(grad)))
    return (ungrouped(parts[0]), ungrouped(parts[1]), ungrouped(parts[2]))


def plain(
    tokens,
    memory,
    token_ids,
    memory_ids,
    out_grad,
    self_query,
    self_key,
    self_value,
    self_output,
    cross_query,
    cross_key,
    cross_value,
    cross_output,
    expand_weight,
    contract_weight,
    norm_gains,
    norm_shifts,
):
    full = (
        lax.all_gather(self_query, ("rows", "mem"), axis=0, tiled=True),
        lax.all_gather(self_key, ("rows", "mem"), axis=0, tiled=True),
        lax.all_gather(self_value, ("rows", "mem"), axis=0, tiled=True),
        lax.all_gather(self_output, ("rows", "mem"), axis=0, tiled=True),
        lax.all_gather(cross_query, ("rows", "mem"), axis=0, tiled=True),
        lax.all_gather(cross_key, ("rows", "mem"), axis=0, tiled=True),
        lax.all_gather(cross_value, ("rows", "mem"), axis=0, tiled=True),
        lax.all_gather(cross_output, ("rows", "mem"), axis=0, tiled=True),
        lax.all_gather(expand_weight, ("rows", "mem"), axis=0, tiled=True),
        lax.all_gather(contract_weight, ("rows", "mem"), axis=0, tiled=True),
        lax.all_gather(jnp.transpose(norm_gains), ("rows", "mem"), axis=0, tiled=True),
        lax.all_gather(jnp.transpose(norm_shifts), ("rows", "mem"), axis=0, tiled=True),
    )
    (
        self_attention_query,
        decoder_match_label,
        self_attention_value,
        self_attention_output,
        encoder_lookup_probe,
        key_cross,
        value_cross,
        cross_attention_output,
        up_projection,
        narrowing_matrix,
        gain_cols,
        shift_cols,
    ) = full
    gain_rows = jnp.transpose(gain_cols).astype(jnp.float32)
    shift_rows = jnp.transpose(shift_cols).astype(jnp.float32)
    rows_here = tokens.shape[0]
    member = lax.axis_index("mem")
    own_ids = lax.dynamic_slice_in_dim(token_ids, member * rows_here, rows_here, 0)
    positions = jnp.arange(tokens.shape[1], dtype=jnp.int32)
    self_allowed = (own_ids[:, :, None] == own_ids[:, None, :]) & (
        positions[:, None] <= positions[None, :]
    )[None]
    query = product(tokens, self_attention_query).astype(jnp.bfloat16)
    keys = product(tokens, decoder_match_label).astype(jnp.bfloat16)
    values = product(tokens, self_attention_value).astype(jnp.bfloat16)
    self_mixed, self_lse = row_map(local_forward, (query, keys, values, self_allowed))
    attention_result = self_mixed.astype(jnp.bfloat16)
    first, first_back = jax.vjp(
        layer_norm,
        ALPHA * tokens.astype(jnp.float32) + product(attention_result, self_attention_output),
        gain_rows[0],
        shift_rows[0],
    )
    first_reduced = first.astype(jnp.bfloat16)
    cross_queries = product(first_reduced, encoder_lookup_probe).astype(jnp.bfloat16)
    memory_rows = lax.all_to_all(memory, "mem", split_axis=0, concat_axis=1, tiled=True)
    row_ids = lax.dynamic_slice_in_dim(memory_ids, member * rows_here, rows_here, 0)
    cross_allowed = row_ids[:, :, None] == own_ids[:, None, :]
    cross_keys = product(memory_rows, key_cross).astype(jnp.bfloat16)
    cross_values = product(memory_rows, value_cross).astype(jnp.bfloat16)
    cross_mixed, cross_lse = row_map(
        local_forward, (cross_queries, cross_keys, cross_values, cross_allowed)
    )
    cross_attention_result = cross_mixed.astype(jnp.bfloat16)
    second, second_back = jax.vjp(
        layer_norm,
        ALPHA * first + product(cross_attention_result, cross_attention_output),
        gain_rows[1],
        shift_rows[1],
    )
    second_reduced = second.astype(jnp.bfloat16)
    hidden_value, gelu_back = jax.vjp(gelu_exact, product(second_reduced, up_projection))
    hidden_activation = hidden_value.astype(jnp.bfloat16)
    result, third_back = jax.vjp(
        layer_norm,
        ALPHA * second + product(hidden_activation, narrowing_matrix),
        gain_rows[2],
        shift_rows[2],
    )
    third_grad, gain_three, shift_three = third_back(out_grad.astype(jnp.float32))
    feedforward_gradient = third_grad.astype(jnp.bfloat16)
    down_projection_gradient = jnp.einsum(
        "ehj,ehc->jc", hidden_activation, feedforward_gradient, preferred_element_type=jnp.float32
    )
    (inner_grad,) = gelu_back(
        jnp.einsum(
            "hpu,ku->hpk",
            feedforward_gradient,
            narrowing_matrix,
            preferred_element_type=jnp.float32,
        )
    )
    inner_reduced = inner_grad.astype(jnp.bfloat16)
    expand_grad = jnp.einsum(
        "iqg,iqe->ge", second_reduced, inner_reduced, preferred_element_type=jnp.float32
    )
    second_total = ALPHA * third_grad + jnp.einsum(
        "iwm,fm->iwf", inner_reduced, up_projection, preferred_element_type=jnp.float32
    )
    second_grad, gain_two, shift_two = second_back(second_total)
    cross_branch_gradient = second_grad.astype(jnp.bfloat16)
    output_cross_grad = jnp.einsum(
        "nhb,nhc->bc",
        cross_attention_result,
        cross_branch_gradient,
        preferred_element_type=jnp.float32,
    )
    crossed_grad = jnp.einsum(
        "qwp,up->qwu",
        cross_branch_gradient,
        cross_attention_output,
        preferred_element_type=jnp.float32,
    ).astype(jnp.bfloat16)
    query_grads, key_grads, value_grads = row_map(
        local_backward,
        (cross_queries, cross_keys, cross_values, cross_allowed, cross_lse, crossed_grad),
    )
    key_low = key_grads.astype(jnp.bfloat16)
    value_low = value_grads.astype(jnp.bfloat16)
    row_grad = jnp.einsum(
        "sme,de->smd", key_low, key_cross, preferred_element_type=jnp.float32
    ) + jnp.einsum("sme,de->smd", value_low, value_cross, preferred_element_type=jnp.float32)
    key_cross_grad = jnp.einsum(
        "smd,sme->de", memory_rows, key_low, preferred_element_type=jnp.float32
    )
    value_cross_grad = jnp.einsum(
        "smd,sme->de", memory_rows, value_low, preferred_element_type=jnp.float32
    )
    memory_grad = lax.all_to_all(
        row_grad.astype(jnp.bfloat16), "mem", split_axis=1, concat_axis=0, tiled=True
    ).astype(row_grad.dtype)
    probe_lowered_precision = query_grads.astype(jnp.bfloat16)
    query_cross_grad = jnp.einsum(
        "nhb,nhc->bc", first_reduced, probe_lowered_precision, preferred_element_type=jnp.float32
    )
    first_total = ALPHA * second_grad + jnp.einsum(
        "qwp,up->qwu",
        probe_lowered_precision,
        encoder_lookup_probe,
        preferred_element_type=jnp.float32,
    )
    first_grad, gain_one, shift_one = first_back(first_total)
    self_branch_gradient = first_grad.astype(jnp.bfloat16)
    output_self_grad = jnp.einsum(
        "nhb,nhc->bc", attention_result, self_branch_gradient, preferred_element_type=jnp.float32
    )
    attended_grad = jnp.einsum(
        "qwp,up->qwu",
        self_branch_gradient,
        self_attention_output,
        preferred_element_type=jnp.float32,
    ).astype(jnp.bfloat16)
    self_query_reduced, decoder_label_lowered, self_value_reduced = row_map(
        local_backward, (query, keys, values, self_allowed, self_lse, attended_grad)
    )
    self_query_reduced = self_query_reduced.astype(jnp.bfloat16)
    decoder_label_lowered = decoder_label_lowered.astype(jnp.bfloat16)
    self_value_reduced = self_value_reduced.astype(jnp.bfloat16)
    query_self_grad = jnp.einsum(
        "nhb,nhc->bc", tokens, self_query_reduced, preferred_element_type=jnp.float32
    )
    key_self_grad = jnp.einsum(
        "nhb,nhc->bc", tokens, decoder_label_lowered, preferred_element_type=jnp.float32
    )
    value_self_grad = jnp.einsum(
        "nhb,nhc->bc", tokens, self_value_reduced, preferred_element_type=jnp.float32
    )
    input_grad = (
        ALPHA * first_grad
        + jnp.einsum(
            "qwp,up->qwu",
            self_query_reduced,
            self_attention_query,
            preferred_element_type=jnp.float32,
        )
        + jnp.einsum(
            "qwp,up->qwu",
            decoder_label_lowered,
            decoder_match_label,
            preferred_element_type=jnp.float32,
        )
        + jnp.einsum(
            "qwp,up->qwu",
            self_value_reduced,
            self_attention_value,
            preferred_element_type=jnp.float32,
        )
    )
    gain_grad = jnp.stack([gain_one, gain_two, gain_three], axis=1)
    shift_grad = jnp.stack([shift_one, shift_two, shift_three], axis=1)
    sums = (
        lax.psum_scatter(query_self_grad, ("rows", "mem"), scatter_dimension=0, tiled=True),
        lax.psum_scatter(key_self_grad, ("rows", "mem"), scatter_dimension=0, tiled=True),
        lax.psum_scatter(value_self_grad, ("rows", "mem"), scatter_dimension=0, tiled=True),
        lax.psum_scatter(output_self_grad, ("rows", "mem"), scatter_dimension=0, tiled=True),
        lax.psum_scatter(query_cross_grad, ("rows", "mem"), scatter_dimension=0, tiled=True),
        lax.psum_scatter(key_cross_grad, ("rows", "mem"), scatter_dimension=0, tiled=True),
        lax.psum_scatter(value_cross_grad, ("rows", "mem"), scatter_dimension=0, tiled=True),
        lax.psum_scatter(output_cross_grad, ("rows", "mem"), scatter_dimension=0, tiled=True),
        lax.psum_scatter(expand_grad, ("rows", "mem"), scatter_dimension=0, tiled=True),
        lax.psum_scatter(
            down_projection_gradient, ("rows", "mem"), scatter_dimension=0, tiled=True
        ),
        lax.psum_scatter(gain_grad, ("rows", "mem"), scatter_dimension=0, tiled=True),
        lax.psum_scatter(shift_grad, ("rows", "mem"), scatter_dimension=0, tiled=True),
    )
    return (
        result,
        input_grad,
        memory_grad,
        sums[0],
        sums[1],
        sums[2],
        sums[3],
        sums[4],
        sums[5],
        sums[6],
        sums[7],
        sums[8],
        sums[9],
        jnp.transpose(sums[10]),
        jnp.transpose(sums[11]),
    )


ALL = slice(None)
TILE = 256
SLOTS = 3
GATHER_SLOTS = 9
VMEM_LIMIT = 61 * 1024 * 1024


def flip(index, unit):
    return index + unit * (1 - 2 * ((index // unit) % 2))


def span(index, size):
    return pl.ds(pl.multiple_of(index * size, size), size)


class Place:
    def __init__(self, n_rows, n_mem):
        self.n_rows, self.n_mem = n_rows, n_mem
        self.digits = (n_rows // 2).bit_length() - 1
        self.row = lax.axis_index("rows")
        self.mem = lax.axis_index("mem")
        self.lane = self.row % 2

    def turn(self, index, stage):
        rising, falling = 2 << stage, 2 << (self.digits - 1 - stage)
        return flip(index, rising) * (1 - self.lane) + flip(index, falling) * self.lane

    def sibling(self):
        return (flip(self.row, 1), self.mem)

    def partner(self, stage):
        return (self.turn(self.row, stage), self.mem)

    def far(self, step):
        return (self.row, (self.mem + step) % self.n_mem)

    def others(self):
        found = [self.far(step) for step in range(1, self.n_mem)]
        found += [self.partner(stage) for stage in range(self.digits)]
        return found + [self.sibling()]

    def tell(self, semaphore):
        for other in self.others():
            pl.semaphore_signal(semaphore, inc=1, device_id=other, device_id_type=MESH)

    def hear(self, semaphore):
        pl.semaphore_wait(semaphore, len(self.others()))

    def greet(self):
        self.tell(pltpu.get_barrier_semaphore())
        self.hear(pltpu.get_barrier_semaphore())


def remote(source, target, send_sem, recv_sem, device):
    return pltpu.make_async_remote_copy(
        src_ref=source,
        dst_ref=target,
        send_sem=send_sem,
        recv_sem=recv_sem,
        device_id=device,
        device_id_type=MESH,
    )


def waits(total):
    return (lambda: total().wait_recv(), lambda: total().wait_send())


class Part:
    def __init__(self, source, target, near=0, straight=False):
        self.source, self.target = source, target
        self.near, self.straight = near, straight


class Gather:
    def __init__(self, place, parts, sems):
        self.place, self.parts = place, parts
        (
            self.own_sem,
            self.far_send,
            self.far_recv,
            self.plane_send,
            self.plane_recv,
            self.core_send,
            self.core_recv,
            self.line_send,
            self.line_recv,
        ) = sems

    def group(self, number, group):
        return self.parts[number].target.at[group]

    def one(self, number, group, member):
        return self.parts[number].target.at[group, member]

    def shard(self, number):
        return self.parts[number].source

    def mine(self, number):
        return self.one(number, self.place.row, self.place.mem)

    def own(self, number):
        return pltpu.make_async_copy(self.shard(number), self.mine(number), self.own_sem.at[number])

    def held(self, stage):
        groups = [self.place.row]
        for before in range(stage):
            groups = groups + [self.place.turn(group, before) for group in groups]
        return groups

    def far_total(self, number):
        part = self.parts[number]
        some = part.target.at[pl.ds(0, 1 << part.near), pl.ds(0, self.place.n_mem - 1)]
        return remote(
            some, some, self.far_send.at[number], self.far_recv.at[number], self.place.far(1)
        )

    def far_hop(self, number, first):
        place = self.place
        for group in self.held(self.parts[number].near):
            target = self.one(number, group, place.mem)
            source = self.shard(number) if first else target
            for step in range(1, place.n_mem):
                remote(
                    source,
                    target,
                    self.far_send.at[number],
                    self.far_recv.at[number],
                    place.far(step),
                ).start()

    def sides(self, step):
        mem, n_mem = self.place.mem, self.place.n_mem
        return (
            ((mem - step >= 0) & (mem + 1 < n_mem), mem - step, 1, mem - 1 - step >= 0),
            ((mem + step < n_mem) & (mem >= 1), mem + step, n_mem - 1, mem + 1 + step < n_mem),
        )

    def line_total(self, number, step, side):
        part, at = self.parts[number], 2 * step + side
        some = part.target.at[pl.ds(0, 1 << part.near), 0]
        sems = (self.line_send.at[at, number], self.line_recv.at[at, number])
        return remote(some, some, *sems, self.place.far(1))

    def line_arrived(self, number, step):
        for side, (_, _, _, receives) in enumerate(self.sides(step)):

            @pl.when(receives)
            def _(side=side):
                self.line_total(number, step, side).wait_recv()

    def line_sent(self, number, step):
        for side, (sends, _, _, _) in enumerate(self.sides(step)):

            @pl.when(sends)
            def _(side=side):
                self.line_total(number, step, side).wait_send()

    def line_hop(self, number, step, first):
        place = self.place
        for side, (sends, member, towards, _) in enumerate(self.sides(step)):
            member = (member + place.n_mem) % place.n_mem

            @pl.when(sends)
            def _(side=side, member=member, towards=towards):
                for group in self.held(self.parts[number].near):
                    target = self.one(number, group, member)
                    remote(
                        self.shard(number) if first else target,
                        target,
                        self.line_send.at[2 * step + side, number],
                        self.line_recv.at[2 * step + side, number],
                        place.far(towards),
                    ).start()

    def plane_total(self, number, stage):
        part = self.parts[number]
        some = part.target.at[pl.ds(0, 1 << stage)]
        if stage < part.near:
            some = part.target.at[pl.ds(0, 1 << stage), 0]
        return remote(
            some,
            some,
            self.plane_send.at[stage, number],
            self.plane_recv.at[stage, number],
            self.place.partner(stage),
        )

    def plane_hop(self, number, stage, first):
        for group in self.held(stage):
            if stage < self.parts[number].near:
                target = self.one(number, group, self.place.mem)
            else:
                target = self.group(number, group)
            remote(
                self.shard(number) if first else target,
                target,
                self.plane_send.at[stage, number],
                self.plane_recv.at[stage, number],
                self.place.partner(stage),
            ).start()

    def core_total(self, number):
        some = self.parts[number].target.at[pl.ds(0, self.place.n_rows // 2)]
        return remote(
            some, some, self.core_send.at[number], self.core_recv.at[number], self.place.sibling()
        )

    def core_hop(self, number, first):
        for group in self.held(self.place.digits):
            block = self.group(number, group)
            remote(
                block,
                block,
                self.core_send.at[number],
                self.core_recv.at[number],
                self.place.sibling(),
            ).start()

    def hops(self, number):
        part, take = self.parts[number], functools.partial
        along = []
        if part.straight:
            along.append((1.6, take(self.far_hop, number)) + waits(take(self.far_total, number)))
        else:
            for step in range(self.place.n_mem - 1):
                along.append(
                    (
                        0.55 if step else 1.4,
                        take(self.line_hop, number, step),
                        take(self.line_arrived, number, step),
                        take(self.line_sent, number, step),
                    )
                )
        plane = []
        for stage in range(self.place.digits):
            total = take(self.plane_total, number, stage)
            plane.append((1.5, take(self.plane_hop, number, stage)) + waits(total))
        core = (1.5, take(self.core_hop, number)) + waits(take(self.core_total, number))
        return plane[: part.near] + along + plane[part.near :] + [core]

    def events(self, number):
        hops = self.hops(number)
        time, found = float(number), []

        def act(at):
            if at == 0:
                self.own(number).start()
            else:
                if at == 1:
                    self.own(number).wait()
                hops[at - 1][2]()
            hops[at][1](at == 0)

        for at in range(len(hops)):
            time += hops[at][0] if at else 0.0
            found.append((time, functools.partial(act, at)))
        return found, time + 0.9

    def sent(self, number):
        for hop in self.hops(number):
            hop[3]()


class Job:
    def __init__(self, left, right, first, target):
        self.left, self.right, self.first, self.target = left, right, first, target
        self.small = right is None
        self.width = target.shape[-1]
        self.large = 0


OUT_SLOTS, LANE_SLOTS, SUM_SLOTS, CORE_RING, FIRST_RING, RING = 2, 3, 2, 2, 6, 4


class Reduce:
    def __init__(self, place, jobs, sems, pool, small):
        self.place, self.jobs, self.small = place, jobs, small
        self.core_send, self.core_recv, self.stage_send, self.stage_recv = sems
        wanted = [place.row]
        for stage in reversed(range(place.digits)):
            wanted = wanted + [place.turn(group, stage) for group in wanted]
        self.wanted = [group // 2 for group in wanted]
        for number, job in enumerate(job for job in jobs if not job.small):
            job.large = number
        used, half = [0], place.n_rows // 2

        def take(count, units):
            first = used[0]
            used[0] += count * units
            return [pool.at[pl.ds(first + i * units, units)] for i in range(count)]

        self.outs = take(OUT_SLOTS, half)
        self.lane_slots = take(LANE_SLOTS, half)
        self.core_ring = take(CORE_RING, half)
        self.sum_slots, self.rings = [], []
        for stage in range(place.digits):
            self.sum_slots.append(take(SUM_SLOTS, self.count(stage)))
            self.rings.append(take(RING if stage else FIRST_RING, self.count(stage)))
        self.rings.append(take(RING, 1))
        self.used = used[0]

    def count(self, stage):
        return max(self.place.n_rows // 4 >> stage, 1)

    def cut(self, ref, job):
        return ref if job.width == ref.shape[-1] else ref.at[:, :, :, pl.ds(0, job.width)]

    def out(self, job):
        return self.cut(self.outs[job.large % OUT_SLOTS], job)

    def lanes(self, job):
        if job.small:
            return self.small.lanes
        return self.cut(self.lane_slots[job.large % LANE_SLOTS], job)

    def core_in(self, job):
        if job.small:
            return self.small.core_in
        return self.cut(self.core_ring[job.large % CORE_RING], job)

    def sums(self, job, stage):
        if job.small:
            return self.small.sums[stage]
        return self.cut(self.sum_slots[stage][job.large % SUM_SLOTS], job)

    def arrived(self, job, stage):
        if job.small:
            return self.small.arrived[stage]
        ring = self.rings[stage]
        units = self.cut(ring[job.large % len(ring)], job)
        if stage == self.place.digits:
            return units.at[0, pl.ds(0, self.place.n_mem - 1)]
        return units

    def previous(self, number, distance):
        found = [n for n in range(number) if not self.jobs[n].small]
        if self.jobs[number].small or len(found) < distance:
            return None
        return found[-distance]

    def core_copy(self, number):
        job = self.jobs[number]
        source = job.left.at[1 - self.place.lane] if job.small else self.out(job)
        return remote(
            source,
            self.core_in(job),
            self.core_send.at[number],
            self.core_recv.at[number],
            self.place.sibling(),
        )

    def product(self, job, side, store):
        half = self.place.n_rows // 2
        group = job.left.shape[1] // half
        width = min(TILE, job.width)
        unit = (self.place.n_mem, group // self.place.n_mem, width)

        def column_step(step, carry):
            source = pl.ds(pl.multiple_of(job.first + step * width, width), width)
            value = dot(job.left[side], job.right[:, source])
            for index in range(half):
                block = value[index * group : (index + 1) * group].reshape(unit)
                store(index, span(step, width), block)
            return carry

        lax.fori_loop(0, job.width // width, column_step, 0)

    def core_stage(self, number):
        job = self.jobs[number]
        if not job.small:
            before = self.previous(number, OUT_SLOTS)
            if before is not None:
                self.core_copy(before).wait_send()
            out = self.out(job)

            def store(index, columns, value):
                out[index, :, :, columns] = value.astype(out.dtype)

            self.product(job, 1 - self.place.lane, store)
        self.core_copy(number).start()

    def lane_stage(self, number):
        job = self.jobs[number]
        before = self.previous(number, LANE_SLOTS)
        if before is not None:
            self.total(before, 0).wait_send()
        lanes, arrived = self.lanes(job), self.core_in(job)
        self.core_copy(number).wait_recv()
        if job.small:
            lanes[...] = job.left[self.place.lane] + arrived[...]
        else:

            def store(index, columns, value):
                total = value + arrived[index, :, :, columns].astype(jnp.float32)
                lanes[index, :, :, columns] = total.astype(lanes.dtype)

            self.product(job, self.place.lane, store)
        self.send(number, 0)

    def unit(self, job, stage, index):
        if stage == 0:
            return self.lanes(job).at[self.wanted[index]]
        return self.sums(job, stage - 1).at[index]

    def piece(self, job, unit, member):
        return unit if job.small else unit.at[member]

    def send(self, number, stage):
        job, place = self.jobs[number], self.place
        arrived = self.arrived(job, stage)
        sems = (self.stage_send.at[stage, number], self.stage_recv.at[stage, number])
        if stage == place.digits:
            unit = self.unit(job, stage, 0)
            for step in range(1, place.n_mem):
                source = self.piece(job, unit, (place.mem + step) % place.n_mem)
                remote(source, arrived.at[step - 1], *sems, place.far(step)).start()
            return
        left = self.count(stage)
        for index in range(left):
            source = self.unit(job, stage, left + index)
            remote(source, arrived.at[index], *sems, place.partner(stage)).start()

    def total(self, number, stage):
        some = self.arrived(self.jobs[number], stage)
        sems = (self.stage_send.at[stage, number], self.stage_recv.at[stage, number])
        return remote(some, some, *sems, self.place.far(1))

    def stage(self, number, stage):
        job, place = self.jobs[number], self.place
        arrived = self.arrived(job, stage)
        if stage == place.digits:
            self.total(number, stage).wait_recv()
            value = self.piece(job, self.unit(job, stage, 0), place.mem)[...].astype(jnp.float32)
            for step in range(place.n_mem - 1):
                value = value + arrived[step].astype(jnp.float32)
            job.target[...] = value
            return
        before = self.previous(number, SUM_SLOTS)
        if before is not None:
            self.total(before, stage + 1).wait_send()
        self.total(number, stage).wait_recv()
        sums = self.sums(job, stage)
        for index in range(self.count(stage)):
            unit, coming, target = self.unit(job, stage, index), arrived.at[index], sums.at[index]
            if job.small:
                target[...] = unit[...] + coming[...]
                continue

            def add(member, carry, unit=unit, coming=coming, target=target):
                value = unit[member].astype(jnp.float32) + coming[member].astype(jnp.float32)
                target[member] = value.astype(target.dtype)
                return carry

            lax.fori_loop(0, place.n_mem, add, 0)
        self.send(number, stage + 1)

    def events(self, number):
        found = [(0.0, functools.partial(self.core_stage, number))]
        found.append((0.9, functools.partial(self.lane_stage, number)))
        time = 2.2 if number < 2 else 3.2
        for stage in range(self.place.digits + 1):
            found.append((time, functools.partial(self.stage, number, stage)))
            time += 1.4
        found[-1] = (found[-1][0] - 0.3, found[-1][1])
        return [(number + time, action) for time, action in found]

    def finish(self):
        n_jobs, last = len(self.jobs), self.place.digits
        out = {self.previous(number, OUT_SLOTS) for number in range(n_jobs)}
        lanes = {self.previous(number, LANE_SLOTS) for number in range(n_jobs)}
        sums = {self.previous(number, SUM_SLOTS) for number in range(n_jobs)}
        for number in range(n_jobs):
            if number not in out:
                self.core_copy(number).wait_send()
            if number not in lanes:
                self.total(number, 0).wait_send()
            if number not in sums:
                for stage in range(1, last + 1):
                    self.total(number, stage).wait_send()


NORMAL = (((1,), (0,)), ((), ()))
TURNED = (((1,), (1,)), ((), ()))
LEFT_TURNED = (((0,), (0,)), ((), ()))


def dot(left, right, dims=NORMAL):
    return lax.dot_general(left, right, dims, preferred_element_type=jnp.float32)


def times(left, weight, store):
    size = weight.shape[-1]
    width = min(TILE, size)

    def column_step(step, carry):
        columns = span(step, width)
        store(columns, dot(left[...], weight[:, :, :, columns].reshape(-1, width)))
        return carry

    lax.fori_loop(0, size // width, column_step, 0)


def times_turned(left, weight, store):
    unit = weight.shape[1] * weight.shape[2]
    units = max(TILE // unit, 1)

    def row_step(step, carry):
        rows = weight[span(step, units)].reshape(units * unit, weight.shape[-1])
        store(span(step, units * unit), dot(left[...], rows, TURNED))
        return carry

    lax.fori_loop(0, weight.shape[0] // units, row_step, 0)


def into(target):
    def store(columns, value):
        target[:, columns] = value.astype(target.dtype)

    return store


ROWS = 32


def by_rows(count, step):
    def body(index, carry):
        step(span(index, ROWS))
        return carry

    lax.fori_loop(0, count // ROWS, body, 0)


def norm_forward(total, gains, index, unit, scale, use):
    gain, shift = gains[index : index + 1, :], gains[index + 3 : index + 4, :]

    def step(rows):
        value = total[rows, :]
        centre = value - jnp.mean(value, axis=-1, keepdims=True)
        spread = jnp.mean(centre * centre, axis=-1, keepdims=True)
        root = lax.rsqrt(spread + EPS)
        scaled = centre * root
        unit[rows, :] = scaled
        scale[rows, :] = root
        use(rows, scaled * gain + shift)

    by_rows(total.shape[0], step)


def norm_slope(incoming, scaled, root, gain):
    width = scaled.shape[1]
    scaled_grad = incoming * gain
    first = jnp.mean(scaled_grad, axis=-1, keepdims=True)
    second = jnp.mean(scaled_grad * scaled, axis=-1, keepdims=True)
    value = root * (scaled_grad - first - scaled * second)
    of_gain = jnp.sum((incoming * scaled).reshape(ROWS // 8, 8, width), axis=0)
    of_shift = jnp.sum(incoming.reshape(ROWS // 8, 8, width), axis=0)
    return value, of_gain, of_shift


def keep_small(index, sums, small):
    for offset, partial in ((index, sums[0]), (index + 3, sums[1])):
        line = jnp.sum(partial, axis=0, keepdims=True)
        for group in range(2 * small.shape[1]):
            small[group % 2, group // 2, offset : offset + 1, :] = line[
                :, group * 128 : (group + 1) * 128
            ]


def norm_backward(grad, gains, index, unit, scale, target, target_low, small):
    gain = gains[index : index + 1, :]

    def body(block, sums):
        rows = span(block, ROWS)
        value, of_gain, of_shift = norm_slope(grad[rows, :], unit[rows, :], scale[rows, :], gain)
        target[rows, :] = value
        target_low[rows, :] = value.astype(target_low.dtype)
        return (sums[0] + of_gain, sums[1] + of_shift)

    zero = jnp.zeros((8, unit.shape[1]), jnp.float32)
    keep_small(index, lax.fori_loop(0, unit.shape[0] // ROWS, body, (zero, zero)), small)


def norm_both(total, grad, gains, index, result, target, target_low, small):
    gain, shift = gains[index : index + 1, :], gains[index + 3 : index + 4, :]

    def body(block, sums):
        rows = span(block, ROWS)
        value = total[rows, :]
        centre = value - jnp.mean(value, axis=-1, keepdims=True)
        spread = jnp.mean(centre * centre, axis=-1, keepdims=True)
        root = lax.rsqrt(spread + EPS)
        scaled = centre * root
        result[rows, :] = scaled * gain + shift
        incoming = grad[rows, :].astype(jnp.float32)
        value, of_gain, of_shift = norm_slope(incoming, scaled, root, gain)
        target[rows, :] = value
        target_low[rows, :] = value.astype(target_low.dtype)
        return (sums[0] + of_gain, sums[1] + of_shift)

    zero = jnp.zeros((8, total.shape[1]), jnp.float32)
    keep_small(index, lax.fori_loop(0, total.shape[0] // ROWS, body, (zero, zero)), small)


def lane_masks(dtype):
    low = lax.broadcasted_iota(jnp.int32, (1, 2 * HEAD_DIM), 1) < HEAD_DIM
    first = jnp.where(low, 1.0, 0.0)
    return first.astype(dtype), (1.0 - first).astype(dtype)


def attention_forward(query, keys, values, bias, mixed, lse):
    masks = lane_masks(query.dtype)
    keep = lane_masks(jnp.float32)

    def pair_step(pair, carry):
        lanes = span(pair, 2 * HEAD_DIM)
        two_query, two_keys, two_values = query[:, lanes], keys[:, lanes], values[:, lanes]
        total = None
        for head in range(2):
            scores = dot(two_keys, two_query * masks[head], TURNED) * SCALE + bias[...]
            top = jnp.max(scores, axis=0, keepdims=True)
            weight = jnp.exp(scores - top)
            norm = jnp.sum(weight, axis=0, keepdims=True)
            probs = (weight * (1.0 / norm)).astype(query.dtype)
            part = dot(probs, two_values, LEFT_TURNED) * keep[head]
            total = part if total is None else total + part
            lse[pair, head : head + 1, :] = top + jnp.log(norm)
        mixed[:, lanes] = total.astype(mixed.dtype)
        return carry

    lax.fori_loop(0, lse.shape[0], pair_step, 0)


def attention_backward(
    query, keys, values, bias, lse, grad, query_grad, key_grad, value_grad, first, last
):
    masks = lane_masks(query.dtype)
    keep = lane_masks(jnp.float32)

    def pair_step(pair, carry):
        lanes = span(pair, 2 * HEAD_DIM)
        two_query, two_keys, two_values = query[:, lanes], keys[:, lanes], values[:, lanes]
        two_grad = grad[:, lanes]
        sums = [None, None, None]
        for head in range(2):
            scores = dot(two_keys, two_query * masks[head], TURNED) * SCALE + bias[...]
            probs = jnp.exp(scores - lse[pair, head : head + 1, :])
            pulled = dot(two_values, two_grad * masks[head], TURNED)
            inner = jnp.sum(probs * pulled, axis=0, keepdims=True)
            slope = (probs * (pulled - inner) * SCALE).astype(query.dtype)
            parts = (
                dot(slope, two_keys, LEFT_TURNED),
                dot(slope, two_query),
                dot(probs.astype(query.dtype), two_grad),
            )
            for index, part in enumerate(parts):
                part = part * keep[head]
                sums[index] = part if sums[index] is None else sums[index] + part
        query_grad[:, lanes] = sums[0].astype(query_grad.dtype)
        key_grad[:, lanes] = sums[1].astype(key_grad.dtype)
        value_grad[:, lanes] = sums[2].astype(value_grad.dtype)
        return carry

    lax.fori_loop(first, last, pair_step, 0)


def turn_blocks(left, eye, store):
    width = eye.shape[0]
    for block in range(left.shape[1] // width):
        columns = pl.ds(block * width, width)
        store(block, dot(eye[...], left[:, columns], TURNED).astype(left.dtype))


def turn_by_lane(left, eye, target):
    group = eye.shape[0] // 2

    def store(block, value):
        target[0, pl.ds(block * group, group), :] = value[:group]
        target[1, pl.ds(block * group, group), :] = value[group:]

    turn_blocks(left, eye, store)


SQUARES = 8


def layer_kernel(places, sizes, *refs):
    n_rows, n_mem, width, ff, shard = sizes
    ref = SimpleNamespace(**jax.tree.map(lambda place: refs[place], places))
    place = Place(n_rows, n_mem)
    many = ff // width
    own_ff = ff // (n_rows * n_mem)
    (
        at_query,
        at_key,
        at_value,
        at_output,
        at_cross_query,
        at_cross_key,
        at_cross_value,
        at_cross_output,
    ) = range(SQUARES)
    full = ref.full
    expand, contract = ref.expand_full, ref.contract_full
    tokens, gains = ref.tokens, ref.gains
    low, turned = SimpleNamespace(**ref.low), SimpleNamespace(**ref.turned)

    order = [
        at_query,
        at_key,
        at_value,
        at_output,
        at_cross_key,
        at_cross_value,
        at_cross_query,
        at_cross_output,
    ]
    pool = ref.pool

    def gather_slot(number):
        return pool.at[pl.ds(number % GATHER_SLOTS * n_rows, n_rows)]

    sources = [ref.squares[index] for index in order]
    sources += [ref.expand.at[:, pl.ds(j * width, width)] for j in range(many)]
    sources += [ref.contract.at[pl.ds(j * shard, shard), :] for j in range(many)]
    stores = [full[index] for index in order] + [expand.at[j] for j in range(many)]
    stores += [contract.at[:, j] for j in range(many)]
    parts = [Part(item, gather_slot(n), n % 2) for n, item in enumerate(sources)]
    parts.insert(SMALL_AT, Part(ref.small, ref.small_full, 0, True))
    gather = Gather(place, parts, ref.gather_sems)

    def keep(number):
        source = gather_slot(number)
        if number >= SQUARES + many:
            source = source.reshape(n_rows * n_mem, shard, width)
        return pltpu.make_async_copy(source, stores[number], ref.keep_sem.at[number])

    count = [0]

    def load_slot(number):
        first = pool.shape[0] - (1 + number % SLOTS) * n_rows
        return pool.at[pl.ds(first, n_rows)]

    def load(source):
        number = count[0]
        count[0] += 1
        slot = load_slot(number)
        pltpu.make_async_copy(source, slot, ref.slot_sem.at[number % SLOTS]).start()
        return number

    def ready(number):
        slot = load_slot(number)
        pltpu.make_async_copy(slot, slot, ref.slot_sem.at[number % SLOTS]).wait()
        return slot

    def contract_rows(j):
        devices = n_rows * n_mem // many
        return contract.at[pl.ds(j * devices, devices)]

    mem_block = ref.memory.shape[1]
    memory, mem_rows = ref.memory, ref.mem_rows

    def memory_own():
        return pltpu.make_async_copy(
            memory.at[place.mem], mem_rows.at[span(place.mem, mem_block)], ref.mem_sem.at[0]
        )

    def memory_total():
        some = mem_rows.at[pl.ds(0, (n_mem - 1) * mem_block)]
        return remote(some, some, ref.mem_sem.at[1], ref.mem_sem.at[2], place.far(1))

    ref.small[...] = jnp.zeros_like(ref.small)
    for member in range(n_mem):

        @pl.when(place.mem == member)
        def _(member=member):
            lanes = slice(member * shard, (member + 1) * shard)
            ref.small[0:3, lanes] = ref.norm_gains[...].astype(jnp.float32)
            ref.small[3:6, lanes] = ref.norm_shifts[...].astype(jnp.float32)

    place.greet()
    actions = []
    whole = []
    for part in range(len(parts)):
        found, time = gather.events(part)
        actions += found
        whole.append(time)
    actions.sort(key=lambda item: item[0])
    start = [action for action in actions if action[0] < 2]
    actions = actions[len(start) :]
    for _, action in start:
        action()
    memory_own().start()
    for step in range(1, n_mem):
        remote(
            memory.at[(place.mem + step) % n_mem],
            mem_rows.at[span(place.mem, mem_block)],
            ref.mem_sem.at[1],
            ref.mem_sem.at[2],
            place.far(step),
        ).start()

    self_bias, cross_bias, eye = ref.self_bias, ref.cross_bias, ref.eye
    own_row = ref.token_ids[pl.ds(place.mem, 1), :].astype(jnp.float32)
    mem_row = ref.memory_ids[pl.ds(place.mem, 1), :].astype(jnp.float32)
    key_place = lax.broadcasted_iota(jnp.int32, self_bias.shape, 0)
    query_place = lax.broadcasted_iota(jnp.int32, self_bias.shape, 1)
    own_wide = jnp.broadcast_to(own_row, self_bias.shape)
    mem_wide = jnp.broadcast_to(mem_row, (cross_bias.shape[1], cross_bias.shape[0]))
    same = (jnp.transpose(own_wide) == own_wide) & (key_place <= query_place)
    self_bias[...] = jnp.where(same, 0.0, NEG)
    cross_bias[...] = jnp.where(jnp.transpose(mem_wide) == own_row, 0.0, NEG)
    eye_row = lax.broadcasted_iota(jnp.int32, eye.shape, 0)
    eye_column = lax.broadcasted_iota(jnp.int32, eye.shape, 1)
    eye[...] = jnp.where(eye_row == eye_column, 1.0, 0.0).astype(eye.dtype)
    turn_by_lane(tokens, eye, turned.tokens)

    accumulated, other = ref.accumulated, ref.other
    hidden, slope, hidden_turned = ref.hidden, ref.slope, ref.hidden_turned

    def small_piece():
        blocks = ref.small_full
        for group in range(n_rows):
            total = None
            for member in range(n_mem):
                value = blocks[group, member]
                total = value if total is None else total + value
            gains[:, group * 128 : (group + 1) * 128] = total

    def query_piece(slot):
        times(tokens, slot, into(ref.query))

    def key_piece(slot):
        times(tokens, slot, into(ref.keys))

    def value_piece(slot):
        times(tokens, slot, into(ref.values))
        attention_forward(
            ref.query, ref.keys, ref.values, self_bias, ref.attended, ref.self_lse
        )

    def output_piece(slot):
        def store(columns, value):
            accumulated[:, columns] = ALPHA * tokens[:, columns].astype(jnp.float32) + value

        times(ref.attended, slot, store)

        def use(rows, value):
            ref.first_low[rows, :] = value.astype(jnp.bfloat16)
            other[rows, :] = value

        norm_forward(accumulated, gains, 0, ref.unit1, ref.scale1, use)
        turn_by_lane(ref.attended, eye, turned.attended)

    def cross_key_piece(slot):
        memory_own().wait()
        memory_total().wait_recv()
        times(mem_rows, slot, into(ref.cross_keys))
        turn_by_lane(mem_rows, eye, turned.memory)

    def cross_value_piece(slot):
        times(mem_rows, slot, into(ref.cross_values))
        turn_by_lane(ref.first_low, eye, turned.first)

    def cross_query_piece(slot):
        times(ref.first_low, slot, into(ref.cross_query))
        attention_forward(
            ref.cross_query,
            ref.cross_keys,
            ref.cross_values,
            cross_bias,
            ref.crossed,
            ref.cross_lse,
        )

    def cross_output_piece(slot):
        def store(columns, value):
            accumulated[:, columns] = ALPHA * other[:, columns] + value

        times(ref.crossed, slot, store)

        def use(rows, value):
            ref.second_low[rows, :] = value.astype(jnp.bfloat16)
            other[rows, :] = value

        norm_forward(accumulated, gains, 1, ref.unit2, ref.scale2, use)
        turn_by_lane(ref.crossed, eye, turned.crossed)

    def expand_piece(j, slot):
        def store(columns, value):
            there = pl.ds(pl.multiple_of(j * width + columns.start, TILE), columns.size)
            bell = 0.5 * (1.0 + lax.erf(value * math.sqrt(0.5)))
            density = jnp.exp(value * value * -0.5) * (1.0 / math.sqrt(2.0 * math.pi))
            hidden[:, there] = (value * bell).astype(hidden.dtype)
            slope[:, there] = (bell + value * density).astype(slope.dtype)

        times(ref.second_low, slot, store)

        def keep(block, value):
            for index in range(value.shape[0] // shard):
                first = j * width + block * value.shape[0] + index * shard
                device, job = first // own_ff, first % own_ff // shard
                group, member = device // n_mem, device % n_mem
                at = group // 2 * n_mem * shard + member * shard
                hidden_turned[job, group % 2, at : at + shard, :] = value[
                    index * shard : (index + 1) * shard
                ]

        turn_blocks(hidden.at[:, pl.ds(j * width, width)], eye, keep)

    def contract_piece(j, slot):
        block = 2 * n_mem * shard
        for index in range(n_rows // 2):
            rows = pl.ds(index * n_mem * shard, n_mem * shard)
            both = jnp.concatenate([hidden_turned[j, 0, rows], hidden_turned[j, 1, rows]], axis=0)
            columns = pl.ds(index * block, block)
            low.branch[:, columns] = dot(eye[...], both, TURNED).astype(jnp.bfloat16)

        def store(columns, value):
            if j == 0:
                accumulated[:, columns] = ALPHA * other[:, columns] + value
            else:
                accumulated[:, columns] = accumulated[:, columns] + value

        times(low.branch, slot, store)

    pieces = [
        query_piece,
        key_piece,
        value_piece,
        output_piece,
        cross_key_piece,
        cross_value_piece,
        cross_query_piece,
        cross_output_piece,
    ]
    pieces += [functools.partial(expand_piece, j) for j in range(many)]
    pieces += [functools.partial(contract_piece, j) for j in range(many)]

    def arrive(part):
        gather.core_total(part).wait_recv()
        if part != SMALL_AT:
            keep(part - (part > SMALL_AT)).start()

    def use(part):
        if part == SMALL_AT:
            small_piece()
        else:
            number = part - (part > SMALL_AT)
            pieces[number](gather_slot(number))

    def settle(part):
        gather.sent(part)
        if part != SMALL_AT:
            keep(part - (part > SMALL_AT)).wait()

    last = 0.0
    for part, time in enumerate(whole):
        time = max(time, last + 0.5)
        actions.append((time, functools.partial(arrive, part)))
        actions.append((time + 0.2, functools.partial(use, part)))
        actions.append((time + 0.45, functools.partial(settle, part)))
        last = time
    actions.sort(key=lambda item: item[0])
    for _, action in actions:
        action()
    place.tell(ref.ready_sem)

    backward_sources, loads = [], []
    used = [0]

    def next_slot():
        slot = ready(loads[used[0]])
        used[0] += 1
        if len(loads) < len(backward_sources):
            loads.append(load(backward_sources[len(loads)]))
        return slot

    small_sums = ref.small_sums
    small_sums[...] = jnp.zeros_like(small_sums)
    def inner_piece(j):
        slot = next_slot()

        def store(columns, value):
            there = pl.ds(pl.multiple_of(j * width + columns.start, TILE), columns.size)
            slope[:, there] = (value * slope[:, there].astype(jnp.float32)).astype(slope.dtype)

        times_turned(low.third, slot, store)

    def second_piece(j):
        slot = next_slot()

        def store(columns, value):
            if j == 0:
                other[:, columns] = ALPHA * accumulated[:, columns] + value
            else:
                other[:, columns] = other[:, columns] + value

        times_turned(slope.at[:, pl.ds(j * width, width)], slot, store)

    def second_norm_piece():
        norm_backward(
            other, gains, 1, ref.unit2, ref.scale2, accumulated, low.second, small_sums
        )

    pairs = width // (2 * HEAD_DIM)

    def cross_start_piece():
        times_turned(low.second, next_slot(), into(low.branch))

    def cross_piece(first, last):
        attention_backward(
            ref.cross_query,
            ref.cross_keys,
            ref.cross_values,
            cross_bias,
            ref.cross_lse,
            low.branch,
            low.cross_query,
            low.cross_key,
            low.cross_value,
            first,
            last,
        )

    def first_piece():
        def store(columns, value):
            other[:, columns] = ALPHA * accumulated[:, columns] + value

        times_turned(low.cross_query, next_slot(), store)
        norm_backward(other, gains, 0, ref.unit1, ref.scale1, accumulated, low.first, small_sums)

    def self_start_piece():
        times_turned(low.first, next_slot(), into(low.branch))

    def self_piece(first, last):
        attention_backward(
            ref.query,
            ref.keys,
            ref.values,
            self_bias,
            ref.self_lse,
            low.branch,
            low.query,
            low.key,
            low.value,
            first,
            last,
        )

    mem_out, mem_in = ref.mem_out, ref.mem_in

    def grad_own():
        return pltpu.make_async_copy(
            mem_out.at[span(place.mem, mem_block)], mem_in.at[place.mem], ref.mem_sem.at[3]
        )

    def grad_total():
        some = mem_in.at[pl.ds(0, n_mem - 1)]
        return remote(some, some, ref.mem_sem.at[4], ref.mem_sem.at[5], place.far(1))

    def memory_key_piece():
        times_turned(low.cross_key, next_slot(), into(other))

    def memory_value_piece():
        def store(columns, value):
            mem_out[:, columns] = (other[:, columns] + value).astype(mem_out.dtype)

        times_turned(low.cross_value, next_slot(), store)
        grad_own().start()
        for step in range(1, n_mem):
            remote(
                mem_out.at[span((place.mem + step) % n_mem, mem_block)],
                mem_in.at[place.mem],
                ref.mem_sem.at[4],
                ref.mem_sem.at[5],
                place.far(step),
            ).start()

    def input_piece(left, start):
        target = ref.input_grad

        def store(columns, value):
            if start:
                target[:, columns] = ALPHA * accumulated[:, columns] + value
            else:
                target[:, columns] = target[:, columns] + value

        times_turned(left, next_slot(), store)

    def memory_end_piece():
        grad_own().wait()
        grad_total().wait_recv()
        for member in range(n_mem):
            ref.memory_grad[member] = mem_in[member].astype(jnp.float32)

    halves = ((0, width // 2), (width // 2, width // 2))
    grads = ref.grads
    plans = []
    for j in range(many):
        for first, columns in halves if j == 0 else ((0, width),):
            target = ref.contract_grad.at[pl.ds(j * shard, shard), pl.ds(first, columns)]
            plans.append((hidden_turned.at[j], low.third, first, target))
    for j in range(many):
        target = ref.expand_grad.at[:, pl.ds(j * width, width)]
        plans.append((turned.second, slope, j * width, target))
    plans += [
        (turned.crossed, low.second, 0, grads[at_cross_output]),
        (turned.memory, low.cross_key, 0, grads[at_cross_key]),
        (turned.memory, low.cross_value, 0, grads[at_cross_value]),
        (turned.first, low.cross_query, 0, grads[at_cross_query]),
        (turned.attended, low.first, 0, grads[at_output]),
        (small_sums, None, 0, ref.small_total),
        (turned.tokens, low.query, 0, grads[at_query]),
        (turned.tokens, low.key, 0, grads[at_key]),
    ]
    for first, columns in halves:
        target = grads[at_value].at[:, pl.ds(first, columns)]
        plans.append((turned.tokens, low.value, first, target))
    jobs = [Job(*plan) for plan in plans]
    reduce = Reduce(place, jobs, ref.reduce_sems, pool, SimpleNamespace(**ref.little))

    inner = [functools.partial(inner_piece, j) for j in range(many)]
    second = [functools.partial(second_piece, j) for j in range(many)]
    middle = pairs // 2
    base = many + 1
    def weight(index):
        return full[index]

    turn = functools.partial(turn_by_lane, ref.second_low, eye, turned.second)
    work = [(base - 1.7, inner[0], contract_rows(0)), (base - 1.3, turn, None)]
    work += [(base - 1.7 + j, inner[j], contract_rows(j)) for j in range(1, many)]
    work += [(base - 0.3 + j, second[j], expand.at[j]) for j in range(many)]
    base = 2 * many + 1
    work += [
        (base - 0.2, second_norm_piece, None),
        (base - 0.15, cross_start_piece, weight(at_cross_output)),
        (base + 0.3, functools.partial(cross_piece, 0, middle), None),
        (base + 0.7, functools.partial(cross_piece, middle, pairs), None),
        (base + 1.3, first_piece, weight(at_cross_query)),
        (base + 1.7, self_start_piece, weight(at_output)),
        (base + 2.3, functools.partial(self_piece, 0, middle), None),
        (base + 3.3, functools.partial(self_piece, middle, pairs), None),
        (base + 3.7, memory_key_piece, weight(at_cross_key)),
        (base + 4.3, memory_value_piece, weight(at_cross_value)),
        (base + 4.7, functools.partial(input_piece, low.query, True), weight(at_query)),
        (base + 5.5, functools.partial(input_piece, low.key, False), weight(at_key)),
        (base + 6.5, functools.partial(input_piece, low.value, False), weight(at_value)),
        (base + 8.5, memory_end_piece, None),
    ]
    work.sort(key=lambda item: item[0])
    backward_sources += [source for _, _, source in work if source is not None]
    loads += [load(backward_sources[0]), load(backward_sources[1])]
    norm_both(
        accumulated, ref.out_grad, gains, 2, ref.result, accumulated, low.third, small_sums
    )

    place.hear(ref.ready_sem)
    actions = [(time, piece) for time, piece, _ in work]
    for number in range(len(jobs)):
        actions += reduce.events(number)
    actions.sort(key=lambda item: item[0])
    for _, action in actions:
        action()

    total = ref.small_total[...]
    own = jnp.zeros((8, shard), jnp.float32)
    for member in range(n_mem):
        here = jnp.where(place.mem == member, 1.0, 0.0)
        own = own + here * total[:, member * shard : (member + 1) * shard]
    ref.gains_grad[...] = own[0:3]
    ref.shifts_grad[...] = own[3:6]
    reduce.finish()
    memory_total().wait_send()
    grad_total().wait_send()


SMALL_AT = 2


def copy_kernel(count, *refs):
    for source, target in zip(refs[:count], refs[count:]):
        target[...] = source[...]


def copied(values):
    near = pl.BlockSpec(memory_space=pltpu.VMEM)
    return pl.pallas_call(
        functools.partial(copy_kernel, len(values)),
        out_shape=[jax.ShapeDtypeStruct(value.shape, value.dtype) for value in values],
        in_specs=[near] * len(values),
        out_specs=[near] * len(values),
        compiler_params=pltpu.CompilerParams(vmem_limit_bytes=VMEM_LIMIT),
        name="results",
    )(*values)


def fused(n_rows, n_mem, ins):
    tokens, memory, squares = ins["tokens"], ins["memory"], ins["squares"]
    expand, contract = ins["expand"], ins["contract"]
    tokens_here, width = tokens.shape
    ff = expand.shape[1]
    shard = squares[0].shape[0]
    mem_tokens = memory.shape[0] * memory.shape[1]
    digits, half, many = (n_rows // 2).bit_length() - 1, n_rows // 2, ff // width
    pairs = width // (2 * HEAD_DIM)
    low, high = jnp.bfloat16, jnp.float32
    n_parts = 1 + SQUARES + 2 * many
    n_jobs = n_parts + 2
    dma, vmem = pltpu.SemaphoreType.DMA, pltpu.VMEM
    anywhere, near = pl.BlockSpec(memory_space=pl.ANY), pl.BlockSpec(memory_space=pltpu.VMEM)

    far_ins = dict(memory=memory)
    in_specs = {
        name: jax.tree.map(lambda _: anywhere if name in far_ins else near, value)
        for name, value in ins.items()
    }

    def out(shape, dtype=high):
        return jax.ShapeDtypeStruct(shape, dtype)

    outs = dict(
        result=out(tokens.shape),
        input_grad=out(tokens.shape),
        memory_grad=out(memory.shape),
        grads=[out(item.shape) for item in squares],
        expand_grad=out(expand.shape),
        contract_grad=out(contract.shape),
        gains_grad=out((3, shard)),
        shifts_grad=out((3, shard)),
    )
    far_outs = dict(
        full=[out((n_rows, n_mem, shard, width), low)] * SQUARES,
        expand_full=out((many, n_rows, n_mem, shard, width), low),
        contract_full=out((n_rows * n_mem, many, shard, width), low),
    )
    out_specs = jax.tree.map(lambda _: near, outs)
    out_specs.update(jax.tree.map(lambda _: anywhere, far_outs))
    outs.update(far_outs)

    def token_rows(dtype):
        return vmem((tokens_here, width), dtype)

    def memory_rows(dtype):
        return vmem((mem_tokens, width), dtype)

    tiny = (8, 128)

    counts = [half >> (stage + 1) for stage in range(digits)]
    units = (OUT_SLOTS + LANE_SLOTS + CORE_RING) * half + RING
    for stage, number in enumerate(counts):
        units += (SUM_SLOTS + (RING if stage else FIRST_RING)) * number
    units = max(units + SLOTS * n_rows, GATHER_SLOTS * n_rows)
    little = dict(
        lanes=vmem((half,) + tiny, high),
        core_in=vmem((half,) + tiny, high),
        sums=[vmem((number,) + tiny, high) for number in counts],
        arrived=[vmem((number,) + tiny, high) for number in counts]
        + [vmem((n_mem - 1,) + tiny, high)],
    )
    left = vmem((2, width // 2, tokens_here), low)
    scratch = dict(
        small=vmem(tiny, high),
        small_full=vmem((n_rows, n_mem) + tiny, high),
        small_total=vmem(tiny, high),
        pool=vmem((units, n_mem, shard, width), low),
        slot_sem=dma((SLOTS,)),
        keep_sem=dma((n_parts - 1,)),
        ready_sem=pltpu.SemaphoreType.REGULAR,
        mem_sem=dma((6,)),
        gather_sems=[
            dma(shape + (n_parts,))
            for shape in ((), (), (), (digits,), (digits,), (), ())
            + ((2 * (n_mem - 1),), (2 * (n_mem - 1),))
        ],
        reduce_sems=[dma(shape + (n_jobs,)) for shape in ((), (), (digits + 1,), (digits + 1,))],
        gains=vmem((8, width), high),
        query=token_rows(low),
        keys=token_rows(low),
        values=token_rows(low),
        attended=token_rows(low),
        first_low=token_rows(low),
        second_low=token_rows(low),
        cross_query=token_rows(low),
        crossed=token_rows(low),
        cross_keys=memory_rows(low),
        cross_values=memory_rows(low),
        mem_rows=memory_rows(low),
        mem_out=memory_rows(low),
        mem_in=vmem(memory.shape, low),
        unit1=token_rows(high),
        unit2=token_rows(high),
        accumulated=token_rows(high),
        other=token_rows(high),
        scale1=vmem((tokens_here, 1), high),
        scale2=vmem((tokens_here, 1), high),
        self_bias=vmem((tokens_here, tokens_here), high),
        cross_bias=vmem((mem_tokens, tokens_here), high),
        self_lse=vmem((pairs, 2, tokens_here), high),
        cross_lse=vmem((pairs, 2, tokens_here), high),
        eye=vmem((TILE, TILE), low),
        hidden=vmem((tokens_here, ff), low),
        slope=vmem((tokens_here, ff), low),
        hidden_turned=vmem((many, 2, width // 2, tokens_here), low),
        turned=dict(
            tokens=left, attended=left, first=left, memory=left, crossed=left, second=left
        ),
        low=dict(
            third=token_rows(low),
            second=token_rows(low),
            first=token_rows(low),
            branch=token_rows(low),
            cross_query=token_rows(low),
            cross_key=memory_rows(low),
            cross_value=memory_rows(low),
            query=token_rows(low),
            key=token_rows(low),
            value=token_rows(low),
        ),
        small_sums=vmem((2, half) + tiny, high),
        little=little,
    )
    in_values, in_tree = jax.tree.flatten(ins)
    out_shapes, out_tree = jax.tree.flatten(outs)
    scratch_shapes, scratch_tree = jax.tree.flatten(scratch)
    places = jax.tree.unflatten(in_tree, range(len(in_values)))
    at = len(in_values)
    places.update(jax.tree.unflatten(out_tree, range(at, at + len(out_shapes))))
    at += len(out_shapes)
    places.update(jax.tree.unflatten(scratch_tree, range(at, at + len(scratch_shapes))))
    values = pl.pallas_call(
        functools.partial(layer_kernel, places, (n_rows, n_mem, width, ff, shard)),
        out_shape=out_shapes,
        in_specs=jax.tree.leaves(in_specs),
        out_specs=jax.tree.leaves(out_specs),
        scratch_shapes=scratch_shapes,
        compiler_params=pltpu.CompilerParams(
            collective_id=0, has_side_effects=True, vmem_limit_bytes=VMEM_LIMIT
        ),
        name="layer",
    )(*in_values)
    found = jax.tree.unflatten(out_tree, values)
    for name in far_outs:
        del found[name]
    return found


def local(n_rows, n_mem, *args):
    (
        tokens,
        memory,
        token_ids,
        memory_ids,
        out_grad,
        self_query,
        self_key,
        self_value,
        self_output,
        cross_query,
        cross_key,
        cross_value,
        cross_output,
        expand_weight,
        contract_weight,
        norm_gains,
        norm_shifts,
    ) = args
    shard, width = self_query.shape
    suits = width == 128 * n_rows and shard % 16 == 0 and tokens.shape[0] == 1
    suits = suits and tokens.shape[1] == TILE and expand_weight.shape[1] == n_mem * width
    if not suits or n_rows < 4 or n_rows & (n_rows - 1) or n_mem < 2:
        return plain(*args)
    found = fused(
        n_rows,
        n_mem,
        dict(
            tokens=tokens[0],
            memory=memory,
            token_ids=token_ids,
            memory_ids=memory_ids,
            out_grad=out_grad[0],
            squares=[
                self_query,
                self_key,
                self_value,
                self_output,
                cross_query,
                cross_key,
                cross_value,
                cross_output,
            ],
            expand=expand_weight,
            contract=contract_weight,
            norm_gains=norm_gains,
            norm_shifts=norm_shifts,
        ),
    )
    values, tree = jax.tree.flatten(found)
    found = SimpleNamespace(**jax.tree.unflatten(tree, copied(values)))
    return (
        found.result[None],
        found.input_grad[None],
        found.memory_grad,
        *found.grads,
        found.expand_grad,
        found.contract_grad,
        found.gains_grad,
        found.shifts_grad,
    )


def solution(mesh):
    in_specs = (
        P(("rows", "mem"), None, None),
        P("rows", "mem", None),
        P("rows", None),
        P("rows", None),
        P(("rows", "mem"), None, None),
        P(("rows", "mem"), None),
        P(("rows", "mem"), None),
        P(("rows", "mem"), None),
        P(("rows", "mem"), None),
        P(("rows", "mem"), None),
        P(("rows", "mem"), None),
        P(("rows", "mem"), None),
        P(("rows", "mem"), None),
        P(("rows", "mem"), None),
        P(("rows", "mem"), None),
        P(None, ("rows", "mem")),
        P(None, ("rows", "mem")),
    )
    out_specs = (
        P(("rows", "mem"), None, None),
        P(("rows", "mem"), None, None),
        P("rows", "mem", None),
        P(("rows", "mem"), None),
        P(("rows", "mem"), None),
        P(("rows", "mem"), None),
        P(("rows", "mem"), None),
        P(("rows", "mem"), None),
        P(("rows", "mem"), None),
        P(("rows", "mem"), None),
        P(("rows", "mem"), None),
        P(("rows", "mem"), None),
        P(("rows", "mem"), None),
        P(None, ("rows", "mem")),
        P(None, ("rows", "mem")),
    )
    layer = functools.partial(local, mesh.shape["rows"], mesh.shape["mem"])
    return jax.shard_map(layer, mesh=mesh, in_specs=in_specs, out_specs=out_specs, check_vma=False)
```

```python
import functools
import math
from types import SimpleNamespace

import jax
import jax.numpy as jnp
from jax import lax
from jax.experimental import pallas as pl
from jax.experimental.pallas import tpu as pltpu
from jax.sharding import PartitionSpec as P

MESH = pl.DeviceIdType.MESH

HEADS = 16
HEAD_DIM = 64


ALPHA = 4.16
EPS = 1e-05
SCALE = 0.125
NEG = -1e30


def layer_norm(hidden_activation, gain, shift):
    centre = hidden_activation - jnp.mean(hidden_activation, axis=-1, keepdims=True)
    spread = jnp.mean(centre * centre, axis=-1, keepdims=True)
    return centre * lax.rsqrt(spread + EPS) * gain + shift


def gelu_exact(value):
    return jax.nn.gelu(value, approximate=False)


def product(left, right):
    return jnp.dot(left, right, preferred_element_type=jnp.float32)


def split_heads(matrix):
    return matrix.reshape(matrix.shape[0], matrix.shape[1] // HEAD_DIM, HEAD_DIM)


def grouped(matrix):
    return jnp.moveaxis(matrix.reshape(matrix.shape[0], HEADS // 4, 4 * HEAD_DIM), 1, 0)


def ungrouped(stack):
    return jnp.moveaxis(stack, 0, 1).reshape(stack.shape[1], stack.shape[0] * stack.shape[2])


def row_map(function, items):
    return lax.map(lambda entry: function(*entry), items)


def score_block(query, keys, allowed):
    raw = jnp.einsum(
        "khe,qhe->hkq", split_heads(keys), split_heads(query), preferred_element_type=jnp.float32
    )
    return jnp.where(allowed[None], raw * SCALE, NEG)


def attend_probs(query, keys, allowed, lse):
    scores = score_block(query, keys, allowed)
    return jnp.where(allowed[None], jnp.exp(scores - lse[:, None, :]), 0.0)


def attend_forward(query, keys, values, allowed):
    scores = score_block(query, keys, allowed)
    top = jnp.max(scores, axis=1)
    weight = jnp.where(allowed[None], jnp.exp(scores - top[:, None, :]), 0.0)
    total = jnp.sum(weight, axis=1)
    probs = (weight / total[:, None, :]).astype(jnp.bfloat16)
    mixed = jnp.einsum(
        "hkq,khe->qhe", probs, split_heads(values), preferred_element_type=jnp.float32
    )
    return (mixed.reshape(query.shape), top + jnp.log(total))


def value_pull(grad, values):
    return jnp.einsum(
        "qhe,khe->hkq", split_heads(grad), split_heads(values), preferred_element_type=jnp.float32
    )


def score_grads(probs, pulled, inner):
    return (probs * (pulled - inner[:, None, :]) * SCALE).astype(jnp.bfloat16)


def query_from(score_grad, keys, shape):
    moved = jnp.einsum(
        "hkq,khe->qhe", score_grad, split_heads(keys), preferred_element_type=jnp.float32
    )
    return moved.reshape(shape)


def key_from(score_grad, query, shape):
    moved = jnp.einsum(
        "hkq,qhe->khe", score_grad, split_heads(query), preferred_element_type=jnp.float32
    )
    return moved.reshape(shape)


def value_from(probs, grad, values):
    moved = jnp.einsum(
        "hkq,qhe->khe",
        probs.astype(jnp.bfloat16),
        split_heads(grad),
        preferred_element_type=jnp.float32,
    )
    return moved.reshape(values.shape)


def local_forward(query, keys, values, allowed):

    def one_group(items):
        return attend_forward(items[0], items[1], items[2], allowed)

    mixed, lse = lax.map(one_group, (grouped(query), grouped(keys), grouped(values)))
    return (ungrouped(mixed), lse)


def local_backward(query, keys, values, allowed, lse, grad):

    def one_group(items):
        part_query, part_keys, part_values, part_lse, part_grad = items
        probs = attend_probs(part_query, part_keys, allowed, part_lse)
        pulled = value_pull(part_grad, part_values)
        inner = jnp.sum(probs * pulled, axis=1)
        score_grad = score_grads(probs, pulled, inner)
        return (
            query_from(score_grad, part_keys, part_query.shape),
            key_from(score_grad, part_query, part_keys.shape),
            value_from(probs, part_grad, part_values),
        )

    parts = lax.map(one_group, (grouped(query), grouped(keys), grouped(values), lse, grouped(grad)))
    return (ungrouped(parts[0]), ungrouped(parts[1]), ungrouped(parts[2]))


def plain(
    tokens,
    memory,
    token_ids,
    memory_ids,
    out_grad,
    self_query,
    self_key,
    self_value,
    self_output,
    cross_query,
    cross_key,
    cross_value,
    cross_output,
    expand_weight,
    contract_weight,
    norm_gains,
    norm_shifts,
):
    full = (
        lax.all_gather(self_query, ("rows", "mem"), axis=0, tiled=True),
        lax.all_gather(self_key, ("rows", "mem"), axis=0, tiled=True),
        lax.all_gather(self_value, ("rows", "mem"), axis=0, tiled=True),
        lax.all_gather(self_output, ("rows", "mem"), axis=0, tiled=True),
        lax.all_gather(cross_query, ("rows", "mem"), axis=0, tiled=True),
        lax.all_gather(cross_key, ("rows", "mem"), axis=0, tiled=True),
        lax.all_gather(cross_value, ("rows", "mem"), axis=0, tiled=True),
        lax.all_gather(cross_output, ("rows", "mem"), axis=0, tiled=True),
        lax.all_gather(expand_weight, ("rows", "mem"), axis=0, tiled=True),
        lax.all_gather(contract_weight, ("rows", "mem"), axis=0, tiled=True),
        lax.all_gather(jnp.transpose(norm_gains), ("rows", "mem"), axis=0, tiled=True),
        lax.all_gather(jnp.transpose(norm_shifts), ("rows", "mem"), axis=0, tiled=True),
    )
    (
        self_attention_query,
        decoder_match_label,
        self_attention_value,
        self_attention_output,
        encoder_lookup_probe,
        key_cross,
        value_cross,
        cross_attention_output,
        up_projection,
        narrowing_matrix,
        gain_cols,
        shift_cols,
    ) = full
    gain_rows = jnp.transpose(gain_cols).astype(jnp.float32)
    shift_rows = jnp.transpose(shift_cols).astype(jnp.float32)
    rows_here = tokens.shape[0]
    member = lax.axis_index("mem")
    own_ids = lax.dynamic_slice_in_dim(token_ids, member * rows_here, rows_here, 0)
    positions = jnp.arange(tokens.shape[1], dtype=jnp.int32)
    self_allowed = (own_ids[:, :, None] == own_ids[:, None, :]) & (
        positions[:, None] <= positions[None, :]
    )[None]
    query = product(tokens, self_attention_query).astype(jnp.bfloat16)
    keys = product(tokens, decoder_match_label).astype(jnp.bfloat16)
    values = product(tokens, self_attention_value).astype(jnp.bfloat16)
    self_mixed, self_lse = row_map(local_forward, (query, keys, values, self_allowed))
    attention_result = self_mixed.astype(jnp.bfloat16)
    first, first_back = jax.vjp(
        layer_norm,
        ALPHA * tokens.astype(jnp.float32) + product(attention_result, self_attention_output),
        gain_rows[0],
        shift_rows[0],
    )
    first_reduced = first.astype(jnp.bfloat16)
    cross_queries = product(first_reduced, encoder_lookup_probe).astype(jnp.bfloat16)
    memory_rows = lax.all_to_all(memory, "mem", split_axis=0, concat_axis=1, tiled=True)
    row_ids = lax.dynamic_slice_in_dim(memory_ids, member * rows_here, rows_here, 0)
    cross_allowed = row_ids[:, :, None] == own_ids[:, None, :]
    cross_keys = product(memory_rows, key_cross).astype(jnp.bfloat16)
    cross_values = product(memory_rows, value_cross).astype(jnp.bfloat16)
    cross_mixed, cross_lse = row_map(
        local_forward, (cross_queries, cross_keys, cross_values, cross_allowed)
    )
    cross_attention_result = cross_mixed.astype(jnp.bfloat16)
    second, second_back = jax.vjp(
        layer_norm,
        ALPHA * first + product(cross_attention_result, cross_attention_output),
        gain_rows[1],
        shift_rows[1],
    )
    second_reduced = second.astype(jnp.bfloat16)
    hidden_value, gelu_back = jax.vjp(gelu_exact, product(second_reduced, up_projection))
    hidden_activation = hidden_value.astype(jnp.bfloat16)
    result, third_back = jax.vjp(
        layer_norm,
        ALPHA * second + product(hidden_activation, narrowing_matrix),
        gain_rows[2],
        shift_rows[2],
    )
    third_grad, gain_three, shift_three = third_back(out_grad.astype(jnp.float32))
    feedforward_gradient = third_grad.astype(jnp.bfloat16)
    down_projection_gradient = jnp.einsum(
        "ehj,ehc->jc", hidden_activation, feedforward_gradient, preferred_element_type=jnp.float32
    )
    (inner_grad,) = gelu_back(
        jnp.einsum(
            "hpu,ku->hpk",
            feedforward_gradient,
            narrowing_matrix,
            preferred_element_type=jnp.float32,
        )
    )
    inner_reduced = inner_grad.astype(jnp.bfloat16)
    expand_grad = jnp.einsum(
        "iqg,iqe->ge", second_reduced, inner_reduced, preferred_element_type=jnp.float32
    )
    second_total = ALPHA * third_grad + jnp.einsum(
        "iwm,fm->iwf", inner_reduced, up_projection, preferred_element_type=jnp.float32
    )
    second_grad, gain_two, shift_two = second_back(second_total)
    cross_branch_gradient = second_grad.astype(jnp.bfloat16)
    output_cross_grad = jnp.einsum(
        "nhb,nhc->bc",
        cross_attention_result,
        cross_branch_gradient,
        preferred_element_type=jnp.float32,
    )
    crossed_grad = jnp.einsum(
        "qwp,up->qwu",
        cross_branch_gradient,
        cross_attention_output,
        preferred_element_type=jnp.float32,
    ).astype(jnp.bfloat16)
    query_grads, key_grads, value_grads = row_map(
        local_backward,
        (cross_queries, cross_keys, cross_values, cross_allowed, cross_lse, crossed_grad),
    )
    key_low = key_grads.astype(jnp.bfloat16)
    value_low = value_grads.astype(jnp.bfloat16)
    row_grad = jnp.einsum(
        "sme,de->smd", key_low, key_cross, preferred_element_type=jnp.float32
    ) + jnp.einsum("sme,de->smd", value_low, value_cross, preferred_element_type=jnp.float32)
    key_cross_grad = jnp.einsum(
        "smd,sme->de", memory_rows, key_low, preferred_element_type=jnp.float32
    )
    value_cross_grad = jnp.einsum(
        "smd,sme->de", memory_rows, value_low, preferred_element_type=jnp.float32
    )
    memory_grad = lax.all_to_all(
        row_grad.astype(jnp.bfloat16), "mem", split_axis=1, concat_axis=0, tiled=True
    ).astype(row_grad.dtype)
    probe_lowered_precision = query_grads.astype(jnp.bfloat16)
    query_cross_grad = jnp.einsum(
        "nhb,nhc->bc", first_reduced, probe_lowered_precision, preferred_element_type=jnp.float32
    )
    first_total = ALPHA * second_grad + jnp.einsum(
        "qwp,up->qwu",
        probe_lowered_precision,
        encoder_lookup_probe,
        preferred_element_type=jnp.float32,
    )
    first_grad, gain_one, shift_one = first_back(first_total)
    self_branch_gradient = first_grad.astype(jnp.bfloat16)
    output_self_grad = jnp.einsum(
        "nhb,nhc->bc", attention_result, self_branch_gradient, preferred_element_type=jnp.float32
    )
    attended_grad = jnp.einsum(
        "qwp,up->qwu",
        self_branch_gradient,
        self_attention_output,
        preferred_element_type=jnp.float32,
    ).astype(jnp.bfloat16)
    self_query_reduced, decoder_label_lowered, self_value_reduced = row_map(
        local_backward, (query, keys, values, self_allowed, self_lse, attended_grad)
    )
    self_query_reduced = self_query_reduced.astype(jnp.bfloat16)
    decoder_label_lowered = decoder_label_lowered.astype(jnp.bfloat16)
    self_value_reduced = self_value_reduced.astype(jnp.bfloat16)
    query_self_grad = jnp.einsum(
        "nhb,nhc->bc", tokens, self_query_reduced, preferred_element_type=jnp.float32
    )
    key_self_grad = jnp.einsum(
        "nhb,nhc->bc", tokens, decoder_label_lowered, preferred_element_type=jnp.float32
    )
    value_self_grad = jnp.einsum(
        "nhb,nhc->bc", tokens, self_value_reduced, preferred_element_type=jnp.float32
    )
    input_grad = (
        ALPHA * first_grad
        + jnp.einsum(
            "qwp,up->qwu",
            self_query_reduced,
            self_attention_query,
            preferred_element_type=jnp.float32,
        )
        + jnp.einsum(
            "qwp,up->qwu",
            decoder_label_lowered,
            decoder_match_label,
            preferred_element_type=jnp.float32,
        )
        + jnp.einsum(
            "qwp,up->qwu",
            self_value_reduced,
            self_attention_value,
            preferred_element_type=jnp.float32,
        )
    )
    gain_grad = jnp.stack([gain_one, gain_two, gain_three], axis=1)
    shift_grad = jnp.stack([shift_one, shift_two, shift_three], axis=1)
    sums = (
        lax.psum_scatter(query_self_grad, ("rows", "mem"), scatter_dimension=0, tiled=True),
        lax.psum_scatter(key_self_grad, ("rows", "mem"), scatter_dimension=0, tiled=True),
        lax.psum_scatter(value_self_grad, ("rows", "mem"), scatter_dimension=0, tiled=True),
        lax.psum_scatter(output_self_grad, ("rows", "mem"), scatter_dimension=0, tiled=True),
        lax.psum_scatter(query_cross_grad, ("rows", "mem"), scatter_dimension=0, tiled=True),
        lax.psum_scatter(key_cross_grad, ("rows", "mem"), scatter_dimension=0, tiled=True),
        lax.psum_scatter(value_cross_grad, ("rows", "mem"), scatter_dimension=0, tiled=True),
        lax.psum_scatter(output_cross_grad, ("rows", "mem"), scatter_dimension=0, tiled=True),
        lax.psum_scatter(expand_grad, ("rows", "mem"), scatter_dimension=0, tiled=True),
        lax.psum_scatter(
            down_projection_gradient, ("rows", "mem"), scatter_dimension=0, tiled=True
        ),
        lax.psum_scatter(gain_grad, ("rows", "mem"), scatter_dimension=0, tiled=True),
        lax.psum_scatter(shift_grad, ("rows", "mem"), scatter_dimension=0, tiled=True),
    )
    return (
        result,
        input_grad,
        memory_grad,
        sums[0],
        sums[1],
        sums[2],
        sums[3],
        sums[4],
        sums[5],
        sums[6],
        sums[7],
        sums[8],
        sums[9],
        jnp.transpose(sums[10]),
        jnp.transpose(sums[11]),
    )


ALL = slice(None)
TILE = 256
SLOTS = 3
GATHER_SLOTS = 9
VMEM_LIMIT = 61 * 1024 * 1024


def flip(index, unit):
    return index + unit * (1 - 2 * ((index // unit) % 2))


def span(index, size):
    return pl.ds(pl.multiple_of(index * size, size), size)


class Place:
    def __init__(self, n_rows, n_mem):
        self.n_rows, self.n_mem = n_rows, n_mem
        self.digits = (n_rows // 2).bit_length() - 1
        self.row = lax.axis_index("rows")
        self.mem = lax.axis_index("mem")
        self.lane = self.row % 2

    def turn(self, index, stage):
        rising, falling = 2 << stage, 2 << (self.digits - 1 - stage)
        return flip(index, rising) * (1 - self.lane) + flip(index, falling) * self.lane

    def sibling(self):
        return (flip(self.row, 1), self.mem)

    def partner(self, stage):
        return (self.turn(self.row, stage), self.mem)

    def far(self, step):
        return (self.row, (self.mem + step) % self.n_mem)

    def others(self):
        found = [self.far(step) for step in range(1, self.n_mem)]
        found += [self.partner(stage) for stage in range(self.digits)]
        return found + [self.sibling()]

    def tell(self, semaphore):
        for other in self.others():
            pl.semaphore_signal(semaphore, inc=1, device_id=other, device_id_type=MESH)

    def hear(self, semaphore):
        pl.semaphore_wait(semaphore, len(self.others()))

    def greet(self):
        self.tell(pltpu.get_barrier_semaphore())
        self.hear(pltpu.get_barrier_semaphore())


def remote(source, target, send_sem, recv_sem, device):
    return pltpu.make_async_remote_copy(
        src_ref=source,
        dst_ref=target,
        send_sem=send_sem,
        recv_sem=recv_sem,
        device_id=device,
        device_id_type=MESH,
    )


def waits(total):
    return (lambda: total().wait_recv(), lambda: total().wait_send())


class Part:
    def __init__(self, source, target, near=0, straight=False):
        self.source, self.target = source, target
        self.near, self.straight = near, straight


class Gather:
    def __init__(self, place, parts, sems):
        self.place, self.parts = place, parts
        (
            self.own_sem,
            self.far_send,
            self.far_recv,
            self.plane_send,
            self.plane_recv,
            self.core_send,
            self.core_recv,
            self.line_send,
            self.line_recv,
        ) = sems

    def group(self, number, group):
        return self.parts[number].target.at[group]

    def one(self, number, group, member):
        return self.parts[number].target.at[group, member]

    def shard(self, number):
        return self.parts[number].source

    def mine(self, number):
        return self.one(number, self.place.row, self.place.mem)

    def own(self, number):
        return pltpu.make_async_copy(self.shard(number), self.mine(number), self.own_sem.at[number])

    def held(self, stage):
        groups = [self.place.row]
        for before in range(stage):
            groups = groups + [self.place.turn(group, before) for group in groups]
        return groups

    def far_total(self, number):
        part = self.parts[number]
        some = part.target.at[pl.ds(0, 1 << part.near), pl.ds(0, self.place.n_mem - 1)]
        return remote(
            some, some, self.far_send.at[number], self.far_recv.at[number], self.place.far(1)
        )

    def far_hop(self, number, first):
        place = self.place
        for group in self.held(self.parts[number].near):
            target = self.one(number, group, place.mem)
            source = self.shard(number) if first else target
            for step in range(1, place.n_mem):
                remote(
                    source,
                    target,
                    self.far_send.at[number],
                    self.far_recv.at[number],
                    place.far(step),
                ).start()

    def sides(self, step):
        mem, n_mem = self.place.mem, self.place.n_mem
        return (
            ((mem - step >= 0) & (mem + 1 < n_mem), mem - step, 1, mem - 1 - step >= 0),
            ((mem + step < n_mem) & (mem >= 1), mem + step, n_mem - 1, mem + 1 + step < n_mem),
        )

    def line_total(self, number, step, side):
        part, at = self.parts[number], 2 * step + side
        some = part.target.at[pl.ds(0, 1 << part.near), 0]
        sems = (self.line_send.at[at, number], self.line_recv.at[at, number])
        return remote(some, some, *sems, self.place.far(1))

    def line_arrived(self, number, step):
        for side, (_, _, _, receives) in enumerate(self.sides(step)):

            @pl.when(receives)
            def _(side=side):
                self.line_total(number, step, side).wait_recv()

    def line_sent(self, number, step):
        for side, (sends, _, _, _) in enumerate(self.sides(step)):

            @pl.when(sends)
            def _(side=side):
                self.line_total(number, step, side).wait_send()

    def line_hop(self, number, step, first):
        place = self.place
        for side, (sends, member, towards, _) in enumerate(self.sides(step)):
            member = (member + place.n_mem) % place.n_mem

            @pl.when(sends)
            def _(side=side, member=member, towards=towards):
                for group in self.held(self.parts[number].near):
                    target = self.one(number, group, member)
                    remote(
                        self.shard(number) if first else target,
                        target,
                        self.line_send.at[2 * step + side, number],
                        self.line_recv.at[2 * step + side, number],
                        place.far(towards),
                    ).start()

    def plane_total(self, number, stage):
        part = self.parts[number]
        some = part.target.at[pl.ds(0, 1 << stage)]
        if stage < part.near:
            some = part.target.at[pl.ds(0, 1 << stage), 0]
        return remote(
            some,
            some,
            self.plane_send.at[stage, number],
            self.plane_recv.at[stage, number],
            self.place.partner(stage),
        )

    def plane_hop(self, number, stage, first):
        for group in self.held(stage):
            if stage < self.parts[number].near:
                target = self.one(number, group, self.place.mem)
            else:
                target = self.group(number, group)
            remote(
                self.shard(number) if first else target,
                target,
                self.plane_send.at[stage, number],
                self.plane_recv.at[stage, number],
                self.place.partner(stage),
            ).start()

    def core_total(self, number):
        some = self.parts[number].target.at[pl.ds(0, self.place.n_rows // 2)]
        return remote(
            some, some, self.core_send.at[number], self.core_recv.at[number], self.place.sibling()
        )

    def core_hop(self, number, first):
        for group in self.held(self.place.digits):
            block = self.group(number, group)
            remote(
                block,
                block,
                self.core_send.at[number],
                self.core_recv.at[number],
                self.place.sibling(),
            ).start()

    def hops(self, number):
        part, take = self.parts[number], functools.partial
        along = []
        if part.straight:
            along.append((1.6, take(self.far_hop, number)) + waits(take(self.far_total, number)))
        else:
            for step in range(self.place.n_mem - 1):
                along.append(
                    (
                        0.55 if step else 1.4,
                        take(self.line_hop, number, step),
                        take(self.line_arrived, number, step),
                        take(self.line_sent, number, step),
                    )
                )
        plane = []
        for stage in range(self.place.digits):
            total = take(self.plane_total, number, stage)
            plane.append((1.5, take(self.plane_hop, number, stage)) + waits(total))
        core = (1.5, take(self.core_hop, number)) + waits(take(self.core_total, number))
        return plane[: part.near] + along + plane[part.near :] + [core]

    def events(self, number):
        hops = self.hops(number)
        time, found = float(number), []

        def act(at):
            if at == 0:
                self.own(number).start()
            else:
                if at == 1:
                    self.own(number).wait()
                hops[at - 1][2]()
            hops[at][1](at == 0)

        for at in range(len(hops)):
            time += hops[at][0] if at else 0.0
            found.append((time, functools.partial(act, at)))
        return found, time + 0.9

    def sent(self, number):
        for hop in self.hops(number):
            hop[3]()


class Job:
    def __init__(self, left, right, first, target):
        self.left, self.right, self.first, self.target = left, right, first, target
        self.small = right is None
        self.width = target.shape[-1]
        self.large = 0


OUT_SLOTS, LANE_SLOTS, SUM_SLOTS, CORE_RING, FIRST_RING, RING = 2, 3, 2, 2, 6, 4


class Reduce:
    def __init__(self, place, jobs, sems, pool, small):
        self.place, self.jobs, self.small = place, jobs, small
        self.core_send, self.core_recv, self.stage_send, self.stage_recv = sems
        wanted = [place.row]
        for stage in reversed(range(place.digits)):
            wanted = wanted + [place.turn(group, stage) for group in wanted]
        self.wanted = [group // 2 for group in wanted]
        for number, job in enumerate(job for job in jobs if not job.small):
            job.large = number
        used, half = [0], place.n_rows // 2

        def take(count, units):
            first = used[0]
            used[0] += count * units
            return [pool.at[pl.ds(first + i * units, units)] for i in range(count)]

        self.outs = take(OUT_SLOTS, half)
        self.lane_slots = take(LANE_SLOTS, half)
        self.core_ring = take(CORE_RING, half)
        self.sum_slots, self.rings = [], []
        for stage in range(place.digits):
            self.sum_slots.append(take(SUM_SLOTS, self.count(stage)))
            self.rings.append(take(RING if stage else FIRST_RING, self.count(stage)))
        self.rings.append(take(RING, 1))
        self.used = used[0]

    def count(self, stage):
        return max(self.place.n_rows // 4 >> stage, 1)

    def cut(self, ref, job):
        return ref if job.width == ref.shape[-1] else ref.at[:, :, :, pl.ds(0, job.width)]

    def out(self, job):
        return self.cut(self.outs[job.large % OUT_SLOTS], job)

    def lanes(self, job):
        if job.small:
            return self.small.lanes
        return self.cut(self.lane_slots[job.large % LANE_SLOTS], job)

    def core_in(self, job):
        if job.small:
            return self.small.core_in
        return self.cut(self.core_ring[job.large % CORE_RING], job)

    def sums(self, job, stage):
        if job.small:
            return self.small.sums[stage]
        return self.cut(self.sum_slots[stage][job.large % SUM_SLOTS], job)

    def arrived(self, job, stage):
        if job.small:
            return self.small.arrived[stage]
        ring = self.rings[stage]
        units = self.cut(ring[job.large % len(ring)], job)
        if stage == self.place.digits:
            return units.at[0, pl.ds(0, self.place.n_mem - 1)]
        return units

    def previous(self, number, distance):
        found = [n for n in range(number) if not self.jobs[n].small]
        if self.jobs[number].small or len(found) < distance:
            return None
        return found[-distance]

    def core_copy(self, number):
        job = self.jobs[number]
        source = job.left.at[1 - self.place.lane] if job.small else self.out(job)
        return remote(
            source,
            self.core_in(job),
            self.core_send.at[number],
            self.core_recv.at[number],
            self.place.sibling(),
        )

    def product(self, job, side, store):
        half = self.place.n_rows // 2
        group = job.left.shape[1] // half
        width = min(TILE, job.width)
        unit = (self.place.n_mem, group // self.place.n_mem, width)

        def column_step(step, carry):
            source = pl.ds(pl.multiple_of(job.first + step * width, width), width)
            value = dot(job.left[side], job.right[:, source])
            for index in range(half):
                block = value[index * group : (index + 1) * group].reshape(unit)
                store(index, span(step, width), block)
            return carry

        lax.fori_loop(0, job.width // width, column_step, 0)

    def core_stage(self, number):
        job = self.jobs[number]
        if not job.small:
            before = self.previous(number, OUT_SLOTS)
            if before is not None:
                self.core_copy(before).wait_send()
            out = self.out(job)

            def store(index, columns, value):
                out[index, :, :, columns] = value.astype(out.dtype)

            self.product(job, 1 - self.place.lane, store)
        self.core_copy(number).start()

    def lane_stage(self, number):
        job = self.jobs[number]
        before = self.previous(number, LANE_SLOTS)
        if before is not None:
            self.total(before, 0).wait_send()
        lanes, arrived = self.lanes(job), self.core_in(job)
        self.core_copy(number).wait_recv()
        if job.small:
            lanes[...] = job.left[self.place.lane] + arrived[...]
        else:

            def store(index, columns, value):
                total = value + arrived[index, :, :, columns].astype(jnp.float32)
                lanes[index, :, :, columns] = total.astype(lanes.dtype)

            self.product(job, self.place.lane, store)
        self.send(number, 0)

    def unit(self, job, stage, index):
        if stage == 0:
            return self.lanes(job).at[self.wanted[index]]
        return self.sums(job, stage - 1).at[index]

    def piece(self, job, unit, member):
        return unit if job.small else unit.at[member]

    def send(self, number, stage):
        job, place = self.jobs[number], self.place
        arrived = self.arrived(job, stage)
        sems = (self.stage_send.at[stage, number], self.stage_recv.at[stage, number])
        if stage == place.digits:
            unit = self.unit(job, stage, 0)
            for step in range(1, place.n_mem):
                source = self.piece(job, unit, (place.mem + step) % place.n_mem)
                remote(source, arrived.at[step - 1], *sems, place.far(step)).start()
            return
        left = self.count(stage)
        for index in range(left):
            source = self.unit(job, stage, left + index)
            remote(source, arrived.at[index], *sems, place.partner(stage)).start()

    def total(self, number, stage):
        some = self.arrived(self.jobs[number], stage)
        sems = (self.stage_send.at[stage, number], self.stage_recv.at[stage, number])
        return remote(some, some, *sems, self.place.far(1))

    def stage(self, number, stage):
        job, place = self.jobs[number], self.place
        arrived = self.arrived(job, stage)
        if stage == place.digits:
            self.total(number, stage).wait_recv()
            value = self.piece(job, self.unit(job, stage, 0), place.mem)[...].astype(jnp.float32)
            for step in range(place.n_mem - 1):
                value = value + arrived[step].astype(jnp.float32)
            job.target[...] = value
            return
        before = self.previous(number, SUM_SLOTS)
        if before is not None:
            self.total(before, stage + 1).wait_send()
        self.total(number, stage).wait_recv()
        sums = self.sums(job, stage)
        for index in range(self.count(stage)):
            unit, coming, target = self.unit(job, stage, index), arrived.at[index], sums.at[index]
            if job.small:
                target[...] = unit[...] + coming[...]
                continue

            def add(member, carry, unit=unit, coming=coming, target=target):
                value = unit[member].astype(jnp.float32) + coming[member].astype(jnp.float32)
                target[member] = value.astype(target.dtype)
                return carry

            lax.fori_loop(0, place.n_mem, add, 0)
        self.send(number, stage + 1)

    def events(self, number):
        found = [(0.0, functools.partial(self.core_stage, number))]
        found.append((0.9, functools.partial(self.lane_stage, number)))
        time = 2.2 if number < 2 else 3.2
        for stage in range(self.place.digits + 1):
            found.append((time, functools.partial(self.stage, number, stage)))
            time += 1.4
        found[-1] = (found[-1][0] - 0.3, found[-1][1])
        return [(number + time, action) for time, action in found]

    def finish(self):
        n_jobs, last = len(self.jobs), self.place.digits
        out = {self.previous(number, OUT_SLOTS) for number in range(n_jobs)}
        lanes = {self.previous(number, LANE_SLOTS) for number in range(n_jobs)}
        sums = {self.previous(number, SUM_SLOTS) for number in range(n_jobs)}
        for number in range(n_jobs):
            if number not in out:
                self.core_copy(number).wait_send()
            if number not in lanes:
                self.total(number, 0).wait_send()
            if number not in sums:
                for stage in range(1, last + 1):
                    self.total(number, stage).wait_send()


NORMAL = (((1,), (0,)), ((), ()))
TURNED = (((1,), (1,)), ((), ()))
LEFT_TURNED = (((0,), (0,)), ((), ()))


def dot(left, right, dims=NORMAL):
    return lax.dot_general(left, right, dims, preferred_element_type=jnp.float32)


def times(left, weight, store, part=0, parts=1):
    size = weight.shape[-1]
    width = min(TILE, size)
    tiles = size // width // parts

    def column_step(step, carry):
        columns = span(step, width)
        store(columns, dot(left[...], weight[:, :, :, columns].reshape(-1, width)))
        return carry

    lax.fori_loop(part * tiles, (part + 1) * tiles, column_step, 0)


def times_turned(left, weight, store):
    unit = weight.shape[1] * weight.shape[2]
    units = max(TILE // unit, 1)

    def row_step(step, carry):
        rows = weight[span(step, units)].reshape(units * unit, weight.shape[-1])
        store(span(step, units * unit), dot(left[...], rows, TURNED))
        return carry

    lax.fori_loop(0, weight.shape[0] // units, row_step, 0)


def into(target):
    def store(columns, value):
        target[:, columns] = value.astype(target.dtype)

    return store


ROWS = 32


def by_rows(count, step):
    def body(index, carry):
        step(span(index, ROWS))
        return carry

    lax.fori_loop(0, count // ROWS, body, 0)


def norm_forward(total, gains, index, unit, scale, use):
    gain, shift = gains[index : index + 1, :], gains[index + 3 : index + 4, :]

    def step(rows):
        value = total[rows, :]
        centre = value - jnp.mean(value, axis=-1, keepdims=True)
        spread = jnp.mean(centre * centre, axis=-1, keepdims=True)
        root = lax.rsqrt(spread + EPS)
        scaled = centre * root
        unit[rows, :] = scaled
        scale[rows, :] = root
        use(rows, scaled * gain + shift)

    by_rows(total.shape[0], step)


def norm_slope(incoming, scaled, root, gain):
    width = scaled.shape[1]
    scaled_grad = incoming * gain
    first = jnp.mean(scaled_grad, axis=-1, keepdims=True)
    second = jnp.mean(scaled_grad * scaled, axis=-1, keepdims=True)
    value = root * (scaled_grad - first - scaled * second)
    of_gain = jnp.sum((incoming * scaled).reshape(ROWS // 8, 8, width), axis=0)
    of_shift = jnp.sum(incoming.reshape(ROWS // 8, 8, width), axis=0)
    return value, of_gain, of_shift


def keep_small(index, sums, small):
    for offset, partial in ((index, sums[0]), (index + 3, sums[1])):
        line = jnp.sum(partial, axis=0, keepdims=True)
        for group in range(2 * small.shape[1]):
            small[group % 2, group // 2, offset : offset + 1, :] = line[
                :, group * 128 : (group + 1) * 128
            ]


def norm_backward(grad, gains, index, unit, scale, target, target_low, small):
    gain = gains[index : index + 1, :]

    def body(block, sums):
        rows = span(block, ROWS)
        value, of_gain, of_shift = norm_slope(grad[rows, :], unit[rows, :], scale[rows, :], gain)
        target[rows, :] = value
        target_low[rows, :] = value.astype(target_low.dtype)
        return (sums[0] + of_gain, sums[1] + of_shift)

    zero = jnp.zeros((8, unit.shape[1]), jnp.float32)
    keep_small(index, lax.fori_loop(0, unit.shape[0] // ROWS, body, (zero, zero)), small)


def norm_both(total, grad, gains, index, result, target, target_low, small):
    gain, shift = gains[index : index + 1, :], gains[index + 3 : index + 4, :]

    def body(block, sums):
        rows = span(block, ROWS)
        value = total[rows, :]
        centre = value - jnp.mean(value, axis=-1, keepdims=True)
        spread = jnp.mean(centre * centre, axis=-1, keepdims=True)
        root = lax.rsqrt(spread + EPS)
        scaled = centre * root
        result[rows, :] = scaled * gain + shift
        incoming = grad[rows, :].astype(jnp.float32)
        value, of_gain, of_shift = norm_slope(incoming, scaled, root, gain)
        target[rows, :] = value
        target_low[rows, :] = value.astype(target_low.dtype)
        return (sums[0] + of_gain, sums[1] + of_shift)

    zero = jnp.zeros((8, total.shape[1]), jnp.float32)
    keep_small(index, lax.fori_loop(0, total.shape[0] // ROWS, body, (zero, zero)), small)


def lane_masks(dtype, scale):
    low = lax.broadcasted_iota(jnp.int32, (1, 2 * HEAD_DIM), 1) < HEAD_DIM
    first = jnp.where(low, scale, 0.0)
    return first.astype(dtype), (scale - first).astype(dtype)


def turned_pair(eye, rows):
    size = rows.shape[1]
    return dot(eye[0:size, 0:size], rows, TURNED).astype(rows.dtype)


def attention_forward(query, keys, values, bias, blocks, eye, mixed, turned, lse, first, last):
    masks = lane_masks(query.dtype, SCALE)

    def pair_step(pair, carry):
        lanes = span(pair, 2 * HEAD_DIM)
        two_query, two_keys, two_values = query[:, lanes], keys[:, lanes], values[:, lanes]
        columns = []
        for q0, q1, k0, k1 in blocks:
            block_values = turned_pair(eye, two_values[k0:k1])
            rows = []
            for head in range(2):
                scores = dot(two_keys[k0:k1], two_query[q0:q1] * masks[head], TURNED)
                scores = scores + bias[k0:k1, q0:q1]
                top = jnp.max(scores, axis=0, keepdims=True)
                weight = jnp.exp(scores - top)
                norm = jnp.sum(weight, axis=0, keepdims=True)
                head_values = block_values[head * HEAD_DIM : (head + 1) * HEAD_DIM]
                rows.append(dot(head_values, weight.astype(query.dtype)) * (1.0 / norm))
                lse[pair, head : head + 1, q0:q1] = top + jnp.log(norm)
            columns.append(jnp.concatenate(rows, axis=0))
        total = jnp.concatenate(columns, axis=1).astype(mixed.dtype)
        turned[pair % 2, span(pair // 2, 2 * HEAD_DIM), :] = total
        mixed[:, lanes] = dot(eye[...], total, TURNED).astype(mixed.dtype)
        return carry

    lax.fori_loop(first, last, pair_step, 0)


def stacked(parts):
    cuts = sorted({at for first, value in parts for at in (first, first + value.shape[0])})
    found = []
    for low, high in zip(cuts, cuts[1:]):
        total = None
        for first, value in parts:
            if first <= low and high <= first + value.shape[0]:
                piece = value[low - first : high - first]
                total = piece if total is None else total + piece
        found.append(total)
    return jnp.concatenate(found, axis=0)


def attention_backward(
    query, keys, values, bias, blocks, eye, lse, grad, query_grad, key_grad, value_grad, first, last
):
    scaled, masks = lane_masks(query.dtype, SCALE), lane_masks(query.dtype, 1.0)

    def pair_step(pair, carry):
        lanes = span(pair, 2 * HEAD_DIM)
        two_query, two_keys, two_values = query[:, lanes], keys[:, lanes], values[:, lanes]
        two_grad = grad[:, lanes]
        of_query, of_keys, of_values = [], [], []
        for q0, q1, k0, k1 in blocks:
            block_keys, block_values = two_keys[k0:k1], two_values[k0:k1]
            slopes, all_probs, heads_query, heads_grad = [], [], [], []
            for head in range(2):
                head_query = two_query[q0:q1] * scaled[head]
                head_grad = two_grad[q0:q1] * masks[head]
                scores = dot(block_keys, head_query, TURNED) + bias[k0:k1, q0:q1]
                probs = jnp.exp(scores - lse[pair, head : head + 1, q0:q1])
                pulled = dot(block_values, head_grad, TURNED)
                inner = jnp.sum(probs * pulled, axis=0, keepdims=True)
                slopes.append((probs * (pulled - inner)).astype(query.dtype))
                all_probs.append(probs.astype(query.dtype))
                heads_query.append(head_query)
                heads_grad.append(head_grad)
            both = jnp.concatenate(slopes, axis=1)
            of_keys.append((k0, dot(both, jnp.concatenate(heads_query, axis=0))))
            both = jnp.concatenate(all_probs, axis=1)
            of_values.append((k0, dot(both, jnp.concatenate(heads_grad, axis=0))))
            block_turned = turned_pair(eye, block_keys * jnp.asarray(SCALE, query.dtype))
            rows = [
                dot(block_turned[head * HEAD_DIM : (head + 1) * HEAD_DIM], slopes[head])
                for head in range(2)
            ]
            of_query.append(jnp.concatenate(rows, axis=0))
        total = jnp.concatenate(of_query, axis=1).astype(query_grad.dtype)
        query_grad[:, lanes] = dot(eye[...], total, TURNED).astype(query_grad.dtype)
        key_grad[:, lanes] = stacked(of_keys).astype(key_grad.dtype)
        value_grad[:, lanes] = stacked(of_values).astype(value_grad.dtype)
        return carry

    lax.fori_loop(first, last, pair_step, 0)


def turn_blocks(left, eye, store):
    width = eye.shape[0]
    for block in range(left.shape[1] // width):
        columns = pl.ds(block * width, width)
        store(block, dot(eye[...], left[:, columns], TURNED).astype(left.dtype))


def turn_by_lane(left, eye, target):
    group = eye.shape[0] // 2

    def store(block, value):
        target[0, pl.ds(block * group, group), :] = value[:group]
        target[1, pl.ds(block * group, group), :] = value[group:]

    turn_blocks(left, eye, store)


SQUARES = 8


def layer_kernel(places, sizes, *refs):
    n_rows, n_mem, width, ff, shard = sizes
    ref = SimpleNamespace(**jax.tree.map(lambda place: refs[place], places))
    place = Place(n_rows, n_mem)
    many = ff // width
    own_ff = ff // (n_rows * n_mem)
    (
        at_query,
        at_key,
        at_value,
        at_output,
        at_cross_query,
        at_cross_key,
        at_cross_value,
        at_cross_output,
    ) = range(SQUARES)
    full = ref.full
    expand, contract = ref.expand_full, ref.contract_full
    tokens, gains = ref.tokens, ref.gains
    low, turned = SimpleNamespace(**ref.low), SimpleNamespace(**ref.turned)

    order = [
        at_query,
        at_key,
        at_value,
        at_output,
        at_cross_key,
        at_cross_value,
        at_cross_query,
        at_cross_output,
    ]
    pool = ref.pool

    def gather_slot(number):
        return pool.at[pl.ds(number % GATHER_SLOTS * n_rows, n_rows)]

    sources = [ref.squares[index] for index in order]
    sources += [ref.expand.at[:, pl.ds(j * width, width)] for j in range(many)]
    sources += [ref.contract.at[pl.ds(j * shard, shard), :] for j in range(many)]
    stores = [full[index] for index in order] + [expand.at[j] for j in range(many)]
    stores += [contract.at[:, :, j] for j in range(many)]
    parts = [Part(item, gather_slot(n), n % 2) for n, item in enumerate(sources)]
    parts.insert(SMALL_AT, Part(ref.small, ref.small_full, 0, True))
    gather = Gather(place, parts, ref.gather_sems)

    def keep(number):
        return pltpu.make_async_copy(gather_slot(number), stores[number], ref.keep_sem.at[number])

    count = [0]

    def load_slot(number):
        first = pool.shape[0] - (1 + number % SLOTS) * n_rows
        return pool.at[pl.ds(first, n_rows)]

    def load(pieces):
        number = count[0]
        count[0] += 1
        for source, first, rows in pieces:
            target = load_slot(number).at[pl.ds(first, rows)]
            pltpu.make_async_copy(source, target, ref.slot_sem.at[number % SLOTS]).start()
        return number

    def ready(number):
        slot = load_slot(number)
        pltpu.make_async_copy(slot, slot, ref.slot_sem.at[number % SLOTS]).wait()
        return slot

    def contract_rows(j):
        groups = n_rows // many
        return [(contract.at[j * groups + i], i * n_mem, n_mem) for i in range(groups)]

    mem_block = ref.memory.shape[1]
    memory, mem_rows = ref.memory, ref.mem_rows

    def memory_own():
        return pltpu.make_async_copy(
            memory.at[place.mem], mem_rows.at[span(place.mem, mem_block)], ref.mem_sem.at[0]
        )

    def memory_total():
        some = mem_rows.at[pl.ds(0, (n_mem - 1) * mem_block)]
        return remote(some, some, ref.mem_sem.at[1], ref.mem_sem.at[2], place.far(1))

    ref.small[...] = jnp.zeros_like(ref.small)
    for member in range(n_mem):

        @pl.when(place.mem == member)
        def _(member=member):
            lanes = slice(member * shard, (member + 1) * shard)
            ref.small[0:3, lanes] = ref.norm_gains[...].astype(jnp.float32)
            ref.small[3:6, lanes] = ref.norm_shifts[...].astype(jnp.float32)

    place.greet()
    memory_own().start()
    for step in range(1, n_mem):
        remote(
            memory.at[(place.mem + step) % n_mem],
            mem_rows.at[span(place.mem, mem_block)],
            ref.mem_sem.at[1],
            ref.mem_sem.at[2],
            place.far(step),
        ).start()

    actions, whole = [], []
    for part in range(len(parts)):
        found, time = gather.events(part)
        for hop, (at, action) in enumerate(found):
            actions.append((HOP + 10 * part + hop, at, action))
        whole.append(time)
    first_hops = [HOP, HOP + 10]
    for code, _, action in actions:
        if code in first_hops:
            action()
    actions = [item for item in actions if item[0] not in first_hops]

    self_bias, cross_bias, eye = ref.self_bias, ref.cross_bias, ref.eye
    own_row = ref.token_ids[pl.ds(place.mem, 1), :].astype(jnp.float32)
    mem_row = ref.memory_ids[pl.ds(place.mem, 1), :].astype(jnp.float32)
    key_place = lax.broadcasted_iota(jnp.int32, self_bias.shape, 0)
    query_place = lax.broadcasted_iota(jnp.int32, self_bias.shape, 1)
    own_wide = jnp.broadcast_to(own_row, self_bias.shape)
    mem_wide = jnp.broadcast_to(mem_row, (cross_bias.shape[1], cross_bias.shape[0]))
    same = (jnp.transpose(own_wide) == own_wide) & (key_place <= query_place)
    self_bias[...] = jnp.where(same, 0.0, NEG)
    cross_bias[...] = jnp.where(jnp.transpose(mem_wide) == own_row, 0.0, NEG)
    eye_row = lax.broadcasted_iota(jnp.int32, eye.shape, 0)
    eye_column = lax.broadcasted_iota(jnp.int32, eye.shape, 1)
    eye[...] = jnp.where(eye_row == eye_column, 1.0, 0.0).astype(eye.dtype)
    turn_by_lane(tokens, eye, turned.tokens)

    accumulated, other = ref.accumulated, ref.other
    hidden, slope, hidden_turned = ref.hidden, ref.slope, ref.hidden_turned

    def small_piece():
        blocks = ref.small_full
        for group in range(n_rows):
            total = None
            for member in range(n_mem):
                value = blocks[group, member]
                total = value if total is None else total + value
            gains[:, group * 128 : (group + 1) * 128] = total

    def query_piece(slot):
        times(tokens, slot, into(ref.query))

    def key_piece(slot):
        times(tokens, slot, into(ref.keys))

    pairs = width // (2 * HEAD_DIM)
    self_blocks = [
        (first, first + 128, max(first - DOC_LIMIT, 0), first + 128)
        for first in range(0, self_bias.shape[1], 128)
    ]
    cross_blocks = [(0, cross_bias.shape[1], 0, cross_bias.shape[0])]

    def value_piece(slot):
        times(tokens, slot, into(ref.values))

    def self_forward(first, last, slot):
        attention_forward(
            ref.query,
            ref.keys,
            ref.values,
            self_bias,
            self_blocks,
            eye,
            ref.attended,
            turned.attended,
            ref.self_lse,
            first,
            last,
        )

    def output_piece(slot):
        def store(columns, value):
            accumulated[:, columns] = ALPHA * tokens[:, columns].astype(jnp.float32) + value

        times(ref.attended, slot, store)

    def output_norm(slot):
        def use(rows, value):
            ref.first_low[rows, :] = value.astype(jnp.bfloat16)
            other[rows, :] = value

        norm_forward(accumulated, gains, 0, ref.unit1, ref.scale1, use)

    def cross_key_piece(slot):
        memory_own().wait()
        memory_total().wait_recv()
        times(mem_rows, slot, into(ref.cross_keys))
        turn_by_lane(mem_rows, eye, turned.memory)

    def cross_value_piece(slot):
        times(mem_rows, slot, into(ref.cross_values))
        turn_by_lane(ref.first_low, eye, turned.first)

    def cross_query_piece(slot):
        times(ref.first_low, slot, into(ref.cross_query))

    def cross_forward(first, last, slot):
        attention_forward(
            ref.cross_query,
            ref.cross_keys,
            ref.cross_values,
            cross_bias,
            cross_blocks,
            eye,
            ref.crossed,
            turned.crossed,
            ref.cross_lse,
            first,
            last,
        )

    def cross_output_piece(slot):
        def store(columns, value):
            accumulated[:, columns] = ALPHA * other[:, columns] + value

        times(ref.crossed, slot, store)

    def cross_output_norm(slot):
        def use(rows, value):
            ref.second_low[rows, :] = value.astype(jnp.bfloat16)
            other[rows, :] = value

        norm_forward(accumulated, gains, 1, ref.unit2, ref.scale2, use)

    def expand_piece(j, half, slot):
        def store(columns, value):
            there = pl.ds(pl.multiple_of(j * width + columns.start, TILE), columns.size)
            bell = 0.5 * (1.0 + lax.erf(value * math.sqrt(0.5)))
            density = jnp.exp(value * value * -0.5) * (1.0 / math.sqrt(2.0 * math.pi))
            hidden[:, there] = (value * bell).astype(hidden.dtype)
            slope[:, there] = (bell + value * density).astype(slope.dtype)

        times(ref.second_low, slot, store, half, 2)

    def expand_turn(j, slot):
        def keep(block, value):
            for index in range(value.shape[0] // shard):
                first = j * width + block * value.shape[0] + index * shard
                device, job = first // own_ff, first % own_ff // shard
                group, member = device // n_mem, device % n_mem
                at = group // 2 * n_mem * shard + member * shard
                hidden_turned[job, group % 2, at : at + shard, :] = value[
                    index * shard : (index + 1) * shard
                ]

        turn_blocks(hidden.at[:, pl.ds(j * width, width)], eye, keep)

    def contract_piece(j, slot):
        block = 2 * n_mem * shard
        for index in range(n_rows // 2):
            rows = pl.ds(index * n_mem * shard, n_mem * shard)
            both = jnp.concatenate([hidden_turned[j, 0, rows], hidden_turned[j, 1, rows]], axis=0)
            columns = pl.ds(index * block, block)
            low.branch[:, columns] = dot(eye[...], both, TURNED).astype(jnp.bfloat16)

        def store(columns, value):
            if j == 0:
                accumulated[:, columns] = ALPHA * other[:, columns] + value
            else:
                accumulated[:, columns] = accumulated[:, columns] + value

        times(low.branch, slot, store)

    quarters = [(pairs * at // 4, pairs * (at + 1) // 4) for at in range(4)]
    pieces = [
        [query_piece],
        [key_piece],
        [value_piece] + [functools.partial(self_forward, *quarter) for quarter in quarters],
        [output_piece, output_norm],
        [cross_key_piece],
        [cross_value_piece],
        [cross_query_piece] + [functools.partial(cross_forward, *quarter) for quarter in quarters],
        [cross_output_piece, cross_output_norm],
    ]
    for j in range(many):
        halves = [functools.partial(expand_piece, j, half) for half in range(2)]
        pieces.append(halves + [functools.partial(expand_turn, j)])
    pieces += [[functools.partial(contract_piece, j)] for j in range(many)]

    def arrive(part):
        gather.core_total(part).wait_recv()
        if part != SMALL_AT:
            keep(part - (part > SMALL_AT)).start()

    def use(part, index):
        if part == SMALL_AT:
            small_piece()
        else:
            number = part - (part > SMALL_AT)
            pieces[number][index](gather_slot(number))

    def settle(part):
        gather.sent(part)
        if part != SMALL_AT:
            keep(part - (part > SMALL_AT)).wait()

    last = 0.0
    for part, time in enumerate(whole):
        time = max(time, last + 0.5)
        actions.append((ARRIVE + part, time, functools.partial(arrive, part)))
        count_here = 1 if part == SMALL_AT else len(pieces[part - (part > SMALL_AT)])
        for index in range(count_here):
            at = time + 0.2 + 0.04 * index
            actions.append((USE + 10 * part + index, at, functools.partial(use, part, index)))
        actions.append((SETTLE + part, time + 0.45, functools.partial(settle, part)))
        last = time
    for action in planned(actions, FORWARD_PLAN):
        action()
    place.tell(ref.ready_sem)

    backward_sources, loads = [], []
    used = [0]

    def next_slot():
        slot = ready(loads[used[0]])
        used[0] += 1
        if len(loads) < len(backward_sources):
            loads.append(load(backward_sources[len(loads)]))
        return slot

    small_sums = ref.small_sums
    small_sums[...] = jnp.zeros_like(small_sums)
    def inner_piece(j):
        slot = next_slot()

        def store(columns, value):
            there = pl.ds(pl.multiple_of(j * width + columns.start, TILE), columns.size)
            slope[:, there] = (value * slope[:, there].astype(jnp.float32)).astype(slope.dtype)

        times_turned(low.third, slot, store)

    def second_piece(j):
        slot = next_slot()

        def store(columns, value):
            if j == 0:
                other[:, columns] = ALPHA * accumulated[:, columns] + value
            else:
                other[:, columns] = other[:, columns] + value

        times_turned(slope.at[:, pl.ds(j * width, width)], slot, store)

    def second_norm_piece():
        norm_backward(
            other, gains, 1, ref.unit2, ref.scale2, accumulated, low.second, small_sums
        )

    def cross_start_piece():
        times_turned(low.second, next_slot(), into(low.branch))

    def cross_piece(first, last):
        attention_backward(
            ref.cross_query,
            ref.cross_keys,
            ref.cross_values,
            cross_bias,
            cross_blocks,
            eye,
            ref.cross_lse,
            low.branch,
            low.cross_query,
            low.cross_key,
            low.cross_value,
            first,
            last,
        )

    def first_piece():
        def store(columns, value):
            other[:, columns] = ALPHA * accumulated[:, columns] + value

        times_turned(low.cross_query, next_slot(), store)

    def first_norm_piece():
        norm_backward(other, gains, 0, ref.unit1, ref.scale1, accumulated, low.first, small_sums)

    def self_start_piece():
        times_turned(low.first, next_slot(), into(low.branch))

    def self_piece(first, last):
        attention_backward(
            ref.query,
            ref.keys,
            ref.values,
            self_bias,
            self_blocks,
            eye,
            ref.self_lse,
            low.branch,
            low.query,
            low.key,
            low.value,
            first,
            last,
        )

    mem_out, mem_in = ref.mem_out, ref.mem_in

    def grad_own():
        return pltpu.make_async_copy(
            mem_out.at[span(place.mem, mem_block)], mem_in.at[place.mem], ref.mem_sem.at[3]
        )

    def grad_total():
        some = mem_in.at[pl.ds(0, n_mem - 1)]
        return remote(some, some, ref.mem_sem.at[4], ref.mem_sem.at[5], place.far(1))

    def memory_key_piece():
        times_turned(low.cross_key, next_slot(), into(other))

    def memory_value_piece():
        def store(columns, value):
            mem_out[:, columns] = (other[:, columns] + value).astype(mem_out.dtype)

        times_turned(low.cross_value, next_slot(), store)
        grad_own().start()
        for step in range(1, n_mem):
            remote(
                mem_out.at[span((place.mem + step) % n_mem, mem_block)],
                mem_in.at[place.mem],
                ref.mem_sem.at[4],
                ref.mem_sem.at[5],
                place.far(step),
            ).start()

    def input_piece(left, start):
        target = ref.input_grad

        def store(columns, value):
            if start:
                target[:, columns] = ALPHA * accumulated[:, columns] + value
            else:
                target[:, columns] = target[:, columns] + value

        times_turned(left, next_slot(), store)

    def memory_end_piece():
        grad_own().wait()
        grad_total().wait_recv()
        for member in range(n_mem):
            ref.memory_grad[member] = mem_in[member].astype(jnp.float32)

    halves = ((0, width // 2), (width // 2, width // 2))
    grads = ref.grads
    plans = []
    for j in range(many):
        for first, columns in halves if j == 0 else ((0, width),):
            target = ref.contract_grad.at[pl.ds(j * shard, shard), pl.ds(first, columns)]
            plans.append((hidden_turned.at[j], low.third, first, target))
    for j in range(many):
        target = ref.expand_grad.at[:, pl.ds(j * width, width)]
        plans.append((turned.second, slope, j * width, target))
    plans += [
        (turned.crossed, low.second, 0, grads[at_cross_output]),
        (turned.memory, low.cross_key, 0, grads[at_cross_key]),
        (turned.memory, low.cross_value, 0, grads[at_cross_value]),
        (turned.first, low.cross_query, 0, grads[at_cross_query]),
        (turned.attended, low.first, 0, grads[at_output]),
        (small_sums, None, 0, ref.small_total),
        (turned.tokens, low.query, 0, grads[at_query]),
        (turned.tokens, low.key, 0, grads[at_key]),
    ]
    for first, columns in halves:
        target = grads[at_value].at[:, pl.ds(first, columns)]
        plans.append((turned.tokens, low.value, first, target))
    jobs = [Job(*plan) for plan in plans]
    reduce = Reduce(place, jobs, ref.reduce_sems, pool, SimpleNamespace(**ref.little))

    inner = [functools.partial(inner_piece, j) for j in range(many)]
    second = [functools.partial(second_piece, j) for j in range(many)]
    base = many + 1
    def weight(index):
        return [(full[index], 0, n_rows)]

    turn = functools.partial(turn_by_lane, ref.second_low, eye, turned.second)
    crosses = [functools.partial(cross_piece, pair, pair + 1) for pair in range(pairs)]
    selves = [functools.partial(self_piece, pair, pair + 1) for pair in range(pairs)]
    work = [(base - 1.7 + j, inner[j], contract_rows(j)) for j in range(2)]
    work += [(base - 1.3, turn, None)]
    work += [(base - 1.7 + j, inner[j], contract_rows(j)) for j in range(2, many)]
    work += [(base - 0.3 + j, second[j], [(expand.at[j], 0, n_rows)]) for j in range(many)]
    base = 2 * many + 1
    work += [
        (base - 0.2, second_norm_piece, None),
        (base - 0.15, cross_start_piece, weight(at_cross_output)),
    ]
    work += [(base + 0.3 + 0.05 * pair, crosses[pair], None) for pair in range(pairs)]
    work += [
        (base + 1.3, first_piece, weight(at_cross_query)),
        (base + 1.31, first_norm_piece, None),
        (base + 1.7, self_start_piece, weight(at_output)),
    ]
    work += [(base + 2.3 + 0.14 * pair, selves[pair], None) for pair in range(pairs)]
    work += [
        (base + 3.7, memory_key_piece, weight(at_cross_key)),
        (base + 4.3, memory_value_piece, weight(at_cross_value)),
        (base + 4.7, functools.partial(input_piece, low.query, True), weight(at_query)),
        (base + 5.5, functools.partial(input_piece, low.key, False), weight(at_key)),
        (base + 6.5, functools.partial(input_piece, low.value, False), weight(at_value)),
        (base + 8.5, memory_end_piece, None),
    ]
    actions = [(WORK + index, at, item) for index, (at, *item) in enumerate(work)]
    for number in range(len(jobs)):
        found = reduce.events(number)
        actions.append((CORE + number, found[0][0], found[0][1:]))
        actions.append((LANE + number, found[1][0], found[1][1:]))
        for stage, (at, action) in enumerate(found[2:]):
            actions.append((STAGE + 10 * number + stage, at, (action,)))
    ordered = planned(actions, BACKWARD_PLAN)
    backward_sources += [item[1] for item in ordered if len(item) > 1 and item[1] is not None]
    loads += [load(backward_sources[0]), load(backward_sources[1])]
    norm_both(
        accumulated, ref.out_grad, gains, 2, ref.result, accumulated, low.third, small_sums
    )

    place.hear(ref.ready_sem)
    for item in ordered:
        item[0]()

    total = ref.small_total[...]
    own = jnp.zeros((8, shard), jnp.float32)
    for member in range(n_mem):
        here = jnp.where(place.mem == member, 1.0, 0.0)
        own = own + here * total[:, member * shard : (member + 1) * shard]
    ref.gains_grad[...] = own[0:3]
    ref.shifts_grad[...] = own[3:6]
    reduce.finish()
    memory_total().wait_send()
    grad_total().wait_send()


SMALL_AT = 2
DOC_LIMIT = 64
HOP, ARRIVE, USE, SETTLE, CORE, LANE, STAGE, WORK = range(1000, 9000, 1000)
FORWARD_PLAN = ()
BACKWARD_PLAN = ()


def planned(actions, plan):
    codes = {code for code, _, _ in actions}
    if codes == set(plan):
        at = {code: number for number, code in enumerate(plan)}
        return [item for code, _, item in sorted(actions, key=lambda action: at[action[0]])]
    return [item for _, _, item in sorted(actions, key=lambda action: action[1])]


def copy_kernel(count, *refs):
    for source, target in zip(refs[:count], refs[count:]):
        target[...] = source[...]


def copied(values):
    near = pl.BlockSpec(memory_space=pltpu.VMEM)
    return pl.pallas_call(
        functools.partial(copy_kernel, len(values)),
        out_shape=[jax.ShapeDtypeStruct(value.shape, value.dtype) for value in values],
        in_specs=[near] * len(values),
        out_specs=[near] * len(values),
        compiler_params=pltpu.CompilerParams(vmem_limit_bytes=VMEM_LIMIT),
        name="results",
    )(*values)


def fused(n_rows, n_mem, ins):
    tokens, memory, squares = ins["tokens"], ins["memory"], ins["squares"]
    expand, contract = ins["expand"], ins["contract"]
    tokens_here, width = tokens.shape
    ff = expand.shape[1]
    shard = squares[0].shape[0]
    mem_tokens = memory.shape[0] * memory.shape[1]
    digits, half, many = (n_rows // 2).bit_length() - 1, n_rows // 2, ff // width
    pairs = width // (2 * HEAD_DIM)
    low, high = jnp.bfloat16, jnp.float32
    n_parts = 1 + SQUARES + 2 * many
    n_jobs = n_parts + 2
    dma, vmem = pltpu.SemaphoreType.DMA, pltpu.VMEM
    anywhere, near = pl.BlockSpec(memory_space=pl.ANY), pl.BlockSpec(memory_space=pltpu.VMEM)

    far_ins = dict(memory=memory)
    in_specs = {
        name: jax.tree.map(lambda _: anywhere if name in far_ins else near, value)
        for name, value in ins.items()
    }

    def out(shape, dtype=high):
        return jax.ShapeDtypeStruct(shape, dtype)

    outs = dict(
        result=out(tokens.shape),
        input_grad=out(tokens.shape),
        memory_grad=out(memory.shape),
        grads=[out(item.shape) for item in squares],
        expand_grad=out(expand.shape),
        contract_grad=out(contract.shape),
        gains_grad=out((3, shard)),
        shifts_grad=out((3, shard)),
    )
    far_outs = dict(
        full=[out((n_rows, n_mem, shard, width), low)] * SQUARES,
        expand_full=out((many, n_rows, n_mem, shard, width), low),
        contract_full=out((n_rows, n_mem, many, shard, width), low),
    )
    out_specs = jax.tree.map(lambda _: near, outs)
    out_specs.update(jax.tree.map(lambda _: anywhere, far_outs))
    outs.update(far_outs)

    def token_rows(dtype):
        return vmem((tokens_here, width), dtype)

    def memory_rows(dtype):
        return vmem((mem_tokens, width), dtype)

    tiny = (8, 128)

    counts = [half >> (stage + 1) for stage in range(digits)]
    units = (OUT_SLOTS + LANE_SLOTS + CORE_RING) * half + RING
    for stage, number in enumerate(counts):
        units += (SUM_SLOTS + (RING if stage else FIRST_RING)) * number
    units = max(units + SLOTS * n_rows, GATHER_SLOTS * n_rows)
    little = dict(
        lanes=vmem((half,) + tiny, high),
        core_in=vmem((half,) + tiny, high),
        sums=[vmem((number,) + tiny, high) for number in counts],
        arrived=[vmem((number,) + tiny, high) for number in counts]
        + [vmem((n_mem - 1,) + tiny, high)],
    )
    left = vmem((2, width // 2, tokens_here), low)
    scratch = dict(
        small=vmem(tiny, high),
        small_full=vmem((n_rows, n_mem) + tiny, high),
        small_total=vmem(tiny, high),
        pool=vmem((units, n_mem, shard, width), low),
        slot_sem=dma((SLOTS,)),
        keep_sem=dma((n_parts - 1,)),
        ready_sem=pltpu.SemaphoreType.REGULAR,
        mem_sem=dma((6,)),
        gather_sems=[
            dma(shape + (n_parts,))
            for shape in ((), (), (), (digits,), (digits,), (), ())
            + ((2 * (n_mem - 1),), (2 * (n_mem - 1),))
        ],
        reduce_sems=[dma(shape + (n_jobs,)) for shape in ((), (), (digits + 1,), (digits + 1,))],
        gains=vmem((8, width), high),
        query=token_rows(low),
        keys=token_rows(low),
        values=token_rows(low),
        attended=token_rows(low),
        first_low=token_rows(low),
        second_low=token_rows(low),
        cross_query=token_rows(low),
        crossed=token_rows(low),
        cross_keys=memory_rows(low),
        cross_values=memory_rows(low),
        mem_rows=memory_rows(low),
        mem_out=memory_rows(low),
        mem_in=vmem(memory.shape, low),
        unit1=token_rows(high),
        unit2=token_rows(high),
        accumulated=token_rows(high),
        other=token_rows(high),
        scale1=vmem((tokens_here, 1), high),
        scale2=vmem((tokens_here, 1), high),
        self_bias=vmem((tokens_here, tokens_here), high),
        cross_bias=vmem((mem_tokens, tokens_here), high),
        self_lse=vmem((pairs, 2, tokens_here), high),
        cross_lse=vmem((pairs, 2, tokens_here), high),
        eye=vmem((TILE, TILE), low),
        hidden=vmem((tokens_here, ff), low),
        slope=vmem((tokens_here, ff), low),
        hidden_turned=vmem((many, 2, width // 2, tokens_here), low),
        turned=dict(
            tokens=left, attended=left, first=left, memory=left, crossed=left, second=left
        ),
        low=dict(
            third=token_rows(low),
            second=token_rows(low),
            first=token_rows(low),
            branch=token_rows(low),
            cross_query=token_rows(low),
            cross_key=memory_rows(low),
            cross_value=memory_rows(low),
            query=token_rows(low),
            key=token_rows(low),
            value=token_rows(low),
        ),
        small_sums=vmem((2, half) + tiny, high),
        little=little,
    )
    in_values, in_tree = jax.tree.flatten(ins)
    out_shapes, out_tree = jax.tree.flatten(outs)
    scratch_shapes, scratch_tree = jax.tree.flatten(scratch)
    places = jax.tree.unflatten(in_tree, range(len(in_values)))
    at = len(in_values)
    places.update(jax.tree.unflatten(out_tree, range(at, at + len(out_shapes))))
    at += len(out_shapes)
    places.update(jax.tree.unflatten(scratch_tree, range(at, at + len(scratch_shapes))))
    values = pl.pallas_call(
        functools.partial(layer_kernel, places, (n_rows, n_mem, width, ff, shard)),
        out_shape=out_shapes,
        in_specs=jax.tree.leaves(in_specs),
        out_specs=jax.tree.leaves(out_specs),
        scratch_shapes=scratch_shapes,
        compiler_params=pltpu.CompilerParams(
            collective_id=0, has_side_effects=True, vmem_limit_bytes=VMEM_LIMIT
        ),
        name="layer",
    )(*in_values)
    found = jax.tree.unflatten(out_tree, values)
    for name in far_outs:
        del found[name]
    return found


def local(n_rows, n_mem, *args):
    (
        tokens,
        memory,
        token_ids,
        memory_ids,
        out_grad,
        self_query,
        self_key,
        self_value,
        self_output,
        cross_query,
        cross_key,
        cross_value,
        cross_output,
        expand_weight,
        contract_weight,
        norm_gains,
        norm_shifts,
    ) = args
    shard, width = self_query.shape
    suits = width == 128 * n_rows and shard % 16 == 0 and tokens.shape[0] == 1
    suits = suits and tokens.shape[1] == TILE and expand_weight.shape[1] == n_mem * width
    if not suits or n_rows < 4 or n_rows & (n_rows - 1) or n_mem < 2:
        return plain(*args)
    found = fused(
        n_rows,
        n_mem,
        dict(
            tokens=tokens[0],
            memory=memory,
            token_ids=token_ids,
            memory_ids=memory_ids,
            out_grad=out_grad[0],
            squares=[
                self_query,
                self_key,
                self_value,
                self_output,
                cross_query,
                cross_key,
                cross_value,
                cross_output,
            ],
            expand=expand_weight,
            contract=contract_weight,
            norm_gains=norm_gains,
            norm_shifts=norm_shifts,
        ),
    )
    values, tree = jax.tree.flatten(found)
    found = SimpleNamespace(**jax.tree.unflatten(tree, copied(values)))
    return (
        found.result[None],
        found.input_grad[None],
        found.memory_grad,
        *found.grads,
        found.expand_grad,
        found.contract_grad,
        found.gains_grad,
        found.shifts_grad,
    )


def solution(mesh):
    in_specs = (
        P(("rows", "mem"), None, None),
        P("rows", "mem", None),
        P("rows", None),
        P("rows", None),
        P(("rows", "mem"), None, None),
        P(("rows", "mem"), None),
        P(("rows", "mem"), None),
        P(("rows", "mem"), None),
        P(("rows", "mem"), None),
        P(("rows", "mem"), None),
        P(("rows", "mem"), None),
        P(("rows", "mem"), None),
        P(("rows", "mem"), None),
        P(("rows", "mem"), None),
        P(("rows", "mem"), None),
        P(None, ("rows", "mem")),
        P(None, ("rows", "mem")),
    )
    out_specs = (
        P(("rows", "mem"), None, None),
        P(("rows", "mem"), None, None),
        P("rows", "mem", None),
        P(("rows", "mem"), None),
        P(("rows", "mem"), None),
        P(("rows", "mem"), None),
        P(("rows", "mem"), None),
        P(("rows", "mem"), None),
        P(("rows", "mem"), None),
        P(("rows", "mem"), None),
        P(("rows", "mem"), None),
        P(("rows", "mem"), None),
        P(("rows", "mem"), None),
        P(None, ("rows", "mem")),
        P(None, ("rows", "mem")),
    )
    layer = functools.partial(local, mesh.shape["rows"], mesh.shape["mem"])
    return jax.shard_map(layer, mesh=mesh, in_specs=in_specs, out_specs=out_specs, check_vma=False)
```

```python
import functools
import math
from types import SimpleNamespace

import jax
import jax.numpy as jnp
from jax import lax
from jax.experimental import pallas as pl
from jax.experimental.pallas import tpu as pltpu
from jax.sharding import PartitionSpec as P

MESH = pl.DeviceIdType.MESH

HEADS = 16
HEAD_DIM = 64


ALPHA = 4.16
EPS = 1e-05
SCALE = 0.125
NEG = -1e30


def layer_norm(hidden_activation, gain, shift):
    centre = hidden_activation - jnp.mean(hidden_activation, axis=-1, keepdims=True)
    spread = jnp.mean(centre * centre, axis=-1, keepdims=True)
    return centre * lax.rsqrt(spread + EPS) * gain + shift


def gelu_exact(value):
    return jax.nn.gelu(value, approximate=False)


def product(left, right):
    return jnp.dot(left, right, preferred_element_type=jnp.float32)


def split_heads(matrix):
    return matrix.reshape(matrix.shape[0], matrix.shape[1] // HEAD_DIM, HEAD_DIM)


def grouped(matrix):
    return jnp.moveaxis(matrix.reshape(matrix.shape[0], HEADS // 4, 4 * HEAD_DIM), 1, 0)


def ungrouped(stack):
    return jnp.moveaxis(stack, 0, 1).reshape(stack.shape[1], stack.shape[0] * stack.shape[2])


def row_map(function, items):
    return lax.map(lambda entry: function(*entry), items)


def score_block(query, keys, allowed):
    raw = jnp.einsum(
        "khe,qhe->hkq", split_heads(keys), split_heads(query), preferred_element_type=jnp.float32
    )
    return jnp.where(allowed[None], raw * SCALE, NEG)


def attend_probs(query, keys, allowed, lse):
    scores = score_block(query, keys, allowed)
    return jnp.where(allowed[None], jnp.exp(scores - lse[:, None, :]), 0.0)


def attend_forward(query, keys, values, allowed):
    scores = score_block(query, keys, allowed)
    top = jnp.max(scores, axis=1)
    weight = jnp.where(allowed[None], jnp.exp(scores - top[:, None, :]), 0.0)
    total = jnp.sum(weight, axis=1)
    probs = (weight / total[:, None, :]).astype(jnp.bfloat16)
    mixed = jnp.einsum(
        "hkq,khe->qhe", probs, split_heads(values), preferred_element_type=jnp.float32
    )
    return (mixed.reshape(query.shape), top + jnp.log(total))


def value_pull(grad, values):
    return jnp.einsum(
        "qhe,khe->hkq", split_heads(grad), split_heads(values), preferred_element_type=jnp.float32
    )


def score_grads(probs, pulled, inner):
    return (probs * (pulled - inner[:, None, :]) * SCALE).astype(jnp.bfloat16)


def query_from(score_grad, keys, shape):
    moved = jnp.einsum(
        "hkq,khe->qhe", score_grad, split_heads(keys), preferred_element_type=jnp.float32
    )
    return moved.reshape(shape)


def key_from(score_grad, query, shape):
    moved = jnp.einsum(
        "hkq,qhe->khe", score_grad, split_heads(query), preferred_element_type=jnp.float32
    )
    return moved.reshape(shape)


def value_from(probs, grad, values):
    moved = jnp.einsum(
        "hkq,qhe->khe",
        probs.astype(jnp.bfloat16),
        split_heads(grad),
        preferred_element_type=jnp.float32,
    )
    return moved.reshape(values.shape)


def local_forward(query, keys, values, allowed):

    def one_group(items):
        return attend_forward(items[0], items[1], items[2], allowed)

    mixed, lse = lax.map(one_group, (grouped(query), grouped(keys), grouped(values)))
    return (ungrouped(mixed), lse)


def local_backward(query, keys, values, allowed, lse, grad):

    def one_group(items):
        part_query, part_keys, part_values, part_lse, part_grad = items
        probs = attend_probs(part_query, part_keys, allowed, part_lse)
        pulled = value_pull(part_grad, part_values)
        inner = jnp.sum(probs * pulled, axis=1)
        score_grad = score_grads(probs, pulled, inner)
        return (
            query_from(score_grad, part_keys, part_query.shape),
            key_from(score_grad, part_query, part_keys.shape),
            value_from(probs, part_grad, part_values),
        )

    parts = lax.map(one_group, (grouped(query), grouped(keys), grouped(values), lse, grouped(grad)))
    return (ungrouped(parts[0]), ungrouped(parts[1]), ungrouped(parts[2]))


def plain(
    tokens,
    memory,
    token_ids,
    memory_ids,
    out_grad,
    self_query,
    self_key,
    self_value,
    self_output,
    cross_query,
    cross_key,
    cross_value,
    cross_output,
    expand_weight,
    contract_weight,
    norm_gains,
    norm_shifts,
):
    full = (
        lax.all_gather(self_query, ("rows", "mem"), axis=0, tiled=True),
        lax.all_gather(self_key, ("rows", "mem"), axis=0, tiled=True),
        lax.all_gather(self_value, ("rows", "mem"), axis=0, tiled=True),
        lax.all_gather(self_output, ("rows", "mem"), axis=0, tiled=True),
        lax.all_gather(cross_query, ("rows", "mem"), axis=0, tiled=True),
        lax.all_gather(cross_key, ("rows", "mem"), axis=0, tiled=True),
        lax.all_gather(cross_value, ("rows", "mem"), axis=0, tiled=True),
        lax.all_gather(cross_output, ("rows", "mem"), axis=0, tiled=True),
        lax.all_gather(expand_weight, ("rows", "mem"), axis=0, tiled=True),
        lax.all_gather(contract_weight, ("rows", "mem"), axis=0, tiled=True),
        lax.all_gather(jnp.transpose(norm_gains), ("rows", "mem"), axis=0, tiled=True),
        lax.all_gather(jnp.transpose(norm_shifts), ("rows", "mem"), axis=0, tiled=True),
    )
    (
        self_attention_query,
        decoder_match_label,
        self_attention_value,
        self_attention_output,
        encoder_lookup_probe,
        key_cross,
        value_cross,
        cross_attention_output,
        up_projection,
        narrowing_matrix,
        gain_cols,
        shift_cols,
    ) = full
    gain_rows = jnp.transpose(gain_cols).astype(jnp.float32)
    shift_rows = jnp.transpose(shift_cols).astype(jnp.float32)
    rows_here = tokens.shape[0]
    member = lax.axis_index("mem")
    own_ids = lax.dynamic_slice_in_dim(token_ids, member * rows_here, rows_here, 0)
    positions = jnp.arange(tokens.shape[1], dtype=jnp.int32)
    self_allowed = (own_ids[:, :, None] == own_ids[:, None, :]) & (
        positions[:, None] <= positions[None, :]
    )[None]
    query = product(tokens, self_attention_query).astype(jnp.bfloat16)
    keys = product(tokens, decoder_match_label).astype(jnp.bfloat16)
    values = product(tokens, self_attention_value).astype(jnp.bfloat16)
    self_mixed, self_lse = row_map(local_forward, (query, keys, values, self_allowed))
    attention_result = self_mixed.astype(jnp.bfloat16)
    first, first_back = jax.vjp(
        layer_norm,
        ALPHA * tokens.astype(jnp.float32) + product(attention_result, self_attention_output),
        gain_rows[0],
        shift_rows[0],
    )
    first_reduced = first.astype(jnp.bfloat16)
    cross_queries = product(first_reduced, encoder_lookup_probe).astype(jnp.bfloat16)
    memory_rows = lax.all_to_all(memory, "mem", split_axis=0, concat_axis=1, tiled=True)
    row_ids = lax.dynamic_slice_in_dim(memory_ids, member * rows_here, rows_here, 0)
    cross_allowed = row_ids[:, :, None] == own_ids[:, None, :]
    cross_keys = product(memory_rows, key_cross).astype(jnp.bfloat16)
    cross_values = product(memory_rows, value_cross).astype(jnp.bfloat16)
    cross_mixed, cross_lse = row_map(
        local_forward, (cross_queries, cross_keys, cross_values, cross_allowed)
    )
    cross_attention_result = cross_mixed.astype(jnp.bfloat16)
    second, second_back = jax.vjp(
        layer_norm,
        ALPHA * first + product(cross_attention_result, cross_attention_output),
        gain_rows[1],
        shift_rows[1],
    )
    second_reduced = second.astype(jnp.bfloat16)
    hidden_value, gelu_back = jax.vjp(gelu_exact, product(second_reduced, up_projection))
    hidden_activation = hidden_value.astype(jnp.bfloat16)
    result, third_back = jax.vjp(
        layer_norm,
        ALPHA * second + product(hidden_activation, narrowing_matrix),
        gain_rows[2],
        shift_rows[2],
    )
    third_grad, gain_three, shift_three = third_back(out_grad.astype(jnp.float32))
    feedforward_gradient = third_grad.astype(jnp.bfloat16)
    down_projection_gradient = jnp.einsum(
        "ehj,ehc->jc", hidden_activation, feedforward_gradient, preferred_element_type=jnp.float32
    )
    (inner_grad,) = gelu_back(
        jnp.einsum(
            "hpu,ku->hpk",
            feedforward_gradient,
            narrowing_matrix,
            preferred_element_type=jnp.float32,
        )
    )
    inner_reduced = inner_grad.astype(jnp.bfloat16)
    expand_grad = jnp.einsum(
        "iqg,iqe->ge", second_reduced, inner_reduced, preferred_element_type=jnp.float32
    )
    second_total = ALPHA * third_grad + jnp.einsum(
        "iwm,fm->iwf", inner_reduced, up_projection, preferred_element_type=jnp.float32
    )
    second_grad, gain_two, shift_two = second_back(second_total)
    cross_branch_gradient = second_grad.astype(jnp.bfloat16)
    output_cross_grad = jnp.einsum(
        "nhb,nhc->bc",
        cross_attention_result,
        cross_branch_gradient,
        preferred_element_type=jnp.float32,
    )
    crossed_grad = jnp.einsum(
        "qwp,up->qwu",
        cross_branch_gradient,
        cross_attention_output,
        preferred_element_type=jnp.float32,
    ).astype(jnp.bfloat16)
    query_grads, key_grads, value_grads = row_map(
        local_backward,
        (cross_queries, cross_keys, cross_values, cross_allowed, cross_lse, crossed_grad),
    )
    key_low = key_grads.astype(jnp.bfloat16)
    value_low = value_grads.astype(jnp.bfloat16)
    row_grad = jnp.einsum(
        "sme,de->smd", key_low, key_cross, preferred_element_type=jnp.float32
    ) + jnp.einsum("sme,de->smd", value_low, value_cross, preferred_element_type=jnp.float32)
    key_cross_grad = jnp.einsum(
        "smd,sme->de", memory_rows, key_low, preferred_element_type=jnp.float32
    )
    value_cross_grad = jnp.einsum(
        "smd,sme->de", memory_rows, value_low, preferred_element_type=jnp.float32
    )
    memory_grad = lax.all_to_all(
        row_grad.astype(jnp.bfloat16), "mem", split_axis=1, concat_axis=0, tiled=True
    ).astype(row_grad.dtype)
    probe_lowered_precision = query_grads.astype(jnp.bfloat16)
    query_cross_grad = jnp.einsum(
        "nhb,nhc->bc", first_reduced, probe_lowered_precision, preferred_element_type=jnp.float32
    )
    first_total = ALPHA * second_grad + jnp.einsum(
        "qwp,up->qwu",
        probe_lowered_precision,
        encoder_lookup_probe,
        preferred_element_type=jnp.float32,
    )
    first_grad, gain_one, shift_one = first_back(first_total)
    self_branch_gradient = first_grad.astype(jnp.bfloat16)
    output_self_grad = jnp.einsum(
        "nhb,nhc->bc", attention_result, self_branch_gradient, preferred_element_type=jnp.float32
    )
    attended_grad = jnp.einsum(
        "qwp,up->qwu",
        self_branch_gradient,
        self_attention_output,
        preferred_element_type=jnp.float32,
    ).astype(jnp.bfloat16)
    self_query_reduced, decoder_label_lowered, self_value_reduced = row_map(
        local_backward, (query, keys, values, self_allowed, self_lse, attended_grad)
    )
    self_query_reduced = self_query_reduced.astype(jnp.bfloat16)
    decoder_label_lowered = decoder_label_lowered.astype(jnp.bfloat16)
    self_value_reduced = self_value_reduced.astype(jnp.bfloat16)
    query_self_grad = jnp.einsum(
        "nhb,nhc->bc", tokens, self_query_reduced, preferred_element_type=jnp.float32
    )
    key_self_grad = jnp.einsum(
        "nhb,nhc->bc", tokens, decoder_label_lowered, preferred_element_type=jnp.float32
    )
    value_self_grad = jnp.einsum(
        "nhb,nhc->bc", tokens, self_value_reduced, preferred_element_type=jnp.float32
    )
    input_grad = (
        ALPHA * first_grad
        + jnp.einsum(
            "qwp,up->qwu",
            self_query_reduced,
            self_attention_query,
            preferred_element_type=jnp.float32,
        )
        + jnp.einsum(
            "qwp,up->qwu",
            decoder_label_lowered,
            decoder_match_label,
            preferred_element_type=jnp.float32,
        )
        + jnp.einsum(
            "qwp,up->qwu",
            self_value_reduced,
            self_attention_value,
            preferred_element_type=jnp.float32,
        )
    )
    gain_grad = jnp.stack([gain_one, gain_two, gain_three], axis=1)
    shift_grad = jnp.stack([shift_one, shift_two, shift_three], axis=1)
    sums = (
        lax.psum_scatter(query_self_grad, ("rows", "mem"), scatter_dimension=0, tiled=True),
        lax.psum_scatter(key_self_grad, ("rows", "mem"), scatter_dimension=0, tiled=True),
        lax.psum_scatter(value_self_grad, ("rows", "mem"), scatter_dimension=0, tiled=True),
        lax.psum_scatter(output_self_grad, ("rows", "mem"), scatter_dimension=0, tiled=True),
        lax.psum_scatter(query_cross_grad, ("rows", "mem"), scatter_dimension=0, tiled=True),
        lax.psum_scatter(key_cross_grad, ("rows", "mem"), scatter_dimension=0, tiled=True),
        lax.psum_scatter(value_cross_grad, ("rows", "mem"), scatter_dimension=0, tiled=True),
        lax.psum_scatter(output_cross_grad, ("rows", "mem"), scatter_dimension=0, tiled=True),
        lax.psum_scatter(expand_grad, ("rows", "mem"), scatter_dimension=0, tiled=True),
        lax.psum_scatter(
            down_projection_gradient, ("rows", "mem"), scatter_dimension=0, tiled=True
        ),
        lax.psum_scatter(gain_grad, ("rows", "mem"), scatter_dimension=0, tiled=True),
        lax.psum_scatter(shift_grad, ("rows", "mem"), scatter_dimension=0, tiled=True),
    )
    return (
        result,
        input_grad,
        memory_grad,
        sums[0],
        sums[1],
        sums[2],
        sums[3],
        sums[4],
        sums[5],
        sums[6],
        sums[7],
        sums[8],
        sums[9],
        jnp.transpose(sums[10]),
        jnp.transpose(sums[11]),
    )


ALL = slice(None)
TILE = 256
SLOTS = 3
GATHER_SLOTS = 9
VMEM_LIMIT = 61 * 1024 * 1024


def flip(index, unit):
    return index + unit * (1 - 2 * ((index // unit) % 2))


def span(index, size):
    return pl.ds(pl.multiple_of(index * size, size), size)


class Place:
    def __init__(self, n_rows, n_mem):
        self.n_rows, self.n_mem = n_rows, n_mem
        self.digits = (n_rows // 2).bit_length() - 1
        self.row = lax.axis_index("rows")
        self.mem = lax.axis_index("mem")
        self.lane = self.row % 2

    def turn(self, index, stage):
        rising, falling = 2 << stage, 2 << (self.digits - 1 - stage)
        return flip(index, rising) * (1 - self.lane) + flip(index, falling) * self.lane

    def sibling(self):
        return (flip(self.row, 1), self.mem)

    def partner(self, stage):
        return (self.turn(self.row, stage), self.mem)

    def far(self, step):
        return (self.row, (self.mem + step) % self.n_mem)

    def others(self):
        found = [self.far(step) for step in range(1, self.n_mem)]
        found += [self.partner(stage) for stage in range(self.digits)]
        return found + [self.sibling()]

    def tell(self, semaphore):
        for other in self.others():
            pl.semaphore_signal(semaphore, inc=1, device_id=other, device_id_type=MESH)

    def hear(self, semaphore):
        pl.semaphore_wait(semaphore, len(self.others()))

    def greet(self):
        self.tell(pltpu.get_barrier_semaphore())
        self.hear(pltpu.get_barrier_semaphore())


def remote(source, target, send_sem, recv_sem, device):
    return pltpu.make_async_remote_copy(
        src_ref=source,
        dst_ref=target,
        send_sem=send_sem,
        recv_sem=recv_sem,
        device_id=device,
        device_id_type=MESH,
    )


def waits(total):
    return (lambda: total().wait_recv(), lambda: total().wait_send())


class Part:
    def __init__(self, source, target, near=0, straight=False):
        self.source, self.target = source, target
        self.near, self.straight = near, straight


class Gather:
    def __init__(self, place, parts, sems):
        self.place, self.parts = place, parts
        (
            self.own_sem,
            self.far_send,
            self.far_recv,
            self.plane_send,
            self.plane_recv,
            self.core_send,
            self.core_recv,
            self.line_send,
            self.line_recv,
        ) = sems

    def group(self, number, group):
        return self.parts[number].target.at[group]

    def one(self, number, group, member):
        return self.parts[number].target.at[group, member]

    def shard(self, number):
        return self.parts[number].source

    def mine(self, number):
        return self.one(number, self.place.row, self.place.mem)

    def own(self, number):
        return pltpu.make_async_copy(self.shard(number), self.mine(number), self.own_sem.at[number])

    def held(self, stage):
        groups = [self.place.row]
        for before in range(stage):
            groups = groups + [self.place.turn(group, before) for group in groups]
        return groups

    def far_total(self, number):
        part = self.parts[number]
        some = part.target.at[pl.ds(0, 1 << part.near), pl.ds(0, self.place.n_mem - 1)]
        return remote(
            some, some, self.far_send.at[number], self.far_recv.at[number], self.place.far(1)
        )

    def far_hop(self, number, first):
        place = self.place
        for group in self.held(self.parts[number].near):
            target = self.one(number, group, place.mem)
            source = self.shard(number) if first else target
            for step in range(1, place.n_mem):
                remote(
                    source,
                    target,
                    self.far_send.at[number],
                    self.far_recv.at[number],
                    place.far(step),
                ).start()

    def sides(self, step):
        mem, n_mem = self.place.mem, self.place.n_mem
        return (
            ((mem - step >= 0) & (mem + 1 < n_mem), mem - step, 1, mem - 1 - step >= 0),
            ((mem + step < n_mem) & (mem >= 1), mem + step, n_mem - 1, mem + 1 + step < n_mem),
        )

    def line_total(self, number, step, side):
        part, at = self.parts[number], 2 * step + side
        some = part.target.at[pl.ds(0, 1 << part.near), 0]
        sems = (self.line_send.at[at, number], self.line_recv.at[at, number])
        return remote(some, some, *sems, self.place.far(1))

    def line_arrived(self, number, step):
        for side, (_, _, _, receives) in enumerate(self.sides(step)):

            @pl.when(receives)
            def _(side=side):
                self.line_total(number, step, side).wait_recv()

    def line_sent(self, number, step):
        for side, (sends, _, _, _) in enumerate(self.sides(step)):

            @pl.when(sends)
            def _(side=side):
                self.line_total(number, step, side).wait_send()

    def line_hop(self, number, step, first):
        place = self.place
        for side, (sends, member, towards, _) in enumerate(self.sides(step)):
            member = (member + place.n_mem) % place.n_mem

            @pl.when(sends)
            def _(side=side, member=member, towards=towards):
                for group in self.held(self.parts[number].near):
                    target = self.one(number, group, member)
                    remote(
                        self.shard(number) if first else target,
                        target,
                        self.line_send.at[2 * step + side, number],
                        self.line_recv.at[2 * step + side, number],
                        place.far(towards),
                    ).start()

    def plane_total(self, number, stage):
        part = self.parts[number]
        some = part.target.at[pl.ds(0, 1 << stage)]
        if stage < part.near:
            some = part.target.at[pl.ds(0, 1 << stage), 0]
        return remote(
            some,
            some,
            self.plane_send.at[stage, number],
            self.plane_recv.at[stage, number],
            self.place.partner(stage),
        )

    def plane_hop(self, number, stage, first):
        for group in self.held(stage):
            if stage < self.parts[number].near:
                target = self.one(number, group, self.place.mem)
            else:
                target = self.group(number, group)
            remote(
                self.shard(number) if first else target,
                target,
                self.plane_send.at[stage, number],
                self.plane_recv.at[stage, number],
                self.place.partner(stage),
            ).start()

    def core_total(self, number):
        some = self.parts[number].target.at[pl.ds(0, self.place.n_rows // 2)]
        return remote(
            some, some, self.core_send.at[number], self.core_recv.at[number], self.place.sibling()
        )

    def core_hop(self, number, first):
        for group in self.held(self.place.digits):
            block = self.group(number, group)
            remote(
                block,
                block,
                self.core_send.at[number],
                self.core_recv.at[number],
                self.place.sibling(),
            ).start()

    def hops(self, number):
        part, take = self.parts[number], functools.partial
        along = []
        if part.straight:
            along.append((1.6, take(self.far_hop, number)) + waits(take(self.far_total, number)))
        else:
            for step in range(self.place.n_mem - 1):
                along.append(
                    (
                        0.55 if step else 1.4,
                        take(self.line_hop, number, step),
                        take(self.line_arrived, number, step),
                        take(self.line_sent, number, step),
                    )
                )
        plane = []
        for stage in range(self.place.digits):
            total = take(self.plane_total, number, stage)
            plane.append((1.5, take(self.plane_hop, number, stage)) + waits(total))
        core = (1.5, take(self.core_hop, number)) + waits(take(self.core_total, number))
        return plane[: part.near] + along + plane[part.near :] + [core]

    def events(self, number):
        hops = self.hops(number)
        time, found = float(number), []

        def act(at):
            if at == 0:
                self.own(number).start()
            else:
                if at == 1:
                    self.own(number).wait()
                hops[at - 1][2]()
            hops[at][1](at == 0)

        for at in range(len(hops)):
            time += hops[at][0] if at else 0.0
            found.append((time, functools.partial(act, at)))
        return found, time + 0.9

    def sent(self, number):
        for hop in self.hops(number):
            hop[3]()


class Job:
    def __init__(self, left, right, first, target):
        self.left, self.right, self.first, self.target = left, right, first, target
        self.small = right is None
        self.width = target.shape[-1]
        self.large = 0


OUT_SLOTS, LANE_SLOTS, SUM_SLOTS, CORE_RING, FIRST_RING, RING = 2, 3, 2, 2, 6, 4


class Reduce:
    def __init__(self, place, jobs, sems, pool, small):
        self.place, self.jobs, self.small = place, jobs, small
        self.core_send, self.core_recv, self.stage_send, self.stage_recv = sems
        wanted = [place.row]
        for stage in reversed(range(place.digits)):
            wanted = wanted + [place.turn(group, stage) for group in wanted]
        self.wanted = [group // 2 for group in wanted]
        for number, job in enumerate(job for job in jobs if not job.small):
            job.large = number
        used, half = [0], place.n_rows // 2

        def take(count, units):
            first = used[0]
            used[0] += count * units
            return [pool.at[pl.ds(first + i * units, units)] for i in range(count)]

        self.outs = take(OUT_SLOTS, half)
        self.lane_slots = take(LANE_SLOTS, half)
        self.core_ring = take(CORE_RING, half)
        self.sum_slots, self.rings = [], []
        for stage in range(place.digits):
            self.sum_slots.append(take(SUM_SLOTS, self.count(stage)))
            self.rings.append(take(RING if stage else FIRST_RING, self.count(stage)))
        self.rings.append(take(RING, 1))
        self.used = used[0]

    def count(self, stage):
        return max(self.place.n_rows // 4 >> stage, 1)

    def cut(self, ref, job):
        return ref if job.width == ref.shape[-1] else ref.at[:, :, :, pl.ds(0, job.width)]

    def out(self, job):
        return self.cut(self.outs[job.large % OUT_SLOTS], job)

    def lanes(self, job):
        if job.small:
            return self.small.lanes
        return self.cut(self.lane_slots[job.large % LANE_SLOTS], job)

    def core_in(self, job):
        if job.small:
            return self.small.core_in
        return self.cut(self.core_ring[job.large % CORE_RING], job)

    def sums(self, job, stage):
        if job.small:
            return self.small.sums[stage]
        return self.cut(self.sum_slots[stage][job.large % SUM_SLOTS], job)

    def arrived(self, job, stage):
        if job.small:
            return self.small.arrived[stage]
        ring = self.rings[stage]
        units = self.cut(ring[job.large % len(ring)], job)
        if stage == self.place.digits:
            return units.at[0, pl.ds(0, self.place.n_mem - 1)]
        return units

    def previous(self, number, distance):
        found = [n for n in range(number) if not self.jobs[n].small]
        if self.jobs[number].small or len(found) < distance:
            return None
        return found[-distance]

    def core_copy(self, number):
        job = self.jobs[number]
        source = job.left.at[1 - self.place.lane] if job.small else self.out(job)
        return remote(
            source,
            self.core_in(job),
            self.core_send.at[number],
            self.core_recv.at[number],
            self.place.sibling(),
        )

    def product(self, job, side, store):
        half = self.place.n_rows // 2
        group = job.left.shape[1] // half
        width = min(TILE, job.width)
        unit = (self.place.n_mem, group // self.place.n_mem, width)

        def column_step(step, carry):
            source = pl.ds(pl.multiple_of(job.first + step * width, width), width)
            value = dot(job.left[side], job.right[:, source])
            for index in range(half):
                block = value[index * group : (index + 1) * group].reshape(unit)
                store(index, span(step, width), block)
            return carry

        lax.fori_loop(0, job.width // width, column_step, 0)

    def core_stage(self, number):
        job = self.jobs[number]
        if not job.small:
            before = self.previous(number, OUT_SLOTS)
            if before is not None:
                self.core_copy(before).wait_send()
            out = self.out(job)

            def store(index, columns, value):
                out[index, :, :, columns] = value.astype(out.dtype)

            self.product(job, 1 - self.place.lane, store)
        self.core_copy(number).start()

    def lane_stage(self, number):
        job = self.jobs[number]
        before = self.previous(number, LANE_SLOTS)
        if before is not None:
            self.total(before, 0).wait_send()
        lanes, arrived = self.lanes(job), self.core_in(job)
        self.core_copy(number).wait_recv()
        if job.small:
            lanes[...] = job.left[self.place.lane] + arrived[...]
        else:

            def store(index, columns, value):
                total = value + arrived[index, :, :, columns].astype(jnp.float32)
                lanes[index, :, :, columns] = total.astype(lanes.dtype)

            self.product(job, self.place.lane, store)
        self.send(number, 0)

    def unit(self, job, stage, index):
        if stage == 0:
            return self.lanes(job).at[self.wanted[index]]
        return self.sums(job, stage - 1).at[index]

    def piece(self, job, unit, member):
        return unit if job.small else unit.at[member]

    def send(self, number, stage):
        job, place = self.jobs[number], self.place
        arrived = self.arrived(job, stage)
        sems = (self.stage_send.at[stage, number], self.stage_recv.at[stage, number])
        if stage == place.digits:
            unit = self.unit(job, stage, 0)
            for step in range(1, place.n_mem):
                source = self.piece(job, unit, (place.mem + step) % place.n_mem)
                remote(source, arrived.at[step - 1], *sems, place.far(step)).start()
            return
        left = self.count(stage)
        for index in range(left):
            source = self.unit(job, stage, left + index)
            remote(source, arrived.at[index], *sems, place.partner(stage)).start()

    def total(self, number, stage):
        some = self.arrived(self.jobs[number], stage)
        sems = (self.stage_send.at[stage, number], self.stage_recv.at[stage, number])
        return remote(some, some, *sems, self.place.far(1))

    def stage(self, number, stage):
        job, place = self.jobs[number], self.place
        arrived = self.arrived(job, stage)
        if stage == place.digits:
            self.total(number, stage).wait_recv()
            value = self.piece(job, self.unit(job, stage, 0), place.mem)[...].astype(jnp.float32)
            for step in range(place.n_mem - 1):
                value = value + arrived[step].astype(jnp.float32)
            job.target[...] = value
            return
        before = self.previous(number, SUM_SLOTS)
        if before is not None:
            self.total(before, stage + 1).wait_send()
        self.total(number, stage).wait_recv()
        sums = self.sums(job, stage)
        for index in range(self.count(stage)):
            unit, coming, target = self.unit(job, stage, index), arrived.at[index], sums.at[index]
            if job.small:
                target[...] = unit[...] + coming[...]
                continue

            def add(member, carry, unit=unit, coming=coming, target=target):
                value = unit[member].astype(jnp.float32) + coming[member].astype(jnp.float32)
                target[member] = value.astype(target.dtype)
                return carry

            lax.fori_loop(0, place.n_mem, add, 0)
        self.send(number, stage + 1)

    def events(self, number):
        found = [(0.0, functools.partial(self.core_stage, number))]
        found.append((0.9, functools.partial(self.lane_stage, number)))
        time = 2.2 if number < 2 else 3.2
        for stage in range(self.place.digits + 1):
            found.append((time, functools.partial(self.stage, number, stage)))
            time += 1.4
        found[-1] = (found[-1][0] - 0.3, found[-1][1])
        return [(number + time, action) for time, action in found]

    def finish(self):
        n_jobs, last = len(self.jobs), self.place.digits
        out = {self.previous(number, OUT_SLOTS) for number in range(n_jobs)}
        lanes = {self.previous(number, LANE_SLOTS) for number in range(n_jobs)}
        sums = {self.previous(number, SUM_SLOTS) for number in range(n_jobs)}
        for number in range(n_jobs):
            if number not in out:
                self.core_copy(number).wait_send()
            if number not in lanes:
                self.total(number, 0).wait_send()
            if number not in sums:
                for stage in range(1, last + 1):
                    self.total(number, stage).wait_send()


NORMAL = (((1,), (0,)), ((), ()))
TURNED = (((1,), (1,)), ((), ()))
LEFT_TURNED = (((0,), (0,)), ((), ()))


def dot(left, right, dims=NORMAL):
    return lax.dot_general(left, right, dims, preferred_element_type=jnp.float32)


def times(left, weight, store, part=0, parts=1):
    size = weight.shape[-1]
    width = min(TILE, size)
    tiles = size // width // parts

    def column_step(step, carry):
        columns = span(step, width)
        store(columns, dot(left[...], weight[:, :, :, columns].reshape(-1, width)))
        return carry

    lax.fori_loop(part * tiles, (part + 1) * tiles, column_step, 0)


def times_turned(left, weight, store):
    unit = weight.shape[1] * weight.shape[2]
    units = max(TILE // unit, 1)

    def row_step(step, carry):
        rows = weight[span(step, units)].reshape(units * unit, weight.shape[-1])
        store(span(step, units * unit), dot(left[...], rows, TURNED))
        return carry

    lax.fori_loop(0, weight.shape[0] // units, row_step, 0)


def into(target):
    def store(columns, value):
        target[:, columns] = value.astype(target.dtype)

    return store


ROWS = 32


def by_rows(count, step):
    def body(index, carry):
        step(span(index, ROWS))
        return carry

    lax.fori_loop(0, count // ROWS, body, 0)


def norm_forward(total, gains, index, unit, scale, use):
    gain, shift = gains[index : index + 1, :], gains[index + 3 : index + 4, :]

    def step(rows):
        value = total[rows, :]
        centre = value - jnp.mean(value, axis=-1, keepdims=True)
        spread = jnp.mean(centre * centre, axis=-1, keepdims=True)
        root = lax.rsqrt(spread + EPS)
        scaled = centre * root
        unit[rows, :] = scaled
        scale[rows, :] = root
        use(rows, scaled * gain + shift)

    by_rows(total.shape[0], step)


def norm_slope(incoming, scaled, root, gain):
    width = scaled.shape[1]
    scaled_grad = incoming * gain
    first = jnp.mean(scaled_grad, axis=-1, keepdims=True)
    second = jnp.mean(scaled_grad * scaled, axis=-1, keepdims=True)
    value = root * (scaled_grad - first - scaled * second)
    of_gain = jnp.sum((incoming * scaled).reshape(ROWS // 8, 8, width), axis=0)
    of_shift = jnp.sum(incoming.reshape(ROWS // 8, 8, width), axis=0)
    return value, of_gain, of_shift


def keep_small(index, sums, small):
    for offset, partial in ((index, sums[0]), (index + 3, sums[1])):
        line = jnp.sum(partial, axis=0, keepdims=True)
        for group in range(2 * small.shape[1]):
            small[group % 2, group // 2, offset : offset + 1, :] = line[
                :, group * 128 : (group + 1) * 128
            ]


def norm_backward(grad, gains, index, unit, scale, target, target_low, small):
    gain = gains[index : index + 1, :]

    def body(block, sums):
        rows = span(block, ROWS)
        value, of_gain, of_shift = norm_slope(grad[rows, :], unit[rows, :], scale[rows, :], gain)
        target[rows, :] = value
        target_low[rows, :] = value.astype(target_low.dtype)
        return (sums[0] + of_gain, sums[1] + of_shift)

    zero = jnp.zeros((8, unit.shape[1]), jnp.float32)
    keep_small(index, lax.fori_loop(0, unit.shape[0] // ROWS, body, (zero, zero)), small)


def norm_both(total, grad, gains, index, result, target, target_low, small):
    gain, shift = gains[index : index + 1, :], gains[index + 3 : index + 4, :]

    def body(block, sums):
        rows = span(block, ROWS)
        value = total[rows, :]
        centre = value - jnp.mean(value, axis=-1, keepdims=True)
        spread = jnp.mean(centre * centre, axis=-1, keepdims=True)
        root = lax.rsqrt(spread + EPS)
        scaled = centre * root
        result[rows, :] = scaled * gain + shift
        incoming = grad[rows, :].astype(jnp.float32)
        value, of_gain, of_shift = norm_slope(incoming, scaled, root, gain)
        target[rows, :] = value
        target_low[rows, :] = value.astype(target_low.dtype)
        return (sums[0] + of_gain, sums[1] + of_shift)

    zero = jnp.zeros((8, total.shape[1]), jnp.float32)
    keep_small(index, lax.fori_loop(0, total.shape[0] // ROWS, body, (zero, zero)), small)


def lane_masks(dtype, scale):
    low = lax.broadcasted_iota(jnp.int32, (1, 2 * HEAD_DIM), 1) < HEAD_DIM
    first = jnp.where(low, scale, 0.0)
    return first.astype(dtype), (scale - first).astype(dtype)


def turned_pair(eye, rows):
    size = rows.shape[1]
    return dot(eye[0:size, 0:size], rows, TURNED).astype(rows.dtype)


def attention_forward(query, keys, values, bias, blocks, eye, mixed, turned, lse, first, last):
    masks = lane_masks(query.dtype, SCALE)

    def pair_step(pair, carry):
        lanes = span(pair, 2 * HEAD_DIM)
        two_query, two_keys, two_values = query[:, lanes], keys[:, lanes], values[:, lanes]
        columns = []
        for q0, q1, k0, k1 in blocks:
            block_values = turned_pair(eye, two_values[k0:k1])
            rows = []
            for head in range(2):
                scores = dot(two_keys[k0:k1], two_query[q0:q1] * masks[head], TURNED)
                scores = scores + bias[k0:k1, q0:q1]
                top = jnp.max(scores, axis=0, keepdims=True)
                weight = jnp.exp(scores - top)
                norm = jnp.sum(weight, axis=0, keepdims=True)
                head_values = block_values[head * HEAD_DIM : (head + 1) * HEAD_DIM]
                rows.append(dot(head_values, weight.astype(query.dtype)) * (1.0 / norm))
                lse[pair, head : head + 1, q0:q1] = top + jnp.log(norm)
            columns.append(jnp.concatenate(rows, axis=0))
        total = jnp.concatenate(columns, axis=1).astype(mixed.dtype)
        turned[pair % 2, span(pair // 2, 2 * HEAD_DIM), :] = total
        mixed[:, lanes] = dot(eye[...], total, TURNED).astype(mixed.dtype)
        return carry

    lax.fori_loop(first, last, pair_step, 0)


def stacked(parts):
    cuts = sorted({at for first, value in parts for at in (first, first + value.shape[0])})
    found = []
    for low, high in zip(cuts, cuts[1:]):
        total = None
        for first, value in parts:
            if first <= low and high <= first + value.shape[0]:
                piece = value[low - first : high - first]
                total = piece if total is None else total + piece
        found.append(total)
    return jnp.concatenate(found, axis=0)


def attention_backward(
    query, keys, values, bias, blocks, eye, lse, grad, query_grad, key_grad, value_grad, first, last
):
    scaled, masks = lane_masks(query.dtype, SCALE), lane_masks(query.dtype, 1.0)

    def pair_step(pair, carry):
        lanes = span(pair, 2 * HEAD_DIM)
        two_query, two_keys, two_values = query[:, lanes], keys[:, lanes], values[:, lanes]
        two_grad = grad[:, lanes]
        of_query, of_keys, of_values = [], [], []
        for q0, q1, k0, k1 in blocks:
            block_keys, block_values = two_keys[k0:k1], two_values[k0:k1]
            slopes, all_probs, heads_query, heads_grad = [], [], [], []
            for head in range(2):
                head_query = two_query[q0:q1] * scaled[head]
                head_grad = two_grad[q0:q1] * masks[head]
                scores = dot(block_keys, head_query, TURNED) + bias[k0:k1, q0:q1]
                probs = jnp.exp(scores - lse[pair, head : head + 1, q0:q1])
                pulled = dot(block_values, head_grad, TURNED)
                inner = jnp.sum(probs * pulled, axis=0, keepdims=True)
                slopes.append((probs * (pulled - inner)).astype(query.dtype))
                all_probs.append(probs.astype(query.dtype))
                heads_query.append(head_query)
                heads_grad.append(head_grad)
            both = jnp.concatenate(slopes, axis=1)
            of_keys.append((k0, dot(both, jnp.concatenate(heads_query, axis=0))))
            both = jnp.concatenate(all_probs, axis=1)
            of_values.append((k0, dot(both, jnp.concatenate(heads_grad, axis=0))))
            block_turned = turned_pair(eye, block_keys * jnp.asarray(SCALE, query.dtype))
            rows = [
                dot(block_turned[head * HEAD_DIM : (head + 1) * HEAD_DIM], slopes[head])
                for head in range(2)
            ]
            of_query.append(jnp.concatenate(rows, axis=0))
        total = jnp.concatenate(of_query, axis=1).astype(query_grad.dtype)
        query_grad[:, lanes] = dot(eye[...], total, TURNED).astype(query_grad.dtype)
        key_grad[:, lanes] = stacked(of_keys).astype(key_grad.dtype)
        value_grad[:, lanes] = stacked(of_values).astype(value_grad.dtype)
        return carry

    lax.fori_loop(first, last, pair_step, 0)


def turn_blocks(left, eye, store):
    width = eye.shape[0]
    for block in range(left.shape[1] // width):
        columns = pl.ds(block * width, width)
        store(block, dot(eye[...], left[:, columns], TURNED).astype(left.dtype))


def turn_by_lane(left, eye, target):
    group = eye.shape[0] // 2

    def store(block, value):
        target[0, pl.ds(block * group, group), :] = value[:group]
        target[1, pl.ds(block * group, group), :] = value[group:]

    turn_blocks(left, eye, store)


SQUARES = 8


def layer_kernel(places, sizes, *refs):
    n_rows, n_mem, width, ff, shard = sizes
    ref = SimpleNamespace(**jax.tree.map(lambda place: refs[place], places))
    place = Place(n_rows, n_mem)
    many = ff // width
    own_ff = ff // (n_rows * n_mem)
    (
        at_query,
        at_key,
        at_value,
        at_output,
        at_cross_query,
        at_cross_key,
        at_cross_value,
        at_cross_output,
    ) = range(SQUARES)
    full = ref.full
    expand, contract = ref.expand_full, ref.contract_full
    tokens, gains = ref.tokens, ref.gains
    low, turned = SimpleNamespace(**ref.low), SimpleNamespace(**ref.turned)

    order = [
        at_query,
        at_key,
        at_value,
        at_output,
        at_cross_key,
        at_cross_value,
        at_cross_query,
        at_cross_output,
    ]
    pool = ref.pool

    def gather_slot(number):
        return pool.at[pl.ds(number % GATHER_SLOTS * n_rows, n_rows)]

    sources = [ref.squares[index] for index in order]
    sources += [ref.expand.at[:, pl.ds(j * width, width)] for j in range(many)]
    sources += [ref.contract.at[pl.ds(j * shard, shard), :] for j in range(many)]
    stores = [full[index] for index in order] + [expand.at[j] for j in range(many)]
    stores += [contract.at[:, :, j] for j in range(many)]
    parts = [Part(item, gather_slot(n), n % 2) for n, item in enumerate(sources)]
    parts.insert(SMALL_AT, Part(ref.small, ref.small_full, 0, True))
    gather = Gather(place, parts, ref.gather_sems)

    def keep(number):
        return pltpu.make_async_copy(gather_slot(number), stores[number], ref.keep_sem.at[number])

    count = [0]

    def load_slot(number):
        first = pool.shape[0] - (1 + number % SLOTS) * n_rows
        return pool.at[pl.ds(first, n_rows)]

    def load(pieces):
        number = count[0]
        count[0] += 1
        for source, first, rows in pieces:
            target = load_slot(number).at[pl.ds(first, rows)]
            pltpu.make_async_copy(source, target, ref.slot_sem.at[number % SLOTS]).start()
        return number

    def ready(number):
        slot = load_slot(number)
        pltpu.make_async_copy(slot, slot, ref.slot_sem.at[number % SLOTS]).wait()
        return slot

    def contract_rows(j):
        groups = n_rows // many
        return [(contract.at[j * groups + i], i * n_mem, n_mem) for i in range(groups)]

    mem_block = ref.memory.shape[1]
    memory, mem_rows = ref.memory, ref.mem_rows

    def memory_own():
        return pltpu.make_async_copy(
            memory.at[place.mem], mem_rows.at[span(place.mem, mem_block)], ref.mem_sem.at[0]
        )

    def memory_total():
        some = mem_rows.at[pl.ds(0, (n_mem - 1) * mem_block)]
        return remote(some, some, ref.mem_sem.at[1], ref.mem_sem.at[2], place.far(1))

    ref.small[...] = jnp.zeros_like(ref.small)
    for member in range(n_mem):

        @pl.when(place.mem == member)
        def _(member=member):
            lanes = slice(member * shard, (member + 1) * shard)
            ref.small[0:3, lanes] = ref.norm_gains[...].astype(jnp.float32)
            ref.small[3:6, lanes] = ref.norm_shifts[...].astype(jnp.float32)

    place.greet()
    memory_own().start()
    for step in range(1, n_mem):
        remote(
            memory.at[(place.mem + step) % n_mem],
            mem_rows.at[span(place.mem, mem_block)],
            ref.mem_sem.at[1],
            ref.mem_sem.at[2],
            place.far(step),
        ).start()

    actions, whole = [], []
    for part in range(len(parts)):
        found, time = gather.events(part)
        for hop, (at, action) in enumerate(found):
            actions.append((HOP + 10 * part + hop, at, action))
        whole.append(time)
    first_hops = [HOP, HOP + 10]
    for code, _, action in actions:
        if code in first_hops:
            action()
    actions = [item for item in actions if item[0] not in first_hops]

    self_bias, cross_bias, eye = ref.self_bias, ref.cross_bias, ref.eye
    own_row = ref.token_ids[pl.ds(place.mem, 1), :].astype(jnp.float32)
    mem_row = ref.memory_ids[pl.ds(place.mem, 1), :].astype(jnp.float32)
    key_place = lax.broadcasted_iota(jnp.int32, self_bias.shape, 0)
    query_place = lax.broadcasted_iota(jnp.int32, self_bias.shape, 1)
    own_wide = jnp.broadcast_to(own_row, self_bias.shape)
    mem_wide = jnp.broadcast_to(mem_row, (cross_bias.shape[1], cross_bias.shape[0]))
    same = (jnp.transpose(own_wide) == own_wide) & (key_place <= query_place)
    self_bias[...] = jnp.where(same, 0.0, NEG)
    cross_bias[...] = jnp.where(jnp.transpose(mem_wide) == own_row, 0.0, NEG)
    eye_row = lax.broadcasted_iota(jnp.int32, eye.shape, 0)
    eye_column = lax.broadcasted_iota(jnp.int32, eye.shape, 1)
    eye[...] = jnp.where(eye_row == eye_column, 1.0, 0.0).astype(eye.dtype)
    turn_by_lane(tokens, eye, turned.tokens)

    accumulated, other = ref.accumulated, ref.other
    hidden, slope, hidden_turned = ref.hidden, ref.slope, ref.hidden_turned

    def small_piece():
        blocks = ref.small_full
        for group in range(n_rows):
            total = None
            for member in range(n_mem):
                value = blocks[group, member]
                total = value if total is None else total + value
            gains[:, group * 128 : (group + 1) * 128] = total

    def query_piece(slot):
        times(tokens, slot, into(ref.query))

    def key_piece(slot):
        times(tokens, slot, into(ref.keys))

    pairs = width // (2 * HEAD_DIM)
    self_blocks = [
        (first, first + 128, max(first - DOC_LIMIT, 0), first + 128)
        for first in range(0, self_bias.shape[1], 128)
    ]
    cross_blocks = [(0, cross_bias.shape[1], 0, cross_bias.shape[0])]

    def value_piece(slot):
        times(tokens, slot, into(ref.values))

    def self_forward(first, last, slot):
        attention_forward(
            ref.query,
            ref.keys,
            ref.values,
            self_bias,
            self_blocks,
            eye,
            ref.attended,
            turned.attended,
            ref.self_lse,
            first,
            last,
        )

    def output_piece(slot):
        def store(columns, value):
            accumulated[:, columns] = ALPHA * tokens[:, columns].astype(jnp.float32) + value

        times(ref.attended, slot, store)

    def output_norm(slot):
        def use(rows, value):
            ref.first_low[rows, :] = value.astype(jnp.bfloat16)
            other[rows, :] = value

        norm_forward(accumulated, gains, 0, ref.unit1, ref.scale1, use)

    def cross_key_piece(slot):
        memory_own().wait()
        memory_total().wait_recv()
        times(mem_rows, slot, into(ref.cross_keys))
        turn_by_lane(mem_rows, eye, turned.memory)

    def cross_value_piece(slot):
        times(mem_rows, slot, into(ref.cross_values))
        turn_by_lane(ref.first_low, eye, turned.first)

    def cross_query_piece(slot):
        times(ref.first_low, slot, into(ref.cross_query))

    def cross_forward(first, last, slot):
        attention_forward(
            ref.cross_query,
            ref.cross_keys,
            ref.cross_values,
            cross_bias,
            cross_blocks,
            eye,
            ref.crossed,
            turned.crossed,
            ref.cross_lse,
            first,
            last,
        )

    def cross_output_piece(slot):
        def store(columns, value):
            accumulated[:, columns] = ALPHA * other[:, columns] + value

        times(ref.crossed, slot, store)

    def cross_output_norm(slot):
        def use(rows, value):
            ref.second_low[rows, :] = value.astype(jnp.bfloat16)
            other[rows, :] = value

        norm_forward(accumulated, gains, 1, ref.unit2, ref.scale2, use)

    def expand_piece(j, half, slot):
        def store(columns, value):
            there = pl.ds(pl.multiple_of(j * width + columns.start, TILE), columns.size)
            bell = 0.5 * (1.0 + lax.erf(value * math.sqrt(0.5)))
            density = jnp.exp(value * value * -0.5) * (1.0 / math.sqrt(2.0 * math.pi))
            hidden[:, there] = (value * bell).astype(hidden.dtype)
            slope[:, there] = (bell + value * density).astype(slope.dtype)

        times(ref.second_low, slot, store, half, 2)

    def expand_turn(j, slot):
        def keep(block, value):
            for index in range(value.shape[0] // shard):
                first = j * width + block * value.shape[0] + index * shard
                device, job = first // own_ff, first % own_ff // shard
                group, member = device // n_mem, device % n_mem
                at = group // 2 * n_mem * shard + member * shard
                hidden_turned[job, group % 2, at : at + shard, :] = value[
                    index * shard : (index + 1) * shard
                ]

        turn_blocks(hidden.at[:, pl.ds(j * width, width)], eye, keep)

    def contract_piece(j, slot):
        block = 2 * n_mem * shard
        for index in range(n_rows // 2):
            rows = pl.ds(index * n_mem * shard, n_mem * shard)
            both = jnp.concatenate([hidden_turned[j, 0, rows], hidden_turned[j, 1, rows]], axis=0)
            columns = pl.ds(index * block, block)
            low.branch[:, columns] = dot(eye[...], both, TURNED).astype(jnp.bfloat16)

        def store(columns, value):
            if j == 0:
                accumulated[:, columns] = ALPHA * other[:, columns] + value
            else:
                accumulated[:, columns] = accumulated[:, columns] + value

        times(low.branch, slot, store)

    quarters = [(pairs * at // 4, pairs * (at + 1) // 4) for at in range(4)]
    pieces = [
        [query_piece],
        [key_piece],
        [value_piece] + [functools.partial(self_forward, *quarter) for quarter in quarters],
        [output_piece, output_norm],
        [cross_key_piece],
        [cross_value_piece],
        [cross_query_piece] + [functools.partial(cross_forward, *quarter) for quarter in quarters],
        [cross_output_piece, cross_output_norm],
    ]
    for j in range(many):
        halves = [functools.partial(expand_piece, j, half) for half in range(2)]
        pieces.append(halves + [functools.partial(expand_turn, j)])
    pieces += [[functools.partial(contract_piece, j)] for j in range(many)]

    def arrive(part):
        gather.core_total(part).wait_recv()
        if part != SMALL_AT:
            keep(part - (part > SMALL_AT)).start()

    def use(part, index):
        if part == SMALL_AT:
            small_piece()
        else:
            number = part - (part > SMALL_AT)
            pieces[number][index](gather_slot(number))

    def settle(part):
        gather.sent(part)
        if part != SMALL_AT:
            keep(part - (part > SMALL_AT)).wait()

    last = 0.0
    for part, time in enumerate(whole):
        time = max(time, last + 0.5)
        actions.append((ARRIVE + part, time, functools.partial(arrive, part)))
        count_here = 1 if part == SMALL_AT else len(pieces[part - (part > SMALL_AT)])
        for index in range(count_here):
            at = time + 0.2 + 0.04 * index
            actions.append((USE + 10 * part + index, at, functools.partial(use, part, index)))
        actions.append((SETTLE + part, time + 0.45, functools.partial(settle, part)))
        last = time
    for action in planned(actions, FORWARD_PLAN):
        action()
    place.tell(ref.ready_sem)

    backward_sources, loads = [], []
    used = [0]

    def next_slot():
        slot = ready(loads[used[0]])
        used[0] += 1
        if len(loads) < len(backward_sources):
            loads.append(load(backward_sources[len(loads)]))
        return slot

    small_sums = ref.small_sums
    small_sums[...] = jnp.zeros_like(small_sums)
    def inner_piece(j):
        slot = next_slot()

        def store(columns, value):
            there = pl.ds(pl.multiple_of(j * width + columns.start, TILE), columns.size)
            slope[:, there] = (value * slope[:, there].astype(jnp.float32)).astype(slope.dtype)

        times_turned(low.third, slot, store)

    def second_piece(j):
        slot = next_slot()

        def store(columns, value):
            if j == 0:
                other[:, columns] = ALPHA * accumulated[:, columns] + value
            else:
                other[:, columns] = other[:, columns] + value

        times_turned(slope.at[:, pl.ds(j * width, width)], slot, store)

    def second_norm_piece():
        norm_backward(
            other, gains, 1, ref.unit2, ref.scale2, accumulated, low.second, small_sums
        )

    def cross_start_piece():
        times_turned(low.second, next_slot(), into(low.branch))

    def cross_piece(first, last):
        attention_backward(
            ref.cross_query,
            ref.cross_keys,
            ref.cross_values,
            cross_bias,
            cross_blocks,
            eye,
            ref.cross_lse,
            low.branch,
            low.cross_query,
            low.cross_key,
            low.cross_value,
            first,
            last,
        )

    def first_piece():
        def store(columns, value):
            other[:, columns] = ALPHA * accumulated[:, columns] + value

        times_turned(low.cross_query, next_slot(), store)

    def first_norm_piece():
        norm_backward(other, gains, 0, ref.unit1, ref.scale1, accumulated, low.first, small_sums)

    def self_start_piece():
        times_turned(low.first, next_slot(), into(low.branch))

    def self_piece(first, last):
        attention_backward(
            ref.query,
            ref.keys,
            ref.values,
            self_bias,
            self_blocks,
            eye,
            ref.self_lse,
            low.branch,
            low.query,
            low.key,
            low.value,
            first,
            last,
        )

    mem_out, mem_in = ref.mem_out, ref.mem_in

    def grad_own():
        return pltpu.make_async_copy(
            mem_out.at[span(place.mem, mem_block)], mem_in.at[place.mem], ref.mem_sem.at[3]
        )

    def grad_total():
        some = mem_in.at[pl.ds(0, n_mem - 1)]
        return remote(some, some, ref.mem_sem.at[4], ref.mem_sem.at[5], place.far(1))

    def memory_key_piece():
        times_turned(low.cross_key, next_slot(), into(other))

    def memory_value_piece():
        def store(columns, value):
            mem_out[:, columns] = (other[:, columns] + value).astype(mem_out.dtype)

        times_turned(low.cross_value, next_slot(), store)
        grad_own().start()
        for step in range(1, n_mem):
            remote(
                mem_out.at[span((place.mem + step) % n_mem, mem_block)],
                mem_in.at[place.mem],
                ref.mem_sem.at[4],
                ref.mem_sem.at[5],
                place.far(step),
            ).start()

    def input_piece(left, start):
        target = ref.input_grad

        def store(columns, value):
            if start:
                target[:, columns] = ALPHA * accumulated[:, columns] + value
            else:
                target[:, columns] = target[:, columns] + value

        times_turned(left, next_slot(), store)

    def memory_end_piece():
        grad_own().wait()
        grad_total().wait_recv()
        for member in range(n_mem):
            ref.memory_grad[member] = mem_in[member].astype(jnp.float32)

    halves = ((0, width // 2), (width // 2, width // 2))
    grads = ref.grads
    plans = []
    for j in range(many):
        for first, columns in halves if j == 0 else ((0, width),):
            target = ref.contract_grad.at[pl.ds(j * shard, shard), pl.ds(first, columns)]
            plans.append((hidden_turned.at[j], low.third, first, target))
    for j in range(many):
        target = ref.expand_grad.at[:, pl.ds(j * width, width)]
        plans.append((turned.second, slope, j * width, target))
    plans += [
        (turned.crossed, low.second, 0, grads[at_cross_output]),
        (turned.memory, low.cross_key, 0, grads[at_cross_key]),
        (turned.memory, low.cross_value, 0, grads[at_cross_value]),
        (turned.first, low.cross_query, 0, grads[at_cross_query]),
        (turned.attended, low.first, 0, grads[at_output]),
        (small_sums, None, 0, ref.small_total),
        (turned.tokens, low.query, 0, grads[at_query]),
        (turned.tokens, low.key, 0, grads[at_key]),
    ]
    for first, columns in halves:
        target = grads[at_value].at[:, pl.ds(first, columns)]
        plans.append((turned.tokens, low.value, first, target))
    jobs = [Job(*plan) for plan in plans]
    reduce = Reduce(place, jobs, ref.reduce_sems, pool, SimpleNamespace(**ref.little))

    inner = [functools.partial(inner_piece, j) for j in range(many)]
    second = [functools.partial(second_piece, j) for j in range(many)]
    base = many + 1
    def weight(index):
        return [(full[index], 0, n_rows)]

    turn = functools.partial(turn_by_lane, ref.second_low, eye, turned.second)
    crosses = [functools.partial(cross_piece, pair, pair + 1) for pair in range(pairs)]
    selves = [functools.partial(self_piece, pair, pair + 1) for pair in range(pairs)]
    work = [(base - 1.7 + j, inner[j], contract_rows(j)) for j in range(2)]
    work += [(base - 1.3, turn, None)]
    work += [(base - 1.7 + j, inner[j], contract_rows(j)) for j in range(2, many)]
    work += [(base - 0.3 + j, second[j], [(expand.at[j], 0, n_rows)]) for j in range(many)]
    base = 2 * many + 1
    work += [
        (base - 0.2, second_norm_piece, None),
        (base - 0.15, cross_start_piece, weight(at_cross_output)),
    ]
    work += [(base + 0.3 + 0.05 * pair, crosses[pair], None) for pair in range(pairs)]
    work += [
        (base + 1.3, first_piece, weight(at_cross_query)),
        (base + 1.31, first_norm_piece, None),
        (base + 1.7, self_start_piece, weight(at_output)),
    ]
    work += [(base + 2.3 + 0.14 * pair, selves[pair], None) for pair in range(pairs)]
    work += [
        (base + 3.7, memory_key_piece, weight(at_cross_key)),
        (base + 4.3, memory_value_piece, weight(at_cross_value)),
        (base + 4.7, functools.partial(input_piece, low.query, True), weight(at_query)),
        (base + 5.5, functools.partial(input_piece, low.key, False), weight(at_key)),
        (base + 6.5, functools.partial(input_piece, low.value, False), weight(at_value)),
        (base + 8.5, memory_end_piece, None),
    ]
    actions = [(WORK + index, at, item) for index, (at, *item) in enumerate(work)]
    for number in range(len(jobs)):
        found = reduce.events(number)
        actions.append((CORE + number, found[0][0], found[0][1:]))
        actions.append((LANE + number, found[1][0], found[1][1:]))
        for stage, (at, action) in enumerate(found[2:]):
            actions.append((STAGE + 10 * number + stage, at, (action,)))
    ordered = planned(actions, BACKWARD_PLAN)
    backward_sources += [item[1] for item in ordered if len(item) > 1 and item[1] is not None]
    loads += [load(backward_sources[0]), load(backward_sources[1])]
    norm_both(
        accumulated, ref.out_grad, gains, 2, ref.result, accumulated, low.third, small_sums
    )

    place.hear(ref.ready_sem)
    for item in ordered:
        item[0]()

    total = ref.small_total[...]
    own = jnp.zeros((8, shard), jnp.float32)
    for member in range(n_mem):
        here = jnp.where(place.mem == member, 1.0, 0.0)
        own = own + here * total[:, member * shard : (member + 1) * shard]
    ref.gains_grad[...] = own[0:3]
    ref.shifts_grad[...] = own[3:6]
    reduce.finish()
    memory_total().wait_send()
    grad_total().wait_send()


SMALL_AT = 2
DOC_LIMIT = 64
HOP, ARRIVE, USE, SETTLE, CORE, LANE, STAGE, WORK = range(1000, 9000, 1000)
FORWARD_PLAN = (
    1001, 1011, 1020, 1002, 1003, 1012, 1030, 1040, 1021, 1004, 1013, 1031, 1041, 1014, 1032, 1050,
    1033, 1005, 1060, 1042, 1070, 2000, 1043, 1015, 1051, 1022, 1080, 1034, 1061, 1044, 1052, 3000,
    2001, 4000, 1023, 3010, 2002, 1071, 1053, 3020, 1062, 1035, 1072, 1081, 1045, 2003, 4001, 1090,
    1073, 3030, 1063, 1054, 3031, 2004, 1064, 1091, 3032, 4002, 1082, 3033, 3034, 1092, 1055, 4003,
    1100, 1110, 3040, 1093, 3041, 1074, 1065, 4004, 1083, 1101, 2005, 1111, 3050, 4005, 1120, 1084,
    1102, 2006, 1130, 1094, 1075, 3060, 4006, 2007, 1121, 1085, 3070, 3071, 1112, 1103, 1113, 3072,
    1122, 1131, 1104, 3073, 2008, 3074, 4007, 1140, 1150, 1114, 1095, 1123, 1132, 3080, 1141, 3081,
    1105, 1133, 1160, 1151, 2009, 1124, 3090, 3091, 4008, 2010, 1115, 1152, 1142, 1134, 3092, 4009,
    3100, 3101, 1143, 3102, 4010, 1161, 1153, 2011, 1144, 3110, 1125, 3111, 1135, 1154, 1162, 3112,
    1163, 2012, 3120, 3121, 1164, 1145, 2013, 3122, 3130, 1155, 4011, 4012, 2014, 4013, 3140, 1165,
    2015, 4014, 3150, 2016, 3160, 4015, 4016,
)
BACKWARD_PLAN = (
    5000, 6000, 5001, 8003, 6001, 5002, 7000, 8000, 7010, 6002, 5003, 8005, 7001, 8001, 6003, 8002,
    5004, 7020, 7002, 7011, 8004, 6004, 5005, 7021, 7030, 7012, 8006, 6005, 5006, 8007, 7040, 6006,
    7022, 5007, 7031, 8008, 8009, 6007, 8010, 5008, 7041, 8011, 7032, 7050, 7060, 8012, 6008, 8013,
    5009, 7051, 8014, 7042, 8015, 8016, 7070, 8017, 8018, 6009, 5010, 7061, 8019, 8020, 7052, 7080,
    6010, 5011, 8021, 7071, 8022, 7090, 8023, 6011, 5012, 7062, 8024, 8025, 7072, 8026, 7081, 6012,
    5013, 7091, 8027, 8028, 7100, 7110, 8029, 8032, 6013, 7082, 7101, 5014, 7120, 6014, 5015, 8030,
    7092, 8033, 7111, 7130, 7102, 6015, 5016, 7121, 8034, 6016, 7112, 7131, 7140, 7150, 5017, 7122,
    8031, 7132, 7141, 7160, 6017, 7151, 5018, 7161, 6018, 7142, 7170, 7152, 7180, 8035, 7171, 7162,
    7181, 7172, 7182,
)


def planned(actions, plan):
    codes = {code for code, _, _ in actions}
    if codes == set(plan):
        at = {code: number for number, code in enumerate(plan)}
        return [item for code, _, item in sorted(actions, key=lambda action: at[action[0]])]
    return [item for _, _, item in sorted(actions, key=lambda action: action[1])]


def copy_kernel(count, *refs):
    for source, target in zip(refs[:count], refs[count:]):
        target[...] = source[...]


def copied(values):
    near = pl.BlockSpec(memory_space=pltpu.VMEM)
    return pl.pallas_call(
        functools.partial(copy_kernel, len(values)),
        out_shape=[jax.ShapeDtypeStruct(value.shape, value.dtype) for value in values],
        in_specs=[near] * len(values),
        out_specs=[near] * len(values),
        compiler_params=pltpu.CompilerParams(vmem_limit_bytes=VMEM_LIMIT),
        name="results",
    )(*values)


def fused(n_rows, n_mem, ins):
    tokens, memory, squares = ins["tokens"], ins["memory"], ins["squares"]
    expand, contract = ins["expand"], ins["contract"]
    tokens_here, width = tokens.shape
    ff = expand.shape[1]
    shard = squares[0].shape[0]
    mem_tokens = memory.shape[0] * memory.shape[1]
    digits, half, many = (n_rows // 2).bit_length() - 1, n_rows // 2, ff // width
    pairs = width // (2 * HEAD_DIM)
    low, high = jnp.bfloat16, jnp.float32
    n_parts = 1 + SQUARES + 2 * many
    n_jobs = n_parts + 2
    dma, vmem = pltpu.SemaphoreType.DMA, pltpu.VMEM
    anywhere, near = pl.BlockSpec(memory_space=pl.ANY), pl.BlockSpec(memory_space=pltpu.VMEM)

    far_ins = dict(memory=memory)
    in_specs = {
        name: jax.tree.map(lambda _: anywhere if name in far_ins else near, value)
        for name, value in ins.items()
    }

    def out(shape, dtype=high):
        return jax.ShapeDtypeStruct(shape, dtype)

    outs = dict(
        result=out(tokens.shape),
        input_grad=out(tokens.shape),
        memory_grad=out(memory.shape),
        grads=[out(item.shape) for item in squares],
        expand_grad=out(expand.shape),
        contract_grad=out(contract.shape),
        gains_grad=out((3, shard)),
        shifts_grad=out((3, shard)),
    )
    far_outs = dict(
        full=[out((n_rows, n_mem, shard, width), low)] * SQUARES,
        expand_full=out((many, n_rows, n_mem, shard, width), low),
        contract_full=out((n_rows, n_mem, many, shard, width), low),
    )
    out_specs = jax.tree.map(lambda _: near, outs)
    out_specs.update(jax.tree.map(lambda _: anywhere, far_outs))
    outs.update(far_outs)

    def token_rows(dtype):
        return vmem((tokens_here, width), dtype)

    def memory_rows(dtype):
        return vmem((mem_tokens, width), dtype)

    tiny = (8, 128)

    counts = [half >> (stage + 1) for stage in range(digits)]
    units = (OUT_SLOTS + LANE_SLOTS + CORE_RING) * half + RING
    for stage, number in enumerate(counts):
        units += (SUM_SLOTS + (RING if stage else FIRST_RING)) * number
    units = max(units + SLOTS * n_rows, GATHER_SLOTS * n_rows)
    little = dict(
        lanes=vmem((half,) + tiny, high),
        core_in=vmem((half,) + tiny, high),
        sums=[vmem((number,) + tiny, high) for number in counts],
        arrived=[vmem((number,) + tiny, high) for number in counts]
        + [vmem((n_mem - 1,) + tiny, high)],
    )
    left = vmem((2, width // 2, tokens_here), low)
    scratch = dict(
        small=vmem(tiny, high),
        small_full=vmem((n_rows, n_mem) + tiny, high),
        small_total=vmem(tiny, high),
        pool=vmem((units, n_mem, shard, width), low),
        slot_sem=dma((SLOTS,)),
        keep_sem=dma((n_parts - 1,)),
        ready_sem=pltpu.SemaphoreType.REGULAR,
        mem_sem=dma((6,)),
        gather_sems=[
            dma(shape + (n_parts,))
            for shape in ((), (), (), (digits,), (digits,), (), ())
            + ((2 * (n_mem - 1),), (2 * (n_mem - 1),))
        ],
        reduce_sems=[dma(shape + (n_jobs,)) for shape in ((), (), (digits + 1,), (digits + 1,))],
        gains=vmem((8, width), high),
        query=token_rows(low),
        keys=token_rows(low),
        values=token_rows(low),
        attended=token_rows(low),
        first_low=token_rows(low),
        second_low=token_rows(low),
        cross_query=token_rows(low),
        crossed=token_rows(low),
        cross_keys=memory_rows(low),
        cross_values=memory_rows(low),
        mem_rows=memory_rows(low),
        mem_out=memory_rows(low),
        mem_in=vmem(memory.shape, low),
        unit1=token_rows(high),
        unit2=token_rows(high),
        accumulated=token_rows(high),
        other=token_rows(high),
        scale1=vmem((tokens_here, 1), high),
        scale2=vmem((tokens_here, 1), high),
        self_bias=vmem((tokens_here, tokens_here), high),
        cross_bias=vmem((mem_tokens, tokens_here), high),
        self_lse=vmem((pairs, 2, tokens_here), high),
        cross_lse=vmem((pairs, 2, tokens_here), high),
        eye=vmem((TILE, TILE), low),
        hidden=vmem((tokens_here, ff), low),
        slope=vmem((tokens_here, ff), low),
        hidden_turned=vmem((many, 2, width // 2, tokens_here), low),
        turned=dict(
            tokens=left, attended=left, first=left, memory=left, crossed=left, second=left
        ),
        low=dict(
            third=token_rows(low),
            second=token_rows(low),
            first=token_rows(low),
            branch=token_rows(low),
            cross_query=token_rows(low),
            cross_key=memory_rows(low),
            cross_value=memory_rows(low),
            query=token_rows(low),
            key=token_rows(low),
            value=token_rows(low),
        ),
        small_sums=vmem((2, half) + tiny, high),
        little=little,
    )
    in_values, in_tree = jax.tree.flatten(ins)
    out_shapes, out_tree = jax.tree.flatten(outs)
    scratch_shapes, scratch_tree = jax.tree.flatten(scratch)
    places = jax.tree.unflatten(in_tree, range(len(in_values)))
    at = len(in_values)
    places.update(jax.tree.unflatten(out_tree, range(at, at + len(out_shapes))))
    at += len(out_shapes)
    places.update(jax.tree.unflatten(scratch_tree, range(at, at + len(scratch_shapes))))
    values = pl.pallas_call(
        functools.partial(layer_kernel, places, (n_rows, n_mem, width, ff, shard)),
        out_shape=out_shapes,
        in_specs=jax.tree.leaves(in_specs),
        out_specs=jax.tree.leaves(out_specs),
        scratch_shapes=scratch_shapes,
        compiler_params=pltpu.CompilerParams(
            collective_id=0, has_side_effects=True, vmem_limit_bytes=VMEM_LIMIT
        ),
        name="layer",
    )(*in_values)
    found = jax.tree.unflatten(out_tree, values)
    for name in far_outs:
        del found[name]
    return found


def local(n_rows, n_mem, *args):
    (
        tokens,
        memory,
        token_ids,
        memory_ids,
        out_grad,
        self_query,
        self_key,
        self_value,
        self_output,
        cross_query,
        cross_key,
        cross_value,
        cross_output,
        expand_weight,
        contract_weight,
        norm_gains,
        norm_shifts,
    ) = args
    shard, width = self_query.shape
    suits = width == 128 * n_rows and shard % 16 == 0 and tokens.shape[0] == 1
    suits = suits and tokens.shape[1] == TILE and expand_weight.shape[1] == n_mem * width
    if not suits or n_rows < 4 or n_rows & (n_rows - 1) or n_mem < 2:
        return plain(*args)
    found = fused(
        n_rows,
        n_mem,
        dict(
            tokens=tokens[0],
            memory=memory,
            token_ids=token_ids,
            memory_ids=memory_ids,
            out_grad=out_grad[0],
            squares=[
                self_query,
                self_key,
                self_value,
                self_output,
                cross_query,
                cross_key,
                cross_value,
                cross_output,
            ],
            expand=expand_weight,
            contract=contract_weight,
            norm_gains=norm_gains,
            norm_shifts=norm_shifts,
        ),
    )
    values, tree = jax.tree.flatten(found)
    found = SimpleNamespace(**jax.tree.unflatten(tree, copied(values)))
    return (
        found.result[None],
        found.input_grad[None],
        found.memory_grad,
        *found.grads,
        found.expand_grad,
        found.contract_grad,
        found.gains_grad,
        found.shifts_grad,
    )


def solution(mesh):
    in_specs = (
        P(("rows", "mem"), None, None),
        P("rows", "mem", None),
        P("rows", None),
        P("rows", None),
        P(("rows", "mem"), None, None),
        P(("rows", "mem"), None),
        P(("rows", "mem"), None),
        P(("rows", "mem"), None),
        P(("rows", "mem"), None),
        P(("rows", "mem"), None),
        P(("rows", "mem"), None),
        P(("rows", "mem"), None),
        P(("rows", "mem"), None),
        P(("rows", "mem"), None),
        P(("rows", "mem"), None),
        P(None, ("rows", "mem")),
        P(None, ("rows", "mem")),
    )
    out_specs = (
        P(("rows", "mem"), None, None),
        P(("rows", "mem"), None, None),
        P("rows", "mem", None),
        P(("rows", "mem"), None),
        P(("rows", "mem"), None),
        P(("rows", "mem"), None),
        P(("rows", "mem"), None),
        P(("rows", "mem"), None),
        P(("rows", "mem"), None),
        P(("rows", "mem"), None),
        P(("rows", "mem"), None),
        P(("rows", "mem"), None),
        P(("rows", "mem"), None),
        P(None, ("rows", "mem")),
        P(None, ("rows", "mem")),
    )
    layer = functools.partial(local, mesh.shape["rows"], mesh.shape["mem"])
    return jax.shard_map(layer, mesh=mesh, in_specs=in_specs, out_specs=out_specs, check_vma=False)
```

```python
import functools
import math
from types import SimpleNamespace

import jax
import jax.numpy as jnp
from jax import lax
from jax.experimental import pallas as pl
from jax.experimental.pallas import tpu as pltpu
from jax.sharding import PartitionSpec as P

MESH = pl.DeviceIdType.MESH

HEADS = 16
HEAD_DIM = 64


ALPHA = 4.16
EPS = 1e-05
SCALE = 0.125
NEG = -1e30


def layer_norm(hidden_activation, gain, shift):
    centre = hidden_activation - jnp.mean(hidden_activation, axis=-1, keepdims=True)
    spread = jnp.mean(centre * centre, axis=-1, keepdims=True)
    return centre * lax.rsqrt(spread + EPS) * gain + shift


def gelu_exact(value):
    return jax.nn.gelu(value, approximate=False)


def product(left, right):
    return jnp.dot(left, right, preferred_element_type=jnp.float32)


def split_heads(matrix):
    return matrix.reshape(matrix.shape[0], matrix.shape[1] // HEAD_DIM, HEAD_DIM)


def grouped(matrix):
    return jnp.moveaxis(matrix.reshape(matrix.shape[0], HEADS // 4, 4 * HEAD_DIM), 1, 0)


def ungrouped(stack):
    return jnp.moveaxis(stack, 0, 1).reshape(stack.shape[1], stack.shape[0] * stack.shape[2])


def row_map(function, items):
    return lax.map(lambda entry: function(*entry), items)


def score_block(query, keys, allowed):
    raw = jnp.einsum(
        "khe,qhe->hkq", split_heads(keys), split_heads(query), preferred_element_type=jnp.float32
    )
    return jnp.where(allowed[None], raw * SCALE, NEG)


def attend_probs(query, keys, allowed, lse):
    scores = score_block(query, keys, allowed)
    return jnp.where(allowed[None], jnp.exp(scores - lse[:, None, :]), 0.0)


def attend_forward(query, keys, values, allowed):
    scores = score_block(query, keys, allowed)
    top = jnp.max(scores, axis=1)
    weight = jnp.where(allowed[None], jnp.exp(scores - top[:, None, :]), 0.0)
    total = jnp.sum(weight, axis=1)
    probs = (weight / total[:, None, :]).astype(jnp.bfloat16)
    mixed = jnp.einsum(
        "hkq,khe->qhe", probs, split_heads(values), preferred_element_type=jnp.float32
    )
    return (mixed.reshape(query.shape), top + jnp.log(total))


def value_pull(grad, values):
    return jnp.einsum(
        "qhe,khe->hkq", split_heads(grad), split_heads(values), preferred_element_type=jnp.float32
    )


def score_grads(probs, pulled, inner):
    return (probs * (pulled - inner[:, None, :]) * SCALE).astype(jnp.bfloat16)


def query_from(score_grad, keys, shape):
    moved = jnp.einsum(
        "hkq,khe->qhe", score_grad, split_heads(keys), preferred_element_type=jnp.float32
    )
    return moved.reshape(shape)


def key_from(score_grad, query, shape):
    moved = jnp.einsum(
        "hkq,qhe->khe", score_grad, split_heads(query), preferred_element_type=jnp.float32
    )
    return moved.reshape(shape)


def value_from(probs, grad, values):
    moved = jnp.einsum(
        "hkq,qhe->khe",
        probs.astype(jnp.bfloat16),
        split_heads(grad),
        preferred_element_type=jnp.float32,
    )
    return moved.reshape(values.shape)


def local_forward(query, keys, values, allowed):

    def one_group(items):
        return attend_forward(items[0], items[1], items[2], allowed)

    mixed, lse = lax.map(one_group, (grouped(query), grouped(keys), grouped(values)))
    return (ungrouped(mixed), lse)


def local_backward(query, keys, values, allowed, lse, grad):

    def one_group(items):
        part_query, part_keys, part_values, part_lse, part_grad = items
        probs = attend_probs(part_query, part_keys, allowed, part_lse)
        pulled = value_pull(part_grad, part_values)
        inner = jnp.sum(probs * pulled, axis=1)
        score_grad = score_grads(probs, pulled, inner)
        return (
            query_from(score_grad, part_keys, part_query.shape),
            key_from(score_grad, part_query, part_keys.shape),
            value_from(probs, part_grad, part_values),
        )

    parts = lax.map(one_group, (grouped(query), grouped(keys), grouped(values), lse, grouped(grad)))
    return (ungrouped(parts[0]), ungrouped(parts[1]), ungrouped(parts[2]))


def plain(
    tokens,
    memory,
    token_ids,
    memory_ids,
    out_grad,
    self_query,
    self_key,
    self_value,
    self_output,
    cross_query,
    cross_key,
    cross_value,
    cross_output,
    expand_weight,
    contract_weight,
    norm_gains,
    norm_shifts,
):
    full = (
        lax.all_gather(self_query, ("rows", "mem"), axis=0, tiled=True),
        lax.all_gather(self_key, ("rows", "mem"), axis=0, tiled=True),
        lax.all_gather(self_value, ("rows", "mem"), axis=0, tiled=True),
        lax.all_gather(self_output, ("rows", "mem"), axis=0, tiled=True),
        lax.all_gather(cross_query, ("rows", "mem"), axis=0, tiled=True),
        lax.all_gather(cross_key, ("rows", "mem"), axis=0, tiled=True),
        lax.all_gather(cross_value, ("rows", "mem"), axis=0, tiled=True),
        lax.all_gather(cross_output, ("rows", "mem"), axis=0, tiled=True),
        lax.all_gather(expand_weight, ("rows", "mem"), axis=0, tiled=True),
        lax.all_gather(contract_weight, ("rows", "mem"), axis=0, tiled=True),
        lax.all_gather(jnp.transpose(norm_gains), ("rows", "mem"), axis=0, tiled=True),
        lax.all_gather(jnp.transpose(norm_shifts), ("rows", "mem"), axis=0, tiled=True),
    )
    (
        self_attention_query,
        decoder_match_label,
        self_attention_value,
        self_attention_output,
        encoder_lookup_probe,
        key_cross,
        value_cross,
        cross_attention_output,
        up_projection,
        narrowing_matrix,
        gain_cols,
        shift_cols,
    ) = full
    gain_rows = jnp.transpose(gain_cols).astype(jnp.float32)
    shift_rows = jnp.transpose(shift_cols).astype(jnp.float32)
    rows_here = tokens.shape[0]
    member = lax.axis_index("mem")
    own_ids = lax.dynamic_slice_in_dim(token_ids, member * rows_here, rows_here, 0)
    positions = jnp.arange(tokens.shape[1], dtype=jnp.int32)
    self_allowed = (own_ids[:, :, None] == own_ids[:, None, :]) & (
        positions[:, None] <= positions[None, :]
    )[None]
    query = product(tokens, self_attention_query).astype(jnp.bfloat16)
    keys = product(tokens, decoder_match_label).astype(jnp.bfloat16)
    values = product(tokens, self_attention_value).astype(jnp.bfloat16)
    self_mixed, self_lse = row_map(local_forward, (query, keys, values, self_allowed))
    attention_result = self_mixed.astype(jnp.bfloat16)
    first, first_back = jax.vjp(
        layer_norm,
        ALPHA * tokens.astype(jnp.float32) + product(attention_result, self_attention_output),
        gain_rows[0],
        shift_rows[0],
    )
    first_reduced = first.astype(jnp.bfloat16)
    cross_queries = product(first_reduced, encoder_lookup_probe).astype(jnp.bfloat16)
    memory_rows = lax.all_to_all(memory, "mem", split_axis=0, concat_axis=1, tiled=True)
    row_ids = lax.dynamic_slice_in_dim(memory_ids, member * rows_here, rows_here, 0)
    cross_allowed = row_ids[:, :, None] == own_ids[:, None, :]
    cross_keys = product(memory_rows, key_cross).astype(jnp.bfloat16)
    cross_values = product(memory_rows, value_cross).astype(jnp.bfloat16)
    cross_mixed, cross_lse = row_map(
        local_forward, (cross_queries, cross_keys, cross_values, cross_allowed)
    )
    cross_attention_result = cross_mixed.astype(jnp.bfloat16)
    second, second_back = jax.vjp(
        layer_norm,
        ALPHA * first + product(cross_attention_result, cross_attention_output),
        gain_rows[1],
        shift_rows[1],
    )
    second_reduced = second.astype(jnp.bfloat16)
    hidden_value, gelu_back = jax.vjp(gelu_exact, product(second_reduced, up_projection))
    hidden_activation = hidden_value.astype(jnp.bfloat16)
    result, third_back = jax.vjp(
        layer_norm,
        ALPHA * second + product(hidden_activation, narrowing_matrix),
        gain_rows[2],
        shift_rows[2],
    )
    third_grad, gain_three, shift_three = third_back(out_grad.astype(jnp.float32))
    feedforward_gradient = third_grad.astype(jnp.bfloat16)
    down_projection_gradient = jnp.einsum(
        "ehj,ehc->jc", hidden_activation, feedforward_gradient, preferred_element_type=jnp.float32
    )
    (inner_grad,) = gelu_back(
        jnp.einsum(
            "hpu,ku->hpk",
            feedforward_gradient,
            narrowing_matrix,
            preferred_element_type=jnp.float32,
        )
    )
    inner_reduced = inner_grad.astype(jnp.bfloat16)
    expand_grad = jnp.einsum(
        "iqg,iqe->ge", second_reduced, inner_reduced, preferred_element_type=jnp.float32
    )
    second_total = ALPHA * third_grad + jnp.einsum(
        "iwm,fm->iwf", inner_reduced, up_projection, preferred_element_type=jnp.float32
    )
    second_grad, gain_two, shift_two = second_back(second_total)
    cross_branch_gradient = second_grad.astype(jnp.bfloat16)
    output_cross_grad = jnp.einsum(
        "nhb,nhc->bc",
        cross_attention_result,
        cross_branch_gradient,
        preferred_element_type=jnp.float32,
    )
    crossed_grad = jnp.einsum(
        "qwp,up->qwu",
        cross_branch_gradient,
        cross_attention_output,
        preferred_element_type=jnp.float32,
    ).astype(jnp.bfloat16)
    query_grads, key_grads, value_grads = row_map(
        local_backward,
        (cross_queries, cross_keys, cross_values, cross_allowed, cross_lse, crossed_grad),
    )
    key_low = key_grads.astype(jnp.bfloat16)
    value_low = value_grads.astype(jnp.bfloat16)
    row_grad = jnp.einsum(
        "sme,de->smd", key_low, key_cross, preferred_element_type=jnp.float32
    ) + jnp.einsum("sme,de->smd", value_low, value_cross, preferred_element_type=jnp.float32)
    key_cross_grad = jnp.einsum(
        "smd,sme->de", memory_rows, key_low, preferred_element_type=jnp.float32
    )
    value_cross_grad = jnp.einsum(
        "smd,sme->de", memory_rows, value_low, preferred_element_type=jnp.float32
    )
    memory_grad = lax.all_to_all(
        row_grad.astype(jnp.bfloat16), "mem", split_axis=1, concat_axis=0, tiled=True
    ).astype(row_grad.dtype)
    probe_lowered_precision = query_grads.astype(jnp.bfloat16)
    query_cross_grad = jnp.einsum(
        "nhb,nhc->bc", first_reduced, probe_lowered_precision, preferred_element_type=jnp.float32
    )
    first_total = ALPHA * second_grad + jnp.einsum(
        "qwp,up->qwu",
        probe_lowered_precision,
        encoder_lookup_probe,
        preferred_element_type=jnp.float32,
    )
    first_grad, gain_one, shift_one = first_back(first_total)
    self_branch_gradient = first_grad.astype(jnp.bfloat16)
    output_self_grad = jnp.einsum(
        "nhb,nhc->bc", attention_result, self_branch_gradient, preferred_element_type=jnp.float32
    )
    attended_grad = jnp.einsum(
        "qwp,up->qwu",
        self_branch_gradient,
        self_attention_output,
        preferred_element_type=jnp.float32,
    ).astype(jnp.bfloat16)
    self_query_reduced, decoder_label_lowered, self_value_reduced = row_map(
        local_backward, (query, keys, values, self_allowed, self_lse, attended_grad)
    )
    self_query_reduced = self_query_reduced.astype(jnp.bfloat16)
    decoder_label_lowered = decoder_label_lowered.astype(jnp.bfloat16)
    self_value_reduced = self_value_reduced.astype(jnp.bfloat16)
    query_self_grad = jnp.einsum(
        "nhb,nhc->bc", tokens, self_query_reduced, preferred_element_type=jnp.float32
    )
    key_self_grad = jnp.einsum(
        "nhb,nhc->bc", tokens, decoder_label_lowered, preferred_element_type=jnp.float32
    )
    value_self_grad = jnp.einsum(
        "nhb,nhc->bc", tokens, self_value_reduced, preferred_element_type=jnp.float32
    )
    input_grad = (
        ALPHA * first_grad
        + jnp.einsum(
            "qwp,up->qwu",
            self_query_reduced,
            self_attention_query,
            preferred_element_type=jnp.float32,
        )
        + jnp.einsum(
            "qwp,up->qwu",
            decoder_label_lowered,
            decoder_match_label,
            preferred_element_type=jnp.float32,
        )
        + jnp.einsum(
            "qwp,up->qwu",
            self_value_reduced,
            self_attention_value,
            preferred_element_type=jnp.float32,
        )
    )
    gain_grad = jnp.stack([gain_one, gain_two, gain_three], axis=1)
    shift_grad = jnp.stack([shift_one, shift_two, shift_three], axis=1)
    sums = (
        lax.psum_scatter(query_self_grad, ("rows", "mem"), scatter_dimension=0, tiled=True),
        lax.psum_scatter(key_self_grad, ("rows", "mem"), scatter_dimension=0, tiled=True),
        lax.psum_scatter(value_self_grad, ("rows", "mem"), scatter_dimension=0, tiled=True),
        lax.psum_scatter(output_self_grad, ("rows", "mem"), scatter_dimension=0, tiled=True),
        lax.psum_scatter(query_cross_grad, ("rows", "mem"), scatter_dimension=0, tiled=True),
        lax.psum_scatter(key_cross_grad, ("rows", "mem"), scatter_dimension=0, tiled=True),
        lax.psum_scatter(value_cross_grad, ("rows", "mem"), scatter_dimension=0, tiled=True),
        lax.psum_scatter(output_cross_grad, ("rows", "mem"), scatter_dimension=0, tiled=True),
        lax.psum_scatter(expand_grad, ("rows", "mem"), scatter_dimension=0, tiled=True),
        lax.psum_scatter(
            down_projection_gradient, ("rows", "mem"), scatter_dimension=0, tiled=True
        ),
        lax.psum_scatter(gain_grad, ("rows", "mem"), scatter_dimension=0, tiled=True),
        lax.psum_scatter(shift_grad, ("rows", "mem"), scatter_dimension=0, tiled=True),
    )
    return (
        result,
        input_grad,
        memory_grad,
        sums[0],
        sums[1],
        sums[2],
        sums[3],
        sums[4],
        sums[5],
        sums[6],
        sums[7],
        sums[8],
        sums[9],
        jnp.transpose(sums[10]),
        jnp.transpose(sums[11]),
    )


ALL = slice(None)
TILE = 256
SLOTS = 3
GATHER_SLOTS = 9
VMEM_LIMIT = 61 * 1024 * 1024


def flip(index, unit):
    return index + unit * (1 - 2 * ((index // unit) % 2))


def span(index, size):
    return pl.ds(pl.multiple_of(index * size, size), size)


class Place:
    def __init__(self, n_rows, n_mem):
        self.n_rows, self.n_mem = n_rows, n_mem
        self.digits = (n_rows // 2).bit_length() - 1
        self.row = lax.axis_index("rows")
        self.mem = lax.axis_index("mem")
        self.lane = self.row % 2

    def turn(self, index, stage):
        rising, falling = 2 << stage, 2 << (self.digits - 1 - stage)
        return flip(index, rising) * (1 - self.lane) + flip(index, falling) * self.lane

    def sibling(self):
        return (flip(self.row, 1), self.mem)

    def partner(self, stage):
        return (self.turn(self.row, stage), self.mem)

    def far(self, step):
        return (self.row, (self.mem + step) % self.n_mem)

    def others(self):
        found = [self.far(step) for step in range(1, self.n_mem)]
        found += [self.partner(stage) for stage in range(self.digits)]
        return found + [self.sibling()]

    def tell(self, semaphore):
        for other in self.others():
            pl.semaphore_signal(semaphore, inc=1, device_id=other, device_id_type=MESH)

    def hear(self, semaphore):
        pl.semaphore_wait(semaphore, len(self.others()))

    def greet(self):
        self.tell(pltpu.get_barrier_semaphore())
        self.hear(pltpu.get_barrier_semaphore())


def remote(source, target, send_sem, recv_sem, device):
    return pltpu.make_async_remote_copy(
        src_ref=source,
        dst_ref=target,
        send_sem=send_sem,
        recv_sem=recv_sem,
        device_id=device,
        device_id_type=MESH,
    )


def waits(total):
    return (lambda: total().wait_recv(), lambda: total().wait_send())


class Part:
    def __init__(self, source, target, near=0, straight=False):
        self.source, self.target = source, target
        self.near, self.straight = near, straight


class Gather:
    def __init__(self, place, parts, sems):
        self.place, self.parts = place, parts
        (
            self.own_sem,
            self.far_send,
            self.far_recv,
            self.plane_send,
            self.plane_recv,
            self.core_send,
            self.core_recv,
            self.line_send,
            self.line_recv,
        ) = sems

    def group(self, number, group):
        return self.parts[number].target.at[group]

    def one(self, number, group, member):
        return self.parts[number].target.at[group, member]

    def shard(self, number):
        return self.parts[number].source

    def mine(self, number):
        return self.one(number, self.place.row, self.place.mem)

    def own(self, number):
        return pltpu.make_async_copy(self.shard(number), self.mine(number), self.own_sem.at[number])

    def held(self, stage):
        groups = [self.place.row]
        for before in range(stage):
            groups = groups + [self.place.turn(group, before) for group in groups]
        return groups

    def far_total(self, number):
        part = self.parts[number]
        some = part.target.at[pl.ds(0, 1 << part.near), pl.ds(0, self.place.n_mem - 1)]
        return remote(
            some, some, self.far_send.at[number], self.far_recv.at[number], self.place.far(1)
        )

    def far_hop(self, number, first):
        place = self.place
        for group in self.held(self.parts[number].near):
            target = self.one(number, group, place.mem)
            source = self.shard(number) if first else target
            for step in range(1, place.n_mem):
                remote(
                    source,
                    target,
                    self.far_send.at[number],
                    self.far_recv.at[number],
                    place.far(step),
                ).start()

    def sides(self, step):
        mem, n_mem = self.place.mem, self.place.n_mem
        return (
            ((mem - step >= 0) & (mem + 1 < n_mem), mem - step, 1, mem - 1 - step >= 0),
            ((mem + step < n_mem) & (mem >= 1), mem + step, n_mem - 1, mem + 1 + step < n_mem),
        )

    def line_total(self, number, step, side):
        part, at = self.parts[number], 2 * step + side
        some = part.target.at[pl.ds(0, 1 << part.near), 0]
        sems = (self.line_send.at[at, number], self.line_recv.at[at, number])
        return remote(some, some, *sems, self.place.far(1))

    def line_arrived(self, number, step):
        for side, (_, _, _, receives) in enumerate(self.sides(step)):

            @pl.when(receives)
            def _(side=side):
                self.line_total(number, step, side).wait_recv()

    def line_sent(self, number, step):
        for side, (sends, _, _, _) in enumerate(self.sides(step)):

            @pl.when(sends)
            def _(side=side):
                self.line_total(number, step, side).wait_send()

    def line_hop(self, number, step, first):
        place = self.place
        for side, (sends, member, towards, _) in enumerate(self.sides(step)):
            member = (member + place.n_mem) % place.n_mem

            @pl.when(sends)
            def _(side=side, member=member, towards=towards):
                for group in self.held(self.parts[number].near):
                    target = self.one(number, group, member)
                    remote(
                        self.shard(number) if first else target,
                        target,
                        self.line_send.at[2 * step + side, number],
                        self.line_recv.at[2 * step + side, number],
                        place.far(towards),
                    ).start()

    def plane_total(self, number, stage):
        part = self.parts[number]
        some = part.target.at[pl.ds(0, 1 << stage)]
        if stage < part.near:
            some = part.target.at[pl.ds(0, 1 << stage), 0]
        return remote(
            some,
            some,
            self.plane_send.at[stage, number],
            self.plane_recv.at[stage, number],
            self.place.partner(stage),
        )

    def plane_hop(self, number, stage, first):
        for group in self.held(stage):
            if stage < self.parts[number].near:
                target = self.one(number, group, self.place.mem)
            else:
                target = self.group(number, group)
            remote(
                self.shard(number) if first else target,
                target,
                self.plane_send.at[stage, number],
                self.plane_recv.at[stage, number],
                self.place.partner(stage),
            ).start()

    def core_total(self, number):
        some = self.parts[number].target.at[pl.ds(0, self.place.n_rows // 2)]
        return remote(
            some, some, self.core_send.at[number], self.core_recv.at[number], self.place.sibling()
        )

    def core_hop(self, number, first):
        for group in self.held(self.place.digits):
            block = self.group(number, group)
            remote(
                block,
                block,
                self.core_send.at[number],
                self.core_recv.at[number],
                self.place.sibling(),
            ).start()

    def hops(self, number):
        part, take = self.parts[number], functools.partial
        along = []
        if part.straight:
            along.append((1.6, take(self.far_hop, number)) + waits(take(self.far_total, number)))
        else:
            for step in range(self.place.n_mem - 1):
                along.append(
                    (
                        0.55 if step else 1.4,
                        take(self.line_hop, number, step),
                        take(self.line_arrived, number, step),
                        take(self.line_sent, number, step),
                    )
                )
        plane = []
        for stage in range(self.place.digits):
            total = take(self.plane_total, number, stage)
            plane.append((1.5, take(self.plane_hop, number, stage)) + waits(total))
        core = (1.5, take(self.core_hop, number)) + waits(take(self.core_total, number))
        return plane[: part.near] + along + plane[part.near :] + [core]

    def events(self, number):
        hops = self.hops(number)
        time, found = float(number), []

        def act(at):
            if at == 0:
                self.own(number).start()
            else:
                if at == 1:
                    self.own(number).wait()
                hops[at - 1][2]()
            hops[at][1](at == 0)

        for at in range(len(hops)):
            time += hops[at][0] if at else 0.0
            found.append((time, functools.partial(act, at)))
        return found, time + 0.9

    def sent(self, number):
        for hop in self.hops(number):
            hop[3]()


class Job:
    def __init__(self, left, right, first, target, early=False):
        self.left, self.right, self.first, self.target = left, right, first, target
        self.small = right is None
        self.early = early
        self.width = target.shape[-1]
        self.large = self.at = 0


OUT_SLOTS, LANE_SLOTS, SUM_SLOTS, CORE_RING, FIRST_RING, RING, EARLY_RING = 2, 3, 2, 2, 6, 4, 3


class Reduce:
    def __init__(self, place, jobs, sems, pool, small):
        self.place, self.jobs, self.small = place, jobs, small
        (
            self.core_send,
            self.core_recv,
            self.stage_send,
            self.stage_recv,
            self.line_send_sem,
            self.line_recv_sem,
        ) = sems
        self.last = place.digits - 1
        self.waited = set()
        wanted = [place.row]
        for stage in reversed(range(place.digits)):
            wanted = wanted + [place.turn(group, stage) for group in wanted]
        self.wanted = [group // 2 for group in wanted]
        large = [job for job in jobs if not job.small]
        for number, job in enumerate(large):
            job.large = number
            job.at = [item for item in large if item.early == job.early].index(job)
        used, half = [0], place.n_rows // 2

        def take(count, units):
            first = used[0]
            used[0] += count * units
            return [pool.at[pl.ds(first + i * units, units)] for i in range(count)]

        self.outs = take(OUT_SLOTS, half)
        self.lane_slots = take(LANE_SLOTS, half)
        self.core_ring = take(CORE_RING, half)
        self.sum_slots, self.rings = [], []
        for stage in range(place.digits):
            self.sum_slots.append(take(SUM_SLOTS, self.count(stage)))
            self.rings.append(take(RING if stage else FIRST_RING, self.count(stage)))
        self.line_ring = take(RING, 2)
        self.early_line_ring = take(EARLY_RING, 4)
        self.early_sums = take(1, SUM_SLOTS)[0]
        self.early_ring = take(1, 1)[0]

    def count(self, stage):
        return self.place.n_rows // 4 >> stage

    def cut(self, ref, job):
        if job.width == ref.shape[-1]:
            return ref
        return ref.at[(ALL,) * (len(ref.shape) - 1) + (pl.ds(0, job.width),)]

    def out(self, job):
        return self.cut(self.outs[job.large % OUT_SLOTS], job)

    def lanes(self, job):
        if job.small:
            return self.small.lanes
        return self.cut(self.lane_slots[job.large % LANE_SLOTS], job)

    def core_in(self, job):
        if job.small:
            return self.small.core_in
        return self.cut(self.core_ring[job.large % CORE_RING], job)

    def sums(self, job, stage):
        if job.small:
            return self.small.sums[stage]
        number = job.at if stage == self.last else job.large
        return self.cut(self.sum_slots[stage][number % SUM_SLOTS], job)

    def arrived(self, job, stage):
        if job.small:
            return self.small.arrived[stage]
        if job.early and stage == self.last:
            return self.cut(self.early_ring.at[0, pl.ds(job.at % self.place.n_mem, 1)], job)
        ring = self.rings[stage]
        number = job.at if stage == self.last else job.large
        return self.cut(ring[number % len(ring)], job)

    def line_units(self, job):
        return 2 if job.early else 1

    def line_in(self, job):
        ring = self.early_line_ring if job.early else self.line_ring
        return self.cut(ring[job.at % len(ring)], job)

    def early_sum(self, job):
        return self.cut(self.early_sums.at[job.at % SUM_SLOTS, pl.ds(0, 2)], job)

    def previous(self, number, distance, plain_only=False, early_only=False):
        found = [
            n
            for n in range(number)
            if not self.jobs[n].small
            and not (plain_only and self.jobs[n].early)
            and not (early_only and not self.jobs[n].early)
        ]
        return found[-distance] if len(found) >= distance else None

    def once(self, key, wait):
        if key not in self.waited:
            self.waited.add(key)
            wait()

    def core_sent(self, number):
        self.once((number, -2), lambda: self.core_copy(number).wait_send())

    def line_sent(self, number):
        def wait():
            for step in range(self.place.n_mem - 1):
                for side, (sends, _, _, _, _) in enumerate(self.ways(step)):

                    @pl.when(sends)
                    def _(step=step, side=side):
                        self.line_total(number, step, side).wait_send()

        self.once((number, -3), wait)

    def stage_sent(self, number, stage):
        self.once((number, stage), lambda: self.total(number, stage).wait_send())

    def next_sent(self, number, stage):
        job = self.jobs[number]
        if not job.small and stage == self.last - job.early:
            self.line_sent(number)
        else:
            self.stage_sent(number, stage + 1)

    def core_copy(self, number):
        job = self.jobs[number]
        source = job.left.at[1 - self.place.lane] if job.small else self.out(job)
        return remote(
            source,
            self.core_in(job),
            self.core_send.at[number],
            self.core_recv.at[number],
            self.place.sibling(),
        )

    def product(self, job, side, store):
        half = self.place.n_rows // 2
        group = job.left.shape[1] // half
        width = min(TILE, job.width)
        unit = (self.place.n_mem, group // self.place.n_mem, width)

        def column_step(step, carry):
            source = pl.ds(pl.multiple_of(job.first + step * width, width), width)
            value = dot(job.left[side], job.right[:, source])
            for index in range(half):
                block = value[index * group : (index + 1) * group].reshape(unit)
                store(index, span(step, width), block)
            return carry

        lax.fori_loop(0, job.width // width, column_step, 0)

    def core_stage(self, number):
        job = self.jobs[number]
        if not job.small:
            before = self.previous(number, OUT_SLOTS)
            if before is not None:
                self.core_sent(before)
            out = self.out(job)

            def store(index, columns, value):
                out[index, :, :, columns] = value.astype(out.dtype)

            self.product(job, 1 - self.place.lane, store)
        self.core_copy(number).start()

    def lane_stage(self, number):
        job = self.jobs[number]
        if not job.small:
            before = self.previous(number, LANE_SLOTS)
            if before is not None:
                self.next_sent(before, -1)
        lanes, arrived = self.lanes(job), self.core_in(job)
        self.core_copy(number).wait_recv()
        if job.small:
            lanes[...] = job.left[self.place.lane] + arrived[...]
        else:

            def store(index, columns, value):
                total = value + arrived[index, :, :, columns].astype(jnp.float32)
                lanes[index, :, :, columns] = total.astype(lanes.dtype)

            self.product(job, self.place.lane, store)
        self.pass_on(number, -1)

    def unit(self, job, stage, index):
        if stage < 0:
            return self.lanes(job).at[self.wanted[index]]
        return self.sums(job, stage).at[index]

    def pass_on(self, number, stage):
        job, place = self.jobs[number], self.place
        if not job.small and stage == self.last - job.early:
            self.line_step(number, 0)
            return
        arrived = self.arrived(job, stage + 1)
        sems = (self.stage_send.at[stage + 1, number], self.stage_recv.at[stage + 1, number])
        if stage == self.last:
            for step in range(1, place.n_mem):
                source = self.unit(job, stage, 0)
                remote(source, arrived.at[step - 1], *sems, place.far(step)).start()
            return
        left = self.count(stage + 1)
        for index in range(left):
            source = self.unit(job, stage, left + index)
            remote(source, arrived.at[index], *sems, place.partner(stage + 1)).start()

    def total(self, number, stage):
        some = self.arrived(self.jobs[number], stage)
        sems = (self.stage_send.at[stage, number], self.stage_recv.at[stage, number])
        return remote(some, some, *sems, self.place.far(1))

    def plane_stage(self, number, stage):
        job, place = self.jobs[number], self.place
        if not job.small:
            before = self.previous(number, SUM_SLOTS, plain_only=stage == self.last)
            if before is not None:
                self.next_sent(before, stage)
        self.total(number, stage).wait_recv()
        arrived, sums = self.arrived(job, stage), self.sums(job, stage)
        for index in range(self.count(stage)):
            unit, coming, target = self.unit(job, stage - 1, index), arrived.at[index], sums.at[index]
            if job.small:
                target[...] = unit[...] + coming[...]
                continue

            def add(member, carry, unit=unit, coming=coming, target=target):
                value = unit[member].astype(jnp.float32) + coming[member].astype(jnp.float32)
                target[member] = value.astype(target.dtype)
                return carry

            lax.fori_loop(0, place.n_mem, add, 0)
        self.pass_on(number, stage)

    def small_end(self, number):
        job = self.jobs[number]
        self.total(number, self.last + 1).wait_recv()
        value = self.unit(job, self.last, 0)[...]
        for step in range(self.place.n_mem - 1):
            value = value + self.small.arrived[self.last + 1][step]
        job.target[...] = value

    def ways(self, step):
        mem, n_mem = self.place.mem, self.place.n_mem
        down = step + mem - (n_mem - 1)
        return (
            (down >= 0, down, n_mem - 1, mem == n_mem - 1, (mem < n_mem - 1) & (down >= -1)),
            (step >= mem, n_mem - 1 - step + mem, 1, mem == 0, (mem > 0) & (step >= mem - 1)),
        )

    def line_total(self, number, step, side):
        job = self.jobs[number]
        units, at = self.line_units(job), 2 * step + side
        some = self.line_in(job).at[pl.ds(side * units, units), step]
        sems = (self.line_send_sem.at[at, number], self.line_recv_sem.at[at, number])
        return remote(some, some, *sems, self.place.far(1))

    def line_step(self, number, step):
        job, place = self.jobs[number], self.place
        units, line = self.line_units(job), self.line_in(job)
        left = self.last - job.early
        for side, (sends, member, towards, first, _) in enumerate(self.ways(step)):
            member = (member + place.n_mem) % place.n_mem
            at = 2 * step + side
            sems = (self.line_send_sem.at[at, number], self.line_recv_sem.at[at, number])

            def send(index, source, side=side, sems=sems, towards=towards):
                remote(source, line.at[side * units + index, step], *sems, place.far(towards)).start()

            @pl.when(sends & first)
            def _(member=member, send=send):
                for index in range(units):
                    send(index, self.unit(job, left, index).at[member])

            if step == 0:
                continue

            @pl.when(sends & jnp.logical_not(first))
            def _(side=side, member=member, send=send):
                self.line_total(number, step - 1, side).wait_recv()
                for index in range(units):
                    coming = line.at[side * units + index, step - 1]
                    own = self.unit(job, left, index).at[member]
                    value = coming[...].astype(jnp.float32) + own[...].astype(jnp.float32)
                    coming[...] = value.astype(coming.dtype)
                    send(index, coming)

    def line_end(self, number):
        job, place = self.jobs[number], self.place
        units, line = self.line_units(job), self.line_in(job)
        left = self.last - job.early
        step = place.n_mem - 2
        if job.early:
            before = self.previous(number, SUM_SLOTS, early_only=True)
            if before is not None:
                self.stage_sent(before, self.last)
            target = self.early_sum(job)
        else:
            target = job.target
        for index in range(units):
            total = target.at[index] if job.early else target
            total[...] = self.unit(job, left, index).at[place.mem][...].astype(total.dtype)
        for side, (_, _, _, _, receives) in enumerate(self.ways(step)):

            @pl.when(receives)
            def _(side=side):
                self.line_total(number, step, side).wait_recv()
                for index in range(units):
                    total = target.at[index] if job.early else target
                    coming = line.at[side * units + index, step]
                    value = total[...].astype(jnp.float32) + coming[...].astype(jnp.float32)
                    total[...] = value.astype(total.dtype)

        if job.early:
            sems = (self.stage_send.at[self.last, number], self.stage_recv.at[self.last, number])
            arrived = self.arrived(job, self.last)
            remote(target.at[1], arrived.at[0], *sems, place.partner(self.last)).start()

    def early_end(self, number):
        job = self.jobs[number]
        self.total(number, self.last).wait_recv()
        mine, coming = self.early_sum(job).at[0], self.arrived(job, self.last).at[0]
        job.target[...] = mine[...].astype(jnp.float32) + coming[...].astype(jnp.float32)

    def events(self, number):
        job, take = self.jobs[number], functools.partial
        found = [(0.0, take(self.core_stage, number)), (0.9, take(self.lane_stage, number))]
        time = 2.2 if number < 3 else 3.2
        for stage in range(self.last + 1 - job.early):
            found.append((time, take(self.plane_stage, number, stage)))
            time += 1.4
        if job.small:
            found.append((time, take(self.small_end, number)))
            return [(number + at, action) for at, action in found]
        time -= 0.8
        for step in range(1, self.place.n_mem - 1):
            found.append((time, take(self.line_step, number, step)))
            time += 0.6
        found.append((time, take(self.line_end, number)))
        if job.early:
            found.append((time + 1.4, take(self.early_end, number)))
        return [(number + at, action) for at, action in found]

    def finish(self):
        for number, job in enumerate(self.jobs):
            self.core_sent(number)
            for stage in range(self.last + 1):
                self.stage_sent(number, stage)
            if job.small:
                self.stage_sent(number, self.last + 1)
            else:
                self.line_sent(number)


NORMAL = (((1,), (0,)), ((), ()))
TURNED = (((1,), (1,)), ((), ()))
LEFT_TURNED = (((0,), (0,)), ((), ()))


def dot(left, right, dims=NORMAL):
    return lax.dot_general(left, right, dims, preferred_element_type=jnp.float32)


def times(left, weight, store, part=0, parts=1):
    size = weight.shape[-1]
    width = min(TILE, size)
    tiles = size // width // parts

    def column_step(step, carry):
        columns = span(step, width)
        store(columns, dot(left[...], weight[:, :, :, columns].reshape(-1, width)))
        return carry

    lax.fori_loop(part * tiles, (part + 1) * tiles, column_step, 0)


def times_turned(left, weight, store):
    unit = weight.shape[1] * weight.shape[2]
    units = max(TILE // unit, 1)

    def row_step(step, carry):
        rows = weight[span(step, units)].reshape(units * unit, weight.shape[-1])
        store(span(step, units * unit), dot(left[...], rows, TURNED))
        return carry

    lax.fori_loop(0, weight.shape[0] // units, row_step, 0)


def into(target):
    def store(columns, value):
        target[:, columns] = value.astype(target.dtype)

    return store


ROWS = 32


def by_rows(count, step):
    def body(index, carry):
        step(span(index, ROWS))
        return carry

    lax.fori_loop(0, count // ROWS, body, 0)


def norm_forward(total, gains, index, unit, scale, use):
    gain, shift = gains[index : index + 1, :], gains[index + 3 : index + 4, :]

    def step(rows):
        value = total[rows, :]
        centre = value - jnp.mean(value, axis=-1, keepdims=True)
        spread = jnp.mean(centre * centre, axis=-1, keepdims=True)
        root = lax.rsqrt(spread + EPS)
        scaled = centre * root
        unit[rows, :] = scaled
        scale[rows, :] = root
        use(rows, scaled * gain + shift)

    by_rows(total.shape[0], step)


def norm_slope(incoming, scaled, root, gain):
    width = scaled.shape[1]
    scaled_grad = incoming * gain
    first = jnp.mean(scaled_grad, axis=-1, keepdims=True)
    second = jnp.mean(scaled_grad * scaled, axis=-1, keepdims=True)
    value = root * (scaled_grad - first - scaled * second)
    of_gain = jnp.sum((incoming * scaled).reshape(ROWS // 8, 8, width), axis=0)
    of_shift = jnp.sum(incoming.reshape(ROWS // 8, 8, width), axis=0)
    return value, of_gain, of_shift


def keep_small(index, sums, small):
    for offset, partial in ((index, sums[0]), (index + 3, sums[1])):
        line = jnp.sum(partial, axis=0, keepdims=True)
        for group in range(2 * small.shape[1]):
            small[group % 2, group // 2, offset : offset + 1, :] = line[
                :, group * 128 : (group + 1) * 128
            ]


def norm_backward(grad, gains, index, unit, scale, target, target_low, small):
    gain = gains[index : index + 1, :]

    def body(block, sums):
        rows = span(block, ROWS)
        value, of_gain, of_shift = norm_slope(grad[rows, :], unit[rows, :], scale[rows, :], gain)
        target[rows, :] = value
        target_low[rows, :] = value.astype(target_low.dtype)
        return (sums[0] + of_gain, sums[1] + of_shift)

    zero = jnp.zeros((8, unit.shape[1]), jnp.float32)
    keep_small(index, lax.fori_loop(0, unit.shape[0] // ROWS, body, (zero, zero)), small)


def norm_both(total, grad, gains, index, result, target, target_low, small):
    gain, shift = gains[index : index + 1, :], gains[index + 3 : index + 4, :]

    def body(block, sums):
        rows = span(block, ROWS)
        value = total[rows, :]
        centre = value - jnp.mean(value, axis=-1, keepdims=True)
        spread = jnp.mean(centre * centre, axis=-1, keepdims=True)
        root = lax.rsqrt(spread + EPS)
        scaled = centre * root
        result[rows, :] = scaled * gain + shift
        incoming = grad[rows, :].astype(jnp.float32)
        value, of_gain, of_shift = norm_slope(incoming, scaled, root, gain)
        target[rows, :] = value
        target_low[rows, :] = value.astype(target_low.dtype)
        return (sums[0] + of_gain, sums[1] + of_shift)

    zero = jnp.zeros((8, total.shape[1]), jnp.float32)
    keep_small(index, lax.fori_loop(0, total.shape[0] // ROWS, body, (zero, zero)), small)


def lane_masks(dtype, scale):
    low = lax.broadcasted_iota(jnp.int32, (1, 2 * HEAD_DIM), 1) < HEAD_DIM
    first = jnp.where(low, scale, 0.0)
    return first.astype(dtype), (scale - first).astype(dtype)


def turned_pair(eye, rows):
    size = rows.shape[1]
    return dot(eye[0:size, 0:size], rows, TURNED).astype(rows.dtype)


def attention_forward(query, keys, values, bias, blocks, eye, mixed, turned, lse, first, last):
    masks = lane_masks(query.dtype, SCALE)

    def pair_step(pair, carry):
        lanes = span(pair, 2 * HEAD_DIM)
        two_query, two_keys, two_values = query[:, lanes], keys[:, lanes], values[:, lanes]
        columns = []
        for q0, q1, k0, k1 in blocks:
            block_values = turned_pair(eye, two_values[k0:k1])
            rows = []
            for head in range(2):
                scores = dot(two_keys[k0:k1], two_query[q0:q1] * masks[head], TURNED)
                scores = scores + bias[k0:k1, q0:q1]
                top = jnp.max(scores, axis=0, keepdims=True)
                weight = jnp.exp(scores - top)
                norm = jnp.sum(weight, axis=0, keepdims=True)
                head_values = block_values[head * HEAD_DIM : (head + 1) * HEAD_DIM]
                rows.append(dot(head_values, weight.astype(query.dtype)) * (1.0 / norm))
                lse[pair, head : head + 1, q0:q1] = top + jnp.log(norm)
            columns.append(jnp.concatenate(rows, axis=0))
        total = jnp.concatenate(columns, axis=1).astype(mixed.dtype)
        turned[pair % 2, span(pair // 2, 2 * HEAD_DIM), :] = total
        mixed[:, lanes] = dot(eye[...], total, TURNED).astype(mixed.dtype)
        return carry

    lax.fori_loop(first, last, pair_step, 0)


def stacked(parts):
    cuts = sorted({at for first, value in parts for at in (first, first + value.shape[0])})
    found = []
    for low, high in zip(cuts, cuts[1:]):
        total = None
        for first, value in parts:
            if first <= low and high <= first + value.shape[0]:
                piece = value[low - first : high - first]
                total = piece if total is None else total + piece
        found.append(total)
    return jnp.concatenate(found, axis=0)


def attention_backward(
    query, keys, values, bias, blocks, eye, lse, grad, query_grad, key_grad, value_grad, first, last
):
    scaled, masks = lane_masks(query.dtype, SCALE), lane_masks(query.dtype, 1.0)

    def pair_step(pair, carry):
        lanes = span(pair, 2 * HEAD_DIM)
        two_query, two_keys, two_values = query[:, lanes], keys[:, lanes], values[:, lanes]
        two_grad = grad[:, lanes]
        of_query, of_keys, of_values = [], [], []
        for q0, q1, k0, k1 in blocks:
            block_keys, block_values = two_keys[k0:k1], two_values[k0:k1]
            slopes, all_probs, heads_query, heads_grad = [], [], [], []
            for head in range(2):
                head_query = two_query[q0:q1] * scaled[head]
                head_grad = two_grad[q0:q1] * masks[head]
                scores = dot(block_keys, head_query, TURNED) + bias[k0:k1, q0:q1]
                probs = jnp.exp(scores - lse[pair, head : head + 1, q0:q1])
                pulled = dot(block_values, head_grad, TURNED)
                inner = jnp.sum(probs * pulled, axis=0, keepdims=True)
                slopes.append((probs * (pulled - inner)).astype(query.dtype))
                all_probs.append(probs.astype(query.dtype))
                heads_query.append(head_query)
                heads_grad.append(head_grad)
            both = jnp.concatenate(slopes, axis=1)
            of_keys.append((k0, dot(both, jnp.concatenate(heads_query, axis=0))))
            both = jnp.concatenate(all_probs, axis=1)
            of_values.append((k0, dot(both, jnp.concatenate(heads_grad, axis=0))))
            block_turned = turned_pair(eye, block_keys * jnp.asarray(SCALE, query.dtype))
            rows = [
                dot(block_turned[head * HEAD_DIM : (head + 1) * HEAD_DIM], slopes[head])
                for head in range(2)
            ]
            of_query.append(jnp.concatenate(rows, axis=0))
        total = jnp.concatenate(of_query, axis=1).astype(query_grad.dtype)
        query_grad[:, lanes] = dot(eye[...], total, TURNED).astype(query_grad.dtype)
        key_grad[:, lanes] = stacked(of_keys).astype(key_grad.dtype)
        value_grad[:, lanes] = stacked(of_values).astype(value_grad.dtype)
        return carry

    lax.fori_loop(first, last, pair_step, 0)


def turn_blocks(left, eye, store):
    width = eye.shape[0]
    for block in range(left.shape[1] // width):
        columns = pl.ds(block * width, width)
        store(block, dot(eye[...], left[:, columns], TURNED).astype(left.dtype))


def turn_by_lane(left, eye, target):
    group = eye.shape[0] // 2

    def store(block, value):
        target[0, pl.ds(block * group, group), :] = value[:group]
        target[1, pl.ds(block * group, group), :] = value[group:]

    turn_blocks(left, eye, store)


SQUARES = 8


def layer_kernel(places, sizes, *refs):
    n_rows, n_mem, width, ff, shard = sizes
    ref = SimpleNamespace(**jax.tree.map(lambda place: refs[place], places))
    place = Place(n_rows, n_mem)
    many = ff // width
    own_ff = ff // (n_rows * n_mem)
    (
        at_query,
        at_key,
        at_value,
        at_output,
        at_cross_query,
        at_cross_key,
        at_cross_value,
        at_cross_output,
    ) = range(SQUARES)
    full = ref.full
    expand, contract = ref.expand_full, ref.contract_full
    tokens, gains = ref.tokens, ref.gains
    low, turned = SimpleNamespace(**ref.low), SimpleNamespace(**ref.turned)

    order = [
        at_query,
        at_key,
        at_value,
        at_output,
        at_cross_key,
        at_cross_value,
        at_cross_query,
        at_cross_output,
    ]
    pool = ref.pool

    def gather_slot(number):
        return pool.at[pl.ds(number % GATHER_SLOTS * n_rows, n_rows)]

    sources = [ref.squares[index] for index in order]
    sources += [ref.expand.at[:, pl.ds(j * width, width)] for j in range(many)]
    sources += [ref.contract.at[pl.ds(j * shard, shard), :] for j in range(many)]
    stores = [full[index] for index in order] + [expand.at[j] for j in range(many)]
    stores += [contract.at[:, :, j] for j in range(many)]
    parts, cuts = [], []
    for n, item in enumerate(sources):
        pieces_here = 2 if n == 0 else width // TILE if n == len(sources) - 1 else 1
        for i in range(pieces_here):
            size = width // pieces_here
            columns = pl.ds(i * size, size)
            near = i if n == 0 else int(n % 5 in (1, 3))
            parts.append(
                Part(item.at[:, columns], gather_slot(n).at[:, :, :, columns], near)
            )
            cuts.append((n, i, pieces_here))
    parts.insert(SMALL_AT, Part(ref.small, ref.small_full, 0, True))
    cuts.insert(SMALL_AT, None)
    gather = Gather(place, parts, ref.gather_sems)

    def keep(number):
        return pltpu.make_async_copy(gather_slot(number), stores[number], ref.keep_sem.at[number])

    count = [0]

    def load_slot(number):
        first = pool.shape[0] - (1 + number % SLOTS) * n_rows
        return pool.at[pl.ds(first, n_rows)]

    def load(pieces):
        number = count[0]
        count[0] += 1
        for source, first, rows in pieces:
            target = load_slot(number).at[pl.ds(first, rows)]
            pltpu.make_async_copy(source, target, ref.slot_sem.at[number % SLOTS]).start()
        return number

    def ready(number):
        slot = load_slot(number)
        pltpu.make_async_copy(slot, slot, ref.slot_sem.at[number % SLOTS]).wait()
        return slot

    def contract_rows(j):
        groups = n_rows // many
        return [(contract.at[j * groups + i], i * n_mem, n_mem) for i in range(groups)]

    mem_block = ref.memory.shape[1]
    memory, mem_rows = ref.memory, ref.mem_rows

    def memory_own():
        return pltpu.make_async_copy(
            memory.at[place.mem], mem_rows.at[span(place.mem, mem_block)], ref.mem_sem.at[0]
        )

    def memory_total():
        some = mem_rows.at[pl.ds(0, (n_mem - 1) * mem_block)]
        return remote(some, some, ref.mem_sem.at[1], ref.mem_sem.at[2], place.far(1))

    ref.small[...] = jnp.zeros_like(ref.small)
    for member in range(n_mem):

        @pl.when(place.mem == member)
        def _(member=member):
            lanes = slice(member * shard, (member + 1) * shard)
            ref.small[0:3, lanes] = ref.norm_gains[...].astype(jnp.float32)
            ref.small[3:6, lanes] = ref.norm_shifts[...].astype(jnp.float32)

    place.greet()
    memory_own().start()
    for step in range(1, n_mem):
        remote(
            memory.at[(place.mem + step) % n_mem],
            mem_rows.at[span(place.mem, mem_block)],
            ref.mem_sem.at[1],
            ref.mem_sem.at[2],
            place.far(step),
        ).start()

    actions, whole = [], []
    for part in range(len(parts)):
        found, time = gather.events(part)
        for hop, (at, action) in enumerate(found):
            actions.append((HOP + 10 * part + hop, at, action))
        whole.append(time)
    first_hops = [HOP, HOP + 10]
    for code, _, action in actions:
        if code in first_hops:
            action()
    actions = [item for item in actions if item[0] not in first_hops]

    self_bias, cross_bias, eye = ref.self_bias, ref.cross_bias, ref.eye
    own_row = ref.token_ids[pl.ds(place.mem, 1), :].astype(jnp.float32)
    mem_row = ref.memory_ids[pl.ds(place.mem, 1), :].astype(jnp.float32)
    key_place = lax.broadcasted_iota(jnp.int32, self_bias.shape, 0)
    query_place = lax.broadcasted_iota(jnp.int32, self_bias.shape, 1)
    own_wide = jnp.broadcast_to(own_row, self_bias.shape)
    mem_wide = jnp.broadcast_to(mem_row, (cross_bias.shape[1], cross_bias.shape[0]))
    same = (jnp.transpose(own_wide) == own_wide) & (key_place <= query_place)
    self_bias[...] = jnp.where(same, 0.0, NEG)
    cross_bias[...] = jnp.where(jnp.transpose(mem_wide) == own_row, 0.0, NEG)
    eye_row = lax.broadcasted_iota(jnp.int32, eye.shape, 0)
    eye_column = lax.broadcasted_iota(jnp.int32, eye.shape, 1)
    eye[...] = jnp.where(eye_row == eye_column, 1.0, 0.0).astype(eye.dtype)
    turn_by_lane(tokens, eye, turned.tokens)

    accumulated, other = ref.accumulated, ref.other
    hidden, slope, hidden_turned = ref.hidden, ref.slope, ref.hidden_turned

    def small_piece():
        blocks = ref.small_full
        for group in range(n_rows):
            total = None
            for member in range(n_mem):
                value = blocks[group, member]
                total = value if total is None else total + value
            gains[:, group * 128 : (group + 1) * 128] = total

    def query_piece(i, count, slot):
        times(tokens, slot, into(ref.query), i, count)

    def key_piece(slot):
        times(tokens, slot, into(ref.keys))

    pairs = width // (2 * HEAD_DIM)
    self_blocks = [
        (first, first + 128, max(first - DOC_LIMIT, 0), first + 128)
        for first in range(0, self_bias.shape[1], 128)
    ]
    cross_blocks = [(0, cross_bias.shape[1], 0, cross_bias.shape[0])]

    def value_piece(slot):
        times(tokens, slot, into(ref.values))

    def self_forward(first, last, slot):
        attention_forward(
            ref.query,
            ref.keys,
            ref.values,
            self_bias,
            self_blocks,
            eye,
            ref.attended,
            turned.attended,
            ref.self_lse,
            first,
            last,
        )

    def output_piece(slot):
        def store(columns, value):
            accumulated[:, columns] = ALPHA * tokens[:, columns].astype(jnp.float32) + value

        times(ref.attended, slot, store)

    def output_norm(slot):
        def use(rows, value):
            ref.first_low[rows, :] = value.astype(jnp.bfloat16)
            other[rows, :] = value

        norm_forward(accumulated, gains, 0, ref.unit1, ref.scale1, use)

    def cross_key_piece(slot):
        memory_own().wait()
        memory_total().wait_recv()
        times(mem_rows, slot, into(ref.cross_keys))
        turn_by_lane(mem_rows, eye, turned.memory)

    def cross_value_piece(slot):
        times(mem_rows, slot, into(ref.cross_values))
        turn_by_lane(ref.first_low, eye, turned.first)

    def cross_query_piece(slot):
        times(ref.first_low, slot, into(ref.cross_query))

    def cross_forward(first, last, slot):
        attention_forward(
            ref.cross_query,
            ref.cross_keys,
            ref.cross_values,
            cross_bias,
            cross_blocks,
            eye,
            ref.crossed,
            turned.crossed,
            ref.cross_lse,
            first,
            last,
        )

    def cross_output_piece(slot):
        def store(columns, value):
            accumulated[:, columns] = ALPHA * other[:, columns] + value

        times(ref.crossed, slot, store)

    def cross_output_norm(slot):
        def use(rows, value):
            ref.second_low[rows, :] = value.astype(jnp.bfloat16)
            other[rows, :] = value

        norm_forward(accumulated, gains, 1, ref.unit2, ref.scale2, use)

    def expand_piece(j, half, slot):
        def store(columns, value):
            there = pl.ds(pl.multiple_of(j * width + columns.start, TILE), columns.size)
            bell = 0.5 * (1.0 + lax.erf(value * math.sqrt(0.5)))
            density = jnp.exp(value * value * -0.5) * (1.0 / math.sqrt(2.0 * math.pi))
            hidden[:, there] = (value * bell).astype(hidden.dtype)
            slope[:, there] = (bell + value * density).astype(slope.dtype)

        times(ref.second_low, slot, store, half, 2)

    def expand_turn(j, slot):
        def keep(block, value):
            for index in range(value.shape[0] // shard):
                first = j * width + block * value.shape[0] + index * shard
                device, job = first // own_ff, first % own_ff // shard
                group, member = device // n_mem, device % n_mem
                at = group // 2 * n_mem * shard + member * shard
                hidden_turned[job, group % 2, at : at + shard, :] = value[
                    index * shard : (index + 1) * shard
                ]

        turn_blocks(hidden.at[:, pl.ds(j * width, width)], eye, keep)

    def contract_turn(j):
        block = 2 * n_mem * shard
        for index in range(n_rows // 2):
            rows = pl.ds(index * n_mem * shard, n_mem * shard)
            both = jnp.concatenate([hidden_turned[j, 0, rows], hidden_turned[j, 1, rows]], axis=0)
            columns = pl.ds(index * block, block)
            low.branch[:, columns] = dot(eye[...], both, TURNED).astype(jnp.bfloat16)

    def contract_piece(j, i, count, slot):
        if i == 0:
            contract_turn(j)

        def store(columns, value):
            if j == 0:
                accumulated[:, columns] = ALPHA * other[:, columns] + value
            else:
                accumulated[:, columns] = accumulated[:, columns] + value

        times(low.branch, slot, store, i, count)

    quarters = [(pairs * at // 4, pairs * (at + 1) // 4) for at in range(4)]
    whole_pieces = [
        [],
        [key_piece],
        [value_piece] + [functools.partial(self_forward, *quarter) for quarter in quarters],
        [output_piece, output_norm],
        [cross_key_piece],
        [cross_value_piece],
        [cross_query_piece] + [functools.partial(cross_forward, *quarter) for quarter in quarters],
        [cross_output_piece, cross_output_norm],
    ]
    for j in range(many):
        halves = [functools.partial(expand_piece, j, half) for half in range(2)]
        whole_pieces.append(halves + [functools.partial(expand_turn, j)])

    def pieces_of(part):
        if part == SMALL_AT:
            return [small_piece]
        n, i, count = cuts[part]
        found = whole_pieces[n] if n < len(whole_pieces) else []
        if n == 0:
            found = [functools.partial(query_piece, i, count)]
        elif n >= len(whole_pieces):
            found = [functools.partial(contract_piece, n - len(whole_pieces), i, count)]
        return [functools.partial(piece, gather_slot(n)) for piece in found]

    def ends_weight(part):
        return part != SMALL_AT and cuts[part][1] == cuts[part][2] - 1

    def arrive(part):
        gather.core_total(part).wait_recv()
        if ends_weight(part):
            keep(cuts[part][0]).start()

    def settle(part):
        gather.sent(part)
        if ends_weight(part):
            keep(cuts[part][0]).wait()

    last = 0.0
    for part, time in enumerate(whole):
        time = max(time, last + 0.5)
        actions.append((ARRIVE + part, time, functools.partial(arrive, part)))
        for index, piece in enumerate(pieces_of(part)):
            actions.append((USE + 10 * part + index, time + 0.2 + 0.04 * index, piece))
        actions.append((SETTLE + part, time + 0.45, functools.partial(settle, part)))
        last = time
    for action in planned(actions, FORWARD_PLAN):
        action()
    place.tell(ref.ready_sem)

    backward_sources, loads = [], []
    used = [0]

    def next_slot():
        slot = ready(loads[used[0]])
        used[0] += 1
        if len(loads) < len(backward_sources):
            loads.append(load(backward_sources[len(loads)]))
        return slot

    small_sums = ref.small_sums
    small_sums[...] = jnp.zeros_like(small_sums)
    def inner_piece(j):
        slot = next_slot()

        def store(columns, value):
            there = pl.ds(pl.multiple_of(j * width + columns.start, TILE), columns.size)
            slope[:, there] = (value * slope[:, there].astype(jnp.float32)).astype(slope.dtype)

        times_turned(low.third, slot, store)

    def second_piece(j):
        slot = next_slot()

        def store(columns, value):
            if j == 0:
                other[:, columns] = ALPHA * accumulated[:, columns] + value
            else:
                other[:, columns] = other[:, columns] + value

        times_turned(slope.at[:, pl.ds(j * width, width)], slot, store)

    def second_norm_piece():
        norm_backward(
            other, gains, 1, ref.unit2, ref.scale2, accumulated, low.second, small_sums
        )

    def cross_start_piece():
        times_turned(low.second, next_slot(), into(low.branch))

    def cross_piece(first, last):
        attention_backward(
            ref.cross_query,
            ref.cross_keys,
            ref.cross_values,
            cross_bias,
            cross_blocks,
            eye,
            ref.cross_lse,
            low.branch,
            low.cross_query,
            low.cross_key,
            low.cross_value,
            first,
            last,
        )

    def first_piece():
        def store(columns, value):
            other[:, columns] = ALPHA * accumulated[:, columns] + value

        times_turned(low.cross_query, next_slot(), store)

    def first_norm_piece():
        norm_backward(other, gains, 0, ref.unit1, ref.scale1, accumulated, low.first, small_sums)

    def self_start_piece():
        times_turned(low.first, next_slot(), into(low.branch))

    def self_piece(first, last):
        attention_backward(
            ref.query,
            ref.keys,
            ref.values,
            self_bias,
            self_blocks,
            eye,
            ref.self_lse,
            low.branch,
            low.query,
            low.key,
            low.value,
            first,
            last,
        )

    mem_out, mem_in = ref.mem_out, ref.mem_in

    def grad_own():
        return pltpu.make_async_copy(
            mem_out.at[span(place.mem, mem_block)], mem_in.at[place.mem], ref.mem_sem.at[3]
        )

    def grad_total():
        some = mem_in.at[pl.ds(0, n_mem - 1)]
        return remote(some, some, ref.mem_sem.at[4], ref.mem_sem.at[5], place.far(1))

    def memory_key_piece():
        times_turned(low.cross_key, next_slot(), into(other))

    def memory_value_piece():
        def store(columns, value):
            mem_out[:, columns] = (other[:, columns] + value).astype(mem_out.dtype)

        times_turned(low.cross_value, next_slot(), store)
        grad_own().start()
        for step in range(1, n_mem):
            remote(
                mem_out.at[span((place.mem + step) % n_mem, mem_block)],
                mem_in.at[place.mem],
                ref.mem_sem.at[4],
                ref.mem_sem.at[5],
                place.far(step),
            ).start()

    def input_piece(left, start):
        target = ref.input_grad

        def store(columns, value):
            if start:
                target[:, columns] = ALPHA * accumulated[:, columns] + value
            else:
                target[:, columns] = target[:, columns] + value

        times_turned(left, next_slot(), store)

    def memory_end_piece():
        grad_own().wait()
        grad_total().wait_recv()
        for member in range(n_mem):
            ref.memory_grad[member] = mem_in[member].astype(jnp.float32)

    quarter = width // 4
    at_first = ((0, quarter), (quarter, quarter), (2 * quarter, 2 * quarter))
    at_last = ((0, 2 * quarter), (2 * quarter, quarter), (3 * quarter, quarter))
    grads = ref.grads
    plans = []
    for j in range(many):
        for first, columns in at_first if j == 0 else ((0, width),):
            target = ref.contract_grad.at[pl.ds(j * shard, shard), pl.ds(first, columns)]
            plans.append((hidden_turned.at[j], low.third, first, target))
    for j in range(many):
        target = ref.expand_grad.at[:, pl.ds(j * width, width)]
        plans.append((turned.second, slope, j * width, target))
    plans += [
        (turned.crossed, low.second, 0, grads[at_cross_output]),
        (turned.memory, low.cross_key, 0, grads[at_cross_key]),
        (turned.memory, low.cross_value, 0, grads[at_cross_value]),
        (turned.first, low.cross_query, 0, grads[at_cross_query]),
        (turned.attended, low.first, 0, grads[at_output]),
        (small_sums, None, 0, ref.small_total),
        (turned.tokens, low.query, 0, grads[at_query]),
        (turned.tokens, low.key, 0, grads[at_key]),
    ]
    for first, columns in at_last:
        target = grads[at_value].at[:, pl.ds(first, columns)]
        plans.append((turned.tokens, low.value, first, target))
    jobs = [
        Job(*plan, plan[1] is not None and number % 5 in EARLY)
        for number, plan in enumerate(plans)
    ]
    reduce = Reduce(place, jobs, ref.reduce_sems, pool, SimpleNamespace(**ref.little))

    inner = [functools.partial(inner_piece, j) for j in range(many)]
    second = [functools.partial(second_piece, j) for j in range(many)]
    base = many + 2
    def weight(index):
        return [(full[index], 0, n_rows)]

    turn = functools.partial(turn_by_lane, ref.second_low, eye, turned.second)
    crosses = [functools.partial(cross_piece, pair, pair + 1) for pair in range(pairs)]
    selves = [functools.partial(self_piece, pair, pair + 1) for pair in range(pairs)]
    work = [(base - 1.7 + j, inner[j], contract_rows(j)) for j in range(2)]
    work += [(base - 1.3, turn, None)]
    work += [(base - 1.7 + j, inner[j], contract_rows(j)) for j in range(2, many)]
    work += [(base - 0.3 + j, second[j], [(expand.at[j], 0, n_rows)]) for j in range(many)]
    base = 2 * many + 2
    work += [
        (base - 0.2, second_norm_piece, None),
        (base - 0.15, cross_start_piece, weight(at_cross_output)),
    ]
    work += [(base + 0.3 + 0.05 * pair, crosses[pair], None) for pair in range(pairs)]
    work += [
        (base + 1.3, first_piece, weight(at_cross_query)),
        (base + 1.31, first_norm_piece, None),
        (base + 1.7, self_start_piece, weight(at_output)),
    ]
    work += [(base + 2.3 + 0.14 * pair, selves[pair], None) for pair in range(pairs)]
    work += [
        (base + 3.7, memory_key_piece, weight(at_cross_key)),
        (base + 4.3, memory_value_piece, weight(at_cross_value)),
        (base + 4.7, functools.partial(input_piece, low.query, True), weight(at_query)),
        (base + 5.5, functools.partial(input_piece, low.key, False), weight(at_key)),
        (base + 6.5, functools.partial(input_piece, low.value, False), weight(at_value)),
        (base + 8.5, memory_end_piece, None),
    ]
    actions = [(WORK + index, at, item) for index, (at, *item) in enumerate(work)]
    for number in range(len(jobs)):
        found = reduce.events(number)
        actions.append((CORE + number, found[0][0], found[0][1:]))
        actions.append((LANE + number, found[1][0], found[1][1:]))
        for stage, (at, action) in enumerate(found[2:]):
            actions.append((STAGE + 10 * number + stage, at, (action,)))
    ordered = planned(actions, BACKWARD_PLAN)
    backward_sources += [item[1] for item in ordered if len(item) > 1 and item[1] is not None]
    loads += [load(backward_sources[0]), load(backward_sources[1])]
    norm_both(
        accumulated, ref.out_grad, gains, 2, ref.result, accumulated, low.third, small_sums
    )

    place.hear(ref.ready_sem)
    for item in ordered:
        item[0]()

    total = ref.small_total[...]
    own = jnp.zeros((8, shard), jnp.float32)
    for member in range(n_mem):
        here = jnp.where(place.mem == member, 1.0, 0.0)
        own = own + here * total[:, member * shard : (member + 1) * shard]
    ref.gains_grad[...] = own[0:3]
    ref.shifts_grad[...] = own[3:6]
    reduce.finish()
    memory_total().wait_send()
    grad_total().wait_send()


SMALL_AT = 2
DOC_LIMIT = 64
EARLY = (2, 4)
HOP, ARRIVE, USE, SETTLE, CORE, LANE, STAGE, WORK = range(1000, 9000, 1000)
FORWARD_PLAN = (
    1001, 1011, 1002, 1003, 1020, 1012, 1013, 1030, 1004, 1040, 1021, 1031, 1041, 1032, 1022, 1050,
    1005, 1042, 1014, 1033, 1015, 2000, 1060, 1051, 1023, 1061, 3000, 1034, 1043, 1052, 2001, 3010,
    4000, 1070, 1062, 1053, 1071, 4001, 2002, 1080, 1035, 1044, 3020, 4002, 1063, 1054, 1090, 2003,
    1081, 1072, 3030, 1045, 1073, 4003, 1082, 1100, 1064, 1055, 1091, 2004, 1083, 3040, 1092, 3041,
    3042, 3043, 3044, 4004, 1110, 1074, 1101, 1111, 2005, 1093, 3050, 1065, 3051, 1102, 4005, 1120,
    1084, 1112, 1075, 2006, 1121, 3060, 1103, 4006, 1094, 1122, 2007, 1085, 1113, 1130, 3070, 4007,
    1140, 1095, 1104, 1141, 2008, 3080, 1131, 3081, 1123, 3082, 3083, 1132, 3084, 4008, 1142, 1105,
    1114, 1150, 1133, 2009, 3090, 3091, 4009, 1124, 1160, 1115, 1143, 1151, 2010, 1161, 3100, 3101,
    3102, 1170, 1134, 1152, 1125, 2011, 1162, 4010, 1153, 1171, 3110, 1144, 3111, 3112, 4011, 2012,
    1180, 1135, 1163, 3120, 3121, 3122, 4012, 1154, 1181, 1145, 1190, 2013, 1172, 3130, 1191, 1173,
    3131, 1192, 1200, 2014, 3132, 1155, 1182, 1164, 4013, 1183, 1201, 3140, 1174, 4014, 1193, 1202,
    2015, 3150, 4015, 1165, 1184, 2016, 1203, 1175, 3160, 1194, 2017, 4016, 1185, 3170, 4017, 2018,
    1204, 1195, 3180, 4018, 2019, 1205, 3190, 4019, 2020, 3200, 4020,
)
BACKWARD_PLAN = (
    5000, 6000, 5001, 6001, 5002, 7000, 6002, 5003, 7010, 7001, 7002, 6003, 5004, 7020, 8000, 7021,
    8002, 7003, 7011, 6004, 5005, 7012, 7022, 7004, 7030, 8001, 8003, 8005, 6005, 7023, 7013, 5006,
    7014, 8006, 7031, 6006, 5007, 7040, 8004, 7041, 7024, 8007, 6007, 5008, 7032, 7050, 7042, 8008,
    7033, 6008, 7043, 5009, 7051, 8009, 7034, 8010, 7052, 7060, 6009, 5010, 7070, 8011, 8012, 8013,
    8014, 8015, 8016, 7061, 8017, 7044, 8018, 7053, 8019, 7071, 6010, 5011, 7080, 7062, 7054, 7072,
    8020, 8021, 7063, 7073, 6011, 5012, 7090, 8022, 8023, 8024, 7064, 8025, 7081, 7091, 6012, 7082,
    7092, 7100, 8026, 5013, 8027, 8028, 8029, 8030, 7083, 6013, 7074, 8031, 5014, 7093, 8032, 7110,
    7101, 7084, 7102, 6014, 5015, 7094, 7120, 7103, 8033, 7111, 7121, 6015, 5016, 7112, 7122, 7130,
    7104, 7113, 6016, 5017, 7123, 7140, 8034, 7131, 7141, 7114, 7132, 6017, 5018, 7142, 6018, 7133,
    7150, 7124, 8035, 5019, 7160, 7143, 7151, 7170, 6019, 5020, 6020, 7161, 7171, 7162, 7180, 7172,
    7152, 7163, 7173, 7190, 7134, 7181, 7191, 7164, 7182, 7174, 7144, 7200, 7192, 7183, 7193, 7184,
    7201, 7202, 7203, 7194, 7204,
)


def planned(actions, plan):
    codes = {code for code, _, _ in actions}
    if codes == set(plan):
        at = {code: number for number, code in enumerate(plan)}
        return [item for code, _, item in sorted(actions, key=lambda action: at[action[0]])]
    return [item for _, _, item in sorted(actions, key=lambda action: action[1])]


def copy_kernel(count, *refs):
    for source, target in zip(refs[:count], refs[count:]):
        target[...] = source[...]


def copied(values):
    steps = 4

    def block(value):
        shape = value.shape
        rows = shape[0] // steps
        if shape[0] % steps or (len(shape) == 2 and rows % 8):
            return pl.BlockSpec(shape, lambda step: (0,) * len(shape))
        return pl.BlockSpec((rows,) + shape[1:], lambda step: (step,) + (0,) * (len(shape) - 1))

    blocks = [block(value) for value in values]
    return pl.pallas_call(
        functools.partial(copy_kernel, len(values)),
        grid=(steps,),
        out_shape=[jax.ShapeDtypeStruct(value.shape, value.dtype) for value in values],
        in_specs=blocks,
        out_specs=blocks,
        compiler_params=pltpu.CompilerParams(vmem_limit_bytes=VMEM_LIMIT),
        name="results",
    )(*values)


def fused(n_rows, n_mem, ins):
    tokens, memory, squares = ins["tokens"], ins["memory"], ins["squares"]
    expand, contract = ins["expand"], ins["contract"]
    tokens_here, width = tokens.shape
    ff = expand.shape[1]
    shard = squares[0].shape[0]
    mem_tokens = memory.shape[0] * memory.shape[1]
    digits, half, many = (n_rows // 2).bit_length() - 1, n_rows // 2, ff // width
    pairs = width // (2 * HEAD_DIM)
    low, high = jnp.bfloat16, jnp.float32
    n_weights = SQUARES + 2 * many
    n_parts = n_weights + 1 + width // TILE
    n_jobs = n_weights + 5
    dma, vmem = pltpu.SemaphoreType.DMA, pltpu.VMEM
    anywhere, near = pl.BlockSpec(memory_space=pl.ANY), pl.BlockSpec(memory_space=pltpu.VMEM)

    far_ins = dict(memory=memory)
    in_specs = {
        name: jax.tree.map(lambda _: anywhere if name in far_ins else near, value)
        for name, value in ins.items()
    }

    def out(shape, dtype=high):
        return jax.ShapeDtypeStruct(shape, dtype)

    outs = dict(
        result=out(tokens.shape),
        input_grad=out(tokens.shape),
        memory_grad=out(memory.shape),
        grads=[out(item.shape) for item in squares],
        expand_grad=out(expand.shape),
        contract_grad=out(contract.shape),
        gains_grad=out((3, shard)),
        shifts_grad=out((3, shard)),
    )
    far_outs = dict(
        full=[out((n_rows, n_mem, shard, width), low)] * SQUARES,
        expand_full=out((many, n_rows, n_mem, shard, width), low),
        contract_full=out((n_rows, n_mem, many, shard, width), low),
    )
    out_specs = jax.tree.map(lambda _: near, outs)
    out_specs.update(jax.tree.map(lambda _: anywhere, far_outs))
    outs.update(far_outs)

    def token_rows(dtype):
        return vmem((tokens_here, width), dtype)

    def memory_rows(dtype):
        return vmem((mem_tokens, width), dtype)

    tiny = (8, 128)

    counts = [half >> (stage + 1) for stage in range(digits)]
    units = (OUT_SLOTS + LANE_SLOTS + CORE_RING) * half
    units += 2 * RING + 4 * EARLY_RING + SUM_SLOTS + 1
    for stage, number in enumerate(counts):
        units += (SUM_SLOTS + (RING if stage else FIRST_RING)) * number
    units = max(units + SLOTS * n_rows, GATHER_SLOTS * n_rows)
    little = dict(
        lanes=vmem((half,) + tiny, high),
        core_in=vmem((half,) + tiny, high),
        sums=[vmem((number,) + tiny, high) for number in counts],
        arrived=[vmem((number,) + tiny, high) for number in counts]
        + [vmem((n_mem - 1,) + tiny, high)],
    )
    left = vmem((2, width // 2, tokens_here), low)
    scratch = dict(
        small=vmem(tiny, high),
        small_full=vmem((n_rows, n_mem) + tiny, high),
        small_total=vmem(tiny, high),
        pool=vmem((units, n_mem, shard, width), low),
        slot_sem=dma((SLOTS,)),
        keep_sem=dma((n_weights,)),
        ready_sem=pltpu.SemaphoreType.REGULAR,
        mem_sem=dma((6,)),
        gather_sems=[
            dma(shape + (n_parts,))
            for shape in ((), (), (), (digits,), (digits,), (), ())
            + ((2 * (n_mem - 1),), (2 * (n_mem - 1),))
        ],
        reduce_sems=[
            dma(shape + (n_jobs,))
            for shape in ((), (), (digits + 1,), (digits + 1,))
            + ((2 * (n_mem - 1),), (2 * (n_mem - 1),))
        ],
        gains=vmem((8, width), high),
        query=token_rows(low),
        keys=token_rows(low),
        values=token_rows(low),
        attended=token_rows(low),
        first_low=token_rows(low),
        second_low=token_rows(low),
        cross_query=token_rows(low),
        crossed=token_rows(low),
        cross_keys=memory_rows(low),
        cross_values=memory_rows(low),
        mem_rows=memory_rows(low),
        mem_out=memory_rows(low),
        mem_in=vmem(memory.shape, low),
        unit1=token_rows(high),
        unit2=token_rows(high),
        accumulated=token_rows(high),
        other=token_rows(high),
        scale1=vmem((tokens_here, 1), high),
        scale2=vmem((tokens_here, 1), high),
        self_bias=vmem((tokens_here, tokens_here), high),
        cross_bias=vmem((mem_tokens, tokens_here), high),
        self_lse=vmem((pairs, 2, tokens_here), high),
        cross_lse=vmem((pairs, 2, tokens_here), high),
        eye=vmem((TILE, TILE), low),
        hidden=vmem((tokens_here, ff), low),
        slope=vmem((tokens_here, ff), low),
        hidden_turned=vmem((many, 2, width // 2, tokens_here), low),
        turned=dict(
            tokens=left, attended=left, first=left, memory=left, crossed=left, second=left
        ),
        low=dict(
            third=token_rows(low),
            second=token_rows(low),
            first=token_rows(low),
            branch=token_rows(low),
            cross_query=token_rows(low),
            cross_key=memory_rows(low),
            cross_value=memory_rows(low),
            query=token_rows(low),
            key=token_rows(low),
            value=token_rows(low),
        ),
        small_sums=vmem((2, half) + tiny, high),
        little=little,
    )
    in_values, in_tree = jax.tree.flatten(ins)
    out_shapes, out_tree = jax.tree.flatten(outs)
    scratch_shapes, scratch_tree = jax.tree.flatten(scratch)
    places = jax.tree.unflatten(in_tree, range(len(in_values)))
    at = len(in_values)
    places.update(jax.tree.unflatten(out_tree, range(at, at + len(out_shapes))))
    at += len(out_shapes)
    places.update(jax.tree.unflatten(scratch_tree, range(at, at + len(scratch_shapes))))
    values = pl.pallas_call(
        functools.partial(layer_kernel, places, (n_rows, n_mem, width, ff, shard)),
        out_shape=out_shapes,
        in_specs=jax.tree.leaves(in_specs),
        out_specs=jax.tree.leaves(out_specs),
        scratch_shapes=scratch_shapes,
        compiler_params=pltpu.CompilerParams(
            collective_id=0, has_side_effects=True, vmem_limit_bytes=VMEM_LIMIT
        ),
        name="layer",
    )(*in_values)
    found = jax.tree.unflatten(out_tree, values)
    for name in far_outs:
        del found[name]
    return found


def local(n_rows, n_mem, *args):
    (
        tokens,
        memory,
        token_ids,
        memory_ids,
        out_grad,
        self_query,
        self_key,
        self_value,
        self_output,
        cross_query,
        cross_key,
        cross_value,
        cross_output,
        expand_weight,
        contract_weight,
        norm_gains,
        norm_shifts,
    ) = args
    shard, width = self_query.shape
    suits = width == 128 * n_rows and shard % 16 == 0 and tokens.shape[0] == 1
    suits = suits and tokens.shape[1] == TILE and expand_weight.shape[1] == n_mem * width
    if not suits or n_rows < 4 or n_rows & (n_rows - 1) or n_mem < 2:
        return plain(*args)
    found = fused(
        n_rows,
        n_mem,
        dict(
            tokens=tokens[0],
            memory=memory,
            token_ids=token_ids,
            memory_ids=memory_ids,
            out_grad=out_grad[0],
            squares=[
                self_query,
                self_key,
                self_value,
                self_output,
                cross_query,
                cross_key,
                cross_value,
                cross_output,
            ],
            expand=expand_weight,
            contract=contract_weight,
            norm_gains=norm_gains,
            norm_shifts=norm_shifts,
        ),
    )
    values, tree = jax.tree.flatten(found)
    found = SimpleNamespace(**jax.tree.unflatten(tree, copied(values)))
    return (
        found.result[None],
        found.input_grad[None],
        found.memory_grad,
        *found.grads,
        found.expand_grad,
        found.contract_grad,
        found.gains_grad,
        found.shifts_grad,
    )


def solution(mesh):
    in_specs = (
        P(("rows", "mem"), None, None),
        P("rows", "mem", None),
        P("rows", None),
        P("rows", None),
        P(("rows", "mem"), None, None),
        P(("rows", "mem"), None),
        P(("rows", "mem"), None),
        P(("rows", "mem"), None),
        P(("rows", "mem"), None),
        P(("rows", "mem"), None),
        P(("rows", "mem"), None),
        P(("rows", "mem"), None),
        P(("rows", "mem"), None),
        P(("rows", "mem"), None),
        P(("rows", "mem"), None),
        P(None, ("rows", "mem")),
        P(None, ("rows", "mem")),
    )
    out_specs = (
        P(("rows", "mem"), None, None),
        P(("rows", "mem"), None, None),
        P("rows", "mem", None),
        P(("rows", "mem"), None),
        P(("rows", "mem"), None),
        P(("rows", "mem"), None),
        P(("rows", "mem"), None),
        P(("rows", "mem"), None),
        P(("rows", "mem"), None),
        P(("rows", "mem"), None),
        P(("rows", "mem"), None),
        P(("rows", "mem"), None),
        P(("rows", "mem"), None),
        P(None, ("rows", "mem")),
        P(None, ("rows", "mem")),
    )
    layer = functools.partial(local, mesh.shape["rows"], mesh.shape["mem"])
    return jax.shard_map(layer, mesh=mesh, in_specs=in_specs, out_specs=out_specs, check_vma=False)
```

```python
import functools
import math
from types import SimpleNamespace

import jax
import jax.numpy as jnp
from jax import lax
from jax.experimental import pallas as pl
from jax.experimental.pallas import tpu as pltpu
from jax.sharding import PartitionSpec as P

MESH = pl.DeviceIdType.MESH

HEADS = 16
HEAD_DIM = 64


ALPHA = 4.16
EPS = 1e-05
SCALE = 0.125
NEG = -1e30


def layer_norm(hidden_activation, gain, shift):
    centre = hidden_activation - jnp.mean(hidden_activation, axis=-1, keepdims=True)
    spread = jnp.mean(centre * centre, axis=-1, keepdims=True)
    return centre * lax.rsqrt(spread + EPS) * gain + shift


def gelu_exact(value):
    return jax.nn.gelu(value, approximate=False)


def product(left, right):
    return jnp.dot(left, right, preferred_element_type=jnp.float32)


def split_heads(matrix):
    return matrix.reshape(matrix.shape[0], matrix.shape[1] // HEAD_DIM, HEAD_DIM)


def grouped(matrix):
    return jnp.moveaxis(matrix.reshape(matrix.shape[0], HEADS // 4, 4 * HEAD_DIM), 1, 0)


def ungrouped(stack):
    return jnp.moveaxis(stack, 0, 1).reshape(stack.shape[1], stack.shape[0] * stack.shape[2])


def row_map(function, items):
    return lax.map(lambda entry: function(*entry), items)


def score_block(query, keys, allowed):
    raw = jnp.einsum(
        "khe,qhe->hkq", split_heads(keys), split_heads(query), preferred_element_type=jnp.float32
    )
    return jnp.where(allowed[None], raw * SCALE, NEG)


def attend_probs(query, keys, allowed, lse):
    scores = score_block(query, keys, allowed)
    return jnp.where(allowed[None], jnp.exp(scores - lse[:, None, :]), 0.0)


def attend_forward(query, keys, values, allowed):
    scores = score_block(query, keys, allowed)
    top = jnp.max(scores, axis=1)
    weight = jnp.where(allowed[None], jnp.exp(scores - top[:, None, :]), 0.0)
    total = jnp.sum(weight, axis=1)
    probs = (weight / total[:, None, :]).astype(jnp.bfloat16)
    mixed = jnp.einsum(
        "hkq,khe->qhe", probs, split_heads(values), preferred_element_type=jnp.float32
    )
    return (mixed.reshape(query.shape), top + jnp.log(total))


def value_pull(grad, values):
    return jnp.einsum(
        "qhe,khe->hkq", split_heads(grad), split_heads(values), preferred_element_type=jnp.float32
    )


def score_grads(probs, pulled, inner):
    return (probs * (pulled - inner[:, None, :]) * SCALE).astype(jnp.bfloat16)


def query_from(score_grad, keys, shape):
    moved = jnp.einsum(
        "hkq,khe->qhe", score_grad, split_heads(keys), preferred_element_type=jnp.float32
    )
    return moved.reshape(shape)


def key_from(score_grad, query, shape):
    moved = jnp.einsum(
        "hkq,qhe->khe", score_grad, split_heads(query), preferred_element_type=jnp.float32
    )
    return moved.reshape(shape)


def value_from(probs, grad, values):
    moved = jnp.einsum(
        "hkq,qhe->khe",
        probs.astype(jnp.bfloat16),
        split_heads(grad),
        preferred_element_type=jnp.float32,
    )
    return moved.reshape(values.shape)


def local_forward(query, keys, values, allowed):

    def one_group(items):
        return attend_forward(items[0], items[1], items[2], allowed)

    mixed, lse = lax.map(one_group, (grouped(query), grouped(keys), grouped(values)))
    return (ungrouped(mixed), lse)


def local_backward(query, keys, values, allowed, lse, grad):

    def one_group(items):
        part_query, part_keys, part_values, part_lse, part_grad = items
        probs = attend_probs(part_query, part_keys, allowed, part_lse)
        pulled = value_pull(part_grad, part_values)
        inner = jnp.sum(probs * pulled, axis=1)
        score_grad = score_grads(probs, pulled, inner)
        return (
            query_from(score_grad, part_keys, part_query.shape),
            key_from(score_grad, part_query, part_keys.shape),
            value_from(probs, part_grad, part_values),
        )

    parts = lax.map(one_group, (grouped(query), grouped(keys), grouped(values), lse, grouped(grad)))
    return (ungrouped(parts[0]), ungrouped(parts[1]), ungrouped(parts[2]))


def plain(
    tokens,
    memory,
    token_ids,
    memory_ids,
    out_grad,
    self_query,
    self_key,
    self_value,
    self_output,
    cross_query,
    cross_key,
    cross_value,
    cross_output,
    expand_weight,
    contract_weight,
    norm_gains,
    norm_shifts,
):
    full = (
        lax.all_gather(self_query, ("rows", "mem"), axis=0, tiled=True),
        lax.all_gather(self_key, ("rows", "mem"), axis=0, tiled=True),
        lax.all_gather(self_value, ("rows", "mem"), axis=0, tiled=True),
        lax.all_gather(self_output, ("rows", "mem"), axis=0, tiled=True),
        lax.all_gather(cross_query, ("rows", "mem"), axis=0, tiled=True),
        lax.all_gather(cross_key, ("rows", "mem"), axis=0, tiled=True),
        lax.all_gather(cross_value, ("rows", "mem"), axis=0, tiled=True),
        lax.all_gather(cross_output, ("rows", "mem"), axis=0, tiled=True),
        lax.all_gather(expand_weight, ("rows", "mem"), axis=0, tiled=True),
        lax.all_gather(contract_weight, ("rows", "mem"), axis=0, tiled=True),
        lax.all_gather(jnp.transpose(norm_gains), ("rows", "mem"), axis=0, tiled=True),
        lax.all_gather(jnp.transpose(norm_shifts), ("rows", "mem"), axis=0, tiled=True),
    )
    (
        self_attention_query,
        decoder_match_label,
        self_attention_value,
        self_attention_output,
        encoder_lookup_probe,
        key_cross,
        value_cross,
        cross_attention_output,
        up_projection,
        narrowing_matrix,
        gain_cols,
        shift_cols,
    ) = full
    gain_rows = jnp.transpose(gain_cols).astype(jnp.float32)
    shift_rows = jnp.transpose(shift_cols).astype(jnp.float32)
    rows_here = tokens.shape[0]
    member = lax.axis_index("mem")
    own_ids = lax.dynamic_slice_in_dim(token_ids, member * rows_here, rows_here, 0)
    positions = jnp.arange(tokens.shape[1], dtype=jnp.int32)
    self_allowed = (own_ids[:, :, None] == own_ids[:, None, :]) & (
        positions[:, None] <= positions[None, :]
    )[None]
    query = product(tokens, self_attention_query).astype(jnp.bfloat16)
    keys = product(tokens, decoder_match_label).astype(jnp.bfloat16)
    values = product(tokens, self_attention_value).astype(jnp.bfloat16)
    self_mixed, self_lse = row_map(local_forward, (query, keys, values, self_allowed))
    attention_result = self_mixed.astype(jnp.bfloat16)
    first, first_back = jax.vjp(
        layer_norm,
        ALPHA * tokens.astype(jnp.float32) + product(attention_result, self_attention_output),
        gain_rows[0],
        shift_rows[0],
    )
    first_reduced = first.astype(jnp.bfloat16)
    cross_queries = product(first_reduced, encoder_lookup_probe).astype(jnp.bfloat16)
    memory_rows = lax.all_to_all(memory, "mem", split_axis=0, concat_axis=1, tiled=True)
    row_ids = lax.dynamic_slice_in_dim(memory_ids, member * rows_here, rows_here, 0)
    cross_allowed = row_ids[:, :, None] == own_ids[:, None, :]
    cross_keys = product(memory_rows, key_cross).astype(jnp.bfloat16)
    cross_values = product(memory_rows, value_cross).astype(jnp.bfloat16)
    cross_mixed, cross_lse = row_map(
        local_forward, (cross_queries, cross_keys, cross_values, cross_allowed)
    )
    cross_attention_result = cross_mixed.astype(jnp.bfloat16)
    second, second_back = jax.vjp(
        layer_norm,
        ALPHA * first + product(cross_attention_result, cross_attention_output),
        gain_rows[1],
        shift_rows[1],
    )
    second_reduced = second.astype(jnp.bfloat16)
    hidden_value, gelu_back = jax.vjp(gelu_exact, product(second_reduced, up_projection))
    hidden_activation = hidden_value.astype(jnp.bfloat16)
    result, third_back = jax.vjp(
        layer_norm,
        ALPHA * second + product(hidden_activation, narrowing_matrix),
        gain_rows[2],
        shift_rows[2],
    )
    third_grad, gain_three, shift_three = third_back(out_grad.astype(jnp.float32))
    feedforward_gradient = third_grad.astype(jnp.bfloat16)
    down_projection_gradient = jnp.einsum(
        "ehj,ehc->jc", hidden_activation, feedforward_gradient, preferred_element_type=jnp.float32
    )
    (inner_grad,) = gelu_back(
        jnp.einsum(
            "hpu,ku->hpk",
            feedforward_gradient,
            narrowing_matrix,
            preferred_element_type=jnp.float32,
        )
    )
    inner_reduced = inner_grad.astype(jnp.bfloat16)
    expand_grad = jnp.einsum(
        "iqg,iqe->ge", second_reduced, inner_reduced, preferred_element_type=jnp.float32
    )
    second_total = ALPHA * third_grad + jnp.einsum(
        "iwm,fm->iwf", inner_reduced, up_projection, preferred_element_type=jnp.float32
    )
    second_grad, gain_two, shift_two = second_back(second_total)
    cross_branch_gradient = second_grad.astype(jnp.bfloat16)
    output_cross_grad = jnp.einsum(
        "nhb,nhc->bc",
        cross_attention_result,
        cross_branch_gradient,
        preferred_element_type=jnp.float32,
    )
    crossed_grad = jnp.einsum(
        "qwp,up->qwu",
        cross_branch_gradient,
        cross_attention_output,
        preferred_element_type=jnp.float32,
    ).astype(jnp.bfloat16)
    query_grads, key_grads, value_grads = row_map(
        local_backward,
        (cross_queries, cross_keys, cross_values, cross_allowed, cross_lse, crossed_grad),
    )
    key_low = key_grads.astype(jnp.bfloat16)
    value_low = value_grads.astype(jnp.bfloat16)
    row_grad = jnp.einsum(
        "sme,de->smd", key_low, key_cross, preferred_element_type=jnp.float32
    ) + jnp.einsum("sme,de->smd", value_low, value_cross, preferred_element_type=jnp.float32)
    key_cross_grad = jnp.einsum(
        "smd,sme->de", memory_rows, key_low, preferred_element_type=jnp.float32
    )
    value_cross_grad = jnp.einsum(
        "smd,sme->de", memory_rows, value_low, preferred_element_type=jnp.float32
    )
    memory_grad = lax.all_to_all(
        row_grad.astype(jnp.bfloat16), "mem", split_axis=1, concat_axis=0, tiled=True
    ).astype(row_grad.dtype)
    probe_lowered_precision = query_grads.astype(jnp.bfloat16)
    query_cross_grad = jnp.einsum(
        "nhb,nhc->bc", first_reduced, probe_lowered_precision, preferred_element_type=jnp.float32
    )
    first_total = ALPHA * second_grad + jnp.einsum(
        "qwp,up->qwu",
        probe_lowered_precision,
        encoder_lookup_probe,
        preferred_element_type=jnp.float32,
    )
    first_grad, gain_one, shift_one = first_back(first_total)
    self_branch_gradient = first_grad.astype(jnp.bfloat16)
    output_self_grad = jnp.einsum(
        "nhb,nhc->bc", attention_result, self_branch_gradient, preferred_element_type=jnp.float32
    )
    attended_grad = jnp.einsum(
        "qwp,up->qwu",
        self_branch_gradient,
        self_attention_output,
        preferred_element_type=jnp.float32,
    ).astype(jnp.bfloat16)
    self_query_reduced, decoder_label_lowered, self_value_reduced = row_map(
        local_backward, (query, keys, values, self_allowed, self_lse, attended_grad)
    )
    self_query_reduced = self_query_reduced.astype(jnp.bfloat16)
    decoder_label_lowered = decoder_label_lowered.astype(jnp.bfloat16)
    self_value_reduced = self_value_reduced.astype(jnp.bfloat16)
    query_self_grad = jnp.einsum(
        "nhb,nhc->bc", tokens, self_query_reduced, preferred_element_type=jnp.float32
    )
    key_self_grad = jnp.einsum(
        "nhb,nhc->bc", tokens, decoder_label_lowered, preferred_element_type=jnp.float32
    )
    value_self_grad = jnp.einsum(
        "nhb,nhc->bc", tokens, self_value_reduced, preferred_element_type=jnp.float32
    )
    input_grad = (
        ALPHA * first_grad
        + jnp.einsum(
            "qwp,up->qwu",
            self_query_reduced,
            self_attention_query,
            preferred_element_type=jnp.float32,
        )
        + jnp.einsum(
            "qwp,up->qwu",
            decoder_label_lowered,
            decoder_match_label,
            preferred_element_type=jnp.float32,
        )
        + jnp.einsum(
            "qwp,up->qwu",
            self_value_reduced,
            self_attention_value,
            preferred_element_type=jnp.float32,
        )
    )
    gain_grad = jnp.stack([gain_one, gain_two, gain_three], axis=1)
    shift_grad = jnp.stack([shift_one, shift_two, shift_three], axis=1)
    sums = (
        lax.psum_scatter(query_self_grad, ("rows", "mem"), scatter_dimension=0, tiled=True),
        lax.psum_scatter(key_self_grad, ("rows", "mem"), scatter_dimension=0, tiled=True),
        lax.psum_scatter(value_self_grad, ("rows", "mem"), scatter_dimension=0, tiled=True),
        lax.psum_scatter(output_self_grad, ("rows", "mem"), scatter_dimension=0, tiled=True),
        lax.psum_scatter(query_cross_grad, ("rows", "mem"), scatter_dimension=0, tiled=True),
        lax.psum_scatter(key_cross_grad, ("rows", "mem"), scatter_dimension=0, tiled=True),
        lax.psum_scatter(value_cross_grad, ("rows", "mem"), scatter_dimension=0, tiled=True),
        lax.psum_scatter(output_cross_grad, ("rows", "mem"), scatter_dimension=0, tiled=True),
        lax.psum_scatter(expand_grad, ("rows", "mem"), scatter_dimension=0, tiled=True),
        lax.psum_scatter(
            down_projection_gradient, ("rows", "mem"), scatter_dimension=0, tiled=True
        ),
        lax.psum_scatter(gain_grad, ("rows", "mem"), scatter_dimension=0, tiled=True),
        lax.psum_scatter(shift_grad, ("rows", "mem"), scatter_dimension=0, tiled=True),
    )
    return (
        result,
        input_grad,
        memory_grad,
        sums[0],
        sums[1],
        sums[2],
        sums[3],
        sums[4],
        sums[5],
        sums[6],
        sums[7],
        sums[8],
        sums[9],
        jnp.transpose(sums[10]),
        jnp.transpose(sums[11]),
    )


ALL = slice(None)
TILE = 256
SLOTS = 3
GATHER_SLOTS = 9
VMEM_LIMIT = 61 * 1024 * 1024


def flip(index, unit):
    return index + unit * (1 - 2 * ((index // unit) % 2))


def span(index, size):
    return pl.ds(pl.multiple_of(index * size, size), size)


class Place:
    def __init__(self, n_rows, n_mem):
        self.n_rows, self.n_mem = n_rows, n_mem
        self.digits = (n_rows // 2).bit_length() - 1
        self.mem_digits = n_mem.bit_length() - 1
        self.row = lax.axis_index("rows")
        self.mem = lax.axis_index("mem")
        self.lane = self.row % 2

    def turn(self, index, stage):
        rising, falling = 2 << stage, 2 << (self.digits - 1 - stage)
        return flip(index, rising) * (1 - self.lane) + flip(index, falling) * self.lane

    def sibling(self):
        return (flip(self.row, 1), self.mem)

    def partner(self, stage):
        return (self.turn(self.row, stage), self.mem)

    def far(self, step):
        return (self.row, (self.mem + step) % self.n_mem)

    def along(self, stage):
        return (self.row, flip(self.mem, 1 << stage))

    def others(self):
        found = [self.far(step) for step in range(1, self.n_mem)]
        found += [self.partner(stage) for stage in range(self.digits)]
        return found + [self.sibling()]

    def tell(self, semaphore):
        for other in self.others():
            pl.semaphore_signal(semaphore, inc=1, device_id=other, device_id_type=MESH)

    def hear(self, semaphore):
        pl.semaphore_wait(semaphore, len(self.others()))

    def greet(self):
        self.tell(pltpu.get_barrier_semaphore())
        self.hear(pltpu.get_barrier_semaphore())


def remote(source, target, send_sem, recv_sem, device):
    return pltpu.make_async_remote_copy(
        src_ref=source,
        dst_ref=target,
        send_sem=send_sem,
        recv_sem=recv_sem,
        device_id=device,
        device_id_type=MESH,
    )


def waits(total):
    return (lambda: total().wait_recv(), lambda: total().wait_send())


class Part:
    def __init__(self, source, target, near=0, straight=False):
        self.source, self.target = source, target
        self.near, self.straight = near, straight


class Gather:
    def __init__(self, place, parts, sems):
        self.place, self.parts = place, parts
        (
            self.own_sem,
            self.far_send,
            self.far_recv,
            self.plane_send,
            self.plane_recv,
            self.core_send,
            self.core_recv,
            self.line_send,
            self.line_recv,
        ) = sems

    def group(self, number, group):
        return self.parts[number].target.at[group]

    def one(self, number, group, member):
        return self.parts[number].target.at[group, member]

    def shard(self, number):
        return self.parts[number].source

    def mine(self, number):
        return self.one(number, self.place.row, self.place.mem)

    def own(self, number):
        return pltpu.make_async_copy(self.shard(number), self.mine(number), self.own_sem.at[number])

    def held(self, stage):
        groups = [self.place.row]
        for before in range(stage):
            groups = groups + [self.place.turn(group, before) for group in groups]
        return groups

    def far_total(self, number):
        part = self.parts[number]
        some = part.target.at[pl.ds(0, 1 << part.near), pl.ds(0, self.place.n_mem - 1)]
        return remote(
            some, some, self.far_send.at[number], self.far_recv.at[number], self.place.far(1)
        )

    def far_hop(self, number, first):
        place = self.place
        for group in self.held(self.parts[number].near):
            target = self.one(number, group, place.mem)
            source = self.shard(number) if first else target
            for step in range(1, place.n_mem):
                remote(
                    source,
                    target,
                    self.far_send.at[number],
                    self.far_recv.at[number],
                    place.far(step),
                ).start()

    def members(self, stage):
        found = [self.place.mem]
        for before in range(stage):
            unit = 1 << (self.place.mem_digits - 1 - before)
            found = found + [flip(member, unit) for member in found]
        return found

    def line_total(self, number, stage):
        part = self.parts[number]
        some = part.target.at[pl.ds(0, 1 << part.near), pl.ds(0, 1 << stage)]
        sems = (self.line_send.at[stage, number], self.line_recv.at[stage, number])
        return remote(some, some, *sems, self.place.far(1))

    def line_hop(self, number, stage, first):
        sems = (self.line_send.at[stage, number], self.line_recv.at[stage, number])
        partner = self.place.along(self.place.mem_digits - 1 - stage)
        for group in self.held(self.parts[number].near):
            for member in self.members(stage):
                target = self.one(number, group, member)
                remote(self.shard(number) if first else target, target, *sems, partner).start()

    def plane_total(self, number, stage):
        part = self.parts[number]
        some = part.target.at[pl.ds(0, 1 << stage)]
        if stage < part.near:
            some = part.target.at[pl.ds(0, 1 << stage), 0]
        return remote(
            some,
            some,
            self.plane_send.at[stage, number],
            self.plane_recv.at[stage, number],
            self.place.partner(stage),
        )

    def plane_hop(self, number, stage, first):
        for group in self.held(stage):
            if stage < self.parts[number].near:
                target = self.one(number, group, self.place.mem)
            else:
                target = self.group(number, group)
            remote(
                self.shard(number) if first else target,
                target,
                self.plane_send.at[stage, number],
                self.plane_recv.at[stage, number],
                self.place.partner(stage),
            ).start()

    def core_total(self, number):
        some = self.parts[number].target.at[pl.ds(0, self.place.n_rows // 2)]
        return remote(
            some, some, self.core_send.at[number], self.core_recv.at[number], self.place.sibling()
        )

    def core_hop(self, number, first):
        for group in self.held(self.place.digits):
            block = self.group(number, group)
            remote(
                block,
                block,
                self.core_send.at[number],
                self.core_recv.at[number],
                self.place.sibling(),
            ).start()

    def hops(self, number):
        part, take = self.parts[number], functools.partial
        along = []
        if part.straight:
            along.append((1.6, take(self.far_hop, number)) + waits(take(self.far_total, number)))
        else:
            for stage in range(self.place.mem_digits):
                total = take(self.line_total, number, stage)
                along.append((0.9 if stage else 1.4, take(self.line_hop, number, stage)) + waits(total))
        plane = []
        for stage in range(self.place.digits):
            total = take(self.plane_total, number, stage)
            plane.append((1.5, take(self.plane_hop, number, stage)) + waits(total))
        core = (1.5, take(self.core_hop, number)) + waits(take(self.core_total, number))
        return plane[: part.near] + along + plane[part.near :] + [core]

    def events(self, number):
        hops = self.hops(number)
        time, found = float(number), []

        def act(at):
            if at == 0:
                self.own(number).start()
            else:
                if at == 1:
                    self.own(number).wait()
                hops[at - 1][2]()
            hops[at][1](at == 0)

        for at in range(len(hops)):
            time += hops[at][0] if at else 0.0
            found.append((time, functools.partial(act, at)))
        return found, time + 0.9

    def sent(self, number):
        for hop in self.hops(number):
            hop[3]()


class Job:
    def __init__(self, left, right, first, target, early=False):
        self.left, self.right, self.first, self.target = left, right, first, target
        self.small = right is None
        self.early = early
        self.width = target.shape[-1]
        self.large = self.at = 0


OUT_SLOTS, LANE_SLOTS, SUM_SLOTS, CORE_RING, FIRST_RING, RING, EARLY_RING = 2, 3, 2, 3, 6, 4, 3


class Reduce:
    def __init__(self, place, jobs, sems, pool, small):
        self.place, self.jobs, self.small = place, jobs, small
        self.core_send, self.core_recv, self.stage_send, self.stage_recv = sems
        digits, n_mem, half = place.digits, place.n_mem, place.n_rows // 2
        self.waited = set()
        wanted = [place.row]
        for stage in reversed(range(digits)):
            wanted = wanted + [place.turn(group, stage) for group in wanted]
        self.wanted = [group // 2 for group in wanted]
        self.members = [place.mem]
        for stage in reversed(range(place.mem_digits)):
            self.members = self.members + [flip(member, 1 << stage) for member in self.members]
        large = [job for job in jobs if not job.small]
        for number, job in enumerate(large):
            job.large = number
            job.at = [item for item in large if item.early == job.early].index(job)
        plane = [(False, digit) for digit in range(digits)]
        mem = [(True, digit) for digit in range(place.mem_digits)]
        self.orders = {False: plane + mem, True: plane[:-1] + mem + plane[-1:]}
        used = [0]

        def take(count, units):
            first = used[0]
            used[0] += count * units
            return [pool.at[pl.ds(first + i * units, units)] for i in range(count)]

        self.outs = take(OUT_SLOTS, half)
        self.lane_slots = take(LANE_SLOTS, half)
        self.core_ring = take(CORE_RING, half)
        self.sum_slots, self.rings = {}, {}
        first_units = half // 2
        first_sums, first_ring = take(SUM_SLOTS, first_units), take(FIRST_RING, first_units)
        for early, order in self.orders.items():
            ring = EARLY_RING if early else RING
            units, pieces, lying = half, n_mem, None
            for stage, (along, digit) in enumerate(order):
                if along:
                    if pieces == n_mem:
                        lying = take(SUM_SLOTS, units), take(ring, units)
                    pieces //= 2
                    offset = n_mem - 2 * pieces
                    slots = [[ref.at[:, pl.ds(offset, pieces)] for ref in refs] for refs in lying]
                else:
                    units //= 2
                    if stage == 0:
                        slots = first_sums, first_ring
                    else:
                        slots = take(SUM_SLOTS, units), take(ring, units)
                        if pieces < n_mem:
                            slots = [[ref.at[:, pl.ds(0, pieces)] for ref in refs] for refs in slots]
                self.sum_slots[early, stage], self.rings[early, stage] = slots

    def cut(self, ref, job):
        if job.width == ref.shape[-1]:
            return ref
        return ref.at[(ALL,) * (len(ref.shape) - 1) + (pl.ds(0, job.width),)]

    def stages(self, job):
        return len(self.orders[job.early])

    def out(self, job):
        return self.cut(self.outs[job.large % OUT_SLOTS], job)

    def lanes(self, job):
        if job.small:
            return self.small.lanes
        return self.cut(self.lane_slots[job.large % LANE_SLOTS], job)

    def core_in(self, job):
        if job.small:
            return self.small.core_in
        return self.cut(self.core_ring[job.large % CORE_RING], job)

    def shared(self, job, stage):
        return stage == 0 and not self.orders[job.early][0][0]

    def sums(self, job, stage):
        slots = self.sum_slots[job.early, stage]
        number = job.large if self.shared(job, stage) else job.at
        return self.cut(slots[number % SUM_SLOTS], job)

    def arrived(self, job, stage):
        if job.small:
            return self.small.arrived[stage]
        ring = self.rings[job.early, stage]
        number = job.large if self.shared(job, stage) else job.at
        return self.cut(ring[number % len(ring)], job)

    def previous(self, number, distance, like=None):
        found = [
            n
            for n in range(number)
            if not self.jobs[n].small and (like is None or self.jobs[n].early == like.early)
        ]
        return found[-distance] if len(found) >= distance else None

    def once(self, key, wait):
        if key not in self.waited:
            self.waited.add(key)
            wait()

    def core_sent(self, number):
        self.once((number, -1), lambda: self.core_copy(number).wait_send())

    def stage_sent(self, number, stage):
        self.once((number, stage), lambda: self.total(number, stage).wait_send())

    def core_copy(self, number):
        job = self.jobs[number]
        source = job.left.at[1 - self.place.lane] if job.small else self.out(job)
        return remote(
            source,
            self.core_in(job),
            self.core_send.at[number],
            self.core_recv.at[number],
            self.place.sibling(),
        )

    def product(self, job, side, store):
        half = self.place.n_rows // 2
        group = job.left.shape[1] // half
        width = min(TILE, job.width)
        unit = (self.place.n_mem, group // self.place.n_mem, width)

        def column_step(step, carry):
            source = pl.ds(pl.multiple_of(job.first + step * width, width), width)
            value = dot(job.left[side], job.right[:, source])
            for index in range(half):
                block = value[index * group : (index + 1) * group].reshape(unit)
                store(index, span(step, width), block)
            return carry

        lax.fori_loop(0, job.width // width, column_step, 0)

    def core_stage(self, number):
        job = self.jobs[number]
        if not job.small:
            before = self.previous(number, OUT_SLOTS)
            if before is not None:
                self.core_sent(before)
            out = self.out(job)

            def store(index, columns, value):
                out[index, :, :, columns] = value.astype(out.dtype)

            self.product(job, 1 - self.place.lane, store)
        self.core_copy(number).start()

    def lane_stage(self, number):
        job = self.jobs[number]
        if not job.small:
            before = self.previous(number, LANE_SLOTS)
            if before is not None:
                self.stage_sent(before, 0)
        lanes, arrived = self.lanes(job), self.core_in(job)
        self.core_copy(number).wait_recv()
        if job.small:
            lanes[...] = job.left[self.place.lane] + arrived[...]
            self.small_send(number, 0)
        else:

            def store(index, columns, value):
                total = value + arrived[index, :, :, columns].astype(jnp.float32)
                lanes[index, :, :, columns] = total.astype(lanes.dtype)

            self.product(job, self.place.lane, store)
            self.send(number, 0)

    def unit(self, job, stage, index):
        if stage == 0:
            return self.lanes(job).at[self.wanted[index]]
        return self.sums(job, stage - 1).at[index]

    def piece(self, job, stage, index, place):
        unit = self.unit(job, stage, index)
        return unit.at[self.members[place] if unit.shape[0] == self.place.n_mem else place]

    def send(self, number, stage):
        job, place = self.jobs[number], self.place
        along, digit = self.orders[job.early][stage]
        arrived = self.arrived(job, stage)
        units, pieces = arrived.shape[:2]
        sems = (self.stage_send.at[stage, number], self.stage_recv.at[stage, number])
        partner = place.along(digit) if along else place.partner(digit)
        for index in range(units):
            if not along:
                source = self.unit(job, stage, units + index)
                remote(source, arrived.at[index], *sems, partner).start()
                continue
            for at in range(pieces):
                source = self.piece(job, stage, index, pieces + at)
                remote(source, arrived.at[index, at], *sems, partner).start()

    def total(self, number, stage):
        some = self.arrived(self.jobs[number], stage)
        sems = (self.stage_send.at[stage, number], self.stage_recv.at[stage, number])
        return remote(some, some, *sems, self.place.far(1))

    def stage(self, number, stage):
        job = self.jobs[number]
        last = stage == self.stages(job) - 1
        if not last:
            before = self.previous(number, SUM_SLOTS, None if self.shared(job, stage) else job)
            if before is not None:
                self.stage_sent(before, stage + 1)
        self.total(number, stage).wait_recv()
        along, _ = self.orders[job.early][stage]
        arrived = self.arrived(job, stage)
        units, pieces = arrived.shape[:2]
        for index in range(units):
            if not along and pieces > 1:
                mine, coming = self.unit(job, stage, index), arrived.at[index]
                target = self.sums(job, stage).at[index]

                def add(at, carry, mine=mine, coming=coming, target=target):
                    value = mine[at].astype(jnp.float32) + coming[at].astype(jnp.float32)
                    target[at] = value.astype(target.dtype)
                    return carry

                lax.fori_loop(0, pieces, add, 0)
                continue
            for at in range(pieces):
                mine = self.piece(job, stage, index, at)
                target = job.target if last else self.sums(job, stage).at[index, at]
                value = mine[...].astype(jnp.float32) + arrived[index, at].astype(jnp.float32)
                target[...] = value.astype(target.dtype)
        if not last:
            self.send(number, stage + 1)

    def small_unit(self, number, stage, index):
        if stage == 0:
            return self.small.lanes.at[self.wanted[index]]
        return self.small.sums[stage - 1].at[index]

    def small_send(self, number, stage):
        place, arrived = self.place, self.small.arrived[stage]
        sems = (self.stage_send.at[stage, number], self.stage_recv.at[stage, number])
        if stage == place.digits:
            for step in range(1, place.n_mem):
                source = self.small_unit(number, stage, 0)
                remote(source, arrived.at[step - 1], *sems, place.far(step)).start()
            return
        left = arrived.shape[0]
        for index in range(left):
            source = self.small_unit(number, stage, left + index)
            remote(source, arrived.at[index], *sems, place.partner(stage)).start()

    def small_stage(self, number, stage):
        self.total(number, stage).wait_recv()
        arrived = self.small.arrived[stage]
        if stage == self.place.digits:
            value = self.small_unit(number, stage, 0)[...]
            for step in range(self.place.n_mem - 1):
                value = value + arrived[step]
            self.jobs[number].target[...] = value
            return
        for index in range(arrived.shape[0]):
            mine = self.small_unit(number, stage, index)
            self.small.sums[stage][index] = mine[...] + arrived[index]
        self.small_send(number, stage + 1)

    def events(self, number):
        job, take = self.jobs[number], functools.partial
        found = [(0.0, take(self.core_stage, number)), (0.9, take(self.lane_stage, number))]
        time = 2.2 if number < 3 else 3.2
        for stage in range(self.place.digits + 1 if job.small else self.stages(job)):
            action = self.small_stage if job.small else self.stage
            found.append((time, take(action, number, stage)))
            time += 1.1
        return [(number + at, action) for at, action in found]

    def finish(self):
        for number, job in enumerate(self.jobs):
            self.core_sent(number)
            for stage in range(self.place.digits + 1 if job.small else self.stages(job)):
                self.stage_sent(number, stage)


NORMAL = (((1,), (0,)), ((), ()))
TURNED = (((1,), (1,)), ((), ()))
LEFT_TURNED = (((0,), (0,)), ((), ()))


def dot(left, right, dims=NORMAL):
    return lax.dot_general(left, right, dims, preferred_element_type=jnp.float32)


def times(left, weight, store, part=0, parts=1):
    size = weight.shape[-1]
    width = min(TILE, size)
    tiles = size // width // parts

    def column_step(step, carry):
        columns = span(step, width)
        store(columns, dot(left[...], weight[:, :, :, columns].reshape(-1, width)))
        return carry

    lax.fori_loop(part * tiles, (part + 1) * tiles, column_step, 0)


def times_turned(left, weight, store):
    unit = weight.shape[1] * weight.shape[2]
    units = max(TILE // unit, 1)

    def row_step(step, carry):
        rows = weight[span(step, units)].reshape(units * unit, weight.shape[-1])
        store(span(step, units * unit), dot(left[...], rows, TURNED))
        return carry

    lax.fori_loop(0, weight.shape[0] // units, row_step, 0)


def into(target):
    def store(columns, value):
        target[:, columns] = value.astype(target.dtype)

    return store


ROWS = 32


def by_rows(count, step):
    def body(index, carry):
        step(span(index, ROWS))
        return carry

    lax.fori_loop(0, count // ROWS, body, 0)


def norm_forward(total, gains, index, unit, scale, use):
    gain, shift = gains[index : index + 1, :], gains[index + 3 : index + 4, :]

    def step(rows):
        value = total[rows, :]
        centre = value - jnp.mean(value, axis=-1, keepdims=True)
        spread = jnp.mean(centre * centre, axis=-1, keepdims=True)
        root = lax.rsqrt(spread + EPS)
        scaled = centre * root
        unit[rows, :] = scaled
        scale[rows, :] = root
        use(rows, scaled * gain + shift)

    by_rows(total.shape[0], step)


def norm_slope(incoming, scaled, root, gain):
    width = scaled.shape[1]
    scaled_grad = incoming * gain
    first = jnp.mean(scaled_grad, axis=-1, keepdims=True)
    second = jnp.mean(scaled_grad * scaled, axis=-1, keepdims=True)
    value = root * (scaled_grad - first - scaled * second)
    of_gain = jnp.sum((incoming * scaled).reshape(ROWS // 8, 8, width), axis=0)
    of_shift = jnp.sum(incoming.reshape(ROWS // 8, 8, width), axis=0)
    return value, of_gain, of_shift


def keep_small(index, sums, small):
    for offset, partial in ((index, sums[0]), (index + 3, sums[1])):
        line = jnp.sum(partial, axis=0, keepdims=True)
        for group in range(2 * small.shape[1]):
            small[group % 2, group // 2, offset : offset + 1, :] = line[
                :, group * 128 : (group + 1) * 128
            ]


def norm_backward(grad, gains, index, unit, scale, target, target_low, small):
    gain = gains[index : index + 1, :]

    def body(block, sums):
        rows = span(block, ROWS)
        value, of_gain, of_shift = norm_slope(grad[rows, :], unit[rows, :], scale[rows, :], gain)
        target[rows, :] = value
        target_low[rows, :] = value.astype(target_low.dtype)
        return (sums[0] + of_gain, sums[1] + of_shift)

    zero = jnp.zeros((8, unit.shape[1]), jnp.float32)
    keep_small(index, lax.fori_loop(0, unit.shape[0] // ROWS, body, (zero, zero)), small)


def norm_both(total, grad, gains, index, result, target, target_low, small):
    gain, shift = gains[index : index + 1, :], gains[index + 3 : index + 4, :]

    def body(block, sums):
        rows = span(block, ROWS)
        value = total[rows, :]
        centre = value - jnp.mean(value, axis=-1, keepdims=True)
        spread = jnp.mean(centre * centre, axis=-1, keepdims=True)
        root = lax.rsqrt(spread + EPS)
        scaled = centre * root
        result[rows, :] = scaled * gain + shift
        incoming = grad[rows, :].astype(jnp.float32)
        value, of_gain, of_shift = norm_slope(incoming, scaled, root, gain)
        target[rows, :] = value
        target_low[rows, :] = value.astype(target_low.dtype)
        return (sums[0] + of_gain, sums[1] + of_shift)

    zero = jnp.zeros((8, total.shape[1]), jnp.float32)
    keep_small(index, lax.fori_loop(0, total.shape[0] // ROWS, body, (zero, zero)), small)


def lane_masks(dtype, scale):
    low = lax.broadcasted_iota(jnp.int32, (1, 2 * HEAD_DIM), 1) < HEAD_DIM
    first = jnp.where(low, scale, 0.0)
    return first.astype(dtype), (scale - first).astype(dtype)


def turned_pair(eye, rows):
    size = rows.shape[1]
    return dot(eye[0:size, 0:size], rows, TURNED).astype(rows.dtype)


def attention_forward(query, keys, values, bias, blocks, eye, mixed, turned, lse, first, last):
    masks = lane_masks(query.dtype, SCALE)

    def pair_step(pair, carry):
        lanes = span(pair, 2 * HEAD_DIM)
        two_query, two_keys, two_values = query[:, lanes], keys[:, lanes], values[:, lanes]
        columns = []
        for q0, q1, k0, k1 in blocks:
            block_values = turned_pair(eye, two_values[k0:k1])
            rows = []
            for head in range(2):
                scores = dot(two_keys[k0:k1], two_query[q0:q1] * masks[head], TURNED)
                scores = scores + bias[k0:k1, q0:q1]
                top = jnp.max(scores, axis=0, keepdims=True)
                weight = jnp.exp(scores - top)
                norm = jnp.sum(weight, axis=0, keepdims=True)
                head_values = block_values[head * HEAD_DIM : (head + 1) * HEAD_DIM]
                rows.append(dot(head_values, weight.astype(query.dtype)) * (1.0 / norm))
                lse[pair, head : head + 1, q0:q1] = top + jnp.log(norm)
            columns.append(jnp.concatenate(rows, axis=0))
        total = jnp.concatenate(columns, axis=1).astype(mixed.dtype)
        turned[pair % 2, span(pair // 2, 2 * HEAD_DIM), :] = total
        mixed[:, lanes] = dot(eye[...], total, TURNED).astype(mixed.dtype)
        return carry

    lax.fori_loop(first, last, pair_step, 0)


def stacked(parts):
    cuts = sorted({at for first, value in parts for at in (first, first + value.shape[0])})
    found = []
    for low, high in zip(cuts, cuts[1:]):
        total = None
        for first, value in parts:
            if first <= low and high <= first + value.shape[0]:
                piece = value[low - first : high - first]
                total = piece if total is None else total + piece
        found.append(total)
    return jnp.concatenate(found, axis=0)


def attention_backward(
    query, keys, values, bias, blocks, eye, lse, grad, query_grad, key_grad, value_grad, first, last
):
    scaled, masks = lane_masks(query.dtype, SCALE), lane_masks(query.dtype, 1.0)

    def pair_step(pair, carry):
        lanes = span(pair, 2 * HEAD_DIM)
        two_query, two_keys, two_values = query[:, lanes], keys[:, lanes], values[:, lanes]
        two_grad = grad[:, lanes]
        of_query, of_keys, of_values = [], [], []
        for q0, q1, k0, k1 in blocks:
            block_keys, block_values = two_keys[k0:k1], two_values[k0:k1]
            slopes, all_probs, heads_query, heads_grad = [], [], [], []
            for head in range(2):
                head_query = two_query[q0:q1] * scaled[head]
                head_grad = two_grad[q0:q1] * masks[head]
                scores = dot(block_keys, head_query, TURNED) + bias[k0:k1, q0:q1]
                probs = jnp.exp(scores - lse[pair, head : head + 1, q0:q1])
                pulled = dot(block_values, head_grad, TURNED)
                inner = jnp.sum(probs * pulled, axis=0, keepdims=True)
                slopes.append((probs * (pulled - inner)).astype(query.dtype))
                all_probs.append(probs.astype(query.dtype))
                heads_query.append(head_query)
                heads_grad.append(head_grad)
            both = jnp.concatenate(slopes, axis=1)
            of_keys.append((k0, dot(both, jnp.concatenate(heads_query, axis=0))))
            both = jnp.concatenate(all_probs, axis=1)
            of_values.append((k0, dot(both, jnp.concatenate(heads_grad, axis=0))))
            block_turned = turned_pair(eye, block_keys * jnp.asarray(SCALE, query.dtype))
            rows = [
                dot(block_turned[head * HEAD_DIM : (head + 1) * HEAD_DIM], slopes[head])
                for head in range(2)
            ]
            of_query.append(jnp.concatenate(rows, axis=0))
        total = jnp.concatenate(of_query, axis=1).astype(query_grad.dtype)
        query_grad[:, lanes] = dot(eye[...], total, TURNED).astype(query_grad.dtype)
        key_grad[:, lanes] = stacked(of_keys).astype(key_grad.dtype)
        value_grad[:, lanes] = stacked(of_values).astype(value_grad.dtype)
        return carry

    lax.fori_loop(first, last, pair_step, 0)


def turn_blocks(left, eye, store):
    width = eye.shape[0]
    for block in range(left.shape[1] // width):
        columns = pl.ds(block * width, width)
        store(block, dot(eye[...], left[:, columns], TURNED).astype(left.dtype))


def turn_by_lane(left, eye, target):
    group = eye.shape[0] // 2

    def store(block, value):
        target[0, pl.ds(block * group, group), :] = value[:group]
        target[1, pl.ds(block * group, group), :] = value[group:]

    turn_blocks(left, eye, store)


SQUARES = 8


def layer_kernel(places, sizes, *refs):
    n_rows, n_mem, width, ff, shard = sizes
    ref = SimpleNamespace(**jax.tree.map(lambda place: refs[place], places))
    place = Place(n_rows, n_mem)
    many = ff // width
    own_ff = ff // (n_rows * n_mem)
    (
        at_query,
        at_key,
        at_value,
        at_output,
        at_cross_query,
        at_cross_key,
        at_cross_value,
        at_cross_output,
    ) = range(SQUARES)
    full = ref.full
    expand, contract = ref.expand_full, ref.contract_full
    tokens, gains = ref.tokens, ref.gains
    low, turned = SimpleNamespace(**ref.low), SimpleNamespace(**ref.turned)

    order = [
        at_query,
        at_key,
        at_value,
        at_output,
        at_cross_key,
        at_cross_value,
        at_cross_query,
        at_cross_output,
    ]
    pool = ref.pool

    def gather_slot(number):
        return pool.at[pl.ds(number % GATHER_SLOTS * n_rows, n_rows)]

    sources = [ref.squares[index] for index in order]
    sources += [ref.expand.at[:, pl.ds(j * width, width)] for j in range(many)]
    sources += [ref.contract.at[pl.ds(j * shard, shard), :] for j in range(many)]
    stores = [full[index] for index in order] + [expand.at[j] for j in range(many)]
    stores += [contract.at[:, :, j] for j in range(many)]
    parts, cuts = [], []
    for n, item in enumerate(sources):
        pieces_here = width // TILE if n in (0, len(sources) - 1) else 1
        for i in range(pieces_here):
            size = width // pieces_here
            columns = pl.ds(i * size, size)
            near = int(i == 2 if n == 0 else n % 5 in NEAR)
            parts.append(
                Part(item.at[:, columns], gather_slot(n).at[:, :, :, columns], near)
            )
            cuts.append((n, i, pieces_here))
    parts.insert(SMALL_AT, Part(ref.small, ref.small_full, 0, True))
    cuts.insert(SMALL_AT, None)
    gather = Gather(place, parts, ref.gather_sems)

    def keep(number):
        return pltpu.make_async_copy(gather_slot(number), stores[number], ref.keep_sem.at[number])

    count = [0]

    def load_slot(number):
        first = pool.shape[0] - (1 + number % SLOTS) * n_rows
        return pool.at[pl.ds(first, n_rows)]

    def load(pieces):
        number = count[0]
        count[0] += 1
        for source, first, rows in pieces:
            target = load_slot(number).at[pl.ds(first, rows)]
            pltpu.make_async_copy(source, target, ref.slot_sem.at[number % SLOTS]).start()
        return number

    def ready(number):
        slot = load_slot(number)
        pltpu.make_async_copy(slot, slot, ref.slot_sem.at[number % SLOTS]).wait()
        return slot

    def contract_rows(j):
        groups = n_rows // many
        return [(contract.at[j * groups + i], i * n_mem, n_mem) for i in range(groups)]

    mem_block = ref.memory.shape[1]
    memory, mem_rows = ref.memory, ref.mem_rows

    def memory_own():
        return pltpu.make_async_copy(
            memory.at[place.mem], mem_rows.at[span(place.mem, mem_block)], ref.mem_sem.at[0]
        )

    def memory_total():
        some = mem_rows.at[pl.ds(0, (n_mem - 1) * mem_block)]
        return remote(some, some, ref.mem_sem.at[1], ref.mem_sem.at[2], place.far(1))

    ref.small[...] = jnp.zeros_like(ref.small)
    for member in range(n_mem):

        @pl.when(place.mem == member)
        def _(member=member):
            lanes = slice(member * shard, (member + 1) * shard)
            ref.small[0:3, lanes] = ref.norm_gains[...].astype(jnp.float32)
            ref.small[3:6, lanes] = ref.norm_shifts[...].astype(jnp.float32)

    place.greet()
    memory_own().start()
    for step in range(1, n_mem):
        remote(
            memory.at[(place.mem + step) % n_mem],
            mem_rows.at[span(place.mem, mem_block)],
            ref.mem_sem.at[1],
            ref.mem_sem.at[2],
            place.far(step),
        ).start()

    actions, whole = [], []
    for part in range(len(parts)):
        found, time = gather.events(part)
        for hop, (at, action) in enumerate(found):
            actions.append((HOP + 10 * part + hop, at, action))
        whole.append(time)
    first_hops = [HOP, HOP + 10]
    for code, _, action in actions:
        if code in first_hops:
            action()
    actions = [item for item in actions if item[0] not in first_hops]

    self_bias, cross_bias, eye = ref.self_bias, ref.cross_bias, ref.eye
    own_row = ref.token_ids[pl.ds(place.mem, 1), :].astype(jnp.float32)
    mem_row = ref.memory_ids[pl.ds(place.mem, 1), :].astype(jnp.float32)
    key_place = lax.broadcasted_iota(jnp.int32, self_bias.shape, 0)
    query_place = lax.broadcasted_iota(jnp.int32, self_bias.shape, 1)
    own_wide = jnp.broadcast_to(own_row, self_bias.shape)
    mem_wide = jnp.broadcast_to(mem_row, (cross_bias.shape[1], cross_bias.shape[0]))
    same = (jnp.transpose(own_wide) == own_wide) & (key_place <= query_place)
    self_bias[...] = jnp.where(same, 0.0, NEG)
    cross_bias[...] = jnp.where(jnp.transpose(mem_wide) == own_row, 0.0, NEG)
    eye_row = lax.broadcasted_iota(jnp.int32, eye.shape, 0)
    eye_column = lax.broadcasted_iota(jnp.int32, eye.shape, 1)
    eye[...] = jnp.where(eye_row == eye_column, 1.0, 0.0).astype(eye.dtype)
    turn_by_lane(tokens, eye, turned.tokens)

    accumulated, other = ref.accumulated, ref.other
    hidden, slope, hidden_turned = ref.hidden, ref.slope, ref.hidden_turned

    def small_piece():
        blocks = ref.small_full
        for group in range(n_rows):
            total = None
            for member in range(n_mem):
                value = blocks[group, member]
                total = value if total is None else total + value
            gains[:, group * 128 : (group + 1) * 128] = total

    def query_piece(i, count, slot):
        times(tokens, slot, into(ref.query), i, count)

    def key_piece(slot):
        times(tokens, slot, into(ref.keys))

    pairs = width // (2 * HEAD_DIM)
    self_blocks = [
        (first, first + 128, max(first - DOC_LIMIT, 0), first + 128)
        for first in range(0, self_bias.shape[1], 128)
    ]
    cross_blocks = [(0, cross_bias.shape[1], 0, cross_bias.shape[0])]

    def value_piece(slot):
        times(tokens, slot, into(ref.values))

    def self_forward(first, last, slot):
        attention_forward(
            ref.query,
            ref.keys,
            ref.values,
            self_bias,
            self_blocks,
            eye,
            ref.attended,
            turned.attended,
            ref.self_lse,
            first,
            last,
        )

    def output_piece(slot):
        def store(columns, value):
            accumulated[:, columns] = ALPHA * tokens[:, columns].astype(jnp.float32) + value

        times(ref.attended, slot, store)

    def output_norm(slot):
        def use(rows, value):
            ref.first_low[rows, :] = value.astype(jnp.bfloat16)
            other[rows, :] = value

        norm_forward(accumulated, gains, 0, ref.unit1, ref.scale1, use)

    def cross_key_piece(slot):
        memory_own().wait()
        memory_total().wait_recv()
        times(mem_rows, slot, into(ref.cross_keys))
        turn_by_lane(mem_rows, eye, turned.memory)

    def cross_value_piece(slot):
        times(mem_rows, slot, into(ref.cross_values))
        turn_by_lane(ref.first_low, eye, turned.first)

    def cross_query_piece(slot):
        times(ref.first_low, slot, into(ref.cross_query))

    def cross_forward(first, last, slot):
        attention_forward(
            ref.cross_query,
            ref.cross_keys,
            ref.cross_values,
            cross_bias,
            cross_blocks,
            eye,
            ref.crossed,
            turned.crossed,
            ref.cross_lse,
            first,
            last,
        )

    def cross_output_piece(slot):
        def store(columns, value):
            accumulated[:, columns] = ALPHA * other[:, columns] + value

        times(ref.crossed, slot, store)

    def cross_output_norm(slot):
        def use(rows, value):
            ref.second_low[rows, :] = value.astype(jnp.bfloat16)
            other[rows, :] = value

        norm_forward(accumulated, gains, 1, ref.unit2, ref.scale2, use)

    def expand_piece(j, half, slot):
        def store(columns, value):
            there = pl.ds(pl.multiple_of(j * width + columns.start, TILE), columns.size)
            bell = 0.5 * (1.0 + lax.erf(value * math.sqrt(0.5)))
            density = jnp.exp(value * value * -0.5) * (1.0 / math.sqrt(2.0 * math.pi))
            hidden[:, there] = (value * bell).astype(hidden.dtype)
            slope[:, there] = (bell + value * density).astype(slope.dtype)

        times(ref.second_low, slot, store, half, 2)

    def expand_turn(j, slot):
        def keep(block, value):
            for index in range(value.shape[0] // shard):
                first = j * width + block * value.shape[0] + index * shard
                device, job = first // own_ff, first % own_ff // shard
                group, member = device // n_mem, device % n_mem
                at = group // 2 * n_mem * shard + member * shard
                hidden_turned[job, group % 2, at : at + shard, :] = value[
                    index * shard : (index + 1) * shard
                ]

        turn_blocks(hidden.at[:, pl.ds(j * width, width)], eye, keep)

    def contract_turn(j):
        block = 2 * n_mem * shard
        for index in range(n_rows // 2):
            rows = pl.ds(index * n_mem * shard, n_mem * shard)
            both = jnp.concatenate([hidden_turned[j, 0, rows], hidden_turned[j, 1, rows]], axis=0)
            columns = pl.ds(index * block, block)
            low.branch[:, columns] = dot(eye[...], both, TURNED).astype(jnp.bfloat16)

    def contract_piece(j, i, count, slot):
        if i == 0:
            contract_turn(j)

        def store(columns, value):
            if j == 0:
                accumulated[:, columns] = ALPHA * other[:, columns] + value
            else:
                accumulated[:, columns] = accumulated[:, columns] + value

        times(low.branch, slot, store, i, count)

    quarters = [(pairs * at // 4, pairs * (at + 1) // 4) for at in range(4)]
    whole_pieces = [
        [],
        [key_piece],
        [value_piece] + [functools.partial(self_forward, *quarter) for quarter in quarters],
        [output_piece, output_norm],
        [cross_key_piece],
        [cross_value_piece],
        [cross_query_piece] + [functools.partial(cross_forward, *quarter) for quarter in quarters],
        [cross_output_piece, cross_output_norm],
    ]
    for j in range(many):
        halves = [functools.partial(expand_piece, j, half) for half in range(2)]
        whole_pieces.append(halves + [functools.partial(expand_turn, j)])

    def pieces_of(part):
        if part == SMALL_AT:
            return [small_piece]
        n, i, count = cuts[part]
        found = whole_pieces[n] if n < len(whole_pieces) else []
        if n == 0:
            found = [functools.partial(query_piece, i, count)]
        elif n >= len(whole_pieces):
            found = [functools.partial(contract_piece, n - len(whole_pieces), i, count)]
        return [functools.partial(piece, gather_slot(n)) for piece in found]

    def ends_weight(part):
        return part != SMALL_AT and cuts[part][1] == cuts[part][2] - 1

    def arrive(part):
        gather.core_total(part).wait_recv()
        if ends_weight(part):
            keep(cuts[part][0]).start()

    def settle(part):
        gather.sent(part)
        if ends_weight(part):
            keep(cuts[part][0]).wait()

    last = 0.0
    for part, time in enumerate(whole):
        time = max(time, last + 0.5)
        actions.append((ARRIVE + part, time, functools.partial(arrive, part)))
        for index, piece in enumerate(pieces_of(part)):
            actions.append((USE + 10 * part + index, time + 0.2 + 0.04 * index, piece))
        actions.append((SETTLE + part, time + 0.45, functools.partial(settle, part)))
        last = time
    for action in planned(actions, FORWARD_PLAN):
        action()
    place.tell(ref.ready_sem)

    backward_sources, loads = [], []
    used = [0]

    def next_slot():
        slot = ready(loads[used[0]])
        used[0] += 1
        if len(loads) < len(backward_sources):
            loads.append(load(backward_sources[len(loads)]))
        return slot

    small_sums = ref.small_sums
    small_sums[...] = jnp.zeros_like(small_sums)
    def inner_piece(j):
        slot = next_slot()

        def store(columns, value):
            there = pl.ds(pl.multiple_of(j * width + columns.start, TILE), columns.size)
            slope[:, there] = (value * slope[:, there].astype(jnp.float32)).astype(slope.dtype)

        times_turned(low.third, slot, store)

    def second_piece(j):
        slot = next_slot()

        def store(columns, value):
            if j == 0:
                other[:, columns] = ALPHA * accumulated[:, columns] + value
            else:
                other[:, columns] = other[:, columns] + value

        times_turned(slope.at[:, pl.ds(j * width, width)], slot, store)

    def second_norm_piece():
        norm_backward(
            other, gains, 1, ref.unit2, ref.scale2, accumulated, low.second, small_sums
        )

    def cross_start_piece():
        times_turned(low.second, next_slot(), into(low.branch))

    def cross_piece(first, last):
        attention_backward(
            ref.cross_query,
            ref.cross_keys,
            ref.cross_values,
            cross_bias,
            cross_blocks,
            eye,
            ref.cross_lse,
            low.branch,
            low.cross_query,
            low.cross_key,
            low.cross_value,
            first,
            last,
        )

    def first_piece():
        def store(columns, value):
            other[:, columns] = ALPHA * accumulated[:, columns] + value

        times_turned(low.cross_query, next_slot(), store)

    def first_norm_piece():
        norm_backward(other, gains, 0, ref.unit1, ref.scale1, accumulated, low.first, small_sums)

    def self_start_piece():
        times_turned(low.first, next_slot(), into(low.branch))

    def self_piece(first, last):
        attention_backward(
            ref.query,
            ref.keys,
            ref.values,
            self_bias,
            self_blocks,
            eye,
            ref.self_lse,
            low.branch,
            low.query,
            low.key,
            low.value,
            first,
            last,
        )

    mem_out, mem_in = ref.mem_out, ref.mem_in

    def grad_own():
        return pltpu.make_async_copy(
            mem_out.at[span(place.mem, mem_block)], mem_in.at[place.mem], ref.mem_sem.at[3]
        )

    def grad_total():
        some = mem_in.at[pl.ds(0, n_mem - 1)]
        return remote(some, some, ref.mem_sem.at[4], ref.mem_sem.at[5], place.far(1))

    def memory_key_piece():
        times_turned(low.cross_key, next_slot(), into(other))

    def memory_value_piece():
        def store(columns, value):
            mem_out[:, columns] = (other[:, columns] + value).astype(mem_out.dtype)

        times_turned(low.cross_value, next_slot(), store)
        grad_own().start()
        for step in range(1, n_mem):
            remote(
                mem_out.at[span((place.mem + step) % n_mem, mem_block)],
                mem_in.at[place.mem],
                ref.mem_sem.at[4],
                ref.mem_sem.at[5],
                place.far(step),
            ).start()

    def input_piece(left, start, end=False):
        target = ref.input_grad_here

        def store(columns, value):
            if start:
                target[:, columns] = ALPHA * accumulated[:, columns] + value
            else:
                target[:, columns] = target[:, columns] + value

        times_turned(left, next_slot(), store)
        if end:
            leaving[1].start()

    def memory_end_piece():
        grad_own().wait()
        grad_total().wait_recv()
        for member in range(n_mem):
            ref.memory_grad_here[member] = mem_in[member].astype(jnp.float32)
        leaving[2].start()

    quarter = width // 4
    at_first = ((0, quarter), (quarter, quarter), (2 * quarter, 2 * quarter))
    at_last = ((0, 2 * quarter), (2 * quarter, quarter), (3 * quarter, quarter))
    grads = ref.grads
    plans = []
    for j in range(many):
        for first, columns in at_first if j == 0 else ((0, width),):
            target = ref.contract_grad.at[pl.ds(j * shard, shard), pl.ds(first, columns)]
            plans.append((hidden_turned.at[j], low.third, first, target))
    for j in range(many):
        target = ref.expand_grad.at[:, pl.ds(j * width, width)]
        plans.append((turned.second, slope, j * width, target))
    plans += [
        (turned.crossed, low.second, 0, grads[at_cross_output]),
        (turned.memory, low.cross_key, 0, grads[at_cross_key]),
        (turned.memory, low.cross_value, 0, grads[at_cross_value]),
        (turned.first, low.cross_query, 0, grads[at_cross_query]),
        (turned.attended, low.first, 0, grads[at_output]),
        (small_sums, None, 0, ref.small_total),
        (turned.tokens, low.query, 0, grads[at_query]),
        (turned.tokens, low.key, 0, grads[at_key]),
    ]
    for first, columns in at_last:
        target = grads[at_value].at[:, pl.ds(first, columns)]
        plans.append((turned.tokens, low.value, first, target))
    jobs = [
        Job(*plan, plan[1] is not None and number % 5 in EARLY)
        for number, plan in enumerate(plans)
    ]
    reduce = Reduce(place, jobs, ref.reduce_sems, pool, SimpleNamespace(**ref.little))

    inner = [functools.partial(inner_piece, j) for j in range(many)]
    second = [functools.partial(second_piece, j) for j in range(many)]
    base = many + 2
    def weight(index):
        return [(full[index], 0, n_rows)]

    turn = functools.partial(turn_by_lane, ref.second_low, eye, turned.second)
    crosses = [functools.partial(cross_piece, pair, pair + 1) for pair in range(pairs)]
    selves = [functools.partial(self_piece, pair, pair + 1) for pair in range(pairs)]
    work = [(base - 1.7 + j, inner[j], contract_rows(j)) for j in range(2)]
    work += [(base - 1.3, turn, None)]
    work += [(base - 1.7 + j, inner[j], contract_rows(j)) for j in range(2, many)]
    work += [(base - 0.3 + j, second[j], [(expand.at[j], 0, n_rows)]) for j in range(many)]
    base = 2 * many + 2
    work += [
        (base - 0.2, second_norm_piece, None),
        (base - 0.15, cross_start_piece, weight(at_cross_output)),
    ]
    work += [(base + 0.3 + 0.05 * pair, crosses[pair], None) for pair in range(pairs)]
    work += [
        (base + 1.3, first_piece, weight(at_cross_query)),
        (base + 1.31, first_norm_piece, None),
        (base + 1.7, self_start_piece, weight(at_output)),
    ]
    work += [(base + 2.3 + 0.14 * pair, selves[pair], None) for pair in range(pairs)]
    work += [
        (base + 3.7, memory_key_piece, weight(at_cross_key)),
        (base + 4.3, memory_value_piece, weight(at_cross_value)),
        (base + 4.7, functools.partial(input_piece, low.query, True), weight(at_query)),
        (base + 5.5, functools.partial(input_piece, low.key, False), weight(at_key)),
        (base + 6.5, functools.partial(input_piece, low.value, False, True), weight(at_value)),
        (base + 8.5, memory_end_piece, None),
    ]
    actions = [(WORK + index, at, item) for index, (at, *item) in enumerate(work)]
    for number in range(len(jobs)):
        found = reduce.events(number)
        actions.append((CORE + number, found[0][0], found[0][1:]))
        actions.append((LANE + number, found[1][0], found[1][1:]))
        for stage, (at, action) in enumerate(found[2:]):
            actions.append((STAGE + 10 * number + stage, at, (action,)))
    ordered = planned(actions, BACKWARD_PLAN)
    backward_sources += [item[1] for item in ordered if len(item) > 1 and item[1] is not None]
    loads += [load(backward_sources[0]), load(backward_sources[1])]
    leaving = [
        pltpu.make_async_copy(ref.result_here, ref.result, ref.out_sem.at[0]),
        pltpu.make_async_copy(ref.input_grad_here, ref.input_grad, ref.out_sem.at[1]),
        pltpu.make_async_copy(ref.memory_grad_here, ref.memory_grad, ref.out_sem.at[2]),
    ]
    norm_both(
        accumulated, ref.out_grad, gains, 2, ref.result_here, accumulated, low.third, small_sums
    )
    leaving[0].start()

    place.hear(ref.ready_sem)
    for item in ordered:
        item[0]()

    total = ref.small_total[...]
    own = jnp.zeros((8, shard), jnp.float32)
    for member in range(n_mem):
        here = jnp.where(place.mem == member, 1.0, 0.0)
        own = own + here * total[:, member * shard : (member + 1) * shard]
    ref.gains_grad[...] = own[0:3]
    ref.shifts_grad[...] = own[3:6]
    reduce.finish()
    for copy in leaving:
        copy.wait()
    memory_total().wait_send()
    grad_total().wait_send()


SMALL_AT = 2
DOC_LIMIT = 64
NEAR, EARLY = (1,), (3,)
HOP, ARRIVE, USE, SETTLE, CORE, LANE, STAGE, WORK = range(1000, 9000, 1000)
FORWARD_PLAN = (
    1001, 1020, 1030, 1002, 1040, 1031, 1011, 1021, 1003, 1041, 1050, 1060, 1022, 1012, 1042, 1070,
    1004, 1032, 1061, 1013, 1051, 1080, 1014, 2000, 2001, 1023, 1033, 3000, 1062, 1034, 1090, 3010,
    1052, 1063, 2002, 3020, 4000, 1064, 1100, 4001, 1043, 1071, 2003, 1053, 1081, 1044, 4002, 1072,
    2004, 1091, 1110, 3030, 1082, 4003, 3040, 4004, 1054, 1101, 2005, 1092, 1111, 1073, 1120, 2006,
    3050, 4005, 1083, 1102, 3060, 3061, 3062, 3063, 1093, 1074, 3064, 1130, 4006, 2007, 3070, 1084,
    1112, 3071, 1103, 4007, 1131, 1140, 1121, 2008, 1113, 1094, 3080, 2009, 1150, 1132, 1141, 1104,
    3090, 1114, 4008, 1160, 1122, 4009, 2010, 3100, 1151, 1142, 3101, 3102, 1123, 3103, 1161, 1133,
    2011, 3104, 3110, 1170, 1124, 4010, 1143, 3111, 1162, 1152, 2012, 4011, 1134, 3120, 3121, 1180,
    3122, 1144, 1153, 1171, 2013, 1181, 1190, 3130, 1172, 4012, 3131, 1200, 1163, 3132, 4013, 1191,
    1182, 2014, 1173, 3140, 1154, 3141, 3142, 1210, 1183, 2015, 3150, 3151, 3152, 1220, 1164, 4014,
    1221, 4015, 1174, 1192, 2016, 1201, 1211, 3160, 1193, 1202, 1222, 1184, 1212, 4016, 2017, 3170,
    1203, 1223, 1194, 1213, 2018, 4017, 3180, 4018, 1204, 2019, 1214, 1224, 2020, 3190, 3200, 2021,
    4019, 4020, 3210, 4021, 2022, 3220, 4022,
)
BACKWARD_PLAN = (
    5000, 5001, 6000, 6001, 5002, 7000, 6002, 5003, 8002, 7001, 8000, 5004, 8003, 7010, 7020, 6003,
    7011, 5005, 8005, 7002, 6004, 7021, 7012, 8001, 7030, 7003, 8006, 6005, 5006, 8007, 7040, 6006,
    7022, 5007, 8004, 7031, 8008, 7023, 7041, 7050, 5008, 7013, 6007, 5009, 8009, 7060, 8010, 7051,
    8011, 7042, 8012, 6008, 7070, 6009, 8013, 8014, 7061, 8015, 7032, 5010, 8016, 7080, 8017, 6010,
    8018, 5011, 7043, 7062, 8019, 7052, 7033, 8020, 7071, 8021, 7090, 8022, 5012, 7081, 7100, 7063,
    8023, 6011, 8024, 7091, 5013, 8025, 6012, 7053, 7072, 7082, 8026, 7092, 8027, 7110, 7101, 6013,
    8028, 7073, 8029, 5014, 7102, 7083, 5015, 8030, 7111, 6014, 5016, 7103, 7130, 6015, 7120, 6016,
    7093, 7112, 8031, 8032, 5017, 7150, 7121, 8033, 7140, 7131, 6017, 7141, 7122, 8035, 7113, 5018,
    7160, 6018, 7151, 5019, 7142, 5020, 7170, 7161, 6019, 7180, 8034, 7123, 7162, 7171, 7132, 7190,
    6020, 7191, 7181, 7143, 7200, 7133, 7152, 7172, 7201, 7182, 7163, 7192, 7173, 7183, 7202, 7193,
    7203,
)


def planned(actions, plan):
    codes = {code for code, _, _ in actions}
    if codes == set(plan):
        at = {code: number for number, code in enumerate(plan)}
        return [item for code, _, item in sorted(actions, key=lambda action: at[action[0]])]
    return [item for _, _, item in sorted(actions, key=lambda action: action[1])]


def copy_kernel(count, *refs):
    sources, targets, held = refs[:count], refs[count : 2 * count], refs[2 * count : 3 * count]
    in_sem, out_sem = refs[3 * count :]
    ins = [pltpu.make_async_copy(sources[i], held[i], in_sem.at[i]) for i in range(count)]
    outs = [pltpu.make_async_copy(held[i], targets[i], out_sem.at[i]) for i in range(count)]
    for copy in ins:
        copy.start()
    for into_held, out_of_held in zip(ins, outs):
        into_held.wait()
        out_of_held.start()
    for copy in outs:
        copy.wait()


def copied(values):
    count = len(values)
    anywhere = pl.BlockSpec(memory_space=pl.ANY)
    dma = pltpu.SemaphoreType.DMA
    return pl.pallas_call(
        functools.partial(copy_kernel, count),
        out_shape=[jax.ShapeDtypeStruct(value.shape, value.dtype) for value in values],
        in_specs=[anywhere] * count,
        out_specs=[anywhere] * count,
        scratch_shapes=[pltpu.VMEM(value.shape, value.dtype) for value in values]
        + [dma((count,)), dma((count,))],
        compiler_params=pltpu.CompilerParams(vmem_limit_bytes=VMEM_LIMIT),
        name="results",
    )(*values)


def fused(n_rows, n_mem, ins):
    tokens, memory, squares = ins["tokens"], ins["memory"], ins["squares"]
    expand, contract = ins["expand"], ins["contract"]
    tokens_here, width = tokens.shape
    ff = expand.shape[1]
    shard = squares[0].shape[0]
    mem_tokens = memory.shape[0] * memory.shape[1]
    digits, half, many = (n_rows // 2).bit_length() - 1, n_rows // 2, ff // width
    pairs = width // (2 * HEAD_DIM)
    low, high = jnp.bfloat16, jnp.float32
    n_weights = SQUARES + 2 * many
    n_parts = n_weights - 1 + 2 * (width // TILE)
    n_jobs = n_weights + 5
    n_stages = digits + n_mem.bit_length() - 1
    dma, vmem = pltpu.SemaphoreType.DMA, pltpu.VMEM
    anywhere, near = pl.BlockSpec(memory_space=pl.ANY), pl.BlockSpec(memory_space=pltpu.VMEM)

    far_ins = dict(memory=memory)
    in_specs = {
        name: jax.tree.map(lambda _: anywhere if name in far_ins else near, value)
        for name, value in ins.items()
    }

    def out(shape, dtype=high):
        return jax.ShapeDtypeStruct(shape, dtype)

    outs = dict(
        result=out(tokens.shape),
        input_grad=out(tokens.shape),
        memory_grad=out(memory.shape),
        grads=[out(item.shape) for item in squares],
        expand_grad=out(expand.shape),
        contract_grad=out(contract.shape),
        gains_grad=out((3, shard)),
        shifts_grad=out((3, shard)),
    )
    far_outs = dict(
        full=[out((n_rows, n_mem, shard, width), low)] * SQUARES,
        expand_full=out((many, n_rows, n_mem, shard, width), low),
        contract_full=out((n_rows, n_mem, many, shard, width), low),
    )
    early_outs = ("result", "input_grad", "memory_grad")
    out_specs = {
        name: anywhere if name in early_outs else jax.tree.map(lambda _: near, value)
        for name, value in outs.items()
    }
    out_specs.update(jax.tree.map(lambda _: anywhere, far_outs))
    outs.update(far_outs)

    def token_rows(dtype):
        return vmem((tokens_here, width), dtype)

    def memory_rows(dtype):
        return vmem((mem_tokens, width), dtype)

    tiny = (8, 128)

    counts = [half >> (stage + 1) for stage in range(digits)]
    units = (OUT_SLOTS + LANE_SLOTS + CORE_RING) * half
    units += (SUM_SLOTS + FIRST_RING) * half // 2
    units += (SUM_SLOTS + RING) * (sum(counts[1:]) + 1)
    units += (SUM_SLOTS + EARLY_RING) * (sum(counts[1:-1]) + 2 + 1)
    units = max(units + SLOTS * n_rows, GATHER_SLOTS * n_rows)
    little = dict(
        lanes=vmem((half,) + tiny, high),
        core_in=vmem((half,) + tiny, high),
        sums=[vmem((number,) + tiny, high) for number in counts],
        arrived=[vmem((number,) + tiny, high) for number in counts]
        + [vmem((n_mem - 1,) + tiny, high)],
    )
    left = vmem((2, width // 2, tokens_here), low)
    scratch = dict(
        result_here=token_rows(high),
        input_grad_here=token_rows(high),
        memory_grad_here=vmem(memory.shape, high),
        out_sem=dma((3,)),
        small=vmem(tiny, high),
        small_full=vmem((n_rows, n_mem) + tiny, high),
        small_total=vmem(tiny, high),
        pool=vmem((units, n_mem, shard, width), low),
        slot_sem=dma((SLOTS,)),
        keep_sem=dma((n_weights,)),
        ready_sem=pltpu.SemaphoreType.REGULAR,
        mem_sem=dma((6,)),
        gather_sems=[
            dma(shape + (n_parts,))
            for shape in ((), (), (), (digits,), (digits,), (), ())
            + ((n_mem.bit_length() - 1,), (n_mem.bit_length() - 1,))
        ],
        reduce_sems=[
            dma(shape + (n_jobs,))
            for shape in ((), (), (n_stages,), (n_stages,))
        ],
        gains=vmem((8, width), high),
        query=token_rows(low),
        keys=token_rows(low),
        values=token_rows(low),
        attended=token_rows(low),
        first_low=token_rows(low),
        second_low=token_rows(low),
        cross_query=token_rows(low),
        crossed=token_rows(low),
        cross_keys=memory_rows(low),
        cross_values=memory_rows(low),
        mem_rows=memory_rows(low),
        mem_out=memory_rows(low),
        mem_in=vmem(memory.shape, low),
        unit1=token_rows(high),
        unit2=token_rows(high),
        accumulated=token_rows(high),
        other=token_rows(high),
        scale1=vmem((tokens_here, 1), high),
        scale2=vmem((tokens_here, 1), high),
        self_bias=vmem((tokens_here, tokens_here), high),
        cross_bias=vmem((mem_tokens, tokens_here), high),
        self_lse=vmem((pairs, 2, tokens_here), high),
        cross_lse=vmem((pairs, 2, tokens_here), high),
        eye=vmem((TILE, TILE), low),
        hidden=vmem((tokens_here, ff), low),
        slope=vmem((tokens_here, ff), low),
        hidden_turned=vmem((many, 2, width // 2, tokens_here), low),
        turned=dict(
            tokens=left, attended=left, first=left, memory=left, crossed=left, second=left
        ),
        low=dict(
            third=token_rows(low),
            second=token_rows(low),
            first=token_rows(low),
            branch=token_rows(low),
            cross_query=token_rows(low),
            cross_key=memory_rows(low),
            cross_value=memory_rows(low),
            query=token_rows(low),
            key=token_rows(low),
            value=token_rows(low),
        ),
        small_sums=vmem((2, half) + tiny, high),
        little=little,
    )
    in_values, in_tree = jax.tree.flatten(ins)
    out_shapes, out_tree = jax.tree.flatten(outs)
    scratch_shapes, scratch_tree = jax.tree.flatten(scratch)
    places = jax.tree.unflatten(in_tree, range(len(in_values)))
    at = len(in_values)
    places.update(jax.tree.unflatten(out_tree, range(at, at + len(out_shapes))))
    at += len(out_shapes)
    places.update(jax.tree.unflatten(scratch_tree, range(at, at + len(scratch_shapes))))
    values = pl.pallas_call(
        functools.partial(layer_kernel, places, (n_rows, n_mem, width, ff, shard)),
        out_shape=out_shapes,
        in_specs=jax.tree.leaves(in_specs),
        out_specs=jax.tree.leaves(out_specs),
        scratch_shapes=scratch_shapes,
        compiler_params=pltpu.CompilerParams(
            collective_id=0, has_side_effects=True, vmem_limit_bytes=VMEM_LIMIT
        ),
        name="layer",
    )(*in_values)
    found = jax.tree.unflatten(out_tree, values)
    for name in far_outs:
        del found[name]
    return found


def local(n_rows, n_mem, *args):
    (
        tokens,
        memory,
        token_ids,
        memory_ids,
        out_grad,
        self_query,
        self_key,
        self_value,
        self_output,
        cross_query,
        cross_key,
        cross_value,
        cross_output,
        expand_weight,
        contract_weight,
        norm_gains,
        norm_shifts,
    ) = args
    shard, width = self_query.shape
    suits = width == 128 * n_rows and shard % 16 == 0 and tokens.shape[0] == 1
    suits = suits and tokens.shape[1] == TILE and expand_weight.shape[1] == n_mem * width
    if not suits or n_rows < 4 or n_rows & (n_rows - 1) or n_mem < 2 or n_mem & (n_mem - 1):
        return plain(*args)
    found = fused(
        n_rows,
        n_mem,
        dict(
            tokens=tokens[0],
            memory=memory,
            token_ids=token_ids,
            memory_ids=memory_ids,
            out_grad=out_grad[0],
            squares=[
                self_query,
                self_key,
                self_value,
                self_output,
                cross_query,
                cross_key,
                cross_value,
                cross_output,
            ],
            expand=expand_weight,
            contract=contract_weight,
            norm_gains=norm_gains,
            norm_shifts=norm_shifts,
        ),
    )
    values, tree = jax.tree.flatten(found)
    found = SimpleNamespace(**jax.tree.unflatten(tree, copied(values)))
    return (
        found.result[None],
        found.input_grad[None],
        found.memory_grad,
        *found.grads,
        found.expand_grad,
        found.contract_grad,
        found.gains_grad,
        found.shifts_grad,
    )


def solution(mesh):
    in_specs = (
        P(("rows", "mem"), None, None),
        P("rows", "mem", None),
        P("rows", None),
        P("rows", None),
        P(("rows", "mem"), None, None),
        P(("rows", "mem"), None),
        P(("rows", "mem"), None),
        P(("rows", "mem"), None),
        P(("rows", "mem"), None),
        P(("rows", "mem"), None),
        P(("rows", "mem"), None),
        P(("rows", "mem"), None),
        P(("rows", "mem"), None),
        P(("rows", "mem"), None),
        P(("rows", "mem"), None),
        P(None, ("rows", "mem")),
        P(None, ("rows", "mem")),
    )
    out_specs = (
        P(("rows", "mem"), None, None),
        P(("rows", "mem"), None, None),
        P("rows", "mem", None),
        P(("rows", "mem"), None),
        P(("rows", "mem"), None),
        P(("rows", "mem"), None),
        P(("rows", "mem"), None),
        P(("rows", "mem"), None),
        P(("rows", "mem"), None),
        P(("rows", "mem"), None),
        P(("rows", "mem"), None),
        P(("rows", "mem"), None),
        P(("rows", "mem"), None),
        P(None, ("rows", "mem")),
        P(None, ("rows", "mem")),
    )
    layer = functools.partial(local, mesh.shape["rows"], mesh.shape["mem"])
    return jax.shard_map(layer, mesh=mesh, in_specs=in_specs, out_specs=out_specs, check_vma=False)
```

```python
import functools
import math
from types import SimpleNamespace

import jax
import jax.numpy as jnp
from jax import lax
from jax.experimental import pallas as pl
from jax.experimental.pallas import tpu as pltpu
from jax.sharding import PartitionSpec as P

MESH = pl.DeviceIdType.MESH

HEADS = 16
HEAD_DIM = 64


ALPHA = 4.16
EPS = 1e-05
SCALE = 0.125
NEG = -1e30


def layer_norm(hidden_activation, gain, shift):
    centre = hidden_activation - jnp.mean(hidden_activation, axis=-1, keepdims=True)
    spread = jnp.mean(centre * centre, axis=-1, keepdims=True)
    return centre * lax.rsqrt(spread + EPS) * gain + shift


def gelu_exact(value):
    return jax.nn.gelu(value, approximate=False)


def product(left, right):
    return jnp.dot(left, right, preferred_element_type=jnp.float32)


def split_heads(matrix):
    return matrix.reshape(matrix.shape[0], matrix.shape[1] // HEAD_DIM, HEAD_DIM)


def grouped(matrix):
    return jnp.moveaxis(matrix.reshape(matrix.shape[0], HEADS // 4, 4 * HEAD_DIM), 1, 0)


def ungrouped(stack):
    return jnp.moveaxis(stack, 0, 1).reshape(stack.shape[1], stack.shape[0] * stack.shape[2])


def row_map(function, items):
    return lax.map(lambda entry: function(*entry), items)


def score_block(query, keys, allowed):
    raw = jnp.einsum(
        "khe,qhe->hkq", split_heads(keys), split_heads(query), preferred_element_type=jnp.float32
    )
    return jnp.where(allowed[None], raw * SCALE, NEG)


def attend_probs(query, keys, allowed, lse):
    scores = score_block(query, keys, allowed)
    return jnp.where(allowed[None], jnp.exp(scores - lse[:, None, :]), 0.0)


def attend_forward(query, keys, values, allowed):
    scores = score_block(query, keys, allowed)
    top = jnp.max(scores, axis=1)
    weight = jnp.where(allowed[None], jnp.exp(scores - top[:, None, :]), 0.0)
    total = jnp.sum(weight, axis=1)
    probs = (weight / total[:, None, :]).astype(jnp.bfloat16)
    mixed = jnp.einsum(
        "hkq,khe->qhe", probs, split_heads(values), preferred_element_type=jnp.float32
    )
    return (mixed.reshape(query.shape), top + jnp.log(total))


def value_pull(grad, values):
    return jnp.einsum(
        "qhe,khe->hkq", split_heads(grad), split_heads(values), preferred_element_type=jnp.float32
    )


def score_grads(probs, pulled, inner):
    return (probs * (pulled - inner[:, None, :]) * SCALE).astype(jnp.bfloat16)


def query_from(score_grad, keys, shape):
    moved = jnp.einsum(
        "hkq,khe->qhe", score_grad, split_heads(keys), preferred_element_type=jnp.float32
    )
    return moved.reshape(shape)


def key_from(score_grad, query, shape):
    moved = jnp.einsum(
        "hkq,qhe->khe", score_grad, split_heads(query), preferred_element_type=jnp.float32
    )
    return moved.reshape(shape)


def value_from(probs, grad, values):
    moved = jnp.einsum(
        "hkq,qhe->khe",
        probs.astype(jnp.bfloat16),
        split_heads(grad),
        preferred_element_type=jnp.float32,
    )
    return moved.reshape(values.shape)


def local_forward(query, keys, values, allowed):

    def one_group(items):
        return attend_forward(items[0], items[1], items[2], allowed)

    mixed, lse = lax.map(one_group, (grouped(query), grouped(keys), grouped(values)))
    return (ungrouped(mixed), lse)


def local_backward(query, keys, values, allowed, lse, grad):

    def one_group(items):
        part_query, part_keys, part_values, part_lse, part_grad = items
        probs = attend_probs(part_query, part_keys, allowed, part_lse)
        pulled = value_pull(part_grad, part_values)
        inner = jnp.sum(probs * pulled, axis=1)
        score_grad = score_grads(probs, pulled, inner)
        return (
            query_from(score_grad, part_keys, part_query.shape),
            key_from(score_grad, part_query, part_keys.shape),
            value_from(probs, part_grad, part_values),
        )

    parts = lax.map(one_group, (grouped(query), grouped(keys), grouped(values), lse, grouped(grad)))
    return (ungrouped(parts[0]), ungrouped(parts[1]), ungrouped(parts[2]))


def plain(
    tokens,
    memory,
    token_ids,
    memory_ids,
    out_grad,
    self_query,
    self_key,
    self_value,
    self_output,
    cross_query,
    cross_key,
    cross_value,
    cross_output,
    expand_weight,
    contract_weight,
    norm_gains,
    norm_shifts,
):
    full = (
        lax.all_gather(self_query, ("rows", "mem"), axis=0, tiled=True),
        lax.all_gather(self_key, ("rows", "mem"), axis=0, tiled=True),
        lax.all_gather(self_value, ("rows", "mem"), axis=0, tiled=True),
        lax.all_gather(self_output, ("rows", "mem"), axis=0, tiled=True),
        lax.all_gather(cross_query, ("rows", "mem"), axis=0, tiled=True),
        lax.all_gather(cross_key, ("rows", "mem"), axis=0, tiled=True),
        lax.all_gather(cross_value, ("rows", "mem"), axis=0, tiled=True),
        lax.all_gather(cross_output, ("rows", "mem"), axis=0, tiled=True),
        lax.all_gather(expand_weight, ("rows", "mem"), axis=0, tiled=True),
        lax.all_gather(contract_weight, ("rows", "mem"), axis=0, tiled=True),
        lax.all_gather(jnp.transpose(norm_gains), ("rows", "mem"), axis=0, tiled=True),
        lax.all_gather(jnp.transpose(norm_shifts), ("rows", "mem"), axis=0, tiled=True),
    )
    (
        self_attention_query,
        decoder_match_label,
        self_attention_value,
        self_attention_output,
        encoder_lookup_probe,
        key_cross,
        value_cross,
        cross_attention_output,
        up_projection,
        narrowing_matrix,
        gain_cols,
        shift_cols,
    ) = full
    gain_rows = jnp.transpose(gain_cols).astype(jnp.float32)
    shift_rows = jnp.transpose(shift_cols).astype(jnp.float32)
    rows_here = tokens.shape[0]
    member = lax.axis_index("mem")
    own_ids = lax.dynamic_slice_in_dim(token_ids, member * rows_here, rows_here, 0)
    positions = jnp.arange(tokens.shape[1], dtype=jnp.int32)
    self_allowed = (own_ids[:, :, None] == own_ids[:, None, :]) & (
        positions[:, None] <= positions[None, :]
    )[None]
    query = product(tokens, self_attention_query).astype(jnp.bfloat16)
    keys = product(tokens, decoder_match_label).astype(jnp.bfloat16)
    values = product(tokens, self_attention_value).astype(jnp.bfloat16)
    self_mixed, self_lse = row_map(local_forward, (query, keys, values, self_allowed))
    attention_result = self_mixed.astype(jnp.bfloat16)
    first, first_back = jax.vjp(
        layer_norm,
        ALPHA * tokens.astype(jnp.float32) + product(attention_result, self_attention_output),
        gain_rows[0],
        shift_rows[0],
    )
    first_reduced = first.astype(jnp.bfloat16)
    cross_queries = product(first_reduced, encoder_lookup_probe).astype(jnp.bfloat16)
    memory_rows = lax.all_to_all(memory, "mem", split_axis=0, concat_axis=1, tiled=True)
    row_ids = lax.dynamic_slice_in_dim(memory_ids, member * rows_here, rows_here, 0)
    cross_allowed = row_ids[:, :, None] == own_ids[:, None, :]
    cross_keys = product(memory_rows, key_cross).astype(jnp.bfloat16)
    cross_values = product(memory_rows, value_cross).astype(jnp.bfloat16)
    cross_mixed, cross_lse = row_map(
        local_forward, (cross_queries, cross_keys, cross_values, cross_allowed)
    )
    cross_attention_result = cross_mixed.astype(jnp.bfloat16)
    second, second_back = jax.vjp(
        layer_norm,
        ALPHA * first + product(cross_attention_result, cross_attention_output),
        gain_rows[1],
        shift_rows[1],
    )
    second_reduced = second.astype(jnp.bfloat16)
    hidden_value, gelu_back = jax.vjp(gelu_exact, product(second_reduced, up_projection))
    hidden_activation = hidden_value.astype(jnp.bfloat16)
    result, third_back = jax.vjp(
        layer_norm,
        ALPHA * second + product(hidden_activation, narrowing_matrix),
        gain_rows[2],
        shift_rows[2],
    )
    third_grad, gain_three, shift_three = third_back(out_grad.astype(jnp.float32))
    feedforward_gradient = third_grad.astype(jnp.bfloat16)
    down_projection_gradient = jnp.einsum(
        "ehj,ehc->jc", hidden_activation, feedforward_gradient, preferred_element_type=jnp.float32
    )
    (inner_grad,) = gelu_back(
        jnp.einsum(
            "hpu,ku->hpk",
            feedforward_gradient,
            narrowing_matrix,
            preferred_element_type=jnp.float32,
        )
    )
    inner_reduced = inner_grad.astype(jnp.bfloat16)
    expand_grad = jnp.einsum(
        "iqg,iqe->ge", second_reduced, inner_reduced, preferred_element_type=jnp.float32
    )
    second_total = ALPHA * third_grad + jnp.einsum(
        "iwm,fm->iwf", inner_reduced, up_projection, preferred_element_type=jnp.float32
    )
    second_grad, gain_two, shift_two = second_back(second_total)
    cross_branch_gradient = second_grad.astype(jnp.bfloat16)
    output_cross_grad = jnp.einsum(
        "nhb,nhc->bc",
        cross_attention_result,
        cross_branch_gradient,
        preferred_element_type=jnp.float32,
    )
    crossed_grad = jnp.einsum(
        "qwp,up->qwu",
        cross_branch_gradient,
        cross_attention_output,
        preferred_element_type=jnp.float32,
    ).astype(jnp.bfloat16)
    query_grads, key_grads, value_grads = row_map(
        local_backward,
        (cross_queries, cross_keys, cross_values, cross_allowed, cross_lse, crossed_grad),
    )
    key_low = key_grads.astype(jnp.bfloat16)
    value_low = value_grads.astype(jnp.bfloat16)
    row_grad = jnp.einsum(
        "sme,de->smd", key_low, key_cross, preferred_element_type=jnp.float32
    ) + jnp.einsum("sme,de->smd", value_low, value_cross, preferred_element_type=jnp.float32)
    key_cross_grad = jnp.einsum(
        "smd,sme->de", memory_rows, key_low, preferred_element_type=jnp.float32
    )
    value_cross_grad = jnp.einsum(
        "smd,sme->de", memory_rows, value_low, preferred_element_type=jnp.float32
    )
    memory_grad = lax.all_to_all(
        row_grad.astype(jnp.bfloat16), "mem", split_axis=1, concat_axis=0, tiled=True
    ).astype(row_grad.dtype)
    probe_lowered_precision = query_grads.astype(jnp.bfloat16)
    query_cross_grad = jnp.einsum(
        "nhb,nhc->bc", first_reduced, probe_lowered_precision, preferred_element_type=jnp.float32
    )
    first_total = ALPHA * second_grad + jnp.einsum(
        "qwp,up->qwu",
        probe_lowered_precision,
        encoder_lookup_probe,
        preferred_element_type=jnp.float32,
    )
    first_grad, gain_one, shift_one = first_back(first_total)
    self_branch_gradient = first_grad.astype(jnp.bfloat16)
    output_self_grad = jnp.einsum(
        "nhb,nhc->bc", attention_result, self_branch_gradient, preferred_element_type=jnp.float32
    )
    attended_grad = jnp.einsum(
        "qwp,up->qwu",
        self_branch_gradient,
        self_attention_output,
        preferred_element_type=jnp.float32,
    ).astype(jnp.bfloat16)
    self_query_reduced, decoder_label_lowered, self_value_reduced = row_map(
        local_backward, (query, keys, values, self_allowed, self_lse, attended_grad)
    )
    self_query_reduced = self_query_reduced.astype(jnp.bfloat16)
    decoder_label_lowered = decoder_label_lowered.astype(jnp.bfloat16)
    self_value_reduced = self_value_reduced.astype(jnp.bfloat16)
    query_self_grad = jnp.einsum(
        "nhb,nhc->bc", tokens, self_query_reduced, preferred_element_type=jnp.float32
    )
    key_self_grad = jnp.einsum(
        "nhb,nhc->bc", tokens, decoder_label_lowered, preferred_element_type=jnp.float32
    )
    value_self_grad = jnp.einsum(
        "nhb,nhc->bc", tokens, self_value_reduced, preferred_element_type=jnp.float32
    )
    input_grad = (
        ALPHA * first_grad
        + jnp.einsum(
            "qwp,up->qwu",
            self_query_reduced,
            self_attention_query,
            preferred_element_type=jnp.float32,
        )
        + jnp.einsum(
            "qwp,up->qwu",
            decoder_label_lowered,
            decoder_match_label,
            preferred_element_type=jnp.float32,
        )
        + jnp.einsum(
            "qwp,up->qwu",
            self_value_reduced,
            self_attention_value,
            preferred_element_type=jnp.float32,
        )
    )
    gain_grad = jnp.stack([gain_one, gain_two, gain_three], axis=1)
    shift_grad = jnp.stack([shift_one, shift_two, shift_three], axis=1)
    sums = (
        lax.psum_scatter(query_self_grad, ("rows", "mem"), scatter_dimension=0, tiled=True),
        lax.psum_scatter(key_self_grad, ("rows", "mem"), scatter_dimension=0, tiled=True),
        lax.psum_scatter(value_self_grad, ("rows", "mem"), scatter_dimension=0, tiled=True),
        lax.psum_scatter(output_self_grad, ("rows", "mem"), scatter_dimension=0, tiled=True),
        lax.psum_scatter(query_cross_grad, ("rows", "mem"), scatter_dimension=0, tiled=True),
        lax.psum_scatter(key_cross_grad, ("rows", "mem"), scatter_dimension=0, tiled=True),
        lax.psum_scatter(value_cross_grad, ("rows", "mem"), scatter_dimension=0, tiled=True),
        lax.psum_scatter(output_cross_grad, ("rows", "mem"), scatter_dimension=0, tiled=True),
        lax.psum_scatter(expand_grad, ("rows", "mem"), scatter_dimension=0, tiled=True),
        lax.psum_scatter(
            down_projection_gradient, ("rows", "mem"), scatter_dimension=0, tiled=True
        ),
        lax.psum_scatter(gain_grad, ("rows", "mem"), scatter_dimension=0, tiled=True),
        lax.psum_scatter(shift_grad, ("rows", "mem"), scatter_dimension=0, tiled=True),
    )
    return (
        result,
        input_grad,
        memory_grad,
        sums[0],
        sums[1],
        sums[2],
        sums[3],
        sums[4],
        sums[5],
        sums[6],
        sums[7],
        sums[8],
        sums[9],
        jnp.transpose(sums[10]),
        jnp.transpose(sums[11]),
    )


ALL = slice(None)
TILE = 256
SLOTS = 3
GATHER_SLOTS = 9
VMEM_LIMIT = 61 * 1024 * 1024


def flip(index, unit):
    return index + unit * (1 - 2 * ((index // unit) % 2))


def span(index, size):
    return pl.ds(pl.multiple_of(index * size, size), size)


class Place:
    def __init__(self, n_rows, n_mem):
        self.n_rows, self.n_mem = n_rows, n_mem
        self.digits = (n_rows // 2).bit_length() - 1
        self.row = lax.axis_index("rows")
        self.mem = lax.axis_index("mem")
        self.lane = self.row % 2

    def turn(self, index, stage):
        rising, falling = 2 << stage, 2 << (self.digits - 1 - stage)
        return flip(index, rising) * (1 - self.lane) + flip(index, falling) * self.lane

    def sibling(self):
        return (flip(self.row, 1), self.mem)

    def partner(self, stage):
        return (self.turn(self.row, stage), self.mem)

    def far(self, step):
        return (self.row, (self.mem + step) % self.n_mem)

    def others(self):
        found = [self.far(step) for step in range(1, self.n_mem)]
        found += [self.partner(stage) for stage in range(self.digits)]
        return found + [self.sibling()]

    def tell(self, semaphore):
        for other in self.others():
            pl.semaphore_signal(semaphore, inc=1, device_id=other, device_id_type=MESH)

    def hear(self, semaphore):
        pl.semaphore_wait(semaphore, len(self.others()))

    def greet(self):
        self.tell(pltpu.get_barrier_semaphore())
        self.hear(pltpu.get_barrier_semaphore())


def remote(source, target, send_sem, recv_sem, device):
    return pltpu.make_async_remote_copy(
        src_ref=source,
        dst_ref=target,
        send_sem=send_sem,
        recv_sem=recv_sem,
        device_id=device,
        device_id_type=MESH,
    )


def waits(total):
    return (lambda: total().wait_recv(), lambda: total().wait_send())


class Part:
    def __init__(self, source, target, near=0, straight=False):
        self.source, self.target = source, target
        self.near, self.straight = near, straight


class Gather:
    def __init__(self, place, parts, sems):
        self.place, self.parts = place, parts
        (
            self.own_sem,
            self.far_send,
            self.far_recv,
            self.plane_send,
            self.plane_recv,
            self.core_send,
            self.core_recv,
            self.line_send,
            self.line_recv,
        ) = sems

    def group(self, number, group):
        return self.parts[number].target.at[group]

    def one(self, number, group, member):
        return self.parts[number].target.at[group, member]

    def shard(self, number):
        return self.parts[number].source

    def mine(self, number):
        return self.one(number, self.place.row, self.place.mem)

    def own(self, number):
        return pltpu.make_async_copy(self.shard(number), self.mine(number), self.own_sem.at[number])

    def held(self, stage):
        groups = [self.place.row]
        for before in range(stage):
            groups = groups + [self.place.turn(group, before) for group in groups]
        return groups

    def far_total(self, number):
        part = self.parts[number]
        some = part.target.at[pl.ds(0, 1 << part.near), pl.ds(0, self.place.n_mem - 1)]
        return remote(
            some, some, self.far_send.at[number], self.far_recv.at[number], self.place.far(1)
        )

    def far_hop(self, number, first):
        place = self.place
        for group in self.held(self.parts[number].near):
            target = self.one(number, group, place.mem)
            source = self.shard(number) if first else target
            for step in range(1, place.n_mem):
                remote(
                    source,
                    target,
                    self.far_send.at[number],
                    self.far_recv.at[number],
                    place.far(step),
                ).start()

    def sides(self, step):
        mem, n_mem = self.place.mem, self.place.n_mem
        return (
            ((mem - step >= 0) & (mem + 1 < n_mem), mem - step, 1, mem - 1 - step >= 0),
            ((mem + step < n_mem) & (mem >= 1), mem + step, n_mem - 1, mem + 1 + step < n_mem),
        )

    def line_total(self, number, step, side):
        part, at = self.parts[number], 2 * step + side
        some = part.target.at[pl.ds(0, 1 << part.near), 0]
        sems = (self.line_send.at[at, number], self.line_recv.at[at, number])
        return remote(some, some, *sems, self.place.far(1))

    def line_arrived(self, number, step):
        for side, (_, _, _, receives) in enumerate(self.sides(step)):

            @pl.when(receives)
            def _(side=side):
                self.line_total(number, step, side).wait_recv()

    def line_sent(self, number, step):
        for side, (sends, _, _, _) in enumerate(self.sides(step)):

            @pl.when(sends)
            def _(side=side):
                self.line_total(number, step, side).wait_send()

    def line_hop(self, number, step, first):
        place = self.place
        for side, (sends, member, towards, _) in enumerate(self.sides(step)):
            member = (member + place.n_mem) % place.n_mem

            @pl.when(sends)
            def _(side=side, member=member, towards=towards):
                for group in self.held(self.parts[number].near):
                    target = self.one(number, group, member)
                    remote(
                        self.shard(number) if first else target,
                        target,
                        self.line_send.at[2 * step + side, number],
                        self.line_recv.at[2 * step + side, number],
                        place.far(towards),
                    ).start()

    def plane_total(self, number, stage):
        part = self.parts[number]
        some = part.target.at[pl.ds(0, 1 << stage)]
        if stage < part.near:
            some = part.target.at[pl.ds(0, 1 << stage), 0]
        return remote(
            some,
            some,
            self.plane_send.at[stage, number],
            self.plane_recv.at[stage, number],
            self.place.partner(stage),
        )

    def plane_hop(self, number, stage, first):
        for group in self.held(stage):
            if stage < self.parts[number].near:
                target = self.one(number, group, self.place.mem)
            else:
                target = self.group(number, group)
            remote(
                self.shard(number) if first else target,
                target,
                self.plane_send.at[stage, number],
                self.plane_recv.at[stage, number],
                self.place.partner(stage),
            ).start()

    def core_total(self, number):
        some = self.parts[number].target.at[pl.ds(0, self.place.n_rows // 2)]
        return remote(
            some, some, self.core_send.at[number], self.core_recv.at[number], self.place.sibling()
        )

    def core_hop(self, number, first):
        for group in self.held(self.place.digits):
            block = self.group(number, group)
            remote(
                block,
                block,
                self.core_send.at[number],
                self.core_recv.at[number],
                self.place.sibling(),
            ).start()

    def hops(self, number):
        part, take = self.parts[number], functools.partial
        along = []
        if part.straight:
            along.append((1.6, take(self.far_hop, number)) + waits(take(self.far_total, number)))
        else:
            for step in range(self.place.n_mem - 1):
                along.append(
                    (
                        0.55 if step else 1.4,
                        take(self.line_hop, number, step),
                        take(self.line_arrived, number, step),
                        take(self.line_sent, number, step),
                    )
                )
        plane = []
        for stage in range(self.place.digits):
            total = take(self.plane_total, number, stage)
            plane.append((1.5, take(self.plane_hop, number, stage)) + waits(total))
        core = (1.5, take(self.core_hop, number)) + waits(take(self.core_total, number))
        return plane[: part.near] + along + plane[part.near :] + [core]

    def events(self, number):
        hops = self.hops(number)
        time, found = float(number), []

        def act(at):
            if at == 0:
                self.own(number).start()
            else:
                if at == 1:
                    self.own(number).wait()
                hops[at - 1][2]()
            hops[at][1](at == 0)

        for at in range(len(hops)):
            time += hops[at][0] if at else 0.0
            found.append((time, functools.partial(act, at)))
        return found, time + 0.9

    def sent(self, number):
        for hop in self.hops(number):
            hop[3]()


class Job:
    def __init__(self, left, right, first, target):
        self.left, self.right, self.first, self.target = left, right, first, target
        self.small = right is None
        self.width = target.shape[-1]
        self.large = 0


OUT_SLOTS, LANE_SLOTS, SUM_SLOTS, CORE_RING, FIRST_RING, RING = 2, 3, 2, 3, 6, 4


class Reduce:
    def __init__(self, place, jobs, sems, pool, small):
        self.place, self.jobs, self.small = place, jobs, small
        self.core_send, self.core_recv, self.stage_send, self.stage_recv = sems
        wanted = [place.row]
        for stage in reversed(range(place.digits)):
            wanted = wanted + [place.turn(group, stage) for group in wanted]
        self.wanted = [group // 2 for group in wanted]
        for number, job in enumerate(job for job in jobs if not job.small):
            job.large = number
        used, half = [0], place.n_rows // 2

        def take(count, units):
            first = used[0]
            used[0] += count * units
            return [pool.at[pl.ds(first + i * units, units)] for i in range(count)]

        self.outs = take(OUT_SLOTS, half)
        self.lane_slots = take(LANE_SLOTS, half)
        self.core_ring = take(CORE_RING, half)
        self.sum_slots, self.rings = [], []
        for stage in range(place.digits):
            self.sum_slots.append(take(SUM_SLOTS, self.count(stage)))
            self.rings.append(take(RING if stage else FIRST_RING, self.count(stage)))
        self.rings.append(take(RING, 1))
        self.used = used[0]

    def count(self, stage):
        return max(self.place.n_rows // 4 >> stage, 1)

    def cut(self, ref, job):
        return ref if job.width == ref.shape[-1] else ref.at[:, :, :, pl.ds(0, job.width)]

    def out(self, job):
        return self.cut(self.outs[job.large % OUT_SLOTS], job)

    def lanes(self, job):
        if job.small:
            return self.small.lanes
        return self.cut(self.lane_slots[job.large % LANE_SLOTS], job)

    def core_in(self, job):
        if job.small:
            return self.small.core_in
        return self.cut(self.core_ring[job.large % CORE_RING], job)

    def sums(self, job, stage):
        if job.small:
            return self.small.sums[stage]
        return self.cut(self.sum_slots[stage][job.large % SUM_SLOTS], job)

    def arrived(self, job, stage):
        if job.small:
            return self.small.arrived[stage]
        ring = self.rings[stage]
        units = self.cut(ring[job.large % len(ring)], job)
        if stage == self.place.digits:
            return units.at[0, pl.ds(0, self.place.n_mem - 1)]
        return units

    def previous(self, number, distance):
        found = [n for n in range(number) if not self.jobs[n].small]
        if self.jobs[number].small or len(found) < distance:
            return None
        return found[-distance]

    def core_copy(self, number):
        job = self.jobs[number]
        source = job.left.at[1 - self.place.lane] if job.small else self.out(job)
        return remote(
            source,
            self.core_in(job),
            self.core_send.at[number],
            self.core_recv.at[number],
            self.place.sibling(),
        )

    def product(self, job, side, store):
        half = self.place.n_rows // 2
        group = job.left.shape[1] // half
        width = min(TILE, job.width)
        unit = (self.place.n_mem, group // self.place.n_mem, width)

        def column_step(step, carry):
            source = pl.ds(pl.multiple_of(job.first + step * width, width), width)
            value = dot(job.left[side], job.right[:, source])
            for index in range(half):
                block = value[index * group : (index + 1) * group].reshape(unit)
                store(index, span(step, width), block)
            return carry

        lax.fori_loop(0, job.width // width, column_step, 0)

    def core_stage(self, number):
        job = self.jobs[number]
        if not job.small:
            before = self.previous(number, OUT_SLOTS)
            if before is not None:
                self.core_copy(before).wait_send()
            out = self.out(job)

            def store(index, columns, value):
                out[index, :, :, columns] = value.astype(out.dtype)

            self.product(job, 1 - self.place.lane, store)
        self.core_copy(number).start()

    def lane_stage(self, number):
        job = self.jobs[number]
        before = self.previous(number, LANE_SLOTS)
        if before is not None:
            self.total(before, 0).wait_send()
        lanes, arrived = self.lanes(job), self.core_in(job)
        self.core_copy(number).wait_recv()
        if job.small:
            lanes[...] = job.left[self.place.lane] + arrived[...]
        else:

            def store(index, columns, value):
                total = value + arrived[index, :, :, columns].astype(jnp.float32)
                lanes[index, :, :, columns] = total.astype(lanes.dtype)

            self.product(job, self.place.lane, store)
        self.send(number, 0)

    def unit(self, job, stage, index):
        if stage == 0:
            return self.lanes(job).at[self.wanted[index]]
        return self.sums(job, stage - 1).at[index]

    def piece(self, job, unit, member):
        return unit if job.small else unit.at[member]

    def send(self, number, stage):
        job, place = self.jobs[number], self.place
        arrived = self.arrived(job, stage)
        sems = (self.stage_send.at[stage, number], self.stage_recv.at[stage, number])
        if stage == place.digits:
            unit = self.unit(job, stage, 0)
            for step in range(1, place.n_mem):
                source = self.piece(job, unit, (place.mem + step) % place.n_mem)
                remote(source, arrived.at[step - 1], *sems, place.far(step)).start()
            return
        left = self.count(stage)
        for index in range(left):
            source = self.unit(job, stage, left + index)
            remote(source, arrived.at[index], *sems, place.partner(stage)).start()

    def total(self, number, stage):
        some = self.arrived(self.jobs[number], stage)
        sems = (self.stage_send.at[stage, number], self.stage_recv.at[stage, number])
        return remote(some, some, *sems, self.place.far(1))

    def stage(self, number, stage):
        job, place = self.jobs[number], self.place
        arrived = self.arrived(job, stage)
        if stage == place.digits:
            self.total(number, stage).wait_recv()
            value = self.piece(job, self.unit(job, stage, 0), place.mem)[...].astype(jnp.float32)
            for step in range(place.n_mem - 1):
                value = value + arrived[step].astype(jnp.float32)
            job.target[...] = value
            return
        before = self.previous(number, SUM_SLOTS)
        if before is not None:
            self.total(before, stage + 1).wait_send()
        self.total(number, stage).wait_recv()
        sums = self.sums(job, stage)
        for index in range(self.count(stage)):
            unit, coming, target = self.unit(job, stage, index), arrived.at[index], sums.at[index]
            if job.small:
                target[...] = unit[...] + coming[...]
                continue

            def add(member, carry, unit=unit, coming=coming, target=target):
                value = unit[member].astype(jnp.float32) + coming[member].astype(jnp.float32)
                target[member] = value.astype(target.dtype)
                return carry

            lax.fori_loop(0, place.n_mem, add, 0)
        self.send(number, stage + 1)

    def events(self, number):
        found = [(0.0, functools.partial(self.core_stage, number))]
        found.append((0.9, functools.partial(self.lane_stage, number)))
        time = 2.2 if number < 2 else 3.2
        for stage in range(self.place.digits + 1):
            found.append((time, functools.partial(self.stage, number, stage)))
            time += 1.4
        found[-1] = (found[-1][0] - 0.3, found[-1][1])
        return [(number + time, action) for time, action in found]

    def finish(self):
        n_jobs, last = len(self.jobs), self.place.digits
        out = {self.previous(number, OUT_SLOTS) for number in range(n_jobs)}
        lanes = {self.previous(number, LANE_SLOTS) for number in range(n_jobs)}
        sums = {self.previous(number, SUM_SLOTS) for number in range(n_jobs)}
        for number in range(n_jobs):
            if number not in out:
                self.core_copy(number).wait_send()
            if number not in lanes:
                self.total(number, 0).wait_send()
            if number not in sums:
                for stage in range(1, last + 1):
                    self.total(number, stage).wait_send()


NORMAL = (((1,), (0,)), ((), ()))
TURNED = (((1,), (1,)), ((), ()))
LEFT_TURNED = (((0,), (0,)), ((), ()))


def dot(left, right, dims=NORMAL):
    return lax.dot_general(left, right, dims, preferred_element_type=jnp.float32)


def times(left, weight, store, part=0, parts=1):
    size = weight.shape[-1]
    width = min(TILE, size)
    tiles = size // width // parts

    def column_step(step, carry):
        columns = span(step, width)
        store(columns, dot(left[...], weight[:, :, :, columns].reshape(-1, width)))
        return carry

    lax.fori_loop(part * tiles, (part + 1) * tiles, column_step, 0)


def times_turned(left, weight, store):
    unit = weight.shape[1] * weight.shape[2]
    units = max(TILE // unit, 1)

    def row_step(step, carry):
        rows = weight[span(step, units)].reshape(units * unit, weight.shape[-1])
        store(span(step, units * unit), dot(left[...], rows, TURNED))
        return carry

    lax.fori_loop(0, weight.shape[0] // units, row_step, 0)


def into(target):
    def store(columns, value):
        target[:, columns] = value.astype(target.dtype)

    return store


ROWS = 32


def by_rows(count, step):
    def body(index, carry):
        step(span(index, ROWS))
        return carry

    lax.fori_loop(0, count // ROWS, body, 0)


def norm_forward(total, gains, index, unit, scale, use):
    gain, shift = gains[index : index + 1, :], gains[index + 3 : index + 4, :]

    def step(rows):
        value = total[rows, :]
        centre = value - jnp.mean(value, axis=-1, keepdims=True)
        spread = jnp.mean(centre * centre, axis=-1, keepdims=True)
        root = lax.rsqrt(spread + EPS)
        scaled = centre * root
        unit[rows, :] = scaled
        scale[rows, :] = root
        use(rows, scaled * gain + shift)

    by_rows(total.shape[0], step)


def norm_slope(incoming, scaled, root, gain):
    width = scaled.shape[1]
    scaled_grad = incoming * gain
    first = jnp.mean(scaled_grad, axis=-1, keepdims=True)
    second = jnp.mean(scaled_grad * scaled, axis=-1, keepdims=True)
    value = root * (scaled_grad - first - scaled * second)
    of_gain = jnp.sum((incoming * scaled).reshape(ROWS // 8, 8, width), axis=0)
    of_shift = jnp.sum(incoming.reshape(ROWS // 8, 8, width), axis=0)
    return value, of_gain, of_shift


def keep_small(index, sums, small):
    for offset, partial in ((index, sums[0]), (index + 3, sums[1])):
        line = jnp.sum(partial, axis=0, keepdims=True)
        for group in range(2 * small.shape[1]):
            small[group % 2, group // 2, offset : offset + 1, :] = line[
                :, group * 128 : (group + 1) * 128
            ]


def norm_backward(grad, gains, index, unit, scale, target, target_low, small):
    gain = gains[index : index + 1, :]

    def body(block, sums):
        rows = span(block, ROWS)
        value, of_gain, of_shift = norm_slope(grad[rows, :], unit[rows, :], scale[rows, :], gain)
        target[rows, :] = value
        target_low[rows, :] = value.astype(target_low.dtype)
        return (sums[0] + of_gain, sums[1] + of_shift)

    zero = jnp.zeros((8, unit.shape[1]), jnp.float32)
    keep_small(index, lax.fori_loop(0, unit.shape[0] // ROWS, body, (zero, zero)), small)


def norm_both(total, grad, gains, index, result, target, target_low, small):
    gain, shift = gains[index : index + 1, :], gains[index + 3 : index + 4, :]

    def body(block, sums):
        rows = span(block, ROWS)
        value = total[rows, :]
        centre = value - jnp.mean(value, axis=-1, keepdims=True)
        spread = jnp.mean(centre * centre, axis=-1, keepdims=True)
        root = lax.rsqrt(spread + EPS)
        scaled = centre * root
        result[rows, :] = scaled * gain + shift
        incoming = grad[rows, :].astype(jnp.float32)
        value, of_gain, of_shift = norm_slope(incoming, scaled, root, gain)
        target[rows, :] = value
        target_low[rows, :] = value.astype(target_low.dtype)
        return (sums[0] + of_gain, sums[1] + of_shift)

    zero = jnp.zeros((8, total.shape[1]), jnp.float32)
    keep_small(index, lax.fori_loop(0, total.shape[0] // ROWS, body, (zero, zero)), small)


def lane_masks(dtype, scale):
    low = lax.broadcasted_iota(jnp.int32, (1, 2 * HEAD_DIM), 1) < HEAD_DIM
    first = jnp.where(low, scale, 0.0)
    return first.astype(dtype), (scale - first).astype(dtype)


def turned_pair(eye, rows):
    size = rows.shape[1]
    return dot(eye[0:size, 0:size], rows, TURNED).astype(rows.dtype)


def attention_forward(query, keys, values, bias, blocks, eye, mixed, turned, lse, first, last):
    masks = lane_masks(query.dtype, SCALE)

    def pair_step(pair, carry):
        lanes = span(pair, 2 * HEAD_DIM)
        two_query, two_keys, two_values = query[:, lanes], keys[:, lanes], values[:, lanes]
        columns = []
        for q0, q1, k0, k1 in blocks:
            block_values = turned_pair(eye, two_values[k0:k1])
            rows = []
            for head in range(2):
                scores = dot(two_keys[k0:k1], two_query[q0:q1] * masks[head], TURNED)
                scores = scores + bias[k0:k1, q0:q1]
                top = jnp.max(scores, axis=0, keepdims=True)
                weight = jnp.exp(scores - top)
                norm = jnp.sum(weight, axis=0, keepdims=True)
                head_values = block_values[head * HEAD_DIM : (head + 1) * HEAD_DIM]
                rows.append(dot(head_values, weight.astype(query.dtype)) * (1.0 / norm))
                lse[pair, head : head + 1, q0:q1] = top + jnp.log(norm)
            columns.append(jnp.concatenate(rows, axis=0))
        total = jnp.concatenate(columns, axis=1).astype(mixed.dtype)
        turned[pair % 2, span(pair // 2, 2 * HEAD_DIM), :] = total
        mixed[:, lanes] = dot(eye[...], total, TURNED).astype(mixed.dtype)
        return carry

    lax.fori_loop(first, last, pair_step, 0)


def stacked(parts):
    cuts = sorted({at for first, value in parts for at in (first, first + value.shape[0])})
    found = []
    for low, high in zip(cuts, cuts[1:]):
        total = None
        for first, value in parts:
            if first <= low and high <= first + value.shape[0]:
                piece = value[low - first : high - first]
                total = piece if total is None else total + piece
        found.append(total)
    return jnp.concatenate(found, axis=0)


def attention_backward(
    query, keys, values, bias, blocks, eye, lse, grad, query_grad, key_grad, value_grad, first, last
):
    scaled, masks = lane_masks(query.dtype, SCALE), lane_masks(query.dtype, 1.0)

    def pair_step(pair, carry):
        lanes = span(pair, 2 * HEAD_DIM)
        two_query, two_keys, two_values = query[:, lanes], keys[:, lanes], values[:, lanes]
        two_grad = grad[:, lanes]
        of_query, of_keys, of_values = [], [], []
        for q0, q1, k0, k1 in blocks:
            block_keys, block_values = two_keys[k0:k1], two_values[k0:k1]
            slopes, all_probs, heads_query, heads_grad = [], [], [], []
            for head in range(2):
                head_query = two_query[q0:q1] * scaled[head]
                head_grad = two_grad[q0:q1] * masks[head]
                scores = dot(block_keys, head_query, TURNED) + bias[k0:k1, q0:q1]
                probs = jnp.exp(scores - lse[pair, head : head + 1, q0:q1])
                pulled = dot(block_values, head_grad, TURNED)
                inner = jnp.sum(probs * pulled, axis=0, keepdims=True)
                slopes.append((probs * (pulled - inner)).astype(query.dtype))
                all_probs.append(probs.astype(query.dtype))
                heads_query.append(head_query)
                heads_grad.append(head_grad)
            both = jnp.concatenate(slopes, axis=1)
            of_keys.append((k0, dot(both, jnp.concatenate(heads_query, axis=0))))
            both = jnp.concatenate(all_probs, axis=1)
            of_values.append((k0, dot(both, jnp.concatenate(heads_grad, axis=0))))
            block_turned = turned_pair(eye, block_keys * jnp.asarray(SCALE, query.dtype))
            rows = [
                dot(block_turned[head * HEAD_DIM : (head + 1) * HEAD_DIM], slopes[head])
                for head in range(2)
            ]
            of_query.append(jnp.concatenate(rows, axis=0))
        total = jnp.concatenate(of_query, axis=1).astype(query_grad.dtype)
        query_grad[:, lanes] = dot(eye[...], total, TURNED).astype(query_grad.dtype)
        key_grad[:, lanes] = stacked(of_keys).astype(key_grad.dtype)
        value_grad[:, lanes] = stacked(of_values).astype(value_grad.dtype)
        return carry

    lax.fori_loop(first, last, pair_step, 0)


def turn_blocks(left, eye, store):
    width = eye.shape[0]
    for block in range(left.shape[1] // width):
        columns = pl.ds(block * width, width)
        store(block, dot(eye[...], left[:, columns], TURNED).astype(left.dtype))


def turn_by_lane(left, eye, target):
    group = eye.shape[0] // 2

    def store(block, value):
        target[0, pl.ds(block * group, group), :] = value[:group]
        target[1, pl.ds(block * group, group), :] = value[group:]

    turn_blocks(left, eye, store)


SQUARES = 8


def layer_kernel(places, sizes, *refs):
    n_rows, n_mem, width, ff, shard = sizes
    ref = SimpleNamespace(**jax.tree.map(lambda place: refs[place], places))
    place = Place(n_rows, n_mem)
    many = ff // width
    own_ff = ff // (n_rows * n_mem)
    (
        at_query,
        at_key,
        at_value,
        at_output,
        at_cross_query,
        at_cross_key,
        at_cross_value,
        at_cross_output,
    ) = range(SQUARES)
    full = ref.full
    expand, contract = ref.expand_full, ref.contract_full
    tokens, gains = ref.tokens, ref.gains
    low, turned = SimpleNamespace(**ref.low), SimpleNamespace(**ref.turned)

    order = [
        at_query,
        at_key,
        at_value,
        at_output,
        at_cross_key,
        at_cross_value,
        at_cross_query,
        at_cross_output,
    ]
    pool = ref.pool

    def gather_slot(number):
        return pool.at[pl.ds(number % GATHER_SLOTS * n_rows, n_rows)]

    sources = [ref.squares[index] for index in order]
    sources += [ref.expand.at[:, pl.ds(j * width, width)] for j in range(many)]
    sources += [ref.contract.at[pl.ds(j * shard, shard), :] for j in range(many)]
    stores = [full[index] for index in order] + [expand.at[j] for j in range(many)]
    stores += [contract.at[:, :, j] for j in range(many)]
    parts = [Part(item, gather_slot(n), n % 2) for n, item in enumerate(sources)]
    parts.insert(SMALL_AT, Part(ref.small, ref.small_full, 0, True))
    gather = Gather(place, parts, ref.gather_sems)

    def keep(number):
        return pltpu.make_async_copy(gather_slot(number), stores[number], ref.keep_sem.at[number])

    count = [0]

    def load_slot(number):
        first = pool.shape[0] - (1 + number % SLOTS) * n_rows
        return pool.at[pl.ds(first, n_rows)]

    def load(pieces):
        number = count[0]
        count[0] += 1
        for source, first, rows in pieces:
            target = load_slot(number).at[pl.ds(first, rows)]
            pltpu.make_async_copy(source, target, ref.slot_sem.at[number % SLOTS]).start()
        return number

    def ready(number):
        slot = load_slot(number)
        pltpu.make_async_copy(slot, slot, ref.slot_sem.at[number % SLOTS]).wait()
        return slot

    def contract_rows(j):
        groups = n_rows // many
        return [(contract.at[j * groups + i], i * n_mem, n_mem) for i in range(groups)]

    mem_block = ref.memory.shape[1]
    memory, mem_rows = ref.memory, ref.mem_rows

    def memory_own():
        return pltpu.make_async_copy(
            memory.at[place.mem], mem_rows.at[span(place.mem, mem_block)], ref.mem_sem.at[0]
        )

    def memory_total():
        some = mem_rows.at[pl.ds(0, (n_mem - 1) * mem_block)]
        return remote(some, some, ref.mem_sem.at[1], ref.mem_sem.at[2], place.far(1))

    ref.small[...] = jnp.zeros_like(ref.small)
    for member in range(n_mem):

        @pl.when(place.mem == member)
        def _(member=member):
            lanes = slice(member * shard, (member + 1) * shard)
            ref.small[0:3, lanes] = ref.norm_gains[...].astype(jnp.float32)
            ref.small[3:6, lanes] = ref.norm_shifts[...].astype(jnp.float32)

    place.greet()
    memory_own().start()
    for step in range(1, n_mem):
        remote(
            memory.at[(place.mem + step) % n_mem],
            mem_rows.at[span(place.mem, mem_block)],
            ref.mem_sem.at[1],
            ref.mem_sem.at[2],
            place.far(step),
        ).start()

    actions, whole = [], []
    for part in range(len(parts)):
        found, time = gather.events(part)
        for hop, (at, action) in enumerate(found):
            actions.append((HOP + 10 * part + hop, at, action))
        whole.append(time)
    first_hops = [HOP, HOP + 10]
    for code, _, action in actions:
        if code in first_hops:
            action()
    actions = [item for item in actions if item[0] not in first_hops]

    self_bias, cross_bias, eye = ref.self_bias, ref.cross_bias, ref.eye
    own_row = ref.token_ids[pl.ds(place.mem, 1), :].astype(jnp.float32)
    mem_row = ref.memory_ids[pl.ds(place.mem, 1), :].astype(jnp.float32)
    key_place = lax.broadcasted_iota(jnp.int32, self_bias.shape, 0)
    query_place = lax.broadcasted_iota(jnp.int32, self_bias.shape, 1)
    own_wide = jnp.broadcast_to(own_row, self_bias.shape)
    mem_wide = jnp.broadcast_to(mem_row, (cross_bias.shape[1], cross_bias.shape[0]))
    same = (jnp.transpose(own_wide) == own_wide) & (key_place <= query_place)
    self_bias[...] = jnp.where(same, 0.0, NEG)
    cross_bias[...] = jnp.where(jnp.transpose(mem_wide) == own_row, 0.0, NEG)
    eye_row = lax.broadcasted_iota(jnp.int32, eye.shape, 0)
    eye_column = lax.broadcasted_iota(jnp.int32, eye.shape, 1)
    eye[...] = jnp.where(eye_row == eye_column, 1.0, 0.0).astype(eye.dtype)
    turn_by_lane(tokens, eye, turned.tokens)

    accumulated, other = ref.accumulated, ref.other
    hidden, slope, hidden_turned = ref.hidden, ref.slope, ref.hidden_turned

    def small_piece():
        blocks = ref.small_full
        for group in range(n_rows):
            total = None
            for member in range(n_mem):
                value = blocks[group, member]
                total = value if total is None else total + value
            gains[:, group * 128 : (group + 1) * 128] = total

    def query_piece(slot):
        times(tokens, slot, into(ref.query))

    def key_piece(slot):
        times(tokens, slot, into(ref.keys))

    pairs = width // (2 * HEAD_DIM)
    self_blocks = [
        (first, first + 128, max(first - DOC_LIMIT, 0), first + 128)
        for first in range(0, self_bias.shape[1], 128)
    ]
    cross_blocks = [(0, cross_bias.shape[1], 0, cross_bias.shape[0])]

    def value_piece(slot):
        times(tokens, slot, into(ref.values))

    def self_forward(first, last, slot):
        attention_forward(
            ref.query,
            ref.keys,
            ref.values,
            self_bias,
            self_blocks,
            eye,
            ref.attended,
            turned.attended,
            ref.self_lse,
            first,
            last,
        )

    def output_piece(slot):
        def store(columns, value):
            accumulated[:, columns] = ALPHA * tokens[:, columns].astype(jnp.float32) + value

        times(ref.attended, slot, store)

    def output_norm(slot):
        def use(rows, value):
            ref.first_low[rows, :] = value.astype(jnp.bfloat16)
            other[rows, :] = value

        norm_forward(accumulated, gains, 0, ref.unit1, ref.scale1, use)

    def cross_key_piece(slot):
        memory_own().wait()
        memory_total().wait_recv()
        times(mem_rows, slot, into(ref.cross_keys))
        turn_by_lane(mem_rows, eye, turned.memory)

    def cross_value_piece(slot):
        times(mem_rows, slot, into(ref.cross_values))
        turn_by_lane(ref.first_low, eye, turned.first)

    def cross_query_piece(slot):
        times(ref.first_low, slot, into(ref.cross_query))

    def cross_forward(first, last, slot):
        attention_forward(
            ref.cross_query,
            ref.cross_keys,
            ref.cross_values,
            cross_bias,
            cross_blocks,
            eye,
            ref.crossed,
            turned.crossed,
            ref.cross_lse,
            first,
            last,
        )

    def cross_output_piece(slot):
        def store(columns, value):
            accumulated[:, columns] = ALPHA * other[:, columns] + value

        times(ref.crossed, slot, store)

    def cross_output_norm(slot):
        def use(rows, value):
            ref.second_low[rows, :] = value.astype(jnp.bfloat16)
            other[rows, :] = value

        norm_forward(accumulated, gains, 1, ref.unit2, ref.scale2, use)

    def expand_piece(j, half, slot):
        def store(columns, value):
            there = pl.ds(pl.multiple_of(j * width + columns.start, TILE), columns.size)
            bell = 0.5 * (1.0 + lax.erf(value * math.sqrt(0.5)))
            density = jnp.exp(value * value * -0.5) * (1.0 / math.sqrt(2.0 * math.pi))
            hidden[:, there] = (value * bell).astype(hidden.dtype)
            slope[:, there] = (bell + value * density).astype(slope.dtype)

        times(ref.second_low, slot, store, half, 2)

    def expand_turn(j, slot):
        def keep(block, value):
            for index in range(value.shape[0] // shard):
                first = j * width + block * value.shape[0] + index * shard
                device, job = first // own_ff, first % own_ff // shard
                group, member = device // n_mem, device % n_mem
                at = group // 2 * n_mem * shard + member * shard
                hidden_turned[job, group % 2, at : at + shard, :] = value[
                    index * shard : (index + 1) * shard
                ]

        turn_blocks(hidden.at[:, pl.ds(j * width, width)], eye, keep)

    def contract_piece(j, slot):
        block = 2 * n_mem * shard
        for index in range(n_rows // 2):
            rows = pl.ds(index * n_mem * shard, n_mem * shard)
            both = jnp.concatenate([hidden_turned[j, 0, rows], hidden_turned[j, 1, rows]], axis=0)
            columns = pl.ds(index * block, block)
            low.branch[:, columns] = dot(eye[...], both, TURNED).astype(jnp.bfloat16)

        def store(columns, value):
            if j == 0:
                accumulated[:, columns] = ALPHA * other[:, columns] + value
            else:
                accumulated[:, columns] = accumulated[:, columns] + value

        times(low.branch, slot, store)

    quarters = [(pairs * at // 2, pairs * (at + 1) // 2) for at in range(2)]
    pieces = [
        [query_piece],
        [key_piece],
        [value_piece] + [functools.partial(self_forward, *quarter) for quarter in quarters],
        [output_piece, output_norm],
        [cross_key_piece],
        [cross_value_piece],
        [cross_query_piece] + [functools.partial(cross_forward, *quarter) for quarter in quarters],
        [cross_output_piece, cross_output_norm],
    ]
    for j in range(many):
        halves = [functools.partial(expand_piece, j, half) for half in range(2)]
        pieces.append(halves + [functools.partial(expand_turn, j)])
    pieces += [[functools.partial(contract_piece, j)] for j in range(many)]

    def arrive(part):
        gather.core_total(part).wait_recv()
        if part != SMALL_AT:
            keep(part - (part > SMALL_AT)).start()

    def use(part, index):
        if part == SMALL_AT:
            small_piece()
        else:
            number = part - (part > SMALL_AT)
            pieces[number][index](gather_slot(number))

    def settle(part):
        gather.sent(part)
        if part != SMALL_AT:
            keep(part - (part > SMALL_AT)).wait()

    last = 0.0
    for part, time in enumerate(whole):
        time = max(time, last + 0.5)
        actions.append((ARRIVE + part, time, functools.partial(arrive, part)))
        count_here = 1 if part == SMALL_AT else len(pieces[part - (part > SMALL_AT)])
        for index in range(count_here):
            at = time + 0.2 + 0.04 * index
            actions.append((USE + 10 * part + index, at, functools.partial(use, part, index)))
        actions.append((SETTLE + part, time + 0.45, functools.partial(settle, part)))
        last = time
    for action in planned(actions, FORWARD_PLAN):
        action()
    place.tell(ref.ready_sem)

    backward_sources, loads = [], []
    used = [0]

    def next_slot():
        slot = ready(loads[used[0]])
        used[0] += 1
        if len(loads) < len(backward_sources):
            loads.append(load(backward_sources[len(loads)]))
        return slot

    small_sums = ref.small_sums
    small_sums[...] = jnp.zeros_like(small_sums)
    def inner_piece(j):
        slot = next_slot()

        def store(columns, value):
            there = pl.ds(pl.multiple_of(j * width + columns.start, TILE), columns.size)
            slope[:, there] = (value * slope[:, there].astype(jnp.float32)).astype(slope.dtype)

        times_turned(low.third, slot, store)

    def second_piece(j):
        slot = next_slot()

        def store(columns, value):
            if j == 0:
                other[:, columns] = ALPHA * accumulated[:, columns] + value
            else:
                other[:, columns] = other[:, columns] + value

        times_turned(slope.at[:, pl.ds(j * width, width)], slot, store)

    def second_norm_piece():
        norm_backward(
            other, gains, 1, ref.unit2, ref.scale2, accumulated, low.second, small_sums
        )

    def cross_start_piece():
        times_turned(low.second, next_slot(), into(low.branch))

    def cross_piece(first, last):
        attention_backward(
            ref.cross_query,
            ref.cross_keys,
            ref.cross_values,
            cross_bias,
            cross_blocks,
            eye,
            ref.cross_lse,
            low.branch,
            low.cross_query,
            low.cross_key,
            low.cross_value,
            first,
            last,
        )

    def first_piece():
        def store(columns, value):
            other[:, columns] = ALPHA * accumulated[:, columns] + value

        times_turned(low.cross_query, next_slot(), store)

    def first_norm_piece():
        norm_backward(other, gains, 0, ref.unit1, ref.scale1, accumulated, low.first, small_sums)

    def self_start_piece():
        times_turned(low.first, next_slot(), into(low.branch))

    def self_piece(first, last):
        attention_backward(
            ref.query,
            ref.keys,
            ref.values,
            self_bias,
            self_blocks,
            eye,
            ref.self_lse,
            low.branch,
            low.query,
            low.key,
            low.value,
            first,
            last,
        )

    mem_out, mem_in = ref.mem_out, ref.mem_in

    def grad_own():
        return pltpu.make_async_copy(
            mem_out.at[span(place.mem, mem_block)], mem_in.at[place.mem], ref.mem_sem.at[3]
        )

    def grad_total():
        some = mem_in.at[pl.ds(0, n_mem - 1)]
        return remote(some, some, ref.mem_sem.at[4], ref.mem_sem.at[5], place.far(1))

    def memory_key_piece():
        times_turned(low.cross_key, next_slot(), into(other))

    def memory_value_piece():
        def store(columns, value):
            mem_out[:, columns] = (other[:, columns] + value).astype(mem_out.dtype)

        times_turned(low.cross_value, next_slot(), store)
        grad_own().start()
        for step in range(1, n_mem):
            remote(
                mem_out.at[span((place.mem + step) % n_mem, mem_block)],
                mem_in.at[place.mem],
                ref.mem_sem.at[4],
                ref.mem_sem.at[5],
                place.far(step),
            ).start()

    def input_piece(left, start, end=False):
        target = ref.input_grad_here

        def store(columns, value):
            if start:
                target[:, columns] = ALPHA * accumulated[:, columns] + value
            else:
                target[:, columns] = target[:, columns] + value

        times_turned(left, next_slot(), store)
        if end:
            leaving[1].start()

    def memory_end_piece():
        grad_own().wait()
        grad_total().wait_recv()
        for member in range(n_mem):
            ref.memory_grad_here[member] = mem_in[member].astype(jnp.float32)
        leaving[2].start()

    halves = ((0, width // 2), (width // 2, width // 2))
    grads = ref.grads
    plans = []
    for j in range(many):
        for first, columns in halves if j == 0 else ((0, width),):
            target = ref.contract_grad.at[pl.ds(j * shard, shard), pl.ds(first, columns)]
            plans.append((hidden_turned.at[j], low.third, first, target))
    for j in range(many):
        target = ref.expand_grad.at[:, pl.ds(j * width, width)]
        plans.append((turned.second, slope, j * width, target))
    plans += [
        (turned.crossed, low.second, 0, grads[at_cross_output]),
        (turned.memory, low.cross_key, 0, grads[at_cross_key]),
        (turned.memory, low.cross_value, 0, grads[at_cross_value]),
        (turned.first, low.cross_query, 0, grads[at_cross_query]),
        (turned.attended, low.first, 0, grads[at_output]),
        (small_sums, None, 0, ref.small_total),
        (turned.tokens, low.query, 0, grads[at_query]),
        (turned.tokens, low.key, 0, grads[at_key]),
    ]
    for first, columns in halves:
        target = grads[at_value].at[:, pl.ds(first, columns)]
        plans.append((turned.tokens, low.value, first, target))
    jobs = [Job(*plan) for plan in plans]
    reduce = Reduce(place, jobs, ref.reduce_sems, pool, SimpleNamespace(**ref.little))

    inner = [functools.partial(inner_piece, j) for j in range(many)]
    second = [functools.partial(second_piece, j) for j in range(many)]
    base = many + 1
    def weight(index):
        return [(full[index], 0, n_rows)]

    turn = functools.partial(turn_by_lane, ref.second_low, eye, turned.second)
    crosses = [functools.partial(cross_piece, first, first + pairs // 2) for first in (0, pairs // 2)]
    selves = [functools.partial(self_piece, first, first + pairs // 2) for first in (0, pairs // 2)]
    work = [(base - 1.7 + j, inner[j], contract_rows(j)) for j in range(2)]
    work += [(base - 1.3, turn, None)]
    work += [(base - 1.7 + j, inner[j], contract_rows(j)) for j in range(2, many)]
    work += [(base - 0.3 + j, second[j], [(expand.at[j], 0, n_rows)]) for j in range(many)]
    base = 2 * many + 1
    work += [
        (base - 0.2, second_norm_piece, None),
        (base - 0.15, cross_start_piece, weight(at_cross_output)),
    ]
    work += [(base + 0.3 + 0.4 * i, crosses[i], None) for i in range(2)]
    work += [
        (base + 1.3, first_piece, weight(at_cross_query)),
        (base + 1.31, first_norm_piece, None),
        (base + 1.7, self_start_piece, weight(at_output)),
    ]
    work += [(base + 2.3 + i, selves[i], None) for i in range(2)]
    work += [
        (base + 3.7, memory_key_piece, weight(at_cross_key)),
        (base + 4.3, memory_value_piece, weight(at_cross_value)),
        (base + 4.7, functools.partial(input_piece, low.query, True), weight(at_query)),
        (base + 5.5, functools.partial(input_piece, low.key, False), weight(at_key)),
        (base + 6.5, functools.partial(input_piece, low.value, False, True), weight(at_value)),
        (base + 8.5, memory_end_piece, None),
    ]
    actions = [(WORK + index, at, item) for index, (at, *item) in enumerate(work)]
    for number in range(len(jobs)):
        found = reduce.events(number)
        actions.append((CORE + number, found[0][0], found[0][1:]))
        actions.append((LANE + number, found[1][0], found[1][1:]))
        for stage, (at, action) in enumerate(found[2:]):
            actions.append((STAGE + 10 * number + stage, at, (action,)))
    ordered = planned(actions, BACKWARD_PLAN)
    backward_sources += [item[1] for item in ordered if len(item) > 1 and item[1] is not None]
    loads += [load(backward_sources[0]), load(backward_sources[1])]
    leaving = [
        pltpu.make_async_copy(ref.result_here, ref.result, ref.out_sem.at[0]),
        pltpu.make_async_copy(ref.input_grad_here, ref.input_grad, ref.out_sem.at[1]),
        pltpu.make_async_copy(ref.memory_grad_here, ref.memory_grad, ref.out_sem.at[2]),
    ]
    norm_both(
        accumulated, ref.out_grad, gains, 2, ref.result_here, accumulated, low.third, small_sums
    )
    leaving[0].start()

    place.hear(ref.ready_sem)
    for item in ordered:
        item[0]()

    total = ref.small_total[...]
    own = jnp.zeros((8, shard), jnp.float32)
    for member in range(n_mem):
        here = jnp.where(place.mem == member, 1.0, 0.0)
        own = own + here * total[:, member * shard : (member + 1) * shard]
    ref.gains_grad[...] = own[0:3]
    ref.shifts_grad[...] = own[3:6]
    reduce.finish()
    for copy in leaving:
        copy.wait()
    memory_total().wait_send()
    grad_total().wait_send()


SMALL_AT = 2
DOC_LIMIT = 64
HOP, ARRIVE, USE, SETTLE, CORE, LANE, STAGE, WORK = range(1000, 9000, 1000)
FORWARD_PLAN = (
    1011, 1020, 1001, 1030, 1002, 1003, 1012, 1040, 1050, 1041, 1031, 1004, 1021, 1013, 1014, 1032,
    1042, 1033, 1060, 1005, 1043, 2000, 1022, 1070, 1044, 1061, 1023, 1015, 1051, 3000, 1034, 2001,
    3010, 4000, 2002, 1052, 1080, 1071, 3020, 1053, 1072, 1035, 1062, 1045, 1081, 4001, 1054, 4002,
    1063, 1090, 2003, 1073, 3030, 1055, 3031, 2004, 1091, 1064, 1082, 2005, 3032, 4003, 1100, 1110,
    1074, 1092, 3040, 3041, 1065, 1083, 1093, 4004, 1101, 2006, 1111, 3050, 4005, 1120, 1084, 1075,
    1094, 1102, 1130, 3060, 1085, 4006, 2007, 3070, 1121, 1112, 1103, 3071, 1113, 2008, 3072, 1104,
    4007, 1131, 1122, 3080, 1140, 1114, 1095, 1150, 3081, 1132, 1123, 1141, 4008, 1133, 1105, 2009,
    1124, 3090, 1115, 1160, 1151, 3091, 1142, 3092, 2010, 1134, 3100, 1152, 3101, 3102, 1125, 4009,
    1143, 1153, 2011, 1161, 3110, 1135, 2012, 1144, 3111, 1162, 3112, 4010, 3120, 1154, 3121, 1163,
    3122, 2013, 1145, 1164, 4011, 1155, 3130, 4012, 4013, 2014, 3140, 2015, 1165, 4014, 3150, 2016,
    4015, 3160, 4016,
)
BACKWARD_PLAN = (
    5000, 5001, 8003, 6000, 5002, 6001, 7000, 6002, 7010, 5003, 7001, 8000, 6003, 5004, 8002, 8004,
    8005, 8001, 7002, 7020, 7011, 6004, 7021, 5005, 7030, 5006, 8006, 6005, 8007, 7040, 6006, 7012,
    5007, 7031, 8008, 8009, 7022, 8010, 6007, 8011, 5008, 7041, 7032, 5009, 7050, 7060, 6008, 8012,
    7051, 5010, 6009, 7042, 7061, 7070, 8013, 6010, 5011, 7052, 8014, 7071, 8015, 7080, 6011, 5012,
    7062, 7081, 7090, 8016, 7072, 5013, 6012, 7091, 7100, 8017, 5014, 7110, 6013, 5015, 7082, 6014,
    7101, 7120, 5016, 7092, 7111, 8018, 8020, 7130, 6015, 7140, 5017, 7102, 7121, 8021, 8022, 7112,
    7131, 6016, 7141, 7150, 8019, 7160, 7122, 6017, 7151, 5018, 7132, 7170, 7142, 6018, 7161, 7152,
    7171, 7180, 7162, 7181, 7172, 8023, 7182,
)


def planned(actions, plan):
    codes = {code for code, _, _ in actions}
    if codes == set(plan):
        at = {code: number for number, code in enumerate(plan)}
        return [item for code, _, item in sorted(actions, key=lambda action: at[action[0]])]
    return [item for _, _, item in sorted(actions, key=lambda action: action[1])]


def copy_kernel(count, *refs):
    for source, target in zip(refs[:count], refs[count:]):
        target[...] = source[...]


def copied(values):
    near = pl.BlockSpec(memory_space=pltpu.VMEM)
    return pl.pallas_call(
        functools.partial(copy_kernel, len(values)),
        out_shape=[jax.ShapeDtypeStruct(value.shape, value.dtype) for value in values],
        in_specs=[near] * len(values),
        out_specs=[near] * len(values),
        compiler_params=pltpu.CompilerParams(vmem_limit_bytes=VMEM_LIMIT),
        name="results",
    )(*values)


def fused(n_rows, n_mem, ins):
    tokens, memory, squares = ins["tokens"], ins["memory"], ins["squares"]
    expand, contract = ins["expand"], ins["contract"]
    tokens_here, width = tokens.shape
    ff = expand.shape[1]
    shard = squares[0].shape[0]
    mem_tokens = memory.shape[0] * memory.shape[1]
    digits, half, many = (n_rows // 2).bit_length() - 1, n_rows // 2, ff // width
    pairs = width // (2 * HEAD_DIM)
    low, high = jnp.bfloat16, jnp.float32
    n_parts = 1 + SQUARES + 2 * many
    n_jobs = n_parts + 2
    dma, vmem = pltpu.SemaphoreType.DMA, pltpu.VMEM
    anywhere, near = pl.BlockSpec(memory_space=pl.ANY), pl.BlockSpec(memory_space=pltpu.VMEM)

    far_ins = dict(memory=memory)
    in_specs = {
        name: jax.tree.map(lambda _: anywhere if name in far_ins else near, value)
        for name, value in ins.items()
    }

    def out(shape, dtype=high):
        return jax.ShapeDtypeStruct(shape, dtype)

    outs = dict(
        result=out(tokens.shape),
        input_grad=out(tokens.shape),
        memory_grad=out(memory.shape),
        grads=[out(item.shape) for item in squares],
        expand_grad=out(expand.shape),
        contract_grad=out(contract.shape),
        gains_grad=out((3, shard)),
        shifts_grad=out((3, shard)),
    )
    far_outs = dict(
        full=[out((n_rows, n_mem, shard, width), low)] * SQUARES,
        expand_full=out((many, n_rows, n_mem, shard, width), low),
        contract_full=out((n_rows, n_mem, many, shard, width), low),
    )
    early_outs = ("result", "input_grad", "memory_grad")
    out_specs = {
        name: anywhere if name in early_outs else jax.tree.map(lambda _: near, value)
        for name, value in outs.items()
    }
    out_specs.update(jax.tree.map(lambda _: anywhere, far_outs))
    outs.update(far_outs)

    def token_rows(dtype):
        return vmem((tokens_here, width), dtype)

    def memory_rows(dtype):
        return vmem((mem_tokens, width), dtype)

    tiny = (8, 128)

    counts = [half >> (stage + 1) for stage in range(digits)]
    units = (OUT_SLOTS + LANE_SLOTS + CORE_RING) * half + RING
    for stage, number in enumerate(counts):
        units += (SUM_SLOTS + (RING if stage else FIRST_RING)) * number
    units = max(units + SLOTS * n_rows, GATHER_SLOTS * n_rows)
    little = dict(
        lanes=vmem((half,) + tiny, high),
        core_in=vmem((half,) + tiny, high),
        sums=[vmem((number,) + tiny, high) for number in counts],
        arrived=[vmem((number,) + tiny, high) for number in counts]
        + [vmem((n_mem - 1,) + tiny, high)],
    )
    left = vmem((2, width // 2, tokens_here), low)
    scratch = dict(
        result_here=token_rows(high),
        input_grad_here=token_rows(high),
        memory_grad_here=vmem(memory.shape, high),
        out_sem=dma((3,)),
        small=vmem(tiny, high),
        small_full=vmem((n_rows, n_mem) + tiny, high),
        small_total=vmem(tiny, high),
        pool=vmem((units, n_mem, shard, width), low),
        slot_sem=dma((SLOTS,)),
        keep_sem=dma((n_parts - 1,)),
        ready_sem=pltpu.SemaphoreType.REGULAR,
        mem_sem=dma((6,)),
        gather_sems=[
            dma(shape + (n_parts,))
            for shape in ((), (), (), (digits,), (digits,), (), ())
            + ((2 * (n_mem - 1),), (2 * (n_mem - 1),))
        ],
        reduce_sems=[dma(shape + (n_jobs,)) for shape in ((), (), (digits + 1,), (digits + 1,))],
        gains=vmem((8, width), high),
        query=token_rows(low),
        keys=token_rows(low),
        values=token_rows(low),
        attended=token_rows(low),
        first_low=token_rows(low),
        second_low=token_rows(low),
        cross_query=token_rows(low),
        crossed=token_rows(low),
        cross_keys=memory_rows(low),
        cross_values=memory_rows(low),
        mem_rows=memory_rows(low),
        mem_out=memory_rows(low),
        mem_in=vmem(memory.shape, low),
        unit1=token_rows(high),
        unit2=token_rows(high),
        accumulated=token_rows(high),
        other=token_rows(high),
        scale1=vmem((tokens_here, 1), high),
        scale2=vmem((tokens_here, 1), high),
        self_bias=vmem((tokens_here, tokens_here), high),
        cross_bias=vmem((mem_tokens, tokens_here), high),
        self_lse=vmem((pairs, 2, tokens_here), high),
        cross_lse=vmem((pairs, 2, tokens_here), high),
        eye=vmem((TILE, TILE), low),
        hidden=vmem((tokens_here, ff), low),
        slope=vmem((tokens_here, ff), low),
        hidden_turned=vmem((many, 2, width // 2, tokens_here), low),
        turned=dict(
            tokens=left, attended=left, first=left, memory=left, crossed=left, second=left
        ),
        low=dict(
            third=token_rows(low),
            second=token_rows(low),
            first=token_rows(low),
            branch=token_rows(low),
            cross_query=token_rows(low),
            cross_key=memory_rows(low),
            cross_value=memory_rows(low),
            query=token_rows(low),
            key=token_rows(low),
            value=token_rows(low),
        ),
        small_sums=vmem((2, half) + tiny, high),
        little=little,
    )
    in_values, in_tree = jax.tree.flatten(ins)
    out_shapes, out_tree = jax.tree.flatten(outs)
    scratch_shapes, scratch_tree = jax.tree.flatten(scratch)
    places = jax.tree.unflatten(in_tree, range(len(in_values)))
    at = len(in_values)
    places.update(jax.tree.unflatten(out_tree, range(at, at + len(out_shapes))))
    at += len(out_shapes)
    places.update(jax.tree.unflatten(scratch_tree, range(at, at + len(scratch_shapes))))
    values = pl.pallas_call(
        functools.partial(layer_kernel, places, (n_rows, n_mem, width, ff, shard)),
        out_shape=out_shapes,
        in_specs=jax.tree.leaves(in_specs),
        out_specs=jax.tree.leaves(out_specs),
        scratch_shapes=scratch_shapes,
        compiler_params=pltpu.CompilerParams(
            collective_id=0, has_side_effects=True, vmem_limit_bytes=VMEM_LIMIT
        ),
        name="layer",
    )(*in_values)
    found = jax.tree.unflatten(out_tree, values)
    for name in far_outs:
        del found[name]
    return found


def local(n_rows, n_mem, *args):
    (
        tokens,
        memory,
        token_ids,
        memory_ids,
        out_grad,
        self_query,
        self_key,
        self_value,
        self_output,
        cross_query,
        cross_key,
        cross_value,
        cross_output,
        expand_weight,
        contract_weight,
        norm_gains,
        norm_shifts,
    ) = args
    shard, width = self_query.shape
    suits = width == 128 * n_rows and shard % 16 == 0 and tokens.shape[0] == 1
    suits = suits and tokens.shape[1] == TILE and expand_weight.shape[1] == n_mem * width
    if not suits or n_rows < 4 or n_rows & (n_rows - 1) or n_mem < 2:
        return plain(*args)
    found = fused(
        n_rows,
        n_mem,
        dict(
            tokens=tokens[0],
            memory=memory,
            token_ids=token_ids,
            memory_ids=memory_ids,
            out_grad=out_grad[0],
            squares=[
                self_query,
                self_key,
                self_value,
                self_output,
                cross_query,
                cross_key,
                cross_value,
                cross_output,
            ],
            expand=expand_weight,
            contract=contract_weight,
            norm_gains=norm_gains,
            norm_shifts=norm_shifts,
        ),
    )
    values, tree = jax.tree.flatten(found)
    found = SimpleNamespace(**jax.tree.unflatten(tree, copied(values)))
    return (
        found.result[None],
        found.input_grad[None],
        found.memory_grad,
        *found.grads,
        found.expand_grad,
        found.contract_grad,
        found.gains_grad,
        found.shifts_grad,
    )


def solution(mesh):
    in_specs = (
        P(("rows", "mem"), None, None),
        P("rows", "mem", None),
        P("rows", None),
        P("rows", None),
        P(("rows", "mem"), None, None),
        P(("rows", "mem"), None),
        P(("rows", "mem"), None),
        P(("rows", "mem"), None),
        P(("rows", "mem"), None),
        P(("rows", "mem"), None),
        P(("rows", "mem"), None),
        P(("rows", "mem"), None),
        P(("rows", "mem"), None),
        P(("rows", "mem"), None),
        P(("rows", "mem"), None),
        P(None, ("rows", "mem")),
        P(None, ("rows", "mem")),
    )
    out_specs = (
        P(("rows", "mem"), None, None),
        P(("rows", "mem"), None, None),
        P("rows", "mem", None),
        P(("rows", "mem"), None),
        P(("rows", "mem"), None),
        P(("rows", "mem"), None),
        P(("rows", "mem"), None),
        P(("rows", "mem"), None),
        P(("rows", "mem"), None),
        P(("rows", "mem"), None),
        P(("rows", "mem"), None),
        P(("rows", "mem"), None),
        P(("rows", "mem"), None),
        P(None, ("rows", "mem")),
        P(None, ("rows", "mem")),
    )
    layer = functools.partial(local, mesh.shape["rows"], mesh.shape["mem"])
    return jax.shard_map(layer, mesh=mesh, in_specs=in_specs, out_specs=out_specs, check_vma=False)
```

```python
import functools
import math
from types import SimpleNamespace

import jax
import jax.numpy as jnp
from jax import lax
from jax.experimental import pallas as pl
from jax.experimental.pallas import tpu as pltpu
from jax.sharding import PartitionSpec as P

MESH = pl.DeviceIdType.MESH

HEADS = 16
HEAD_DIM = 64


ALPHA = 4.16
EPS = 1e-05
SCALE = 0.125
NEG = -1e30


def layer_norm(hidden_activation, gain, shift):
    centre = hidden_activation - jnp.mean(hidden_activation, axis=-1, keepdims=True)
    spread = jnp.mean(centre * centre, axis=-1, keepdims=True)
    return centre * lax.rsqrt(spread + EPS) * gain + shift


def gelu_exact(value):
    return jax.nn.gelu(value, approximate=False)


def product(left, right):
    return jnp.dot(left, right, preferred_element_type=jnp.float32)


def split_heads(matrix):
    return matrix.reshape(matrix.shape[0], matrix.shape[1] // HEAD_DIM, HEAD_DIM)


def grouped(matrix):
    return jnp.moveaxis(matrix.reshape(matrix.shape[0], HEADS // 4, 4 * HEAD_DIM), 1, 0)


def ungrouped(stack):
    return jnp.moveaxis(stack, 0, 1).reshape(stack.shape[1], stack.shape[0] * stack.shape[2])


def row_map(function, items):
    return lax.map(lambda entry: function(*entry), items)


def score_block(query, keys, allowed):
    raw = jnp.einsum(
        "khe,qhe->hkq", split_heads(keys), split_heads(query), preferred_element_type=jnp.float32
    )
    return jnp.where(allowed[None], raw * SCALE, NEG)


def attend_probs(query, keys, allowed, lse):
    scores = score_block(query, keys, allowed)
    return jnp.where(allowed[None], jnp.exp(scores - lse[:, None, :]), 0.0)


def attend_forward(query, keys, values, allowed):
    scores = score_block(query, keys, allowed)
    top = jnp.max(scores, axis=1)
    weight = jnp.where(allowed[None], jnp.exp(scores - top[:, None, :]), 0.0)
    total = jnp.sum(weight, axis=1)
    probs = (weight / total[:, None, :]).astype(jnp.bfloat16)
    mixed = jnp.einsum(
        "hkq,khe->qhe", probs, split_heads(values), preferred_element_type=jnp.float32
    )
    return (mixed.reshape(query.shape), top + jnp.log(total))


def value_pull(grad, values):
    return jnp.einsum(
        "qhe,khe->hkq", split_heads(grad), split_heads(values), preferred_element_type=jnp.float32
    )


def score_grads(probs, pulled, inner):
    return (probs * (pulled - inner[:, None, :]) * SCALE).astype(jnp.bfloat16)


def query_from(score_grad, keys, shape):
    moved = jnp.einsum(
        "hkq,khe->qhe", score_grad, split_heads(keys), preferred_element_type=jnp.float32
    )
    return moved.reshape(shape)


def key_from(score_grad, query, shape):
    moved = jnp.einsum(
        "hkq,qhe->khe", score_grad, split_heads(query), preferred_element_type=jnp.float32
    )
    return moved.reshape(shape)


def value_from(probs, grad, values):
    moved = jnp.einsum(
        "hkq,qhe->khe",
        probs.astype(jnp.bfloat16),
        split_heads(grad),
        preferred_element_type=jnp.float32,
    )
    return moved.reshape(values.shape)


def local_forward(query, keys, values, allowed):

    def one_group(items):
        return attend_forward(items[0], items[1], items[2], allowed)

    mixed, lse = lax.map(one_group, (grouped(query), grouped(keys), grouped(values)))
    return (ungrouped(mixed), lse)


def local_backward(query, keys, values, allowed, lse, grad):

    def one_group(items):
        part_query, part_keys, part_values, part_lse, part_grad = items
        probs = attend_probs(part_query, part_keys, allowed, part_lse)
        pulled = value_pull(part_grad, part_values)
        inner = jnp.sum(probs * pulled, axis=1)
        score_grad = score_grads(probs, pulled, inner)
        return (
            query_from(score_grad, part_keys, part_query.shape),
            key_from(score_grad, part_query, part_keys.shape),
            value_from(probs, part_grad, part_values),
        )

    parts = lax.map(one_group, (grouped(query), grouped(keys), grouped(values), lse, grouped(grad)))
    return (ungrouped(parts[0]), ungrouped(parts[1]), ungrouped(parts[2]))


def plain(
    tokens,
    memory,
    token_ids,
    memory_ids,
    out_grad,
    self_query,
    self_key,
    self_value,
    self_output,
    cross_query,
    cross_key,
    cross_value,
    cross_output,
    expand_weight,
    contract_weight,
    norm_gains,
    norm_shifts,
):
    full = (
        lax.all_gather(self_query, ("rows", "mem"), axis=0, tiled=True),
        lax.all_gather(self_key, ("rows", "mem"), axis=0, tiled=True),
        lax.all_gather(self_value, ("rows", "mem"), axis=0, tiled=True),
        lax.all_gather(self_output, ("rows", "mem"), axis=0, tiled=True),
        lax.all_gather(cross_query, ("rows", "mem"), axis=0, tiled=True),
        lax.all_gather(cross_key, ("rows", "mem"), axis=0, tiled=True),
        lax.all_gather(cross_value, ("rows", "mem"), axis=0, tiled=True),
        lax.all_gather(cross_output, ("rows", "mem"), axis=0, tiled=True),
        lax.all_gather(expand_weight, ("rows", "mem"), axis=0, tiled=True),
        lax.all_gather(contract_weight, ("rows", "mem"), axis=0, tiled=True),
        lax.all_gather(jnp.transpose(norm_gains), ("rows", "mem"), axis=0, tiled=True),
        lax.all_gather(jnp.transpose(norm_shifts), ("rows", "mem"), axis=0, tiled=True),
    )
    (
        self_attention_query,
        decoder_match_label,
        self_attention_value,
        self_attention_output,
        encoder_lookup_probe,
        key_cross,
        value_cross,
        cross_attention_output,
        up_projection,
        narrowing_matrix,
        gain_cols,
        shift_cols,
    ) = full
    gain_rows = jnp.transpose(gain_cols).astype(jnp.float32)
    shift_rows = jnp.transpose(shift_cols).astype(jnp.float32)
    rows_here = tokens.shape[0]
    member = lax.axis_index("mem")
    own_ids = lax.dynamic_slice_in_dim(token_ids, member * rows_here, rows_here, 0)
    positions = jnp.arange(tokens.shape[1], dtype=jnp.int32)
    self_allowed = (own_ids[:, :, None] == own_ids[:, None, :]) & (
        positions[:, None] <= positions[None, :]
    )[None]
    query = product(tokens, self_attention_query).astype(jnp.bfloat16)
    keys = product(tokens, decoder_match_label).astype(jnp.bfloat16)
    values = product(tokens, self_attention_value).astype(jnp.bfloat16)
    self_mixed, self_lse = row_map(local_forward, (query, keys, values, self_allowed))
    attention_result = self_mixed.astype(jnp.bfloat16)
    first, first_back = jax.vjp(
        layer_norm,
        ALPHA * tokens.astype(jnp.float32) + product(attention_result, self_attention_output),
        gain_rows[0],
        shift_rows[0],
    )
    first_reduced = first.astype(jnp.bfloat16)
    cross_queries = product(first_reduced, encoder_lookup_probe).astype(jnp.bfloat16)
    memory_rows = lax.all_to_all(memory, "mem", split_axis=0, concat_axis=1, tiled=True)
    row_ids = lax.dynamic_slice_in_dim(memory_ids, member * rows_here, rows_here, 0)
    cross_allowed = row_ids[:, :, None] == own_ids[:, None, :]
    cross_keys = product(memory_rows, key_cross).astype(jnp.bfloat16)
    cross_values = product(memory_rows, value_cross).astype(jnp.bfloat16)
    cross_mixed, cross_lse = row_map(
        local_forward, (cross_queries, cross_keys, cross_values, cross_allowed)
    )
    cross_attention_result = cross_mixed.astype(jnp.bfloat16)
    second, second_back = jax.vjp(
        layer_norm,
        ALPHA * first + product(cross_attention_result, cross_attention_output),
        gain_rows[1],
        shift_rows[1],
    )
    second_reduced = second.astype(jnp.bfloat16)
    hidden_value, gelu_back = jax.vjp(gelu_exact, product(second_reduced, up_projection))
    hidden_activation = hidden_value.astype(jnp.bfloat16)
    result, third_back = jax.vjp(
        layer_norm,
        ALPHA * second + product(hidden_activation, narrowing_matrix),
        gain_rows[2],
        shift_rows[2],
    )
    third_grad, gain_three, shift_three = third_back(out_grad.astype(jnp.float32))
    feedforward_gradient = third_grad.astype(jnp.bfloat16)
    down_projection_gradient = jnp.einsum(
        "ehj,ehc->jc", hidden_activation, feedforward_gradient, preferred_element_type=jnp.float32
    )
    (inner_grad,) = gelu_back(
        jnp.einsum(
            "hpu,ku->hpk",
            feedforward_gradient,
            narrowing_matrix,
            preferred_element_type=jnp.float32,
        )
    )
    inner_reduced = inner_grad.astype(jnp.bfloat16)
    expand_grad = jnp.einsum(
        "iqg,iqe->ge", second_reduced, inner_reduced, preferred_element_type=jnp.float32
    )
    second_total = ALPHA * third_grad + jnp.einsum(
        "iwm,fm->iwf", inner_reduced, up_projection, preferred_element_type=jnp.float32
    )
    second_grad, gain_two, shift_two = second_back(second_total)
    cross_branch_gradient = second_grad.astype(jnp.bfloat16)
    output_cross_grad = jnp.einsum(
        "nhb,nhc->bc",
        cross_attention_result,
        cross_branch_gradient,
        preferred_element_type=jnp.float32,
    )
    crossed_grad = jnp.einsum(
        "qwp,up->qwu",
        cross_branch_gradient,
        cross_attention_output,
        preferred_element_type=jnp.float32,
    ).astype(jnp.bfloat16)
    query_grads, key_grads, value_grads = row_map(
        local_backward,
        (cross_queries, cross_keys, cross_values, cross_allowed, cross_lse, crossed_grad),
    )
    key_low = key_grads.astype(jnp.bfloat16)
    value_low = value_grads.astype(jnp.bfloat16)
    row_grad = jnp.einsum(
        "sme,de->smd", key_low, key_cross, preferred_element_type=jnp.float32
    ) + jnp.einsum("sme,de->smd", value_low, value_cross, preferred_element_type=jnp.float32)
    key_cross_grad = jnp.einsum(
        "smd,sme->de", memory_rows, key_low, preferred_element_type=jnp.float32
    )
    value_cross_grad = jnp.einsum(
        "smd,sme->de", memory_rows, value_low, preferred_element_type=jnp.float32
    )
    memory_grad = lax.all_to_all(
        row_grad.astype(jnp.bfloat16), "mem", split_axis=1, concat_axis=0, tiled=True
    ).astype(row_grad.dtype)
    probe_lowered_precision = query_grads.astype(jnp.bfloat16)
    query_cross_grad = jnp.einsum(
        "nhb,nhc->bc", first_reduced, probe_lowered_precision, preferred_element_type=jnp.float32
    )
    first_total = ALPHA * second_grad + jnp.einsum(
        "qwp,up->qwu",
        probe_lowered_precision,
        encoder_lookup_probe,
        preferred_element_type=jnp.float32,
    )
    first_grad, gain_one, shift_one = first_back(first_total)
    self_branch_gradient = first_grad.astype(jnp.bfloat16)
    output_self_grad = jnp.einsum(
        "nhb,nhc->bc", attention_result, self_branch_gradient, preferred_element_type=jnp.float32
    )
    attended_grad = jnp.einsum(
        "qwp,up->qwu",
        self_branch_gradient,
        self_attention_output,
        preferred_element_type=jnp.float32,
    ).astype(jnp.bfloat16)
    self_query_reduced, decoder_label_lowered, self_value_reduced = row_map(
        local_backward, (query, keys, values, self_allowed, self_lse, attended_grad)
    )
    self_query_reduced = self_query_reduced.astype(jnp.bfloat16)
    decoder_label_lowered = decoder_label_lowered.astype(jnp.bfloat16)
    self_value_reduced = self_value_reduced.astype(jnp.bfloat16)
    query_self_grad = jnp.einsum(
        "nhb,nhc->bc", tokens, self_query_reduced, preferred_element_type=jnp.float32
    )
    key_self_grad = jnp.einsum(
        "nhb,nhc->bc", tokens, decoder_label_lowered, preferred_element_type=jnp.float32
    )
    value_self_grad = jnp.einsum(
        "nhb,nhc->bc", tokens, self_value_reduced, preferred_element_type=jnp.float32
    )
    input_grad = (
        ALPHA * first_grad
        + jnp.einsum(
            "qwp,up->qwu",
            self_query_reduced,
            self_attention_query,
            preferred_element_type=jnp.float32,
        )
        + jnp.einsum(
            "qwp,up->qwu",
            decoder_label_lowered,
            decoder_match_label,
            preferred_element_type=jnp.float32,
        )
        + jnp.einsum(
            "qwp,up->qwu",
            self_value_reduced,
            self_attention_value,
            preferred_element_type=jnp.float32,
        )
    )
    gain_grad = jnp.stack([gain_one, gain_two, gain_three], axis=1)
    shift_grad = jnp.stack([shift_one, shift_two, shift_three], axis=1)
    sums = (
        lax.psum_scatter(query_self_grad, ("rows", "mem"), scatter_dimension=0, tiled=True),
        lax.psum_scatter(key_self_grad, ("rows", "mem"), scatter_dimension=0, tiled=True),
        lax.psum_scatter(value_self_grad, ("rows", "mem"), scatter_dimension=0, tiled=True),
        lax.psum_scatter(output_self_grad, ("rows", "mem"), scatter_dimension=0, tiled=True),
        lax.psum_scatter(query_cross_grad, ("rows", "mem"), scatter_dimension=0, tiled=True),
        lax.psum_scatter(key_cross_grad, ("rows", "mem"), scatter_dimension=0, tiled=True),
        lax.psum_scatter(value_cross_grad, ("rows", "mem"), scatter_dimension=0, tiled=True),
        lax.psum_scatter(output_cross_grad, ("rows", "mem"), scatter_dimension=0, tiled=True),
        lax.psum_scatter(expand_grad, ("rows", "mem"), scatter_dimension=0, tiled=True),
        lax.psum_scatter(
            down_projection_gradient, ("rows", "mem"), scatter_dimension=0, tiled=True
        ),
        lax.psum_scatter(gain_grad, ("rows", "mem"), scatter_dimension=0, tiled=True),
        lax.psum_scatter(shift_grad, ("rows", "mem"), scatter_dimension=0, tiled=True),
    )
    return (
        result,
        input_grad,
        memory_grad,
        sums[0],
        sums[1],
        sums[2],
        sums[3],
        sums[4],
        sums[5],
        sums[6],
        sums[7],
        sums[8],
        sums[9],
        jnp.transpose(sums[10]),
        jnp.transpose(sums[11]),
    )


ALL = slice(None)
TILE = 256
SLOTS = 3
GATHER_SLOTS = 9
VMEM_LIMIT = 61 * 1024 * 1024


def flip(index, unit):
    return index + unit * (1 - 2 * ((index // unit) % 2))


def span(index, size):
    return pl.ds(pl.multiple_of(index * size, size), size)


class Place:
    def __init__(self, n_rows, n_mem):
        self.n_rows, self.n_mem = n_rows, n_mem
        self.digits = (n_rows // 2).bit_length() - 1
        self.row = lax.axis_index("rows")
        self.mem = lax.axis_index("mem")
        self.lane = self.row % 2

    def turn(self, index, stage):
        rising, falling = 2 << stage, 2 << (self.digits - 1 - stage)
        return flip(index, rising) * (1 - self.lane) + flip(index, falling) * self.lane

    def sibling(self):
        return (flip(self.row, 1), self.mem)

    def partner(self, stage):
        return (self.turn(self.row, stage), self.mem)

    def far(self, step):
        return (self.row, (self.mem + step) % self.n_mem)

    def others(self):
        found = [self.far(step) for step in range(1, self.n_mem)]
        found += [self.partner(stage) for stage in range(self.digits)]
        return found + [self.sibling()]

    def tell(self, semaphore):
        for other in self.others():
            pl.semaphore_signal(semaphore, inc=1, device_id=other, device_id_type=MESH)

    def hear(self, semaphore):
        pl.semaphore_wait(semaphore, len(self.others()))

    def greet(self):
        self.tell(pltpu.get_barrier_semaphore())
        self.hear(pltpu.get_barrier_semaphore())


def remote(source, target, send_sem, recv_sem, device):
    return pltpu.make_async_remote_copy(
        src_ref=source,
        dst_ref=target,
        send_sem=send_sem,
        recv_sem=recv_sem,
        device_id=device,
        device_id_type=MESH,
    )


def waits(total):
    return (lambda: total().wait_recv(), lambda: total().wait_send())


class Part:
    def __init__(self, source, target, near=0, straight=False):
        self.source, self.target = source, target
        self.near, self.straight = near, straight


class Gather:
    def __init__(self, place, parts, sems):
        self.place, self.parts = place, parts
        (
            self.own_sem,
            self.far_send,
            self.far_recv,
            self.plane_send,
            self.plane_recv,
            self.core_send,
            self.core_recv,
            self.line_send,
            self.line_recv,
        ) = sems

    def group(self, number, group):
        return self.parts[number].target.at[group]

    def one(self, number, group, member):
        return self.parts[number].target.at[group, member]

    def shard(self, number):
        return self.parts[number].source

    def mine(self, number):
        return self.one(number, self.place.row, self.place.mem)

    def own(self, number):
        return pltpu.make_async_copy(self.shard(number), self.mine(number), self.own_sem.at[number])

    def held(self, stage):
        groups = [self.place.row]
        for before in range(stage):
            groups = groups + [self.place.turn(group, before) for group in groups]
        return groups

    def far_total(self, number):
        part = self.parts[number]
        some = part.target.at[pl.ds(0, 1 << part.near), pl.ds(0, self.place.n_mem - 1)]
        return remote(
            some, some, self.far_send.at[number], self.far_recv.at[number], self.place.far(1)
        )

    def far_hop(self, number, first):
        place = self.place
        for group in self.held(self.parts[number].near):
            target = self.one(number, group, place.mem)
            source = self.shard(number) if first else target
            for step in range(1, place.n_mem):
                remote(
                    source,
                    target,
                    self.far_send.at[number],
                    self.far_recv.at[number],
                    place.far(step),
                ).start()

    def sides(self, step):
        mem, n_mem = self.place.mem, self.place.n_mem
        return (
            ((mem - step >= 0) & (mem + 1 < n_mem), mem - step, 1, mem - 1 - step >= 0),
            ((mem + step < n_mem) & (mem >= 1), mem + step, n_mem - 1, mem + 1 + step < n_mem),
        )

    def line_total(self, number, step, side):
        part, at = self.parts[number], 2 * step + side
        some = part.target.at[pl.ds(0, 1 << part.near), 0]
        sems = (self.line_send.at[at, number], self.line_recv.at[at, number])
        return remote(some, some, *sems, self.place.far(1))

    def line_arrived(self, number, step):
        for side, (_, _, _, receives) in enumerate(self.sides(step)):

            @pl.when(receives)
            def _(side=side):
                self.line_total(number, step, side).wait_recv()

    def line_sent(self, number, step):
        for side, (sends, _, _, _) in enumerate(self.sides(step)):

            @pl.when(sends)
            def _(side=side):
                self.line_total(number, step, side).wait_send()

    def line_hop(self, number, step, first):
        place = self.place
        for side, (sends, member, towards, _) in enumerate(self.sides(step)):
            member = (member + place.n_mem) % place.n_mem

            @pl.when(sends)
            def _(side=side, member=member, towards=towards):
                for group in self.held(self.parts[number].near):
                    target = self.one(number, group, member)
                    remote(
                        self.shard(number) if first else target,
                        target,
                        self.line_send.at[2 * step + side, number],
                        self.line_recv.at[2 * step + side, number],
                        place.far(towards),
                    ).start()

    def plane_total(self, number, stage):
        part = self.parts[number]
        some = part.target.at[pl.ds(0, 1 << stage)]
        if stage < part.near:
            some = part.target.at[pl.ds(0, 1 << stage), 0]
        return remote(
            some,
            some,
            self.plane_send.at[stage, number],
            self.plane_recv.at[stage, number],
            self.place.partner(stage),
        )

    def plane_hop(self, number, stage, first):
        for group in self.held(stage):
            if stage < self.parts[number].near:
                target = self.one(number, group, self.place.mem)
            else:
                target = self.group(number, group)
            remote(
                self.shard(number) if first else target,
                target,
                self.plane_send.at[stage, number],
                self.plane_recv.at[stage, number],
                self.place.partner(stage),
            ).start()

    def core_total(self, number):
        some = self.parts[number].target.at[pl.ds(0, self.place.n_rows // 2)]
        return remote(
            some, some, self.core_send.at[number], self.core_recv.at[number], self.place.sibling()
        )

    def core_hop(self, number, first):
        for group in self.held(self.place.digits):
            block = self.group(number, group)
            remote(
                block,
                block,
                self.core_send.at[number],
                self.core_recv.at[number],
                self.place.sibling(),
            ).start()

    def hops(self, number):
        part, take = self.parts[number], functools.partial
        along = []
        if part.straight:
            along.append((1.6, take(self.far_hop, number)) + waits(take(self.far_total, number)))
        else:
            for step in range(self.place.n_mem - 1):
                along.append(
                    (
                        0.55 if step else 1.4,
                        take(self.line_hop, number, step),
                        take(self.line_arrived, number, step),
                        take(self.line_sent, number, step),
                    )
                )
        plane = []
        for stage in range(self.place.digits):
            total = take(self.plane_total, number, stage)
            plane.append((1.5, take(self.plane_hop, number, stage)) + waits(total))
        core = (1.5, take(self.core_hop, number)) + waits(take(self.core_total, number))
        return plane[: part.near] + along + plane[part.near :] + [core]

    def events(self, number):
        hops = self.hops(number)
        time, found = float(number), []

        def act(at):
            if at == 0:
                self.own(number).start()
            else:
                if at == 1:
                    self.own(number).wait()
                hops[at - 1][2]()
            hops[at][1](at == 0)

        for at in range(len(hops)):
            time += hops[at][0] if at else 0.0
            found.append((time, functools.partial(act, at)))
        return found, time + 0.9

    def sent(self, number):
        for hop in self.hops(number):
            hop[3]()


class Job:
    def __init__(self, left, right, first, target):
        self.left, self.right, self.first, self.target = left, right, first, target
        self.small = right is None
        self.width = target.shape[-1]
        self.large = 0


OUT_SLOTS, LANE_SLOTS, SUM_SLOTS, CORE_RING, FIRST_RING, RING = 2, 3, 2, 2, 6, 4


class Reduce:
    def __init__(self, place, jobs, sems, pool, small):
        self.place, self.jobs, self.small = place, jobs, small
        self.core_send, self.core_recv, self.stage_send, self.stage_recv = sems
        wanted = [place.row]
        for stage in reversed(range(place.digits)):
            wanted = wanted + [place.turn(group, stage) for group in wanted]
        self.wanted = [group // 2 for group in wanted]
        for number, job in enumerate(job for job in jobs if not job.small):
            job.large = number
        used, half = [0], place.n_rows // 2

        def take(count, units):
            first = used[0]
            used[0] += count * units
            return [pool.at[pl.ds(first + i * units, units)] for i in range(count)]

        self.outs = take(OUT_SLOTS, half)
        self.lane_slots = take(LANE_SLOTS, half)
        self.core_ring = take(CORE_RING, half)
        self.sum_slots, self.rings = [], []
        for stage in range(place.digits):
            self.sum_slots.append(take(SUM_SLOTS, self.count(stage)))
            self.rings.append(take(RING if stage else FIRST_RING, self.count(stage)))
        self.rings.append(take(RING, 1))
        self.used = used[0]

    def count(self, stage):
        return max(self.place.n_rows // 4 >> stage, 1)

    def cut(self, ref, job):
        return ref if job.width == ref.shape[-1] else ref.at[:, :, :, pl.ds(0, job.width)]

    def out(self, job):
        return self.cut(self.outs[job.large % OUT_SLOTS], job)

    def lanes(self, job):
        if job.small:
            return self.small.lanes
        return self.cut(self.lane_slots[job.large % LANE_SLOTS], job)

    def core_in(self, job):
        if job.small:
            return self.small.core_in
        return self.cut(self.core_ring[job.large % CORE_RING], job)

    def sums(self, job, stage):
        if job.small:
            return self.small.sums[stage]
        return self.cut(self.sum_slots[stage][job.large % SUM_SLOTS], job)

    def arrived(self, job, stage):
        if job.small:
            return self.small.arrived[stage]
        ring = self.rings[stage]
        units = self.cut(ring[job.large % len(ring)], job)
        if stage == self.place.digits:
            return units.at[0, pl.ds(0, self.place.n_mem - 1)]
        return units

    def previous(self, number, distance):
        found = [n for n in range(number) if not self.jobs[n].small]
        if self.jobs[number].small or len(found) < distance:
            return None
        return found[-distance]

    def core_copy(self, number):
        job = self.jobs[number]
        source = job.left.at[1 - self.place.lane] if job.small else self.out(job)
        return remote(
            source,
            self.core_in(job),
            self.core_send.at[number],
            self.core_recv.at[number],
            self.place.sibling(),
        )

    def product(self, job, side, store):
        half = self.place.n_rows // 2
        group = job.left.shape[1] // half
        width = min(TILE, job.width)
        unit = (self.place.n_mem, group // self.place.n_mem, width)

        def column_step(step, carry):
            source = pl.ds(pl.multiple_of(job.first + step * width, width), width)
            value = dot(job.left[side], job.right[:, source])
            for index in range(half):
                block = value[index * group : (index + 1) * group].reshape(unit)
                store(index, span(step, width), block)
            return carry

        lax.fori_loop(0, job.width // width, column_step, 0)

    def core_stage(self, number):
        job = self.jobs[number]
        if not job.small:
            before = self.previous(number, OUT_SLOTS)
            if before is not None:
                self.core_copy(before).wait_send()
            out = self.out(job)

            def store(index, columns, value):
                out[index, :, :, columns] = value.astype(out.dtype)

            self.product(job, 1 - self.place.lane, store)
        self.core_copy(number).start()

    def lane_stage(self, number):
        job = self.jobs[number]
        before = self.previous(number, LANE_SLOTS)
        if before is not None:
            self.total(before, 0).wait_send()
        lanes, arrived = self.lanes(job), self.core_in(job)
        self.core_copy(number).wait_recv()
        if job.small:
            lanes[...] = job.left[self.place.lane] + arrived[...]
        else:

            def store(index, columns, value):
                total = value + arrived[index, :, :, columns].astype(jnp.float32)
                lanes[index, :, :, columns] = total.astype(lanes.dtype)

            self.product(job, self.place.lane, store)
        self.send(number, 0)

    def unit(self, job, stage, index):
        if stage == 0:
            return self.lanes(job).at[self.wanted[index]]
        return self.sums(job, stage - 1).at[index]

    def piece(self, job, unit, member):
        return unit if job.small else unit.at[member]

    def send(self, number, stage):
        job, place = self.jobs[number], self.place
        arrived = self.arrived(job, stage)
        sems = (self.stage_send.at[stage, number], self.stage_recv.at[stage, number])
        if stage == place.digits:
            unit = self.unit(job, stage, 0)
            for step in range(1, place.n_mem):
                source = self.piece(job, unit, (place.mem + step) % place.n_mem)
                remote(source, arrived.at[step - 1], *sems, place.far(step)).start()
            return
        left = self.count(stage)
        for index in range(left):
            source = self.unit(job, stage, left + index)
            remote(source, arrived.at[index], *sems, place.partner(stage)).start()

    def total(self, number, stage):
        some = self.arrived(self.jobs[number], stage)
        sems = (self.stage_send.at[stage, number], self.stage_recv.at[stage, number])
        return remote(some, some, *sems, self.place.far(1))

    def stage(self, number, stage):
        job, place = self.jobs[number], self.place
        arrived = self.arrived(job, stage)
        if stage == place.digits:
            self.total(number, stage).wait_recv()
            value = self.piece(job, self.unit(job, stage, 0), place.mem)[...].astype(jnp.float32)
            for step in range(place.n_mem - 1):
                value = value + arrived[step].astype(jnp.float32)
            job.target[...] = value
            return
        before = self.previous(number, SUM_SLOTS)
        if before is not None:
            self.total(before, stage + 1).wait_send()
        self.total(number, stage).wait_recv()
        sums = self.sums(job, stage)
        for index in range(self.count(stage)):
            unit, coming, target = self.unit(job, stage, index), arrived.at[index], sums.at[index]
            if job.small:
                target[...] = unit[...] + coming[...]
                continue

            def add(member, carry, unit=unit, coming=coming, target=target):
                value = unit[member].astype(jnp.float32) + coming[member].astype(jnp.float32)
                target[member] = value.astype(target.dtype)
                return carry

            lax.fori_loop(0, place.n_mem, add, 0)
        self.send(number, stage + 1)

    def events(self, number):
        found = [(0.0, functools.partial(self.core_stage, number))]
        found.append((0.9, functools.partial(self.lane_stage, number)))
        time = 2.2 if number < 2 else 3.2
        for stage in range(self.place.digits + 1):
            found.append((time, functools.partial(self.stage, number, stage)))
            time += 1.4
        found[-1] = (found[-1][0] - 0.3, found[-1][1])
        return [(number + time, action) for time, action in found]

    def finish(self):
        n_jobs, last = len(self.jobs), self.place.digits
        out = {self.previous(number, OUT_SLOTS) for number in range(n_jobs)}
        lanes = {self.previous(number, LANE_SLOTS) for number in range(n_jobs)}
        sums = {self.previous(number, SUM_SLOTS) for number in range(n_jobs)}
        for number in range(n_jobs):
            if number not in out:
                self.core_copy(number).wait_send()
            if number not in lanes:
                self.total(number, 0).wait_send()
            if number not in sums:
                for stage in range(1, last + 1):
                    self.total(number, stage).wait_send()


NORMAL = (((1,), (0,)), ((), ()))
TURNED = (((1,), (1,)), ((), ()))
LEFT_TURNED = (((0,), (0,)), ((), ()))


def dot(left, right, dims=NORMAL):
    return lax.dot_general(left, right, dims, preferred_element_type=jnp.float32)


def times(left, weight, store, part=0, parts=1):
    size = weight.shape[-1]
    width = min(TILE, size)
    tiles = size // width // parts

    def column_step(step, carry):
        columns = span(step, width)
        store(columns, dot(left[...], weight[:, :, :, columns].reshape(-1, width)))
        return carry

    lax.fori_loop(part * tiles, (part + 1) * tiles, column_step, 0)


def times_turned(left, weight, store):
    unit = weight.shape[1] * weight.shape[2]
    units = max(TILE // unit, 1)

    def row_step(step, carry):
        rows = weight[span(step, units)].reshape(units * unit, weight.shape[-1])
        store(span(step, units * unit), dot(left[...], rows, TURNED))
        return carry

    lax.fori_loop(0, weight.shape[0] // units, row_step, 0)


def into(target):
    def store(columns, value):
        target[:, columns] = value.astype(target.dtype)

    return store


ROWS = 32


def by_rows(count, step):
    def body(index, carry):
        step(span(index, ROWS))
        return carry

    lax.fori_loop(0, count // ROWS, body, 0)


def norm_forward(total, gains, index, unit, scale, use):
    gain, shift = gains[index : index + 1, :], gains[index + 3 : index + 4, :]

    def step(rows):
        value = total[rows, :]
        centre = value - jnp.mean(value, axis=-1, keepdims=True)
        spread = jnp.mean(centre * centre, axis=-1, keepdims=True)
        root = lax.rsqrt(spread + EPS)
        scaled = centre * root
        unit[rows, :] = scaled
        scale[rows, :] = root
        use(rows, scaled * gain + shift)

    by_rows(total.shape[0], step)


def norm_slope(incoming, scaled, root, gain):
    width = scaled.shape[1]
    scaled_grad = incoming * gain
    first = jnp.mean(scaled_grad, axis=-1, keepdims=True)
    second = jnp.mean(scaled_grad * scaled, axis=-1, keepdims=True)
    value = root * (scaled_grad - first - scaled * second)
    of_gain = jnp.sum((incoming * scaled).reshape(ROWS // 8, 8, width), axis=0)
    of_shift = jnp.sum(incoming.reshape(ROWS // 8, 8, width), axis=0)
    return value, of_gain, of_shift


def keep_small(index, sums, small):
    for offset, partial in ((index, sums[0]), (index + 3, sums[1])):
        line = jnp.sum(partial, axis=0, keepdims=True)
        for group in range(2 * small.shape[1]):
            small[group % 2, group // 2, offset : offset + 1, :] = line[
                :, group * 128 : (group + 1) * 128
            ]


def norm_backward(grad, gains, index, unit, scale, target, target_low, small):
    gain = gains[index : index + 1, :]

    def body(block, sums):
        rows = span(block, ROWS)
        value, of_gain, of_shift = norm_slope(grad[rows, :], unit[rows, :], scale[rows, :], gain)
        target[rows, :] = value
        target_low[rows, :] = value.astype(target_low.dtype)
        return (sums[0] + of_gain, sums[1] + of_shift)

    zero = jnp.zeros((8, unit.shape[1]), jnp.float32)
    keep_small(index, lax.fori_loop(0, unit.shape[0] // ROWS, body, (zero, zero)), small)


def norm_both(total, grad, gains, index, result, target, target_low, small):
    gain, shift = gains[index : index + 1, :], gains[index + 3 : index + 4, :]

    def body(block, sums):
        rows = span(block, ROWS)
        value = total[rows, :]
        centre = value - jnp.mean(value, axis=-1, keepdims=True)
        spread = jnp.mean(centre * centre, axis=-1, keepdims=True)
        root = lax.rsqrt(spread + EPS)
        scaled = centre * root
        result[rows, :] = scaled * gain + shift
        incoming = grad[rows, :].astype(jnp.float32)
        value, of_gain, of_shift = norm_slope(incoming, scaled, root, gain)
        target[rows, :] = value
        target_low[rows, :] = value.astype(target_low.dtype)
        return (sums[0] + of_gain, sums[1] + of_shift)

    zero = jnp.zeros((8, total.shape[1]), jnp.float32)
    keep_small(index, lax.fori_loop(0, total.shape[0] // ROWS, body, (zero, zero)), small)


def lane_masks(dtype, scale):
    low = lax.broadcasted_iota(jnp.int32, (1, 2 * HEAD_DIM), 1) < HEAD_DIM
    first = jnp.where(low, scale, 0.0)
    return first.astype(dtype), (scale - first).astype(dtype)


def turned_pair(eye, rows):
    size = rows.shape[1]
    return dot(eye[0:size, 0:size], rows, TURNED).astype(rows.dtype)


def attention_forward(query, keys, values, bias, blocks, eye, mixed, turned, lse, first, last):
    masks = lane_masks(query.dtype, SCALE)

    def pair_step(pair, carry):
        lanes = span(pair, 2 * HEAD_DIM)
        two_query, two_keys, two_values = query[:, lanes], keys[:, lanes], values[:, lanes]
        columns = []
        for q0, q1, k0, k1 in blocks:
            block_values = turned_pair(eye, two_values[k0:k1])
            rows = []
            for head in range(2):
                scores = dot(two_keys[k0:k1], two_query[q0:q1] * masks[head], TURNED)
                scores = scores + bias[k0:k1, q0:q1]
                top = jnp.max(scores, axis=0, keepdims=True)
                weight = jnp.exp(scores - top)
                norm = jnp.sum(weight, axis=0, keepdims=True)
                head_values = block_values[head * HEAD_DIM : (head + 1) * HEAD_DIM]
                rows.append(dot(head_values, weight.astype(query.dtype)) * (1.0 / norm))
                lse[pair, head : head + 1, q0:q1] = top + jnp.log(norm)
            columns.append(jnp.concatenate(rows, axis=0))
        total = jnp.concatenate(columns, axis=1).astype(mixed.dtype)
        turned[pair % 2, span(pair // 2, 2 * HEAD_DIM), :] = total
        mixed[:, lanes] = dot(eye[...], total, TURNED).astype(mixed.dtype)
        return carry

    lax.fori_loop(first, last, pair_step, 0)


def stacked(parts):
    cuts = sorted({at for first, value in parts for at in (first, first + value.shape[0])})
    found = []
    for low, high in zip(cuts, cuts[1:]):
        total = None
        for first, value in parts:
            if first <= low and high <= first + value.shape[0]:
                piece = value[low - first : high - first]
                total = piece if total is None else total + piece
        found.append(total)
    return jnp.concatenate(found, axis=0)


def attention_backward(
    query, keys, values, bias, blocks, eye, lse, grad, query_grad, key_grad, value_grad, first, last
):
    scaled, masks = lane_masks(query.dtype, SCALE), lane_masks(query.dtype, 1.0)

    def pair_step(pair, carry):
        lanes = span(pair, 2 * HEAD_DIM)
        two_query, two_keys, two_values = query[:, lanes], keys[:, lanes], values[:, lanes]
        two_grad = grad[:, lanes]
        of_query, of_keys, of_values = [], [], []
        for q0, q1, k0, k1 in blocks:
            block_keys, block_values = two_keys[k0:k1], two_values[k0:k1]
            slopes, all_probs, heads_query, heads_grad = [], [], [], []
            for head in range(2):
                head_query = two_query[q0:q1] * scaled[head]
                head_grad = two_grad[q0:q1] * masks[head]
                scores = dot(block_keys, head_query, TURNED) + bias[k0:k1, q0:q1]
                probs = jnp.exp(scores - lse[pair, head : head + 1, q0:q1])
                pulled = dot(block_values, head_grad, TURNED)
                inner = jnp.sum(probs * pulled, axis=0, keepdims=True)
                slopes.append((probs * (pulled - inner)).astype(query.dtype))
                all_probs.append(probs.astype(query.dtype))
                heads_query.append(head_query)
                heads_grad.append(head_grad)
            both = jnp.concatenate(slopes, axis=1)
            of_keys.append((k0, dot(both, jnp.concatenate(heads_query, axis=0))))
            both = jnp.concatenate(all_probs, axis=1)
            of_values.append((k0, dot(both, jnp.concatenate(heads_grad, axis=0))))
            block_turned = turned_pair(eye, block_keys * jnp.asarray(SCALE, query.dtype))
            rows = [
                dot(block_turned[head * HEAD_DIM : (head + 1) * HEAD_DIM], slopes[head])
                for head in range(2)
            ]
            of_query.append(jnp.concatenate(rows, axis=0))
        total = jnp.concatenate(of_query, axis=1).astype(query_grad.dtype)
        query_grad[:, lanes] = dot(eye[...], total, TURNED).astype(query_grad.dtype)
        key_grad[:, lanes] = stacked(of_keys).astype(key_grad.dtype)
        value_grad[:, lanes] = stacked(of_values).astype(value_grad.dtype)
        return carry

    lax.fori_loop(first, last, pair_step, 0)


def turn_blocks(left, eye, store):
    width = eye.shape[0]
    for block in range(left.shape[1] // width):
        columns = pl.ds(block * width, width)
        store(block, dot(eye[...], left[:, columns], TURNED).astype(left.dtype))


def turn_by_lane(left, eye, target):
    group = eye.shape[0] // 2

    def store(block, value):
        target[0, pl.ds(block * group, group), :] = value[:group]
        target[1, pl.ds(block * group, group), :] = value[group:]

    turn_blocks(left, eye, store)


SQUARES = 8


def layer_kernel(places, sizes, *refs):
    n_rows, n_mem, width, ff, shard = sizes
    ref = SimpleNamespace(**jax.tree.map(lambda place: refs[place], places))
    place = Place(n_rows, n_mem)
    many = ff // width
    own_ff = ff // (n_rows * n_mem)
    (
        at_query,
        at_key,
        at_value,
        at_output,
        at_cross_query,
        at_cross_key,
        at_cross_value,
        at_cross_output,
    ) = range(SQUARES)
    full = ref.full
    expand, contract = ref.expand_full, ref.contract_full
    tokens, gains = ref.tokens, ref.gains
    low, turned = SimpleNamespace(**ref.low), SimpleNamespace(**ref.turned)

    order = [
        at_query,
        at_key,
        at_value,
        at_output,
        at_cross_key,
        at_cross_value,
        at_cross_query,
        at_cross_output,
    ]
    pool = ref.pool

    def gather_slot(number):
        return pool.at[pl.ds(number % GATHER_SLOTS * n_rows, n_rows)]

    sources = [ref.squares[index] for index in order]
    sources += [ref.expand.at[:, pl.ds(j * width, width)] for j in range(many)]
    sources += [ref.contract.at[pl.ds(j * shard, shard), :] for j in range(many)]
    stores = [full[index] for index in order] + [expand.at[j] for j in range(many)]
    stores += [contract.at[:, :, j] for j in range(many)]
    parts = [Part(item, gather_slot(n), n % 2) for n, item in enumerate(sources)]
    parts.insert(SMALL_AT, Part(ref.small, ref.small_full, 0, True))
    gather = Gather(place, parts, ref.gather_sems)

    def keep(number):
        return pltpu.make_async_copy(gather_slot(number), stores[number], ref.keep_sem.at[number])

    count = [0]

    def load_slot(number):
        first = pool.shape[0] - (1 + number % SLOTS) * n_rows
        return pool.at[pl.ds(first, n_rows)]

    def load(pieces):
        number = count[0]
        count[0] += 1
        for source, first, rows in pieces:
            target = load_slot(number).at[pl.ds(first, rows)]
            pltpu.make_async_copy(source, target, ref.slot_sem.at[number % SLOTS]).start()
        return number

    def ready(number):
        slot = load_slot(number)
        pltpu.make_async_copy(slot, slot, ref.slot_sem.at[number % SLOTS]).wait()
        return slot

    def contract_rows(j):
        groups = n_rows // many
        return [(contract.at[j * groups + i], i * n_mem, n_mem) for i in range(groups)]

    mem_block = ref.memory.shape[1]
    memory, mem_rows = ref.memory, ref.mem_rows

    def memory_own():
        return pltpu.make_async_copy(
            memory.at[place.mem], mem_rows.at[span(place.mem, mem_block)], ref.mem_sem.at[0]
        )

    def memory_total():
        some = mem_rows.at[pl.ds(0, (n_mem - 1) * mem_block)]
        return remote(some, some, ref.mem_sem.at[1], ref.mem_sem.at[2], place.far(1))

    ref.small[...] = jnp.zeros_like(ref.small)
    for member in range(n_mem):

        @pl.when(place.mem == member)
        def _(member=member):
            lanes = slice(member * shard, (member + 1) * shard)
            ref.small[0:3, lanes] = ref.norm_gains[...].astype(jnp.float32)
            ref.small[3:6, lanes] = ref.norm_shifts[...].astype(jnp.float32)

    place.greet()
    memory_own().start()
    for step in range(1, n_mem):
        remote(
            memory.at[(place.mem + step) % n_mem],
            mem_rows.at[span(place.mem, mem_block)],
            ref.mem_sem.at[1],
            ref.mem_sem.at[2],
            place.far(step),
        ).start()

    actions, whole = [], []
    for part in range(len(parts)):
        found, time = gather.events(part)
        for hop, (at, action) in enumerate(found):
            actions.append((HOP + 10 * part + hop, at, action))
        whole.append(time)
    first_hops = [HOP, HOP + 10]
    for code, _, action in actions:
        if code in first_hops:
            action()
    actions = [item for item in actions if item[0] not in first_hops]

    self_bias, cross_bias, eye = ref.self_bias, ref.cross_bias, ref.eye
    own_row = ref.token_ids[pl.ds(place.mem, 1), :].astype(jnp.float32)
    mem_row = ref.memory_ids[pl.ds(place.mem, 1), :].astype(jnp.float32)
    key_place = lax.broadcasted_iota(jnp.int32, self_bias.shape, 0)
    query_place = lax.broadcasted_iota(jnp.int32, self_bias.shape, 1)
    own_wide = jnp.broadcast_to(own_row, self_bias.shape)
    mem_wide = jnp.broadcast_to(mem_row, (cross_bias.shape[1], cross_bias.shape[0]))
    same = (jnp.transpose(own_wide) == own_wide) & (key_place <= query_place)
    self_bias[...] = jnp.where(same, 0.0, NEG)
    cross_bias[...] = jnp.where(jnp.transpose(mem_wide) == own_row, 0.0, NEG)
    eye_row = lax.broadcasted_iota(jnp.int32, eye.shape, 0)
    eye_column = lax.broadcasted_iota(jnp.int32, eye.shape, 1)
    eye[...] = jnp.where(eye_row == eye_column, 1.0, 0.0).astype(eye.dtype)
    turn_by_lane(tokens, eye, turned.tokens)

    accumulated, other = ref.accumulated, ref.other
    hidden, slope, hidden_turned = ref.hidden, ref.slope, ref.hidden_turned

    def small_piece():
        blocks = ref.small_full
        for group in range(n_rows):
            total = None
            for member in range(n_mem):
                value = blocks[group, member]
                total = value if total is None else total + value
            gains[:, group * 128 : (group + 1) * 128] = total

    def query_piece(slot):
        times(tokens, slot, into(ref.query))

    def key_piece(slot):
        times(tokens, slot, into(ref.keys))

    pairs = width // (2 * HEAD_DIM)
    self_blocks = [
        (first, first + 128, max(first - DOC_LIMIT, 0), first + 128)
        for first in range(0, self_bias.shape[1], 128)
    ]
    cross_blocks = [(0, cross_bias.shape[1], 0, cross_bias.shape[0])]

    def value_piece(slot):
        times(tokens, slot, into(ref.values))

    def self_forward(first, last, slot):
        attention_forward(
            ref.query,
            ref.keys,
            ref.values,
            self_bias,
            self_blocks,
            eye,
            ref.attended,
            turned.attended,
            ref.self_lse,
            first,
            last,
        )

    def output_piece(slot):
        def store(columns, value):
            accumulated[:, columns] = ALPHA * tokens[:, columns].astype(jnp.float32) + value

        times(ref.attended, slot, store)

    def output_norm(slot):
        def use(rows, value):
            ref.first_low[rows, :] = value.astype(jnp.bfloat16)
            other[rows, :] = value

        norm_forward(accumulated, gains, 0, ref.unit1, ref.scale1, use)

    def cross_key_piece(slot):
        memory_own().wait()
        memory_total().wait_recv()
        times(mem_rows, slot, into(ref.cross_keys))
        turn_by_lane(mem_rows, eye, turned.memory)

    def cross_value_piece(slot):
        times(mem_rows, slot, into(ref.cross_values))
        turn_by_lane(ref.first_low, eye, turned.first)

    def cross_query_piece(slot):
        times(ref.first_low, slot, into(ref.cross_query))

    def cross_forward(first, last, slot):
        attention_forward(
            ref.cross_query,
            ref.cross_keys,
            ref.cross_values,
            cross_bias,
            cross_blocks,
            eye,
            ref.crossed,
            turned.crossed,
            ref.cross_lse,
            first,
            last,
        )

    def cross_output_piece(slot):
        def store(columns, value):
            accumulated[:, columns] = ALPHA * other[:, columns] + value

        times(ref.crossed, slot, store)

    def cross_output_norm(slot):
        def use(rows, value):
            ref.second_low[rows, :] = value.astype(jnp.bfloat16)
            other[rows, :] = value

        norm_forward(accumulated, gains, 1, ref.unit2, ref.scale2, use)

    def expand_piece(j, half, slot):
        def store(columns, value):
            there = pl.ds(pl.multiple_of(j * width + columns.start, TILE), columns.size)
            bell = 0.5 * (1.0 + lax.erf(value * math.sqrt(0.5)))
            density = jnp.exp(value * value * -0.5) * (1.0 / math.sqrt(2.0 * math.pi))
            hidden[:, there] = (value * bell).astype(hidden.dtype)
            slope[:, there] = (bell + value * density).astype(slope.dtype)

        times(ref.second_low, slot, store, half, 2)

    def expand_turn(j, slot):
        def keep(block, value):
            for index in range(value.shape[0] // shard):
                first = j * width + block * value.shape[0] + index * shard
                device, job = first // own_ff, first % own_ff // shard
                group, member = device // n_mem, device % n_mem
                at = group // 2 * n_mem * shard + member * shard
                hidden_turned[job, group % 2, at : at + shard, :] = value[
                    index * shard : (index + 1) * shard
                ]

        turn_blocks(hidden.at[:, pl.ds(j * width, width)], eye, keep)

    def contract_piece(j, slot):
        block = 2 * n_mem * shard
        for index in range(n_rows // 2):
            rows = pl.ds(index * n_mem * shard, n_mem * shard)
            both = jnp.concatenate([hidden_turned[j, 0, rows], hidden_turned[j, 1, rows]], axis=0)
            columns = pl.ds(index * block, block)
            low.branch[:, columns] = dot(eye[...], both, TURNED).astype(jnp.bfloat16)

        def store(columns, value):
            if j == 0:
                accumulated[:, columns] = ALPHA * other[:, columns] + value
            else:
                accumulated[:, columns] = accumulated[:, columns] + value

        times(low.branch, slot, store)

    quarters = [(pairs * at // 4, pairs * (at + 1) // 4) for at in range(4)]
    pieces = [
        [query_piece],
        [key_piece],
        [value_piece] + [functools.partial(self_forward, *quarter) for quarter in quarters],
        [output_piece, output_norm],
        [cross_key_piece],
        [cross_value_piece],
        [cross_query_piece] + [functools.partial(cross_forward, *quarter) for quarter in quarters],
        [cross_output_piece, cross_output_norm],
    ]
    for j in range(many):
        halves = [functools.partial(expand_piece, j, half) for half in range(2)]
        pieces.append(halves + [functools.partial(expand_turn, j)])
    pieces += [[functools.partial(contract_piece, j)] for j in range(many)]

    def arrive(part):
        gather.core_total(part).wait_recv()
        if part != SMALL_AT:
            keep(part - (part > SMALL_AT)).start()

    def use(part, index):
        if part == SMALL_AT:
            small_piece()
        else:
            number = part - (part > SMALL_AT)
            pieces[number][index](gather_slot(number))

    def settle(part):
        gather.sent(part)
        if part != SMALL_AT:
            keep(part - (part > SMALL_AT)).wait()

    last = 0.0
    for part, time in enumerate(whole):
        time = max(time, last + 0.5)
        actions.append((ARRIVE + part, time, functools.partial(arrive, part)))
        count_here = 1 if part == SMALL_AT else len(pieces[part - (part > SMALL_AT)])
        for index in range(count_here):
            at = time + 0.2 + 0.04 * index
            actions.append((USE + 10 * part + index, at, functools.partial(use, part, index)))
        actions.append((SETTLE + part, time + 0.45, functools.partial(settle, part)))
        last = time
    for action in planned(actions, FORWARD_PLAN):
        action()
    place.tell(ref.ready_sem)

    backward_sources, loads = [], []
    used = [0]

    def next_slot():
        slot = ready(loads[used[0]])
        used[0] += 1
        if len(loads) < len(backward_sources):
            loads.append(load(backward_sources[len(loads)]))
        return slot

    small_sums = ref.small_sums
    small_sums[...] = jnp.zeros_like(small_sums)
    def inner_piece(j):
        slot = next_slot()

        def store(columns, value):
            there = pl.ds(pl.multiple_of(j * width + columns.start, TILE), columns.size)
            slope[:, there] = (value * slope[:, there].astype(jnp.float32)).astype(slope.dtype)

        times_turned(low.third, slot, store)

    def second_piece(j):
        slot = next_slot()

        def store(columns, value):
            if j == 0:
                other[:, columns] = ALPHA * accumulated[:, columns] + value
            else:
                other[:, columns] = other[:, columns] + value

        times_turned(slope.at[:, pl.ds(j * width, width)], slot, store)

    def second_norm_piece():
        norm_backward(
            other, gains, 1, ref.unit2, ref.scale2, accumulated, low.second, small_sums
        )

    def cross_start_piece():
        times_turned(low.second, next_slot(), into(low.branch))

    def cross_piece(first, last):
        attention_backward(
            ref.cross_query,
            ref.cross_keys,
            ref.cross_values,
            cross_bias,
            cross_blocks,
            eye,
            ref.cross_lse,
            low.branch,
            low.cross_query,
            low.cross_key,
            low.cross_value,
            first,
            last,
        )

    def first_piece():
        def store(columns, value):
            other[:, columns] = ALPHA * accumulated[:, columns] + value

        times_turned(low.cross_query, next_slot(), store)

    def first_norm_piece():
        norm_backward(other, gains, 0, ref.unit1, ref.scale1, accumulated, low.first, small_sums)

    def self_start_piece():
        times_turned(low.first, next_slot(), into(low.branch))

    def self_piece(first, last):
        attention_backward(
            ref.query,
            ref.keys,
            ref.values,
            self_bias,
            self_blocks,
            eye,
            ref.self_lse,
            low.branch,
            low.query,
            low.key,
            low.value,
            first,
            last,
        )

    mem_out, mem_in = ref.mem_out, ref.mem_in

    def grad_own():
        return pltpu.make_async_copy(
            mem_out.at[span(place.mem, mem_block)], mem_in.at[place.mem], ref.mem_sem.at[3]
        )

    def grad_total():
        some = mem_in.at[pl.ds(0, n_mem - 1)]
        return remote(some, some, ref.mem_sem.at[4], ref.mem_sem.at[5], place.far(1))

    def memory_key_piece():
        times_turned(low.cross_key, next_slot(), into(other))

    def memory_value_piece():
        def store(columns, value):
            mem_out[:, columns] = (other[:, columns] + value).astype(mem_out.dtype)

        times_turned(low.cross_value, next_slot(), store)
        grad_own().start()
        for step in range(1, n_mem):
            remote(
                mem_out.at[span((place.mem + step) % n_mem, mem_block)],
                mem_in.at[place.mem],
                ref.mem_sem.at[4],
                ref.mem_sem.at[5],
                place.far(step),
            ).start()

    def input_piece(left, start, end=False):
        target = ref.input_grad_here

        def store(columns, value):
            if start:
                target[:, columns] = ALPHA * accumulated[:, columns] + value
            else:
                target[:, columns] = target[:, columns] + value

        times_turned(left, next_slot(), store)
        if end:
            leaving[1].start()

    def memory_end_piece():
        grad_own().wait()
        grad_total().wait_recv()
        for member in range(n_mem):
            ref.memory_grad_here[member] = mem_in[member].astype(jnp.float32)
        leaving[2].start()

    halves = ((0, width // 2), (width // 2, width // 2))
    grads = ref.grads
    plans = []
    for j in range(many):
        for first, columns in halves if j == 0 else ((0, width),):
            target = ref.contract_grad.at[pl.ds(j * shard, shard), pl.ds(first, columns)]
            plans.append((hidden_turned.at[j], low.third, first, target))
    for j in range(many):
        target = ref.expand_grad.at[:, pl.ds(j * width, width)]
        plans.append((turned.second, slope, j * width, target))
    plans += [
        (turned.crossed, low.second, 0, grads[at_cross_output]),
        (turned.memory, low.cross_key, 0, grads[at_cross_key]),
        (turned.memory, low.cross_value, 0, grads[at_cross_value]),
        (turned.first, low.cross_query, 0, grads[at_cross_query]),
        (turned.attended, low.first, 0, grads[at_output]),
        (small_sums, None, 0, ref.small_total),
        (turned.tokens, low.query, 0, grads[at_query]),
        (turned.tokens, low.key, 0, grads[at_key]),
    ]
    for first, columns in halves:
        target = grads[at_value].at[:, pl.ds(first, columns)]
        plans.append((turned.tokens, low.value, first, target))
    jobs = [Job(*plan) for plan in plans]
    reduce = Reduce(place, jobs, ref.reduce_sems, pool, SimpleNamespace(**ref.little))

    inner = [functools.partial(inner_piece, j) for j in range(many)]
    second = [functools.partial(second_piece, j) for j in range(many)]
    base = many + 1
    def weight(index):
        return [(full[index], 0, n_rows)]

    turn = functools.partial(turn_by_lane, ref.second_low, eye, turned.second)
    crosses = [functools.partial(cross_piece, pair, pair + 1) for pair in range(pairs)]
    selves = [functools.partial(self_piece, pair, pair + 1) for pair in range(pairs)]
    work = [(base - 1.7 + j, inner[j], contract_rows(j)) for j in range(2)]
    work += [(base - 1.3, turn, None)]
    work += [(base - 1.7 + j, inner[j], contract_rows(j)) for j in range(2, many)]
    work += [(base - 0.3 + j, second[j], [(expand.at[j], 0, n_rows)]) for j in range(many)]
    base = 2 * many + 1
    work += [
        (base - 0.2, second_norm_piece, None),
        (base - 0.15, cross_start_piece, weight(at_cross_output)),
    ]
    work += [(base + 0.3 + 0.05 * pair, crosses[pair], None) for pair in range(pairs)]
    work += [
        (base + 1.3, first_piece, weight(at_cross_query)),
        (base + 1.31, first_norm_piece, None),
        (base + 1.7, self_start_piece, weight(at_output)),
    ]
    work += [(base + 2.3 + 0.14 * pair, selves[pair], None) for pair in range(pairs)]
    work += [
        (base + 3.7, memory_key_piece, weight(at_cross_key)),
        (base + 4.3, memory_value_piece, weight(at_cross_value)),
        (base + 4.7, functools.partial(input_piece, low.query, True), weight(at_query)),
        (base + 5.5, functools.partial(input_piece, low.key, False), weight(at_key)),
        (base + 6.5, functools.partial(input_piece, low.value, False, True), weight(at_value)),
        (base + 8.5, memory_end_piece, None),
    ]
    actions = [(WORK + index, at, item) for index, (at, *item) in enumerate(work)]
    for number in range(len(jobs)):
        found = reduce.events(number)
        actions.append((CORE + number, found[0][0], found[0][1:]))
        actions.append((LANE + number, found[1][0], found[1][1:]))
        for stage, (at, action) in enumerate(found[2:]):
            actions.append((STAGE + 10 * number + stage, at, (action,)))
    ordered = planned(actions, BACKWARD_PLAN)
    backward_sources += [item[1] for item in ordered if len(item) > 1 and item[1] is not None]
    loads += [load(backward_sources[0]), load(backward_sources[1])]
    leaving = [
        pltpu.make_async_copy(ref.result_here, ref.result, ref.out_sem.at[0]),
        pltpu.make_async_copy(ref.input_grad_here, ref.input_grad, ref.out_sem.at[1]),
        pltpu.make_async_copy(ref.memory_grad_here, ref.memory_grad, ref.out_sem.at[2]),
    ]
    norm_both(
        accumulated, ref.out_grad, gains, 2, ref.result_here, accumulated, low.third, small_sums
    )
    leaving[0].start()

    place.hear(ref.ready_sem)
    for item in ordered:
        item[0]()

    total = ref.small_total[...]
    own = jnp.zeros((8, shard), jnp.float32)
    for member in range(n_mem):
        here = jnp.where(place.mem == member, 1.0, 0.0)
        own = own + here * total[:, member * shard : (member + 1) * shard]
    ref.gains_grad[...] = own[0:3]
    ref.shifts_grad[...] = own[3:6]
    reduce.finish()
    for copy in leaving:
        copy.wait()
    memory_total().wait_send()
    grad_total().wait_send()


SMALL_AT = 2
DOC_LIMIT = 64
HOP, ARRIVE, USE, SETTLE, CORE, LANE, STAGE, WORK = range(1000, 9000, 1000)
FORWARD_PLAN = (
    1020, 1001, 1011, 1021, 1002, 1012, 1003, 1030, 1040, 1013, 1004, 1031, 1041, 1032, 1005, 1033,
    1050, 1042, 1060, 1014, 1022, 2000, 1070, 3000, 1051, 1043, 1034, 4000, 1015, 1061, 2001, 1044,
    3010, 1052, 1023, 1080, 1035, 1071, 4001, 1053, 1062, 2002, 3020, 1081, 2003, 3030, 1045, 1063,
    1072, 1054, 1090, 1064, 4002, 3031, 2004, 3032, 1091, 3033, 1082, 1073, 1092, 1055, 3034, 4003,
    1100, 1110, 1093, 2005, 1083, 3040, 1074, 3041, 4004, 1101, 1065, 1084, 3050, 4005, 1120, 1111,
    2006, 1075, 1102, 3060, 1130, 4006, 1094, 2007, 1121, 3070, 1085, 1112, 1103, 3071, 1113, 1095,
    3072, 1131, 1104, 1122, 3073, 3074, 4007, 1140, 2008, 1114, 3080, 1150, 1132, 1105, 1133, 1123,
    1141, 3081, 2009, 1124, 1160, 1115, 2010, 3090, 1134, 1151, 3091, 3092, 1142, 1152, 4008, 2011,
    3100, 3101, 4009, 1143, 1161, 1153, 3102, 4010, 3110, 1125, 3111, 1144, 1162, 1154, 1135, 2012,
    3112, 1163, 4011, 1145, 3120, 3121, 1164, 3122, 2013, 1155, 3130, 2014, 4012, 3140, 4013, 2015,
    1165, 4014, 3150, 2016, 4015, 3160, 4016,
)
BACKWARD_PLAN = (
    5000, 8003, 8000, 6000, 5001, 6001, 5002, 7000, 8005, 7010, 6002, 5003, 8001, 7001, 8006, 6003,
    5004, 7020, 7002, 8002, 8007, 8004, 6004, 5005, 7011, 7030, 7021, 6005, 5006, 8008, 7012, 7040,
    6006, 5007, 8009, 7022, 7031, 7050, 8010, 8011, 6007, 5008, 8012, 7041, 8013, 7060, 6008, 5009,
    7032, 8014, 7051, 8015, 8016, 8017, 6009, 8018, 5010, 7042, 7052, 7061, 8019, 8020, 7070, 8021,
    6010, 5011, 8030, 8022, 7071, 7062, 7080, 8023, 7090, 6011, 8024, 5012, 8025, 8026, 7081, 7072,
    6012, 7091, 5013, 8027, 7100, 7110, 8028, 6013, 7082, 5014, 7101, 8029, 6014, 7092, 7120, 5015,
    8032, 7111, 6015, 5016, 7102, 8033, 7130, 7121, 7140, 7112, 6016, 8031, 8034, 5017, 7150, 7131,
    7141, 6017, 5018, 7122, 7151, 8035, 7160, 7132, 7142, 7170, 7161, 6018, 7180, 7152, 7171, 7162,
    7181, 7172, 7182,
)


def planned(actions, plan):
    codes = {code for code, _, _ in actions}
    if codes == set(plan):
        at = {code: number for number, code in enumerate(plan)}
        return [item for code, _, item in sorted(actions, key=lambda action: at[action[0]])]
    return [item for _, _, item in sorted(actions, key=lambda action: action[1])]


def copy_kernel(count, *refs):
    for source, target in zip(refs[:count], refs[count:]):
        target[...] = source[...]


def copied(values):
    near = pl.BlockSpec(memory_space=pltpu.VMEM)
    return pl.pallas_call(
        functools.partial(copy_kernel, len(values)),
        out_shape=[jax.ShapeDtypeStruct(value.shape, value.dtype) for value in values],
        in_specs=[near] * len(values),
        out_specs=[near] * len(values),
        compiler_params=pltpu.CompilerParams(vmem_limit_bytes=VMEM_LIMIT),
        name="results",
    )(*values)


def fused(n_rows, n_mem, ins):
    tokens, memory, squares = ins["tokens"], ins["memory"], ins["squares"]
    expand, contract = ins["expand"], ins["contract"]
    tokens_here, width = tokens.shape
    ff = expand.shape[1]
    shard = squares[0].shape[0]
    mem_tokens = memory.shape[0] * memory.shape[1]
    digits, half, many = (n_rows // 2).bit_length() - 1, n_rows // 2, ff // width
    pairs = width // (2 * HEAD_DIM)
    low, high = jnp.bfloat16, jnp.float32
    n_parts = 1 + SQUARES + 2 * many
    n_jobs = n_parts + 2
    dma, vmem = pltpu.SemaphoreType.DMA, pltpu.VMEM
    anywhere, near = pl.BlockSpec(memory_space=pl.ANY), pl.BlockSpec(memory_space=pltpu.VMEM)

    far_ins = dict(memory=memory)
    in_specs = {
        name: jax.tree.map(lambda _: anywhere if name in far_ins else near, value)
        for name, value in ins.items()
    }

    def out(shape, dtype=high):
        return jax.ShapeDtypeStruct(shape, dtype)

    outs = dict(
        result=out(tokens.shape),
        input_grad=out(tokens.shape),
        memory_grad=out(memory.shape),
        grads=[out(item.shape) for item in squares],
        expand_grad=out(expand.shape),
        contract_grad=out(contract.shape),
        gains_grad=out((3, shard)),
        shifts_grad=out((3, shard)),
    )
    far_outs = dict(
        full=[out((n_rows, n_mem, shard, width), low)] * SQUARES,
        expand_full=out((many, n_rows, n_mem, shard, width), low),
        contract_full=out((n_rows, n_mem, many, shard, width), low),
    )
    early_outs = ("result", "input_grad", "memory_grad")
    out_specs = {
        name: anywhere if name in early_outs else jax.tree.map(lambda _: near, value)
        for name, value in outs.items()
    }
    out_specs.update(jax.tree.map(lambda _: anywhere, far_outs))
    outs.update(far_outs)

    def token_rows(dtype):
        return vmem((tokens_here, width), dtype)

    def memory_rows(dtype):
        return vmem((mem_tokens, width), dtype)

    tiny = (8, 128)

    counts = [half >> (stage + 1) for stage in range(digits)]
    units = (OUT_SLOTS + LANE_SLOTS + CORE_RING) * half + RING
    for stage, number in enumerate(counts):
        units += (SUM_SLOTS + (RING if stage else FIRST_RING)) * number
    units = max(units + SLOTS * n_rows, GATHER_SLOTS * n_rows)
    little = dict(
        lanes=vmem((half,) + tiny, high),
        core_in=vmem((half,) + tiny, high),
        sums=[vmem((number,) + tiny, high) for number in counts],
        arrived=[vmem((number,) + tiny, high) for number in counts]
        + [vmem((n_mem - 1,) + tiny, high)],
    )
    left = vmem((2, width // 2, tokens_here), low)
    scratch = dict(
        result_here=token_rows(high),
        input_grad_here=token_rows(high),
        memory_grad_here=vmem(memory.shape, high),
        out_sem=dma((3,)),
        small=vmem(tiny, high),
        small_full=vmem((n_rows, n_mem) + tiny, high),
        small_total=vmem(tiny, high),
        pool=vmem((units, n_mem, shard, width), low),
        slot_sem=dma((SLOTS,)),
        keep_sem=dma((n_parts - 1,)),
        ready_sem=pltpu.SemaphoreType.REGULAR,
        mem_sem=dma((6,)),
        gather_sems=[
            dma(shape + (n_parts,))
            for shape in ((), (), (), (digits,), (digits,), (), ())
            + ((2 * (n_mem - 1),), (2 * (n_mem - 1),))
        ],
        reduce_sems=[dma(shape + (n_jobs,)) for shape in ((), (), (digits + 1,), (digits + 1,))],
        gains=vmem((8, width), high),
        query=token_rows(low),
        keys=token_rows(low),
        values=token_rows(low),
        attended=token_rows(low),
        first_low=token_rows(low),
        second_low=token_rows(low),
        cross_query=token_rows(low),
        crossed=token_rows(low),
        cross_keys=memory_rows(low),
        cross_values=memory_rows(low),
        mem_rows=memory_rows(low),
        mem_out=memory_rows(low),
        mem_in=vmem(memory.shape, low),
        unit1=token_rows(high),
        unit2=token_rows(high),
        accumulated=token_rows(high),
        other=token_rows(high),
        scale1=vmem((tokens_here, 1), high),
        scale2=vmem((tokens_here, 1), high),
        self_bias=vmem((tokens_here, tokens_here), high),
        cross_bias=vmem((mem_tokens, tokens_here), high),
        self_lse=vmem((pairs, 2, tokens_here), high),
        cross_lse=vmem((pairs, 2, tokens_here), high),
        eye=vmem((TILE, TILE), low),
        hidden=vmem((tokens_here, ff), low),
        slope=vmem((tokens_here, ff), low),
        hidden_turned=vmem((many, 2, width // 2, tokens_here), low),
        turned=dict(
            tokens=left, attended=left, first=left, memory=left, crossed=left, second=left
        ),
        low=dict(
            third=token_rows(low),
            second=token_rows(low),
            first=token_rows(low),
            branch=token_rows(low),
            cross_query=token_rows(low),
            cross_key=memory_rows(low),
            cross_value=memory_rows(low),
            query=token_rows(low),
            key=token_rows(low),
            value=token_rows(low),
        ),
        small_sums=vmem((2, half) + tiny, high),
        little=little,
    )
    in_values, in_tree = jax.tree.flatten(ins)
    out_shapes, out_tree = jax.tree.flatten(outs)
    scratch_shapes, scratch_tree = jax.tree.flatten(scratch)
    places = jax.tree.unflatten(in_tree, range(len(in_values)))
    at = len(in_values)
    places.update(jax.tree.unflatten(out_tree, range(at, at + len(out_shapes))))
    at += len(out_shapes)
    places.update(jax.tree.unflatten(scratch_tree, range(at, at + len(scratch_shapes))))
    values = pl.pallas_call(
        functools.partial(layer_kernel, places, (n_rows, n_mem, width, ff, shard)),
        out_shape=out_shapes,
        in_specs=jax.tree.leaves(in_specs),
        out_specs=jax.tree.leaves(out_specs),
        scratch_shapes=scratch_shapes,
        compiler_params=pltpu.CompilerParams(
            collective_id=0, has_side_effects=True, vmem_limit_bytes=VMEM_LIMIT
        ),
        name="layer",
    )(*in_values)
    found = jax.tree.unflatten(out_tree, values)
    for name in far_outs:
        del found[name]
    return found


def local(n_rows, n_mem, *args):
    (
        tokens,
        memory,
        token_ids,
        memory_ids,
        out_grad,
        self_query,
        self_key,
        self_value,
        self_output,
        cross_query,
        cross_key,
        cross_value,
        cross_output,
        expand_weight,
        contract_weight,
        norm_gains,
        norm_shifts,
    ) = args
    shard, width = self_query.shape
    suits = width == 128 * n_rows and shard % 16 == 0 and tokens.shape[0] == 1
    suits = suits and tokens.shape[1] == TILE and expand_weight.shape[1] == n_mem * width
    if not suits or n_rows < 4 or n_rows & (n_rows - 1) or n_mem < 2:
        return plain(*args)
    found = fused(
        n_rows,
        n_mem,
        dict(
            tokens=tokens[0],
            memory=memory,
            token_ids=token_ids,
            memory_ids=memory_ids,
            out_grad=out_grad[0],
            squares=[
                self_query,
                self_key,
                self_value,
                self_output,
                cross_query,
                cross_key,
                cross_value,
                cross_output,
            ],
            expand=expand_weight,
            contract=contract_weight,
            norm_gains=norm_gains,
            norm_shifts=norm_shifts,
        ),
    )
    values, tree = jax.tree.flatten(found)
    found = SimpleNamespace(**jax.tree.unflatten(tree, copied(values)))
    return (
        found.result[None],
        found.input_grad[None],
        found.memory_grad,
        *found.grads,
        found.expand_grad,
        found.contract_grad,
        found.gains_grad,
        found.shifts_grad,
    )


def solution(mesh):
    in_specs = (
        P(("rows", "mem"), None, None),
        P("rows", "mem", None),
        P("rows", None),
        P("rows", None),
        P(("rows", "mem"), None, None),
        P(("rows", "mem"), None),
        P(("rows", "mem"), None),
        P(("rows", "mem"), None),
        P(("rows", "mem"), None),
        P(("rows", "mem"), None),
        P(("rows", "mem"), None),
        P(("rows", "mem"), None),
        P(("rows", "mem"), None),
        P(("rows", "mem"), None),
        P(("rows", "mem"), None),
        P(None, ("rows", "mem")),
        P(None, ("rows", "mem")),
    )
    out_specs = (
        P(("rows", "mem"), None, None),
        P(("rows", "mem"), None, None),
        P("rows", "mem", None),
        P(("rows", "mem"), None),
        P(("rows", "mem"), None),
        P(("rows", "mem"), None),
        P(("rows", "mem"), None),
        P(("rows", "mem"), None),
        P(("rows", "mem"), None),
        P(("rows", "mem"), None),
        P(("rows", "mem"), None),
        P(("rows", "mem"), None),
        P(("rows", "mem"), None),
        P(None, ("rows", "mem")),
        P(None, ("rows", "mem")),
    )
    layer = functools.partial(local, mesh.shape["rows"], mesh.shape["mem"])
    return jax.shard_map(layer, mesh=mesh, in_specs=in_specs, out_specs=out_specs, check_vma=False)
```

```python
import functools
import math
from types import SimpleNamespace

import jax
import jax.numpy as jnp
from jax import lax
from jax.experimental import pallas as pl
from jax.experimental.pallas import tpu as pltpu
from jax.sharding import PartitionSpec as P

MESH = pl.DeviceIdType.MESH

HEADS = 16
HEAD_DIM = 64


ALPHA = 4.16
EPS = 1e-05
SCALE = 0.125
NEG = -1e30


def layer_norm(hidden_activation, gain, shift):
    centre = hidden_activation - jnp.mean(hidden_activation, axis=-1, keepdims=True)
    spread = jnp.mean(centre * centre, axis=-1, keepdims=True)
    return centre * lax.rsqrt(spread + EPS) * gain + shift


def gelu_exact(value):
    return jax.nn.gelu(value, approximate=False)


def product(left, right):
    return jnp.dot(left, right, preferred_element_type=jnp.float32)


def split_heads(matrix):
    return matrix.reshape(matrix.shape[0], matrix.shape[1] // HEAD_DIM, HEAD_DIM)


def grouped(matrix):
    return jnp.moveaxis(matrix.reshape(matrix.shape[0], HEADS // 4, 4 * HEAD_DIM), 1, 0)


def ungrouped(stack):
    return jnp.moveaxis(stack, 0, 1).reshape(stack.shape[1], stack.shape[0] * stack.shape[2])


def row_map(function, items):
    return lax.map(lambda entry: function(*entry), items)


def score_block(query, keys, allowed):
    raw = jnp.einsum(
        "khe,qhe->hkq", split_heads(keys), split_heads(query), preferred_element_type=jnp.float32
    )
    return jnp.where(allowed[None], raw * SCALE, NEG)


def attend_probs(query, keys, allowed, lse):
    scores = score_block(query, keys, allowed)
    return jnp.where(allowed[None], jnp.exp(scores - lse[:, None, :]), 0.0)


def attend_forward(query, keys, values, allowed):
    scores = score_block(query, keys, allowed)
    top = jnp.max(scores, axis=1)
    weight = jnp.where(allowed[None], jnp.exp(scores - top[:, None, :]), 0.0)
    total = jnp.sum(weight, axis=1)
    probs = (weight / total[:, None, :]).astype(jnp.bfloat16)
    mixed = jnp.einsum(
        "hkq,khe->qhe", probs, split_heads(values), preferred_element_type=jnp.float32
    )
    return (mixed.reshape(query.shape), top + jnp.log(total))


def value_pull(grad, values):
    return jnp.einsum(
        "qhe,khe->hkq", split_heads(grad), split_heads(values), preferred_element_type=jnp.float32
    )


def score_grads(probs, pulled, inner):
    return (probs * (pulled - inner[:, None, :]) * SCALE).astype(jnp.bfloat16)


def query_from(score_grad, keys, shape):
    moved = jnp.einsum(
        "hkq,khe->qhe", score_grad, split_heads(keys), preferred_element_type=jnp.float32
    )
    return moved.reshape(shape)


def key_from(score_grad, query, shape):
    moved = jnp.einsum(
        "hkq,qhe->khe", score_grad, split_heads(query), preferred_element_type=jnp.float32
    )
    return moved.reshape(shape)


def value_from(probs, grad, values):
    moved = jnp.einsum(
        "hkq,qhe->khe",
        probs.astype(jnp.bfloat16),
        split_heads(grad),
        preferred_element_type=jnp.float32,
    )
    return moved.reshape(values.shape)


def local_forward(query, keys, values, allowed):

    def one_group(items):
        return attend_forward(items[0], items[1], items[2], allowed)

    mixed, lse = lax.map(one_group, (grouped(query), grouped(keys), grouped(values)))
    return (ungrouped(mixed), lse)


def local_backward(query, keys, values, allowed, lse, grad):

    def one_group(items):
        part_query, part_keys, part_values, part_lse, part_grad = items
        probs = attend_probs(part_query, part_keys, allowed, part_lse)
        pulled = value_pull(part_grad, part_values)
        inner = jnp.sum(probs * pulled, axis=1)
        score_grad = score_grads(probs, pulled, inner)
        return (
            query_from(score_grad, part_keys, part_query.shape),
            key_from(score_grad, part_query, part_keys.shape),
            value_from(probs, part_grad, part_values),
        )

    parts = lax.map(one_group, (grouped(query), grouped(keys), grouped(values), lse, grouped(grad)))
    return (ungrouped(parts[0]), ungrouped(parts[1]), ungrouped(parts[2]))


def plain(
    tokens,
    memory,
    token_ids,
    memory_ids,
    out_grad,
    self_query,
    self_key,
    self_value,
    self_output,
    cross_query,
    cross_key,
    cross_value,
    cross_output,
    expand_weight,
    contract_weight,
    norm_gains,
    norm_shifts,
):
    full = (
        lax.all_gather(self_query, ("rows", "mem"), axis=0, tiled=True),
        lax.all_gather(self_key, ("rows", "mem"), axis=0, tiled=True),
        lax.all_gather(self_value, ("rows", "mem"), axis=0, tiled=True),
        lax.all_gather(self_output, ("rows", "mem"), axis=0, tiled=True),
        lax.all_gather(cross_query, ("rows", "mem"), axis=0, tiled=True),
        lax.all_gather(cross_key, ("rows", "mem"), axis=0, tiled=True),
        lax.all_gather(cross_value, ("rows", "mem"), axis=0, tiled=True),
        lax.all_gather(cross_output, ("rows", "mem"), axis=0, tiled=True),
        lax.all_gather(expand_weight, ("rows", "mem"), axis=0, tiled=True),
        lax.all_gather(contract_weight, ("rows", "mem"), axis=0, tiled=True),
        lax.all_gather(jnp.transpose(norm_gains), ("rows", "mem"), axis=0, tiled=True),
        lax.all_gather(jnp.transpose(norm_shifts), ("rows", "mem"), axis=0, tiled=True),
    )
    (
        self_attention_query,
        decoder_match_label,
        self_attention_value,
        self_attention_output,
        encoder_lookup_probe,
        key_cross,
        value_cross,
        cross_attention_output,
        up_projection,
        narrowing_matrix,
        gain_cols,
        shift_cols,
    ) = full
    gain_rows = jnp.transpose(gain_cols).astype(jnp.float32)
    shift_rows = jnp.transpose(shift_cols).astype(jnp.float32)
    rows_here = tokens.shape[0]
    member = lax.axis_index("mem")
    own_ids = lax.dynamic_slice_in_dim(token_ids, member * rows_here, rows_here, 0)
    positions = jnp.arange(tokens.shape[1], dtype=jnp.int32)
    self_allowed = (own_ids[:, :, None] == own_ids[:, None, :]) & (
        positions[:, None] <= positions[None, :]
    )[None]
    query = product(tokens, self_attention_query).astype(jnp.bfloat16)
    keys = product(tokens, decoder_match_label).astype(jnp.bfloat16)
    values = product(tokens, self_attention_value).astype(jnp.bfloat16)
    self_mixed, self_lse = row_map(local_forward, (query, keys, values, self_allowed))
    attention_result = self_mixed.astype(jnp.bfloat16)
    first, first_back = jax.vjp(
        layer_norm,
        ALPHA * tokens.astype(jnp.float32) + product(attention_result, self_attention_output),
        gain_rows[0],
        shift_rows[0],
    )
    first_reduced = first.astype(jnp.bfloat16)
    cross_queries = product(first_reduced, encoder_lookup_probe).astype(jnp.bfloat16)
    memory_rows = lax.all_to_all(memory, "mem", split_axis=0, concat_axis=1, tiled=True)
    row_ids = lax.dynamic_slice_in_dim(memory_ids, member * rows_here, rows_here, 0)
    cross_allowed = row_ids[:, :, None] == own_ids[:, None, :]
    cross_keys = product(memory_rows, key_cross).astype(jnp.bfloat16)
    cross_values = product(memory_rows, value_cross).astype(jnp.bfloat16)
    cross_mixed, cross_lse = row_map(
        local_forward, (cross_queries, cross_keys, cross_values, cross_allowed)
    )
    cross_attention_result = cross_mixed.astype(jnp.bfloat16)
    second, second_back = jax.vjp(
        layer_norm,
        ALPHA * first + product(cross_attention_result, cross_attention_output),
        gain_rows[1],
        shift_rows[1],
    )
    second_reduced = second.astype(jnp.bfloat16)
    hidden_value, gelu_back = jax.vjp(gelu_exact, product(second_reduced, up_projection))
    hidden_activation = hidden_value.astype(jnp.bfloat16)
    result, third_back = jax.vjp(
        layer_norm,
        ALPHA * second + product(hidden_activation, narrowing_matrix),
        gain_rows[2],
        shift_rows[2],
    )
    third_grad, gain_three, shift_three = third_back(out_grad.astype(jnp.float32))
    feedforward_gradient = third_grad.astype(jnp.bfloat16)
    down_projection_gradient = jnp.einsum(
        "ehj,ehc->jc", hidden_activation, feedforward_gradient, preferred_element_type=jnp.float32
    )
    (inner_grad,) = gelu_back(
        jnp.einsum(
            "hpu,ku->hpk",
            feedforward_gradient,
            narrowing_matrix,
            preferred_element_type=jnp.float32,
        )
    )
    inner_reduced = inner_grad.astype(jnp.bfloat16)
    expand_grad = jnp.einsum(
        "iqg,iqe->ge", second_reduced, inner_reduced, preferred_element_type=jnp.float32
    )
    second_total = ALPHA * third_grad + jnp.einsum(
        "iwm,fm->iwf", inner_reduced, up_projection, preferred_element_type=jnp.float32
    )
    second_grad, gain_two, shift_two = second_back(second_total)
    cross_branch_gradient = second_grad.astype(jnp.bfloat16)
    output_cross_grad = jnp.einsum(
        "nhb,nhc->bc",
        cross_attention_result,
        cross_branch_gradient,
        preferred_element_type=jnp.float32,
    )
    crossed_grad = jnp.einsum(
        "qwp,up->qwu",
        cross_branch_gradient,
        cross_attention_output,
        preferred_element_type=jnp.float32,
    ).astype(jnp.bfloat16)
    query_grads, key_grads, value_grads = row_map(
        local_backward,
        (cross_queries, cross_keys, cross_values, cross_allowed, cross_lse, crossed_grad),
    )
    key_low = key_grads.astype(jnp.bfloat16)
    value_low = value_grads.astype(jnp.bfloat16)
    row_grad = jnp.einsum(
        "sme,de->smd", key_low, key_cross, preferred_element_type=jnp.float32
    ) + jnp.einsum("sme,de->smd", value_low, value_cross, preferred_element_type=jnp.float32)
    key_cross_grad = jnp.einsum(
        "smd,sme->de", memory_rows, key_low, preferred_element_type=jnp.float32
    )
    value_cross_grad = jnp.einsum(
        "smd,sme->de", memory_rows, value_low, preferred_element_type=jnp.float32
    )
    memory_grad = lax.all_to_all(
        row_grad.astype(jnp.bfloat16), "mem", split_axis=1, concat_axis=0, tiled=True
    ).astype(row_grad.dtype)
    probe_lowered_precision = query_grads.astype(jnp.bfloat16)
    query_cross_grad = jnp.einsum(
        "nhb,nhc->bc", first_reduced, probe_lowered_precision, preferred_element_type=jnp.float32
    )
    first_total = ALPHA * second_grad + jnp.einsum(
        "qwp,up->qwu",
        probe_lowered_precision,
        encoder_lookup_probe,
        preferred_element_type=jnp.float32,
    )
    first_grad, gain_one, shift_one = first_back(first_total)
    self_branch_gradient = first_grad.astype(jnp.bfloat16)
    output_self_grad = jnp.einsum(
        "nhb,nhc->bc", attention_result, self_branch_gradient, preferred_element_type=jnp.float32
    )
    attended_grad = jnp.einsum(
        "qwp,up->qwu",
        self_branch_gradient,
        self_attention_output,
        preferred_element_type=jnp.float32,
    ).astype(jnp.bfloat16)
    self_query_reduced, decoder_label_lowered, self_value_reduced = row_map(
        local_backward, (query, keys, values, self_allowed, self_lse, attended_grad)
    )
    self_query_reduced = self_query_reduced.astype(jnp.bfloat16)
    decoder_label_lowered = decoder_label_lowered.astype(jnp.bfloat16)
    self_value_reduced = self_value_reduced.astype(jnp.bfloat16)
    query_self_grad = jnp.einsum(
        "nhb,nhc->bc", tokens, self_query_reduced, preferred_element_type=jnp.float32
    )
    key_self_grad = jnp.einsum(
        "nhb,nhc->bc", tokens, decoder_label_lowered, preferred_element_type=jnp.float32
    )
    value_self_grad = jnp.einsum(
        "nhb,nhc->bc", tokens, self_value_reduced, preferred_element_type=jnp.float32
    )
    input_grad = (
        ALPHA * first_grad
        + jnp.einsum(
            "qwp,up->qwu",
            self_query_reduced,
            self_attention_query,
            preferred_element_type=jnp.float32,
        )
        + jnp.einsum(
            "qwp,up->qwu",
            decoder_label_lowered,
            decoder_match_label,
            preferred_element_type=jnp.float32,
        )
        + jnp.einsum(
            "qwp,up->qwu",
            self_value_reduced,
            self_attention_value,
            preferred_element_type=jnp.float32,
        )
    )
    gain_grad = jnp.stack([gain_one, gain_two, gain_three], axis=1)
    shift_grad = jnp.stack([shift_one, shift_two, shift_three], axis=1)
    sums = (
        lax.psum_scatter(query_self_grad, ("rows", "mem"), scatter_dimension=0, tiled=True),
        lax.psum_scatter(key_self_grad, ("rows", "mem"), scatter_dimension=0, tiled=True),
        lax.psum_scatter(value_self_grad, ("rows", "mem"), scatter_dimension=0, tiled=True),
        lax.psum_scatter(output_self_grad, ("rows", "mem"), scatter_dimension=0, tiled=True),
        lax.psum_scatter(query_cross_grad, ("rows", "mem"), scatter_dimension=0, tiled=True),
        lax.psum_scatter(key_cross_grad, ("rows", "mem"), scatter_dimension=0, tiled=True),
        lax.psum_scatter(value_cross_grad, ("rows", "mem"), scatter_dimension=0, tiled=True),
        lax.psum_scatter(output_cross_grad, ("rows", "mem"), scatter_dimension=0, tiled=True),
        lax.psum_scatter(expand_grad, ("rows", "mem"), scatter_dimension=0, tiled=True),
        lax.psum_scatter(
            down_projection_gradient, ("rows", "mem"), scatter_dimension=0, tiled=True
        ),
        lax.psum_scatter(gain_grad, ("rows", "mem"), scatter_dimension=0, tiled=True),
        lax.psum_scatter(shift_grad, ("rows", "mem"), scatter_dimension=0, tiled=True),
    )
    return (
        result,
        input_grad,
        memory_grad,
        sums[0],
        sums[1],
        sums[2],
        sums[3],
        sums[4],
        sums[5],
        sums[6],
        sums[7],
        sums[8],
        sums[9],
        jnp.transpose(sums[10]),
        jnp.transpose(sums[11]),
    )


ALL = slice(None)
TILE = 256
SLOTS = 3
GATHER_SLOTS = 10
VMEM_LIMIT = 61 * 1024 * 1024


def flip(index, unit):
    return index + unit * (1 - 2 * ((index // unit) % 2))


def span(index, size):
    return pl.ds(pl.multiple_of(index * size, size), size)


class Place:
    def __init__(self, n_rows, n_mem):
        self.n_rows, self.n_mem = n_rows, n_mem
        self.digits = (n_rows // 2).bit_length() - 1
        self.row = lax.axis_index("rows")
        self.mem = lax.axis_index("mem")
        self.lane = self.row % 2

    def turn(self, index, stage):
        rising, falling = 2 << stage, 2 << (self.digits - 1 - stage)
        return flip(index, rising) * (1 - self.lane) + flip(index, falling) * self.lane

    def sibling(self):
        return (flip(self.row, 1), self.mem)

    def partner(self, stage):
        return (self.turn(self.row, stage), self.mem)

    def far(self, step):
        return (self.row, (self.mem + step) % self.n_mem)

    def others(self):
        found = [self.far(step) for step in range(1, self.n_mem)]
        found += [self.partner(stage) for stage in range(self.digits)]
        return found + [self.sibling()]

    def tell(self, semaphore):
        for other in self.others():
            pl.semaphore_signal(semaphore, inc=1, device_id=other, device_id_type=MESH)

    def hear(self, semaphore):
        pl.semaphore_wait(semaphore, len(self.others()))

    def greet(self):
        self.tell(pltpu.get_barrier_semaphore())
        self.hear(pltpu.get_barrier_semaphore())


def remote(source, target, send_sem, recv_sem, device):
    return pltpu.make_async_remote_copy(
        src_ref=source,
        dst_ref=target,
        send_sem=send_sem,
        recv_sem=recv_sem,
        device_id=device,
        device_id_type=MESH,
    )


def waits(total):
    return (lambda: total().wait_recv(), lambda: total().wait_send())


class Part:
    def __init__(self, source, target, near=0, straight=False):
        self.source, self.target = source, target
        self.near, self.straight = near, straight


class Gather:
    def __init__(self, place, parts, sems):
        self.place, self.parts = place, parts
        (
            self.own_sem,
            self.far_send,
            self.far_recv,
            self.plane_send,
            self.plane_recv,
            self.core_send,
            self.core_recv,
            self.line_send,
            self.line_recv,
        ) = sems

    def group(self, number, group):
        return self.parts[number].target.at[group]

    def one(self, number, group, member):
        return self.parts[number].target.at[group, member]

    def shard(self, number):
        return self.parts[number].source

    def mine(self, number):
        return self.one(number, self.place.row, self.place.mem)

    def own(self, number):
        return pltpu.make_async_copy(self.shard(number), self.mine(number), self.own_sem.at[number])

    def held(self, stage):
        groups = [self.place.row]
        for before in range(stage):
            groups = groups + [self.place.turn(group, before) for group in groups]
        return groups

    def far_total(self, number):
        part = self.parts[number]
        some = part.target.at[pl.ds(0, 1 << part.near), pl.ds(0, self.place.n_mem - 1)]
        return remote(
            some, some, self.far_send.at[number], self.far_recv.at[number], self.place.far(1)
        )

    def far_hop(self, number, first):
        place = self.place
        for group in self.held(self.parts[number].near):
            target = self.one(number, group, place.mem)
            source = self.shard(number) if first else target
            for step in range(1, place.n_mem):
                remote(
                    source,
                    target,
                    self.far_send.at[number],
                    self.far_recv.at[number],
                    place.far(step),
                ).start()

    def sides(self, step):
        mem, n_mem = self.place.mem, self.place.n_mem
        return (
            ((mem - step >= 0) & (mem + 1 < n_mem), mem - step, 1, mem - 1 - step >= 0),
            ((mem + step < n_mem) & (mem >= 1), mem + step, n_mem - 1, mem + 1 + step < n_mem),
        )

    def line_total(self, number, step, side):
        part, at = self.parts[number], 2 * step + side
        some = part.target.at[pl.ds(0, 1 << part.near), 0]
        sems = (self.line_send.at[at, number], self.line_recv.at[at, number])
        return remote(some, some, *sems, self.place.far(1))

    def line_arrived(self, number, step):
        for side, (_, _, _, receives) in enumerate(self.sides(step)):

            @pl.when(receives)
            def _(side=side):
                self.line_total(number, step, side).wait_recv()

    def line_sent(self, number, step):
        for side, (sends, _, _, _) in enumerate(self.sides(step)):

            @pl.when(sends)
            def _(side=side):
                self.line_total(number, step, side).wait_send()

    def line_hop(self, number, step, first):
        place = self.place
        for side, (sends, member, towards, _) in enumerate(self.sides(step)):
            member = (member + place.n_mem) % place.n_mem

            @pl.when(sends)
            def _(side=side, member=member, towards=towards):
                for group in self.held(self.parts[number].near):
                    target = self.one(number, group, member)
                    remote(
                        self.shard(number) if first else target,
                        target,
                        self.line_send.at[2 * step + side, number],
                        self.line_recv.at[2 * step + side, number],
                        place.far(towards),
                    ).start()

    def plane_total(self, number, stage):
        part = self.parts[number]
        some = part.target.at[pl.ds(0, 1 << stage)]
        if stage < part.near:
            some = part.target.at[pl.ds(0, 1 << stage), 0]
        return remote(
            some,
            some,
            self.plane_send.at[stage, number],
            self.plane_recv.at[stage, number],
            self.place.partner(stage),
        )

    def plane_hop(self, number, stage, first):
        for group in self.held(stage):
            if stage < self.parts[number].near:
                target = self.one(number, group, self.place.mem)
            else:
                target = self.group(number, group)
            remote(
                self.shard(number) if first else target,
                target,
                self.plane_send.at[stage, number],
                self.plane_recv.at[stage, number],
                self.place.partner(stage),
            ).start()

    def core_total(self, number):
        some = self.parts[number].target.at[pl.ds(0, self.place.n_rows // 2)]
        return remote(
            some, some, self.core_send.at[number], self.core_recv.at[number], self.place.sibling()
        )

    def core_hop(self, number, first):
        for group in self.held(self.place.digits):
            block = self.group(number, group)
            remote(
                block,
                block,
                self.core_send.at[number],
                self.core_recv.at[number],
                self.place.sibling(),
            ).start()

    def hops(self, number):
        part, take = self.parts[number], functools.partial
        along = []
        if part.straight:
            along.append((1.6, take(self.far_hop, number)) + waits(take(self.far_total, number)))
        else:
            for step in range(self.place.n_mem - 1):
                along.append(
                    (
                        0.55 if step else 1.4,
                        take(self.line_hop, number, step),
                        take(self.line_arrived, number, step),
                        take(self.line_sent, number, step),
                    )
                )
        plane = []
        for stage in range(self.place.digits):
            total = take(self.plane_total, number, stage)
            plane.append((1.5, take(self.plane_hop, number, stage)) + waits(total))
        core = (1.5, take(self.core_hop, number)) + waits(take(self.core_total, number))
        return plane[: part.near] + along + plane[part.near :] + [core]

    def events(self, number):
        hops = self.hops(number)
        time, found = float(number), []

        def act(at):
            if at == 0:
                self.own(number).start()
            else:
                if at == 1:
                    self.own(number).wait()
                hops[at - 1][2]()
            hops[at][1](at == 0)

        for at in range(len(hops)):
            time += hops[at][0] if at else 0.0
            found.append((time, functools.partial(act, at)))
        return found, time + 0.9

    def sent(self, number):
        for hop in self.hops(number):
            hop[3]()


class Job:
    def __init__(self, left, right, first, target):
        self.left, self.right, self.first, self.target = left, right, first, target
        self.small = right is None
        self.width = target.shape[-1]
        self.large = 0


OUT_SLOTS, LANE_SLOTS, SUM_SLOTS, CORE_RING, FIRST_RING, RING = 2, 3, 2, 2, 6, 4


class Reduce:
    def __init__(self, place, jobs, sems, pool, small):
        self.place, self.jobs, self.small = place, jobs, small
        self.core_send, self.core_recv, self.stage_send, self.stage_recv = sems
        wanted = [place.row]
        for stage in reversed(range(place.digits)):
            wanted = wanted + [place.turn(group, stage) for group in wanted]
        self.wanted = [group // 2 for group in wanted]
        for number, job in enumerate(job for job in jobs if not job.small):
            job.large = number
        used, half = [0], place.n_rows // 2

        def take(count, units):
            first = used[0]
            used[0] += count * units
            return [pool.at[pl.ds(first + i * units, units)] for i in range(count)]

        self.outs = take(OUT_SLOTS, half)
        self.lane_slots = take(LANE_SLOTS, half)
        self.core_ring = take(CORE_RING, half)
        self.sum_slots, self.rings = [], []
        for stage in range(place.digits):
            self.sum_slots.append(take(SUM_SLOTS, self.count(stage)))
            self.rings.append(take(RING if stage else FIRST_RING, self.count(stage)))
        self.rings.append(take(RING, 1))
        self.used = used[0]

    def count(self, stage):
        return max(self.place.n_rows // 4 >> stage, 1)

    def cut(self, ref, job):
        return ref if job.width == ref.shape[-1] else ref.at[:, :, :, pl.ds(0, job.width)]

    def out(self, job):
        return self.cut(self.outs[job.large % OUT_SLOTS], job)

    def lanes(self, job):
        if job.small:
            return self.small.lanes
        return self.cut(self.lane_slots[job.large % LANE_SLOTS], job)

    def core_in(self, job):
        if job.small:
            return self.small.core_in
        return self.cut(self.core_ring[job.large % CORE_RING], job)

    def sums(self, job, stage):
        if job.small:
            return self.small.sums[stage]
        return self.cut(self.sum_slots[stage][job.large % SUM_SLOTS], job)

    def arrived(self, job, stage):
        if job.small:
            return self.small.arrived[stage]
        ring = self.rings[stage]
        units = self.cut(ring[job.large % len(ring)], job)
        if stage == self.place.digits:
            return units.at[0, pl.ds(0, self.place.n_mem - 1)]
        return units

    def previous(self, number, distance):
        found = [n for n in range(number) if not self.jobs[n].small]
        if self.jobs[number].small or len(found) < distance:
            return None
        return found[-distance]

    def core_copy(self, number):
        job = self.jobs[number]
        source = job.left.at[1 - self.place.lane] if job.small else self.out(job)
        return remote(
            source,
            self.core_in(job),
            self.core_send.at[number],
            self.core_recv.at[number],
            self.place.sibling(),
        )

    def product(self, job, side, store):
        half = self.place.n_rows // 2
        group = job.left.shape[1] // half
        width = min(TILE, job.width)
        unit = (self.place.n_mem, group // self.place.n_mem, width)

        def column_step(step, carry):
            source = pl.ds(pl.multiple_of(job.first + step * width, width), width)
            value = dot(job.left[side], job.right[:, source])
            for index in range(half):
                block = value[index * group : (index + 1) * group].reshape(unit)
                store(index, span(step, width), block)
            return carry

        lax.fori_loop(0, job.width // width, column_step, 0)

    def core_stage(self, number):
        job = self.jobs[number]
        if not job.small:
            before = self.previous(number, OUT_SLOTS)
            if before is not None:
                self.core_copy(before).wait_send()
            out = self.out(job)

            def store(index, columns, value):
                out[index, :, :, columns] = value.astype(out.dtype)

            self.product(job, 1 - self.place.lane, store)
        self.core_copy(number).start()

    def lane_stage(self, number):
        job = self.jobs[number]
        before = self.previous(number, LANE_SLOTS)
        if before is not None:
            self.total(before, 0).wait_send()
        lanes, arrived = self.lanes(job), self.core_in(job)
        self.core_copy(number).wait_recv()
        if job.small:
            lanes[...] = job.left[self.place.lane] + arrived[...]
        else:

            def store(index, columns, value):
                total = value + arrived[index, :, :, columns].astype(jnp.float32)
                lanes[index, :, :, columns] = total.astype(lanes.dtype)

            self.product(job, self.place.lane, store)
        self.send(number, 0)

    def unit(self, job, stage, index):
        if stage == 0:
            return self.lanes(job).at[self.wanted[index]]
        return self.sums(job, stage - 1).at[index]

    def piece(self, job, unit, member):
        return unit if job.small else unit.at[member]

    def send(self, number, stage):
        job, place = self.jobs[number], self.place
        arrived = self.arrived(job, stage)
        sems = (self.stage_send.at[stage, number], self.stage_recv.at[stage, number])
        if stage == place.digits:
            unit = self.unit(job, stage, 0)
            for step in range(1, place.n_mem):
                source = self.piece(job, unit, (place.mem + step) % place.n_mem)
                remote(source, arrived.at[step - 1], *sems, place.far(step)).start()
            return
        left = self.count(stage)
        for index in range(left):
            source = self.unit(job, stage, left + index)
            remote(source, arrived.at[index], *sems, place.partner(stage)).start()

    def total(self, number, stage):
        some = self.arrived(self.jobs[number], stage)
        sems = (self.stage_send.at[stage, number], self.stage_recv.at[stage, number])
        return remote(some, some, *sems, self.place.far(1))

    def stage(self, number, stage):
        job, place = self.jobs[number], self.place
        arrived = self.arrived(job, stage)
        if stage == place.digits:
            self.total(number, stage).wait_recv()
            value = self.piece(job, self.unit(job, stage, 0), place.mem)[...].astype(jnp.float32)
            for step in range(place.n_mem - 1):
                value = value + arrived[step].astype(jnp.float32)
            job.target[...] = value
            return
        before = self.previous(number, SUM_SLOTS)
        if before is not None:
            self.total(before, stage + 1).wait_send()
        self.total(number, stage).wait_recv()
        sums = self.sums(job, stage)
        for index in range(self.count(stage)):
            unit, coming, target = self.unit(job, stage, index), arrived.at[index], sums.at[index]
            if job.small:
                target[...] = unit[...] + coming[...]
                continue

            def add(member, carry, unit=unit, coming=coming, target=target):
                value = unit[member].astype(jnp.float32) + coming[member].astype(jnp.float32)
                target[member] = value.astype(target.dtype)
                return carry

            lax.fori_loop(0, place.n_mem, add, 0)
        self.send(number, stage + 1)

    def events(self, number):
        found = [(0.0, functools.partial(self.core_stage, number))]
        found.append((0.9, functools.partial(self.lane_stage, number)))
        time = 2.2 if number < 2 else 3.2
        for stage in range(self.place.digits + 1):
            found.append((time, functools.partial(self.stage, number, stage)))
            time += 1.4
        found[-1] = (found[-1][0] - 0.3, found[-1][1])
        return [(number + time, action) for time, action in found]

    def finish(self):
        n_jobs, last = len(self.jobs), self.place.digits
        out = {self.previous(number, OUT_SLOTS) for number in range(n_jobs)}
        lanes = {self.previous(number, LANE_SLOTS) for number in range(n_jobs)}
        sums = {self.previous(number, SUM_SLOTS) for number in range(n_jobs)}
        for number in range(n_jobs):
            if number not in out:
                self.core_copy(number).wait_send()
            if number not in lanes:
                self.total(number, 0).wait_send()
            if number not in sums:
                for stage in range(1, last + 1):
                    self.total(number, stage).wait_send()


NORMAL = (((1,), (0,)), ((), ()))
TURNED = (((1,), (1,)), ((), ()))
LEFT_TURNED = (((0,), (0,)), ((), ()))


def dot(left, right, dims=NORMAL):
    return lax.dot_general(left, right, dims, preferred_element_type=jnp.float32)


def times(left, weight, store, part=0, parts=1):
    size = weight.shape[-1]
    width = min(TILE, size)
    tiles = size // width // parts

    def column_step(step, carry):
        columns = span(step, width)
        store(columns, dot(left[...], weight[:, :, :, columns].reshape(-1, width)))
        return carry

    lax.fori_loop(part * tiles, (part + 1) * tiles, column_step, 0)


def times_turned(left, weight, store):
    unit = weight.shape[1] * weight.shape[2]
    units = max(TILE // unit, 1)

    def row_step(step, carry):
        rows = weight[span(step, units)].reshape(units * unit, weight.shape[-1])
        store(span(step, units * unit), dot(left[...], rows, TURNED))
        return carry

    lax.fori_loop(0, weight.shape[0] // units, row_step, 0)


def into(target):
    def store(columns, value):
        target[:, columns] = value.astype(target.dtype)

    return store


ROWS = 32


def by_rows(count, step):
    def body(index, carry):
        step(span(index, ROWS))
        return carry

    lax.fori_loop(0, count // ROWS, body, 0)


def norm_forward(total, gains, index, unit, scale, use):
    gain, shift = gains[index : index + 1, :], gains[index + 3 : index + 4, :]

    def step(rows):
        value = total[rows, :]
        centre = value - jnp.mean(value, axis=-1, keepdims=True)
        spread = jnp.mean(centre * centre, axis=-1, keepdims=True)
        root = lax.rsqrt(spread + EPS)
        scaled = centre * root
        unit[rows, :] = scaled
        scale[rows, :] = root
        use(rows, scaled * gain + shift)

    by_rows(total.shape[0], step)


def norm_slope(incoming, scaled, root, gain):
    width = scaled.shape[1]
    scaled_grad = incoming * gain
    first = jnp.mean(scaled_grad, axis=-1, keepdims=True)
    second = jnp.mean(scaled_grad * scaled, axis=-1, keepdims=True)
    value = root * (scaled_grad - first - scaled * second)
    of_gain = jnp.sum((incoming * scaled).reshape(ROWS // 8, 8, width), axis=0)
    of_shift = jnp.sum(incoming.reshape(ROWS // 8, 8, width), axis=0)
    return value, of_gain, of_shift


def keep_small(index, sums, small):
    for offset, partial in ((index, sums[0]), (index + 3, sums[1])):
        line = jnp.sum(partial, axis=0, keepdims=True)
        for group in range(2 * small.shape[1]):
            small[group % 2, group // 2, offset : offset + 1, :] = line[
                :, group * 128 : (group + 1) * 128
            ]


def norm_backward(grad, gains, index, unit, scale, target, target_low, small):
    gain = gains[index : index + 1, :]

    def body(block, sums):
        rows = span(block, ROWS)
        value, of_gain, of_shift = norm_slope(grad[rows, :], unit[rows, :], scale[rows, :], gain)
        target[rows, :] = value
        target_low[rows, :] = value.astype(target_low.dtype)
        return (sums[0] + of_gain, sums[1] + of_shift)

    zero = jnp.zeros((8, unit.shape[1]), jnp.float32)
    keep_small(index, lax.fori_loop(0, unit.shape[0] // ROWS, body, (zero, zero)), small)


def norm_both(total, grad, gains, index, result, target, target_low, small):
    gain, shift = gains[index : index + 1, :], gains[index + 3 : index + 4, :]

    def body(block, sums):
        rows = span(block, ROWS)
        value = total[rows, :]
        centre = value - jnp.mean(value, axis=-1, keepdims=True)
        spread = jnp.mean(centre * centre, axis=-1, keepdims=True)
        root = lax.rsqrt(spread + EPS)
        scaled = centre * root
        result[rows, :] = scaled * gain + shift
        incoming = grad[rows, :].astype(jnp.float32)
        value, of_gain, of_shift = norm_slope(incoming, scaled, root, gain)
        target[rows, :] = value
        target_low[rows, :] = value.astype(target_low.dtype)
        return (sums[0] + of_gain, sums[1] + of_shift)

    zero = jnp.zeros((8, total.shape[1]), jnp.float32)
    keep_small(index, lax.fori_loop(0, total.shape[0] // ROWS, body, (zero, zero)), small)


def lane_masks(dtype, scale):
    low = lax.broadcasted_iota(jnp.int32, (1, 2 * HEAD_DIM), 1) < HEAD_DIM
    first = jnp.where(low, scale, 0.0)
    return first.astype(dtype), (scale - first).astype(dtype)


def turned_pair(eye, rows):
    size = rows.shape[1]
    return dot(eye[0:size, 0:size], rows, TURNED).astype(rows.dtype)


def attention_forward(query, keys, values, bias, blocks, eye, mixed, turned, lse, first, last):
    masks = lane_masks(query.dtype, SCALE)

    def pair_step(pair, carry):
        lanes = span(pair, 2 * HEAD_DIM)
        two_query, two_keys, two_values = query[:, lanes], keys[:, lanes], values[:, lanes]
        columns = []
        for q0, q1, k0, k1 in blocks:
            block_values = turned_pair(eye, two_values[k0:k1])
            rows = []
            for head in range(2):
                scores = dot(two_keys[k0:k1], two_query[q0:q1] * masks[head], TURNED)
                scores = scores + bias[k0:k1, q0:q1]
                top = jnp.max(scores, axis=0, keepdims=True)
                weight = jnp.exp(scores - top)
                norm = jnp.sum(weight, axis=0, keepdims=True)
                head_values = block_values[head * HEAD_DIM : (head + 1) * HEAD_DIM]
                rows.append(dot(head_values, weight.astype(query.dtype)) * (1.0 / norm))
                lse[pair, head : head + 1, q0:q1] = top + jnp.log(norm)
            columns.append(jnp.concatenate(rows, axis=0))
        total = jnp.concatenate(columns, axis=1).astype(mixed.dtype)
        turned[pair % 2, span(pair // 2, 2 * HEAD_DIM), :] = total
        mixed[:, lanes] = dot(eye[...], total, TURNED).astype(mixed.dtype)
        return carry

    lax.fori_loop(first, last, pair_step, 0)


def stacked(parts):
    cuts = sorted({at for first, value in parts for at in (first, first + value.shape[0])})
    found = []
    for low, high in zip(cuts, cuts[1:]):
        total = None
        for first, value in parts:
            if first <= low and high <= first + value.shape[0]:
                piece = value[low - first : high - first]
                total = piece if total is None else total + piece
        found.append(total)
    return jnp.concatenate(found, axis=0)


def attention_backward(
    query, keys, values, bias, blocks, eye, lse, grad, query_grad, key_grad, value_grad, first, last
):
    scaled, masks = lane_masks(query.dtype, SCALE), lane_masks(query.dtype, 1.0)

    def pair_step(pair, carry):
        lanes = span(pair, 2 * HEAD_DIM)
        two_query, two_keys, two_values = query[:, lanes], keys[:, lanes], values[:, lanes]
        two_grad = grad[:, lanes]
        of_query, of_keys, of_values = [], [], []
        for q0, q1, k0, k1 in blocks:
            block_keys, block_values = two_keys[k0:k1], two_values[k0:k1]
            slopes, all_probs, heads_query, heads_grad = [], [], [], []
            for head in range(2):
                head_query = two_query[q0:q1] * scaled[head]
                head_grad = two_grad[q0:q1] * masks[head]
                scores = dot(block_keys, head_query, TURNED) + bias[k0:k1, q0:q1]
                probs = jnp.exp(scores - lse[pair, head : head + 1, q0:q1])
                pulled = dot(block_values, head_grad, TURNED)
                inner = jnp.sum(probs * pulled, axis=0, keepdims=True)
                slopes.append((probs * (pulled - inner)).astype(query.dtype))
                all_probs.append(probs.astype(query.dtype))
                heads_query.append(head_query)
                heads_grad.append(head_grad)
            both = jnp.concatenate(slopes, axis=1)
            of_keys.append((k0, dot(both, jnp.concatenate(heads_query, axis=0))))
            both = jnp.concatenate(all_probs, axis=1)
            of_values.append((k0, dot(both, jnp.concatenate(heads_grad, axis=0))))
            block_turned = turned_pair(eye, block_keys * jnp.asarray(SCALE, query.dtype))
            rows = [
                dot(block_turned[head * HEAD_DIM : (head + 1) * HEAD_DIM], slopes[head])
                for head in range(2)
            ]
            of_query.append(jnp.concatenate(rows, axis=0))
        total = jnp.concatenate(of_query, axis=1).astype(query_grad.dtype)
        query_grad[:, lanes] = dot(eye[...], total, TURNED).astype(query_grad.dtype)
        key_grad[:, lanes] = stacked(of_keys).astype(key_grad.dtype)
        value_grad[:, lanes] = stacked(of_values).astype(value_grad.dtype)
        return carry

    lax.fori_loop(first, last, pair_step, 0)


def turn_blocks(left, eye, store):
    width = eye.shape[0]
    for block in range(left.shape[1] // width):
        columns = pl.ds(block * width, width)
        store(block, dot(eye[...], left[:, columns], TURNED).astype(left.dtype))


def turn_by_lane(left, eye, target):
    group = eye.shape[0] // 2

    def store(block, value):
        target[0, pl.ds(block * group, group), :] = value[:group]
        target[1, pl.ds(block * group, group), :] = value[group:]

    turn_blocks(left, eye, store)


SQUARES = 8


def layer_kernel(places, sizes, *refs):
    n_rows, n_mem, width, ff, shard = sizes
    ref = SimpleNamespace(**jax.tree.map(lambda place: refs[place], places))
    place = Place(n_rows, n_mem)
    many = ff // width
    own_ff = ff // (n_rows * n_mem)
    (
        at_query,
        at_key,
        at_value,
        at_output,
        at_cross_query,
        at_cross_key,
        at_cross_value,
        at_cross_output,
    ) = range(SQUARES)
    full = ref.full
    expand, contract = ref.expand_full, ref.contract_full
    tokens, gains = ref.tokens, ref.gains
    low, turned = SimpleNamespace(**ref.low), SimpleNamespace(**ref.turned)

    order = [
        at_query,
        at_key,
        at_value,
        at_output,
        at_cross_key,
        at_cross_value,
        at_cross_query,
        at_cross_output,
    ]
    pool = ref.pool

    def gather_slot(number):
        return pool.at[pl.ds(number % GATHER_SLOTS * n_rows, n_rows)]

    sources = [ref.squares[index] for index in order]
    sources += [ref.expand.at[:, pl.ds(j * width, width)] for j in range(many)]
    sources += [ref.contract.at[pl.ds(j * shard, shard), :] for j in range(many)]
    stores = [full[index] for index in order] + [expand.at[j] for j in range(many)]
    stores += [contract.at[:, :, j] for j in range(many)]
    parts = [Part(item, gather_slot(n), int(n % 4 == 3)) for n, item in enumerate(sources)]
    parts.insert(SMALL_AT, Part(ref.small, ref.small_full, 0, True))
    gather = Gather(place, parts, ref.gather_sems)

    def keep(number):
        return pltpu.make_async_copy(gather_slot(number), stores[number], ref.keep_sem.at[number])

    count = [0]

    def load_slot(number):
        first = pool.shape[0] - (1 + number % SLOTS) * n_rows
        return pool.at[pl.ds(first, n_rows)]

    def load(pieces):
        number = count[0]
        count[0] += 1
        for source, first, rows in pieces:
            target = load_slot(number).at[pl.ds(first, rows)]
            pltpu.make_async_copy(source, target, ref.slot_sem.at[number % SLOTS]).start()
        return number

    def ready(number):
        slot = load_slot(number)
        pltpu.make_async_copy(slot, slot, ref.slot_sem.at[number % SLOTS]).wait()
        return slot

    def contract_rows(j):
        groups = n_rows // many
        return [(contract.at[j * groups + i], i * n_mem, n_mem) for i in range(groups)]

    mem_block = ref.memory.shape[1]
    memory, mem_rows = ref.memory, ref.mem_rows

    def memory_own():
        return pltpu.make_async_copy(
            memory.at[place.mem], mem_rows.at[span(place.mem, mem_block)], ref.mem_sem.at[0]
        )

    def memory_total():
        some = mem_rows.at[pl.ds(0, (n_mem - 1) * mem_block)]
        return remote(some, some, ref.mem_sem.at[1], ref.mem_sem.at[2], place.far(1))

    ref.small[...] = jnp.zeros_like(ref.small)
    for member in range(n_mem):

        @pl.when(place.mem == member)
        def _(member=member):
            lanes = slice(member * shard, (member + 1) * shard)
            ref.small[0:3, lanes] = ref.norm_gains[...].astype(jnp.float32)
            ref.small[3:6, lanes] = ref.norm_shifts[...].astype(jnp.float32)

    place.greet()
    memory_own().start()
    for step in range(1, n_mem):
        remote(
            memory.at[(place.mem + step) % n_mem],
            mem_rows.at[span(place.mem, mem_block)],
            ref.mem_sem.at[1],
            ref.mem_sem.at[2],
            place.far(step),
        ).start()

    actions, whole = [], []
    for part in range(len(parts)):
        found, time = gather.events(part)
        for hop, (at, action) in enumerate(found):
            actions.append((HOP + 10 * part + hop, at, action))
        whole.append(time)
    first_hops = [HOP, HOP + 10]
    for code, _, action in actions:
        if code in first_hops:
            action()
    actions = [item for item in actions if item[0] not in first_hops]

    self_bias, cross_bias, eye = ref.self_bias, ref.cross_bias, ref.eye
    own_row = ref.token_ids[pl.ds(place.mem, 1), :].astype(jnp.float32)
    mem_row = ref.memory_ids[pl.ds(place.mem, 1), :].astype(jnp.float32)
    key_place = lax.broadcasted_iota(jnp.int32, self_bias.shape, 0)
    query_place = lax.broadcasted_iota(jnp.int32, self_bias.shape, 1)
    own_wide = jnp.broadcast_to(own_row, self_bias.shape)
    mem_wide = jnp.broadcast_to(mem_row, (cross_bias.shape[1], cross_bias.shape[0]))
    same = (jnp.transpose(own_wide) == own_wide) & (key_place <= query_place)
    self_bias[...] = jnp.where(same, 0.0, NEG)
    cross_bias[...] = jnp.where(jnp.transpose(mem_wide) == own_row, 0.0, NEG)
    eye_row = lax.broadcasted_iota(jnp.int32, eye.shape, 0)
    eye_column = lax.broadcasted_iota(jnp.int32, eye.shape, 1)
    eye[...] = jnp.where(eye_row == eye_column, 1.0, 0.0).astype(eye.dtype)
    turn_by_lane(tokens, eye, turned.tokens)

    accumulated, other = ref.accumulated, ref.other
    hidden, slope, hidden_turned = ref.hidden, ref.slope, ref.hidden_turned

    def small_piece():
        blocks = ref.small_full
        for group in range(n_rows):
            total = None
            for member in range(n_mem):
                value = blocks[group, member]
                total = value if total is None else total + value
            gains[:, group * 128 : (group + 1) * 128] = total

    def query_piece(slot):
        times(tokens, slot, into(ref.query))

    def key_piece(slot):
        times(tokens, slot, into(ref.keys))

    pairs = width // (2 * HEAD_DIM)
    self_blocks = [
        (first, first + 128, max(first - DOC_LIMIT, 0), first + 128)
        for first in range(0, self_bias.shape[1], 128)
    ]
    cross_blocks = [(0, cross_bias.shape[1], 0, cross_bias.shape[0])]

    def value_piece(slot):
        times(tokens, slot, into(ref.values))

    def self_forward(first, last, slot):
        attention_forward(
            ref.query,
            ref.keys,
            ref.values,
            self_bias,
            self_blocks,
            eye,
            ref.attended,
            turned.attended,
            ref.self_lse,
            first,
            last,
        )

    def output_piece(slot):
        def store(columns, value):
            accumulated[:, columns] = ALPHA * tokens[:, columns].astype(jnp.float32) + value

        times(ref.attended, slot, store)

    def output_norm(slot):
        def use(rows, value):
            ref.first_low[rows, :] = value.astype(jnp.bfloat16)
            other[rows, :] = value

        norm_forward(accumulated, gains, 0, ref.unit1, ref.scale1, use)

    def cross_key_piece(slot):
        memory_own().wait()
        memory_total().wait_recv()
        times(mem_rows, slot, into(ref.cross_keys))
        turn_by_lane(mem_rows, eye, turned.memory)

    def cross_value_piece(slot):
        times(mem_rows, slot, into(ref.cross_values))
        turn_by_lane(ref.first_low, eye, turned.first)

    def cross_query_piece(slot):
        times(ref.first_low, slot, into(ref.cross_query))

    def cross_forward(first, last, slot):
        attention_forward(
            ref.cross_query,
            ref.cross_keys,
            ref.cross_values,
            cross_bias,
            cross_blocks,
            eye,
            ref.crossed,
            turned.crossed,
            ref.cross_lse,
            first,
            last,
        )

    def cross_output_piece(slot):
        def store(columns, value):
            accumulated[:, columns] = ALPHA * other[:, columns] + value

        times(ref.crossed, slot, store)

    def cross_output_norm(slot):
        def use(rows, value):
            ref.second_low[rows, :] = value.astype(jnp.bfloat16)
            other[rows, :] = value

        norm_forward(accumulated, gains, 1, ref.unit2, ref.scale2, use)

    def expand_piece(j, half, slot):
        def store(columns, value):
            there = pl.ds(pl.multiple_of(j * width + columns.start, TILE), columns.size)
            bell = 0.5 * (1.0 + lax.erf(value * math.sqrt(0.5)))
            density = jnp.exp(value * value * -0.5) * (1.0 / math.sqrt(2.0 * math.pi))
            hidden[:, there] = (value * bell).astype(hidden.dtype)
            slope[:, there] = (bell + value * density).astype(slope.dtype)

        times(ref.second_low, slot, store, half, 2)

    def expand_turn(j, slot):
        def keep(block, value):
            for index in range(value.shape[0] // shard):
                first = j * width + block * value.shape[0] + index * shard
                device, job = first // own_ff, first % own_ff // shard
                group, member = device // n_mem, device % n_mem
                at = group // 2 * n_mem * shard + member * shard
                hidden_turned[job, group % 2, at : at + shard, :] = value[
                    index * shard : (index + 1) * shard
                ]

        turn_blocks(hidden.at[:, pl.ds(j * width, width)], eye, keep)

    def contract_piece(j, slot):
        block = 2 * n_mem * shard
        for index in range(n_rows // 2):
            rows = pl.ds(index * n_mem * shard, n_mem * shard)
            both = jnp.concatenate([hidden_turned[j, 0, rows], hidden_turned[j, 1, rows]], axis=0)
            columns = pl.ds(index * block, block)
            low.branch[:, columns] = dot(eye[...], both, TURNED).astype(jnp.bfloat16)

        def store(columns, value):
            if j == 0:
                accumulated[:, columns] = ALPHA * other[:, columns] + value
            else:
                accumulated[:, columns] = accumulated[:, columns] + value

        times(low.branch, slot, store)

    quarters = [(pairs * at // 4, pairs * (at + 1) // 4) for at in range(4)]
    pieces = [
        [query_piece],
        [key_piece],
        [value_piece] + [functools.partial(self_forward, *quarter) for quarter in quarters],
        [output_piece, output_norm],
        [cross_key_piece],
        [cross_value_piece],
        [cross_query_piece] + [functools.partial(cross_forward, *quarter) for quarter in quarters],
        [cross_output_piece, cross_output_norm],
    ]
    for j in range(many):
        halves = [functools.partial(expand_piece, j, half) for half in range(2)]
        pieces.append(halves + [functools.partial(expand_turn, j)])
    pieces += [[functools.partial(contract_piece, j)] for j in range(many)]

    def arrive(part):
        gather.core_total(part).wait_recv()
        if part != SMALL_AT:
            keep(part - (part > SMALL_AT)).start()

    def use(part, index):
        if part == SMALL_AT:
            small_piece()
        else:
            number = part - (part > SMALL_AT)
            pieces[number][index](gather_slot(number))

    def settle(part):
        gather.sent(part)
        if part != SMALL_AT:
            keep(part - (part > SMALL_AT)).wait()

    last = 0.0
    for part, time in enumerate(whole):
        time = max(time, last + 0.5)
        actions.append((ARRIVE + part, time, functools.partial(arrive, part)))
        count_here = 1 if part == SMALL_AT else len(pieces[part - (part > SMALL_AT)])
        for index in range(count_here):
            at = time + 0.2 + 0.04 * index
            actions.append((USE + 10 * part + index, at, functools.partial(use, part, index)))
        actions.append((SETTLE + part, time + 0.45, functools.partial(settle, part)))
        last = time
    for action in planned(actions, FORWARD_PLAN):
        action()
    place.tell(ref.ready_sem)

    backward_sources, loads = [], []
    used = [0]

    def next_slot():
        slot = ready(loads[used[0]])
        used[0] += 1
        if len(loads) < len(backward_sources):
            loads.append(load(backward_sources[len(loads)]))
        return slot

    small_sums = ref.small_sums
    small_sums[...] = jnp.zeros_like(small_sums)
    def inner_piece(j):
        slot = next_slot()

        def store(columns, value):
            there = pl.ds(pl.multiple_of(j * width + columns.start, TILE), columns.size)
            slope[:, there] = (value * slope[:, there].astype(jnp.float32)).astype(slope.dtype)

        times_turned(low.third, slot, store)

    def second_piece(j):
        slot = next_slot()

        def store(columns, value):
            if j == 0:
                other[:, columns] = ALPHA * accumulated[:, columns] + value
            else:
                other[:, columns] = other[:, columns] + value

        times_turned(slope.at[:, pl.ds(j * width, width)], slot, store)

    def second_norm_piece():
        norm_backward(
            other, gains, 1, ref.unit2, ref.scale2, accumulated, low.second, small_sums
        )

    def cross_start_piece():
        times_turned(low.second, next_slot(), into(low.branch))

    def cross_piece(first, last):
        attention_backward(
            ref.cross_query,
            ref.cross_keys,
            ref.cross_values,
            cross_bias,
            cross_blocks,
            eye,
            ref.cross_lse,
            low.branch,
            low.cross_query,
            low.cross_key,
            low.cross_value,
            first,
            last,
        )

    def first_piece():
        def store(columns, value):
            other[:, columns] = ALPHA * accumulated[:, columns] + value

        times_turned(low.cross_query, next_slot(), store)

    def first_norm_piece():
        norm_backward(other, gains, 0, ref.unit1, ref.scale1, accumulated, low.first, small_sums)

    def self_start_piece():
        times_turned(low.first, next_slot(), into(low.branch))

    def self_piece(first, last):
        attention_backward(
            ref.query,
            ref.keys,
            ref.values,
            self_bias,
            self_blocks,
            eye,
            ref.self_lse,
            low.branch,
            low.query,
            low.key,
            low.value,
            first,
            last,
        )

    mem_out, mem_in = ref.mem_out, ref.mem_in

    def grad_own():
        return pltpu.make_async_copy(
            mem_out.at[span(place.mem, mem_block)], mem_in.at[place.mem], ref.mem_sem.at[3]
        )

    def grad_total():
        some = mem_in.at[pl.ds(0, n_mem - 1)]
        return remote(some, some, ref.mem_sem.at[4], ref.mem_sem.at[5], place.far(1))

    def memory_key_piece():
        times_turned(low.cross_key, next_slot(), into(other))

    def memory_value_piece():
        def store(columns, value):
            mem_out[:, columns] = (other[:, columns] + value).astype(mem_out.dtype)

        times_turned(low.cross_value, next_slot(), store)
        grad_own().start()
        for step in range(1, n_mem):
            remote(
                mem_out.at[span((place.mem + step) % n_mem, mem_block)],
                mem_in.at[place.mem],
                ref.mem_sem.at[4],
                ref.mem_sem.at[5],
                place.far(step),
            ).start()

    def input_piece(left, start):
        target = ref.input_grad

        def store(columns, value):
            if start:
                target[:, columns] = ALPHA * accumulated[:, columns] + value
            else:
                target[:, columns] = target[:, columns] + value

        times_turned(left, next_slot(), store)

    def memory_end_piece():
        grad_own().wait()
        grad_total().wait_recv()
        for member in range(n_mem):
            ref.memory_grad[member] = mem_in[member].astype(jnp.float32)

    halves = ((0, width // 2), (width // 2, width // 2))
    grads = ref.grads
    plans = []
    for j in range(many):
        for first, columns in halves if j == 0 else ((0, width),):
            target = ref.contract_grad.at[pl.ds(j * shard, shard), pl.ds(first, columns)]
            plans.append((hidden_turned.at[j], low.third, first, target))
    for j in range(many):
        target = ref.expand_grad.at[:, pl.ds(j * width, width)]
        plans.append((turned.second, slope, j * width, target))
    plans += [
        (turned.crossed, low.second, 0, grads[at_cross_output]),
        (turned.memory, low.cross_key, 0, grads[at_cross_key]),
        (turned.memory, low.cross_value, 0, grads[at_cross_value]),
        (turned.first, low.cross_query, 0, grads[at_cross_query]),
        (turned.attended, low.first, 0, grads[at_output]),
        (small_sums, None, 0, ref.small_total),
        (turned.tokens, low.query, 0, grads[at_query]),
        (turned.tokens, low.key, 0, grads[at_key]),
    ]
    for first, columns in halves:
        target = grads[at_value].at[:, pl.ds(first, columns)]
        plans.append((turned.tokens, low.value, first, target))
    jobs = [Job(*plan) for plan in plans]
    reduce = Reduce(place, jobs, ref.reduce_sems, pool, SimpleNamespace(**ref.little))

    inner = [functools.partial(inner_piece, j) for j in range(many)]
    second = [functools.partial(second_piece, j) for j in range(many)]
    base = many + 1
    def weight(index):
        return [(full[index], 0, n_rows)]

    turn = functools.partial(turn_by_lane, ref.second_low, eye, turned.second)
    crosses = [functools.partial(cross_piece, pair, pair + 1) for pair in range(pairs)]
    selves = [functools.partial(self_piece, pair, pair + 1) for pair in range(pairs)]
    work = [(base - 1.7 + j, inner[j], contract_rows(j)) for j in range(2)]
    work += [(base - 1.3, turn, None)]
    work += [(base - 1.7 + j, inner[j], contract_rows(j)) for j in range(2, many)]
    work += [(base - 0.3 + j, second[j], [(expand.at[j], 0, n_rows)]) for j in range(many)]
    base = 2 * many + 1
    work += [
        (base - 0.2, second_norm_piece, None),
        (base - 0.15, cross_start_piece, weight(at_cross_output)),
    ]
    work += [(base + 0.3 + 0.05 * pair, crosses[pair], None) for pair in range(pairs)]
    work += [
        (base + 1.3, first_piece, weight(at_cross_query)),
        (base + 1.31, first_norm_piece, None),
        (base + 1.7, self_start_piece, weight(at_output)),
    ]
    work += [(base + 2.3 + 0.14 * pair, selves[pair], None) for pair in range(pairs)]
    work += [
        (base + 3.7, memory_key_piece, weight(at_cross_key)),
        (base + 4.3, memory_value_piece, weight(at_cross_value)),
        (base + 4.7, functools.partial(input_piece, low.query, True), weight(at_query)),
        (base + 5.5, functools.partial(input_piece, low.key, False), weight(at_key)),
        (base + 6.5, functools.partial(input_piece, low.value, False), weight(at_value)),
        (base + 8.5, memory_end_piece, None),
    ]
    actions = [(WORK + index, at, item) for index, (at, *item) in enumerate(work)]
    for number in range(len(jobs)):
        found = reduce.events(number)
        actions.append((CORE + number, found[0][0], found[0][1:]))
        actions.append((LANE + number, found[1][0], found[1][1:]))
        for stage, (at, action) in enumerate(found[2:]):
            actions.append((STAGE + 10 * number + stage, at, (action,)))
    ordered = planned(actions, BACKWARD_PLAN)
    backward_sources += [item[1] for item in ordered if len(item) > 1 and item[1] is not None]
    loads += [load(backward_sources[0]), load(backward_sources[1])]
    norm_both(
        accumulated, ref.out_grad, gains, 2, ref.result, accumulated, low.third, small_sums
    )

    place.hear(ref.ready_sem)
    for item in ordered:
        item[0]()

    total = ref.small_total[...]
    own = jnp.zeros((8, shard), jnp.float32)
    for member in range(n_mem):
        here = jnp.where(place.mem == member, 1.0, 0.0)
        own = own + here * total[:, member * shard : (member + 1) * shard]
    ref.gains_grad[...] = own[0:3]
    ref.shifts_grad[...] = own[3:6]
    reduce.finish()
    memory_total().wait_send()
    grad_total().wait_send()


SMALL_AT = 2
DOC_LIMIT = 64
HOP, ARRIVE, USE, SETTLE, CORE, LANE, STAGE, WORK = range(1000, 9000, 1000)
FORWARD_PLAN = (
    1001, 1011, 1020, 1002, 1003, 1012, 1030, 1040, 1021, 1004, 1013, 1031, 1041, 1014, 1032, 1050,
    1033, 1005, 1060, 1042, 1070, 2000, 1043, 1015, 1051, 1022, 1080, 1034, 1061, 1044, 1052, 3000,
    2001, 4000, 1023, 3010, 2002, 1071, 1053, 3020, 1062, 1035, 1072, 1081, 1045, 2003, 4001, 1090,
    1073, 3030, 1063, 1054, 3031, 2004, 1064, 1091, 3032, 4002, 1082, 3033, 3034, 1092, 1055, 4003,
    1100, 1110, 3040, 1093, 3041, 1074, 1065, 4004, 1083, 1101, 2005, 1111, 3050, 4005, 1120, 1084,
    1102, 2006, 1130, 1094, 1075, 3060, 4006, 2007, 1121, 1085, 3070, 3071, 1112, 1103, 1113, 3072,
    1122, 1131, 1104, 3073, 2008, 3074, 4007, 1140, 1150, 1114, 1095, 1123, 1132, 3080, 1141, 3081,
    1105, 1133, 1160, 1151, 2009, 1124, 3090, 3091, 4008, 2010, 1115, 1152, 1142, 1134, 3092, 4009,
    3100, 3101, 1143, 3102, 4010, 1161, 1153, 2011, 1144, 3110, 1125, 3111, 1135, 1154, 1162, 3112,
    1163, 2012, 3120, 3121, 1164, 1145, 2013, 3122, 3130, 1155, 4011, 4012, 2014, 4013, 3140, 1165,
    2015, 4014, 3150, 2016, 3160, 4015, 4016,
)
BACKWARD_PLAN = (
    5000, 6000, 5001, 8003, 6001, 5002, 7000, 8000, 7010, 6002, 5003, 8005, 7001, 8001, 6003, 8002,
    5004, 7020, 7002, 7011, 8004, 6004, 5005, 7021, 7030, 7012, 8006, 6005, 5006, 8007, 7040, 6006,
    7022, 5007, 7031, 8008, 8009, 6007, 8010, 5008, 7041, 8011, 7032, 7050, 7060, 8012, 6008, 8013,
    5009, 7051, 8014, 7042, 8015, 8016, 7070, 8017, 8018, 6009, 5010, 7061, 8019, 8020, 7052, 7080,
    6010, 5011, 8021, 7071, 8022, 7090, 8023, 6011, 5012, 7062, 8024, 8025, 7072, 8026, 7081, 6012,
    5013, 7091, 8027, 8028, 7100, 7110, 8029, 8032, 6013, 7082, 7101, 5014, 7120, 6014, 5015, 8030,
    7092, 8033, 7111, 7130, 7102, 6015, 5016, 7121, 8034, 6016, 7112, 7131, 7140, 7150, 5017, 7122,
    8031, 7132, 7141, 7160, 6017, 7151, 5018, 7161, 6018, 7142, 7170, 7152, 7180, 8035, 7171, 7162,
    7181, 7172, 7182,
)


def planned(actions, plan):
    codes = {code for code, _, _ in actions}
    if codes == set(plan):
        at = {code: number for number, code in enumerate(plan)}
        return [item for code, _, item in sorted(actions, key=lambda action: at[action[0]])]
    return [item for _, _, item in sorted(actions, key=lambda action: action[1])]


def copy_kernel(count, *refs):
    for source, target in zip(refs[:count], refs[count:]):
        target[...] = source[...]


def copied(values):
    near = pl.BlockSpec(memory_space=pltpu.VMEM)
    return pl.pallas_call(
        functools.partial(copy_kernel, len(values)),
        out_shape=[jax.ShapeDtypeStruct(value.shape, value.dtype) for value in values],
        in_specs=[near] * len(values),
        out_specs=[near] * len(values),
        compiler_params=pltpu.CompilerParams(vmem_limit_bytes=VMEM_LIMIT),
        name="results",
    )(*values)


def fused(n_rows, n_mem, ins):
    tokens, memory, squares = ins["tokens"], ins["memory"], ins["squares"]
    expand, contract = ins["expand"], ins["contract"]
    tokens_here, width = tokens.shape
    ff = expand.shape[1]
    shard = squares[0].shape[0]
    mem_tokens = memory.shape[0] * memory.shape[1]
    digits, half, many = (n_rows // 2).bit_length() - 1, n_rows // 2, ff // width
    pairs = width // (2 * HEAD_DIM)
    low, high = jnp.bfloat16, jnp.float32
    n_parts = 1 + SQUARES + 2 * many
    n_jobs = n_parts + 2
    dma, vmem = pltpu.SemaphoreType.DMA, pltpu.VMEM
    anywhere, near = pl.BlockSpec(memory_space=pl.ANY), pl.BlockSpec(memory_space=pltpu.VMEM)

    far_ins = dict(memory=memory)
    in_specs = {
        name: jax.tree.map(lambda _: anywhere if name in far_ins else near, value)
        for name, value in ins.items()
    }

    def out(shape, dtype=high):
        return jax.ShapeDtypeStruct(shape, dtype)

    outs = dict(
        result=out(tokens.shape),
        input_grad=out(tokens.shape),
        memory_grad=out(memory.shape),
        grads=[out(item.shape) for item in squares],
        expand_grad=out(expand.shape),
        contract_grad=out(contract.shape),
        gains_grad=out((3, shard)),
        shifts_grad=out((3, shard)),
    )
    far_outs = dict(
        full=[out((n_rows, n_mem, shard, width), low)] * SQUARES,
        expand_full=out((many, n_rows, n_mem, shard, width), low),
        contract_full=out((n_rows, n_mem, many, shard, width), low),
    )
    out_specs = jax.tree.map(lambda _: near, outs)
    out_specs.update(jax.tree.map(lambda _: anywhere, far_outs))
    outs.update(far_outs)

    def token_rows(dtype):
        return vmem((tokens_here, width), dtype)

    def memory_rows(dtype):
        return vmem((mem_tokens, width), dtype)

    tiny = (8, 128)

    counts = [half >> (stage + 1) for stage in range(digits)]
    units = (OUT_SLOTS + LANE_SLOTS + CORE_RING) * half + RING
    for stage, number in enumerate(counts):
        units += (SUM_SLOTS + (RING if stage else FIRST_RING)) * number
    units = max(units + SLOTS * n_rows, GATHER_SLOTS * n_rows)
    little = dict(
        lanes=vmem((half,) + tiny, high),
        core_in=vmem((half,) + tiny, high),
        sums=[vmem((number,) + tiny, high) for number in counts],
        arrived=[vmem((number,) + tiny, high) for number in counts]
        + [vmem((n_mem - 1,) + tiny, high)],
    )
    left = vmem((2, width // 2, tokens_here), low)
    scratch = dict(
        small=vmem(tiny, high),
        small_full=vmem((n_rows, n_mem) + tiny, high),
        small_total=vmem(tiny, high),
        pool=vmem((units, n_mem, shard, width), low),
        slot_sem=dma((SLOTS,)),
        keep_sem=dma((n_parts - 1,)),
        ready_sem=pltpu.SemaphoreType.REGULAR,
        mem_sem=dma((6,)),
        gather_sems=[
            dma(shape + (n_parts,))
            for shape in ((), (), (), (digits,), (digits,), (), ())
            + ((2 * (n_mem - 1),), (2 * (n_mem - 1),))
        ],
        reduce_sems=[dma(shape + (n_jobs,)) for shape in ((), (), (digits + 1,), (digits + 1,))],
        gains=vmem((8, width), high),
        query=token_rows(low),
        keys=token_rows(low),
        values=token_rows(low),
        attended=token_rows(low),
        first_low=token_rows(low),
        second_low=token_rows(low),
        cross_query=token_rows(low),
        crossed=token_rows(low),
        cross_keys=memory_rows(low),
        cross_values=memory_rows(low),
        mem_rows=memory_rows(low),
        mem_out=memory_rows(low),
        mem_in=vmem(memory.shape, low),
        unit1=token_rows(high),
        unit2=token_rows(high),
        accumulated=token_rows(high),
        other=token_rows(high),
        scale1=vmem((tokens_here, 1), high),
        scale2=vmem((tokens_here, 1), high),
        self_bias=vmem((tokens_here, tokens_here), high),
        cross_bias=vmem((mem_tokens, tokens_here), high),
        self_lse=vmem((pairs, 2, tokens_here), high),
        cross_lse=vmem((pairs, 2, tokens_here), high),
        eye=vmem((TILE, TILE), low),
        hidden=vmem((tokens_here, ff), low),
        slope=vmem((tokens_here, ff), low),
        hidden_turned=vmem((many, 2, width // 2, tokens_here), low),
        turned=dict(
            tokens=left, attended=left, first=left, memory=left, crossed=left, second=left
        ),
        low=dict(
            third=token_rows(low),
            second=token_rows(low),
            first=token_rows(low),
            branch=token_rows(low),
            cross_query=token_rows(low),
            cross_key=memory_rows(low),
            cross_value=memory_rows(low),
            query=token_rows(low),
            key=token_rows(low),
            value=token_rows(low),
        ),
        small_sums=vmem((2, half) + tiny, high),
        little=little,
    )
    in_values, in_tree = jax.tree.flatten(ins)
    out_shapes, out_tree = jax.tree.flatten(outs)
    scratch_shapes, scratch_tree = jax.tree.flatten(scratch)
    places = jax.tree.unflatten(in_tree, range(len(in_values)))
    at = len(in_values)
    places.update(jax.tree.unflatten(out_tree, range(at, at + len(out_shapes))))
    at += len(out_shapes)
    places.update(jax.tree.unflatten(scratch_tree, range(at, at + len(scratch_shapes))))
    values = pl.pallas_call(
        functools.partial(layer_kernel, places, (n_rows, n_mem, width, ff, shard)),
        out_shape=out_shapes,
        in_specs=jax.tree.leaves(in_specs),
        out_specs=jax.tree.leaves(out_specs),
        scratch_shapes=scratch_shapes,
        compiler_params=pltpu.CompilerParams(
            collective_id=0, has_side_effects=True, vmem_limit_bytes=VMEM_LIMIT
        ),
        name="layer",
    )(*in_values)
    found = jax.tree.unflatten(out_tree, values)
    for name in far_outs:
        del found[name]
    return found


def local(n_rows, n_mem, *args):
    (
        tokens,
        memory,
        token_ids,
        memory_ids,
        out_grad,
        self_query,
        self_key,
        self_value,
        self_output,
        cross_query,
        cross_key,
        cross_value,
        cross_output,
        expand_weight,
        contract_weight,
        norm_gains,
        norm_shifts,
    ) = args
    shard, width = self_query.shape
    suits = width == 128 * n_rows and shard % 16 == 0 and tokens.shape[0] == 1
    suits = suits and tokens.shape[1] == TILE and expand_weight.shape[1] == n_mem * width
    if not suits or n_rows < 4 or n_rows & (n_rows - 1) or n_mem < 2:
        return plain(*args)
    found = fused(
        n_rows,
        n_mem,
        dict(
            tokens=tokens[0],
            memory=memory,
            token_ids=token_ids,
            memory_ids=memory_ids,
            out_grad=out_grad[0],
            squares=[
                self_query,
                self_key,
                self_value,
                self_output,
                cross_query,
                cross_key,
                cross_value,
                cross_output,
            ],
            expand=expand_weight,
            contract=contract_weight,
            norm_gains=norm_gains,
            norm_shifts=norm_shifts,
        ),
    )
    values, tree = jax.tree.flatten(found)
    found = SimpleNamespace(**jax.tree.unflatten(tree, copied(values)))
    return (
        found.result[None],
        found.input_grad[None],
        found.memory_grad,
        *found.grads,
        found.expand_grad,
        found.contract_grad,
        found.gains_grad,
        found.shifts_grad,
    )


def solution(mesh):
    in_specs = (
        P(("rows", "mem"), None, None),
        P("rows", "mem", None),
        P("rows", None),
        P("rows", None),
        P(("rows", "mem"), None, None),
        P(("rows", "mem"), None),
        P(("rows", "mem"), None),
        P(("rows", "mem"), None),
        P(("rows", "mem"), None),
        P(("rows", "mem"), None),
        P(("rows", "mem"), None),
        P(("rows", "mem"), None),
        P(("rows", "mem"), None),
        P(("rows", "mem"), None),
        P(("rows", "mem"), None),
        P(None, ("rows", "mem")),
        P(None, ("rows", "mem")),
    )
    out_specs = (
        P(("rows", "mem"), None, None),
        P(("rows", "mem"), None, None),
        P("rows", "mem", None),
        P(("rows", "mem"), None),
        P(("rows", "mem"), None),
        P(("rows", "mem"), None),
        P(("rows", "mem"), None),
        P(("rows", "mem"), None),
        P(("rows", "mem"), None),
        P(("rows", "mem"), None),
        P(("rows", "mem"), None),
        P(("rows", "mem"), None),
        P(("rows", "mem"), None),
        P(None, ("rows", "mem")),
        P(None, ("rows", "mem")),
    )
    layer = functools.partial(local, mesh.shape["rows"], mesh.shape["mem"])
    return jax.shard_map(layer, mesh=mesh, in_specs=in_specs, out_specs=out_specs, check_vma=False)
```

```python
import functools
import math
from types import SimpleNamespace

import jax
import jax.numpy as jnp
from jax import lax
from jax.experimental import pallas as pl
from jax.experimental.pallas import tpu as pltpu
from jax.sharding import PartitionSpec as P

MESH = pl.DeviceIdType.MESH

HEADS = 16
HEAD_DIM = 64


ALPHA = 4.16
EPS = 1e-05
SCALE = 0.125
NEG = -1e30


def layer_norm(hidden_activation, gain, shift):
    centre = hidden_activation - jnp.mean(hidden_activation, axis=-1, keepdims=True)
    spread = jnp.mean(centre * centre, axis=-1, keepdims=True)
    return centre * lax.rsqrt(spread + EPS) * gain + shift


def gelu_exact(value):
    return jax.nn.gelu(value, approximate=False)


def product(left, right):
    return jnp.dot(left, right, preferred_element_type=jnp.float32)


def split_heads(matrix):
    return matrix.reshape(matrix.shape[0], matrix.shape[1] // HEAD_DIM, HEAD_DIM)


def grouped(matrix):
    return jnp.moveaxis(matrix.reshape(matrix.shape[0], HEADS // 4, 4 * HEAD_DIM), 1, 0)


def ungrouped(stack):
    return jnp.moveaxis(stack, 0, 1).reshape(stack.shape[1], stack.shape[0] * stack.shape[2])


def row_map(function, items):
    return lax.map(lambda entry: function(*entry), items)


def score_block(query, keys, allowed):
    raw = jnp.einsum(
        "khe,qhe->hkq", split_heads(keys), split_heads(query), preferred_element_type=jnp.float32
    )
    return jnp.where(allowed[None], raw * SCALE, NEG)


def attend_probs(query, keys, allowed, lse):
    scores = score_block(query, keys, allowed)
    return jnp.where(allowed[None], jnp.exp(scores - lse[:, None, :]), 0.0)


def attend_forward(query, keys, values, allowed):
    scores = score_block(query, keys, allowed)
    top = jnp.max(scores, axis=1)
    weight = jnp.where(allowed[None], jnp.exp(scores - top[:, None, :]), 0.0)
    total = jnp.sum(weight, axis=1)
    probs = (weight / total[:, None, :]).astype(jnp.bfloat16)
    mixed = jnp.einsum(
        "hkq,khe->qhe", probs, split_heads(values), preferred_element_type=jnp.float32
    )
    return (mixed.reshape(query.shape), top + jnp.log(total))


def value_pull(grad, values):
    return jnp.einsum(
        "qhe,khe->hkq", split_heads(grad), split_heads(values), preferred_element_type=jnp.float32
    )


def score_grads(probs, pulled, inner):
    return (probs * (pulled - inner[:, None, :]) * SCALE).astype(jnp.bfloat16)


def query_from(score_grad, keys, shape):
    moved = jnp.einsum(
        "hkq,khe->qhe", score_grad, split_heads(keys), preferred_element_type=jnp.float32
    )
    return moved.reshape(shape)


def key_from(score_grad, query, shape):
    moved = jnp.einsum(
        "hkq,qhe->khe", score_grad, split_heads(query), preferred_element_type=jnp.float32
    )
    return moved.reshape(shape)


def value_from(probs, grad, values):
    moved = jnp.einsum(
        "hkq,qhe->khe",
        probs.astype(jnp.bfloat16),
        split_heads(grad),
        preferred_element_type=jnp.float32,
    )
    return moved.reshape(values.shape)


def local_forward(query, keys, values, allowed):

    def one_group(items):
        return attend_forward(items[0], items[1], items[2], allowed)

    mixed, lse = lax.map(one_group, (grouped(query), grouped(keys), grouped(values)))
    return (ungrouped(mixed), lse)


def local_backward(query, keys, values, allowed, lse, grad):

    def one_group(items):
        part_query, part_keys, part_values, part_lse, part_grad = items
        probs = attend_probs(part_query, part_keys, allowed, part_lse)
        pulled = value_pull(part_grad, part_values)
        inner = jnp.sum(probs * pulled, axis=1)
        score_grad = score_grads(probs, pulled, inner)
        return (
            query_from(score_grad, part_keys, part_query.shape),
            key_from(score_grad, part_query, part_keys.shape),
            value_from(probs, part_grad, part_values),
        )

    parts = lax.map(one_group, (grouped(query), grouped(keys), grouped(values), lse, grouped(grad)))
    return (ungrouped(parts[0]), ungrouped(parts[1]), ungrouped(parts[2]))


def plain(
    tokens,
    memory,
    token_ids,
    memory_ids,
    out_grad,
    self_query,
    self_key,
    self_value,
    self_output,
    cross_query,
    cross_key,
    cross_value,
    cross_output,
    expand_weight,
    contract_weight,
    norm_gains,
    norm_shifts,
):
    full = (
        lax.all_gather(self_query, ("rows", "mem"), axis=0, tiled=True),
        lax.all_gather(self_key, ("rows", "mem"), axis=0, tiled=True),
        lax.all_gather(self_value, ("rows", "mem"), axis=0, tiled=True),
        lax.all_gather(self_output, ("rows", "mem"), axis=0, tiled=True),
        lax.all_gather(cross_query, ("rows", "mem"), axis=0, tiled=True),
        lax.all_gather(cross_key, ("rows", "mem"), axis=0, tiled=True),
        lax.all_gather(cross_value, ("rows", "mem"), axis=0, tiled=True),
        lax.all_gather(cross_output, ("rows", "mem"), axis=0, tiled=True),
        lax.all_gather(expand_weight, ("rows", "mem"), axis=0, tiled=True),
        lax.all_gather(contract_weight, ("rows", "mem"), axis=0, tiled=True),
        lax.all_gather(jnp.transpose(norm_gains), ("rows", "mem"), axis=0, tiled=True),
        lax.all_gather(jnp.transpose(norm_shifts), ("rows", "mem"), axis=0, tiled=True),
    )
    (
        self_attention_query,
        decoder_match_label,
        self_attention_value,
        self_attention_output,
        encoder_lookup_probe,
        key_cross,
        value_cross,
        cross_attention_output,
        up_projection,
        narrowing_matrix,
        gain_cols,
        shift_cols,
    ) = full
    gain_rows = jnp.transpose(gain_cols).astype(jnp.float32)
    shift_rows = jnp.transpose(shift_cols).astype(jnp.float32)
    rows_here = tokens.shape[0]
    member = lax.axis_index("mem")
    own_ids = lax.dynamic_slice_in_dim(token_ids, member * rows_here, rows_here, 0)
    positions = jnp.arange(tokens.shape[1], dtype=jnp.int32)
    self_allowed = (own_ids[:, :, None] == own_ids[:, None, :]) & (
        positions[:, None] <= positions[None, :]
    )[None]
    query = product(tokens, self_attention_query).astype(jnp.bfloat16)
    keys = product(tokens, decoder_match_label).astype(jnp.bfloat16)
    values = product(tokens, self_attention_value).astype(jnp.bfloat16)
    self_mixed, self_lse = row_map(local_forward, (query, keys, values, self_allowed))
    attention_result = self_mixed.astype(jnp.bfloat16)
    first, first_back = jax.vjp(
        layer_norm,
        ALPHA * tokens.astype(jnp.float32) + product(attention_result, self_attention_output),
        gain_rows[0],
        shift_rows[0],
    )
    first_reduced = first.astype(jnp.bfloat16)
    cross_queries = product(first_reduced, encoder_lookup_probe).astype(jnp.bfloat16)
    memory_rows = lax.all_to_all(memory, "mem", split_axis=0, concat_axis=1, tiled=True)
    row_ids = lax.dynamic_slice_in_dim(memory_ids, member * rows_here, rows_here, 0)
    cross_allowed = row_ids[:, :, None] == own_ids[:, None, :]
    cross_keys = product(memory_rows, key_cross).astype(jnp.bfloat16)
    cross_values = product(memory_rows, value_cross).astype(jnp.bfloat16)
    cross_mixed, cross_lse = row_map(
        local_forward, (cross_queries, cross_keys, cross_values, cross_allowed)
    )
    cross_attention_result = cross_mixed.astype(jnp.bfloat16)
    second, second_back = jax.vjp(
        layer_norm,
        ALPHA * first + product(cross_attention_result, cross_attention_output),
        gain_rows[1],
        shift_rows[1],
    )
    second_reduced = second.astype(jnp.bfloat16)
    hidden_value, gelu_back = jax.vjp(gelu_exact, product(second_reduced, up_projection))
    hidden_activation = hidden_value.astype(jnp.bfloat16)
    result, third_back = jax.vjp(
        layer_norm,
        ALPHA * second + product(hidden_activation, narrowing_matrix),
        gain_rows[2],
        shift_rows[2],
    )
    third_grad, gain_three, shift_three = third_back(out_grad.astype(jnp.float32))
    feedforward_gradient = third_grad.astype(jnp.bfloat16)
    down_projection_gradient = jnp.einsum(
        "ehj,ehc->jc", hidden_activation, feedforward_gradient, preferred_element_type=jnp.float32
    )
    (inner_grad,) = gelu_back(
        jnp.einsum(
            "hpu,ku->hpk",
            feedforward_gradient,
            narrowing_matrix,
            preferred_element_type=jnp.float32,
        )
    )
    inner_reduced = inner_grad.astype(jnp.bfloat16)
    expand_grad = jnp.einsum(
        "iqg,iqe->ge", second_reduced, inner_reduced, preferred_element_type=jnp.float32
    )
    second_total = ALPHA * third_grad + jnp.einsum(
        "iwm,fm->iwf", inner_reduced, up_projection, preferred_element_type=jnp.float32
    )
    second_grad, gain_two, shift_two = second_back(second_total)
    cross_branch_gradient = second_grad.astype(jnp.bfloat16)
    output_cross_grad = jnp.einsum(
        "nhb,nhc->bc",
        cross_attention_result,
        cross_branch_gradient,
        preferred_element_type=jnp.float32,
    )
    crossed_grad = jnp.einsum(
        "qwp,up->qwu",
        cross_branch_gradient,
        cross_attention_output,
        preferred_element_type=jnp.float32,
    ).astype(jnp.bfloat16)
    query_grads, key_grads, value_grads = row_map(
        local_backward,
        (cross_queries, cross_keys, cross_values, cross_allowed, cross_lse, crossed_grad),
    )
    key_low = key_grads.astype(jnp.bfloat16)
    value_low = value_grads.astype(jnp.bfloat16)
    row_grad = jnp.einsum(
        "sme,de->smd", key_low, key_cross, preferred_element_type=jnp.float32
    ) + jnp.einsum("sme,de->smd", value_low, value_cross, preferred_element_type=jnp.float32)
    key_cross_grad = jnp.einsum(
        "smd,sme->de", memory_rows, key_low, preferred_element_type=jnp.float32
    )
    value_cross_grad = jnp.einsum(
        "smd,sme->de", memory_rows, value_low, preferred_element_type=jnp.float32
    )
    memory_grad = lax.all_to_all(
        row_grad.astype(jnp.bfloat16), "mem", split_axis=1, concat_axis=0, tiled=True
    ).astype(row_grad.dtype)
    probe_lowered_precision = query_grads.astype(jnp.bfloat16)
    query_cross_grad = jnp.einsum(
        "nhb,nhc->bc", first_reduced, probe_lowered_precision, preferred_element_type=jnp.float32
    )
    first_total = ALPHA * second_grad + jnp.einsum(
        "qwp,up->qwu",
        probe_lowered_precision,
        encoder_lookup_probe,
        preferred_element_type=jnp.float32,
    )
    first_grad, gain_one, shift_one = first_back(first_total)
    self_branch_gradient = first_grad.astype(jnp.bfloat16)
    output_self_grad = jnp.einsum(
        "nhb,nhc->bc", attention_result, self_branch_gradient, preferred_element_type=jnp.float32
    )
    attended_grad = jnp.einsum(
        "qwp,up->qwu",
        self_branch_gradient,
        self_attention_output,
        preferred_element_type=jnp.float32,
    ).astype(jnp.bfloat16)
    self_query_reduced, decoder_label_lowered, self_value_reduced = row_map(
        local_backward, (query, keys, values, self_allowed, self_lse, attended_grad)
    )
    self_query_reduced = self_query_reduced.astype(jnp.bfloat16)
    decoder_label_lowered = decoder_label_lowered.astype(jnp.bfloat16)
    self_value_reduced = self_value_reduced.astype(jnp.bfloat16)
    query_self_grad = jnp.einsum(
        "nhb,nhc->bc", tokens, self_query_reduced, preferred_element_type=jnp.float32
    )
    key_self_grad = jnp.einsum(
        "nhb,nhc->bc", tokens, decoder_label_lowered, preferred_element_type=jnp.float32
    )
    value_self_grad = jnp.einsum(
        "nhb,nhc->bc", tokens, self_value_reduced, preferred_element_type=jnp.float32
    )
    input_grad = (
        ALPHA * first_grad
        + jnp.einsum(
            "qwp,up->qwu",
            self_query_reduced,
            self_attention_query,
            preferred_element_type=jnp.float32,
        )
        + jnp.einsum(
            "qwp,up->qwu",
            decoder_label_lowered,
            decoder_match_label,
            preferred_element_type=jnp.float32,
        )
        + jnp.einsum(
            "qwp,up->qwu",
            self_value_reduced,
            self_attention_value,
            preferred_element_type=jnp.float32,
        )
    )
    gain_grad = jnp.stack([gain_one, gain_two, gain_three], axis=1)
    shift_grad = jnp.stack([shift_one, shift_two, shift_three], axis=1)
    sums = (
        lax.psum_scatter(query_self_grad, ("rows", "mem"), scatter_dimension=0, tiled=True),
        lax.psum_scatter(key_self_grad, ("rows", "mem"), scatter_dimension=0, tiled=True),
        lax.psum_scatter(value_self_grad, ("rows", "mem"), scatter_dimension=0, tiled=True),
        lax.psum_scatter(output_self_grad, ("rows", "mem"), scatter_dimension=0, tiled=True),
        lax.psum_scatter(query_cross_grad, ("rows", "mem"), scatter_dimension=0, tiled=True),
        lax.psum_scatter(key_cross_grad, ("rows", "mem"), scatter_dimension=0, tiled=True),
        lax.psum_scatter(value_cross_grad, ("rows", "mem"), scatter_dimension=0, tiled=True),
        lax.psum_scatter(output_cross_grad, ("rows", "mem"), scatter_dimension=0, tiled=True),
        lax.psum_scatter(expand_grad, ("rows", "mem"), scatter_dimension=0, tiled=True),
        lax.psum_scatter(
            down_projection_gradient, ("rows", "mem"), scatter_dimension=0, tiled=True
        ),
        lax.psum_scatter(gain_grad, ("rows", "mem"), scatter_dimension=0, tiled=True),
        lax.psum_scatter(shift_grad, ("rows", "mem"), scatter_dimension=0, tiled=True),
    )
    return (
        result,
        input_grad,
        memory_grad,
        sums[0],
        sums[1],
        sums[2],
        sums[3],
        sums[4],
        sums[5],
        sums[6],
        sums[7],
        sums[8],
        sums[9],
        jnp.transpose(sums[10]),
        jnp.transpose(sums[11]),
    )


ALL = slice(None)
TILE = 256
SLOTS = 3
GATHER_SLOTS = 10
VMEM_LIMIT = 61 * 1024 * 1024


def flip(index, unit):
    return index + unit * (1 - 2 * ((index // unit) % 2))


def span(index, size):
    return pl.ds(pl.multiple_of(index * size, size), size)


class Place:
    def __init__(self, n_rows, n_mem):
        self.n_rows, self.n_mem = n_rows, n_mem
        self.digits = (n_rows // 2).bit_length() - 1
        self.row = lax.axis_index("rows")
        self.mem = lax.axis_index("mem")
        self.lane = self.row % 2

    def turn(self, index, stage):
        rising, falling = 2 << stage, 2 << (self.digits - 1 - stage)
        return flip(index, rising) * (1 - self.lane) + flip(index, falling) * self.lane

    def sibling(self):
        return (flip(self.row, 1), self.mem)

    def partner(self, stage):
        return (self.turn(self.row, stage), self.mem)

    def far(self, step):
        return (self.row, (self.mem + step) % self.n_mem)

    def others(self):
        found = [self.far(step) for step in range(1, self.n_mem)]
        found += [self.partner(stage) for stage in range(self.digits)]
        return found + [self.sibling()]

    def tell(self, semaphore):
        for other in self.others():
            pl.semaphore_signal(semaphore, inc=1, device_id=other, device_id_type=MESH)

    def hear(self, semaphore):
        pl.semaphore_wait(semaphore, len(self.others()))

    def greet(self):
        self.tell(pltpu.get_barrier_semaphore())
        self.hear(pltpu.get_barrier_semaphore())


def remote(source, target, send_sem, recv_sem, device):
    return pltpu.make_async_remote_copy(
        src_ref=source,
        dst_ref=target,
        send_sem=send_sem,
        recv_sem=recv_sem,
        device_id=device,
        device_id_type=MESH,
    )


def waits(total):
    return (lambda: total().wait_recv(), lambda: total().wait_send())


class Part:
    def __init__(self, source, target, near=0, straight=False):
        self.source, self.target = source, target
        self.near, self.straight = near, straight


class Gather:
    def __init__(self, place, parts, sems):
        self.place, self.parts = place, parts
        (
            self.own_sem,
            self.far_send,
            self.far_recv,
            self.plane_send,
            self.plane_recv,
            self.core_send,
            self.core_recv,
            self.line_send,
            self.line_recv,
        ) = sems

    def group(self, number, group):
        return self.parts[number].target.at[group]

    def one(self, number, group, member):
        return self.parts[number].target.at[group, member]

    def shard(self, number):
        return self.parts[number].source

    def mine(self, number):
        return self.one(number, self.place.row, self.place.mem)

    def own(self, number):
        return pltpu.make_async_copy(self.shard(number), self.mine(number), self.own_sem.at[number])

    def held(self, stage):
        groups = [self.place.row]
        for before in range(stage):
            groups = groups + [self.place.turn(group, before) for group in groups]
        return groups

    def far_total(self, number):
        part = self.parts[number]
        some = part.target.at[pl.ds(0, 1 << part.near), pl.ds(0, self.place.n_mem - 1)]
        return remote(
            some, some, self.far_send.at[number], self.far_recv.at[number], self.place.far(1)
        )

    def far_hop(self, number, first):
        place = self.place
        for group in self.held(self.parts[number].near):
            target = self.one(number, group, place.mem)
            source = self.shard(number) if first else target
            for step in range(1, place.n_mem):
                remote(
                    source,
                    target,
                    self.far_send.at[number],
                    self.far_recv.at[number],
                    place.far(step),
                ).start()

    def sides(self, step):
        mem, n_mem = self.place.mem, self.place.n_mem
        return (
            ((mem - step >= 0) & (mem + 1 < n_mem), mem - step, 1, mem - 1 - step >= 0),
            ((mem + step < n_mem) & (mem >= 1), mem + step, n_mem - 1, mem + 1 + step < n_mem),
        )

    def line_total(self, number, step, side):
        part, at = self.parts[number], 2 * step + side
        some = part.target.at[pl.ds(0, 1 << part.near), 0]
        sems = (self.line_send.at[at, number], self.line_recv.at[at, number])
        return remote(some, some, *sems, self.place.far(1))

    def line_arrived(self, number, step):
        for side, (_, _, _, receives) in enumerate(self.sides(step)):

            @pl.when(receives)
            def _(side=side):
                self.line_total(number, step, side).wait_recv()

    def line_sent(self, number, step):
        for side, (sends, _, _, _) in enumerate(self.sides(step)):

            @pl.when(sends)
            def _(side=side):
                self.line_total(number, step, side).wait_send()

    def line_hop(self, number, step, first):
        place = self.place
        for side, (sends, member, towards, _) in enumerate(self.sides(step)):
            member = (member + place.n_mem) % place.n_mem

            @pl.when(sends)
            def _(side=side, member=member, towards=towards):
                for group in self.held(self.parts[number].near):
                    target = self.one(number, group, member)
                    remote(
                        self.shard(number) if first else target,
                        target,
                        self.line_send.at[2 * step + side, number],
                        self.line_recv.at[2 * step + side, number],
                        place.far(towards),
                    ).start()

    def plane_total(self, number, stage):
        part = self.parts[number]
        some = part.target.at[pl.ds(0, 1 << stage)]
        if stage < part.near:
            some = part.target.at[pl.ds(0, 1 << stage), 0]
        return remote(
            some,
            some,
            self.plane_send.at[stage, number],
            self.plane_recv.at[stage, number],
            self.place.partner(stage),
        )

    def plane_hop(self, number, stage, first):
        for group in self.held(stage):
            if stage < self.parts[number].near:
                target = self.one(number, group, self.place.mem)
            else:
                target = self.group(number, group)
            remote(
                self.shard(number) if first else target,
                target,
                self.plane_send.at[stage, number],
                self.plane_recv.at[stage, number],
                self.place.partner(stage),
            ).start()

    def core_total(self, number):
        some = self.parts[number].target.at[pl.ds(0, self.place.n_rows // 2)]
        return remote(
            some, some, self.core_send.at[number], self.core_recv.at[number], self.place.sibling()
        )

    def core_hop(self, number, first):
        for group in self.held(self.place.digits):
            block = self.group(number, group)
            remote(
                block,
                block,
                self.core_send.at[number],
                self.core_recv.at[number],
                self.place.sibling(),
            ).start()

    def hops(self, number):
        part, take = self.parts[number], functools.partial
        along = []
        if part.straight:
            along.append((1.6, take(self.far_hop, number)) + waits(take(self.far_total, number)))
        else:
            for step in range(self.place.n_mem - 1):
                along.append(
                    (
                        0.55 if step else 1.4,
                        take(self.line_hop, number, step),
                        take(self.line_arrived, number, step),
                        take(self.line_sent, number, step),
                    )
                )
        plane = []
        for stage in range(self.place.digits):
            total = take(self.plane_total, number, stage)
            plane.append((1.5, take(self.plane_hop, number, stage)) + waits(total))
        core = (1.5, take(self.core_hop, number)) + waits(take(self.core_total, number))
        return plane[: part.near] + along + plane[part.near :] + [core]

    def events(self, number):
        hops = self.hops(number)
        time, found = float(number), []

        def act(at):
            if at == 0:
                self.own(number).start()
            else:
                if at == 1:
                    self.own(number).wait()
                hops[at - 1][2]()
            hops[at][1](at == 0)

        for at in range(len(hops)):
            time += hops[at][0] if at else 0.0
            found.append((time, functools.partial(act, at)))
        return found, time + 0.9

    def sent(self, number):
        for hop in self.hops(number):
            hop[3]()


class Job:
    def __init__(self, left, right, first, target):
        self.left, self.right, self.first, self.target = left, right, first, target
        self.small = right is None
        self.width = target.shape[-1]
        self.large = 0


OUT_SLOTS, LANE_SLOTS, SUM_SLOTS, CORE_RING, FIRST_RING, RING = 2, 3, 2, 2, 6, 4


class Reduce:
    def __init__(self, place, jobs, sems, pool, small):
        self.place, self.jobs, self.small = place, jobs, small
        self.core_send, self.core_recv, self.stage_send, self.stage_recv = sems
        wanted = [place.row]
        for stage in reversed(range(place.digits)):
            wanted = wanted + [place.turn(group, stage) for group in wanted]
        self.wanted = [group // 2 for group in wanted]
        for number, job in enumerate(job for job in jobs if not job.small):
            job.large = number
        used, half = [0], place.n_rows // 2

        def take(count, units):
            first = used[0]
            used[0] += count * units
            return [pool.at[pl.ds(first + i * units, units)] for i in range(count)]

        self.outs = take(OUT_SLOTS, half)
        self.lane_slots = take(LANE_SLOTS, half)
        self.core_ring = take(CORE_RING, half)
        self.sum_slots, self.rings = [], []
        for stage in range(place.digits):
            self.sum_slots.append(take(SUM_SLOTS, self.count(stage)))
            self.rings.append(take(RING if stage else FIRST_RING, self.count(stage)))
        self.rings.append(take(RING, 1))
        self.used = used[0]

    def count(self, stage):
        return max(self.place.n_rows // 4 >> stage, 1)

    def cut(self, ref, job):
        return ref if job.width == ref.shape[-1] else ref.at[:, :, :, pl.ds(0, job.width)]

    def out(self, job):
        return self.cut(self.outs[job.large % OUT_SLOTS], job)

    def lanes(self, job):
        if job.small:
            return self.small.lanes
        return self.cut(self.lane_slots[job.large % LANE_SLOTS], job)

    def core_in(self, job):
        if job.small:
            return self.small.core_in
        return self.cut(self.core_ring[job.large % CORE_RING], job)

    def sums(self, job, stage):
        if job.small:
            return self.small.sums[stage]
        return self.cut(self.sum_slots[stage][job.large % SUM_SLOTS], job)

    def arrived(self, job, stage):
        if job.small:
            return self.small.arrived[stage]
        ring = self.rings[stage]
        units = self.cut(ring[job.large % len(ring)], job)
        if stage == self.place.digits:
            return units.at[0, pl.ds(0, self.place.n_mem - 1)]
        return units

    def previous(self, number, distance):
        found = [n for n in range(number) if not self.jobs[n].small]
        if self.jobs[number].small or len(found) < distance:
            return None
        return found[-distance]

    def core_copy(self, number):
        job = self.jobs[number]
        source = job.left.at[1 - self.place.lane] if job.small else self.out(job)
        return remote(
            source,
            self.core_in(job),
            self.core_send.at[number],
            self.core_recv.at[number],
            self.place.sibling(),
        )

    def product(self, job, side, store):
        half = self.place.n_rows // 2
        group = job.left.shape[1] // half
        width = min(TILE, job.width)
        unit = (self.place.n_mem, group // self.place.n_mem, width)

        def column_step(step, carry):
            source = pl.ds(pl.multiple_of(job.first + step * width, width), width)
            value = dot(job.left[side], job.right[:, source])
            for index in range(half):
                block = value[index * group : (index + 1) * group].reshape(unit)
                store(index, span(step, width), block)
            return carry

        lax.fori_loop(0, job.width // width, column_step, 0)

    def core_stage(self, number):
        job = self.jobs[number]
        if not job.small:
            before = self.previous(number, OUT_SLOTS)
            if before is not None:
                self.core_copy(before).wait_send()
            out = self.out(job)

            def store(index, columns, value):
                out[index, :, :, columns] = value.astype(out.dtype)

            self.product(job, 1 - self.place.lane, store)
        self.core_copy(number).start()

    def lane_stage(self, number):
        job = self.jobs[number]
        before = self.previous(number, LANE_SLOTS)
        if before is not None:
            self.total(before, 0).wait_send()
        lanes, arrived = self.lanes(job), self.core_in(job)
        self.core_copy(number).wait_recv()
        if job.small:
            lanes[...] = job.left[self.place.lane] + arrived[...]
        else:

            def store(index, columns, value):
                total = value + arrived[index, :, :, columns].astype(jnp.float32)
                lanes[index, :, :, columns] = total.astype(lanes.dtype)

            self.product(job, self.place.lane, store)
        self.send(number, 0)

    def unit(self, job, stage, index):
        if stage == 0:
            return self.lanes(job).at[self.wanted[index]]
        return self.sums(job, stage - 1).at[index]

    def piece(self, job, unit, member):
        return unit if job.small else unit.at[member]

    def send(self, number, stage):
        job, place = self.jobs[number], self.place
        arrived = self.arrived(job, stage)
        sems = (self.stage_send.at[stage, number], self.stage_recv.at[stage, number])
        if stage == place.digits:
            unit = self.unit(job, stage, 0)
            for step in range(1, place.n_mem):
                source = self.piece(job, unit, (place.mem + step) % place.n_mem)
                remote(source, arrived.at[step - 1], *sems, place.far(step)).start()
            return
        left = self.count(stage)
        for index in range(left):
            source = self.unit(job, stage, left + index)
            remote(source, arrived.at[index], *sems, place.partner(stage)).start()

    def total(self, number, stage):
        some = self.arrived(self.jobs[number], stage)
        sems = (self.stage_send.at[stage, number], self.stage_recv.at[stage, number])
        return remote(some, some, *sems, self.place.far(1))

    def stage(self, number, stage):
        job, place = self.jobs[number], self.place
        arrived = self.arrived(job, stage)
        if stage == place.digits:
            self.total(number, stage).wait_recv()
            value = self.piece(job, self.unit(job, stage, 0), place.mem)[...].astype(jnp.float32)
            for step in range(place.n_mem - 1):
                value = value + arrived[step].astype(jnp.float32)
            job.target[...] = value
            return
        before = self.previous(number, SUM_SLOTS)
        if before is not None:
            self.total(before, stage + 1).wait_send()
        self.total(number, stage).wait_recv()
        sums = self.sums(job, stage)
        for index in range(self.count(stage)):
            unit, coming, target = self.unit(job, stage, index), arrived.at[index], sums.at[index]
            if job.small:
                target[...] = unit[...] + coming[...]
                continue

            def add(member, carry, unit=unit, coming=coming, target=target):
                value = unit[member].astype(jnp.float32) + coming[member].astype(jnp.float32)
                target[member] = value.astype(target.dtype)
                return carry

            lax.fori_loop(0, place.n_mem, add, 0)
        self.send(number, stage + 1)

    def events(self, number):
        found = [(0.0, functools.partial(self.core_stage, number))]
        found.append((0.9, functools.partial(self.lane_stage, number)))
        time = 2.2 if number < 2 else 3.2
        for stage in range(self.place.digits + 1):
            found.append((time, functools.partial(self.stage, number, stage)))
            time += 1.4
        found[-1] = (found[-1][0] - 0.3, found[-1][1])
        return [(number + time, action) for time, action in found]

    def finish(self):
        n_jobs, last = len(self.jobs), self.place.digits
        out = {self.previous(number, OUT_SLOTS) for number in range(n_jobs)}
        lanes = {self.previous(number, LANE_SLOTS) for number in range(n_jobs)}
        sums = {self.previous(number, SUM_SLOTS) for number in range(n_jobs)}
        for number in range(n_jobs):
            if number not in out:
                self.core_copy(number).wait_send()
            if number not in lanes:
                self.total(number, 0).wait_send()
            if number not in sums:
                for stage in range(1, last + 1):
                    self.total(number, stage).wait_send()


NORMAL = (((1,), (0,)), ((), ()))
TURNED = (((1,), (1,)), ((), ()))
LEFT_TURNED = (((0,), (0,)), ((), ()))


def dot(left, right, dims=NORMAL):
    return lax.dot_general(left, right, dims, preferred_element_type=jnp.float32)


def times(left, weight, store, part=0, parts=1):
    size = weight.shape[-1]
    width = min(TILE, size)
    tiles = size // width // parts

    def column_step(step, carry):
        columns = span(step, width)
        store(columns, dot(left[...], weight[:, :, :, columns].reshape(-1, width)))
        return carry

    lax.fori_loop(part * tiles, (part + 1) * tiles, column_step, 0)


def times_turned(left, weight, store):
    unit = weight.shape[1] * weight.shape[2]
    units = max(TILE // unit, 1)

    def row_step(step, carry):
        rows = weight[span(step, units)].reshape(units * unit, weight.shape[-1])
        store(span(step, units * unit), dot(left[...], rows, TURNED))
        return carry

    lax.fori_loop(0, weight.shape[0] // units, row_step, 0)


def into(target):
    def store(columns, value):
        target[:, columns] = value.astype(target.dtype)

    return store


ROWS = 32


def by_rows(count, step):
    def body(index, carry):
        step(span(index, ROWS))
        return carry

    lax.fori_loop(0, count // ROWS, body, 0)


def norm_forward(total, gains, index, unit, scale, use):
    gain, shift = gains[index : index + 1, :], gains[index + 3 : index + 4, :]

    def step(rows):
        value = total[rows, :]
        centre = value - jnp.mean(value, axis=-1, keepdims=True)
        spread = jnp.mean(centre * centre, axis=-1, keepdims=True)
        root = lax.rsqrt(spread + EPS)
        scaled = centre * root
        unit[rows, :] = scaled
        scale[rows, :] = root
        use(rows, scaled * gain + shift)

    by_rows(total.shape[0], step)


def norm_slope(incoming, scaled, root, gain):
    width = scaled.shape[1]
    scaled_grad = incoming * gain
    first = jnp.mean(scaled_grad, axis=-1, keepdims=True)
    second = jnp.mean(scaled_grad * scaled, axis=-1, keepdims=True)
    value = root * (scaled_grad - first - scaled * second)
    of_gain = jnp.sum((incoming * scaled).reshape(ROWS // 8, 8, width), axis=0)
    of_shift = jnp.sum(incoming.reshape(ROWS // 8, 8, width), axis=0)
    return value, of_gain, of_shift


def keep_small(index, sums, small):
    for offset, partial in ((index, sums[0]), (index + 3, sums[1])):
        line = jnp.sum(partial, axis=0, keepdims=True)
        for group in range(2 * small.shape[1]):
            small[group % 2, group // 2, offset : offset + 1, :] = line[
                :, group * 128 : (group + 1) * 128
            ]


def norm_backward(grad, gains, index, unit, scale, target, target_low, small):
    gain = gains[index : index + 1, :]

    def body(block, sums):
        rows = span(block, ROWS)
        value, of_gain, of_shift = norm_slope(grad[rows, :], unit[rows, :], scale[rows, :], gain)
        target[rows, :] = value
        target_low[rows, :] = value.astype(target_low.dtype)
        return (sums[0] + of_gain, sums[1] + of_shift)

    zero = jnp.zeros((8, unit.shape[1]), jnp.float32)
    keep_small(index, lax.fori_loop(0, unit.shape[0] // ROWS, body, (zero, zero)), small)


def norm_both(total, grad, gains, index, result, target, target_low, small):
    gain, shift = gains[index : index + 1, :], gains[index + 3 : index + 4, :]

    def body(block, sums):
        rows = span(block, ROWS)
        value = total[rows, :]
        centre = value - jnp.mean(value, axis=-1, keepdims=True)
        spread = jnp.mean(centre * centre, axis=-1, keepdims=True)
        root = lax.rsqrt(spread + EPS)
        scaled = centre * root
        result[rows, :] = scaled * gain + shift
        incoming = grad[rows, :].astype(jnp.float32)
        value, of_gain, of_shift = norm_slope(incoming, scaled, root, gain)
        target[rows, :] = value
        target_low[rows, :] = value.astype(target_low.dtype)
        return (sums[0] + of_gain, sums[1] + of_shift)

    zero = jnp.zeros((8, total.shape[1]), jnp.float32)
    keep_small(index, lax.fori_loop(0, total.shape[0] // ROWS, body, (zero, zero)), small)


def lane_masks(dtype, scale):
    low = lax.broadcasted_iota(jnp.int32, (1, 2 * HEAD_DIM), 1) < HEAD_DIM
    first = jnp.where(low, scale, 0.0)
    return first.astype(dtype), (scale - first).astype(dtype)


def turned_pair(eye, rows):
    size = rows.shape[1]
    return dot(eye[0:size, 0:size], rows, TURNED).astype(rows.dtype)


def attention_forward(query, keys, values, bias, blocks, eye, mixed, turned, lse, first, last):
    masks = lane_masks(query.dtype, SCALE)

    def pair_step(pair, carry):
        lanes = span(pair, 2 * HEAD_DIM)
        two_query, two_keys, two_values = query[:, lanes], keys[:, lanes], values[:, lanes]
        columns = []
        for q0, q1, k0, k1 in blocks:
            block_values = turned_pair(eye, two_values[k0:k1])
            rows = []
            for head in range(2):
                scores = dot(two_keys[k0:k1], two_query[q0:q1] * masks[head], TURNED)
                scores = scores + bias[k0:k1, q0:q1]
                top = jnp.max(scores, axis=0, keepdims=True)
                weight = jnp.exp(scores - top)
                norm = jnp.sum(weight, axis=0, keepdims=True)
                head_values = block_values[head * HEAD_DIM : (head + 1) * HEAD_DIM]
                rows.append(dot(head_values, weight.astype(query.dtype)) * (1.0 / norm))
                lse[pair, head : head + 1, q0:q1] = top + jnp.log(norm)
            columns.append(jnp.concatenate(rows, axis=0))
        total = jnp.concatenate(columns, axis=1).astype(mixed.dtype)
        turned[pair % 2, span(pair // 2, 2 * HEAD_DIM), :] = total
        mixed[:, lanes] = dot(eye[...], total, TURNED).astype(mixed.dtype)
        return carry

    lax.fori_loop(first, last, pair_step, 0)


def stacked(parts):
    cuts = sorted({at for first, value in parts for at in (first, first + value.shape[0])})
    found = []
    for low, high in zip(cuts, cuts[1:]):
        total = None
        for first, value in parts:
            if first <= low and high <= first + value.shape[0]:
                piece = value[low - first : high - first]
                total = piece if total is None else total + piece
        found.append(total)
    return jnp.concatenate(found, axis=0)


def attention_backward(
    query, keys, values, bias, blocks, eye, lse, grad, query_grad, key_grad, value_grad, first, last
):
    scaled, masks = lane_masks(query.dtype, SCALE), lane_masks(query.dtype, 1.0)

    def pair_step(pair, carry):
        lanes = span(pair, 2 * HEAD_DIM)
        two_query, two_keys, two_values = query[:, lanes], keys[:, lanes], values[:, lanes]
        two_grad = grad[:, lanes]
        of_query, of_keys, of_values = [], [], []
        for q0, q1, k0, k1 in blocks:
            block_keys, block_values = two_keys[k0:k1], two_values[k0:k1]
            slopes, all_probs, heads_query, heads_grad = [], [], [], []
            for head in range(2):
                head_query = two_query[q0:q1] * scaled[head]
                head_grad = two_grad[q0:q1] * masks[head]
                scores = dot(block_keys, head_query, TURNED) + bias[k0:k1, q0:q1]
                probs = jnp.exp(scores - lse[pair, head : head + 1, q0:q1])
                pulled = dot(block_values, head_grad, TURNED)
                inner = jnp.sum(probs * pulled, axis=0, keepdims=True)
                slopes.append((probs * (pulled - inner)).astype(query.dtype))
                all_probs.append(probs.astype(query.dtype))
                heads_query.append(head_query)
                heads_grad.append(head_grad)
            both = jnp.concatenate(slopes, axis=1)
            of_keys.append((k0, dot(both, jnp.concatenate(heads_query, axis=0))))
            both = jnp.concatenate(all_probs, axis=1)
            of_values.append((k0, dot(both, jnp.concatenate(heads_grad, axis=0))))
            block_turned = turned_pair(eye, block_keys * jnp.asarray(SCALE, query.dtype))
            rows = [
                dot(block_turned[head * HEAD_DIM : (head + 1) * HEAD_DIM], slopes[head])
                for head in range(2)
            ]
            of_query.append(jnp.concatenate(rows, axis=0))
        total = jnp.concatenate(of_query, axis=1).astype(query_grad.dtype)
        query_grad[:, lanes] = dot(eye[...], total, TURNED).astype(query_grad.dtype)
        key_grad[:, lanes] = stacked(of_keys).astype(key_grad.dtype)
        value_grad[:, lanes] = stacked(of_values).astype(value_grad.dtype)
        return carry

    lax.fori_loop(first, last, pair_step, 0)


def turn_blocks(left, eye, store):
    width = eye.shape[0]
    for block in range(left.shape[1] // width):
        columns = pl.ds(block * width, width)
        store(block, dot(eye[...], left[:, columns], TURNED).astype(left.dtype))


def turn_by_lane(left, eye, target):
    group = eye.shape[0] // 2

    def store(block, value):
        target[0, pl.ds(block * group, group), :] = value[:group]
        target[1, pl.ds(block * group, group), :] = value[group:]

    turn_blocks(left, eye, store)


SQUARES = 8


def layer_kernel(places, sizes, *refs):
    n_rows, n_mem, width, ff, shard = sizes
    ref = SimpleNamespace(**jax.tree.map(lambda place: refs[place], places))
    place = Place(n_rows, n_mem)
    many = ff // width
    own_ff = ff // (n_rows * n_mem)
    (
        at_query,
        at_key,
        at_value,
        at_output,
        at_cross_query,
        at_cross_key,
        at_cross_value,
        at_cross_output,
    ) = range(SQUARES)
    full = ref.full
    expand, contract = ref.expand_full, ref.contract_full
    tokens, gains = ref.tokens, ref.gains
    low, turned = SimpleNamespace(**ref.low), SimpleNamespace(**ref.turned)

    order = [
        at_query,
        at_key,
        at_value,
        at_output,
        at_cross_key,
        at_cross_value,
        at_cross_query,
        at_cross_output,
    ]
    pool = ref.pool

    def gather_slot(number):
        return pool.at[pl.ds(number % GATHER_SLOTS * n_rows, n_rows)]

    sources = [ref.squares[index] for index in order]
    sources += [ref.expand.at[:, pl.ds(j * width, width)] for j in range(many)]
    sources += [ref.contract.at[pl.ds(j * shard, shard), :] for j in range(many)]
    stores = [full[index] for index in order] + [expand.at[j] for j in range(many)]
    stores += [contract.at[:, :, j] for j in range(many)]
    parts = [Part(item, gather_slot(n), int(n % 2 == 1 or n % 8 == 2)) for n, item in enumerate(sources)]
    parts.insert(SMALL_AT, Part(ref.small, ref.small_full, 0, True))
    gather = Gather(place, parts, ref.gather_sems)

    def keep(number):
        return pltpu.make_async_copy(gather_slot(number), stores[number], ref.keep_sem.at[number])

    count = [0]

    def load_slot(number):
        first = pool.shape[0] - (1 + number % SLOTS) * n_rows
        return pool.at[pl.ds(first, n_rows)]

    def load(pieces):
        number = count[0]
        count[0] += 1
        for source, first, rows in pieces:
            target = load_slot(number).at[pl.ds(first, rows)]
            pltpu.make_async_copy(source, target, ref.slot_sem.at[number % SLOTS]).start()
        return number

    def ready(number):
        slot = load_slot(number)
        pltpu.make_async_copy(slot, slot, ref.slot_sem.at[number % SLOTS]).wait()
        return slot

    def contract_rows(j):
        groups = n_rows // many
        return [(contract.at[j * groups + i], i * n_mem, n_mem) for i in range(groups)]

    mem_block = ref.memory.shape[1]
    memory, mem_rows = ref.memory, ref.mem_rows

    def memory_own():
        return pltpu.make_async_copy(
            memory.at[place.mem], mem_rows.at[span(place.mem, mem_block)], ref.mem_sem.at[0]
        )

    def memory_total():
        some = mem_rows.at[pl.ds(0, (n_mem - 1) * mem_block)]
        return remote(some, some, ref.mem_sem.at[1], ref.mem_sem.at[2], place.far(1))

    ref.small[...] = jnp.zeros_like(ref.small)
    for member in range(n_mem):

        @pl.when(place.mem == member)
        def _(member=member):
            lanes = slice(member * shard, (member + 1) * shard)
            ref.small[0:3, lanes] = ref.norm_gains[...].astype(jnp.float32)
            ref.small[3:6, lanes] = ref.norm_shifts[...].astype(jnp.float32)

    place.greet()
    memory_own().start()
    for step in range(1, n_mem):
        remote(
            memory.at[(place.mem + step) % n_mem],
            mem_rows.at[span(place.mem, mem_block)],
            ref.mem_sem.at[1],
            ref.mem_sem.at[2],
            place.far(step),
        ).start()

    actions, whole = [], []
    for part in range(len(parts)):
        found, time = gather.events(part)
        for hop, (at, action) in enumerate(found):
            actions.append((HOP + 10 * part + hop, at, action))
        whole.append(time)
    first_hops = [HOP, HOP + 10]
    for code, _, action in actions:
        if code in first_hops:
            action()
    actions = [item for item in actions if item[0] not in first_hops]

    self_bias, cross_bias, eye = ref.self_bias, ref.cross_bias, ref.eye
    own_row = ref.token_ids[pl.ds(place.mem, 1), :].astype(jnp.float32)
    mem_row = ref.memory_ids[pl.ds(place.mem, 1), :].astype(jnp.float32)
    key_place = lax.broadcasted_iota(jnp.int32, self_bias.shape, 0)
    query_place = lax.broadcasted_iota(jnp.int32, self_bias.shape, 1)
    own_wide = jnp.broadcast_to(own_row, self_bias.shape)
    mem_wide = jnp.broadcast_to(mem_row, (cross_bias.shape[1], cross_bias.shape[0]))
    same = (jnp.transpose(own_wide) == own_wide) & (key_place <= query_place)
    self_bias[...] = jnp.where(same, 0.0, NEG)
    cross_bias[...] = jnp.where(jnp.transpose(mem_wide) == own_row, 0.0, NEG)
    eye_row = lax.broadcasted_iota(jnp.int32, eye.shape, 0)
    eye_column = lax.broadcasted_iota(jnp.int32, eye.shape, 1)
    eye[...] = jnp.where(eye_row == eye_column, 1.0, 0.0).astype(eye.dtype)
    turn_by_lane(tokens, eye, turned.tokens)

    accumulated, other = ref.accumulated, ref.other
    hidden, slope, hidden_turned = ref.hidden, ref.slope, ref.hidden_turned

    def small_piece():
        blocks = ref.small_full
        for group in range(n_rows):
            total = None
            for member in range(n_mem):
                value = blocks[group, member]
                total = value if total is None else total + value
            gains[:, group * 128 : (group + 1) * 128] = total

    def query_piece(slot):
        times(tokens, slot, into(ref.query))

    def key_piece(slot):
        times(tokens, slot, into(ref.keys))

    pairs = width // (2 * HEAD_DIM)
    self_blocks = [
        (first, first + 128, max(first - DOC_LIMIT, 0), first + 128)
        for first in range(0, self_bias.shape[1], 128)
    ]
    cross_blocks = [(0, cross_bias.shape[1], 0, cross_bias.shape[0])]

    def value_piece(slot):
        times(tokens, slot, into(ref.values))

    def self_forward(first, last, slot):
        attention_forward(
            ref.query,
            ref.keys,
            ref.values,
            self_bias,
            self_blocks,
            eye,
            ref.attended,
            turned.attended,
            ref.self_lse,
            first,
            last,
        )

    def output_piece(slot):
        def store(columns, value):
            accumulated[:, columns] = ALPHA * tokens[:, columns].astype(jnp.float32) + value

        times(ref.attended, slot, store)

    def output_norm(slot):
        def use(rows, value):
            ref.first_low[rows, :] = value.astype(jnp.bfloat16)
            other[rows, :] = value

        norm_forward(accumulated, gains, 0, ref.unit1, ref.scale1, use)

    def cross_key_piece(slot):
        memory_own().wait()
        memory_total().wait_recv()
        times(mem_rows, slot, into(ref.cross_keys))
        turn_by_lane(mem_rows, eye, turned.memory)

    def cross_value_piece(slot):
        times(mem_rows, slot, into(ref.cross_values))
        turn_by_lane(ref.first_low, eye, turned.first)

    def cross_query_piece(slot):
        times(ref.first_low, slot, into(ref.cross_query))

    def cross_forward(first, last, slot):
        attention_forward(
            ref.cross_query,
            ref.cross_keys,
            ref.cross_values,
            cross_bias,
            cross_blocks,
            eye,
            ref.crossed,
            turned.crossed,
            ref.cross_lse,
            first,
            last,
        )

    def cross_output_piece(slot):
        def store(columns, value):
            accumulated[:, columns] = ALPHA * other[:, columns] + value

        times(ref.crossed, slot, store)

    def cross_output_norm(slot):
        def use(rows, value):
            ref.second_low[rows, :] = value.astype(jnp.bfloat16)
            other[rows, :] = value

        norm_forward(accumulated, gains, 1, ref.unit2, ref.scale2, use)

    def expand_piece(j, half, slot):
        def store(columns, value):
            there = pl.ds(pl.multiple_of(j * width + columns.start, TILE), columns.size)
            bell = 0.5 * (1.0 + lax.erf(value * math.sqrt(0.5)))
            density = jnp.exp(value * value * -0.5) * (1.0 / math.sqrt(2.0 * math.pi))
            hidden[:, there] = (value * bell).astype(hidden.dtype)
            slope[:, there] = (bell + value * density).astype(slope.dtype)

        times(ref.second_low, slot, store, half, 2)

    def expand_turn(j, slot):
        def keep(block, value):
            for index in range(value.shape[0] // shard):
                first = j * width + block * value.shape[0] + index * shard
                device, job = first // own_ff, first % own_ff // shard
                group, member = device // n_mem, device % n_mem
                at = group // 2 * n_mem * shard + member * shard
                hidden_turned[job, group % 2, at : at + shard, :] = value[
                    index * shard : (index + 1) * shard
                ]

        turn_blocks(hidden.at[:, pl.ds(j * width, width)], eye, keep)

    def contract_piece(j, slot):
        block = 2 * n_mem * shard
        for index in range(n_rows // 2):
            rows = pl.ds(index * n_mem * shard, n_mem * shard)
            both = jnp.concatenate([hidden_turned[j, 0, rows], hidden_turned[j, 1, rows]], axis=0)
            columns = pl.ds(index * block, block)
            low.branch[:, columns] = dot(eye[...], both, TURNED).astype(jnp.bfloat16)

        def store(columns, value):
            if j == 0:
                accumulated[:, columns] = ALPHA * other[:, columns] + value
            else:
                accumulated[:, columns] = accumulated[:, columns] + value

        times(low.branch, slot, store)

    quarters = [(pairs * at // 4, pairs * (at + 1) // 4) for at in range(4)]
    pieces = [
        [query_piece],
        [key_piece],
        [value_piece] + [functools.partial(self_forward, *quarter) for quarter in quarters],
        [output_piece, output_norm],
        [cross_key_piece],
        [cross_value_piece],
        [cross_query_piece] + [functools.partial(cross_forward, *quarter) for quarter in quarters],
        [cross_output_piece, cross_output_norm],
    ]
    for j in range(many):
        halves = [functools.partial(expand_piece, j, half) for half in range(2)]
        pieces.append(halves + [functools.partial(expand_turn, j)])
    pieces += [[functools.partial(contract_piece, j)] for j in range(many)]

    def arrive(part):
        gather.core_total(part).wait_recv()
        if part != SMALL_AT:
            keep(part - (part > SMALL_AT)).start()

    def use(part, index):
        if part == SMALL_AT:
            small_piece()
        else:
            number = part - (part > SMALL_AT)
            pieces[number][index](gather_slot(number))

    def settle(part):
        gather.sent(part)
        if part != SMALL_AT:
            keep(part - (part > SMALL_AT)).wait()

    last = 0.0
    for part, time in enumerate(whole):
        time = max(time, last + 0.5)
        actions.append((ARRIVE + part, time, functools.partial(arrive, part)))
        count_here = 1 if part == SMALL_AT else len(pieces[part - (part > SMALL_AT)])
        for index in range(count_here):
            at = time + 0.2 + 0.04 * index
            actions.append((USE + 10 * part + index, at, functools.partial(use, part, index)))
        actions.append((SETTLE + part, time + 0.45, functools.partial(settle, part)))
        last = time
    for action in planned(actions, FORWARD_PLAN):
        action()
    place.tell(ref.ready_sem)

    backward_sources, loads = [], []
    used = [0]

    def next_slot():
        slot = ready(loads[used[0]])
        used[0] += 1
        if len(loads) < len(backward_sources):
            loads.append(load(backward_sources[len(loads)]))
        return slot

    small_sums = ref.small_sums
    small_sums[...] = jnp.zeros_like(small_sums)
    def inner_piece(j):
        slot = next_slot()

        def store(columns, value):
            there = pl.ds(pl.multiple_of(j * width + columns.start, TILE), columns.size)
            slope[:, there] = (value * slope[:, there].astype(jnp.float32)).astype(slope.dtype)

        times_turned(low.third, slot, store)

    def second_piece(j):
        slot = next_slot()

        def store(columns, value):
            if j == 0:
                other[:, columns] = ALPHA * accumulated[:, columns] + value
            else:
                other[:, columns] = other[:, columns] + value

        times_turned(slope.at[:, pl.ds(j * width, width)], slot, store)

    def second_norm_piece():
        norm_backward(
            other, gains, 1, ref.unit2, ref.scale2, accumulated, low.second, small_sums
        )

    def cross_start_piece():
        times_turned(low.second, next_slot(), into(low.branch))

    def cross_piece(first, last):
        attention_backward(
            ref.cross_query,
            ref.cross_keys,
            ref.cross_values,
            cross_bias,
            cross_blocks,
            eye,
            ref.cross_lse,
            low.branch,
            low.cross_query,
            low.cross_key,
            low.cross_value,
            first,
            last,
        )

    def first_piece():
        def store(columns, value):
            other[:, columns] = ALPHA * accumulated[:, columns] + value

        times_turned(low.cross_query, next_slot(), store)

    def first_norm_piece():
        norm_backward(other, gains, 0, ref.unit1, ref.scale1, accumulated, low.first, small_sums)

    def self_start_piece():
        times_turned(low.first, next_slot(), into(low.branch))

    def self_piece(first, last):
        attention_backward(
            ref.query,
            ref.keys,
            ref.values,
            self_bias,
            self_blocks,
            eye,
            ref.self_lse,
            low.branch,
            low.query,
            low.key,
            low.value,
            first,
            last,
        )

    mem_out, mem_in = ref.mem_out, ref.mem_in

    def grad_own():
        return pltpu.make_async_copy(
            mem_out.at[span(place.mem, mem_block)], mem_in.at[place.mem], ref.mem_sem.at[3]
        )

    def grad_total():
        some = mem_in.at[pl.ds(0, n_mem - 1)]
        return remote(some, some, ref.mem_sem.at[4], ref.mem_sem.at[5], place.far(1))

    def memory_key_piece():
        times_turned(low.cross_key, next_slot(), into(other))

    def memory_value_piece():
        def store(columns, value):
            mem_out[:, columns] = (other[:, columns] + value).astype(mem_out.dtype)

        times_turned(low.cross_value, next_slot(), store)
        grad_own().start()
        for step in range(1, n_mem):
            remote(
                mem_out.at[span((place.mem + step) % n_mem, mem_block)],
                mem_in.at[place.mem],
                ref.mem_sem.at[4],
                ref.mem_sem.at[5],
                place.far(step),
            ).start()

    def input_piece(left, start):
        target = ref.input_grad

        def store(columns, value):
            if start:
                target[:, columns] = ALPHA * accumulated[:, columns] + value
            else:
                target[:, columns] = target[:, columns] + value

        times_turned(left, next_slot(), store)

    def memory_end_piece():
        grad_own().wait()
        grad_total().wait_recv()
        for member in range(n_mem):
            ref.memory_grad[member] = mem_in[member].astype(jnp.float32)

    halves = ((0, width // 2), (width // 2, width // 2))
    grads = ref.grads
    plans = []
    for j in range(many):
        for first, columns in halves if j == 0 else ((0, width),):
            target = ref.contract_grad.at[pl.ds(j * shard, shard), pl.ds(first, columns)]
            plans.append((hidden_turned.at[j], low.third, first, target))
    for j in range(many):
        target = ref.expand_grad.at[:, pl.ds(j * width, width)]
        plans.append((turned.second, slope, j * width, target))
    plans += [
        (turned.crossed, low.second, 0, grads[at_cross_output]),
        (turned.memory, low.cross_key, 0, grads[at_cross_key]),
        (turned.memory, low.cross_value, 0, grads[at_cross_value]),
        (turned.first, low.cross_query, 0, grads[at_cross_query]),
        (turned.attended, low.first, 0, grads[at_output]),
        (small_sums, None, 0, ref.small_total),
        (turned.tokens, low.query, 0, grads[at_query]),
        (turned.tokens, low.key, 0, grads[at_key]),
    ]
    for first, columns in halves:
        target = grads[at_value].at[:, pl.ds(first, columns)]
        plans.append((turned.tokens, low.value, first, target))
    jobs = [Job(*plan) for plan in plans]
    reduce = Reduce(place, jobs, ref.reduce_sems, pool, SimpleNamespace(**ref.little))

    inner = [functools.partial(inner_piece, j) for j in range(many)]
    second = [functools.partial(second_piece, j) for j in range(many)]
    base = many + 1
    def weight(index):
        return [(full[index], 0, n_rows)]

    turn = functools.partial(turn_by_lane, ref.second_low, eye, turned.second)
    crosses = [functools.partial(cross_piece, pair, pair + 1) for pair in range(pairs)]
    selves = [functools.partial(self_piece, pair, pair + 1) for pair in range(pairs)]
    work = [(base - 1.7 + j, inner[j], contract_rows(j)) for j in range(2)]
    work += [(base - 1.3, turn, None)]
    work += [(base - 1.7 + j, inner[j], contract_rows(j)) for j in range(2, many)]
    work += [(base - 0.3 + j, second[j], [(expand.at[j], 0, n_rows)]) for j in range(many)]
    base = 2 * many + 1
    work += [
        (base - 0.2, second_norm_piece, None),
        (base - 0.15, cross_start_piece, weight(at_cross_output)),
    ]
    work += [(base + 0.3 + 0.05 * pair, crosses[pair], None) for pair in range(pairs)]
    work += [
        (base + 1.3, first_piece, weight(at_cross_query)),
        (base + 1.31, first_norm_piece, None),
        (base + 1.7, self_start_piece, weight(at_output)),
    ]
    work += [(base + 2.3 + 0.14 * pair, selves[pair], None) for pair in range(pairs)]
    work += [
        (base + 3.7, memory_key_piece, weight(at_cross_key)),
        (base + 4.3, memory_value_piece, weight(at_cross_value)),
        (base + 4.7, functools.partial(input_piece, low.query, True), weight(at_query)),
        (base + 5.5, functools.partial(input_piece, low.key, False), weight(at_key)),
        (base + 6.5, functools.partial(input_piece, low.value, False), weight(at_value)),
        (base + 8.5, memory_end_piece, None),
    ]
    actions = [(WORK + index, at, item) for index, (at, *item) in enumerate(work)]
    for number in range(len(jobs)):
        found = reduce.events(number)
        actions.append((CORE + number, found[0][0], found[0][1:]))
        actions.append((LANE + number, found[1][0], found[1][1:]))
        for stage, (at, action) in enumerate(found[2:]):
            actions.append((STAGE + 10 * number + stage, at, (action,)))
    ordered = planned(actions, BACKWARD_PLAN)
    backward_sources += [item[1] for item in ordered if len(item) > 1 and item[1] is not None]
    loads += [load(backward_sources[0]), load(backward_sources[1])]
    norm_both(
        accumulated, ref.out_grad, gains, 2, ref.result, accumulated, low.third, small_sums
    )

    place.hear(ref.ready_sem)
    for item in ordered:
        item[0]()

    total = ref.small_total[...]
    own = jnp.zeros((8, shard), jnp.float32)
    for member in range(n_mem):
        here = jnp.where(place.mem == member, 1.0, 0.0)
        own = own + here * total[:, member * shard : (member + 1) * shard]
    ref.gains_grad[...] = own[0:3]
    ref.shifts_grad[...] = own[3:6]
    reduce.finish()
    memory_total().wait_send()
    grad_total().wait_send()


SMALL_AT = 2
DOC_LIMIT = 64
HOP, ARRIVE, USE, SETTLE, CORE, LANE, STAGE, WORK = range(1000, 9000, 1000)
FORWARD_PLAN = (
    1001, 1011, 1020, 1002, 1003, 1012, 1030, 1040, 1021, 1004, 1013, 1031, 1041, 1014, 1032, 1050,
    1033, 1005, 1060, 1042, 1070, 2000, 1043, 1015, 1051, 1022, 1080, 1034, 1061, 1044, 1052, 3000,
    2001, 4000, 1023, 3010, 2002, 1071, 1053, 3020, 1062, 1035, 1072, 1081, 1045, 2003, 4001, 1090,
    1073, 3030, 1063, 1054, 3031, 2004, 1064, 1091, 3032, 4002, 1082, 3033, 3034, 1092, 1055, 4003,
    1100, 1110, 3040, 1093, 3041, 1074, 1065, 4004, 1083, 1101, 2005, 1111, 3050, 4005, 1120, 1084,
    1102, 2006, 1130, 1094, 1075, 3060, 4006, 2007, 1121, 1085, 3070, 3071, 1112, 1103, 1113, 3072,
    1122, 1131, 1104, 3073, 2008, 3074, 4007, 1140, 1150, 1114, 1095, 1123, 1132, 3080, 1141, 3081,
    1105, 1133, 1160, 1151, 2009, 1124, 3090, 3091, 4008, 2010, 1115, 1152, 1142, 1134, 3092, 4009,
    3100, 3101, 1143, 3102, 4010, 1161, 1153, 2011, 1144, 3110, 1125, 3111, 1135, 1154, 1162, 3112,
    1163, 2012, 3120, 3121, 1164, 1145, 2013, 3122, 3130, 1155, 4011, 4012, 2014, 4013, 3140, 1165,
    2015, 4014, 3150, 2016, 3160, 4015, 4016,
)
BACKWARD_PLAN = (
    5000, 6000, 5001, 8003, 6001, 5002, 7000, 8000, 7010, 6002, 5003, 8005, 7001, 8001, 6003, 8002,
    5004, 7020, 7002, 7011, 8004, 6004, 5005, 7021, 7030, 7012, 8006, 6005, 5006, 8007, 7040, 6006,
    7022, 5007, 7031, 8008, 8009, 6007, 8010, 5008, 7041, 8011, 7032, 7050, 7060, 8012, 6008, 8013,
    5009, 7051, 8014, 7042, 8015, 8016, 7070, 8017, 8018, 6009, 5010, 7061, 8019, 8020, 7052, 7080,
    6010, 5011, 8021, 7071, 8022, 7090, 8023, 6011, 5012, 7062, 8024, 8025, 7072, 8026, 7081, 6012,
    5013, 7091, 8027, 8028, 7100, 7110, 8029, 8032, 6013, 7082, 7101, 5014, 7120, 6014, 5015, 8030,
    7092, 8033, 7111, 7130, 7102, 6015, 5016, 7121, 8034, 6016, 7112, 7131, 7140, 7150, 5017, 7122,
    8031, 7132, 7141, 7160, 6017, 7151, 5018, 7161, 6018, 7142, 7170, 7152, 7180, 8035, 7171, 7162,
    7181, 7172, 7182,
)


def planned(actions, plan):
    codes = {code for code, _, _ in actions}
    if codes == set(plan):
        at = {code: number for number, code in enumerate(plan)}
        return [item for code, _, item in sorted(actions, key=lambda action: at[action[0]])]
    return [item for _, _, item in sorted(actions, key=lambda action: action[1])]


def copy_kernel(count, *refs):
    for source, target in zip(refs[:count], refs[count:]):
        target[...] = source[...]


def copied(values):
    near = pl.BlockSpec(memory_space=pltpu.VMEM)
    return pl.pallas_call(
        functools.partial(copy_kernel, len(values)),
        out_shape=[jax.ShapeDtypeStruct(value.shape, value.dtype) for value in values],
        in_specs=[near] * len(values),
        out_specs=[near] * len(values),
        compiler_params=pltpu.CompilerParams(vmem_limit_bytes=VMEM_LIMIT),
        name="results",
    )(*values)


def fused(n_rows, n_mem, ins):
    tokens, memory, squares = ins["tokens"], ins["memory"], ins["squares"]
    expand, contract = ins["expand"], ins["contract"]
    tokens_here, width = tokens.shape
    ff = expand.shape[1]
    shard = squares[0].shape[0]
    mem_tokens = memory.shape[0] * memory.shape[1]
    digits, half, many = (n_rows // 2).bit_length() - 1, n_rows // 2, ff // width
    pairs = width // (2 * HEAD_DIM)
    low, high = jnp.bfloat16, jnp.float32
    n_parts = 1 + SQUARES + 2 * many
    n_jobs = n_parts + 2
    dma, vmem = pltpu.SemaphoreType.DMA, pltpu.VMEM
    anywhere, near = pl.BlockSpec(memory_space=pl.ANY), pl.BlockSpec(memory_space=pltpu.VMEM)

    far_ins = dict(memory=memory)
    in_specs = {
        name: jax.tree.map(lambda _: anywhere if name in far_ins else near, value)
        for name, value in ins.items()
    }

    def out(shape, dtype=high):
        return jax.ShapeDtypeStruct(shape, dtype)

    outs = dict(
        result=out(tokens.shape),
        input_grad=out(tokens.shape),
        memory_grad=out(memory.shape),
        grads=[out(item.shape) for item in squares],
        expand_grad=out(expand.shape),
        contract_grad=out(contract.shape),
        gains_grad=out((3, shard)),
        shifts_grad=out((3, shard)),
    )
    far_outs = dict(
        full=[out((n_rows, n_mem, shard, width), low)] * SQUARES,
        expand_full=out((many, n_rows, n_mem, shard, width), low),
        contract_full=out((n_rows, n_mem, many, shard, width), low),
    )
    out_specs = jax.tree.map(lambda _: near, outs)
    out_specs.update(jax.tree.map(lambda _: anywhere, far_outs))
    outs.update(far_outs)

    def token_rows(dtype):
        return vmem((tokens_here, width), dtype)

    def memory_rows(dtype):
        return vmem((mem_tokens, width), dtype)

    tiny = (8, 128)

    counts = [half >> (stage + 1) for stage in range(digits)]
    units = (OUT_SLOTS + LANE_SLOTS + CORE_RING) * half + RING
    for stage, number in enumerate(counts):
        units += (SUM_SLOTS + (RING if stage else FIRST_RING)) * number
    units = max(units + SLOTS * n_rows, GATHER_SLOTS * n_rows)
    little = dict(
        lanes=vmem((half,) + tiny, high),
        core_in=vmem((half,) + tiny, high),
        sums=[vmem((number,) + tiny, high) for number in counts],
        arrived=[vmem((number,) + tiny, high) for number in counts]
        + [vmem((n_mem - 1,) + tiny, high)],
    )
    left = vmem((2, width // 2, tokens_here), low)
    scratch = dict(
        small=vmem(tiny, high),
        small_full=vmem((n_rows, n_mem) + tiny, high),
        small_total=vmem(tiny, high),
        pool=vmem((units, n_mem, shard, width), low),
        slot_sem=dma((SLOTS,)),
        keep_sem=dma((n_parts - 1,)),
        ready_sem=pltpu.SemaphoreType.REGULAR,
        mem_sem=dma((6,)),
        gather_sems=[
            dma(shape + (n_parts,))
            for shape in ((), (), (), (digits,), (digits,), (), ())
            + ((2 * (n_mem - 1),), (2 * (n_mem - 1),))
        ],
        reduce_sems=[dma(shape + (n_jobs,)) for shape in ((), (), (digits + 1,), (digits + 1,))],
        gains=vmem((8, width), high),
        query=token_rows(low),
        keys=token_rows(low),
        values=token_rows(low),
        attended=token_rows(low),
        first_low=token_rows(low),
        second_low=token_rows(low),
        cross_query=token_rows(low),
        crossed=token_rows(low),
        cross_keys=memory_rows(low),
        cross_values=memory_rows(low),
        mem_rows=memory_rows(low),
        mem_out=memory_rows(low),
        mem_in=vmem(memory.shape, low),
        unit1=token_rows(high),
        unit2=token_rows(high),
        accumulated=token_rows(high),
        other=token_rows(high),
        scale1=vmem((tokens_here, 1), high),
        scale2=vmem((tokens_here, 1), high),
        self_bias=vmem((tokens_here, tokens_here), high),
        cross_bias=vmem((mem_tokens, tokens_here), high),
        self_lse=vmem((pairs, 2, tokens_here), high),
        cross_lse=vmem((pairs, 2, tokens_here), high),
        eye=vmem((TILE, TILE), low),
        hidden=vmem((tokens_here, ff), low),
        slope=vmem((tokens_here, ff), low),
        hidden_turned=vmem((many, 2, width // 2, tokens_here), low),
        turned=dict(
            tokens=left, attended=left, first=left, memory=left, crossed=left, second=left
        ),
        low=dict(
            third=token_rows(low),
            second=token_rows(low),
            first=token_rows(low),
            branch=token_rows(low),
            cross_query=token_rows(low),
            cross_key=memory_rows(low),
            cross_value=memory_rows(low),
            query=token_rows(low),
            key=token_rows(low),
            value=token_rows(low),
        ),
        small_sums=vmem((2, half) + tiny, high),
        little=little,
    )
    in_values, in_tree = jax.tree.flatten(ins)
    out_shapes, out_tree = jax.tree.flatten(outs)
    scratch_shapes, scratch_tree = jax.tree.flatten(scratch)
    places = jax.tree.unflatten(in_tree, range(len(in_values)))
    at = len(in_values)
    places.update(jax.tree.unflatten(out_tree, range(at, at + len(out_shapes))))
    at += len(out_shapes)
    places.update(jax.tree.unflatten(scratch_tree, range(at, at + len(scratch_shapes))))
    values = pl.pallas_call(
        functools.partial(layer_kernel, places, (n_rows, n_mem, width, ff, shard)),
        out_shape=out_shapes,
        in_specs=jax.tree.leaves(in_specs),
        out_specs=jax.tree.leaves(out_specs),
        scratch_shapes=scratch_shapes,
        compiler_params=pltpu.CompilerParams(
            collective_id=0, has_side_effects=True, vmem_limit_bytes=VMEM_LIMIT
        ),
        name="layer",
    )(*in_values)
    found = jax.tree.unflatten(out_tree, values)
    for name in far_outs:
        del found[name]
    return found


def local(n_rows, n_mem, *args):
    (
        tokens,
        memory,
        token_ids,
        memory_ids,
        out_grad,
        self_query,
        self_key,
        self_value,
        self_output,
        cross_query,
        cross_key,
        cross_value,
        cross_output,
        expand_weight,
        contract_weight,
        norm_gains,
        norm_shifts,
    ) = args
    shard, width = self_query.shape
    suits = width == 128 * n_rows and shard % 16 == 0 and tokens.shape[0] == 1
    suits = suits and tokens.shape[1] == TILE and expand_weight.shape[1] == n_mem * width
    if not suits or n_rows < 4 or n_rows & (n_rows - 1) or n_mem < 2:
        return plain(*args)
    found = fused(
        n_rows,
        n_mem,
        dict(
            tokens=tokens[0],
            memory=memory,
            token_ids=token_ids,
            memory_ids=memory_ids,
            out_grad=out_grad[0],
            squares=[
                self_query,
                self_key,
                self_value,
                self_output,
                cross_query,
                cross_key,
                cross_value,
                cross_output,
            ],
            expand=expand_weight,
            contract=contract_weight,
            norm_gains=norm_gains,
            norm_shifts=norm_shifts,
        ),
    )
    values, tree = jax.tree.flatten(found)
    found = SimpleNamespace(**jax.tree.unflatten(tree, copied(values)))
    return (
        found.result[None],
        found.input_grad[None],
        found.memory_grad,
        *found.grads,
        found.expand_grad,
        found.contract_grad,
        found.gains_grad,
        found.shifts_grad,
    )


def solution(mesh):
    in_specs = (
        P(("rows", "mem"), None, None),
        P("rows", "mem", None),
        P("rows", None),
        P("rows", None),
        P(("rows", "mem"), None, None),
        P(("rows", "mem"), None),
        P(("rows", "mem"), None),
        P(("rows", "mem"), None),
        P(("rows", "mem"), None),
        P(("rows", "mem"), None),
        P(("rows", "mem"), None),
        P(("rows", "mem"), None),
        P(("rows", "mem"), None),
        P(("rows", "mem"), None),
        P(("rows", "mem"), None),
        P(None, ("rows", "mem")),
        P(None, ("rows", "mem")),
    )
    out_specs = (
        P(("rows", "mem"), None, None),
        P(("rows", "mem"), None, None),
        P("rows", "mem", None),
        P(("rows", "mem"), None),
        P(("rows", "mem"), None),
        P(("rows", "mem"), None),
        P(("rows", "mem"), None),
        P(("rows", "mem"), None),
        P(("rows", "mem"), None),
        P(("rows", "mem"), None),
        P(("rows", "mem"), None),
        P(("rows", "mem"), None),
        P(("rows", "mem"), None),
        P(None, ("rows", "mem")),
        P(None, ("rows", "mem")),
    )
    layer = functools.partial(local, mesh.shape["rows"], mesh.shape["mem"])
    return jax.shard_map(layer, mesh=mesh, in_specs=in_specs, out_specs=out_specs, check_vma=False)
```
